32 devices in a mesh: ctx: 8 (over z, x), fsdp: 4 (over y, core).
Axes of the slice: x: 2, y: 2, z: 4, core: 2. Of those that a mesh axis runs over, the one named last changes fastest.
Arguments:
- tokens: bfloat16 [4, 2048, 768], P('fsdp', 'ctx'), may hold values from -6 to 6
- cotangent: bfloat16 [4, 2048, 768], P('fsdp', 'ctx'), may hold values from -6 to 6
- seq_lengths: int32 [4, 2], P('fsdp'), may hold values from 1024 to 1024, as said below
- block_order: int32 [4, 16], P('fsdp'), may hold values from 0 to 15, as said below
- routes: int32 [2, 4, 2048, 2], P(None, 'fsdp', 'ctx'), may hold values from 0 to 11, all different within a row; in each aligned block of 256 rows (0 to 255, 256 to 511, ..., all dimensions but the last counted through in order) at most 64 rows name the same one
- gains: bfloat16 [2, 2, 768], P(None, None, 'fsdp'), may hold values from 0.5 to 1.5
- qkv_weights: bfloat16 [2, 3, 768, 768], P(None, None, 'fsdp'), may hold values from -0.21875 to 0.21875
- out_weight: bfloat16 [2, 768, 768], P(None, 'fsdp'), may hold values from -3 to 3
- router: bfloat16 [2, 768, 16], P(None, 'fsdp'), may hold values from -0.125 to 0.125
- const_values: bfloat16 [2, 2, 768], P(None, None, 'fsdp'), may hold values from -6 to 6
- w_gate_up: bfloat16 [2, 8, 2, 768, 2048], P(None, None, None, None, 'fsdp'), may hold values from -0.21875 to 0.21875
- w_down: bfloat16 [2, 8, 2048, 768], P(None, None, 'fsdp'), may hold values from -0.125 to 0.125
Outputs:
- output: float32 [4, 2048, 768], P('fsdp', 'ctx')
- input_grad: float32 [4, 2048, 768], P('fsdp', 'ctx')
- grad_gains: float32 [2, 2, 768], P(None, None, 'fsdp')
- grad_qkv: float32 [2, 3, 768, 768], P(None, None, 'fsdp')
- grad_out: float32 [2, 768, 768], P(None, 'fsdp')
- grad_router: float32 [2, 768, 16], P(None, 'fsdp')
- grad_const: float32 [2, 2, 768], P(None, None, 'fsdp')
- grad_gate_up: float32 [2, 8, 2, 768, 2048], P(None, None, None, None, 'fsdp')
- grad_down: float32 [2, 8, 2048, 768], P(None, None, 'fsdp')
The draws below stay inside these ranges and needn't reach their ends.
Inputs may be any that keep to these rules, and one draw needn't show every extreme that they name: `seq_lengths`: the first sequence of a pack holds 1024 to half the pack's tokens, the second the rest; in some pack the first holds exactly 1024. `block_order`: A pack is cut into blocks of 128 positions; entries 2c and 2c + 1 of a pack's row name the blocks that index c of ctx holds, in that order, the first from the pack's first half and the second from its second half; every block is named once. `routes`: each row names two different experts; among one device's 256 rows of a layer no expert is named more than 64 times, a bound that some block reaches.
All inputs are finite; a program needn't handle non-finite values.
Results may differ from the reference program's by a relative error of at most 0.035.
Values may be sent and summed in bfloat16 or wider, within the bound.
A program may use at most 384 MiB of HBM per device.

```python
import math
import jax
import jax.numpy as jnp
import numpy as np
from jax import lax

D = 768
HEADS = 12
HEAD_DIM = 64
FF = 2048
NF = 8
NC = 2
LAYERS = 2
MINLEN = 1024
TOK_DEV = 256
NE = 12
RC = 16
BLK = 128
MOST = 64
PACK_LEN = 2048
PACKS = 4
N_CTX = 8


def draw_seq_lengths(key, part):
    key = jax.random.fold_in(key, 11)
    length_key, pick_key = jax.random.split(key)
    first_length = jax.random.randint(length_key, (PACKS,), MINLEN, PACK_LEN // 2 + 1)
    chosen_pack = jax.random.randint(pick_key, (), 0, PACKS)
    first_length = jnp.where(jnp.arange(PACKS) == chosen_pack, MINLEN, first_length)
    return jnp.stack([first_length, PACK_LEN - first_length], axis=1).astype(jnp.int32)


def permute_one(single_key):
    return jax.random.permutation(single_key, PACK_LEN // (2 * BLK))


def draw_block_order(key, part):
    key = jax.random.fold_in(key, 23)
    device_count = PACK_LEN // (2 * BLK)
    lower_half = jax.vmap(permute_one)(jax.random.split(jax.random.fold_in(key, 1), PACKS))
    upper_half = jax.vmap(permute_one)(jax.random.split(jax.random.fold_in(key, 2), PACKS)) + device_count
    return jnp.stack([lower_half, upper_half], axis=2).reshape(PACKS, 2 * device_count).astype(jnp.int32)


def level_of(rng, shape, cuts, low, largest):
    level = 1.0
    for position, parts in cuts:
        steps = jax.random.uniform(jax.random.fold_in(jax.random.fold_in(rng, 6), position), (parts,), jnp.float32, low / len(cuts), largest / len(cuts))
        level = level * jnp.repeat(jnp.exp(steps), shape[position] // parts).reshape((-1,) + (1,) * (len(shape) - 1 - position))
    return level


def shared_out(stream_key, own, number, rows, number_of, top, most, skew):
    order = jax.random.permutation(stream_key, number_of)
    crowded, common = shares(number_of, rows * top, most, skew, True), shares(number_of, rows * top, most, skew, False)
    places = jnp.arange(number_of)

    def named(sizes, rotation):
        used = int((sizes > 0).sum())
        fixed = max(1, used // 4)
        shifted = fixed + (places - fixed + rotation * (used - fixed)) % max(1, number_of - fixed)
        return jnp.zeros((number_of,), jnp.int32).at[order[jnp.where(places < fixed, places, shifted)]].set(jnp.asarray(sizes, jnp.int32))

    sizes = jnp.where(number % 4 == 0, named(crowded, number // 4), named(common, number - number // 4 - 1))
    mixed = jax.random.permutation(jax.random.fold_in(own, 3), number_of)
    source_of, sink = mixed[0:number_of // 2 * 2:2], mixed[1:number_of // 2 * 2:2]
    margin = jnp.minimum(sizes[source_of] - 1, most - sizes[sink]) // 2
    margin = jnp.where((source_of == order[0]) | (sink == order[0]) | (sizes[sink] == 0), 0, jnp.maximum(margin, 0))
    shifted = jax.random.randint(jax.random.fold_in(own, 4), (number_of // 2,), 0, 1 << 20) % (margin + 1)
    sizes = sizes.at[source_of].add(-shifted).at[sink].add(shifted)
    items = jnp.searchsorted(jnp.cumsum(sizes), jnp.arange(rows * top), side="right").astype(jnp.int32)
    listing = items.reshape(top, rows).T
    listing = listing[jax.random.permutation(jax.random.fold_in(own, 1), rows)]
    rotation = jax.random.randint(jax.random.fold_in(own, 2), (rows, 1), 0, top)
    return jnp.take_along_axis(listing, (jnp.arange(top)[None, :] + rotation) % top, axis=1)


def shares(count, total, limit, slope, full):
    loads = [(1 << 20) // math.isqrt(grade ** slope) + 1 for grade in range(1, count + 1)]
    largest = limit if full else min(limit, max(-(-total // count), total * loads[0] // sum(loads)))
    least = 1 if total - largest >= count - 1 else 0
    counts, surplus = [largest] + [least] * (count - 1), total - largest - least * (count - 1)
    while surplus > 0:
        candidates = [i for i in range(1, count) if counts[i] < largest] or [i for i in range(1, count) if counts[i] < limit]
        pool, budget = sum([loads[i] for i in candidates]), surplus
        for i in candidates:
            more = min(limit - counts[i], max(1, budget * loads[i] // pool), surplus)
            counts[i] = counts[i] + more
            surplus = surplus - more
    return np.array(counts)


def centred(rng, dims, deviation, most, shards=(), kind=jnp.bfloat16):
    values = jax.random.normal(rng, dims, jnp.float32) * deviation
    if len(shards) > 0:
        values = level_of(rng, dims, shards, -0.22, 0.18) * values
    return jnp.clip(values, min=-most, max=most).astype(kind)


def setup_inputs(seed: int = 0) -> dict:
    streams_of = jax.random.split(jax.random.key(seed), 13)
    tokens = centred(streams_of[0], (PACKS, PACK_LEN, D), 1.0, 6.0, ((0, 4), (1, 8)))
    cotangent = centred(streams_of[1], (PACKS, PACK_LEN, D), 1.0, 6.0, ((0, 4), (1, 8)))
    seq_lengths = draw_seq_lengths(jax.random.fold_in(streams_of[12], 71), 0)
    block_order = draw_block_order(jax.random.fold_in(streams_of[12], 71), 0)
    routes_keys = jax.random.split(jax.random.fold_in(streams_of[4], 1), LAYERS * PACKS * PACK_LEN // TOK_DEV)
    routes_turns = jax.random.permutation(jax.random.fold_in(streams_of[4], 3), LAYERS * PACKS * PACK_LEN // TOK_DEV)
    routes = jax.vmap(lambda own, number: shared_out(jax.random.fold_in(streams_of[4], 2), own, number, TOK_DEV, NE, 2, MOST, 1))(routes_keys, routes_turns).reshape((LAYERS, PACKS, PACK_LEN, 2))
    gains = jnp.clip(1.0 + 0.1 * jax.random.normal(streams_of[5], (LAYERS, 2, D), jnp.float32), 0.5, 1.5).astype(jnp.bfloat16)
    qkv_weights = centred(streams_of[6], (LAYERS, 3, D, D), D ** -0.5, 0.21875, ((2, 4),))
    out_weight = centred(streams_of[7], (LAYERS, D, D), (max(D // 192, 1)) ** -0.5, 3.0, ((1, 4),))
    router = centred(streams_of[8], (LAYERS, D, RC), (3 * D) ** -0.5, 0.125, ((1, 4),))
    const_values = centred(streams_of[9], (LAYERS, NC, D), 1.0, 6.0, ((2, 4),))
    w_gate_up = centred(streams_of[10], (LAYERS, NF, 2, D, FF), D ** -0.5, 0.21875, ((4, 4),))
    w_down = centred(streams_of[11], (LAYERS, NF, FF, D), FF ** -0.5, 0.125, ((2, 4),))
    return {"tokens": tokens, "cotangent": cotangent, "seq_lengths": seq_lengths, "block_order": block_order, "routes": routes, "gains": gains, "qkv_weights": qkv_weights, "out_weight": out_weight, "router": router, "const_values": const_values, "w_gate_up": w_gate_up, "w_down": w_down}


@jax.custom_vjp
def low(v):
    return lax.optimization_barrier(v.astype(jnp.bfloat16)).astype(jnp.float32)

@jax.custom_vjp
def low_back(v):
    return v

def low_keep(v):
    return (low(v), None)

def low_pass(kept, grad):
    return (grad,)

def back_keep(v):
    return (v, None)

def back_low(kept, grad):
    return (low(grad),)
low.defvjp(low_keep, low_pass)
low_back.defvjp(back_keep, back_low)
highest = lax.Precision.HIGHEST

def layout_tables(lengths, order_row):
    pack_rows = jnp.arange(PACK_LEN, dtype=jnp.int32)
    owner = pack_rows // TOK_DEV
    which_half = pack_rows % TOK_DEV // BLK
    block_ids = order_row[2 * owner + which_half]
    pack_pos = block_ids * BLK + pack_rows % BLK
    segment = (pack_pos >= lengths[0]).astype(jnp.int32)
    seq_pos = pack_pos - segment * lengths[0]
    return (pack_pos, segment, seq_pos)

def rms_norm(values, gain):
    return values * lax.rsqrt(lax.optimization_barrier(jnp.mean(values * values, axis=-1, keepdims=True)) + 1e-06) * gain

def rotate_pairs(values, seq_pos):
    half_size = values.shape[-1] // 2
    frequency = jnp.exp(-jnp.log(10000.0) * jnp.arange(half_size, dtype=jnp.float32) / half_size)
    angles = seq_pos.astype(jnp.float32)[:, None] * frequency[None, :]
    cosine_table = jnp.cos(angles)[:, None, :]
    sine_table = jnp.sin(angles)[:, None, :]
    first_half = values[..., :half_size]
    second_half = values[..., half_size:]
    return jnp.concatenate([first_half * cosine_table - second_half * sine_table, second_half * cosine_table + first_half * sine_table], axis=-1)

def attention(queries, keys, values, pack_pos, segment):
    count = queries.shape[0]
    block_rows = 512 if count % 512 == 0 else count
    blocks = count // block_rows
    score_scale = HEAD_DIM ** (-0.5)

    def block_fn(members):
        query_block, block_pos, block_seg = members
        scores = jnp.einsum('qhd,khd->hqk', query_block, keys, precision=highest) * score_scale
        scores = low_back(scores)
        allowed = (block_seg[:, None] == segment[None, :]) & (pack_pos[None, :] <= block_pos[:, None])
        scores = jnp.where(allowed[None], scores, -1e+30)
        weights = low(jax.nn.softmax(scores, axis=-1))
        return jnp.einsum('hqk,khd->qhd', weights, values, precision=highest)
    outputs = lax.map(jax.checkpoint(block_fn), (queries.reshape(blocks, block_rows, HEADS, HEAD_DIM), pack_pos.reshape(blocks, block_rows), segment.reshape(blocks, block_rows)))
    return outputs.reshape(count, HEADS * HEAD_DIM)

def expert_groups(route_ids):
    hit_count = lax.optimization_barrier(jnp.sum((route_ids[:, :, None] == jnp.arange(NE, dtype=jnp.int32)[None, None, :]).astype(jnp.int32), axis=1))
    blocked = hit_count.reshape(N_CTX, TOK_DEV, NE)
    slot_index = jnp.cumsum(blocked, axis=1) - 1
    owners = jnp.arange(N_CTX, dtype=jnp.int32)[:, None]
    local_rows = jnp.broadcast_to(jnp.arange(TOK_DEV, dtype=jnp.int32)[None, :], (N_CTX, TOK_DEV))
    slot_table = jnp.zeros((N_CTX, NF, MOST), jnp.int32)
    for expert in range(NF):
        target = jnp.where(blocked[:, :, expert] > 0, slot_index[:, :, expert], MOST)
        slot_table = slot_table.at[owners, expert, target].set(local_rows, mode='drop')
    group_rows = owners[:, :, None] * TOK_DEV + slot_table
    token_slots = (owners[:, :, None] * (NF * MOST) + jnp.arange(NF, dtype=jnp.int32)[None, None, :] * MOST + jnp.clip(slot_index[:, :, :NF], 0, MOST - 1)).reshape(N_CTX * TOK_DEV, NF)
    return (group_rows, token_slots)

def layer_forward(stream, previous, params, route_ids, tables):
    gain, qkv, out_proj, router_w, const_vals, gate_up, down = params
    pack_pos, segment, seq_pos = tables
    count = stream.shape[0]
    head_shape = (count, HEADS, HEAD_DIM)
    normed = low(rms_norm(stream, gain[0]))
    queries = low(rotate_pairs(low_back(jnp.dot(normed, qkv[0], precision=highest)).reshape(head_shape), seq_pos))
    keys = low(rotate_pairs(low_back(jnp.dot(normed, qkv[1], precision=highest)).reshape(head_shape), seq_pos))
    values = low(low_back(jnp.dot(normed, qkv[2], precision=highest))).reshape(head_shape)
    mixed = low(low_back(attention(queries, keys, values, pack_pos, segment)))
    hidden_state = stream + low_back(jnp.dot(mixed, out_proj, precision=highest))
    expert_in = rms_norm(hidden_state, gain[1])
    expert_low = low(expert_in)
    raw_logits = low_back(jnp.dot(expert_low, router_w, precision=highest))
    logits = raw_logits[:, :NE] + previous
    chosen = (route_ids[:, :, None] == jnp.arange(NE, dtype=jnp.int32)[None, None, :]).astype(jnp.float32)
    picked = lax.optimization_barrier(jnp.sum(chosen * logits[:, None, :], axis=-1))
    gate_weights = jax.nn.softmax(picked, axis=-1)
    coeffs = lax.optimization_barrier(jnp.sum(gate_weights[:, :, None] * chosen, axis=1))
    group_rows, token_slots = expert_groups(route_ids)
    inputs = expert_low[group_rows]
    gate_up_out = low_back(jnp.einsum('nemd,ecdf->necmf', inputs, gate_up, precision=highest))
    hidden_low = low(jax.nn.silu(gate_up_out[:, :, 0]) * gate_up_out[:, :, 1])
    result = low_back(jnp.einsum('nemf,efd->nemd', hidden_low, down, precision=highest))
    token_result = result.reshape(-1, D)[token_slots]
    expert_mix = lax.optimization_barrier(jnp.sum(coeffs[:, :NF, None] * token_result, axis=1)) + coeffs[:, NF + 1:NF + 2] * expert_in
    for const_index in range(NC):
        column = NE + 2 * const_index
        mixing = jax.nn.softmax(raw_logits[:, column:column + 2], axis=-1)
        expert_mix = expert_mix + coeffs[:, NF + 2 + const_index:NF + 3 + const_index] * (mixing[:, 0:1] * expert_in + mixing[:, 1:2] * const_vals[const_index][None, :])
    return (hidden_state + expert_mix, logits)

def forward(stream, gains_f, qkv_f, out_f, router_f, const_f, gate_up_f, down_f, route_pack, tables):
    previous = jnp.zeros((stream.shape[0], NE), jnp.float32)
    for layer_index in range(LAYERS):
        params = (gains_f[layer_index], qkv_f[layer_index], out_f[layer_index], router_f[layer_index], const_f[layer_index], gate_up_f[layer_index], down_f[layer_index])
        stream, previous = layer_forward(stream, previous, params, route_pack[layer_index], tables)
    return stream

def reference(tokens, cotangent, seq_lengths, block_order, routes, gains, qkv_weights, out_weight, router, const_values, w_gate_up, w_down):
    weights = tuple((member.astype(jnp.float32) for member in (gains, qkv_weights, out_weight, router, const_values, w_gate_up, w_down)))

    def one_pack(totals, members):
        stream, upstream, lengths, order_row, route_pack = members
        tables = layout_tables(lengths, order_row)

        def apply_layers(stream_in, *params):
            return forward(stream_in, *params, route_pack, tables)
        result, pullback = jax.vjp(apply_layers, stream.astype(jnp.float32), *weights)
        grads = pullback(upstream.astype(jnp.float32))
        totals = tuple((earlier + added for earlier, added in zip(totals, grads[1:])))
        return (totals, (result, grads[0]))
    starting = tuple((jnp.zeros(member.shape, jnp.float32) for member in weights))
    totals, (outputs, input_grads) = lax.scan(one_pack, starting, (tokens, cotangent, seq_lengths, block_order, jnp.moveaxis(routes, 1, 0)))
    return (outputs, input_grads, totals[0], totals[1], totals[2], totals[3], totals[4], totals[5], totals[6])
```

```python
import jax
import jax.numpy as jnp
import numpy as np
from jax import lax
from jax.experimental import pallas as pl
from jax.experimental.pallas import tpu as pltpu
from jax.sharding import PartitionSpec as P

HEADS = 12
HEAD_DIM = 64
NF = 8
NC = 2
LAYERS = 2
NE = 12
MOST = 64
GROUP_HEADS = 3


def from_behind(x, axis, by):
    devices = lax.axis_size(axis)
    return lax.ppermute(x, axis, [(i, (i + by) % devices) for i in range(devices)])


def layout_tables(lengths, order_row, tok_count):
    block_len = tok_count // 2
    pack_len = order_row.shape[0] * block_len
    pack_rows = jnp.arange(pack_len, dtype=jnp.int32)
    owner = pack_rows // tok_count
    which_half = pack_rows % tok_count // block_len
    block_ids = order_row[2 * owner + which_half]
    pack_pos = block_ids * block_len + pack_rows % block_len
    segment = (pack_pos >= lengths[0]).astype(jnp.int32)
    seq_pos = pack_pos - segment * lengths[0]
    return (pack_pos, segment, seq_pos)


def angle_tables(seq_pos, head_size):
    half_size = head_size // 2
    frequency = jnp.exp(-jnp.log(10000.0) * jnp.arange(half_size, dtype=jnp.float32) / half_size)
    angles = seq_pos.astype(jnp.float32)[:, None] * frequency[None, :]
    return (jnp.cos(angles)[:, None, :], jnp.sin(angles)[:, None, :])


def rotate_pairs(values, cosine_table, sine_table, direction):
    half_size = values.shape[-1] // 2
    first_half = values[..., :half_size]
    second_half = values[..., half_size:]
    return jnp.concatenate(
        [
            first_half * cosine_table - direction * second_half * sine_table,
            second_half * cosine_table + direction * first_half * sine_table,
        ],
        axis=-1,
    )


def rms_parts(values):
    inverse = lax.rsqrt(jnp.mean(values * values, axis=-1, keepdims=True) + 1e-06)
    return (values * inverse, inverse)


def rms_back(grad_normed, base_values, inverse):
    return inverse * (
        grad_normed - base_values * jnp.mean(grad_normed * base_values, axis=-1, keepdims=True)
    )


def expert_forward(inputs_low, gate_up_use, down_use):
    gate_up_out = jnp.einsum(
        "emd,ecdf->ecmf", inputs_low, gate_up_use, preferred_element_type=jnp.float32
    )
    hidden_low = (jax.nn.silu(gate_up_out[:, 0]) * gate_up_out[:, 1]).astype(jnp.bfloat16)
    partial_value = jnp.einsum(
        "emf,efd->emd", hidden_low, down_use, preferred_element_type=jnp.float32
    )
    return (gate_up_out, hidden_low, partial_value)


def expert_backward(inputs_low, gate_up_out, hidden_low, grad_part_low, gate_up_use, down_use):
    grad_down = jnp.einsum(
        "emf,emd->efd", hidden_low, grad_part_low, preferred_element_type=jnp.float32
    )
    grad_hidden = jnp.einsum(
        "emd,efd->emf", grad_part_low, down_use, preferred_element_type=jnp.float32
    )
    gate_out = gate_up_out[:, 0]
    sigmoid_gate = jax.nn.sigmoid(gate_out)
    grad_pair_low = jnp.stack(
        [
            grad_hidden
            * gate_up_out[:, 1]
            * sigmoid_gate
            * (1.0 + gate_out * (1.0 - sigmoid_gate)),
            grad_hidden * gate_out * sigmoid_gate,
        ],
        axis=1,
    ).astype(jnp.bfloat16)
    grad_gate_up = jnp.einsum(
        "emd,ecmf->ecdf", inputs_low, grad_pair_low, preferred_element_type=jnp.float32
    )
    grad_rows = jnp.einsum(
        "ecmf,ecdf->emd", grad_pair_low, gate_up_use, preferred_element_type=jnp.float32
    )
    return (grad_gate_up, grad_down, grad_rows)


def shards(
    tokens,
    cotangent,
    seq_lengths,
    block_order,
    routes,
    gains,
    qkv_weights,
    out_weight,
    router,
    const_values,
    w_gate_up,
    w_down,
):
    tok_count = tokens.shape[1]
    width = tokens.shape[2]
    ctx_size = lax.axis_size("ctx")
    own_index = lax.axis_index("ctx")
    score_scale = HEAD_DIM ** (-0.5)
    pack_pos, segment, seq_pos = layout_tables(seq_lengths[0], block_order[0], tok_count)
    own_start = own_index * tok_count
    query_pos = lax.dynamic_slice_in_dim(pack_pos, own_start, tok_count)
    query_seg = lax.dynamic_slice_in_dim(segment, own_start, tok_count)
    cosine_table, sine_table = angle_tables(
        lax.dynamic_slice_in_dim(seq_pos, own_start, tok_count), HEAD_DIM
    )
    head_shape = (tok_count, HEADS, HEAD_DIM)
    expert_ids = jnp.arange(NE, dtype=jnp.int32)
    slot_ids = jnp.arange(MOST, dtype=jnp.int32)
    row_ids = jnp.arange(tok_count, dtype=jnp.int32)

    def allowed_pairs(key_offset, key_count):
        key_pos = lax.dynamic_slice_in_dim(pack_pos, key_offset, key_count)
        key_seg = lax.dynamic_slice_in_dim(segment, key_offset, key_count)
        return (query_seg[:, None] == key_seg[None, :]) & (key_pos[None, :] <= query_pos[:, None])

    stream = tokens[0].astype(jnp.float32)
    previous = jnp.zeros((tok_count, NE), jnp.float32)
    saved = []
    for layer_index in range(LAYERS):
        gain_all, qkv_all, out_all, router_all, const_all = (
            lax.all_gather(gains[layer_index], "fsdp", axis=1, tiled=True),
            lax.all_gather(qkv_weights[layer_index], "fsdp", axis=1, tiled=True),
            lax.all_gather(out_weight[layer_index], "fsdp", axis=0, tiled=True),
            lax.all_gather(router[layer_index], "fsdp", axis=0, tiled=True),
            lax.all_gather(const_values[layer_index], "fsdp", axis=1, tiled=True),
        )
        gain_float = gain_all.astype(jnp.float32)
        base_one, inverse_one = rms_parts(stream)
        normed_low = (base_one * gain_float[0]).astype(jnp.bfloat16)
        projected = jnp.einsum(
            "td,cde->cte", normed_low, qkv_all, preferred_element_type=jnp.float32
        )
        queries_low = rotate_pairs(
            projected[0].reshape(head_shape), cosine_table, sine_table, 1.0
        ).astype(jnp.bfloat16)
        keys_low = rotate_pairs(
            projected[1].reshape(head_shape), cosine_table, sine_table, 1.0
        ).astype(jnp.bfloat16)
        values_low = projected[2].reshape(head_shape).astype(jnp.bfloat16)

        def fold_step(running, shard_piece, offset, queries_use=queries_low):
            keys_piece, values_piece = shard_piece
            allowed = allowed_pairs(offset, keys_piece.shape[0])[None]
            scores = (
                jnp.einsum(
                    "qhd,khd->hqk", queries_use, keys_piece, preferred_element_type=jnp.float32
                )
                * score_scale
            )
            scores = jnp.where(allowed, scores, -1e30)
            top_old, total_old, accumulated = running
            top_new = jnp.maximum(top_old, jnp.max(scores, axis=-1))
            weights = jnp.where(allowed, jnp.exp(scores - top_new[..., None]), 0.0)
            factor = jnp.exp(top_old - top_new)
            accumulated = jnp.einsum(
                "hqk,khd->hqd",
                weights.astype(jnp.bfloat16),
                values_piece,
                preferred_element_type=jnp.float32,
            )
            return (top_new, jnp.sum(weights, axis=-1), accumulated)

        starting = (
            jnp.full((HEADS, tok_count), -1e30, jnp.float32),
            jnp.zeros((HEADS, tok_count), jnp.float32),
            jnp.zeros((HEADS, tok_count, HEAD_DIM), jnp.float32),
        )
        top_value, total_sum, accumulated = fold_step(
            starting,
            (
                lax.all_gather(keys_low, "ctx", axis=0, tiled=True),
                lax.all_gather(values_low, "ctx", axis=0, tiled=True),
            ),
            jnp.int32(0),
        )
        log_total = top_value + jnp.log(total_sum)
        attended = jnp.transpose(accumulated / total_sum[..., None], (1, 0, 2))
        mixed_low = attended.reshape(tok_count, width).astype(jnp.bfloat16)
        hidden_state = stream + jnp.dot(mixed_low, out_all, preferred_element_type=jnp.float32)
        base_two, inverse_two = rms_parts(hidden_state)
        expert_in = base_two * gain_float[1]
        expert_low = expert_in.astype(jnp.bfloat16)
        raw_logits = jnp.dot(expert_low, router_all, preferred_element_type=jnp.float32)
        logits = raw_logits[:, :NE] + previous
        route_ids = routes[layer_index, 0]
        chosen = route_ids[:, :, None] == expert_ids[None, None, :]
        chosen_f = chosen.astype(jnp.float32)
        hit_count = jnp.sum(chosen.astype(jnp.int32), axis=1)
        slot_index = jnp.cumsum(hit_count, axis=0) - 1
        picked = jnp.sum(chosen_f * logits[:, None, :], axis=-1)
        gate_weights = jax.nn.softmax(picked, axis=-1)
        coeffs = jnp.sum(gate_weights[:, :, None] * chosen_f, axis=1)
        slot_table = jnp.zeros((NF, MOST), jnp.int32)
        for expert in range(NF):
            target = jnp.where(hit_count[:, expert] > 0, slot_index[:, expert], MOST)
            slot_table = slot_table.at[expert, target].set(row_ids, mode="drop")
        filled = (slot_ids[None, :] < jnp.sum(hit_count[:, :NF], axis=0)[:, None]).astype(
            jnp.float32
        )
        rows_low = expert_low[slot_table]
        inputs_low = lax.all_gather(rows_low, "fsdp", axis=1, tiled=True)
        gate_up_out, hidden_low, partial_value = expert_forward(
            inputs_low, w_gate_up[layer_index], w_down[layer_index]
        )
        result = lax.psum_scatter(
            partial_value.astype(jnp.bfloat16), "fsdp", scatter_dimension=1, tiled=True
        ).astype(jnp.float32)
        flat_index = jnp.arange(NF, dtype=jnp.int32)[None, :] * MOST + jnp.clip(
            slot_index[:, :NF], 0, MOST - 1
        )
        token_result = result.reshape(NF * MOST, width)[flat_index]
        expert_mix = (
            jnp.sum(coeffs[:, :NF, None] * token_result, axis=1)
            + coeffs[:, NF + 1 : NF + 2] * expert_in
        )
        mixings = []
        for const_index in range(NC):
            column = NE + 2 * const_index
            mixing = jax.nn.softmax(raw_logits[:, column : column + 2], axis=-1)
            mixings.append(mixing)
            expert_mix = expert_mix + coeffs[:, NF + 2 + const_index : NF + 3 + const_index] * (
                mixing[:, 0:1] * expert_in
                + mixing[:, 1:2] * const_all[const_index].astype(jnp.float32)[None, :]
            )
        saved.append(
            (
                gain_float,
                qkv_all,
                out_all,
                router_all,
                const_all,
                base_one,
                inverse_one,
                normed_low,
                queries_low,
                keys_low,
                values_low,
                log_total,
                attended,
                mixed_low,
                base_two,
                inverse_two,
                expert_in,
                expert_low,
                chosen_f,
                hit_count,
                gate_weights,
                coeffs,
                slot_table,
                filled,
                inputs_low,
                gate_up_out,
                hidden_low,
                flat_index,
                token_result,
                mixings,
            )
        )
        stream = hidden_state + expert_mix
        previous = logits
    grad_stream = cotangent[0].astype(jnp.float32)
    grad_previous = jnp.zeros((tok_count, NE), jnp.float32)
    layer_grads = [None] * LAYERS
    for layer_index in reversed(range(LAYERS)):
        (
            gain_float,
            qkv_all,
            out_all,
            router_all,
            const_all,
            base_one,
            inverse_one,
            normed_low,
            queries_low,
            keys_low,
            values_low,
            log_total,
            attended,
            mixed_low,
            base_two,
            inverse_two,
            expert_in,
            expert_low,
            chosen_f,
            hit_count,
            gate_weights,
            coeffs,
            slot_table,
            filled,
            inputs_low,
            gate_up_out,
            hidden_low,
            flat_index,
            token_result,
            mixings,
        ) = saved[layer_index]
        grad_mix = grad_stream
        dot_input = jnp.sum(grad_mix * expert_in, axis=-1, keepdims=True)
        coef_grads = [
            jnp.sum(grad_mix[:, None, :] * token_result, axis=-1),
            jnp.zeros((tok_count, 1), jnp.float32),
            dot_input,
        ]
        grad_in = grad_mix * coeffs[:, NF + 1 : NF + 2]
        const_cols = []
        const_grads = []
        for const_index in range(NC):
            mixing = mixings[const_index]
            const_row = const_all[const_index].astype(jnp.float32)[None, :]
            dot_const = jnp.sum(grad_mix * const_row, axis=-1, keepdims=True)
            share = coeffs[:, NF + 2 + const_index : NF + 3 + const_index]
            coef_grads.append(mixing[:, 0:1] * dot_input + mixing[:, 1:2] * dot_const)
            grad_in = grad_in + grad_mix * (share * mixing[:, 0:1])
            grad_mixing = share * jnp.concatenate([dot_input, dot_const], axis=1)
            const_cols.append(
                mixing * (grad_mixing - jnp.sum(mixing * grad_mixing, axis=-1, keepdims=True))
            )
            const_grads.append(jnp.sum(grad_mix * (share * mixing[:, 1:2]), axis=0))
        grad_coeffs = jnp.concatenate(coef_grads, axis=1)
        grad_gates = jnp.sum(chosen_f * grad_coeffs[:, None, :], axis=-1)
        grad_picked = gate_weights * (
            grad_gates - jnp.sum(gate_weights * grad_gates, axis=-1, keepdims=True)
        )
        grad_logits = jnp.sum(grad_picked[:, :, None] * chosen_f, axis=1) + grad_previous
        grad_previous = grad_logits
        grad_raw_low = jnp.concatenate([grad_logits] + const_cols, axis=1).astype(jnp.bfloat16)
        grad_router = jnp.einsum(
            "td,tc->dc", expert_low, grad_raw_low, preferred_element_type=jnp.float32
        )
        grad_in = grad_in + jnp.einsum(
            "tc,dc->td", grad_raw_low, router_all, preferred_element_type=jnp.float32
        )
        slot_weight = (
            jnp.take_along_axis(jnp.transpose(coeffs[:, :NF]), slot_table, axis=1) * filled
        )
        grad_result_low = (grad_mix[slot_table] * slot_weight[:, :, None]).astype(jnp.bfloat16)
        grad_part_low = lax.all_gather(grad_result_low, "fsdp", axis=1, tiled=True)
        grad_gate_up, grad_down, grad_rows = expert_backward(
            inputs_low,
            gate_up_out,
            hidden_low,
            grad_part_low,
            w_gate_up[layer_index],
            w_down[layer_index],
        )
        grad_rows = lax.psum_scatter(
            grad_rows.astype(jnp.bfloat16), "fsdp", scatter_dimension=1, tiled=True
        ).astype(jnp.float32)
        token_grads = grad_rows.reshape(NF * MOST, width)[flat_index]
        grad_in = grad_in + jnp.sum(
            jnp.where(hit_count[:, :NF, None] > 0, token_grads, 0.0), axis=1
        )
        grad_gain_two = jnp.sum(grad_in * base_two, axis=0)
        grad_hidden_state = grad_stream + rms_back(grad_in * gain_float[1], base_two, inverse_two)
        grad_out_low = grad_hidden_state.astype(jnp.bfloat16)
        grad_out_w = jnp.einsum(
            "td,te->de", mixed_low, grad_out_low, preferred_element_type=jnp.float32
        )
        grad_attended = (
            jnp.einsum("te,de->td", grad_out_low, out_all, preferred_element_type=jnp.float32)
            .astype(jnp.bfloat16)
            .reshape(head_shape)
        )
        delta = jnp.transpose(jnp.sum(grad_attended.astype(jnp.float32) * attended, axis=-1))

        def visit(
            turn_index,
            carried,
            queries_use=queries_low,
            grad_use=grad_attended,
            log_use=log_total,
            delta_use=delta,
        ):
            keys_piece, values_piece, key_grads, value_grads, query_grads = carried
            source = (own_index - turn_index) % ctx_size
            allowed = allowed_pairs(source * tok_count, tok_count)[None]
            scores = (
                jnp.einsum(
                    "qhd,khd->hqk", queries_use, keys_piece, preferred_element_type=jnp.float32
                )
                * score_scale
            )
            probs = jnp.where(
                allowed, jnp.exp(jnp.where(allowed, scores, -1e30) - log_use[..., None]), 0.0
            )
            value_grads = value_grads + jnp.einsum(
                "hqk,qhd->khd",
                probs.astype(jnp.bfloat16),
                grad_use,
                preferred_element_type=jnp.float32,
            )
            prob_grads = jnp.einsum(
                "qhd,khd->hqk", grad_use, values_piece, preferred_element_type=jnp.float32
            )
            score_grads = (probs * (prob_grads - delta_use[..., None])).astype(jnp.bfloat16)
            query_grads = query_grads + jnp.einsum(
                "hqk,khd->qhd", score_grads, keys_piece, preferred_element_type=jnp.float32
            )
            key_grads = key_grads + jnp.einsum(
                "hqk,qhd->khd", score_grads, queries_use, preferred_element_type=jnp.float32
            )
            keys_piece, values_piece = from_behind((keys_piece, values_piece), "ctx", 1)
            key_grads, value_grads = (
                from_behind(key_grads.astype(jnp.bfloat16), "ctx", 1).astype(key_grads.dtype),
                from_behind(value_grads.astype(jnp.bfloat16), "ctx", 1).astype(value_grads.dtype),
            )
            return (keys_piece, values_piece, key_grads, value_grads, query_grads)

        zero_heads = jnp.zeros(head_shape, jnp.float32)
        finished = lax.fori_loop(
            0, ctx_size, visit, (keys_low, values_low, zero_heads, zero_heads, zero_heads)
        )
        grad_query = (
            rotate_pairs(finished[4] * score_scale, cosine_table, sine_table, -1.0)
            .astype(jnp.bfloat16)
            .reshape(tok_count, width)
        )
        grad_key = (
            rotate_pairs(finished[2] * score_scale, cosine_table, sine_table, -1.0)
            .astype(jnp.bfloat16)
            .reshape(tok_count, width)
        )
        grad_value = finished[3].astype(jnp.bfloat16).reshape(tok_count, width)
        grad_proj_low = jnp.stack([grad_query, grad_key, grad_value], axis=0)
        grad_qkv = jnp.einsum(
            "td,cte->cde", normed_low, grad_proj_low, preferred_element_type=jnp.float32
        )
        grad_normed = jnp.einsum(
            "cte,cde->td", grad_proj_low, qkv_all, preferred_element_type=jnp.float32
        )
        grad_gain_one = jnp.sum(grad_normed * base_one, axis=0)
        grad_stream = grad_hidden_state + rms_back(
            grad_normed * gain_float[0], base_one, inverse_one
        )
        gains_shard, qkv_shard, out_shard, router_shard, const_shard = (
            lax.psum_scatter(
                jnp.stack([grad_gain_one, grad_gain_two]).astype(jnp.bfloat16),
                "fsdp",
                scatter_dimension=1,
                tiled=True,
            ).astype(jnp.float32),
            lax.psum_scatter(
                grad_qkv.astype(jnp.bfloat16), "fsdp", scatter_dimension=1, tiled=True
            ).astype(jnp.float32),
            lax.psum_scatter(
                grad_out_w.astype(jnp.bfloat16), "fsdp", scatter_dimension=0, tiled=True
            ).astype(jnp.float32),
            lax.psum_scatter(
                grad_router.astype(jnp.bfloat16), "fsdp", scatter_dimension=0, tiled=True
            ).astype(jnp.float32),
            lax.psum_scatter(
                jnp.stack(const_grads).astype(jnp.bfloat16), "fsdp", scatter_dimension=1, tiled=True
            ).astype(jnp.float32),
        )
        layer_grads[layer_index] = (
            lax.psum(gains_shard.astype(jnp.bfloat16), "ctx").astype(jnp.float32),
            lax.psum(qkv_shard.astype(jnp.bfloat16), "ctx").astype(jnp.float32),
            lax.psum(out_shard.astype(jnp.bfloat16), "ctx").astype(jnp.float32),
            lax.psum(router_shard.astype(jnp.bfloat16), "ctx").astype(jnp.float32),
            lax.psum(const_shard.astype(jnp.bfloat16), "ctx").astype(jnp.float32),
            lax.psum(grad_gate_up.astype(jnp.bfloat16), "ctx").astype(jnp.float32),
            lax.psum(grad_down.astype(jnp.bfloat16), "ctx").astype(jnp.float32),
        )
    stacked = [
        jnp.stack([layer_grads[layer_index][member_index] for layer_index in range(LAYERS)])
        for member_index in range(7)
    ]
    return (
        stream[None],
        grad_stream[None],
        stacked[0],
        stacked[1],
        stacked[2],
        stacked[3],
        stacked[4],
        stacked[5],
        stacked[6],
    )


MINLEN = 1024
ROUT = 56
RAW, COEF, SLOT, LOGI = 0, 16, 32, 40
VMEM_MB = 60


def nt(a, b):
    return lax.dot_general(a, b, (((1,), (1,)), ((), ())), preferred_element_type=jnp.float32)


def nn(a, b):
    return lax.dot_general(a, b, (((1,), (0,)), ((), ())), preferred_element_type=jnp.float32)


def tn(a, b):
    return lax.dot_general(a, b, (((0,), (0,)), ((), ())), preferred_element_type=jnp.float32)


def params_of(mb=VMEM_MB, **more):
    return pltpu.CompilerParams(vmem_limit_bytes=mb * 2**20, **more)


def block_call(fn, outs, args, name):
    def kernel(*refs):
        results = fn(*[ref[...] for ref in refs[: len(args)]])
        for ref, value in zip(refs[len(args) :], results):
            ref[...] = value

    return pl.pallas_call(
        kernel,
        out_shape=outs,
        in_specs=[pl.BlockSpec(memory_space=pltpu.VMEM)] * len(args),
        out_specs=[pl.BlockSpec(memory_space=pltpu.VMEM)] * len(outs),
        compiler_params=params_of(),
        name=name,
    )(*args)


def shape_of(dims, kind):
    return jax.ShapeDtypeStruct(dims, kind)


def rms_factor(values):
    return lax.rsqrt(jnp.mean(values * values, axis=-1, keepdims=True) + 1e-06)


def to_rows(columns, count):
    lane = lax.broadcasted_iota(jnp.int32, (columns[0].shape[0], 128), 1)
    packed = jnp.zeros(lane.shape, jnp.float32)
    for index, column in enumerate(columns):
        packed = jnp.where(lane == index, column, packed)
    return jnp.transpose(packed)[:count]


def to_columns(rows):
    count = rows[0].shape[1]
    sub = lax.broadcasted_iota(jnp.int32, (128, count), 0)
    packed = jnp.zeros(sub.shape, jnp.float32)
    for index, row in enumerate(rows):
        packed = jnp.where(sub == index, row, packed)
    packed = jnp.transpose(packed)
    return [packed[:, index : index + 1] for index in range(len(rows))]


def swap_halves(values):
    lanes = values.shape[1]
    lane = lax.broadcasted_iota(jnp.int32, values.shape, 1)
    ahead = pltpu.roll(values, lanes - 32, 1)
    behind = pltpu.roll(values, 32, 1)
    return jnp.where(lane % 64 < 32, ahead, behind)


def spin(values, cosine, sine):
    return values * cosine + swap_halves(values) * sine


def attn_fwd_kernel(inv, n1, w, cosine, sine, qkv, o, lse, ob, rows):
    blocks, blk, _ = n1.shape
    lanes = o.shape[1]
    seq = blocks * blk
    step = 2 * blk
    for b in range(blocks):
        rows[b * blk : (b + 1) * blk, :] = n1[inv[b]]
    for i in range(seq // step):
        part = slice(i * step, (i + 1) * step)
        y = nn(rows[part, :], w[...])
        cos2 = jnp.concatenate([cosine[part, :]] * (lanes // 128), axis=1)
        sin2 = jnp.concatenate([sine[part, :]] * (lanes // 128), axis=1)
        q = spin(y[:, :lanes], cos2, sin2).astype(jnp.bfloat16)
        qkv[part, :lanes] = q * jnp.asarray(HEAD_DIM**-0.5, jnp.bfloat16)
        qkv[part, lanes : 2 * lanes] = spin(y[:, lanes : 2 * lanes], cos2, sin2).astype(jnp.bfloat16)
        qkv[part, 2 * lanes :] = y[:, 2 * lanes :].astype(jnp.bfloat16)
    lane = lax.broadcasted_iota(jnp.int32, (step, 128), 1)
    for i in range(seq // step):
        part = slice(i * step, (i + 1) * step)
        span = (i + 1) * step
        seen = lax.broadcasted_iota(jnp.int32, (step, span), 1) <= (
            lax.broadcasted_iota(jnp.int32, (step, span), 0) + i * step
        )
        logs = jnp.zeros((step, 128), jnp.float32)
        for head in range(GROUP_HEADS):
            tile, side = head // 2, head % 2
            at = tile * 128
            mine = lane // 64 == side
            q = jnp.where(mine, qkv[part, at : at + 128], jnp.asarray(0, jnp.bfloat16))
            s = nt(q, qkv[:span, lanes + at : lanes + at + 128])
            s = jnp.where(seen, s, -1e30)
            top = jnp.max(s, axis=1, keepdims=True)
            p = jnp.exp(s - top)
            total = jnp.sum(p, axis=1, keepdims=True)
            out = nn(p.astype(jnp.bfloat16), qkv[:span, 2 * lanes + at : 2 * lanes + at + 128]) / total
            logs = jnp.where(lane == head, top + jnp.log(total), logs)
            if side == 0:
                kept = jnp.where(mine, out, 0.0)
            else:
                kept = jnp.where(mine, out, kept)
            o[part, at : at + 128] = kept
        lse[part, :] = logs
    for b in range(blocks):
        ob[inv[b]] = o[b * blk : (b + 1) * blk, :].astype(jnp.bfloat16)


def attn_forward(inv, n1, w, cosine, sine):
    blocks, blk, width = n1.shape
    lanes = w.shape[1] // 3
    seq = blocks * blk
    vm = pl.BlockSpec(memory_space=pltpu.VMEM)
    return pl.pallas_call(
        attn_fwd_kernel,
        out_shape=[
            shape_of((seq, 3 * lanes), jnp.bfloat16),
            shape_of((seq, lanes), jnp.float32),
            shape_of((seq, 128), jnp.float32),
            shape_of((blocks, blk, lanes), jnp.bfloat16),
        ],
        in_specs=[pl.BlockSpec(memory_space=pltpu.SMEM)] + [vm] * 4,
        out_specs=[vm] * 4,
        scratch_shapes=[pltpu.VMEM((seq, width), jnp.bfloat16)],
        compiler_params=params_of(),
        name="attn_fwd",
    )(inv, n1, w, cosine, sine)


def attn_bwd_kernel(inv, n1, w, cosine, sine, qkv, o, lse, go, gn, gw, rows, gos, grads, acc):
    blocks, blk, width = n1.shape
    lanes = o.shape[1]
    seq = blocks * blk
    step = 2 * blk
    zero = jnp.asarray(0, jnp.bfloat16)
    for b in range(blocks):
        rows[b * blk : (b + 1) * blk, :] = n1[inv[b]]
        gos[b * blk : (b + 1) * blk, :] = go[inv[b]]
    acc[...] = jnp.zeros_like(acc)
    lane = lax.broadcasted_iota(jnp.int32, (step, 128), 1)
    for i in range(seq // step):
        part = slice(i * step, (i + 1) * step)
        span = (i + 1) * step
        seen = lax.broadcasted_iota(jnp.int32, (step, span), 1) <= (
            lax.broadcasted_iota(jnp.int32, (step, span), 0) + i * step
        )
        key_lane = lax.broadcasted_iota(jnp.int32, (span, 128), 1)
        for head in range(GROUP_HEADS):
            tile, side = head // 2, head % 2
            at = tile * 128
            mine = lane // 64 == side
            q = jnp.where(mine, qkv[part, at : at + 128], zero)
            g = jnp.where(mine, gos[part, at : at + 128], zero)
            k = qkv[:span, lanes + at : lanes + at + 128]
            v = qkv[:span, 2 * lanes + at : 2 * lanes + at + 128]
            delta = jnp.sum(g.astype(jnp.float32) * o[part, at : at + 128], axis=1, keepdims=True)
            s = nt(q, k)
            p = jnp.where(seen, jnp.exp(jnp.where(seen, s, -1e30) - lse[part, head : head + 1]), 0.0)
            ds = (p * (nt(g, v) - delta)).astype(jnp.bfloat16)
            acc[:span, 2 * lanes + at : 2 * lanes + at + 128] += tn(p.astype(jnp.bfloat16), g)
            acc[:span, lanes + at : lanes + at + 128] += tn(ds, q)
            acc[part, at : at + 128] += nn(ds, jnp.where(key_lane // 64 == side, k, zero))
    for i in range(seq // step):
        part = slice(i * step, (i + 1) * step)
        cos2 = jnp.concatenate([cosine[part, :]] * (lanes // 128), axis=1)
        sin2 = jnp.concatenate([sine[part, :]] * (lanes // 128), axis=1)
        grads[part, :lanes] = spin(acc[part, :lanes] * HEAD_DIM**-0.5, cos2, -sin2).astype(jnp.bfloat16)
        grads[part, lanes : 2 * lanes] = spin(acc[part, lanes : 2 * lanes], cos2, -sin2).astype(jnp.bfloat16)
        grads[part, 2 * lanes :] = acc[part, 2 * lanes :].astype(jnp.bfloat16)
    for b in range(blocks):
        gn[inv[b]] = nt(grads[b * blk : (b + 1) * blk, :], w[...]).astype(jnp.bfloat16)
    for i in range(width // 256):
        gw[i * 256 : (i + 1) * 256, :] = tn(rows[:, i * 256 : (i + 1) * 256], grads[...]).astype(jnp.bfloat16)


def attn_backward(inv, n1, w, cosine, sine, qkv, o, lse, go):
    blocks, blk, width = n1.shape
    lanes = w.shape[1] // 3
    seq = blocks * blk
    vm = pl.BlockSpec(memory_space=pltpu.VMEM)
    return pl.pallas_call(
        attn_bwd_kernel,
        out_shape=[
            shape_of((blocks, blk, width), jnp.bfloat16),
            shape_of((width, 3 * lanes), jnp.bfloat16),
        ],
        in_specs=[pl.BlockSpec(memory_space=pltpu.SMEM)] + [vm] * 8,
        out_specs=[vm] * 2,
        scratch_shapes=[
            pltpu.VMEM((seq, width), jnp.bfloat16),
            pltpu.VMEM((seq, lanes), jnp.bfloat16),
            pltpu.VMEM((seq, 3 * lanes), jnp.bfloat16),
            pltpu.VMEM((seq, 3 * lanes), jnp.float32),
        ],
        compiler_params=params_of(),
        name="attn_bwd",
    )(inv, n1, w, cosine, sine, qkv, o, lse, go)


def routing(raw, before, routes):
    count = raw.shape[1]
    ids = lax.broadcasted_iota(jnp.int32, (16, count), 0)
    logits = raw + before
    first, second = ids == routes[0:1], ids == routes[1:2]
    z0 = jnp.sum(jnp.where(first, logits, 0.0), axis=0, keepdims=True)
    z1 = jnp.sum(jnp.where(second, logits, 0.0), axis=0, keepdims=True)
    top = jnp.maximum(z0, z1)
    e0, e1 = jnp.exp(z0 - top), jnp.exp(z1 - top)
    total = e0 + e1
    coef = jnp.where(first, e0 / total, 0.0) + jnp.where(second, e1 / total, 0.0)
    hits = jnp.where(first | second, 1.0, 0.0)
    upto = lax.broadcasted_iota(jnp.int32, (count, count), 0) <= lax.broadcasted_iota(jnp.int32, (count, count), 1)
    place = nn(hits.astype(jnp.bfloat16), jnp.where(upto, 1.0, 0.0).astype(jnp.bfloat16)) - 1.0
    slot = jnp.where(hits > 0, place, -1.0)
    return jnp.concatenate([raw, coef, slot[:NF], logits], axis=0)


def one_hot(slot):
    count = slot.shape[1]
    ids = lax.broadcasted_iota(jnp.int32, (NF, MOST, count), 1)
    hit = ids == slot.astype(jnp.int32)[:, None, :]
    return jnp.where(hit, 1.0, 0.0).reshape(NF * MOST, count)


def slot_values(hot, rows):
    count = rows.shape[1]
    wide = jnp.broadcast_to(rows[:, None, :], (NF, MOST, count)).reshape(NF * MOST, count)
    return jnp.sum(hot * wide, axis=1, keepdims=True)


def ffn_fwd_kernel(ub, routes, before, router, wgu, wd, part, table, hot_s, x_s, y_s, coef_s):
    e = pl.program_id(0)
    packs = ub.shape[0]

    @pl.when(e == 0)
    def _():
        for d in range(packs):
            rows = routing(nt(router[...], ub[d]), before[d], routes[d])
            table[d] = rows
            hot = one_hot(rows[SLOT : SLOT + NF])
            coef_s[d] = slot_values(hot, rows[COEF : COEF + NF])
            hot_low = hot.astype(jnp.bfloat16)
            hot_s[d] = hot_low
            x = nn(hot_low, ub[d]).astype(jnp.bfloat16)
            for n in range(NF):
                x_s[n, d * MOST : (d + 1) * MOST, :] = x[n * MOST : (n + 1) * MOST]

    x = x_s[e]
    gate, up = nn(x, wgu[0, 0, 0]), nn(x, wgu[0, 0, 1])
    hid = (gate * jax.nn.sigmoid(gate) * up).astype(jnp.bfloat16)
    out = nn(hid, wd[0, 0])
    at = pl.ds(pl.multiple_of(e * MOST, MOST), MOST)
    for d in range(packs):
        y_s[d, at, :] = (out[d * MOST : (d + 1) * MOST] * coef_s[d, at, :]).astype(jnp.bfloat16)

    @pl.when(e == NF - 1)
    def _():
        for d in range(packs):
            part[d] = tn(hot_s[d], y_s[d]).astype(jnp.bfloat16)


def whole_spec(dims):
    return pl.BlockSpec(dims, lambda *_: (0,) * len(dims))


def ffn_forward(layer, ub, routes, before, router, wgu, wd):
    packs, count, width = ub.shape
    hidden = wd.shape[2]
    return pl.pallas_call(
        ffn_fwd_kernel,
        grid=(NF,),
        out_shape=[
            shape_of((packs, count, width), jnp.bfloat16),
            shape_of((packs, ROUT, count), jnp.float32),
        ],
        in_specs=[
            whole_spec(ub.shape),
            whole_spec(routes.shape),
            whole_spec(before.shape),
            whole_spec(router.shape),
            pl.BlockSpec((1, 1, 2, width, hidden), lambda e: (layer, e, 0, 0, 0)),
            pl.BlockSpec((1, 1, hidden, width), lambda e: (layer, e, 0, 0)),
        ],
        out_specs=[whole_spec((packs, count, width)), whole_spec((packs, ROUT, count))],
        scratch_shapes=[
            pltpu.VMEM((packs, NF * MOST, count), jnp.bfloat16),
            pltpu.VMEM((NF, packs * MOST, width), jnp.bfloat16),
            pltpu.VMEM((packs, NF * MOST, width), jnp.bfloat16),
            pltpu.VMEM((packs, NF * MOST, 1), jnp.float32),
        ],
        compiler_params=params_of(),
        name="ffn_fwd",
    )(ub, routes, before, router, wgu, wd)


def silu_parts(gate, up, ghid):
    sig = jax.nn.sigmoid(gate)
    act = gate * sig
    dg = (ghid * up * sig * (1.0 + gate * (1.0 - sig))).astype(jnp.bfloat16)
    du = (ghid * act).astype(jnp.bfloat16)
    return act * up, dg, du


def ffn_bwd_kernel(ub, gm, table, wgu, wd, part, gcoef, hot_s, x_s, g_s, y_s, coef_s, gc_s):
    e = pl.program_id(0)
    packs = ub.shape[0]

    @pl.when(e == 0)
    def _():
        for d in range(packs):
            hot = one_hot(table[d, SLOT : SLOT + NF, :])
            coef_s[d] = slot_values(hot, table[d, COEF : COEF + NF, :])
            hot_low = hot.astype(jnp.bfloat16)
            hot_s[d] = hot_low
            x = nn(hot_low, ub[d]).astype(jnp.bfloat16)
            g = nn(hot_low, gm[d]).astype(jnp.bfloat16)
            for n in range(NF):
                x_s[n, d * MOST : (d + 1) * MOST, :] = x[n * MOST : (n + 1) * MOST]
                g_s[n, d * MOST : (d + 1) * MOST, :] = g[n * MOST : (n + 1) * MOST]

    x = x_s[e]
    at = pl.ds(pl.multiple_of(e * MOST, MOST), MOST)
    coef = jnp.concatenate([coef_s[d, at, :] for d in range(packs)], axis=0)
    gate, up = nn(x, wgu[0, 0, 0]), nn(x, wgu[0, 0, 1])
    ghid = nt(g_s[e], wd[0, 0])
    hid, dg, du = silu_parts(gate, up, ghid * coef)
    dots = jnp.sum(hid * ghid, axis=1, keepdims=True)
    out = nt(dg, wgu[0, 0, 0]) + nt(du, wgu[0, 0, 1])
    for d in range(packs):
        y_s[d, at, :] = out[d * MOST : (d + 1) * MOST].astype(jnp.bfloat16)
        gc_s[d, at, :] = dots[d * MOST : (d + 1) * MOST]

    @pl.when(e == NF - 1)
    def _():
        for d in range(packs):
            part[d] = tn(hot_s[d], y_s[d]).astype(jnp.bfloat16)
            spread = hot_s[d].astype(jnp.float32) * gc_s[d]
            gcoef[d] = jnp.sum(spread.reshape(NF, MOST, spread.shape[1]), axis=1)


def ffn_backward(layer, ub, gm, table, wgu, wd):
    packs, count, width = ub.shape
    hidden = wd.shape[2]
    return pl.pallas_call(
        ffn_bwd_kernel,
        grid=(NF,),
        out_shape=[
            shape_of((packs, count, width), jnp.bfloat16),
            shape_of((packs, NF, count), jnp.float32),
        ],
        in_specs=[
            whole_spec(ub.shape),
            whole_spec(gm.shape),
            whole_spec(table.shape),
            pl.BlockSpec((1, 1, 2, width, hidden), lambda e: (layer, e, 0, 0, 0)),
            pl.BlockSpec((1, 1, hidden, width), lambda e: (layer, e, 0, 0)),
        ],
        out_specs=[whole_spec((packs, count, width)), whole_spec((packs, NF, count))],
        scratch_shapes=[
            pltpu.VMEM((packs, NF * MOST, count), jnp.bfloat16),
            pltpu.VMEM((NF, packs * MOST, width), jnp.bfloat16),
            pltpu.VMEM((NF, packs * MOST, width), jnp.bfloat16),
            pltpu.VMEM((packs, NF * MOST, width), jnp.bfloat16),
            pltpu.VMEM((packs, NF * MOST, 1), jnp.float32),
            pltpu.VMEM((packs, NF * MOST, 1), jnp.float32),
        ],
        compiler_params=params_of(),
        name="ffn_bwd",
    )(ub, gm, table, wgu, wd)


def dispatch_kernel(small, u, gm, x, g):
    rows = small[0]
    hot = one_hot(rows[NF : 2 * NF])
    coef = slot_values(hot, rows[:NF])
    hot = hot.astype(jnp.bfloat16)
    x[...] = nn(hot, u[0]).astype(jnp.bfloat16).reshape(x.shape)
    g[...] = (nn(hot, gm[0]) * coef).astype(jnp.bfloat16).reshape(g.shape)


def dispatch(small, u, gm):
    devices, count, width = u.shape
    grouped = pl.BlockSpec((NF, 1, MOST, width), lambda d: (0, d, 0, 0))
    outs = shape_of((NF, devices, MOST, width), jnp.bfloat16)
    return pl.pallas_call(
        dispatch_kernel,
        grid=(devices,),
        out_shape=[outs, outs],
        in_specs=[
            pl.BlockSpec((1, 2 * NF, count), lambda d: (d, 0, 0)),
            pl.BlockSpec((1, count, width), lambda d: (d, 0, 0)),
            pl.BlockSpec((1, count, width), lambda d: (d, 0, 0)),
        ],
        out_specs=[grouped, grouped],
        compiler_params=params_of(),
        name="dispatch",
    )(small, u, gm)


def dw_kernel(*refs):
    x, g, wgu, wd, dgu, dd, dg_s, du_s, hid_s = refs[:4] + refs[-5:]
    rows = x.shape[1]
    chunk = 256

    def pieces(i, _):
        part = pl.ds(pl.multiple_of(i * chunk, chunk), chunk)
        xs = x[0, part, :]
        hid, dg, du = silu_parts(nn(xs, wgu[0, 0, 0]), nn(xs, wgu[0, 0, 1]), nt(g[0, part, :], wd[0, 0]))
        hid_s[part, :] = hid.astype(jnp.bfloat16)
        dg_s[part, :] = dg
        du_s[part, :] = du
        return 0

    lax.fori_loop(0, rows // chunk, pieces, 0)

    def first(i, _):
        part = pl.ds(pl.multiple_of(i * 256, 256), 256)
        xs = x[0, :, part]
        dgu[0, 0, 0, part, :] = tn(xs, dg_s[...])
        dgu[0, 0, 1, part, :] = tn(xs, du_s[...])
        return 0

    lax.fori_loop(0, x.shape[2] // 256, first, 0)

    def second(i, _):
        part = pl.ds(pl.multiple_of(i * 256, 256), 256)
        dd[0, 0, part, :] = tn(hid_s[:, part], g[0])
        return 0

    lax.fori_loop(0, hid_s.shape[1] // 256, second, 0)


def weight_grads(layer, x, g, wgu, wd, earlier):
    _, rows, width = x.shape
    hidden = wd.shape[2]
    gu_spec = pl.BlockSpec((1, 1, 2, width, hidden), lambda e: (layer, e, 0, 0, 0))
    d_spec = pl.BlockSpec((1, 1, hidden, width), lambda e: (layer, e, 0, 0))
    row_spec = pl.BlockSpec((1, rows, width), lambda e: (e, 0, 0))
    kernel = dw_kernel
    return pl.pallas_call(
        kernel,
        grid=(NF,),
        out_shape=[shape_of(wgu.shape, jnp.float32), shape_of(wd.shape, jnp.float32)],
        in_specs=[row_spec, row_spec, gu_spec, d_spec] + [pl.BlockSpec(memory_space=pl.ANY)] * len(earlier),
        out_specs=[gu_spec, d_spec],
        input_output_aliases={4 + i: i for i in range(len(earlier))},
        scratch_shapes=[pltpu.VMEM((rows, hidden), jnp.bfloat16)] * 3,
        compiler_params=params_of(),
        name="weight_grads",
    )(x, g, wgu, wd, *earlier)


def norm_low(x, gain):
    return ((x * rms_factor(x)) * gain).astype(jnp.bfloat16)


def post_attention(ob, x, wo, gain):
    groups = wo.shape[0]
    inner = wo.shape[1]
    blk = ob.shape[1]
    halves = []
    for h in range(2):
        total = x[h * blk : (h + 1) * blk]
        for g in range(groups):
            total = total + nn(ob[h * groups + g][:, :inner], wo[g])
        halves.append(total)
    hst = jnp.concatenate(halves, axis=0)
    return hst, norm_low(hst, gain)


def mixing_rows(table):
    raw, coef = table[RAW : RAW + 16], table[COEF : COEF + 16]
    pairs = []
    for c in range(NC):
        r0, r1 = raw[NE + 2 * c : NE + 2 * c + 1], raw[NE + 2 * c + 1 : NE + 2 * c + 2]
        top = jnp.maximum(r0, r1)
        e0, e1 = jnp.exp(r0 - top), jnp.exp(r1 - top)
        pairs.append((e0 / (e0 + e1), e1 / (e0 + e1)))
    shares = [coef[NF + 2 + c : NF + 3 + c] for c in range(NC)]
    scale_u = coef[NF + 1 : NF + 2]
    for c in range(NC):
        scale_u = scale_u + shares[c] * pairs[c][0]
    return pairs, shares, scale_u, [shares[c] * pairs[c][1] for c in range(NC)]


def combine(hst, parts, table, gain, consts, next_gain):
    _, _, scale_u, scale_c = mixing_rows(table)
    columns = to_columns([scale_u] + scale_c)
    u = (hst * rms_factor(hst)) * gain
    moe = columns[0] * u
    for f in range(parts.shape[0]):
        moe = moe + parts[f].astype(jnp.float32)
    for c in range(NC):
        moe = moe + columns[1 + c] * consts[c : c + 1].astype(jnp.float32)
    x = hst + moe
    return x, norm_low(x, next_gain)


def middle(gx, parts, gcoef, table, routes, gprev, hst, ub, gain, consts, router, wo, ob):
    groups = wo.shape[0]
    inner = wo.shape[1]
    blk = ob.shape[1]
    consts = consts.astype(jnp.float32)
    pairs, shares, scale_u, scale_c = mixing_rows(table)
    columns = to_columns([scale_u] + scale_c)
    factor = rms_factor(hst)
    base = hst * factor
    u = base * gain
    dots = [jnp.sum(gx * u, axis=1, keepdims=True)]
    dots += [jnp.sum(gx * consts[c : c + 1], axis=1, keepdims=True) for c in range(NC)]
    dots = to_rows(dots, 8)
    dot_u = dots[0:1]
    dot_c = [dots[1 + c : 2 + c] for c in range(NC)]
    ids = lax.broadcasted_iota(jnp.int32, (16, gx.shape[0]), 0)
    grads = jnp.concatenate([gcoef, jnp.zeros_like(gcoef)], axis=0)
    grads = jnp.where(ids == NF + 1, dot_u, grads)
    raw_rows = []
    for c in range(NC):
        a0, a1 = pairs[c]
        grads = jnp.where(ids == NF + 2 + c, a0 * dot_u + a1 * dot_c[c], grads)
        g0, g1 = shares[c] * dot_u, shares[c] * dot_c[c]
        both = a0 * g0 + a1 * g1
        raw_rows += [a0 * (g0 - both), a1 * (g1 - both)]
    logits = table[LOGI : LOGI + 16]
    first, second = ids == routes[0:1], ids == routes[1:2]

    def pick(chosen, rows):
        return jnp.sum(jnp.where(chosen, rows, 0.0), axis=0, keepdims=True)

    z0, z1 = pick(first, logits), pick(second, logits)
    top = jnp.maximum(z0, z1)
    e0, e1 = jnp.exp(z0 - top), jnp.exp(z1 - top)
    w0, w1 = e0 / (e0 + e1), e1 / (e0 + e1)
    gg0, gg1 = pick(first, grads), pick(second, grads)
    both = w0 * gg0 + w1 * gg1
    glog = jnp.where(first, w0 * (gg0 - both), 0.0) + jnp.where(second, w1 * (gg1 - both), 0.0) + gprev
    graw = glog
    for index, row in enumerate(raw_rows):
        graw = jnp.where(ids == NE + index, row, graw)
    graw = graw.astype(jnp.bfloat16)
    grad_router = nn(graw, ub)
    gu = gx * columns[0] + tn(graw, router)
    for f in range(parts.shape[0]):
        gu = gu + parts[f].astype(jnp.float32)
    small = [jnp.sum(gu * base, axis=0, keepdims=True)]
    small += [jnp.sum(gx * columns[1 + c], axis=0, keepdims=True) for c in range(NC)]
    gb = gu * gain
    ghst = gx + factor * (gb - base * jnp.mean(gb * base, axis=-1, keepdims=True))
    gy = ghst.astype(jnp.bfloat16)
    lanes = ob.shape[2]
    go, gwo = [None] * (2 * groups), []
    for g in range(groups):
        value = nt(gy, wo[g]).astype(jnp.bfloat16)
        value = jnp.concatenate([value, jnp.zeros((value.shape[0], lanes - inner), jnp.bfloat16)], axis=1)
        for h in range(2):
            go[h * groups + g] = value[h * blk : (h + 1) * blk]
        mixed = jnp.concatenate([ob[g], ob[groups + g]], axis=0)
        gwo.append(tn(mixed, gy)[:inner].astype(jnp.bfloat16))
    return ghst, jnp.stack(go), jnp.concatenate(gwo, axis=0), jnp.concatenate(small + [grad_router], axis=0), glog


def finish(parts, ghst, x, gain):
    groups = parts.shape[0] // 2
    halves = []
    for h in range(2):
        total = parts[h * groups].astype(jnp.float32)
        for g in range(1, groups):
            total = total + parts[h * groups + g].astype(jnp.float32)
        halves.append(total)
    gn = jnp.concatenate(halves, axis=0)
    factor = rms_factor(x)
    base = x * factor
    gb = gn * gain
    gx = ghst + factor * (gb - base * jnp.mean(gb * base, axis=-1, keepdims=True))
    return gx, gx.astype(jnp.bfloat16), jnp.sum(gn * base, axis=0, keepdims=True)


def turn_tables(seq):
    half = HEAD_DIM // 2
    frequency = np.exp((-np.log(np.float32(10000.0)) * np.arange(half, dtype=np.float32) / np.float32(half)))
    angles = np.arange(seq, dtype=np.float32)[:, None] * frequency.astype(np.float32)[None, :]
    cosine, sine = np.cos(angles), np.sin(angles)
    cosine = np.concatenate([cosine, cosine] * 2, axis=1).astype(np.float32)
    sine = np.concatenate([-sine, sine] * 2, axis=1).astype(np.float32)
    return jnp.asarray(cosine), jnp.asarray(sine)


def by_heads(
    tokens,
    cotangent,
    seq_lengths,
    block_order,
    routes,
    gains,
    qkv_weights,
    out_weight,
    router,
    const_values,
    w_gate_up,
    w_down,
):
    count, width = tokens.shape[1], tokens.shape[2]
    ctx_size, packs = lax.axis_size("ctx"), lax.axis_size("fsdp")
    groups = ctx_size // 2
    blk = count // 2
    seq = blk * ctx_size
    own, pack = lax.axis_index("ctx"), lax.axis_index("fsdp")
    sequence, group = own // groups, own % groups
    inner = GROUP_HEADS * HEAD_DIM
    lanes = -(-inner // 128) * 128
    shard = width // packs
    f32, bf = jnp.float32, jnp.bfloat16

    cosine, sine = turn_tables(seq)
    order = lax.dynamic_index_in_dim(block_order[0].reshape(ctx_size, 2), sequence, 1, keepdims=False) - ctx_size * sequence
    ids = jnp.arange(ctx_size, dtype=jnp.int32)
    inv = jnp.sum(jnp.where(order[None, :] == ids[:, None], ids[None, :], 0), axis=1)

    smalls = jnp.concatenate([gains, const_values, jnp.swapaxes(router, 1, 2)], axis=1)
    smalls = lax.all_gather(smalls, "fsdp", axis=2, tiled=True)
    qkv_cols = lax.dynamic_slice_in_dim(qkv_weights, group * inner, inner, axis=3)
    qkv_cols = jnp.pad(qkv_cols, ((0, 0), (0, 0), (0, 0), (0, lanes - inner)))
    qkv_cols = jnp.swapaxes(qkv_cols, 1, 2).reshape(LAYERS, shard, 3 * lanes)
    w_attn = [lax.all_gather(qkv_cols[l], "fsdp", axis=0, tiled=True) for l in range(LAYERS)]
    w_out = [lax.all_gather(out_weight[l], "fsdp", axis=0, tiled=False) for l in range(LAYERS)]
    routes_t = jnp.swapaxes(routes[:, 0], 1, 2)
    routes_f = lax.all_gather(routes_t, "fsdp", axis=1, tiled=False)

    def gain_of(l, which):
        return smalls[l, which : which + 1].astype(f32)

    x = tokens[0].astype(f32)
    gm_low = cotangent[0]
    gm_all = [None, lax.all_gather(gm_low, ("ctx", "fsdp"), axis=0, tiled=False)]
    before = jnp.zeros((packs, 16, count), f32)
    (n1,) = block_call(lambda a, b: (norm_low(a, b),), [shape_of((count, width), bf)], (x, gain_of(0, 0)), "norm")
    kept = []
    for l in range(LAYERS):
        consts, router_t = smalls[l, 2 : 2 + NC], smalls[l, 2 + NC :]
        send = jnp.broadcast_to(n1.reshape(2, 1, blk, width), (2, groups, blk, width)).reshape(ctx_size, blk, width)
        n1_all = lax.all_to_all(send, "ctx", 0, 0)
        qkv, o, lse, ob = attn_forward(inv, n1_all, w_attn[l], cosine, sine)
        ob = lax.all_to_all(ob, "ctx", 0, 0)
        hst, ub = block_call(
            post_attention,
            [shape_of((count, width), f32), shape_of((count, width), bf)],
            (ob, x, w_out[l], gain_of(l, 1)),
            "post_attention",
        )
        ub_f = lax.all_gather(ub, "fsdp", axis=0, tiled=False)
        ub_all = lax.all_gather(ub, ("ctx", "fsdp"), axis=0, tiled=False)
        parts, table_f = ffn_forward(l, ub_f, routes_f[l], before, router_t, w_gate_up, w_down)
        before = table_f[:, LOGI : LOGI + 16]
        table = lax.dynamic_index_in_dim(table_f, pack, 0, keepdims=False)
        small_all = lax.all_gather(
            jnp.concatenate([table[COEF : COEF + NF], table[SLOT : SLOT + NF]], axis=0), ("ctx", "fsdp"), axis=0, tiled=False
        )
        parts = lax.all_to_all(parts, "fsdp", 0, 0)
        x_next, n1 = block_call(
            combine,
            [shape_of((count, width), f32), shape_of((count, width), bf)],
            (hst, parts, table, gain_of(l, 1), consts, gain_of(min(l + 1, LAYERS - 1), 0)),
            "combine",
        )
        kept.append((x, n1_all, qkv, o, lse, ob, hst, ub, ub_f, ub_all, table_f, table, small_all, consts, router_t))
        x = x_next
    output = x
    gx = cotangent[0].astype(f32)
    gprev = jnp.zeros((16, count), f32)
    small_grads, qkv_grads, out_grads = [None] * LAYERS, [None] * LAYERS, [None] * LAYERS
    done = ()
    for l in reversed(range(LAYERS)):
        x, n1_all, qkv, o, lse, ob, hst, ub, ub_f, ub_all, table_f, table, small_all, consts, router_t = kept[l]
        gm_f = lax.all_gather(gm_low, "fsdp", axis=0, tiled=False)
        if gm_all[l] is None:
            gm_all[l] = lax.all_gather(gm_low, ("ctx", "fsdp"), axis=0, tiled=False)
        parts, gcoef = ffn_backward(l, ub_f, gm_f, table_f, w_gate_up, w_down)
        parts = lax.all_to_all(parts, "fsdp", 0, 0)
        gcoef = jnp.sum(lax.all_to_all(gcoef, "fsdp", 0, 0), axis=0)
        ghst, go, gwo, small, gprev = block_call(
            middle,
            [
                shape_of((count, width), f32),
                shape_of((ctx_size, blk, lanes), bf),
                shape_of((width, width), bf),
                shape_of((1 + NC + 16, width), f32),
                shape_of((16, count), f32),
            ],
            (gx, parts, gcoef, table, routes_t[l], gprev, hst, ub, gain_of(l, 1), consts, router_t, w_out[l], ob),
            "middle",
        )
        out_grads[l] = lax.psum(lax.psum_scatter(gwo, "fsdp", scatter_dimension=0, tiled=True), "ctx")
        go = lax.all_to_all(go, "ctx", 0, 0)
        gn, gw = attn_backward(inv, n1_all, w_attn[l], cosine, sine, qkv, o, lse, go)
        gw = lax.psum_scatter(gw, "fsdp", scatter_dimension=0, tiled=True)
        gw = lax.all_gather(gw, "ctx", axis=0, tiled=False).reshape(2, groups, shard, 3, lanes)[..., :inner]
        gw = jnp.sum(gw.astype(f32), axis=0)
        qkv_grads[l] = jnp.transpose(gw, (2, 1, 0, 3)).reshape(3, shard, width)
        gn = lax.all_to_all(gn, "ctx", 0, 0)
        gx, gm_low, gain_grad = block_call(
            finish,
            [shape_of((count, width), f32), shape_of((count, width), bf), shape_of((1, width), f32)],
            (gn, ghst, x, gain_of(l, 0)),
            "finish",
        )
        small_grads[l] = jnp.concatenate([gain_grad, small], axis=0)
        x_all, g_all = dispatch(small_all, ub_all, gm_all[l])
        rows = x_all.shape[1] * x_all.shape[2]
        done = weight_grads(l, x_all.reshape(NF, rows, width), g_all.reshape(NF, rows, width), w_gate_up, w_down, done)
    small = lax.psum(jnp.stack(small_grads).astype(bf), ("ctx", "fsdp"))
    small = lax.dynamic_slice_in_dim(small, pack * shard, shard, axis=2).astype(f32)
    return (
        output[None],
        gx[None],
        small[:, :2],
        jnp.stack(qkv_grads),
        jnp.stack(out_grads).astype(f32),
        jnp.swapaxes(small[:, 2 + NC :], 1, 2),
        small[:, 2 : 2 + NC],
        done[0],
        done[1],
    )


def solution(mesh):
    placed = (
        P("fsdp", "ctx", None),
        P("fsdp", "ctx", None),
        P("fsdp", None),
        P("fsdp", None),
        P(None, "fsdp", "ctx", None),
        P(None, None, "fsdp"),
        P(None, None, "fsdp", None),
        P(None, "fsdp", None),
        P(None, "fsdp", None),
        P(None, None, "fsdp"),
        P(None, None, None, None, "fsdp"),
        P(None, None, "fsdp", None),
    )
    contexts, packs = mesh.shape["ctx"], mesh.shape["fsdp"]
    blocks_of_heads = HEADS // GROUP_HEADS

    def plan(*args):
        tokens = args[0]
        even = tokens.shape[1] * contexts == 2 * MINLEN
        grouped = contexts == 2 * blocks_of_heads and packs == blocks_of_heads
        return (by_heads if even and grouped else shards)(*args)

    return jax.shard_map(
        plan,
        mesh=mesh,
        in_specs=placed,
        out_specs=(
            P("fsdp", "ctx", None),
            P("fsdp", "ctx", None),
            P(None, None, "fsdp"),
            P(None, None, "fsdp", None),
            P(None, "fsdp", None),
            P(None, "fsdp", None),
            P(None, None, "fsdp"),
            P(None, None, None, None, "fsdp"),
            P(None, None, "fsdp", None),
        ),
        check_vma=False,
    )
```

```python
import jax
import jax.numpy as jnp
import numpy as np
from jax import lax
from jax.experimental import pallas as pl
from jax.experimental.pallas import tpu as pltpu
from jax.sharding import PartitionSpec as P

HEADS = 12
HEAD_DIM = 64
NF = 8
NC = 2
LAYERS = 2
NE = 12
MOST = 64
GROUP_HEADS = 3


def from_behind(x, axis, by):
    devices = lax.axis_size(axis)
    return lax.ppermute(x, axis, [(i, (i + by) % devices) for i in range(devices)])


def layout_tables(lengths, order_row, tok_count):
    block_len = tok_count // 2
    pack_len = order_row.shape[0] * block_len
    pack_rows = jnp.arange(pack_len, dtype=jnp.int32)
    owner = pack_rows // tok_count
    which_half = pack_rows % tok_count // block_len
    block_ids = order_row[2 * owner + which_half]
    pack_pos = block_ids * block_len + pack_rows % block_len
    segment = (pack_pos >= lengths[0]).astype(jnp.int32)
    seq_pos = pack_pos - segment * lengths[0]
    return (pack_pos, segment, seq_pos)


def angle_tables(seq_pos, head_size):
    half_size = head_size // 2
    frequency = jnp.exp(-jnp.log(10000.0) * jnp.arange(half_size, dtype=jnp.float32) / half_size)
    angles = seq_pos.astype(jnp.float32)[:, None] * frequency[None, :]
    return (jnp.cos(angles)[:, None, :], jnp.sin(angles)[:, None, :])


def rotate_pairs(values, cosine_table, sine_table, direction):
    half_size = values.shape[-1] // 2
    first_half = values[..., :half_size]
    second_half = values[..., half_size:]
    return jnp.concatenate(
        [
            first_half * cosine_table - direction * second_half * sine_table,
            second_half * cosine_table + direction * first_half * sine_table,
        ],
        axis=-1,
    )


def rms_parts(values):
    inverse = lax.rsqrt(jnp.mean(values * values, axis=-1, keepdims=True) + 1e-06)
    return (values * inverse, inverse)


def rms_back(grad_normed, base_values, inverse):
    return inverse * (
        grad_normed - base_values * jnp.mean(grad_normed * base_values, axis=-1, keepdims=True)
    )


def expert_forward(inputs_low, gate_up_use, down_use):
    gate_up_out = jnp.einsum(
        "emd,ecdf->ecmf", inputs_low, gate_up_use, preferred_element_type=jnp.float32
    )
    hidden_low = (jax.nn.silu(gate_up_out[:, 0]) * gate_up_out[:, 1]).astype(jnp.bfloat16)
    partial_value = jnp.einsum(
        "emf,efd->emd", hidden_low, down_use, preferred_element_type=jnp.float32
    )
    return (gate_up_out, hidden_low, partial_value)


def expert_backward(inputs_low, gate_up_out, hidden_low, grad_part_low, gate_up_use, down_use):
    grad_down = jnp.einsum(
        "emf,emd->efd", hidden_low, grad_part_low, preferred_element_type=jnp.float32
    )
    grad_hidden = jnp.einsum(
        "emd,efd->emf", grad_part_low, down_use, preferred_element_type=jnp.float32
    )
    gate_out = gate_up_out[:, 0]
    sigmoid_gate = jax.nn.sigmoid(gate_out)
    grad_pair_low = jnp.stack(
        [
            grad_hidden
            * gate_up_out[:, 1]
            * sigmoid_gate
            * (1.0 + gate_out * (1.0 - sigmoid_gate)),
            grad_hidden * gate_out * sigmoid_gate,
        ],
        axis=1,
    ).astype(jnp.bfloat16)
    grad_gate_up = jnp.einsum(
        "emd,ecmf->ecdf", inputs_low, grad_pair_low, preferred_element_type=jnp.float32
    )
    grad_rows = jnp.einsum(
        "ecmf,ecdf->emd", grad_pair_low, gate_up_use, preferred_element_type=jnp.float32
    )
    return (grad_gate_up, grad_down, grad_rows)


def shards(
    tokens,
    cotangent,
    seq_lengths,
    block_order,
    routes,
    gains,
    qkv_weights,
    out_weight,
    router,
    const_values,
    w_gate_up,
    w_down,
):
    tok_count = tokens.shape[1]
    width = tokens.shape[2]
    ctx_size = lax.axis_size("ctx")
    own_index = lax.axis_index("ctx")
    score_scale = HEAD_DIM ** (-0.5)
    pack_pos, segment, seq_pos = layout_tables(seq_lengths[0], block_order[0], tok_count)
    own_start = own_index * tok_count
    query_pos = lax.dynamic_slice_in_dim(pack_pos, own_start, tok_count)
    query_seg = lax.dynamic_slice_in_dim(segment, own_start, tok_count)
    cosine_table, sine_table = angle_tables(
        lax.dynamic_slice_in_dim(seq_pos, own_start, tok_count), HEAD_DIM
    )
    head_shape = (tok_count, HEADS, HEAD_DIM)
    expert_ids = jnp.arange(NE, dtype=jnp.int32)
    slot_ids = jnp.arange(MOST, dtype=jnp.int32)
    row_ids = jnp.arange(tok_count, dtype=jnp.int32)

    def allowed_pairs(key_offset, key_count):
        key_pos = lax.dynamic_slice_in_dim(pack_pos, key_offset, key_count)
        key_seg = lax.dynamic_slice_in_dim(segment, key_offset, key_count)
        return (query_seg[:, None] == key_seg[None, :]) & (key_pos[None, :] <= query_pos[:, None])

    stream = tokens[0].astype(jnp.float32)
    previous = jnp.zeros((tok_count, NE), jnp.float32)
    saved = []
    for layer_index in range(LAYERS):
        gain_all, qkv_all, out_all, router_all, const_all = (
            lax.all_gather(gains[layer_index], "fsdp", axis=1, tiled=True),
            lax.all_gather(qkv_weights[layer_index], "fsdp", axis=1, tiled=True),
            lax.all_gather(out_weight[layer_index], "fsdp", axis=0, tiled=True),
            lax.all_gather(router[layer_index], "fsdp", axis=0, tiled=True),
            lax.all_gather(const_values[layer_index], "fsdp", axis=1, tiled=True),
        )
        gain_float = gain_all.astype(jnp.float32)
        base_one, inverse_one = rms_parts(stream)
        normed_low = (base_one * gain_float[0]).astype(jnp.bfloat16)
        projected = jnp.einsum(
            "td,cde->cte", normed_low, qkv_all, preferred_element_type=jnp.float32
        )
        queries_low = rotate_pairs(
            projected[0].reshape(head_shape), cosine_table, sine_table, 1.0
        ).astype(jnp.bfloat16)
        keys_low = rotate_pairs(
            projected[1].reshape(head_shape), cosine_table, sine_table, 1.0
        ).astype(jnp.bfloat16)
        values_low = projected[2].reshape(head_shape).astype(jnp.bfloat16)

        def fold_step(running, shard_piece, offset, queries_use=queries_low):
            keys_piece, values_piece = shard_piece
            allowed = allowed_pairs(offset, keys_piece.shape[0])[None]
            scores = (
                jnp.einsum(
                    "qhd,khd->hqk", queries_use, keys_piece, preferred_element_type=jnp.float32
                )
                * score_scale
            )
            scores = jnp.where(allowed, scores, -1e30)
            top_old, total_old, accumulated = running
            top_new = jnp.maximum(top_old, jnp.max(scores, axis=-1))
            weights = jnp.where(allowed, jnp.exp(scores - top_new[..., None]), 0.0)
            factor = jnp.exp(top_old - top_new)
            accumulated = jnp.einsum(
                "hqk,khd->hqd",
                weights.astype(jnp.bfloat16),
                values_piece,
                preferred_element_type=jnp.float32,
            )
            return (top_new, jnp.sum(weights, axis=-1), accumulated)

        starting = (
            jnp.full((HEADS, tok_count), -1e30, jnp.float32),
            jnp.zeros((HEADS, tok_count), jnp.float32),
            jnp.zeros((HEADS, tok_count, HEAD_DIM), jnp.float32),
        )
        top_value, total_sum, accumulated = fold_step(
            starting,
            (
                lax.all_gather(keys_low, "ctx", axis=0, tiled=True),
                lax.all_gather(values_low, "ctx", axis=0, tiled=True),
            ),
            jnp.int32(0),
        )
        log_total = top_value + jnp.log(total_sum)
        attended = jnp.transpose(accumulated / total_sum[..., None], (1, 0, 2))
        mixed_low = attended.reshape(tok_count, width).astype(jnp.bfloat16)
        hidden_state = stream + jnp.dot(mixed_low, out_all, preferred_element_type=jnp.float32)
        base_two, inverse_two = rms_parts(hidden_state)
        expert_in = base_two * gain_float[1]
        expert_low = expert_in.astype(jnp.bfloat16)
        raw_logits = jnp.dot(expert_low, router_all, preferred_element_type=jnp.float32)
        logits = raw_logits[:, :NE] + previous
        route_ids = routes[layer_index, 0]
        chosen = route_ids[:, :, None] == expert_ids[None, None, :]
        chosen_f = chosen.astype(jnp.float32)
        hit_count = jnp.sum(chosen.astype(jnp.int32), axis=1)
        slot_index = jnp.cumsum(hit_count, axis=0) - 1
        picked = jnp.sum(chosen_f * logits[:, None, :], axis=-1)
        gate_weights = jax.nn.softmax(picked, axis=-1)
        coeffs = jnp.sum(gate_weights[:, :, None] * chosen_f, axis=1)
        slot_table = jnp.zeros((NF, MOST), jnp.int32)
        for expert in range(NF):
            target = jnp.where(hit_count[:, expert] > 0, slot_index[:, expert], MOST)
            slot_table = slot_table.at[expert, target].set(row_ids, mode="drop")
        filled = (slot_ids[None, :] < jnp.sum(hit_count[:, :NF], axis=0)[:, None]).astype(
            jnp.float32
        )
        rows_low = expert_low[slot_table]
        inputs_low = lax.all_gather(rows_low, "fsdp", axis=1, tiled=True)
        gate_up_out, hidden_low, partial_value = expert_forward(
            inputs_low, w_gate_up[layer_index], w_down[layer_index]
        )
        result = lax.psum_scatter(
            partial_value.astype(jnp.bfloat16), "fsdp", scatter_dimension=1, tiled=True
        ).astype(jnp.float32)
        flat_index = jnp.arange(NF, dtype=jnp.int32)[None, :] * MOST + jnp.clip(
            slot_index[:, :NF], 0, MOST - 1
        )
        token_result = result.reshape(NF * MOST, width)[flat_index]
        expert_mix = (
            jnp.sum(coeffs[:, :NF, None] * token_result, axis=1)
            + coeffs[:, NF + 1 : NF + 2] * expert_in
        )
        mixings = []
        for const_index in range(NC):
            column = NE + 2 * const_index
            mixing = jax.nn.softmax(raw_logits[:, column : column + 2], axis=-1)
            mixings.append(mixing)
            expert_mix = expert_mix + coeffs[:, NF + 2 + const_index : NF + 3 + const_index] * (
                mixing[:, 0:1] * expert_in
                + mixing[:, 1:2] * const_all[const_index].astype(jnp.float32)[None, :]
            )
        saved.append(
            (
                gain_float,
                qkv_all,
                out_all,
                router_all,
                const_all,
                base_one,
                inverse_one,
                normed_low,
                queries_low,
                keys_low,
                values_low,
                log_total,
                attended,
                mixed_low,
                base_two,
                inverse_two,
                expert_in,
                expert_low,
                chosen_f,
                hit_count,
                gate_weights,
                coeffs,
                slot_table,
                filled,
                inputs_low,
                gate_up_out,
                hidden_low,
                flat_index,
                token_result,
                mixings,
            )
        )
        stream = hidden_state + expert_mix
        previous = logits
    grad_stream = cotangent[0].astype(jnp.float32)
    grad_previous = jnp.zeros((tok_count, NE), jnp.float32)
    layer_grads = [None] * LAYERS
    for layer_index in reversed(range(LAYERS)):
        (
            gain_float,
            qkv_all,
            out_all,
            router_all,
            const_all,
            base_one,
            inverse_one,
            normed_low,
            queries_low,
            keys_low,
            values_low,
            log_total,
            attended,
            mixed_low,
            base_two,
            inverse_two,
            expert_in,
            expert_low,
            chosen_f,
            hit_count,
            gate_weights,
            coeffs,
            slot_table,
            filled,
            inputs_low,
            gate_up_out,
            hidden_low,
            flat_index,
            token_result,
            mixings,
        ) = saved[layer_index]
        grad_mix = grad_stream
        dot_input = jnp.sum(grad_mix * expert_in, axis=-1, keepdims=True)
        coef_grads = [
            jnp.sum(grad_mix[:, None, :] * token_result, axis=-1),
            jnp.zeros((tok_count, 1), jnp.float32),
            dot_input,
        ]
        grad_in = grad_mix * coeffs[:, NF + 1 : NF + 2]
        const_cols = []
        const_grads = []
        for const_index in range(NC):
            mixing = mixings[const_index]
            const_row = const_all[const_index].astype(jnp.float32)[None, :]
            dot_const = jnp.sum(grad_mix * const_row, axis=-1, keepdims=True)
            share = coeffs[:, NF + 2 + const_index : NF + 3 + const_index]
            coef_grads.append(mixing[:, 0:1] * dot_input + mixing[:, 1:2] * dot_const)
            grad_in = grad_in + grad_mix * (share * mixing[:, 0:1])
            grad_mixing = share * jnp.concatenate([dot_input, dot_const], axis=1)
            const_cols.append(
                mixing * (grad_mixing - jnp.sum(mixing * grad_mixing, axis=-1, keepdims=True))
            )
            const_grads.append(jnp.sum(grad_mix * (share * mixing[:, 1:2]), axis=0))
        grad_coeffs = jnp.concatenate(coef_grads, axis=1)
        grad_gates = jnp.sum(chosen_f * grad_coeffs[:, None, :], axis=-1)
        grad_picked = gate_weights * (
            grad_gates - jnp.sum(gate_weights * grad_gates, axis=-1, keepdims=True)
        )
        grad_logits = jnp.sum(grad_picked[:, :, None] * chosen_f, axis=1) + grad_previous
        grad_previous = grad_logits
        grad_raw_low = jnp.concatenate([grad_logits] + const_cols, axis=1).astype(jnp.bfloat16)
        grad_router = jnp.einsum(
            "td,tc->dc", expert_low, grad_raw_low, preferred_element_type=jnp.float32
        )
        grad_in = grad_in + jnp.einsum(
            "tc,dc->td", grad_raw_low, router_all, preferred_element_type=jnp.float32
        )
        slot_weight = (
            jnp.take_along_axis(jnp.transpose(coeffs[:, :NF]), slot_table, axis=1) * filled
        )
        grad_result_low = (grad_mix[slot_table] * slot_weight[:, :, None]).astype(jnp.bfloat16)
        grad_part_low = lax.all_gather(grad_result_low, "fsdp", axis=1, tiled=True)
        grad_gate_up, grad_down, grad_rows = expert_backward(
            inputs_low,
            gate_up_out,
            hidden_low,
            grad_part_low,
            w_gate_up[layer_index],
            w_down[layer_index],
        )
        grad_rows = lax.psum_scatter(
            grad_rows.astype(jnp.bfloat16), "fsdp", scatter_dimension=1, tiled=True
        ).astype(jnp.float32)
        token_grads = grad_rows.reshape(NF * MOST, width)[flat_index]
        grad_in = grad_in + jnp.sum(
            jnp.where(hit_count[:, :NF, None] > 0, token_grads, 0.0), axis=1
        )
        grad_gain_two = jnp.sum(grad_in * base_two, axis=0)
        grad_hidden_state = grad_stream + rms_back(grad_in * gain_float[1], base_two, inverse_two)
        grad_out_low = grad_hidden_state.astype(jnp.bfloat16)
        grad_out_w = jnp.einsum(
            "td,te->de", mixed_low, grad_out_low, preferred_element_type=jnp.float32
        )
        grad_attended = (
            jnp.einsum("te,de->td", grad_out_low, out_all, preferred_element_type=jnp.float32)
            .astype(jnp.bfloat16)
            .reshape(head_shape)
        )
        delta = jnp.transpose(jnp.sum(grad_attended.astype(jnp.float32) * attended, axis=-1))

        def visit(
            turn_index,
            carried,
            queries_use=queries_low,
            grad_use=grad_attended,
            log_use=log_total,
            delta_use=delta,
        ):
            keys_piece, values_piece, key_grads, value_grads, query_grads = carried
            source = (own_index - turn_index) % ctx_size
            allowed = allowed_pairs(source * tok_count, tok_count)[None]
            scores = (
                jnp.einsum(
                    "qhd,khd->hqk", queries_use, keys_piece, preferred_element_type=jnp.float32
                )
                * score_scale
            )
            probs = jnp.where(
                allowed, jnp.exp(jnp.where(allowed, scores, -1e30) - log_use[..., None]), 0.0
            )
            value_grads = value_grads + jnp.einsum(
                "hqk,qhd->khd",
                probs.astype(jnp.bfloat16),
                grad_use,
                preferred_element_type=jnp.float32,
            )
            prob_grads = jnp.einsum(
                "qhd,khd->hqk", grad_use, values_piece, preferred_element_type=jnp.float32
            )
            score_grads = (probs * (prob_grads - delta_use[..., None])).astype(jnp.bfloat16)
            query_grads = query_grads + jnp.einsum(
                "hqk,khd->qhd", score_grads, keys_piece, preferred_element_type=jnp.float32
            )
            key_grads = key_grads + jnp.einsum(
                "hqk,qhd->khd", score_grads, queries_use, preferred_element_type=jnp.float32
            )
            keys_piece, values_piece = from_behind((keys_piece, values_piece), "ctx", 1)
            key_grads, value_grads = (
                from_behind(key_grads.astype(jnp.bfloat16), "ctx", 1).astype(key_grads.dtype),
                from_behind(value_grads.astype(jnp.bfloat16), "ctx", 1).astype(value_grads.dtype),
            )
            return (keys_piece, values_piece, key_grads, value_grads, query_grads)

        zero_heads = jnp.zeros(head_shape, jnp.float32)
        finished = lax.fori_loop(
            0, ctx_size, visit, (keys_low, values_low, zero_heads, zero_heads, zero_heads)
        )
        grad_query = (
            rotate_pairs(finished[4] * score_scale, cosine_table, sine_table, -1.0)
            .astype(jnp.bfloat16)
            .reshape(tok_count, width)
        )
        grad_key = (
            rotate_pairs(finished[2] * score_scale, cosine_table, sine_table, -1.0)
            .astype(jnp.bfloat16)
            .reshape(tok_count, width)
        )
        grad_value = finished[3].astype(jnp.bfloat16).reshape(tok_count, width)
        grad_proj_low = jnp.stack([grad_query, grad_key, grad_value], axis=0)
        grad_qkv = jnp.einsum(
            "td,cte->cde", normed_low, grad_proj_low, preferred_element_type=jnp.float32
        )
        grad_normed = jnp.einsum(
            "cte,cde->td", grad_proj_low, qkv_all, preferred_element_type=jnp.float32
        )
        grad_gain_one = jnp.sum(grad_normed * base_one, axis=0)
        grad_stream = grad_hidden_state + rms_back(
            grad_normed * gain_float[0], base_one, inverse_one
        )
        gains_shard, qkv_shard, out_shard, router_shard, const_shard = (
            lax.psum_scatter(
                jnp.stack([grad_gain_one, grad_gain_two]).astype(jnp.bfloat16),
                "fsdp",
                scatter_dimension=1,
                tiled=True,
            ).astype(jnp.float32),
            lax.psum_scatter(
                grad_qkv.astype(jnp.bfloat16), "fsdp", scatter_dimension=1, tiled=True
            ).astype(jnp.float32),
            lax.psum_scatter(
                grad_out_w.astype(jnp.bfloat16), "fsdp", scatter_dimension=0, tiled=True
            ).astype(jnp.float32),
            lax.psum_scatter(
                grad_router.astype(jnp.bfloat16), "fsdp", scatter_dimension=0, tiled=True
            ).astype(jnp.float32),
            lax.psum_scatter(
                jnp.stack(const_grads).astype(jnp.bfloat16), "fsdp", scatter_dimension=1, tiled=True
            ).astype(jnp.float32),
        )
        layer_grads[layer_index] = (
            lax.psum(gains_shard.astype(jnp.bfloat16), "ctx").astype(jnp.float32),
            lax.psum(qkv_shard.astype(jnp.bfloat16), "ctx").astype(jnp.float32),
            lax.psum(out_shard.astype(jnp.bfloat16), "ctx").astype(jnp.float32),
            lax.psum(router_shard.astype(jnp.bfloat16), "ctx").astype(jnp.float32),
            lax.psum(const_shard.astype(jnp.bfloat16), "ctx").astype(jnp.float32),
            lax.psum(grad_gate_up.astype(jnp.bfloat16), "ctx").astype(jnp.float32),
            lax.psum(grad_down.astype(jnp.bfloat16), "ctx").astype(jnp.float32),
        )
    stacked = [
        jnp.stack([layer_grads[layer_index][member_index] for layer_index in range(LAYERS)])
        for member_index in range(7)
    ]
    return (
        stream[None],
        grad_stream[None],
        stacked[0],
        stacked[1],
        stacked[2],
        stacked[3],
        stacked[4],
        stacked[5],
        stacked[6],
    )


MINLEN = 1024
ROUT = 56
RAW, COEF, SLOT, LOGI = 0, 16, 32, 40
VMEM_MB = 60


def nt(a, b):
    return lax.dot_general(a, b, (((1,), (1,)), ((), ())), preferred_element_type=jnp.float32)


def nn(a, b):
    return lax.dot_general(a, b, (((1,), (0,)), ((), ())), preferred_element_type=jnp.float32)


def tn(a, b):
    return lax.dot_general(a, b, (((0,), (0,)), ((), ())), preferred_element_type=jnp.float32)


def params_of(mb=VMEM_MB, **more):
    return pltpu.CompilerParams(vmem_limit_bytes=mb * 2**20, **more)


def shape_of(dims, kind):
    return jax.ShapeDtypeStruct(dims, kind)


def rms_factor(values):
    return lax.rsqrt(jnp.mean(values * values, axis=-1, keepdims=True) + 1e-06)


def to_rows(columns, count):
    lane = lax.broadcasted_iota(jnp.int32, (columns[0].shape[0], 128), 1)
    packed = jnp.zeros(lane.shape, jnp.float32)
    for index, column in enumerate(columns):
        packed = jnp.where(lane == index, column, packed)
    return jnp.transpose(packed)[:count]


def to_columns(rows):
    count = rows[0].shape[1]
    sub = lax.broadcasted_iota(jnp.int32, (128, count), 0)
    packed = jnp.zeros(sub.shape, jnp.float32)
    for index, row in enumerate(rows):
        packed = jnp.where(sub == index, row, packed)
    packed = jnp.transpose(packed)
    return [packed[:, index : index + 1] for index in range(len(rows))]


def swap_halves(values):
    lanes = values.shape[1]
    lane = lax.broadcasted_iota(jnp.int32, values.shape, 1)
    ahead = pltpu.roll(values, lanes - 32, 1)
    behind = pltpu.roll(values, 32, 1)
    return jnp.where(lane % 64 < 32, ahead, behind)


def spin(values, cosine, sine):
    return values * cosine + swap_halves(values) * sine


def place():
    own, pack = lax.axis_index("ctx"), lax.axis_index("fsdp")
    return own // 2, own % 2, pack // 2, pack % 2


def remote(src, dst, send, recv, ctx, fsdp):
    return pltpu.make_async_remote_copy(
        src_ref=src,
        dst_ref=dst,
        send_sem=send,
        recv_sem=recv,
        device_id=(ctx, fsdp),
        device_id_type=pl.DeviceIdType.MESH,
    )


def greet_plane(contexts):
    own = lax.axis_index("ctx")
    _, _, y, k = place()
    barrier = pltpu.get_barrier_semaphore()
    for ctx in range(contexts):
        for core in range(2):

            @pl.when(jnp.logical_or(ctx != own, core != k))
            def _():
                pl.semaphore_signal(barrier, inc=1, device_id=(ctx, 2 * y + core), device_id_type=pl.DeviceIdType.MESH)

    return barrier, 2 * contexts - 1


def greet_packs():
    own = lax.axis_index("ctx")
    _, _, y, k = place()
    barrier = pltpu.get_barrier_semaphore()
    for fsdp in (2 * y + 1 - k, 2 * (1 - y) + k, 2 * (1 - y) + 1 - k):
        pl.semaphore_signal(barrier, inc=1, device_id=(own, fsdp), device_id_type=pl.DeviceIdType.MESH)
    return barrier, 3


def attn_fwd_kernel(
    order, inv, x, small, w, cosine, sine, wo,
    n1s, qkv, o, lse, ob, hst, ub,
    n1own, n1r, osort, osend, orecv,
    n_send, n_recv, f_send, f_recv, o_send, o_recv,
):
    blocks, blk, _ = n1r.shape
    lanes = o.shape[1]
    seq = blocks * blk
    step = 2 * blk
    own = lax.axis_index("ctx")
    z, xx, y, k = place()
    depth = blocks // 2
    same = xx == k

    barrier, others = greet_plane(blocks)
    n1 = norm_low(x[...], small[0:1, :].astype(jnp.float32))
    n1own[0] = n1[:blk]
    n1own[1] = n1[blk:]
    pl.semaphore_wait(barrier, others)

    def n1_copy(zz):
        return remote(n1own.at[zz // 2], n1r.at[own], n_send.at[zz], n_recv.at[z], 2 * zz + k, 2 * y + xx)

    for zz in range(depth):
        alone = jnp.logical_and(same, zz == z)

        @pl.when(jnp.logical_not(alone))
        def _():
            n1_copy(zz).start()

        @pl.when(alone)
        def _():
            n1r[own] = n1own[zz // 2]

    def forward_copy(zz):
        slot = n1r.at[2 * zz + k]
        return remote(slot, slot, f_send.at[zz], f_recv.at[zz], own, 2 * y + 1 - k)

    for zz in range(depth):

        @pl.when(jnp.logical_not(jnp.logical_and(same, zz == z)))
        def _():
            remote(n1own.at[0], n1r.at[2 * zz + k], n_send.at[zz], n_recv.at[zz], 2 * zz + k, 2 * y + xx).wait_recv()

        forward_copy(zz).start()
    for zz in range(depth):
        slot = n1r.at[2 * zz + 1 - k]
        remote(slot, slot, f_send.at[zz], f_recv.at[zz], own, 2 * y + 1 - k).wait_recv()

    for b in range(blocks):
        n1s[b * blk : (b + 1) * blk, :] = n1r[inv[b]]
    for i in range(seq // step):
        part = slice(i * step, (i + 1) * step)
        out = nn(n1s[part, :], w[...])
        cos2 = jnp.concatenate([cosine[part, :]] * (lanes // 128), axis=1)
        sin2 = jnp.concatenate([sine[part, :]] * (lanes // 128), axis=1)
        q = spin(out[:, :lanes], cos2, sin2).astype(jnp.bfloat16)
        qkv[part, :lanes] = q * jnp.asarray(HEAD_DIM**-0.5, jnp.bfloat16)
        qkv[part, lanes : 2 * lanes] = spin(out[:, lanes : 2 * lanes], cos2, sin2).astype(jnp.bfloat16)
        qkv[part, 2 * lanes :] = out[:, 2 * lanes :].astype(jnp.bfloat16)
    lane = lax.broadcasted_iota(jnp.int32, (step, 128), 1)
    for i in range(seq // step):
        part = slice(i * step, (i + 1) * step)
        span = (i + 1) * step
        seen = lax.broadcasted_iota(jnp.int32, (step, span), 1) <= (
            lax.broadcasted_iota(jnp.int32, (step, span), 0) + i * step
        )
        logs = jnp.zeros((step, 128), jnp.float32)
        for head in range(GROUP_HEADS):
            tile, side = head // 2, head % 2
            at = tile * 128
            mine = lane // 64 == side
            q = jnp.where(mine, qkv[part, at : at + 128], jnp.asarray(0, jnp.bfloat16))
            s = nt(q, qkv[:span, lanes + at : lanes + at + 128])
            s = jnp.where(seen, s, -1e30)
            top = jnp.max(s, axis=1, keepdims=True)
            p = jnp.exp(s - top)
            total = jnp.sum(p, axis=1, keepdims=True)
            out = nn(p.astype(jnp.bfloat16), qkv[:span, 2 * lanes + at : 2 * lanes + at + 128]) / total
            logs = jnp.where(lane == head, top + jnp.log(total), logs)
            if side == 0:
                kept = jnp.where(mine, out, 0.0)
            else:
                kept = jnp.where(mine, out, kept)
            o[part, at : at + 128] = kept
        lse[part, :] = logs
        osort[2 * i] = o[part, :][:blk].astype(jnp.bfloat16)
        osort[2 * i + 1] = o[part, :][blk:].astype(jnp.bfloat16)

    mine_at = 2 * z + k

    def o_copy(ctx):
        return remote(osend.at[ctx], orecv.at[mine_at], o_send.at[ctx], o_recv.at[mine_at], ctx, 2 * y + xx)

    for ctx in range(blocks):
        alone = jnp.logical_and(same, ctx == own)
        osend[ctx] = osort[order[ctx]]

        @pl.when(jnp.logical_not(alone))
        def _():
            o_copy(ctx).start()

        @pl.when(alone)
        def _():
            orecv[mine_at] = osend[ctx]

    for src in range(blocks):

        @pl.when(jnp.logical_not(jnp.logical_and(same, src == mine_at)))
        def _():
            remote(osend.at[0], orecv.at[src], o_send.at[0], o_recv.at[src], 2 * (src // 2) + k, 2 * y + src % 2).wait_recv()

    ob[...] = orecv[...]
    total, low = post_attention(orecv[...], x[...], wo[...], small[1:2, :].astype(jnp.float32))
    hst[...] = total
    ub[...] = low
    for zz in range(depth):

        @pl.when(jnp.logical_not(jnp.logical_and(same, zz == z)))
        def _():
            n1_copy(zz).wait_send()

        forward_copy(zz).wait_send()
    for ctx in range(blocks):

        @pl.when(jnp.logical_not(jnp.logical_and(same, ctx == own)))
        def _():
            o_copy(ctx).wait_send()


def attn_forward(order, inv, x, small, w, cosine, sine, wo, number):
    count, width = x.shape
    blocks, blk = order.shape[0], count // 2
    lanes = w.shape[1] // 3
    seq = blocks * blk
    vm = pl.BlockSpec(memory_space=pltpu.VMEM)
    sm = pl.BlockSpec(memory_space=pltpu.SMEM)
    bf = jnp.bfloat16
    dma = pltpu.SemaphoreType.DMA
    return pl.pallas_call(
        attn_fwd_kernel,
        out_shape=[
            shape_of((seq, width), bf),
            shape_of((seq, 3 * lanes), bf),
            shape_of((seq, lanes), jnp.float32),
            shape_of((seq, 128), jnp.float32),
            shape_of((blocks, blk, lanes), bf),
            shape_of((count, width), jnp.float32),
            shape_of((count, width), bf),
        ],
        in_specs=[sm] * 2 + [vm] * 6,
        out_specs=[vm] * 7,
        scratch_shapes=[
            pltpu.VMEM((2, blk, width), bf),
            pltpu.VMEM((blocks, blk, width), bf),
            pltpu.VMEM((blocks, blk, lanes), bf),
            pltpu.VMEM((blocks, blk, lanes), bf),
            pltpu.VMEM((blocks, blk, lanes), bf),
        ]
        + [dma((blocks // 2,))] * 4
        + [dma((blocks,))] * 2,
        compiler_params=params_of(collective_id=number, has_side_effects=True),
        name="attn_fwd",
    )(order, inv, x, small, w, cosine, sine, wo)


def attn_bwd_kernel(
    order, inv, n1s, w, cosine, sine, qkv, o, lse, go, ghst, x, small,
    gx, gm, ggain, gw,
    gor, gos, grads, acc, keep, sib_out, sib_in, gn_out, gnr,
    o_send, o_recv, s_send, s_recv, g_send, g_recv,
):
    blocks, blk, width = grads.shape
    lanes = o.shape[1]
    seq = blocks * blk
    step = 2 * blk
    zero = jnp.asarray(0, jnp.bfloat16)
    own = lax.axis_index("ctx")
    z, xx, y, k = place()
    depth = blocks // 2
    same = xx == k

    barrier, others = greet_plane(blocks)
    acc[...] = jnp.zeros_like(acc)
    pl.semaphore_wait(barrier, others)

    def go_copy(unit):
        return remote(go.at[unit], gor.at[own], o_send.at[unit], o_recv.at[own], 2 * (unit // 2) + k, 2 * y + unit % 2)

    for unit in range(blocks):
        alone = jnp.logical_and(same, unit == 2 * z + k)

        @pl.when(jnp.logical_not(alone))
        def _():
            go_copy(unit).start()

        @pl.when(alone)
        def _():
            gor[own] = go[unit]

    for ctx in range(blocks):

        @pl.when(jnp.logical_not(jnp.logical_and(same, ctx == own)))
        def _():
            remote(go.at[0], gor.at[ctx], o_send.at[0], o_recv.at[ctx], ctx, 2 * y + xx).wait_recv()

    for b in range(blocks):
        gos[b * blk : (b + 1) * blk, :] = gor[inv[b]]
    lane = lax.broadcasted_iota(jnp.int32, (step, 128), 1)
    for i in range(seq // step):
        part = slice(i * step, (i + 1) * step)
        span = (i + 1) * step
        seen = lax.broadcasted_iota(jnp.int32, (step, span), 1) <= (
            lax.broadcasted_iota(jnp.int32, (step, span), 0) + i * step
        )
        key_lane = lax.broadcasted_iota(jnp.int32, (span, 128), 1)
        for head in range(GROUP_HEADS):
            tile, side = head // 2, head % 2
            at = tile * 128
            mine = lane // 64 == side
            q = jnp.where(mine, qkv[part, at : at + 128], zero)
            g = jnp.where(mine, gos[part, at : at + 128], zero)
            keys = qkv[:span, lanes + at : lanes + at + 128]
            values = qkv[:span, 2 * lanes + at : 2 * lanes + at + 128]
            delta = jnp.sum(g.astype(jnp.float32) * o[part, at : at + 128], axis=1, keepdims=True)
            s = nt(q, keys)
            p = jnp.where(seen, jnp.exp(jnp.where(seen, s, -1e30) - lse[part, head : head + 1]), 0.0)
            ds = (p * (nt(g, values) - delta)).astype(jnp.bfloat16)
            acc[:span, 2 * lanes + at : 2 * lanes + at + 128] += tn(p.astype(jnp.bfloat16), g)
            acc[:span, lanes + at : lanes + at + 128] += tn(ds, q)
            acc[part, at : at + 128] += nn(ds, jnp.where(key_lane // 64 == side, keys, zero))
    for b in range(blocks):
        part = slice(b * blk, (b + 1) * blk)
        cos2 = jnp.concatenate([cosine[part, :]] * (lanes // 128), axis=1)
        sin2 = jnp.concatenate([sine[part, :]] * (lanes // 128), axis=1)
        grads[b, :, :lanes] = spin(acc[part, :lanes] * HEAD_DIM**-0.5, cos2, -sin2).astype(jnp.bfloat16)
        grads[b, :, lanes : 2 * lanes] = spin(acc[part, lanes : 2 * lanes], cos2, -sin2).astype(jnp.bfloat16)
        grads[b, :, 2 * lanes :] = acc[part, 2 * lanes :].astype(jnp.bfloat16)

    def sib_copy(zz):
        return remote(sib_out.at[zz], sib_in.at[zz], s_send.at[zz], s_recv.at[zz], own, 2 * y + 1 - k)

    def gn_copy(zz):
        return remote(gn_out.at[zz], gnr.at[z], g_send.at[zz], g_recv.at[z], 2 * zz + k, 2 * y + xx)

    for zz in range(depth):
        sib_out[zz] = nt(grads[order[2 * zz + 1 - k]], w[...]).astype(jnp.bfloat16)
        sib_copy(zz).start()
    for zz in range(depth):
        keep[zz] = nt(grads[order[2 * zz + k]], w[...])
    for zz in range(depth):
        sib_copy(zz).wait_recv()
        alone = jnp.logical_and(same, zz == z)
        gn_out[zz] = (keep[zz] + sib_in[zz].astype(jnp.float32)).astype(jnp.bfloat16)

        @pl.when(jnp.logical_not(alone))
        def _():
            gn_copy(zz).start()

        @pl.when(alone)
        def _():
            gnr[z] = gn_out[zz]

    for i in range(width // 256):
        part = slice(i * 256, (i + 1) * 256)
        total = jnp.zeros((256, 3 * lanes), jnp.float32)
        gw[part, :] = tn(n1s[:, part], grads[...].reshape(seq, 3 * lanes)).astype(jnp.bfloat16)
    for zz in range(depth):

        @pl.when(jnp.logical_not(jnp.logical_and(same, zz == z)))
        def _():
            remote(gn_out.at[0], gnr.at[zz], g_send.at[0], g_recv.at[zz], 2 * zz + k, 2 * y + xx).wait_recv()

    halves = []
    for h in range(2):
        total = gnr[h * (depth // 2)].astype(jnp.float32)
        for zz in range(1, depth // 2):
            total = total + gnr[h * (depth // 2) + zz].astype(jnp.float32)
        halves.append(total)
    gn = jnp.concatenate(halves, axis=0)
    values = x[...]
    factor = rms_factor(values)
    base = values * factor
    gb = gn * small[0:1, :].astype(jnp.float32)
    grad = ghst[...] + factor * (gb - base * jnp.mean(gb * base, axis=-1, keepdims=True))
    gx[...] = grad
    gm[...] = grad.astype(jnp.bfloat16)
    ggain[...] = jnp.sum(gn * base, axis=0, keepdims=True)
    for unit in range(blocks):

        @pl.when(jnp.logical_not(jnp.logical_and(same, unit == 2 * z + k)))
        def _():
            go_copy(unit).wait_send()

    for zz in range(depth):
        sib_copy(zz).wait_send()

        @pl.when(jnp.logical_not(jnp.logical_and(same, zz == z)))
        def _():
            gn_copy(zz).wait_send()


def attn_backward(order, inv, n1s, w, cosine, sine, qkv, o, lse, go, ghst, x, small, number):
    blocks, blk, lanes = go.shape
    seq, width = n1s.shape
    count = x.shape[0]
    depth = blocks // 2
    vm = pl.BlockSpec(memory_space=pltpu.VMEM)
    sm = pl.BlockSpec(memory_space=pltpu.SMEM)
    bf = jnp.bfloat16
    dma = pltpu.SemaphoreType.DMA
    return pl.pallas_call(
        attn_bwd_kernel,
        out_shape=[
            shape_of((count, width), jnp.float32),
            shape_of((count, width), bf),
            shape_of((1, width), jnp.float32),
            shape_of((width, 3 * lanes), bf),
        ],
        in_specs=[sm] * 2 + [vm] * 11,
        out_specs=[vm] * 4,
        scratch_shapes=[
            pltpu.VMEM((blocks, blk, lanes), bf),
            pltpu.VMEM((seq, lanes), bf),
            pltpu.VMEM((blocks, blk, 3 * lanes), bf),
            pltpu.VMEM((seq, 3 * lanes), jnp.float32),
            pltpu.VMEM((depth, blk, width), jnp.float32),
            pltpu.VMEM((depth, blk, width), bf),
            pltpu.VMEM((depth, blk, width), bf),
            pltpu.VMEM((depth, blk, width), bf),
            pltpu.VMEM((depth, blk, width), bf),
        ]
        + [dma((blocks,))] * 2
        + [dma((depth,))] * 4,
        compiler_params=params_of(collective_id=number, has_side_effects=True),
        name="attn_bwd",
    )(order, inv, n1s, w, cosine, sine, qkv, o, lse, go, ghst, x, small)


def routing(raw, before, routes):
    count = raw.shape[1]
    ids = lax.broadcasted_iota(jnp.int32, (16, count), 0)
    logits = raw + before
    first, second = ids == routes[0:1], ids == routes[1:2]
    z0 = jnp.sum(jnp.where(first, logits, 0.0), axis=0, keepdims=True)
    z1 = jnp.sum(jnp.where(second, logits, 0.0), axis=0, keepdims=True)
    top = jnp.maximum(z0, z1)
    e0, e1 = jnp.exp(z0 - top), jnp.exp(z1 - top)
    total = e0 + e1
    coef = jnp.where(first, e0 / total, 0.0) + jnp.where(second, e1 / total, 0.0)
    hits = jnp.where(first | second, 1.0, 0.0)
    upto = lax.broadcasted_iota(jnp.int32, (count, count), 0) <= lax.broadcasted_iota(jnp.int32, (count, count), 1)
    place = nn(hits.astype(jnp.bfloat16), jnp.where(upto, 1.0, 0.0).astype(jnp.bfloat16)) - 1.0
    slot = jnp.where(hits > 0, place, -1.0)
    return jnp.concatenate([raw, coef, slot[:NF], logits], axis=0)


def one_hot(slot):
    count = slot.shape[1]
    ids = lax.broadcasted_iota(jnp.int32, (NF, MOST, count), 1)
    hit = ids == slot.astype(jnp.int32)[:, None, :]
    return jnp.where(hit, 1.0, 0.0).reshape(NF * MOST, count)


def slot_values(hot, rows):
    count = rows.shape[1]
    wide = jnp.broadcast_to(rows[:, None, :], (NF, MOST, count)).reshape(NF * MOST, count)
    return jnp.sum(hot * wide, axis=1, keepdims=True)


def swap_rows(own, rows, send, recv, forward_send, forward_recv):
    ctx = lax.axis_index("ctx")
    _, _, y, k = place()
    beside, across = 2 * y + 1 - k, 2 * (1 - y) + k
    far = remote(own, rows.at[2], send.at[0], recv.at[0], ctx, across)
    near = remote(own, rows.at[1], send.at[1], recv.at[1], ctx, beside)
    onward = remote(rows.at[2], rows.at[3], forward_send, forward_recv, ctx, beside)
    far.start()
    near.start()
    return near, far, onward


def sum_rows(parts, beside_in, mid, across_in, send, recv):
    ctx = lax.axis_index("ctx")
    _, _, y, k = place()
    beside, across = 2 * y + 1 - k, 2 * (1 - y) + k
    first = remote(parts.at[3], beside_in.at[1], send.at[0], recv.at[0], ctx, beside)
    second = remote(parts.at[1], beside_in.at[0], send.at[1], recv.at[1], ctx, beside)
    third = remote(mid, across_in, send.at[2], recv.at[2], ctx, across)
    return first, second, third


def ffn_fwd_kernel(
    ub, hst, small, routes, before, wgu, wd,
    ubf, table, ext, x_next,
    rows_s, hot_s, x_s, y_s, coef_s, parts, beside_in, mid, across_in,
    a_send, a_recv, r_send, r_recv,
):
    e = pl.program_id(0)
    packs = ubf.shape[0]
    count, width = ub.shape
    router = small[2 + NC :, :]

    def gathers():
        return swap_rows(ub, rows_s, a_send, a_recv, a_send.at[2], a_recv.at[2])

    def sums():
        return sum_rows(parts, beside_in, mid, across_in, r_send, r_recv)

    @pl.when(e == 0)
    def _():
        barrier, others = greet_packs()
        rows_s[0] = ub[...]

        def prepare(d):
            rows = routing(nt(router, rows_s[d]), before[d], routes[d])
            table[d] = rows
            hot = one_hot(rows[SLOT : SLOT + NF])
            coef_s[d] = slot_values(hot, rows[COEF : COEF + NF])
            hot_low = hot.astype(jnp.bfloat16)
            hot_s[d] = hot_low
            x = nn(hot_low, rows_s[d]).astype(jnp.bfloat16)
            for n in range(NF):
                x_s[n, d * MOST : (d + 1) * MOST, :] = x[n * MOST : (n + 1) * MOST]

        pl.semaphore_wait(barrier, others)
        near, far, onward = gathers()
        prepare(0)
        near.wait_recv()
        prepare(1)
        far.wait_recv()
        onward.start()
        prepare(2)
        onward.wait_recv()
        prepare(3)
        ubf[...] = rows_s[...]
        ext[:count, :] = ub[...]
        rows = table[0]
        ext[count:, :] = jnp.zeros((16, width), jnp.bfloat16)
        ext[count:, :count] = rows[COEF : COEF + 16].astype(jnp.bfloat16)
        slots = jnp.concatenate([rows[SLOT : SLOT + NF], jnp.zeros((16 - NF, count), jnp.float32)], axis=0)
        ext[count:, count : 2 * count] = slots.astype(jnp.bfloat16)
        near.wait_send()
        far.wait_send()
        onward.wait_send()

    x = x_s[e]
    gate, up = nn(x, wgu[0, 0, 0]), nn(x, wgu[0, 0, 1])
    hid = (gate * jax.nn.sigmoid(gate) * up).astype(jnp.bfloat16)
    out = nn(hid, wd[0, 0])
    at = pl.ds(pl.multiple_of(e * MOST, MOST), MOST)
    for d in range(packs):
        y_s[d, at, :] = (out[d * MOST : (d + 1) * MOST] * coef_s[d, at, :]).astype(jnp.bfloat16)

    @pl.when(e == NF - 1)
    def _():
        first, second, third = sums()
        parts[3] = tn(hot_s[3], y_s[3]).astype(jnp.bfloat16)
        first.start()
        parts[1] = tn(hot_s[1], y_s[1]).astype(jnp.bfloat16)
        second.start()
        away = tn(hot_s[2], y_s[2])
        first.wait_recv()
        mid[...] = (away + beside_in[1].astype(jnp.float32)).astype(jnp.bfloat16)
        third.start()
        home = tn(hot_s[0], y_s[0])
        _, _, scale_u, scale_c = mixing_rows(table[0])
        columns = to_columns([scale_u] + scale_c)
        values = hst[...]
        moe = home + columns[0] * ((values * rms_factor(values)) * small[1:2, :].astype(jnp.float32))
        for c in range(NC):
            moe = moe + columns[1 + c] * small[2 + c : 3 + c, :].astype(jnp.float32)
        second.wait_recv()
        moe = moe + beside_in[0].astype(jnp.float32)
        third.wait_recv()
        x_next[...] = values + (moe + across_in[...].astype(jnp.float32))
        first.wait_send()
        second.wait_send()
        third.wait_send()


def whole_spec(dims):
    return pl.BlockSpec(dims, lambda *_: (0,) * len(dims))


def exchange_scratch(packs, count, width):
    bf = jnp.bfloat16
    return [
        pltpu.VMEM((packs, count, width), bf),
        pltpu.VMEM((2, count, width), bf),
        pltpu.VMEM((count, width), bf),
        pltpu.VMEM((count, width), bf),
    ]


def ffn_forward(layer, ub, hst, small, routes, before, wgu, wd, number):
    count, width = ub.shape
    packs = routes.shape[0]
    hidden = wd.shape[2]
    bf = jnp.bfloat16
    outs = [
        shape_of((packs, count, width), bf),
        shape_of((packs, ROUT, count), jnp.float32),
        shape_of((count + 16, width), bf),
        shape_of((count, width), jnp.float32),
    ]
    return pl.pallas_call(
        ffn_fwd_kernel,
        grid=(NF,),
        out_shape=outs,
        in_specs=[whole_spec(a.shape) for a in (ub, hst, small, routes, before)]
        + [
            pl.BlockSpec((1, 1, 2, width, hidden), lambda e: (layer, e, 0, 0, 0)),
            pl.BlockSpec((1, 1, hidden, width), lambda e: (layer, e, 0, 0)),
        ],
        out_specs=[whole_spec(a.shape) for a in outs],
        scratch_shapes=[
            pltpu.VMEM((packs, count, width), bf),
            pltpu.VMEM((packs, NF * MOST, count), bf),
            pltpu.VMEM((NF, packs * MOST, width), bf),
            pltpu.VMEM((packs, NF * MOST, width), bf),
            pltpu.VMEM((packs, NF * MOST, 1), jnp.float32),
        ]
        + exchange_scratch(packs, count, width)
        + [pltpu.SemaphoreType.DMA((3,))] * 4,
        compiler_params=params_of(collective_id=number, has_side_effects=True),
        name="ffn_fwd",
    )(ub, hst, small, routes, before, wgu, wd)


def silu_parts(gate, up, ghid):
    sig = jax.nn.sigmoid(gate)
    act = gate * sig
    dg = (ghid * up * sig * (1.0 + gate * (1.0 - sig))).astype(jnp.bfloat16)
    du = (ghid * act).astype(jnp.bfloat16)
    return act * up, dg, du


def ffn_bwd_kernel(
    gm, gx, ubf, table, hst, small, routes, gprev, wo, ob, wgu, wd,
    ghst, go, gwo, gsmall, glog,
    rows_s, hot_s, x_s, g_s, y_s, coef_s, gc_s, gcoef, gcoef_in, parts, beside_in, mid, across_in,
    a_send, a_recv, r_send, r_recv, c_send, c_recv,
):
    e = pl.program_id(0)
    packs = ubf.shape[0]
    ctx = lax.axis_index("ctx")
    _, _, y, k = place()
    peers = [None, 2 * y + 1 - k, 2 * (1 - y) + k, 2 * (1 - y) + 1 - k]

    def gathers():
        return swap_rows(gm, rows_s, a_send, a_recv, a_send.at[2], a_recv.at[2])

    def sums():
        return sum_rows(parts, beside_in, mid, across_in, r_send, r_recv)

    @pl.when(e == 0)
    def _():
        barrier, others = greet_packs()
        rows_s[0] = gm[...]

        def prepare(d):
            hot = one_hot(table[d, SLOT : SLOT + NF, :])
            coef_s[d] = slot_values(hot, table[d, COEF : COEF + NF, :])
            hot_low = hot.astype(jnp.bfloat16)
            hot_s[d] = hot_low
            x = nn(hot_low, ubf[d]).astype(jnp.bfloat16)
            for n in range(NF):
                x_s[n, d * MOST : (d + 1) * MOST, :] = x[n * MOST : (n + 1) * MOST]

        def spread(d):
            g = nn(hot_s[d], rows_s[d]).astype(jnp.bfloat16)
            for n in range(NF):
                g_s[n, d * MOST : (d + 1) * MOST, :] = g[n * MOST : (n + 1) * MOST]

        pl.semaphore_wait(barrier, others)
        near, far, onward = gathers()
        for d in range(packs):
            prepare(d)
        spread(0)
        near.wait_recv()
        far.wait_recv()
        onward.start()
        spread(1)
        spread(2)
        onward.wait_recv()
        spread(3)
        near.wait_send()
        far.wait_send()
        onward.wait_send()

    x = x_s[e]
    at = pl.ds(pl.multiple_of(e * MOST, MOST), MOST)
    coef = jnp.concatenate([coef_s[d, at, :] for d in range(packs)], axis=0)
    gate, up = nn(x, wgu[0, 0, 0]), nn(x, wgu[0, 0, 1])
    ghid = nt(g_s[e], wd[0, 0])
    hid, dg, du = silu_parts(gate, up, ghid * coef)
    dots = jnp.sum(hid * ghid, axis=1, keepdims=True)
    out = nt(dg, wgu[0, 0, 0]) + nt(du, wgu[0, 0, 1])
    for d in range(packs):
        y_s[d, at, :] = out[d * MOST : (d + 1) * MOST].astype(jnp.bfloat16)
        gc_s[d, at, :] = dots[d * MOST : (d + 1) * MOST]

    @pl.when(e == NF - 1)
    def _():
        first, second, third = sums()

        def coef_copy(d):
            return remote(gcoef.at[d], gcoef_in.at[d - 1], c_send.at[d - 1], c_recv.at[d - 1], ctx, peers[d])

        parts[3] = tn(hot_s[3], y_s[3]).astype(jnp.bfloat16)
        first.start()
        parts[1] = tn(hot_s[1], y_s[1]).astype(jnp.bfloat16)
        second.start()
        for d in range(packs):
            wide = hot_s[d].astype(jnp.float32) * gc_s[d]
            gcoef[d] = jnp.sum(wide.reshape(NF, MOST, wide.shape[1]), axis=1)
            if d > 0:
                coef_copy(d).start()
        away = tn(hot_s[2], y_s[2])
        first.wait_recv()
        mid[...] = (away + beside_in[1].astype(jnp.float32)).astype(jnp.bfloat16)
        third.start()
        home = tn(hot_s[0], y_s[0])
        second.wait_recv()
        home = home + beside_in[0].astype(jnp.float32)
        total = gcoef[0]
        for d in range(1, packs):
            coef_copy(d).wait_recv()
            total = total + gcoef_in[d - 1]
        third.wait_recv()
        home = home + across_in[...].astype(jnp.float32)
        results = middle(
            gx[...], home, total, table[0], routes[...], gprev[...], hst[...], ubf[0],
            small[...], wo[...], ob[...],
        )
        for ref, value in zip((ghst, go, gwo, gsmall, glog), results):
            ref[...] = value
        first.wait_send()
        second.wait_send()
        third.wait_send()
        for d in range(1, packs):
            coef_copy(d).wait_send()


def ffn_backward(layer, gm, gx, ubf, table, hst, small, routes, gprev, wo, ob, wgu, wd, number):
    packs, count, width = ubf.shape
    hidden = wd.shape[2]
    bf, f32 = jnp.bfloat16, jnp.float32
    outs = [
        shape_of((count, width), f32),
        shape_of(ob.shape, bf),
        shape_of((width, width), bf),
        shape_of((1 + NC + 16, width), f32),
        shape_of((16, count), f32),
    ]
    args = (gm, gx, ubf, table, hst, small, routes, gprev, wo, ob)
    dma = pltpu.SemaphoreType.DMA
    return pl.pallas_call(
        ffn_bwd_kernel,
        grid=(NF,),
        out_shape=outs,
        in_specs=[whole_spec(a.shape) for a in args]
        + [
            pl.BlockSpec((1, 1, 2, width, hidden), lambda e: (layer, e, 0, 0, 0)),
            pl.BlockSpec((1, 1, hidden, width), lambda e: (layer, e, 0, 0)),
        ],
        out_specs=[whole_spec(a.shape) for a in outs],
        scratch_shapes=[
            pltpu.VMEM((packs, count, width), bf),
            pltpu.VMEM((packs, NF * MOST, count), bf),
            pltpu.VMEM((NF, packs * MOST, width), bf),
            pltpu.VMEM((NF, packs * MOST, width), bf),
            pltpu.VMEM((packs, NF * MOST, width), bf),
            pltpu.VMEM((packs, NF * MOST, 1), f32),
            pltpu.VMEM((packs, NF * MOST, 1), f32),
            pltpu.VMEM((packs, NF, count), f32),
            pltpu.VMEM((packs - 1, NF, count), f32),
        ]
        + exchange_scratch(packs, count, width)
        + [dma((3,))] * 6,
        compiler_params=params_of(collective_id=number, has_side_effects=True),
        name="ffn_bwd",
    )(*args, wgu, wd)


def dispatch_kernel(ext, gm, x, g):
    count = gm.shape[1]
    rows = ext[0, count:, :].astype(jnp.float32)
    coef, slot = rows[:NF, :count], rows[:NF, count : 2 * count].astype(jnp.int32)
    ids = lax.broadcasted_iota(jnp.int32, (NF, MOST, count), 1)
    hit = ids == slot[:, None, :]
    hot = jnp.where(hit, 1.0, 0.0).astype(jnp.bfloat16).reshape(NF * MOST, count)
    weighted = jnp.where(hit, coef[:, None, :], 0.0).astype(jnp.bfloat16).reshape(NF * MOST, count)
    x[...] = nn(hot, ext[0, :count, :]).astype(jnp.bfloat16).reshape(x.shape)
    g[...] = nn(weighted, gm[0]).astype(jnp.bfloat16).reshape(g.shape)


def dispatch(ext, gm):
    devices, count, width = gm.shape
    grouped = pl.BlockSpec((NF, 1, MOST, width), lambda d: (0, d, 0, 0))
    outs = shape_of((NF, devices, MOST, width), jnp.bfloat16)
    return pl.pallas_call(
        dispatch_kernel,
        grid=(devices,),
        out_shape=[outs, outs],
        in_specs=[
            pl.BlockSpec((1,) + ext.shape[1:], lambda d: (d, 0, 0)),
            pl.BlockSpec((1, count, width), lambda d: (d, 0, 0)),
        ],
        out_specs=[grouped, grouped],
        compiler_params=params_of(),
        name="dispatch",
    )(ext, gm)


def dw_kernel(*refs):
    x, g, wgu, wd, dgu, dd, dg_s, du_s, hid_s = refs[:4] + refs[-5:]
    rows = x.shape[1]
    chunk = 256

    def pieces(i, _):
        part = pl.ds(pl.multiple_of(i * chunk, chunk), chunk)
        xs = x[0, part, :]
        hid, dg, du = silu_parts(nn(xs, wgu[0, 0, 0]), nn(xs, wgu[0, 0, 1]), nt(g[0, part, :], wd[0, 0]))
        hid_s[part, :] = hid.astype(jnp.bfloat16)
        dg_s[part, :] = dg
        du_s[part, :] = du
        return 0

    lax.fori_loop(0, rows // chunk, pieces, 0)

    def first(i, _):
        part = pl.ds(pl.multiple_of(i * 256, 256), 256)
        xs = x[0, :, part]
        dgu[0, 0, 0, part, :] = tn(xs, dg_s[...])
        dgu[0, 0, 1, part, :] = tn(xs, du_s[...])
        return 0

    lax.fori_loop(0, x.shape[2] // 256, first, 0)

    def second(i, _):
        part = pl.ds(pl.multiple_of(i * 256, 256), 256)
        dd[0, 0, part, :] = tn(hid_s[:, part], g[0])
        return 0

    lax.fori_loop(0, hid_s.shape[1] // 256, second, 0)


def weight_grads(layer, x, g, wgu, wd, earlier):
    _, rows, width = x.shape
    hidden = wd.shape[2]
    gu_spec = pl.BlockSpec((1, 1, 2, width, hidden), lambda e: (layer, e, 0, 0, 0))
    d_spec = pl.BlockSpec((1, 1, hidden, width), lambda e: (layer, e, 0, 0))
    row_spec = pl.BlockSpec((1, rows, width), lambda e: (e, 0, 0))
    kernel = dw_kernel
    return pl.pallas_call(
        kernel,
        grid=(NF,),
        out_shape=[shape_of(wgu.shape, jnp.float32), shape_of(wd.shape, jnp.float32)],
        in_specs=[row_spec, row_spec, gu_spec, d_spec] + [pl.BlockSpec(memory_space=pl.ANY)] * len(earlier),
        out_specs=[gu_spec, d_spec],
        input_output_aliases={4 + i: i for i in range(len(earlier))},
        scratch_shapes=[pltpu.VMEM((rows, hidden), jnp.bfloat16)] * 3,
        compiler_params=params_of(),
        name="weight_grads",
    )(x, g, wgu, wd, *earlier)


def norm_low(x, gain):
    return ((x * rms_factor(x)) * gain).astype(jnp.bfloat16)


def post_attention(ob, x, wo, gain):
    groups = wo.shape[0]
    inner = wo.shape[1]
    blk = ob.shape[1]
    halves = []
    for h in range(2):
        total = x[h * blk : (h + 1) * blk]
        for g in range(groups):
            total = total + nn(ob[h * groups + g][:, :inner], wo[g])
        halves.append(total)
    hst = jnp.concatenate(halves, axis=0)
    return hst, norm_low(hst, gain)


def mixing_rows(table):
    raw, coef = table[RAW : RAW + 16], table[COEF : COEF + 16]
    pairs = []
    for c in range(NC):
        r0, r1 = raw[NE + 2 * c : NE + 2 * c + 1], raw[NE + 2 * c + 1 : NE + 2 * c + 2]
        top = jnp.maximum(r0, r1)
        e0, e1 = jnp.exp(r0 - top), jnp.exp(r1 - top)
        pairs.append((e0 / (e0 + e1), e1 / (e0 + e1)))
    shares = [coef[NF + 2 + c : NF + 3 + c] for c in range(NC)]
    scale_u = coef[NF + 1 : NF + 2]
    for c in range(NC):
        scale_u = scale_u + shares[c] * pairs[c][0]
    return pairs, shares, scale_u, [shares[c] * pairs[c][1] for c in range(NC)]


def middle(gx, parts, gcoef, table, routes, gprev, hst, ub, small, wo, ob):
    groups = wo.shape[0]
    inner = wo.shape[1]
    blk = ob.shape[1]
    gain = small[1:2].astype(jnp.float32)
    consts = small[2 : 2 + NC].astype(jnp.float32)
    router = small[2 + NC :]
    pairs, shares, scale_u, scale_c = mixing_rows(table)
    columns = to_columns([scale_u] + scale_c)
    factor = rms_factor(hst)
    base = hst * factor
    u = base * gain
    dots = [jnp.sum(gx * u, axis=1, keepdims=True)]
    dots += [jnp.sum(gx * consts[c : c + 1], axis=1, keepdims=True) for c in range(NC)]
    dots = to_rows(dots, 8)
    dot_u = dots[0:1]
    dot_c = [dots[1 + c : 2 + c] for c in range(NC)]
    ids = lax.broadcasted_iota(jnp.int32, (16, gx.shape[0]), 0)
    grads = jnp.concatenate([gcoef, jnp.zeros_like(gcoef)], axis=0)
    grads = jnp.where(ids == NF + 1, dot_u, grads)
    raw_rows = []
    for c in range(NC):
        a0, a1 = pairs[c]
        grads = jnp.where(ids == NF + 2 + c, a0 * dot_u + a1 * dot_c[c], grads)
        g0, g1 = shares[c] * dot_u, shares[c] * dot_c[c]
        both = a0 * g0 + a1 * g1
        raw_rows += [a0 * (g0 - both), a1 * (g1 - both)]
    logits = table[LOGI : LOGI + 16]
    first, second = ids == routes[0:1], ids == routes[1:2]

    def pick(chosen, rows):
        return jnp.sum(jnp.where(chosen, rows, 0.0), axis=0, keepdims=True)

    z0, z1 = pick(first, logits), pick(second, logits)
    top = jnp.maximum(z0, z1)
    e0, e1 = jnp.exp(z0 - top), jnp.exp(z1 - top)
    w0, w1 = e0 / (e0 + e1), e1 / (e0 + e1)
    gg0, gg1 = pick(first, grads), pick(second, grads)
    both = w0 * gg0 + w1 * gg1
    glog = jnp.where(first, w0 * (gg0 - both), 0.0) + jnp.where(second, w1 * (gg1 - both), 0.0) + gprev
    graw = glog
    for index, row in enumerate(raw_rows):
        graw = jnp.where(ids == NE + index, row, graw)
    graw = graw.astype(jnp.bfloat16)
    grad_router = nn(graw, ub)
    gu = gx * columns[0] + tn(graw, router) + parts
    sums = [jnp.sum(gu * base, axis=0, keepdims=True)]
    sums += [jnp.sum(gx * columns[1 + c], axis=0, keepdims=True) for c in range(NC)]
    gb = gu * gain
    ghst = gx + factor * (gb - base * jnp.mean(gb * base, axis=-1, keepdims=True))
    gy = ghst.astype(jnp.bfloat16)
    lanes = ob.shape[2]
    go, gwo = [None] * (2 * groups), []
    for g in range(groups):
        value = nt(gy, wo[g]).astype(jnp.bfloat16)
        value = jnp.concatenate([value, jnp.zeros((value.shape[0], lanes - inner), jnp.bfloat16)], axis=1)
        for h in range(2):
            go[h * groups + g] = value[h * blk : (h + 1) * blk]
        mixed = jnp.concatenate([ob[g], ob[groups + g]], axis=0)
        gwo.append(tn(mixed, gy)[:inner].astype(jnp.bfloat16))
    return ghst, jnp.stack(go), jnp.concatenate(gwo, axis=0), jnp.concatenate(sums + [grad_router], axis=0), glog


def turn_tables(seq):
    half = HEAD_DIM // 2
    frequency = np.exp((-np.log(np.float32(10000.0)) * np.arange(half, dtype=np.float32) / np.float32(half)))
    angles = np.arange(seq, dtype=np.float32)[:, None] * frequency.astype(np.float32)[None, :]
    cosine, sine = np.cos(angles), np.sin(angles)
    cosine = np.concatenate([cosine, cosine] * 2, axis=1).astype(np.float32)
    sine = np.concatenate([-sine, sine] * 2, axis=1).astype(np.float32)
    return jnp.asarray(cosine), jnp.asarray(sine)


def by_heads(
    tokens,
    cotangent,
    seq_lengths,
    block_order,
    routes,
    gains,
    qkv_weights,
    out_weight,
    router,
    const_values,
    w_gate_up,
    w_down,
):
    count, width = tokens.shape[1], tokens.shape[2]
    ctx_size, packs = lax.axis_size("ctx"), lax.axis_size("fsdp")
    groups = ctx_size // 2
    blk = count // 2
    seq = blk * ctx_size
    pack = lax.axis_index("fsdp")
    z, xx, y, k = place()
    sequence = z // 2
    inner = GROUP_HEADS * HEAD_DIM
    lanes = -(-inner // 128) * 128
    shard = width // packs
    f32, bf = jnp.float32, jnp.bfloat16
    everyone = ("ctx", "fsdp")

    cosine, sine = turn_tables(seq)
    routes_t = jnp.swapaxes(routes[:, 0], 1, 2)
    ints = jnp.concatenate([routes_t.reshape(-1), block_order[0]])
    ints = jnp.pad(ints, (0, -ints.size % 1024)).reshape(-1, 128)
    ints = lax.all_gather(ints, "fsdp", axis=0, tiled=False).reshape(packs, -1)
    near = jnp.stack([pack, 2 * y + 1 - k, 2 * (1 - y) + k, 2 * (1 - y) + 1 - k])
    routes_f = ints[near][:, : routes_t.size].reshape((packs,) + routes_t.shape)
    order = lax.dynamic_index_in_dim(ints, 2 * y + xx, 0, keepdims=False)[routes_t.size : routes_t.size + 2 * ctx_size].reshape(ctx_size, 2)
    order = lax.dynamic_index_in_dim(order, sequence, 1, keepdims=False) - ctx_size * sequence
    ids = jnp.arange(ctx_size, dtype=jnp.int32)
    inv = jnp.sum(jnp.where(order[None, :] == ids[:, None], ids[None, :], 0), axis=1)

    smalls = jnp.concatenate([gains, const_values, jnp.swapaxes(router, 1, 2)], axis=1)
    per_layer = smalls.shape[1]
    smalls = lax.all_gather(smalls.reshape(LAYERS * per_layer, shard), "fsdp", axis=1, tiled=True)
    smalls = [smalls[l * per_layer : (l + 1) * per_layer] for l in range(LAYERS)]
    pairs = lax.dynamic_slice_in_dim(qkv_weights, 2 * inner * (z % 2), 2 * inner, axis=3)
    pairs = pairs.reshape(LAYERS, 3, shard, 2, inner)
    pairs = jnp.pad(pairs, ((0, 0),) * 4 + ((0, lanes - inner),))
    pairs = jnp.transpose(pairs, (0, 3, 2, 1, 4)).reshape(LAYERS, 2, shard, 3 * lanes)
    w_attn, w_out = [], []
    for l in range(LAYERS):
        send = jnp.concatenate([pairs[l], pairs[l]], axis=0)
        w_attn.append(lax.all_to_all(send, "fsdp", 0, 0).reshape(width, 3 * lanes))
        w_out.append(lax.all_gather(out_weight[l], "fsdp", axis=0, tiled=False))

    gm_all = [None, lax.all_gather(cotangent[0], everyone, axis=0, tiled=False)]
    x = tokens[0].astype(f32)
    before = jnp.zeros((packs, 16, count), f32)
    kept, ext_all = [], [None] * LAYERS
    for l in range(LAYERS):
        if l == 1:
            x, gm_all[1] = lax.optimization_barrier((x, gm_all[1]))
        n1s, qkv, o, lse, ob, hst, ub = attn_forward(order, inv, x, smalls[l], w_attn[l], cosine, sine, w_out[l], 2 * l)
        ubf, table, ext, x_next = ffn_forward(
            l, ub, hst, smalls[l], routes_f[:, l], before, w_gate_up, w_down, 2 * l + 1
        )
        before = table[:, LOGI : LOGI + 16]
        ext_all[l] = lax.all_gather(ext, everyone, axis=0, tiled=False)
        kept.append((x, n1s, qkv, o, lse, ob, hst, ubf, table))
        x = x_next
    output = x
    gm = cotangent[0]
    gx = gm.astype(f32)
    gprev = jnp.zeros((16, count), f32)
    small_grads, qkv_grads, out_grads = [None] * LAYERS, [None] * LAYERS, [None] * LAYERS
    for l in reversed(range(LAYERS)):
        x, n1s, qkv, o, lse, ob, hst, ubf, table = kept[l]
        number = 2 * LAYERS + 2 * l
        gm, ext_all[l - 1 if l else 1] = lax.optimization_barrier((gm, ext_all[l - 1 if l else 1]))
        ghst, go, gwo, small, gprev = ffn_backward(
            l, gm, gx, ubf, table, hst, smalls[l], routes_t[l], gprev, w_out[l], ob, w_gate_up, w_down, number
        )
        out_grads[l] = lax.psum_scatter(gwo, "fsdp", scatter_dimension=0, tiled=True)
        gx, gm, gain_grad, gw = attn_backward(
            order, inv, n1s, w_attn[l], cosine, sine, qkv, o, lse, go, ghst, x, smalls[l], number + 1
        )
        if l > 0:
            gm_all[l - 1] = lax.all_gather(gm, everyone, axis=0, tiled=False)
        small_grads[l] = jnp.concatenate([gain_grad, small], axis=0)
        gw = gw.reshape(width, 3, lanes)[:, :, :inner].reshape(width, 1, 3 * inner)
        gw = lax.dynamic_update_slice_in_dim(
            jnp.zeros((width, groups, 3 * inner), bf), gw, 2 * (z % 2) + k, axis=1
        ).reshape(width, 3 * width)
        qkv_grads[l] = lax.psum_scatter(gw, "fsdp", scatter_dimension=0, tiled=True)
    done = ()
    for l in reversed(range(LAYERS)):
        x_all, g_all = dispatch(ext_all[l], gm_all[l])
        rows = x_all.shape[1] * x_all.shape[2]
        done = weight_grads(l, x_all.reshape(NF, rows, width), g_all.reshape(NF, rows, width), w_gate_up, w_down, done)
    small = lax.psum(jnp.stack(small_grads).astype(bf), everyone)
    small = lax.dynamic_slice_in_dim(small, pack * shard, shard, axis=2).astype(f32)
    dense = jnp.concatenate([jnp.stack(qkv_grads), jnp.stack(out_grads)], axis=2)
    dense = lax.psum(dense, "ctx").astype(f32)
    qkv_sum = dense[:, :, : 3 * width].reshape(LAYERS, shard, groups, 3, inner)
    return (
        output[None],
        gx[None],
        small[:, :2],
        jnp.transpose(qkv_sum, (0, 3, 1, 2, 4)).reshape(LAYERS, 3, shard, width),
        dense[:, :, 3 * width :],
        jnp.swapaxes(small[:, 2 + NC :], 1, 2),
        small[:, 2 : 2 + NC],
        done[0],
        done[1],
    )


def solution(mesh):
    placed = (
        P("fsdp", "ctx", None),
        P("fsdp", "ctx", None),
        P("fsdp", None),
        P("fsdp", None),
        P(None, "fsdp", "ctx", None),
        P(None, None, "fsdp"),
        P(None, None, "fsdp", None),
        P(None, "fsdp", None),
        P(None, "fsdp", None),
        P(None, None, "fsdp"),
        P(None, None, None, None, "fsdp"),
        P(None, None, "fsdp", None),
    )
    contexts, packs = mesh.shape["ctx"], mesh.shape["fsdp"]
    blocks_of_heads = HEADS // GROUP_HEADS

    def plan(*args):
        tokens = args[0]
        even = tokens.shape[1] * contexts == 2 * MINLEN
        grouped = contexts == 2 * blocks_of_heads and packs == blocks_of_heads
        return (by_heads if even and grouped else shards)(*args)

    return jax.shard_map(
        plan,
        mesh=mesh,
        in_specs=placed,
        out_specs=(
            P("fsdp", "ctx", None),
            P("fsdp", "ctx", None),
            P(None, None, "fsdp"),
            P(None, None, "fsdp", None),
            P(None, "fsdp", None),
            P(None, "fsdp", None),
            P(None, None, "fsdp"),
            P(None, None, None, None, "fsdp"),
            P(None, None, "fsdp", None),
        ),
        check_vma=False,
    )
```

```python
import jax
import jax.numpy as jnp
import numpy as np
from jax import lax
from jax.experimental import pallas as pl
from jax.experimental.pallas import tpu as pltpu
from jax.sharding import PartitionSpec as P

HEADS = 12
HEAD_DIM = 64
NF = 8
NC = 2
LAYERS = 2
NE = 12
MOST = 64
GROUP_HEADS = 3


def from_behind(x, axis, by):
    devices = lax.axis_size(axis)
    return lax.ppermute(x, axis, [(i, (i + by) % devices) for i in range(devices)])


def layout_tables(lengths, order_row, tok_count):
    block_len = tok_count // 2
    pack_len = order_row.shape[0] * block_len
    pack_rows = jnp.arange(pack_len, dtype=jnp.int32)
    owner = pack_rows // tok_count
    which_half = pack_rows % tok_count // block_len
    block_ids = order_row[2 * owner + which_half]
    pack_pos = block_ids * block_len + pack_rows % block_len
    segment = (pack_pos >= lengths[0]).astype(jnp.int32)
    seq_pos = pack_pos - segment * lengths[0]
    return (pack_pos, segment, seq_pos)


def angle_tables(seq_pos, head_size):
    half_size = head_size // 2
    frequency = jnp.exp(-jnp.log(10000.0) * jnp.arange(half_size, dtype=jnp.float32) / half_size)
    angles = seq_pos.astype(jnp.float32)[:, None] * frequency[None, :]
    return (jnp.cos(angles)[:, None, :], jnp.sin(angles)[:, None, :])


def rotate_pairs(values, cosine_table, sine_table, direction):
    half_size = values.shape[-1] // 2
    first_half = values[..., :half_size]
    second_half = values[..., half_size:]
    return jnp.concatenate(
        [
            first_half * cosine_table - direction * second_half * sine_table,
            second_half * cosine_table + direction * first_half * sine_table,
        ],
        axis=-1,
    )


def rms_parts(values):
    inverse = lax.rsqrt(jnp.mean(values * values, axis=-1, keepdims=True) + 1e-06)
    return (values * inverse, inverse)


def rms_back(grad_normed, base_values, inverse):
    return inverse * (
        grad_normed - base_values * jnp.mean(grad_normed * base_values, axis=-1, keepdims=True)
    )


def expert_forward(inputs_low, gate_up_use, down_use):
    gate_up_out = jnp.einsum(
        "emd,ecdf->ecmf", inputs_low, gate_up_use, preferred_element_type=jnp.float32
    )
    hidden_low = (jax.nn.silu(gate_up_out[:, 0]) * gate_up_out[:, 1]).astype(jnp.bfloat16)
    partial_value = jnp.einsum(
        "emf,efd->emd", hidden_low, down_use, preferred_element_type=jnp.float32
    )
    return (gate_up_out, hidden_low, partial_value)


def expert_backward(inputs_low, gate_up_out, hidden_low, grad_part_low, gate_up_use, down_use):
    grad_down = jnp.einsum(
        "emf,emd->efd", hidden_low, grad_part_low, preferred_element_type=jnp.float32
    )
    grad_hidden = jnp.einsum(
        "emd,efd->emf", grad_part_low, down_use, preferred_element_type=jnp.float32
    )
    gate_out = gate_up_out[:, 0]
    sigmoid_gate = jax.nn.sigmoid(gate_out)
    grad_pair_low = jnp.stack(
        [
            grad_hidden
            * gate_up_out[:, 1]
            * sigmoid_gate
            * (1.0 + gate_out * (1.0 - sigmoid_gate)),
            grad_hidden * gate_out * sigmoid_gate,
        ],
        axis=1,
    ).astype(jnp.bfloat16)
    grad_gate_up = jnp.einsum(
        "emd,ecmf->ecdf", inputs_low, grad_pair_low, preferred_element_type=jnp.float32
    )
    grad_rows = jnp.einsum(
        "ecmf,ecdf->emd", grad_pair_low, gate_up_use, preferred_element_type=jnp.float32
    )
    return (grad_gate_up, grad_down, grad_rows)


def shards(
    tokens,
    cotangent,
    seq_lengths,
    block_order,
    routes,
    gains,
    qkv_weights,
    out_weight,
    router,
    const_values,
    w_gate_up,
    w_down,
):
    tok_count = tokens.shape[1]
    width = tokens.shape[2]
    ctx_size = lax.axis_size("ctx")
    own_index = lax.axis_index("ctx")
    score_scale = HEAD_DIM ** (-0.5)
    pack_pos, segment, seq_pos = layout_tables(seq_lengths[0], block_order[0], tok_count)
    own_start = own_index * tok_count
    query_pos = lax.dynamic_slice_in_dim(pack_pos, own_start, tok_count)
    query_seg = lax.dynamic_slice_in_dim(segment, own_start, tok_count)
    cosine_table, sine_table = angle_tables(
        lax.dynamic_slice_in_dim(seq_pos, own_start, tok_count), HEAD_DIM
    )
    head_shape = (tok_count, HEADS, HEAD_DIM)
    expert_ids = jnp.arange(NE, dtype=jnp.int32)
    slot_ids = jnp.arange(MOST, dtype=jnp.int32)
    row_ids = jnp.arange(tok_count, dtype=jnp.int32)

    def allowed_pairs(key_offset, key_count):
        key_pos = lax.dynamic_slice_in_dim(pack_pos, key_offset, key_count)
        key_seg = lax.dynamic_slice_in_dim(segment, key_offset, key_count)
        return (query_seg[:, None] == key_seg[None, :]) & (key_pos[None, :] <= query_pos[:, None])

    stream = tokens[0].astype(jnp.float32)
    previous = jnp.zeros((tok_count, NE), jnp.float32)
    saved = []
    for layer_index in range(LAYERS):
        gain_all, qkv_all, out_all, router_all, const_all = (
            lax.all_gather(gains[layer_index], "fsdp", axis=1, tiled=True),
            lax.all_gather(qkv_weights[layer_index], "fsdp", axis=1, tiled=True),
            lax.all_gather(out_weight[layer_index], "fsdp", axis=0, tiled=True),
            lax.all_gather(router[layer_index], "fsdp", axis=0, tiled=True),
            lax.all_gather(const_values[layer_index], "fsdp", axis=1, tiled=True),
        )
        gain_float = gain_all.astype(jnp.float32)
        base_one, inverse_one = rms_parts(stream)
        normed_low = (base_one * gain_float[0]).astype(jnp.bfloat16)
        projected = jnp.einsum(
            "td,cde->cte", normed_low, qkv_all, preferred_element_type=jnp.float32
        )
        queries_low = rotate_pairs(
            projected[0].reshape(head_shape), cosine_table, sine_table, 1.0
        ).astype(jnp.bfloat16)
        keys_low = rotate_pairs(
            projected[1].reshape(head_shape), cosine_table, sine_table, 1.0
        ).astype(jnp.bfloat16)
        values_low = projected[2].reshape(head_shape).astype(jnp.bfloat16)

        def fold_step(running, shard_piece, offset, queries_use=queries_low):
            keys_piece, values_piece = shard_piece
            allowed = allowed_pairs(offset, keys_piece.shape[0])[None]
            scores = (
                jnp.einsum(
                    "qhd,khd->hqk", queries_use, keys_piece, preferred_element_type=jnp.float32
                )
                * score_scale
            )
            scores = jnp.where(allowed, scores, -1e30)
            top_old, total_old, accumulated = running
            top_new = jnp.maximum(top_old, jnp.max(scores, axis=-1))
            weights = jnp.where(allowed, jnp.exp(scores - top_new[..., None]), 0.0)
            factor = jnp.exp(top_old - top_new)
            accumulated = jnp.einsum(
                "hqk,khd->hqd",
                weights.astype(jnp.bfloat16),
                values_piece,
                preferred_element_type=jnp.float32,
            )
            return (top_new, jnp.sum(weights, axis=-1), accumulated)

        starting = (
            jnp.full((HEADS, tok_count), -1e30, jnp.float32),
            jnp.zeros((HEADS, tok_count), jnp.float32),
            jnp.zeros((HEADS, tok_count, HEAD_DIM), jnp.float32),
        )
        top_value, total_sum, accumulated = fold_step(
            starting,
            (
                lax.all_gather(keys_low, "ctx", axis=0, tiled=True),
                lax.all_gather(values_low, "ctx", axis=0, tiled=True),
            ),
            jnp.int32(0),
        )
        log_total = top_value + jnp.log(total_sum)
        attended = jnp.transpose(accumulated / total_sum[..., None], (1, 0, 2))
        mixed_low = attended.reshape(tok_count, width).astype(jnp.bfloat16)
        hidden_state = stream + jnp.dot(mixed_low, out_all, preferred_element_type=jnp.float32)
        base_two, inverse_two = rms_parts(hidden_state)
        expert_in = base_two * gain_float[1]
        expert_low = expert_in.astype(jnp.bfloat16)
        raw_logits = jnp.dot(expert_low, router_all, preferred_element_type=jnp.float32)
        logits = raw_logits[:, :NE] + previous
        route_ids = routes[layer_index, 0]
        chosen = route_ids[:, :, None] == expert_ids[None, None, :]
        chosen_f = chosen.astype(jnp.float32)
        hit_count = jnp.sum(chosen.astype(jnp.int32), axis=1)
        slot_index = jnp.cumsum(hit_count, axis=0) - 1
        picked = jnp.sum(chosen_f * logits[:, None, :], axis=-1)
        gate_weights = jax.nn.softmax(picked, axis=-1)
        coeffs = jnp.sum(gate_weights[:, :, None] * chosen_f, axis=1)
        slot_table = jnp.zeros((NF, MOST), jnp.int32)
        for expert in range(NF):
            target = jnp.where(hit_count[:, expert] > 0, slot_index[:, expert], MOST)
            slot_table = slot_table.at[expert, target].set(row_ids, mode="drop")
        filled = (slot_ids[None, :] < jnp.sum(hit_count[:, :NF], axis=0)[:, None]).astype(
            jnp.float32
        )
        rows_low = expert_low[slot_table]
        inputs_low = lax.all_gather(rows_low, "fsdp", axis=1, tiled=True)
        gate_up_out, hidden_low, partial_value = expert_forward(
            inputs_low, w_gate_up[layer_index], w_down[layer_index]
        )
        result = lax.psum_scatter(
            partial_value.astype(jnp.bfloat16), "fsdp", scatter_dimension=1, tiled=True
        ).astype(jnp.float32)
        flat_index = jnp.arange(NF, dtype=jnp.int32)[None, :] * MOST + jnp.clip(
            slot_index[:, :NF], 0, MOST - 1
        )
        token_result = result.reshape(NF * MOST, width)[flat_index]
        expert_mix = (
            jnp.sum(coeffs[:, :NF, None] * token_result, axis=1)
            + coeffs[:, NF + 1 : NF + 2] * expert_in
        )
        mixings = []
        for const_index in range(NC):
            column = NE + 2 * const_index
            mixing = jax.nn.softmax(raw_logits[:, column : column + 2], axis=-1)
            mixings.append(mixing)
            expert_mix = expert_mix + coeffs[:, NF + 2 + const_index : NF + 3 + const_index] * (
                mixing[:, 0:1] * expert_in
                + mixing[:, 1:2] * const_all[const_index].astype(jnp.float32)[None, :]
            )
        saved.append(
            (
                gain_float,
                qkv_all,
                out_all,
                router_all,
                const_all,
                base_one,
                inverse_one,
                normed_low,
                queries_low,
                keys_low,
                values_low,
                log_total,
                attended,
                mixed_low,
                base_two,
                inverse_two,
                expert_in,
                expert_low,
                chosen_f,
                hit_count,
                gate_weights,
                coeffs,
                slot_table,
                filled,
                inputs_low,
                gate_up_out,
                hidden_low,
                flat_index,
                token_result,
                mixings,
            )
        )
        stream = hidden_state + expert_mix
        previous = logits
    grad_stream = cotangent[0].astype(jnp.float32)
    grad_previous = jnp.zeros((tok_count, NE), jnp.float32)
    layer_grads = [None] * LAYERS
    for layer_index in reversed(range(LAYERS)):
        (
            gain_float,
            qkv_all,
            out_all,
            router_all,
            const_all,
            base_one,
            inverse_one,
            normed_low,
            queries_low,
            keys_low,
            values_low,
            log_total,
            attended,
            mixed_low,
            base_two,
            inverse_two,
            expert_in,
            expert_low,
            chosen_f,
            hit_count,
            gate_weights,
            coeffs,
            slot_table,
            filled,
            inputs_low,
            gate_up_out,
            hidden_low,
            flat_index,
            token_result,
            mixings,
        ) = saved[layer_index]
        grad_mix = grad_stream
        dot_input = jnp.sum(grad_mix * expert_in, axis=-1, keepdims=True)
        coef_grads = [
            jnp.sum(grad_mix[:, None, :] * token_result, axis=-1),
            jnp.zeros((tok_count, 1), jnp.float32),
            dot_input,
        ]
        grad_in = grad_mix * coeffs[:, NF + 1 : NF + 2]
        const_cols = []
        const_grads = []
        for const_index in range(NC):
            mixing = mixings[const_index]
            const_row = const_all[const_index].astype(jnp.float32)[None, :]
            dot_const = jnp.sum(grad_mix * const_row, axis=-1, keepdims=True)
            share = coeffs[:, NF + 2 + const_index : NF + 3 + const_index]
            coef_grads.append(mixing[:, 0:1] * dot_input + mixing[:, 1:2] * dot_const)
            grad_in = grad_in + grad_mix * (share * mixing[:, 0:1])
            grad_mixing = share * jnp.concatenate([dot_input, dot_const], axis=1)
            const_cols.append(
                mixing * (grad_mixing - jnp.sum(mixing * grad_mixing, axis=-1, keepdims=True))
            )
            const_grads.append(jnp.sum(grad_mix * (share * mixing[:, 1:2]), axis=0))
        grad_coeffs = jnp.concatenate(coef_grads, axis=1)
        grad_gates = jnp.sum(chosen_f * grad_coeffs[:, None, :], axis=-1)
        grad_picked = gate_weights * (
            grad_gates - jnp.sum(gate_weights * grad_gates, axis=-1, keepdims=True)
        )
        grad_logits = jnp.sum(grad_picked[:, :, None] * chosen_f, axis=1) + grad_previous
        grad_previous = grad_logits
        grad_raw_low = jnp.concatenate([grad_logits] + const_cols, axis=1).astype(jnp.bfloat16)
        grad_router = jnp.einsum(
            "td,tc->dc", expert_low, grad_raw_low, preferred_element_type=jnp.float32
        )
        grad_in = grad_in + jnp.einsum(
            "tc,dc->td", grad_raw_low, router_all, preferred_element_type=jnp.float32
        )
        slot_weight = (
            jnp.take_along_axis(jnp.transpose(coeffs[:, :NF]), slot_table, axis=1) * filled
        )
        grad_result_low = (grad_mix[slot_table] * slot_weight[:, :, None]).astype(jnp.bfloat16)
        grad_part_low = lax.all_gather(grad_result_low, "fsdp", axis=1, tiled=True)
        grad_gate_up, grad_down, grad_rows = expert_backward(
            inputs_low,
            gate_up_out,
            hidden_low,
            grad_part_low,
            w_gate_up[layer_index],
            w_down[layer_index],
        )
        grad_rows = lax.psum_scatter(
            grad_rows.astype(jnp.bfloat16), "fsdp", scatter_dimension=1, tiled=True
        ).astype(jnp.float32)
        token_grads = grad_rows.reshape(NF * MOST, width)[flat_index]
        grad_in = grad_in + jnp.sum(
            jnp.where(hit_count[:, :NF, None] > 0, token_grads, 0.0), axis=1
        )
        grad_gain_two = jnp.sum(grad_in * base_two, axis=0)
        grad_hidden_state = grad_stream + rms_back(grad_in * gain_float[1], base_two, inverse_two)
        grad_out_low = grad_hidden_state.astype(jnp.bfloat16)
        grad_out_w = jnp.einsum(
            "td,te->de", mixed_low, grad_out_low, preferred_element_type=jnp.float32
        )
        grad_attended = (
            jnp.einsum("te,de->td", grad_out_low, out_all, preferred_element_type=jnp.float32)
            .astype(jnp.bfloat16)
            .reshape(head_shape)
        )
        delta = jnp.transpose(jnp.sum(grad_attended.astype(jnp.float32) * attended, axis=-1))

        def visit(
            turn_index,
            carried,
            queries_use=queries_low,
            grad_use=grad_attended,
            log_use=log_total,
            delta_use=delta,
        ):
            keys_piece, values_piece, key_grads, value_grads, query_grads = carried
            source = (own_index - turn_index) % ctx_size
            allowed = allowed_pairs(source * tok_count, tok_count)[None]
            scores = (
                jnp.einsum(
                    "qhd,khd->hqk", queries_use, keys_piece, preferred_element_type=jnp.float32
                )
                * score_scale
            )
            probs = jnp.where(
                allowed, jnp.exp(jnp.where(allowed, scores, -1e30) - log_use[..., None]), 0.0
            )
            value_grads = value_grads + jnp.einsum(
                "hqk,qhd->khd",
                probs.astype(jnp.bfloat16),
                grad_use,
                preferred_element_type=jnp.float32,
            )
            prob_grads = jnp.einsum(
                "qhd,khd->hqk", grad_use, values_piece, preferred_element_type=jnp.float32
            )
            score_grads = (probs * (prob_grads - delta_use[..., None])).astype(jnp.bfloat16)
            query_grads = query_grads + jnp.einsum(
                "hqk,khd->qhd", score_grads, keys_piece, preferred_element_type=jnp.float32
            )
            key_grads = key_grads + jnp.einsum(
                "hqk,qhd->khd", score_grads, queries_use, preferred_element_type=jnp.float32
            )
            keys_piece, values_piece = from_behind((keys_piece, values_piece), "ctx", 1)
            key_grads, value_grads = (
                from_behind(key_grads.astype(jnp.bfloat16), "ctx", 1).astype(key_grads.dtype),
                from_behind(value_grads.astype(jnp.bfloat16), "ctx", 1).astype(value_grads.dtype),
            )
            return (keys_piece, values_piece, key_grads, value_grads, query_grads)

        zero_heads = jnp.zeros(head_shape, jnp.float32)
        finished = lax.fori_loop(
            0, ctx_size, visit, (keys_low, values_low, zero_heads, zero_heads, zero_heads)
        )
        grad_query = (
            rotate_pairs(finished[4] * score_scale, cosine_table, sine_table, -1.0)
            .astype(jnp.bfloat16)
            .reshape(tok_count, width)
        )
        grad_key = (
            rotate_pairs(finished[2] * score_scale, cosine_table, sine_table, -1.0)
            .astype(jnp.bfloat16)
            .reshape(tok_count, width)
        )
        grad_value = finished[3].astype(jnp.bfloat16).reshape(tok_count, width)
        grad_proj_low = jnp.stack([grad_query, grad_key, grad_value], axis=0)
        grad_qkv = jnp.einsum(
            "td,cte->cde", normed_low, grad_proj_low, preferred_element_type=jnp.float32
        )
        grad_normed = jnp.einsum(
            "cte,cde->td", grad_proj_low, qkv_all, preferred_element_type=jnp.float32
        )
        grad_gain_one = jnp.sum(grad_normed * base_one, axis=0)
        grad_stream = grad_hidden_state + rms_back(
            grad_normed * gain_float[0], base_one, inverse_one
        )
        gains_shard, qkv_shard, out_shard, router_shard, const_shard = (
            lax.psum_scatter(
                jnp.stack([grad_gain_one, grad_gain_two]).astype(jnp.bfloat16),
                "fsdp",
                scatter_dimension=1,
                tiled=True,
            ).astype(jnp.float32),
            lax.psum_scatter(
                grad_qkv.astype(jnp.bfloat16), "fsdp", scatter_dimension=1, tiled=True
            ).astype(jnp.float32),
            lax.psum_scatter(
                grad_out_w.astype(jnp.bfloat16), "fsdp", scatter_dimension=0, tiled=True
            ).astype(jnp.float32),
            lax.psum_scatter(
                grad_router.astype(jnp.bfloat16), "fsdp", scatter_dimension=0, tiled=True
            ).astype(jnp.float32),
            lax.psum_scatter(
                jnp.stack(const_grads).astype(jnp.bfloat16), "fsdp", scatter_dimension=1, tiled=True
            ).astype(jnp.float32),
        )
        layer_grads[layer_index] = (
            lax.psum(gains_shard.astype(jnp.bfloat16), "ctx").astype(jnp.float32),
            lax.psum(qkv_shard.astype(jnp.bfloat16), "ctx").astype(jnp.float32),
            lax.psum(out_shard.astype(jnp.bfloat16), "ctx").astype(jnp.float32),
            lax.psum(router_shard.astype(jnp.bfloat16), "ctx").astype(jnp.float32),
            lax.psum(const_shard.astype(jnp.bfloat16), "ctx").astype(jnp.float32),
            lax.psum(grad_gate_up.astype(jnp.bfloat16), "ctx").astype(jnp.float32),
            lax.psum(grad_down.astype(jnp.bfloat16), "ctx").astype(jnp.float32),
        )
    stacked = [
        jnp.stack([layer_grads[layer_index][member_index] for layer_index in range(LAYERS)])
        for member_index in range(7)
    ]
    return (
        stream[None],
        grad_stream[None],
        stacked[0],
        stacked[1],
        stacked[2],
        stacked[3],
        stacked[4],
        stacked[5],
        stacked[6],
    )


MINLEN = 1024
ROUT = 56
RAW, COEF, SLOT, LOGI = 0, 16, 32, 40
VMEM_MB = 60


def nt(a, b):
    return lax.dot_general(a, b, (((1,), (1,)), ((), ())), preferred_element_type=jnp.float32)


def nn(a, b):
    return lax.dot_general(a, b, (((1,), (0,)), ((), ())), preferred_element_type=jnp.float32)


def tn(a, b):
    return lax.dot_general(a, b, (((0,), (0,)), ((), ())), preferred_element_type=jnp.float32)


def params_of(mb=VMEM_MB, **more):
    return pltpu.CompilerParams(vmem_limit_bytes=mb * 2**20, **more)


def shape_of(dims, kind):
    return jax.ShapeDtypeStruct(dims, kind)


def rms_factor(values):
    return lax.rsqrt(jnp.mean(values * values, axis=-1, keepdims=True) + 1e-06)


def to_rows(columns, count):
    lane = lax.broadcasted_iota(jnp.int32, (columns[0].shape[0], 128), 1)
    packed = jnp.zeros(lane.shape, jnp.float32)
    for index, column in enumerate(columns):
        packed = jnp.where(lane == index, column, packed)
    return jnp.transpose(packed)[:count]


def to_columns(rows):
    count = rows[0].shape[1]
    sub = lax.broadcasted_iota(jnp.int32, (128, count), 0)
    packed = jnp.zeros(sub.shape, jnp.float32)
    for index, row in enumerate(rows):
        packed = jnp.where(sub == index, row, packed)
    packed = jnp.transpose(packed)
    return [packed[:, index : index + 1] for index in range(len(rows))]


def swap_halves(values):
    lanes = values.shape[1]
    lane = lax.broadcasted_iota(jnp.int32, values.shape, 1)
    ahead = pltpu.roll(values, lanes - 32, 1)
    behind = pltpu.roll(values, 32, 1)
    return jnp.where(lane % 64 < 32, ahead, behind)


def spin(values, cosine, sine):
    return values * cosine + swap_halves(values) * sine


def place():
    own, pack = lax.axis_index("ctx"), lax.axis_index("fsdp")
    return own // 2, own % 2, pack // 2, pack % 2


def remote(src, dst, send, recv, ctx, fsdp):
    return pltpu.make_async_remote_copy(
        src_ref=src,
        dst_ref=dst,
        send_sem=send,
        recv_sem=recv,
        device_id=(ctx, fsdp),
        device_id_type=pl.DeviceIdType.MESH,
    )


def greet_plane(contexts, across=False):
    own = lax.axis_index("ctx")
    _, _, y, k = place()
    barrier = pltpu.get_barrier_semaphore()
    if across:
        for core in (k, 1 - k):
            device = (own, 2 * (1 - y) + core)
            pl.semaphore_signal(barrier, inc=1, device_id=device, device_id_type=pl.DeviceIdType.MESH)
    for ctx in range(contexts):
        for core in range(2):

            @pl.when(jnp.logical_or(ctx != own, core != k))
            def _():
                pl.semaphore_signal(barrier, inc=1, device_id=(ctx, 2 * y + core), device_id_type=pl.DeviceIdType.MESH)

    return barrier, 2 * contexts - 1 + (2 if across else 0)


def greet_packs():
    own = lax.axis_index("ctx")
    _, _, y, k = place()
    barrier = pltpu.get_barrier_semaphore()
    for fsdp in (2 * y + 1 - k, 2 * (1 - y) + k, 2 * (1 - y) + 1 - k):
        pl.semaphore_signal(barrier, inc=1, device_id=(own, fsdp), device_id_type=pl.DeviceIdType.MESH)
    return barrier, 3


def attn_fwd_kernel(
    order, inv, x, small, wq, cosine, sine, wo_own,
    n1s, qkv, o, lse, ob, hst, ub, w, wo,
    n1own, n1r, osort, osend, orecv, cols, w_s, wo_s,
    n_send, n_recv, f_send, f_recv, o_send, o_recv, w_send, w_recv, v_send, v_recv,
):
    blocks, blk, _ = n1r.shape
    lanes = o.shape[1]
    seq = blocks * blk
    step = 2 * blk
    own = lax.axis_index("ctx")
    z, xx, y, k = place()
    depth = blocks // 2
    same = xx == k
    pack = lax.axis_index("fsdp")
    inner = wo_own.shape[1]
    beside, over, corner = 2 * y + 1 - k, 2 * (1 - y) + k, 2 * (1 - y) + 1 - k

    barrier, others = greet_plane(blocks, across=True)
    n1 = norm_low(x[...], small[0:1, :].astype(jnp.float32))
    n1own[0] = n1[:blk]
    n1own[1] = n1[blk:]
    pl.semaphore_wait(barrier, others)

    def n1_copy(zz):
        return remote(n1own.at[zz // 2], n1r.at[own], n_send.at[zz], n_recv.at[z], 2 * zz + k, 2 * y + xx)

    for zz in range(depth):
        alone = jnp.logical_and(same, zz == z)

        @pl.when(jnp.logical_not(alone))
        def _():
            n1_copy(zz).start()

        @pl.when(alone)
        def _():
            n1r[own] = n1own[zz // 2]

    for half in range(2):

        @pl.when(z % 2 == half)
        def _():
            for core in range(2):
                first = (2 * half + core) * inner
                for c in range(3):
                    cols[core, :, c * lanes : c * lanes + inner] = wq[0, c, :, first : first + inner]
                    cols[core, :, c * lanes + inner : (c + 1) * lanes] = jnp.zeros((inner, lanes - inner), jnp.bfloat16)

    def rows_of(device):
        return pl.ds(pl.multiple_of(device * inner, inner), inner)

    def w_copy(index):
        device, core = ((beside, 1 - k), (over, k), (corner, 1 - k))[index]
        return remote(cols.at[core], w_s.at[rows_of(pack), :], w_send.at[index], w_recv.at[index], own, device)

    def w_wait(index):
        rows = w_s.at[rows_of((beside, over, corner)[index]), :]
        remote(cols.at[0], rows, w_send.at[index], w_recv.at[index], own, beside).wait_recv()

    w_s[rows_of(pack), :] = cols[k]
    wo_s[pack] = wo_own[0]
    for index in (1, 2, 0):
        w_copy(index).start()
    v_far = remote(wo_s.at[pack], wo_s.at[pack], v_send.at[0], v_recv.at[0], own, over)
    v_near = remote(wo_s.at[pack], wo_s.at[pack], v_send.at[1], v_recv.at[1], own, beside)
    v_on = remote(wo_s.at[over], wo_s.at[over], v_send.at[2], v_recv.at[2], own, beside)
    v_far.start()
    v_near.start()

    def forward_copy(zz):
        slot = n1r.at[2 * zz + k]
        return remote(slot, slot, f_send.at[zz], f_recv.at[zz], own, 2 * y + 1 - k)

    for zz in range(depth):

        @pl.when(jnp.logical_not(jnp.logical_and(same, zz == z)))
        def _():
            remote(n1own.at[0], n1r.at[2 * zz + k], n_send.at[zz], n_recv.at[zz], 2 * zz + k, 2 * y + xx).wait_recv()

        forward_copy(zz).start()
    for zz in range(depth):
        slot = n1r.at[2 * zz + 1 - k]
        remote(slot, slot, f_send.at[zz], f_recv.at[zz], own, 2 * y + 1 - k).wait_recv()

    for index in range(3):
        w_wait(index)
    w[...] = w_s[...]
    for b in range(blocks):
        n1s[b * blk : (b + 1) * blk, :] = n1r[inv[b]]
    for i in range(seq // step):
        part = slice(i * step, (i + 1) * step)
        out = nn(n1s[part, :], w_s[...])
        cos2 = jnp.concatenate([cosine[part, :]] * (lanes // 128), axis=1)
        sin2 = jnp.concatenate([sine[part, :]] * (lanes // 128), axis=1)
        q = spin(out[:, :lanes], cos2, sin2).astype(jnp.bfloat16)
        qkv[part, :lanes] = q * jnp.asarray(HEAD_DIM**-0.5, jnp.bfloat16)
        qkv[part, lanes : 2 * lanes] = spin(out[:, lanes : 2 * lanes], cos2, sin2).astype(jnp.bfloat16)
        qkv[part, 2 * lanes :] = out[:, 2 * lanes :].astype(jnp.bfloat16)
    lane = lax.broadcasted_iota(jnp.int32, (step, 128), 1)
    for i in range(seq // step):
        part = slice(i * step, (i + 1) * step)
        span = (i + 1) * step
        seen = lax.broadcasted_iota(jnp.int32, (step, span), 1) <= (
            lax.broadcasted_iota(jnp.int32, (step, span), 0) + i * step
        )
        logs = jnp.zeros((step, 128), jnp.float32)
        for head in range(GROUP_HEADS):
            tile, side = head // 2, head % 2
            at = tile * 128
            mine = lane // 64 == side
            q = jnp.where(mine, qkv[part, at : at + 128], jnp.asarray(0, jnp.bfloat16))
            s = nt(q, qkv[:span, lanes + at : lanes + at + 128])
            s = jnp.where(seen, s, -1e30)
            top = jnp.max(s, axis=1, keepdims=True)
            p = jnp.exp(s - top)
            total = jnp.sum(p, axis=1, keepdims=True)
            out = nn(p.astype(jnp.bfloat16), qkv[:span, 2 * lanes + at : 2 * lanes + at + 128]) / total
            logs = jnp.where(lane == head, top + jnp.log(total), logs)
            if side == 0:
                kept = jnp.where(mine, out, 0.0)
            else:
                kept = jnp.where(mine, out, kept)
            o[part, at : at + 128] = kept
        lse[part, :] = logs
        osort[2 * i] = o[part, :][:blk].astype(jnp.bfloat16)
        osort[2 * i + 1] = o[part, :][blk:].astype(jnp.bfloat16)

    mine_at = 2 * z + k
    remote(wo_s.at[over], wo_s.at[over], v_send.at[0], v_recv.at[0], own, over).wait_recv()
    v_on.start()

    def o_copy(ctx):
        return remote(osend.at[ctx], orecv.at[mine_at], o_send.at[ctx], o_recv.at[mine_at], ctx, 2 * y + xx)

    for ctx in range(blocks):
        alone = jnp.logical_and(same, ctx == own)
        osend[ctx] = osort[order[ctx]]

        @pl.when(jnp.logical_not(alone))
        def _():
            o_copy(ctx).start()

        @pl.when(alone)
        def _():
            orecv[mine_at] = osend[ctx]

    for src in range(blocks):

        @pl.when(jnp.logical_not(jnp.logical_and(same, src == mine_at)))
        def _():
            remote(osend.at[0], orecv.at[src], o_send.at[0], o_recv.at[src], 2 * (src // 2) + k, 2 * y + src % 2).wait_recv()

    ob[...] = orecv[...]
    remote(wo_s.at[beside], wo_s.at[beside], v_send.at[1], v_recv.at[1], own, beside).wait_recv()
    remote(wo_s.at[corner], wo_s.at[corner], v_send.at[2], v_recv.at[2], own, beside).wait_recv()
    wo[...] = wo_s[...]
    total, low = post_attention(orecv[...], x[...], wo_s[...], small[1:2, :].astype(jnp.float32))
    hst[...] = total
    ub[...] = low
    for zz in range(depth):

        @pl.when(jnp.logical_not(jnp.logical_and(same, zz == z)))
        def _():
            n1_copy(zz).wait_send()

        forward_copy(zz).wait_send()
    for index in range(3):
        w_copy(index).wait_send()
    v_far.wait_send()
    v_near.wait_send()
    v_on.wait_send()
    for ctx in range(blocks):

        @pl.when(jnp.logical_not(jnp.logical_and(same, ctx == own)))
        def _():
            o_copy(ctx).wait_send()


def attn_forward(layer, order, inv, x, small, wq, cosine, sine, wo, number):
    count, width = x.shape
    blocks, blk = order.shape[0], count // 2
    packs, inner = width // wo.shape[1], wo.shape[1]
    lanes = -(-inner // 128) * 128
    seq = blocks * blk
    vm = pl.BlockSpec(memory_space=pltpu.VMEM)
    sm = pl.BlockSpec(memory_space=pltpu.SMEM)
    bf = jnp.bfloat16
    dma = pltpu.SemaphoreType.DMA
    return pl.pallas_call(
        attn_fwd_kernel,
        grid=(1,),
        out_shape=[
            shape_of((seq, width), bf),
            shape_of((seq, 3 * lanes), bf),
            shape_of((seq, lanes), jnp.float32),
            shape_of((seq, 128), jnp.float32),
            shape_of((blocks, blk, lanes), bf),
            shape_of((count, width), jnp.float32),
            shape_of((count, width), bf),
            shape_of((width, 3 * lanes), bf),
            shape_of((packs, inner, width), bf),
        ],
        in_specs=[sm, sm, vm, vm]
        + [pl.BlockSpec((1, 3, inner, width), lambda _: (layer, 0, 0, 0)), vm, vm]
        + [pl.BlockSpec((1, inner, width), lambda _: (layer, 0, 0))],
        out_specs=[vm] * 9,
        scratch_shapes=[
            pltpu.VMEM((2, blk, width), bf),
            pltpu.VMEM((blocks, blk, width), bf),
            pltpu.VMEM((blocks, blk, lanes), bf),
            pltpu.VMEM((blocks, blk, lanes), bf),
            pltpu.VMEM((blocks, blk, lanes), bf),
            pltpu.VMEM((2, inner, 3 * lanes), bf),
            pltpu.VMEM((width, 3 * lanes), bf),
            pltpu.VMEM((packs, inner, width), bf),
        ]
        + [dma((blocks // 2,))] * 4
        + [dma((blocks,))] * 2
        + [dma((3,))] * 4,
        compiler_params=params_of(collective_id=number, has_side_effects=True),
        name="attn_fwd",
    )(order, inv, x, small, wq, cosine, sine, wo)


def attn_bwd_kernel(
    order, inv, n1s, w, cosine, sine, qkv, o, lse, go, ghst, x, small, gsmall,
    gx, gm, gw,
    gor, gos, grads, acc, keep, sib_out, sib_in, gn_out, gnr,
    o_send, o_recv, s_send, s_recv, g_send, g_recv,
):
    blocks, blk, width = grads.shape
    lanes = o.shape[1]
    seq = blocks * blk
    step = 2 * blk
    zero = jnp.asarray(0, jnp.bfloat16)
    own = lax.axis_index("ctx")
    z, xx, y, k = place()
    depth = blocks // 2
    same = xx == k

    barrier, others = greet_plane(blocks)
    acc[...] = jnp.zeros_like(acc)
    pl.semaphore_wait(barrier, others)

    def go_copy(unit):
        return remote(go.at[unit], gor.at[own], o_send.at[unit], o_recv.at[own], 2 * (unit // 2) + k, 2 * y + unit % 2)

    for unit in range(blocks):
        alone = jnp.logical_and(same, unit == 2 * z + k)

        @pl.when(jnp.logical_not(alone))
        def _():
            go_copy(unit).start()

        @pl.when(alone)
        def _():
            gor[own] = go[unit]

    for ctx in range(blocks):

        @pl.when(jnp.logical_not(jnp.logical_and(same, ctx == own)))
        def _():
            remote(go.at[0], gor.at[ctx], o_send.at[0], o_recv.at[ctx], ctx, 2 * y + xx).wait_recv()

    for b in range(blocks):
        gos[b * blk : (b + 1) * blk, :] = gor[inv[b]]
    lane = lax.broadcasted_iota(jnp.int32, (step, 128), 1)
    for i in range(seq // step):
        part = slice(i * step, (i + 1) * step)
        span = (i + 1) * step
        seen = lax.broadcasted_iota(jnp.int32, (step, span), 1) <= (
            lax.broadcasted_iota(jnp.int32, (step, span), 0) + i * step
        )
        key_lane = lax.broadcasted_iota(jnp.int32, (span, 128), 1)
        for head in range(GROUP_HEADS):
            tile, side = head // 2, head % 2
            at = tile * 128
            mine = lane // 64 == side
            q = jnp.where(mine, qkv[part, at : at + 128], zero)
            g = jnp.where(mine, gos[part, at : at + 128], zero)
            keys = qkv[:span, lanes + at : lanes + at + 128]
            values = qkv[:span, 2 * lanes + at : 2 * lanes + at + 128]
            delta = jnp.sum(g.astype(jnp.float32) * o[part, at : at + 128], axis=1, keepdims=True)
            s = nt(q, keys)
            p = jnp.where(seen, jnp.exp(jnp.where(seen, s, -1e30) - lse[part, head : head + 1]), 0.0)
            ds = (p * (nt(g, values) - delta)).astype(jnp.bfloat16)
            acc[:span, 2 * lanes + at : 2 * lanes + at + 128] += tn(p.astype(jnp.bfloat16), g)
            acc[:span, lanes + at : lanes + at + 128] += tn(ds, q)
            acc[part, at : at + 128] += nn(ds, jnp.where(key_lane // 64 == side, keys, zero))
    for b in range(blocks):
        part = slice(b * blk, (b + 1) * blk)
        cos2 = jnp.concatenate([cosine[part, :]] * (lanes // 128), axis=1)
        sin2 = jnp.concatenate([sine[part, :]] * (lanes // 128), axis=1)
        grads[b, :, :lanes] = spin(acc[part, :lanes] * HEAD_DIM**-0.5, cos2, -sin2).astype(jnp.bfloat16)
        grads[b, :, lanes : 2 * lanes] = spin(acc[part, lanes : 2 * lanes], cos2, -sin2).astype(jnp.bfloat16)
        grads[b, :, 2 * lanes :] = acc[part, 2 * lanes :].astype(jnp.bfloat16)

    def sib_copy(zz):
        return remote(sib_out.at[zz], sib_in.at[zz], s_send.at[zz], s_recv.at[zz], own, 2 * y + 1 - k)

    def gn_copy(zz):
        return remote(gn_out.at[zz], gnr.at[z], g_send.at[zz], g_recv.at[z], 2 * zz + k, 2 * y + xx)

    for zz in range(depth):
        sib_out[zz] = nt(grads[order[2 * zz + 1 - k]], w[...]).astype(jnp.bfloat16)
        sib_copy(zz).start()
    for zz in range(depth):
        keep[zz] = nt(grads[order[2 * zz + k]], w[...])
    for zz in range(depth):
        sib_copy(zz).wait_recv()
        alone = jnp.logical_and(same, zz == z)
        gn_out[zz] = (keep[zz] + sib_in[zz].astype(jnp.float32)).astype(jnp.bfloat16)

        @pl.when(jnp.logical_not(alone))
        def _():
            gn_copy(zz).start()

        @pl.when(alone)
        def _():
            gnr[z] = gn_out[zz]

    groups = depth
    inner = GROUP_HEADS * HEAD_DIM
    gw[:, : 3 * width] = jnp.zeros((width, 3 * width), jnp.bfloat16)
    for i in range(width // 256):
        part = slice(i * 256, (i + 1) * 256)
        piece = tn(n1s[:, part], grads[...].reshape(seq, 3 * lanes)).astype(jnp.bfloat16)
        for group in range(groups):

            @pl.when(2 * (z % 2) + k == group)
            def _():
                for c in range(3):
                    first = c * width + group * inner
                    gw[part, first : first + inner] = piece[:, c * lanes : c * lanes + inner]

    for zz in range(depth):

        @pl.when(jnp.logical_not(jnp.logical_and(same, zz == z)))
        def _():
            remote(gn_out.at[0], gnr.at[zz], g_send.at[0], g_recv.at[zz], 2 * zz + k, 2 * y + xx).wait_recv()

    halves = []
    for h in range(2):
        total = gnr[h * (depth // 2)].astype(jnp.float32)
        for zz in range(1, depth // 2):
            total = total + gnr[h * (depth // 2) + zz].astype(jnp.float32)
        halves.append(total)
    gn = jnp.concatenate(halves, axis=0)
    values = x[...]
    factor = rms_factor(values)
    base = values * factor
    gb = gn * small[0:1, :].astype(jnp.float32)
    grad = ghst[...] + factor * (gb - base * jnp.mean(gb * base, axis=-1, keepdims=True))
    gx[...] = grad
    gm[...] = grad.astype(jnp.bfloat16)
    sums = jnp.concatenate([jnp.sum(gn * base, axis=0, keepdims=True), gsmall[...]], axis=0)
    sums = jnp.concatenate([sums, jnp.zeros((128 - sums.shape[0], width), jnp.float32)], axis=0)
    gw[:, 3 * width :] = jnp.transpose(sums).astype(jnp.bfloat16)
    for unit in range(blocks):

        @pl.when(jnp.logical_not(jnp.logical_and(same, unit == 2 * z + k)))
        def _():
            go_copy(unit).wait_send()

    for zz in range(depth):
        sib_copy(zz).wait_send()

        @pl.when(jnp.logical_not(jnp.logical_and(same, zz == z)))
        def _():
            gn_copy(zz).wait_send()


def attn_backward(order, inv, n1s, w, cosine, sine, qkv, o, lse, go, ghst, x, small, gsmall, number):
    blocks, blk, lanes = go.shape
    seq, width = n1s.shape
    count = x.shape[0]
    depth = blocks // 2
    vm = pl.BlockSpec(memory_space=pltpu.VMEM)
    sm = pl.BlockSpec(memory_space=pltpu.SMEM)
    bf = jnp.bfloat16
    dma = pltpu.SemaphoreType.DMA
    return pl.pallas_call(
        attn_bwd_kernel,
        out_shape=[
            shape_of((count, width), jnp.float32),
            shape_of((count, width), bf),
            shape_of((width, 3 * width + 128), bf),
        ],
        in_specs=[sm] * 2 + [vm] * 12,
        out_specs=[vm] * 3,
        scratch_shapes=[
            pltpu.VMEM((blocks, blk, lanes), bf),
            pltpu.VMEM((seq, lanes), bf),
            pltpu.VMEM((blocks, blk, 3 * lanes), bf),
            pltpu.VMEM((seq, 3 * lanes), jnp.float32),
            pltpu.VMEM((depth, blk, width), jnp.float32),
            pltpu.VMEM((depth, blk, width), bf),
            pltpu.VMEM((depth, blk, width), bf),
            pltpu.VMEM((depth, blk, width), bf),
            pltpu.VMEM((depth, blk, width), bf),
        ]
        + [dma((blocks,))] * 2
        + [dma((depth,))] * 4,
        compiler_params=params_of(collective_id=number, has_side_effects=True),
        name="attn_bwd",
    )(order, inv, n1s, w, cosine, sine, qkv, o, lse, go, ghst, x, small, gsmall)


def routing(raw, before, routes):
    count = raw.shape[1]
    ids = lax.broadcasted_iota(jnp.int32, (16, count), 0)
    logits = raw + before
    first, second = ids == routes[0:1], ids == routes[1:2]
    z0 = jnp.sum(jnp.where(first, logits, 0.0), axis=0, keepdims=True)
    z1 = jnp.sum(jnp.where(second, logits, 0.0), axis=0, keepdims=True)
    top = jnp.maximum(z0, z1)
    e0, e1 = jnp.exp(z0 - top), jnp.exp(z1 - top)
    total = e0 + e1
    coef = jnp.where(first, e0 / total, 0.0) + jnp.where(second, e1 / total, 0.0)
    hits = jnp.where(first | second, 1.0, 0.0)
    upto = lax.broadcasted_iota(jnp.int32, (count, count), 0) <= lax.broadcasted_iota(jnp.int32, (count, count), 1)
    place = nn(hits.astype(jnp.bfloat16), jnp.where(upto, 1.0, 0.0).astype(jnp.bfloat16)) - 1.0
    slot = jnp.where(hits > 0, place, -1.0)
    return jnp.concatenate([raw, coef, slot[:NF], logits], axis=0)


def one_hot(slot):
    count = slot.shape[1]
    ids = lax.broadcasted_iota(jnp.int32, (NF, MOST, count), 1)
    hit = ids == slot.astype(jnp.int32)[:, None, :]
    return jnp.where(hit, 1.0, 0.0).reshape(NF * MOST, count)


def slot_values(hot, rows):
    count = rows.shape[1]
    wide = jnp.broadcast_to(rows[:, None, :], (NF, MOST, count)).reshape(NF * MOST, count)
    return jnp.sum(hot * wide, axis=1, keepdims=True)


def swap_rows(own, rows, send, recv, forward_send, forward_recv):
    ctx = lax.axis_index("ctx")
    _, _, y, k = place()
    beside, across = 2 * y + 1 - k, 2 * (1 - y) + k
    far = remote(own, rows.at[2], send.at[0], recv.at[0], ctx, across)
    near = remote(own, rows.at[1], send.at[1], recv.at[1], ctx, beside)
    onward = remote(rows.at[2], rows.at[3], forward_send, forward_recv, ctx, beside)
    far.start()
    near.start()
    return near, far, onward


def sum_rows(parts, beside_in, mid, across_in, send, recv):
    ctx = lax.axis_index("ctx")
    _, _, y, k = place()
    beside, across = 2 * y + 1 - k, 2 * (1 - y) + k
    first = remote(parts.at[3], beside_in.at[1], send.at[0], recv.at[0], ctx, beside)
    second = remote(parts.at[1], beside_in.at[0], send.at[1], recv.at[1], ctx, beside)
    third = remote(mid, across_in, send.at[2], recv.at[2], ctx, across)
    return first, second, third


def ffn_fwd_kernel(
    ub, hst, small, routes, before, wgu, wd,
    ubf, table, ext, x_next,
    rows_s, hot_s, x_s, y_s, coef_s, parts, beside_in, mid, across_in,
    a_send, a_recv, r_send, r_recv,
):
    e = pl.program_id(0)
    packs = ubf.shape[0]
    count, width = ub.shape
    router = small[2 + NC :, :]

    def gathers():
        return swap_rows(ub, rows_s, a_send, a_recv, a_send.at[2], a_recv.at[2])

    def sums():
        return sum_rows(parts, beside_in, mid, across_in, r_send, r_recv)

    @pl.when(e == 0)
    def _():
        barrier, others = greet_packs()
        rows_s[0] = ub[...]

        def prepare(d):
            rows = routing(nt(router, rows_s[d]), before[d], routes[d])
            table[d] = rows
            hot = one_hot(rows[SLOT : SLOT + NF])
            coef_s[d] = slot_values(hot, rows[COEF : COEF + NF])
            hot_low = hot.astype(jnp.bfloat16)
            hot_s[d] = hot_low
            x = nn(hot_low, rows_s[d]).astype(jnp.bfloat16)
            for n in range(NF):
                x_s[n, d * MOST : (d + 1) * MOST, :] = x[n * MOST : (n + 1) * MOST]

        pl.semaphore_wait(barrier, others)
        near, far, onward = gathers()
        prepare(0)
        near.wait_recv()
        prepare(1)
        far.wait_recv()
        onward.start()
        prepare(2)
        onward.wait_recv()
        prepare(3)
        ubf[...] = rows_s[...]
        ext[:count, :] = ub[...]
        rows = table[0]
        ext[count:, :] = jnp.zeros((16, width), jnp.bfloat16)
        ext[count:, :count] = rows[COEF : COEF + 16].astype(jnp.bfloat16)
        slots = jnp.concatenate([rows[SLOT : SLOT + NF], jnp.zeros((16 - NF, count), jnp.float32)], axis=0)
        ext[count:, count : 2 * count] = slots.astype(jnp.bfloat16)
        near.wait_send()
        far.wait_send()
        onward.wait_send()

    x = x_s[e]
    gate, up = nn(x, wgu[0, 0, 0]), nn(x, wgu[0, 0, 1])
    hid = (gate * jax.nn.sigmoid(gate) * up).astype(jnp.bfloat16)
    out = nn(hid, wd[0, 0])
    at = pl.ds(pl.multiple_of(e * MOST, MOST), MOST)
    for d in range(packs):
        y_s[d, at, :] = (out[d * MOST : (d + 1) * MOST] * coef_s[d, at, :]).astype(jnp.bfloat16)

    @pl.when(e == NF - 1)
    def _():
        first, second, third = sums()
        parts[3] = tn(hot_s[3], y_s[3]).astype(jnp.bfloat16)
        first.start()
        parts[1] = tn(hot_s[1], y_s[1]).astype(jnp.bfloat16)
        second.start()
        away = tn(hot_s[2], y_s[2])
        first.wait_recv()
        mid[...] = (away + beside_in[1].astype(jnp.float32)).astype(jnp.bfloat16)
        third.start()
        home = tn(hot_s[0], y_s[0])
        _, _, scale_u, scale_c = mixing_rows(table[0])
        columns = to_columns([scale_u] + scale_c)
        values = hst[...]
        moe = home + columns[0] * ((values * rms_factor(values)) * small[1:2, :].astype(jnp.float32))
        for c in range(NC):
            moe = moe + columns[1 + c] * small[2 + c : 3 + c, :].astype(jnp.float32)
        second.wait_recv()
        moe = moe + beside_in[0].astype(jnp.float32)
        third.wait_recv()
        x_next[...] = values + (moe + across_in[...].astype(jnp.float32))
        first.wait_send()
        second.wait_send()
        third.wait_send()


def whole_spec(dims):
    return pl.BlockSpec(dims, lambda *_: (0,) * len(dims))


def exchange_scratch(packs, count, width):
    bf = jnp.bfloat16
    return [
        pltpu.VMEM((packs, count, width), bf),
        pltpu.VMEM((2, count, width), bf),
        pltpu.VMEM((count, width), bf),
        pltpu.VMEM((count, width), bf),
    ]


def ffn_forward(layer, ub, hst, small, routes, before, wgu, wd, number):
    count, width = ub.shape
    packs = routes.shape[0]
    hidden = wd.shape[2]
    bf = jnp.bfloat16
    outs = [
        shape_of((packs, count, width), bf),
        shape_of((packs, ROUT, count), jnp.float32),
        shape_of((count + 16, width), bf),
        shape_of((count, width), jnp.float32),
    ]
    return pl.pallas_call(
        ffn_fwd_kernel,
        grid=(NF,),
        out_shape=outs,
        in_specs=[whole_spec(a.shape) for a in (ub, hst, small, routes, before)]
        + [
            pl.BlockSpec((1, 1, 2, width, hidden), lambda e: (layer, e, 0, 0, 0)),
            pl.BlockSpec((1, 1, hidden, width), lambda e: (layer, e, 0, 0)),
        ],
        out_specs=[whole_spec(a.shape) for a in outs],
        scratch_shapes=[
            pltpu.VMEM((packs, count, width), bf),
            pltpu.VMEM((packs, NF * MOST, count), bf),
            pltpu.VMEM((NF, packs * MOST, width), bf),
            pltpu.VMEM((packs, NF * MOST, width), bf),
            pltpu.VMEM((packs, NF * MOST, 1), jnp.float32),
        ]
        + exchange_scratch(packs, count, width)
        + [pltpu.SemaphoreType.DMA((3,))] * 4,
        compiler_params=params_of(collective_id=number, has_side_effects=True),
        name="ffn_fwd",
    )(ub, hst, small, routes, before, wgu, wd)


def silu_parts(gate, up, ghid):
    sig = jax.nn.sigmoid(gate)
    act = gate * sig
    dg = (ghid * up * sig * (1.0 + gate * (1.0 - sig))).astype(jnp.bfloat16)
    du = (ghid * act).astype(jnp.bfloat16)
    return act * up, dg, du


def ffn_bwd_kernel(
    gm, gx, ubf, table, hst, small, routes, gprev, wo, ob, wgu, wd,
    ghst, go, gwo, gsmall, glog,
    rows_s, hot_s, x_s, g_s, y_s, coef_s, gc_s, gcoef, gcoef_in, parts, beside_in, mid, across_in,
    a_send, a_recv, r_send, r_recv, c_send, c_recv,
):
    e = pl.program_id(0)
    packs = ubf.shape[0]
    ctx = lax.axis_index("ctx")
    _, _, y, k = place()
    peers = [None, 2 * y + 1 - k, 2 * (1 - y) + k, 2 * (1 - y) + 1 - k]

    def gathers():
        return swap_rows(gm, rows_s, a_send, a_recv, a_send.at[2], a_recv.at[2])

    def sums():
        return sum_rows(parts, beside_in, mid, across_in, r_send, r_recv)

    @pl.when(e == 0)
    def _():
        barrier, others = greet_packs()
        rows_s[0] = gm[...]

        def prepare(d):
            hot = one_hot(table[d, SLOT : SLOT + NF, :])
            coef_s[d] = slot_values(hot, table[d, COEF : COEF + NF, :])
            hot_low = hot.astype(jnp.bfloat16)
            hot_s[d] = hot_low
            x = nn(hot_low, ubf[d]).astype(jnp.bfloat16)
            for n in range(NF):
                x_s[n, d * MOST : (d + 1) * MOST, :] = x[n * MOST : (n + 1) * MOST]

        def spread(d):
            g = nn(hot_s[d], rows_s[d]).astype(jnp.bfloat16)
            for n in range(NF):
                g_s[n, d * MOST : (d + 1) * MOST, :] = g[n * MOST : (n + 1) * MOST]

        pl.semaphore_wait(barrier, others)
        near, far, onward = gathers()
        for d in range(packs):
            prepare(d)
        spread(0)
        near.wait_recv()
        far.wait_recv()
        onward.start()
        spread(1)
        spread(2)
        onward.wait_recv()
        spread(3)
        near.wait_send()
        far.wait_send()
        onward.wait_send()

    x = x_s[e]
    at = pl.ds(pl.multiple_of(e * MOST, MOST), MOST)
    coef = jnp.concatenate([coef_s[d, at, :] for d in range(packs)], axis=0)
    gate, up = nn(x, wgu[0, 0, 0]), nn(x, wgu[0, 0, 1])
    ghid = nt(g_s[e], wd[0, 0])
    hid, dg, du = silu_parts(gate, up, ghid * coef)
    dots = jnp.sum(hid * ghid, axis=1, keepdims=True)
    out = nt(dg, wgu[0, 0, 0]) + nt(du, wgu[0, 0, 1])
    for d in range(packs):
        y_s[d, at, :] = out[d * MOST : (d + 1) * MOST].astype(jnp.bfloat16)
        gc_s[d, at, :] = dots[d * MOST : (d + 1) * MOST]

    @pl.when(e == NF - 1)
    def _():
        first, second, third = sums()

        def coef_copy(d):
            return remote(gcoef.at[d], gcoef_in.at[d - 1], c_send.at[d - 1], c_recv.at[d - 1], ctx, peers[d])

        parts[3] = tn(hot_s[3], y_s[3]).astype(jnp.bfloat16)
        first.start()
        parts[1] = tn(hot_s[1], y_s[1]).astype(jnp.bfloat16)
        second.start()
        for d in range(packs):
            wide = hot_s[d].astype(jnp.float32) * gc_s[d]
            gcoef[d] = jnp.sum(wide.reshape(NF, MOST, wide.shape[1]), axis=1)
            if d > 0:
                coef_copy(d).start()
        away = tn(hot_s[2], y_s[2])
        first.wait_recv()
        mid[...] = (away + beside_in[1].astype(jnp.float32)).astype(jnp.bfloat16)
        third.start()
        home = tn(hot_s[0], y_s[0])
        second.wait_recv()
        home = home + beside_in[0].astype(jnp.float32)
        total = gcoef[0]
        for d in range(1, packs):
            coef_copy(d).wait_recv()
            total = total + gcoef_in[d - 1]
        third.wait_recv()
        home = home + across_in[...].astype(jnp.float32)
        results = middle(
            gx[...], home, total, table[0], routes[...], gprev[...], hst[...], ubf[0],
            small[...], wo[...], ob[...],
        )
        for ref, value in zip((ghst, go, gwo, gsmall, glog), results):
            ref[...] = value
        first.wait_send()
        second.wait_send()
        third.wait_send()
        for d in range(1, packs):
            coef_copy(d).wait_send()


def ffn_backward(layer, gm, gx, ubf, table, hst, small, routes, gprev, wo, ob, wgu, wd, number):
    packs, count, width = ubf.shape
    hidden = wd.shape[2]
    bf, f32 = jnp.bfloat16, jnp.float32
    outs = [
        shape_of((count, width), f32),
        shape_of(ob.shape, bf),
        shape_of((width, width), bf),
        shape_of((1 + NC + 16, width), f32),
        shape_of((16, count), f32),
    ]
    args = (gm, gx, ubf, table, hst, small, routes, gprev, wo, ob)
    dma = pltpu.SemaphoreType.DMA
    return pl.pallas_call(
        ffn_bwd_kernel,
        grid=(NF,),
        out_shape=outs,
        in_specs=[whole_spec(a.shape) for a in args]
        + [
            pl.BlockSpec((1, 1, 2, width, hidden), lambda e: (layer, e, 0, 0, 0)),
            pl.BlockSpec((1, 1, hidden, width), lambda e: (layer, e, 0, 0)),
        ],
        out_specs=[whole_spec(a.shape) for a in outs],
        scratch_shapes=[
            pltpu.VMEM((packs, count, width), bf),
            pltpu.VMEM((packs, NF * MOST, count), bf),
            pltpu.VMEM((NF, packs * MOST, width), bf),
            pltpu.VMEM((NF, packs * MOST, width), bf),
            pltpu.VMEM((packs, NF * MOST, width), bf),
            pltpu.VMEM((packs, NF * MOST, 1), f32),
            pltpu.VMEM((packs, NF * MOST, 1), f32),
            pltpu.VMEM((packs, NF, count), f32),
            pltpu.VMEM((packs - 1, NF, count), f32),
        ]
        + exchange_scratch(packs, count, width)
        + [dma((3,))] * 6,
        compiler_params=params_of(collective_id=number, has_side_effects=True),
        name="ffn_bwd",
    )(*args, wgu, wd)


def dispatch_kernel(ext, gm, x, g):
    count = gm.shape[1]
    rows = ext[0, count:, :].astype(jnp.float32)
    coef, slot = rows[:NF, :count], rows[:NF, count : 2 * count].astype(jnp.int32)
    ids = lax.broadcasted_iota(jnp.int32, (NF, MOST, count), 1)
    hit = ids == slot[:, None, :]
    hot = jnp.where(hit, 1.0, 0.0).astype(jnp.bfloat16).reshape(NF * MOST, count)
    weighted = jnp.where(hit, coef[:, None, :], 0.0).astype(jnp.bfloat16).reshape(NF * MOST, count)
    x[...] = nn(hot, ext[0, :count, :]).astype(jnp.bfloat16).reshape(x.shape)
    g[...] = nn(weighted, gm[0]).astype(jnp.bfloat16).reshape(g.shape)


def dispatch(ext, gm):
    devices, count, width = gm.shape
    grouped = pl.BlockSpec((NF, 1, MOST, width), lambda d: (0, d, 0, 0))
    outs = shape_of((NF, devices, MOST, width), jnp.bfloat16)
    return pl.pallas_call(
        dispatch_kernel,
        grid=(devices,),
        out_shape=[outs, outs],
        in_specs=[
            pl.BlockSpec((1,) + ext.shape[1:], lambda d: (d, 0, 0)),
            pl.BlockSpec((1, count, width), lambda d: (d, 0, 0)),
        ],
        out_specs=[grouped, grouped],
        compiler_params=params_of(),
        name="dispatch",
    )(ext, gm)


def dw_kernel(*refs):
    x, g, wgu, wd, dgu, dd, dg_s, du_s, hid_s = refs[:4] + refs[-5:]
    rows = x.shape[1]
    chunk = 256

    def pieces(i, _):
        part = pl.ds(pl.multiple_of(i * chunk, chunk), chunk)
        xs = x[0, part, :]
        hid, dg, du = silu_parts(nn(xs, wgu[0, 0, 0]), nn(xs, wgu[0, 0, 1]), nt(g[0, part, :], wd[0, 0]))
        hid_s[part, :] = hid.astype(jnp.bfloat16)
        dg_s[part, :] = dg
        du_s[part, :] = du
        return 0

    lax.fori_loop(0, rows // chunk, pieces, 0)

    def first(i, _):
        part = pl.ds(pl.multiple_of(i * 256, 256), 256)
        xs = x[0, :, part]
        dgu[0, 0, 0, part, :] = tn(xs, dg_s[...])
        dgu[0, 0, 1, part, :] = tn(xs, du_s[...])
        return 0

    lax.fori_loop(0, x.shape[2] // 256, first, 0)

    def second(i, _):
        part = pl.ds(pl.multiple_of(i * 256, 256), 256)
        dd[0, 0, part, :] = tn(hid_s[:, part], g[0])
        return 0

    lax.fori_loop(0, hid_s.shape[1] // 256, second, 0)


def weight_grads(layer, x, g, wgu, wd, earlier):
    _, rows, width = x.shape
    hidden = wd.shape[2]
    gu_spec = pl.BlockSpec((1, 1, 2, width, hidden), lambda e: (layer, e, 0, 0, 0))
    d_spec = pl.BlockSpec((1, 1, hidden, width), lambda e: (layer, e, 0, 0))
    row_spec = pl.BlockSpec((1, rows, width), lambda e: (e, 0, 0))
    kernel = dw_kernel
    return pl.pallas_call(
        kernel,
        grid=(NF,),
        out_shape=[shape_of(wgu.shape, jnp.float32), shape_of(wd.shape, jnp.float32)],
        in_specs=[row_spec, row_spec, gu_spec, d_spec] + [pl.BlockSpec(memory_space=pl.ANY)] * len(earlier),
        out_specs=[gu_spec, d_spec],
        input_output_aliases={4 + i: i for i in range(len(earlier))},
        scratch_shapes=[pltpu.VMEM((rows, hidden), jnp.bfloat16)] * 3,
        compiler_params=params_of(),
        name="weight_grads",
    )(x, g, wgu, wd, *earlier)


def norm_low(x, gain):
    return ((x * rms_factor(x)) * gain).astype(jnp.bfloat16)


def post_attention(ob, x, wo, gain):
    groups = wo.shape[0]
    inner = wo.shape[1]
    blk = ob.shape[1]
    halves = []
    for h in range(2):
        total = x[h * blk : (h + 1) * blk]
        for g in range(groups):
            total = total + nn(ob[h * groups + g][:, :inner], wo[g])
        halves.append(total)
    hst = jnp.concatenate(halves, axis=0)
    return hst, norm_low(hst, gain)


def mixing_rows(table):
    raw, coef = table[RAW : RAW + 16], table[COEF : COEF + 16]
    pairs = []
    for c in range(NC):
        r0, r1 = raw[NE + 2 * c : NE + 2 * c + 1], raw[NE + 2 * c + 1 : NE + 2 * c + 2]
        top = jnp.maximum(r0, r1)
        e0, e1 = jnp.exp(r0 - top), jnp.exp(r1 - top)
        pairs.append((e0 / (e0 + e1), e1 / (e0 + e1)))
    shares = [coef[NF + 2 + c : NF + 3 + c] for c in range(NC)]
    scale_u = coef[NF + 1 : NF + 2]
    for c in range(NC):
        scale_u = scale_u + shares[c] * pairs[c][0]
    return pairs, shares, scale_u, [shares[c] * pairs[c][1] for c in range(NC)]


def middle(gx, parts, gcoef, table, routes, gprev, hst, ub, small, wo, ob):
    groups = wo.shape[0]
    inner = wo.shape[1]
    blk = ob.shape[1]
    gain = small[1:2].astype(jnp.float32)
    consts = small[2 : 2 + NC].astype(jnp.float32)
    router = small[2 + NC :]
    pairs, shares, scale_u, scale_c = mixing_rows(table)
    columns = to_columns([scale_u] + scale_c)
    factor = rms_factor(hst)
    base = hst * factor
    u = base * gain
    dots = [jnp.sum(gx * u, axis=1, keepdims=True)]
    dots += [jnp.sum(gx * consts[c : c + 1], axis=1, keepdims=True) for c in range(NC)]
    dots = to_rows(dots, 8)
    dot_u = dots[0:1]
    dot_c = [dots[1 + c : 2 + c] for c in range(NC)]
    ids = lax.broadcasted_iota(jnp.int32, (16, gx.shape[0]), 0)
    grads = jnp.concatenate([gcoef, jnp.zeros_like(gcoef)], axis=0)
    grads = jnp.where(ids == NF + 1, dot_u, grads)
    raw_rows = []
    for c in range(NC):
        a0, a1 = pairs[c]
        grads = jnp.where(ids == NF + 2 + c, a0 * dot_u + a1 * dot_c[c], grads)
        g0, g1 = shares[c] * dot_u, shares[c] * dot_c[c]
        both = a0 * g0 + a1 * g1
        raw_rows += [a0 * (g0 - both), a1 * (g1 - both)]
    logits = table[LOGI : LOGI + 16]
    first, second = ids == routes[0:1], ids == routes[1:2]

    def pick(chosen, rows):
        return jnp.sum(jnp.where(chosen, rows, 0.0), axis=0, keepdims=True)

    z0, z1 = pick(first, logits), pick(second, logits)
    top = jnp.maximum(z0, z1)
    e0, e1 = jnp.exp(z0 - top), jnp.exp(z1 - top)
    w0, w1 = e0 / (e0 + e1), e1 / (e0 + e1)
    gg0, gg1 = pick(first, grads), pick(second, grads)
    both = w0 * gg0 + w1 * gg1
    glog = jnp.where(first, w0 * (gg0 - both), 0.0) + jnp.where(second, w1 * (gg1 - both), 0.0) + gprev
    graw = glog
    for index, row in enumerate(raw_rows):
        graw = jnp.where(ids == NE + index, row, graw)
    graw = graw.astype(jnp.bfloat16)
    grad_router = nn(graw, ub)
    gu = gx * columns[0] + tn(graw, router) + parts
    sums = [jnp.sum(gu * base, axis=0, keepdims=True)]
    sums += [jnp.sum(gx * columns[1 + c], axis=0, keepdims=True) for c in range(NC)]
    gb = gu * gain
    ghst = gx + factor * (gb - base * jnp.mean(gb * base, axis=-1, keepdims=True))
    gy = ghst.astype(jnp.bfloat16)
    lanes = ob.shape[2]
    go, gwo = [None] * (2 * groups), []
    for g in range(groups):
        value = nt(gy, wo[g]).astype(jnp.bfloat16)
        value = jnp.concatenate([value, jnp.zeros((value.shape[0], lanes - inner), jnp.bfloat16)], axis=1)
        for h in range(2):
            go[h * groups + g] = value[h * blk : (h + 1) * blk]
        mixed = jnp.concatenate([ob[g], ob[groups + g]], axis=0)
        gwo.append(tn(mixed, gy)[:inner].astype(jnp.bfloat16))
    return ghst, jnp.stack(go), jnp.concatenate(gwo, axis=0), jnp.concatenate(sums + [grad_router], axis=0), glog


def turn_tables(seq):
    half = HEAD_DIM // 2
    frequency = np.exp((-np.log(np.float32(10000.0)) * np.arange(half, dtype=np.float32) / np.float32(half)))
    angles = np.arange(seq, dtype=np.float32)[:, None] * frequency.astype(np.float32)[None, :]
    cosine, sine = np.cos(angles), np.sin(angles)
    cosine = np.concatenate([cosine, cosine] * 2, axis=1).astype(np.float32)
    sine = np.concatenate([-sine, sine] * 2, axis=1).astype(np.float32)
    return jnp.asarray(cosine), jnp.asarray(sine)


def by_heads(
    tokens,
    cotangent,
    seq_lengths,
    block_order,
    routes,
    gains,
    qkv_weights,
    out_weight,
    router,
    const_values,
    w_gate_up,
    w_down,
):
    count, width = tokens.shape[1], tokens.shape[2]
    ctx_size, packs = lax.axis_size("ctx"), lax.axis_size("fsdp")
    blk = count // 2
    seq = blk * ctx_size
    pack = lax.axis_index("fsdp")
    z, xx, y, k = place()
    sequence = z // 2
    shard = width // packs
    f32, bf = jnp.float32, jnp.bfloat16
    everyone = ("ctx", "fsdp")

    cosine, sine = turn_tables(seq)
    routes_t = jnp.swapaxes(routes[:, 0], 1, 2)
    smalls = jnp.concatenate([gains, const_values, jnp.swapaxes(router, 1, 2)], axis=1)
    per_layer = smalls.shape[1]
    ints = jnp.concatenate([routes_t.reshape(-1), block_order[0]])
    places = ints.size
    ints = jnp.pad(ints, (0, -places % shard)).astype(bf).reshape(-1, shard)
    smalls = jnp.concatenate([smalls.reshape(LAYERS * per_layer, shard), ints], axis=0)
    smalls = jnp.pad(smalls, ((0, -smalls.shape[0] % 16), (0, 0)))
    smalls = lax.all_gather(smalls, "fsdp", axis=1, tiled=True)
    ints = smalls[LAYERS * per_layer : LAYERS * per_layer + ints.shape[0]].reshape(-1, packs, shard)
    ints = jnp.swapaxes(ints, 0, 1).reshape(packs, -1).astype(jnp.int32)
    smalls = [smalls[l * per_layer : (l + 1) * per_layer] for l in range(LAYERS)]
    near = jnp.stack([pack, 2 * y + 1 - k, 2 * (1 - y) + k, 2 * (1 - y) + 1 - k])
    routes_f = ints[near][:, : routes_t.size].reshape((packs,) + routes_t.shape)
    order = lax.dynamic_index_in_dim(ints, 2 * y + xx, 0, keepdims=False)
    order = order[routes_t.size : places].reshape(ctx_size, 2)
    order = lax.dynamic_index_in_dim(order, sequence, 1, keepdims=False) - ctx_size * sequence
    ids = jnp.arange(ctx_size, dtype=jnp.int32)
    inv = jnp.sum(jnp.where(order[None, :] == ids[:, None], ids[None, :], 0), axis=1)

    gm_all = [None, lax.all_gather(cotangent[0], everyone, axis=0, tiled=False)]
    x = tokens[0].astype(f32)
    before = jnp.zeros((packs, 16, count), f32)
    kept, ext_all = [], [None] * LAYERS
    for l in range(LAYERS):
        if l == 1:
            x, gm_all[1] = lax.optimization_barrier((x, gm_all[1]))
        n1s, qkv, o, lse, ob, hst, ub, w, wo = attn_forward(
            l, order, inv, x, smalls[l], qkv_weights, cosine, sine, out_weight, 2 * l
        )
        ubf, table, ext, x_next = ffn_forward(
            l, ub, hst, smalls[l], routes_f[:, l], before, w_gate_up, w_down, 2 * l + 1
        )
        before = table[:, LOGI : LOGI + 16]
        ext_all[l] = lax.all_gather(ext, everyone, axis=0, tiled=False)
        kept.append((x, n1s, qkv, o, lse, ob, hst, w, wo, ubf, table))
        x = x_next
    output = x
    gm = cotangent[0]
    gx = gm.astype(f32)
    gprev = jnp.zeros((16, count), f32)
    small_grads, qkv_grads, out_grads = [None] * LAYERS, [None] * LAYERS, [None] * LAYERS
    for l in reversed(range(LAYERS)):
        x, n1s, qkv, o, lse, ob, hst, w, wo, ubf, table = kept[l]
        number = 2 * LAYERS + 2 * l
        gm, ext_all[l - 1 if l else 1] = lax.optimization_barrier((gm, ext_all[l - 1 if l else 1]))
        ghst, go, gwo, small, gprev = ffn_backward(
            l, gm, gx, ubf, table, hst, smalls[l], routes_t[l], gprev, wo, ob, w_gate_up, w_down, number
        )
        gx, gm, gw = attn_backward(
            order, inv, n1s, w, cosine, sine, qkv, o, lse, go, ghst, x, smalls[l], small, number + 1
        )
        if l > 0:
            gm_all[l - 1] = lax.all_gather(gm, everyone, axis=0, tiled=False)
            gw, gwo, gm_all[l - 1] = lax.optimization_barrier((gw, gwo, gm_all[l - 1]))
        out_grads[l] = lax.psum_scatter(gwo, "fsdp", scatter_dimension=0, tiled=True)
        qkv_grads[l] = lax.psum_scatter(gw, "fsdp", scatter_dimension=0, tiled=True)
    done = ()
    for l in reversed(range(LAYERS)):
        x_all, g_all = dispatch(ext_all[l], gm_all[l])
        rows = x_all.shape[1] * x_all.shape[2]
        done = weight_grads(l, x_all.reshape(NF, rows, width), g_all.reshape(NF, rows, width), w_gate_up, w_down, done)
        if l > 0:
            qkv_grads, out_grads, done = lax.optimization_barrier((qkv_grads, out_grads, done))
    dense = jnp.concatenate([jnp.stack(qkv_grads), jnp.stack(out_grads)], axis=2)
    dense = lax.psum(dense, "ctx").astype(f32)
    qkv_sum = jnp.stack([dense[:, :, c * width : (c + 1) * width] for c in range(3)], axis=1)
    small = jnp.swapaxes(dense[:, :, 3 * width : 3 * width + 128], 1, 2)
    return (
        output[None],
        gx[None],
        small[:, :2],
        qkv_sum,
        dense[:, :, 3 * width + 128 :],
        dense[:, :, 3 * width + 2 + NC : 3 * width + 2 + NC + 16],
        small[:, 2 : 2 + NC],
        done[0],
        done[1],
    )


def solution(mesh):
    placed = (
        P("fsdp", "ctx", None),
        P("fsdp", "ctx", None),
        P("fsdp", None),
        P("fsdp", None),
        P(None, "fsdp", "ctx", None),
        P(None, None, "fsdp"),
        P(None, None, "fsdp", None),
        P(None, "fsdp", None),
        P(None, "fsdp", None),
        P(None, None, "fsdp"),
        P(None, None, None, None, "fsdp"),
        P(None, None, "fsdp", None),
    )
    contexts, packs = mesh.shape["ctx"], mesh.shape["fsdp"]
    blocks_of_heads = HEADS // GROUP_HEADS

    def plan(*args):
        tokens = args[0]
        even = tokens.shape[1] * contexts == 2 * MINLEN
        grouped = contexts == 2 * blocks_of_heads and packs == blocks_of_heads
        return (by_heads if even and grouped else shards)(*args)

    return jax.shard_map(
        plan,
        mesh=mesh,
        in_specs=placed,
        out_specs=(
            P("fsdp", "ctx", None),
            P("fsdp", "ctx", None),
            P(None, None, "fsdp"),
            P(None, None, "fsdp", None),
            P(None, "fsdp", None),
            P(None, "fsdp", None),
            P(None, None, "fsdp"),
            P(None, None, None, None, "fsdp"),
            P(None, None, "fsdp", None),
        ),
        check_vma=False,
    )
```

```python
import functools

import jax
import jax.numpy as jnp
import numpy as np
from jax import lax
from jax.experimental import pallas as pl
from jax.experimental.pallas import tpu as pltpu
from jax.sharding import PartitionSpec as P

HEADS = 12
HEAD_DIM = 64
NF = 8
NC = 2
LAYERS = 2
NE = 12
MOST = 64
GROUP_HEADS = 3


def from_behind(x, axis, by):
    devices = lax.axis_size(axis)
    return lax.ppermute(x, axis, [(i, (i + by) % devices) for i in range(devices)])


def layout_tables(lengths, order_row, tok_count):
    block_len = tok_count // 2
    pack_len = order_row.shape[0] * block_len
    pack_rows = jnp.arange(pack_len, dtype=jnp.int32)
    owner = pack_rows // tok_count
    which_half = pack_rows % tok_count // block_len
    block_ids = order_row[2 * owner + which_half]
    pack_pos = block_ids * block_len + pack_rows % block_len
    segment = (pack_pos >= lengths[0]).astype(jnp.int32)
    seq_pos = pack_pos - segment * lengths[0]
    return (pack_pos, segment, seq_pos)


def angle_tables(seq_pos, head_size):
    half_size = head_size // 2
    frequency = jnp.exp(-jnp.log(10000.0) * jnp.arange(half_size, dtype=jnp.float32) / half_size)
    angles = seq_pos.astype(jnp.float32)[:, None] * frequency[None, :]
    return (jnp.cos(angles)[:, None, :], jnp.sin(angles)[:, None, :])


def rotate_pairs(values, cosine_table, sine_table, direction):
    half_size = values.shape[-1] // 2
    first_half = values[..., :half_size]
    second_half = values[..., half_size:]
    return jnp.concatenate(
        [
            first_half * cosine_table - direction * second_half * sine_table,
            second_half * cosine_table + direction * first_half * sine_table,
        ],
        axis=-1,
    )


def rms_parts(values):
    inverse = lax.rsqrt(jnp.mean(values * values, axis=-1, keepdims=True) + 1e-06)
    return (values * inverse, inverse)


def rms_back(grad_normed, base_values, inverse):
    return inverse * (
        grad_normed - base_values * jnp.mean(grad_normed * base_values, axis=-1, keepdims=True)
    )


def expert_forward(inputs_low, gate_up_use, down_use):
    gate_up_out = jnp.einsum(
        "emd,ecdf->ecmf", inputs_low, gate_up_use, preferred_element_type=jnp.float32
    )
    hidden_low = (jax.nn.silu(gate_up_out[:, 0]) * gate_up_out[:, 1]).astype(jnp.bfloat16)
    partial_value = jnp.einsum(
        "emf,efd->emd", hidden_low, down_use, preferred_element_type=jnp.float32
    )
    return (gate_up_out, hidden_low, partial_value)


def expert_backward(inputs_low, gate_up_out, hidden_low, grad_part_low, gate_up_use, down_use):
    grad_down = jnp.einsum(
        "emf,emd->efd", hidden_low, grad_part_low, preferred_element_type=jnp.float32
    )
    grad_hidden = jnp.einsum(
        "emd,efd->emf", grad_part_low, down_use, preferred_element_type=jnp.float32
    )
    gate_out = gate_up_out[:, 0]
    sigmoid_gate = jax.nn.sigmoid(gate_out)
    grad_pair_low = jnp.stack(
        [
            grad_hidden
            * gate_up_out[:, 1]
            * sigmoid_gate
            * (1.0 + gate_out * (1.0 - sigmoid_gate)),
            grad_hidden * gate_out * sigmoid_gate,
        ],
        axis=1,
    ).astype(jnp.bfloat16)
    grad_gate_up = jnp.einsum(
        "emd,ecmf->ecdf", inputs_low, grad_pair_low, preferred_element_type=jnp.float32
    )
    grad_rows = jnp.einsum(
        "ecmf,ecdf->emd", grad_pair_low, gate_up_use, preferred_element_type=jnp.float32
    )
    return (grad_gate_up, grad_down, grad_rows)


def shards(
    tokens,
    cotangent,
    seq_lengths,
    block_order,
    routes,
    gains,
    qkv_weights,
    out_weight,
    router,
    const_values,
    w_gate_up,
    w_down,
):
    tok_count = tokens.shape[1]
    width = tokens.shape[2]
    ctx_size = lax.axis_size("ctx")
    own_index = lax.axis_index("ctx")
    score_scale = HEAD_DIM ** (-0.5)
    pack_pos, segment, seq_pos = layout_tables(seq_lengths[0], block_order[0], tok_count)
    own_start = own_index * tok_count
    query_pos = lax.dynamic_slice_in_dim(pack_pos, own_start, tok_count)
    query_seg = lax.dynamic_slice_in_dim(segment, own_start, tok_count)
    cosine_table, sine_table = angle_tables(
        lax.dynamic_slice_in_dim(seq_pos, own_start, tok_count), HEAD_DIM
    )
    head_shape = (tok_count, HEADS, HEAD_DIM)
    expert_ids = jnp.arange(NE, dtype=jnp.int32)
    slot_ids = jnp.arange(MOST, dtype=jnp.int32)
    row_ids = jnp.arange(tok_count, dtype=jnp.int32)

    def allowed_pairs(key_offset, key_count):
        key_pos = lax.dynamic_slice_in_dim(pack_pos, key_offset, key_count)
        key_seg = lax.dynamic_slice_in_dim(segment, key_offset, key_count)
        return (query_seg[:, None] == key_seg[None, :]) & (key_pos[None, :] <= query_pos[:, None])

    stream = tokens[0].astype(jnp.float32)
    previous = jnp.zeros((tok_count, NE), jnp.float32)
    saved = []
    for layer_index in range(LAYERS):
        gain_all, qkv_all, out_all, router_all, const_all = (
            lax.all_gather(gains[layer_index], "fsdp", axis=1, tiled=True),
            lax.all_gather(qkv_weights[layer_index], "fsdp", axis=1, tiled=True),
            lax.all_gather(out_weight[layer_index], "fsdp", axis=0, tiled=True),
            lax.all_gather(router[layer_index], "fsdp", axis=0, tiled=True),
            lax.all_gather(const_values[layer_index], "fsdp", axis=1, tiled=True),
        )
        gain_float = gain_all.astype(jnp.float32)
        base_one, inverse_one = rms_parts(stream)
        normed_low = (base_one * gain_float[0]).astype(jnp.bfloat16)
        projected = jnp.einsum(
            "td,cde->cte", normed_low, qkv_all, preferred_element_type=jnp.float32
        )
        queries_low = rotate_pairs(
            projected[0].reshape(head_shape), cosine_table, sine_table, 1.0
        ).astype(jnp.bfloat16)
        keys_low = rotate_pairs(
            projected[1].reshape(head_shape), cosine_table, sine_table, 1.0
        ).astype(jnp.bfloat16)
        values_low = projected[2].reshape(head_shape).astype(jnp.bfloat16)

        def fold_step(running, shard_piece, offset, queries_use=queries_low):
            keys_piece, values_piece = shard_piece
            allowed = allowed_pairs(offset, keys_piece.shape[0])[None]
            scores = (
                jnp.einsum(
                    "qhd,khd->hqk", queries_use, keys_piece, preferred_element_type=jnp.float32
                )
                * score_scale
            )
            scores = jnp.where(allowed, scores, -1e30)
            top_old, total_old, accumulated = running
            top_new = jnp.maximum(top_old, jnp.max(scores, axis=-1))
            weights = jnp.where(allowed, jnp.exp(scores - top_new[..., None]), 0.0)
            factor = jnp.exp(top_old - top_new)
            accumulated = jnp.einsum(
                "hqk,khd->hqd",
                weights.astype(jnp.bfloat16),
                values_piece,
                preferred_element_type=jnp.float32,
            )
            return (top_new, jnp.sum(weights, axis=-1), accumulated)

        starting = (
            jnp.full((HEADS, tok_count), -1e30, jnp.float32),
            jnp.zeros((HEADS, tok_count), jnp.float32),
            jnp.zeros((HEADS, tok_count, HEAD_DIM), jnp.float32),
        )
        top_value, total_sum, accumulated = fold_step(
            starting,
            (
                lax.all_gather(keys_low, "ctx", axis=0, tiled=True),
                lax.all_gather(values_low, "ctx", axis=0, tiled=True),
            ),
            jnp.int32(0),
        )
        log_total = top_value + jnp.log(total_sum)
        attended = jnp.transpose(accumulated / total_sum[..., None], (1, 0, 2))
        mixed_low = attended.reshape(tok_count, width).astype(jnp.bfloat16)
        hidden_state = stream + jnp.dot(mixed_low, out_all, preferred_element_type=jnp.float32)
        base_two, inverse_two = rms_parts(hidden_state)
        expert_in = base_two * gain_float[1]
        expert_low = expert_in.astype(jnp.bfloat16)
        raw_logits = jnp.dot(expert_low, router_all, preferred_element_type=jnp.float32)
        logits = raw_logits[:, :NE] + previous
        route_ids = routes[layer_index, 0]
        chosen = route_ids[:, :, None] == expert_ids[None, None, :]
        chosen_f = chosen.astype(jnp.float32)
        hit_count = jnp.sum(chosen.astype(jnp.int32), axis=1)
        slot_index = jnp.cumsum(hit_count, axis=0) - 1
        picked = jnp.sum(chosen_f * logits[:, None, :], axis=-1)
        gate_weights = jax.nn.softmax(picked, axis=-1)
        coeffs = jnp.sum(gate_weights[:, :, None] * chosen_f, axis=1)
        slot_table = jnp.zeros((NF, MOST), jnp.int32)
        for expert in range(NF):
            target = jnp.where(hit_count[:, expert] > 0, slot_index[:, expert], MOST)
            slot_table = slot_table.at[expert, target].set(row_ids, mode="drop")
        filled = (slot_ids[None, :] < jnp.sum(hit_count[:, :NF], axis=0)[:, None]).astype(
            jnp.float32
        )
        rows_low = expert_low[slot_table]
        inputs_low = lax.all_gather(rows_low, "fsdp", axis=1, tiled=True)
        gate_up_out, hidden_low, partial_value = expert_forward(
            inputs_low, w_gate_up[layer_index], w_down[layer_index]
        )
        result = lax.psum_scatter(
            partial_value.astype(jnp.bfloat16), "fsdp", scatter_dimension=1, tiled=True
        ).astype(jnp.float32)
        flat_index = jnp.arange(NF, dtype=jnp.int32)[None, :] * MOST + jnp.clip(
            slot_index[:, :NF], 0, MOST - 1
        )
        token_result = result.reshape(NF * MOST, width)[flat_index]
        expert_mix = (
            jnp.sum(coeffs[:, :NF, None] * token_result, axis=1)
            + coeffs[:, NF + 1 : NF + 2] * expert_in
        )
        mixings = []
        for const_index in range(NC):
            column = NE + 2 * const_index
            mixing = jax.nn.softmax(raw_logits[:, column : column + 2], axis=-1)
            mixings.append(mixing)
            expert_mix = expert_mix + coeffs[:, NF + 2 + const_index : NF + 3 + const_index] * (
                mixing[:, 0:1] * expert_in
                + mixing[:, 1:2] * const_all[const_index].astype(jnp.float32)[None, :]
            )
        saved.append(
            (
                gain_float,
                qkv_all,
                out_all,
                router_all,
                const_all,
                base_one,
                inverse_one,
                normed_low,
                queries_low,
                keys_low,
                values_low,
                log_total,
                attended,
                mixed_low,
                base_two,
                inverse_two,
                expert_in,
                expert_low,
                chosen_f,
                hit_count,
                gate_weights,
                coeffs,
                slot_table,
                filled,
                inputs_low,
                gate_up_out,
                hidden_low,
                flat_index,
                token_result,
                mixings,
            )
        )
        stream = hidden_state + expert_mix
        previous = logits
    grad_stream = cotangent[0].astype(jnp.float32)
    grad_previous = jnp.zeros((tok_count, NE), jnp.float32)
    layer_grads = [None] * LAYERS
    for layer_index in reversed(range(LAYERS)):
        (
            gain_float,
            qkv_all,
            out_all,
            router_all,
            const_all,
            base_one,
            inverse_one,
            normed_low,
            queries_low,
            keys_low,
            values_low,
            log_total,
            attended,
            mixed_low,
            base_two,
            inverse_two,
            expert_in,
            expert_low,
            chosen_f,
            hit_count,
            gate_weights,
            coeffs,
            slot_table,
            filled,
            inputs_low,
            gate_up_out,
            hidden_low,
            flat_index,
            token_result,
            mixings,
        ) = saved[layer_index]
        grad_mix = grad_stream
        dot_input = jnp.sum(grad_mix * expert_in, axis=-1, keepdims=True)
        coef_grads = [
            jnp.sum(grad_mix[:, None, :] * token_result, axis=-1),
            jnp.zeros((tok_count, 1), jnp.float32),
            dot_input,
        ]
        grad_in = grad_mix * coeffs[:, NF + 1 : NF + 2]
        const_cols = []
        const_grads = []
        for const_index in range(NC):
            mixing = mixings[const_index]
            const_row = const_all[const_index].astype(jnp.float32)[None, :]
            dot_const = jnp.sum(grad_mix * const_row, axis=-1, keepdims=True)
            share = coeffs[:, NF + 2 + const_index : NF + 3 + const_index]
            coef_grads.append(mixing[:, 0:1] * dot_input + mixing[:, 1:2] * dot_const)
            grad_in = grad_in + grad_mix * (share * mixing[:, 0:1])
            grad_mixing = share * jnp.concatenate([dot_input, dot_const], axis=1)
            const_cols.append(
                mixing * (grad_mixing - jnp.sum(mixing * grad_mixing, axis=-1, keepdims=True))
            )
            const_grads.append(jnp.sum(grad_mix * (share * mixing[:, 1:2]), axis=0))
        grad_coeffs = jnp.concatenate(coef_grads, axis=1)
        grad_gates = jnp.sum(chosen_f * grad_coeffs[:, None, :], axis=-1)
        grad_picked = gate_weights * (
            grad_gates - jnp.sum(gate_weights * grad_gates, axis=-1, keepdims=True)
        )
        grad_logits = jnp.sum(grad_picked[:, :, None] * chosen_f, axis=1) + grad_previous
        grad_previous = grad_logits
        grad_raw_low = jnp.concatenate([grad_logits] + const_cols, axis=1).astype(jnp.bfloat16)
        grad_router = jnp.einsum(
            "td,tc->dc", expert_low, grad_raw_low, preferred_element_type=jnp.float32
        )
        grad_in = grad_in + jnp.einsum(
            "tc,dc->td", grad_raw_low, router_all, preferred_element_type=jnp.float32
        )
        slot_weight = (
            jnp.take_along_axis(jnp.transpose(coeffs[:, :NF]), slot_table, axis=1) * filled
        )
        grad_result_low = (grad_mix[slot_table] * slot_weight[:, :, None]).astype(jnp.bfloat16)
        grad_part_low = lax.all_gather(grad_result_low, "fsdp", axis=1, tiled=True)
        grad_gate_up, grad_down, grad_rows = expert_backward(
            inputs_low,
            gate_up_out,
            hidden_low,
            grad_part_low,
            w_gate_up[layer_index],
            w_down[layer_index],
        )
        grad_rows = lax.psum_scatter(
            grad_rows.astype(jnp.bfloat16), "fsdp", scatter_dimension=1, tiled=True
        ).astype(jnp.float32)
        token_grads = grad_rows.reshape(NF * MOST, width)[flat_index]
        grad_in = grad_in + jnp.sum(
            jnp.where(hit_count[:, :NF, None] > 0, token_grads, 0.0), axis=1
        )
        grad_gain_two = jnp.sum(grad_in * base_two, axis=0)
        grad_hidden_state = grad_stream + rms_back(grad_in * gain_float[1], base_two, inverse_two)
        grad_out_low = grad_hidden_state.astype(jnp.bfloat16)
        grad_out_w = jnp.einsum(
            "td,te->de", mixed_low, grad_out_low, preferred_element_type=jnp.float32
        )
        grad_attended = (
            jnp.einsum("te,de->td", grad_out_low, out_all, preferred_element_type=jnp.float32)
            .astype(jnp.bfloat16)
            .reshape(head_shape)
        )
        delta = jnp.transpose(jnp.sum(grad_attended.astype(jnp.float32) * attended, axis=-1))

        def visit(
            turn_index,
            carried,
            queries_use=queries_low,
            grad_use=grad_attended,
            log_use=log_total,
            delta_use=delta,
        ):
            keys_piece, values_piece, key_grads, value_grads, query_grads = carried
            source = (own_index - turn_index) % ctx_size
            allowed = allowed_pairs(source * tok_count, tok_count)[None]
            scores = (
                jnp.einsum(
                    "qhd,khd->hqk", queries_use, keys_piece, preferred_element_type=jnp.float32
                )
                * score_scale
            )
            probs = jnp.where(
                allowed, jnp.exp(jnp.where(allowed, scores, -1e30) - log_use[..., None]), 0.0
            )
            value_grads = value_grads + jnp.einsum(
                "hqk,qhd->khd",
                probs.astype(jnp.bfloat16),
                grad_use,
                preferred_element_type=jnp.float32,
            )
            prob_grads = jnp.einsum(
                "qhd,khd->hqk", grad_use, values_piece, preferred_element_type=jnp.float32
            )
            score_grads = (probs * (prob_grads - delta_use[..., None])).astype(jnp.bfloat16)
            query_grads = query_grads + jnp.einsum(
                "hqk,khd->qhd", score_grads, keys_piece, preferred_element_type=jnp.float32
            )
            key_grads = key_grads + jnp.einsum(
                "hqk,qhd->khd", score_grads, queries_use, preferred_element_type=jnp.float32
            )
            keys_piece, values_piece = from_behind((keys_piece, values_piece), "ctx", 1)
            key_grads, value_grads = (
                from_behind(key_grads.astype(jnp.bfloat16), "ctx", 1).astype(key_grads.dtype),
                from_behind(value_grads.astype(jnp.bfloat16), "ctx", 1).astype(value_grads.dtype),
            )
            return (keys_piece, values_piece, key_grads, value_grads, query_grads)

        zero_heads = jnp.zeros(head_shape, jnp.float32)
        finished = lax.fori_loop(
            0, ctx_size, visit, (keys_low, values_low, zero_heads, zero_heads, zero_heads)
        )
        grad_query = (
            rotate_pairs(finished[4] * score_scale, cosine_table, sine_table, -1.0)
            .astype(jnp.bfloat16)
            .reshape(tok_count, width)
        )
        grad_key = (
            rotate_pairs(finished[2] * score_scale, cosine_table, sine_table, -1.0)
            .astype(jnp.bfloat16)
            .reshape(tok_count, width)
        )
        grad_value = finished[3].astype(jnp.bfloat16).reshape(tok_count, width)
        grad_proj_low = jnp.stack([grad_query, grad_key, grad_value], axis=0)
        grad_qkv = jnp.einsum(
            "td,cte->cde", normed_low, grad_proj_low, preferred_element_type=jnp.float32
        )
        grad_normed = jnp.einsum(
            "cte,cde->td", grad_proj_low, qkv_all, preferred_element_type=jnp.float32
        )
        grad_gain_one = jnp.sum(grad_normed * base_one, axis=0)
        grad_stream = grad_hidden_state + rms_back(
            grad_normed * gain_float[0], base_one, inverse_one
        )
        gains_shard, qkv_shard, out_shard, router_shard, const_shard = (
            lax.psum_scatter(
                jnp.stack([grad_gain_one, grad_gain_two]).astype(jnp.bfloat16),
                "fsdp",
                scatter_dimension=1,
                tiled=True,
            ).astype(jnp.float32),
            lax.psum_scatter(
                grad_qkv.astype(jnp.bfloat16), "fsdp", scatter_dimension=1, tiled=True
            ).astype(jnp.float32),
            lax.psum_scatter(
                grad_out_w.astype(jnp.bfloat16), "fsdp", scatter_dimension=0, tiled=True
            ).astype(jnp.float32),
            lax.psum_scatter(
                grad_router.astype(jnp.bfloat16), "fsdp", scatter_dimension=0, tiled=True
            ).astype(jnp.float32),
            lax.psum_scatter(
                jnp.stack(const_grads).astype(jnp.bfloat16), "fsdp", scatter_dimension=1, tiled=True
            ).astype(jnp.float32),
        )
        layer_grads[layer_index] = (
            lax.psum(gains_shard.astype(jnp.bfloat16), "ctx").astype(jnp.float32),
            lax.psum(qkv_shard.astype(jnp.bfloat16), "ctx").astype(jnp.float32),
            lax.psum(out_shard.astype(jnp.bfloat16), "ctx").astype(jnp.float32),
            lax.psum(router_shard.astype(jnp.bfloat16), "ctx").astype(jnp.float32),
            lax.psum(const_shard.astype(jnp.bfloat16), "ctx").astype(jnp.float32),
            lax.psum(grad_gate_up.astype(jnp.bfloat16), "ctx").astype(jnp.float32),
            lax.psum(grad_down.astype(jnp.bfloat16), "ctx").astype(jnp.float32),
        )
    stacked = [
        jnp.stack([layer_grads[layer_index][member_index] for layer_index in range(LAYERS)])
        for member_index in range(7)
    ]
    return (
        stream[None],
        grad_stream[None],
        stacked[0],
        stacked[1],
        stacked[2],
        stacked[3],
        stacked[4],
        stacked[5],
        stacked[6],
    )


MINLEN = 1024
GRAD_LANES = 768
ROUT = 56
RAW, COEF, SLOT, LOGI = 0, 16, 32, 40
VMEM_MB = 60
BRIEF = pl.CostEstimate(flops=1, bytes_accessed=1, transcendentals=0)


def nt(a, b):
    return lax.dot_general(a, b, (((1,), (1,)), ((), ())), preferred_element_type=jnp.float32)


def nn(a, b):
    return lax.dot_general(a, b, (((1,), (0,)), ((), ())), preferred_element_type=jnp.float32)


def tn(a, b):
    return lax.dot_general(a, b, (((0,), (0,)), ((), ())), preferred_element_type=jnp.float32)


def params_of(mb=VMEM_MB, **more):
    return pltpu.CompilerParams(vmem_limit_bytes=mb * 2**20, **more)


def shape_of(dims, kind):
    return jax.ShapeDtypeStruct(dims, kind)


def rms_factor(values):
    return lax.rsqrt(jnp.mean(values * values, axis=-1, keepdims=True) + 1e-06)


def to_rows(columns, count):
    lane = lax.broadcasted_iota(jnp.int32, (columns[0].shape[0], 128), 1)
    packed = jnp.zeros(lane.shape, jnp.float32)
    for index, column in enumerate(columns):
        packed = jnp.where(lane == index, column, packed)
    return jnp.transpose(packed)[:count]


def to_columns(rows):
    count = rows[0].shape[1]
    sub = lax.broadcasted_iota(jnp.int32, (128, count), 0)
    packed = jnp.zeros(sub.shape, jnp.float32)
    for index, row in enumerate(rows):
        packed = jnp.where(sub == index, row, packed)
    packed = jnp.transpose(packed)
    return [packed[:, index : index + 1] for index in range(len(rows))]


def swap_halves(values):
    lanes = values.shape[1]
    lane = lax.broadcasted_iota(jnp.int32, values.shape, 1)
    ahead = pltpu.roll(values, lanes - 32, 1)
    behind = pltpu.roll(values, 32, 1)
    return jnp.where(lane % 64 < 32, ahead, behind)


def spin(values, cosine, sine):
    return values * cosine + swap_halves(values) * sine


def place():
    own, pack = lax.axis_index("ctx"), lax.axis_index("fsdp")
    return own // 2, own % 2, pack // 2, pack % 2


def remote(src, dst, send, recv, ctx, fsdp):
    return pltpu.make_async_remote_copy(
        src_ref=src,
        dst_ref=dst,
        send_sem=send,
        recv_sem=recv,
        device_id=(ctx, fsdp),
        device_id_type=pl.DeviceIdType.MESH,
    )


def greet_plane(contexts, across=False):
    own = lax.axis_index("ctx")
    _, _, y, k = place()
    barrier = pltpu.get_barrier_semaphore()
    if across:
        for core in (k, 1 - k):
            device = (own, 2 * (1 - y) + core)
            pl.semaphore_signal(barrier, inc=1, device_id=device, device_id_type=pl.DeviceIdType.MESH)
    for ctx in range(contexts):
        for core in range(2):

            @pl.when(jnp.logical_or(ctx != own, core != k))
            def _():
                pl.semaphore_signal(barrier, inc=1, device_id=(ctx, 2 * y + core), device_id_type=pl.DeviceIdType.MESH)

    return barrier, 2 * contexts - 1 + (2 if across else 0)


def greet_packs():
    own = lax.axis_index("ctx")
    _, _, y, k = place()
    barrier = pltpu.get_barrier_semaphore()
    for fsdp in (2 * y + 1 - k, 2 * (1 - y) + k, 2 * (1 - y) + 1 - k):
        pl.semaphore_signal(barrier, inc=1, device_id=(own, fsdp), device_id_type=pl.DeviceIdType.MESH)
    return barrier, 3


def attn_fwd_kernel(
    order, inv, x, small, wq, cosine, sine, wo_own,
    n1s, qkv, o, lse, ob, hst, ub, w, wo,
    n1own, n1r, osort, osend, orecv, cols, w_s, wo_s,
    n_send, n_recv, f_send, f_recv, o_send, o_recv, w_send, w_recv, v_send, v_recv,
):
    blocks, blk, _ = n1r.shape
    lanes = o.shape[1]
    seq = blocks * blk
    step = 2 * blk
    own = lax.axis_index("ctx")
    z, xx, y, k = place()
    depth = blocks // 2
    same = xx == k
    pack = lax.axis_index("fsdp")
    inner = wo_own.shape[1]
    beside, over, corner = 2 * y + 1 - k, 2 * (1 - y) + k, 2 * (1 - y) + 1 - k

    barrier, others = greet_plane(blocks, across=True)
    n1 = norm_low(x[...], small[0:1, :].astype(jnp.float32))
    n1own[0] = n1[:blk]
    n1own[1] = n1[blk:]
    pl.semaphore_wait(barrier, others)

    def n1_copy(zz):
        return remote(n1own.at[zz // 2], n1r.at[own], n_send.at[zz], n_recv.at[z], 2 * zz + k, 2 * y + xx)

    for zz in range(depth):
        alone = jnp.logical_and(same, zz == z)

        @pl.when(jnp.logical_not(alone))
        def _():
            n1_copy(zz).start()

        @pl.when(alone)
        def _():
            n1r[own] = n1own[zz // 2]

    for half in range(2):

        @pl.when(z % 2 == half)
        def _():
            for core in range(2):
                first = (2 * half + core) * inner
                for c in range(3):
                    cols[core, :, c * lanes : c * lanes + inner] = wq[0, c, :, first : first + inner]
                    cols[core, :, c * lanes + inner : (c + 1) * lanes] = jnp.zeros((inner, lanes - inner), jnp.bfloat16)

    def rows_of(device):
        return pl.ds(pl.multiple_of(device * inner, inner), inner)

    def w_copy(index):
        device, core = ((beside, 1 - k), (over, k), (corner, 1 - k))[index]
        return remote(cols.at[core], w_s.at[rows_of(pack), :], w_send.at[index], w_recv.at[index], own, device)

    def w_wait(index):
        rows = w_s.at[rows_of((beside, over, corner)[index]), :]
        remote(cols.at[0], rows, w_send.at[index], w_recv.at[index], own, beside).wait_recv()

    w_s[rows_of(pack), :] = cols[k]
    wo_s[pack] = wo_own[0]
    for index in (1, 2, 0):
        w_copy(index).start()
    v_far = remote(wo_s.at[pack], wo_s.at[pack], v_send.at[0], v_recv.at[0], own, over)
    v_near = remote(wo_s.at[pack], wo_s.at[pack], v_send.at[1], v_recv.at[1], own, beside)
    v_on = remote(wo_s.at[over], wo_s.at[over], v_send.at[2], v_recv.at[2], own, beside)
    v_far.start()
    v_near.start()

    def forward_copy(zz):
        slot = n1r.at[2 * zz + k]
        return remote(slot, slot, f_send.at[zz], f_recv.at[zz], own, 2 * y + 1 - k)

    for zz in range(depth):

        @pl.when(jnp.logical_not(jnp.logical_and(same, zz == z)))
        def _():
            remote(n1own.at[0], n1r.at[2 * zz + k], n_send.at[zz], n_recv.at[zz], 2 * zz + k, 2 * y + xx).wait_recv()

        forward_copy(zz).start()
    for zz in range(depth):
        slot = n1r.at[2 * zz + 1 - k]
        remote(slot, slot, f_send.at[zz], f_recv.at[zz], own, 2 * y + 1 - k).wait_recv()

    for index in range(3):
        w_wait(index)
    w[...] = w_s[...]
    for b in range(blocks):
        n1s[b * blk : (b + 1) * blk, :] = n1r[inv[b]]
    for i in range(seq // step):
        part = slice(i * step, (i + 1) * step)
        out = nn(n1s[part, :], w_s[...])
        cos2 = jnp.concatenate([cosine[part, :]] * (lanes // 128), axis=1)
        sin2 = jnp.concatenate([sine[part, :]] * (lanes // 128), axis=1)
        q = spin(out[:, :lanes], cos2, sin2).astype(jnp.bfloat16)
        qkv[part, :lanes] = q * jnp.asarray(HEAD_DIM**-0.5, jnp.bfloat16)
        qkv[part, lanes : 2 * lanes] = spin(out[:, lanes : 2 * lanes], cos2, sin2).astype(jnp.bfloat16)
        qkv[part, 2 * lanes :] = out[:, 2 * lanes :].astype(jnp.bfloat16)
    lane = lax.broadcasted_iota(jnp.int32, (step, 128), 1)
    for i in range(seq // step):
        part = slice(i * step, (i + 1) * step)
        span = (i + 1) * step
        seen = lax.broadcasted_iota(jnp.int32, (step, span), 1) <= (
            lax.broadcasted_iota(jnp.int32, (step, span), 0) + i * step
        )
        logs = jnp.zeros((step, 128), jnp.float32)
        for head in range(GROUP_HEADS):
            tile, side = head // 2, head % 2
            at = tile * 128
            mine = lane // 64 == side
            q = jnp.where(mine, qkv[part, at : at + 128], jnp.asarray(0, jnp.bfloat16))
            s = nt(q, qkv[:span, lanes + at : lanes + at + 128])
            s = jnp.where(seen, s, -1e30)
            top = jnp.max(s, axis=1, keepdims=True)
            p = jnp.exp(s - top)
            total = jnp.sum(p, axis=1, keepdims=True)
            out = nn(p.astype(jnp.bfloat16), qkv[:span, 2 * lanes + at : 2 * lanes + at + 128]) / total
            logs = jnp.where(lane == head, top + jnp.log(total), logs)
            if side == 0:
                kept = jnp.where(mine, out, 0.0)
            else:
                kept = jnp.where(mine, out, kept)
            o[part, at : at + 128] = kept
        lse[part, :] = logs
        osort[2 * i] = o[part, :][:blk].astype(jnp.bfloat16)
        osort[2 * i + 1] = o[part, :][blk:].astype(jnp.bfloat16)

    mine_at = 2 * z + k
    remote(wo_s.at[over], wo_s.at[over], v_send.at[0], v_recv.at[0], own, over).wait_recv()
    v_on.start()

    def o_copy(ctx):
        return remote(osend.at[ctx], orecv.at[mine_at], o_send.at[ctx], o_recv.at[mine_at], ctx, 2 * y + xx)

    for ctx in range(blocks):
        alone = jnp.logical_and(same, ctx == own)
        osend[ctx] = osort[order[ctx]]

        @pl.when(jnp.logical_not(alone))
        def _():
            o_copy(ctx).start()

        @pl.when(alone)
        def _():
            orecv[mine_at] = osend[ctx]

    for src in range(blocks):

        @pl.when(jnp.logical_not(jnp.logical_and(same, src == mine_at)))
        def _():
            remote(osend.at[0], orecv.at[src], o_send.at[0], o_recv.at[src], 2 * (src // 2) + k, 2 * y + src % 2).wait_recv()

    ob[...] = orecv[...]
    remote(wo_s.at[beside], wo_s.at[beside], v_send.at[1], v_recv.at[1], own, beside).wait_recv()
    remote(wo_s.at[corner], wo_s.at[corner], v_send.at[2], v_recv.at[2], own, beside).wait_recv()
    wo[...] = wo_s[...]
    total, low = post_attention(orecv[...], x[...], wo_s[...], small[1:2, :].astype(jnp.float32))
    hst[...] = total
    ub[...] = low
    for zz in range(depth):

        @pl.when(jnp.logical_not(jnp.logical_and(same, zz == z)))
        def _():
            n1_copy(zz).wait_send()

        forward_copy(zz).wait_send()
    for index in range(3):
        w_copy(index).wait_send()
    v_far.wait_send()
    v_near.wait_send()
    v_on.wait_send()
    for ctx in range(blocks):

        @pl.when(jnp.logical_not(jnp.logical_and(same, ctx == own)))
        def _():
            o_copy(ctx).wait_send()


def attn_forward(layer, order, inv, x, small, wq, cosine, sine, wo, number):
    count, width = x.shape
    blocks, blk = order.shape[0], count // 2
    packs, inner = width // wo.shape[1], wo.shape[1]
    lanes = -(-inner // 128) * 128
    seq = blocks * blk
    vm = pl.BlockSpec(memory_space=pltpu.VMEM)
    sm = pl.BlockSpec(memory_space=pltpu.SMEM)
    bf = jnp.bfloat16
    dma = pltpu.SemaphoreType.DMA
    return pl.pallas_call(
        attn_fwd_kernel,
        grid=(1,),
        out_shape=[
            shape_of((seq, width), bf),
            shape_of((seq, 3 * lanes), bf),
            shape_of((seq, lanes), jnp.float32),
            shape_of((seq, 128), jnp.float32),
            shape_of((blocks, blk, lanes), bf),
            shape_of((count, width), jnp.float32),
            shape_of((count, width), bf),
            shape_of((width, 3 * lanes), bf),
            shape_of((packs, inner, width), bf),
        ],
        in_specs=[sm, sm, vm, vm]
        + [pl.BlockSpec((1, 3, inner, width), lambda _: (layer, 0, 0, 0)), vm, vm]
        + [pl.BlockSpec((1, inner, width), lambda _: (layer, 0, 0))],
        out_specs=[vm] * 9,
        scratch_shapes=[
            pltpu.VMEM((2, blk, width), bf),
            pltpu.VMEM((blocks, blk, width), bf),
            pltpu.VMEM((blocks, blk, lanes), bf),
            pltpu.VMEM((blocks, blk, lanes), bf),
            pltpu.VMEM((blocks, blk, lanes), bf),
            pltpu.VMEM((2, inner, 3 * lanes), bf),
            pltpu.VMEM((width, 3 * lanes), bf),
            pltpu.VMEM((packs, inner, width), bf),
        ]
        + [dma((blocks // 2,))] * 4
        + [dma((blocks,))] * 2
        + [dma((3,))] * 4,
        compiler_params=params_of(collective_id=number, has_side_effects=True),
        cost_estimate=BRIEF,
        name="attn_fwd",
    )(order, inv, x, small, wq, cosine, sine, wo)


def attn_bwd_kernel(
    order, inv, n1s, w, cosine, sine, qkv, o, lse, go, ghst, x, small, gsmall,
    gx, gm, gw,
    gor, gos, grads, acc, keep, sib_out, sib_in, gn_out, gnr,
    o_send, o_recv, s_send, s_recv, g_send, g_recv,
):
    blocks, blk, width = grads.shape
    lanes = o.shape[1]
    seq = blocks * blk
    step = 2 * blk
    zero = jnp.asarray(0, jnp.bfloat16)
    own = lax.axis_index("ctx")
    z, xx, y, k = place()
    depth = blocks // 2
    same = xx == k

    barrier, others = greet_plane(blocks)
    acc[...] = jnp.zeros_like(acc)
    pl.semaphore_wait(barrier, others)

    def go_copy(unit):
        return remote(go.at[unit], gor.at[own], o_send.at[unit], o_recv.at[own], 2 * (unit // 2) + k, 2 * y + unit % 2)

    for unit in range(blocks):
        alone = jnp.logical_and(same, unit == 2 * z + k)

        @pl.when(jnp.logical_not(alone))
        def _():
            go_copy(unit).start()

        @pl.when(alone)
        def _():
            gor[own] = go[unit]

    for ctx in range(blocks):

        @pl.when(jnp.logical_not(jnp.logical_and(same, ctx == own)))
        def _():
            remote(go.at[0], gor.at[ctx], o_send.at[0], o_recv.at[ctx], ctx, 2 * y + xx).wait_recv()

    for b in range(blocks):
        gos[b * blk : (b + 1) * blk, :] = gor[inv[b]]
    lane = lax.broadcasted_iota(jnp.int32, (step, 128), 1)
    for i in range(seq // step):
        part = slice(i * step, (i + 1) * step)
        span = (i + 1) * step
        seen = lax.broadcasted_iota(jnp.int32, (step, span), 1) <= (
            lax.broadcasted_iota(jnp.int32, (step, span), 0) + i * step
        )
        key_lane = lax.broadcasted_iota(jnp.int32, (span, 128), 1)
        for head in range(GROUP_HEADS):
            tile, side = head // 2, head % 2
            at = tile * 128
            mine = lane // 64 == side
            q = jnp.where(mine, qkv[part, at : at + 128], zero)
            g = jnp.where(mine, gos[part, at : at + 128], zero)
            keys = qkv[:span, lanes + at : lanes + at + 128]
            values = qkv[:span, 2 * lanes + at : 2 * lanes + at + 128]
            delta = jnp.sum(g.astype(jnp.float32) * o[part, at : at + 128], axis=1, keepdims=True)
            s = nt(q, keys)
            p = jnp.where(seen, jnp.exp(jnp.where(seen, s, -1e30) - lse[part, head : head + 1]), 0.0)
            ds = (p * (nt(g, values) - delta)).astype(jnp.bfloat16)
            acc[:span, 2 * lanes + at : 2 * lanes + at + 128] += tn(p.astype(jnp.bfloat16), g)
            acc[:span, lanes + at : lanes + at + 128] += tn(ds, q)
            acc[part, at : at + 128] += nn(ds, jnp.where(key_lane // 64 == side, keys, zero))
    for b in range(blocks):
        part = slice(b * blk, (b + 1) * blk)
        cos2 = jnp.concatenate([cosine[part, :]] * (lanes // 128), axis=1)
        sin2 = jnp.concatenate([sine[part, :]] * (lanes // 128), axis=1)
        grads[b, :, :lanes] = spin(acc[part, :lanes] * HEAD_DIM**-0.5, cos2, -sin2).astype(jnp.bfloat16)
        grads[b, :, lanes : 2 * lanes] = spin(acc[part, lanes : 2 * lanes], cos2, -sin2).astype(jnp.bfloat16)
        grads[b, :, 2 * lanes :] = acc[part, 2 * lanes :].astype(jnp.bfloat16)

    def sib_copy(zz):
        return remote(sib_out.at[zz], sib_in.at[zz], s_send.at[zz], s_recv.at[zz], own, 2 * y + 1 - k)

    def gn_copy(zz):
        return remote(gn_out.at[zz], gnr.at[z], g_send.at[zz], g_recv.at[z], 2 * zz + k, 2 * y + xx)

    for zz in range(depth):
        sib_out[zz] = nt(grads[order[2 * zz + 1 - k]], w[...]).astype(jnp.bfloat16)
        sib_copy(zz).start()
    for zz in range(depth):
        keep[zz] = nt(grads[order[2 * zz + k]], w[...])
    for zz in range(depth):
        sib_copy(zz).wait_recv()
        alone = jnp.logical_and(same, zz == z)
        gn_out[zz] = (keep[zz] + sib_in[zz].astype(jnp.float32)).astype(jnp.bfloat16)

        @pl.when(jnp.logical_not(alone))
        def _():
            gn_copy(zz).start()

        @pl.when(alone)
        def _():
            gnr[z] = gn_out[zz]

    inner = GROUP_HEADS * HEAD_DIM
    gw[:, 128 + 3 * inner :] = jnp.zeros((width, gw.shape[1] - 128 - 3 * inner), jnp.bfloat16)
    for i in range(width // 256):
        part = slice(i * 256, (i + 1) * 256)
        piece = tn(n1s[:, part], grads[...].reshape(seq, 3 * lanes)).astype(jnp.bfloat16)
        for c in range(3):
            gw[part, 128 + c * inner : 128 + (c + 1) * inner] = piece[:, c * lanes : c * lanes + inner]
    for zz in range(depth):

        @pl.when(jnp.logical_not(jnp.logical_and(same, zz == z)))
        def _():
            remote(gn_out.at[0], gnr.at[zz], g_send.at[0], g_recv.at[zz], 2 * zz + k, 2 * y + xx).wait_recv()

    halves = []
    for h in range(2):
        total = gnr[h * (depth // 2)].astype(jnp.float32)
        for zz in range(1, depth // 2):
            total = total + gnr[h * (depth // 2) + zz].astype(jnp.float32)
        halves.append(total)
    gn = jnp.concatenate(halves, axis=0)
    values = x[...]
    factor = rms_factor(values)
    base = values * factor
    gb = gn * small[0:1, :].astype(jnp.float32)
    grad = ghst[...] + factor * (gb - base * jnp.mean(gb * base, axis=-1, keepdims=True))
    gx[...] = grad
    gm[...] = grad.astype(jnp.bfloat16)
    sums = jnp.concatenate([jnp.sum(gn * base, axis=0, keepdims=True), gsmall[...]], axis=0)
    sums = jnp.concatenate([sums, jnp.zeros((128 - sums.shape[0], width), jnp.float32)], axis=0)
    gw[:, :128] = jnp.transpose(sums).astype(jnp.bfloat16)
    for unit in range(blocks):

        @pl.when(jnp.logical_not(jnp.logical_and(same, unit == 2 * z + k)))
        def _():
            go_copy(unit).wait_send()

    for zz in range(depth):
        sib_copy(zz).wait_send()

        @pl.when(jnp.logical_not(jnp.logical_and(same, zz == z)))
        def _():
            gn_copy(zz).wait_send()


def attn_backward(order, inv, n1s, w, cosine, sine, qkv, o, lse, go, ghst, x, small, gsmall, number):
    blocks, blk, lanes = go.shape
    seq, width = n1s.shape
    count = x.shape[0]
    depth = blocks // 2
    vm = pl.BlockSpec(memory_space=pltpu.VMEM)
    sm = pl.BlockSpec(memory_space=pltpu.SMEM)
    bf = jnp.bfloat16
    dma = pltpu.SemaphoreType.DMA
    return pl.pallas_call(
        attn_bwd_kernel,
        out_shape=[
            shape_of((count, width), jnp.float32),
            shape_of((count, width), bf),
            shape_of((width, GRAD_LANES), bf),
        ],
        in_specs=[sm] * 2 + [vm] * 12,
        out_specs=[vm] * 3,
        scratch_shapes=[
            pltpu.VMEM((blocks, blk, lanes), bf),
            pltpu.VMEM((seq, lanes), bf),
            pltpu.VMEM((blocks, blk, 3 * lanes), bf),
            pltpu.VMEM((seq, 3 * lanes), jnp.float32),
            pltpu.VMEM((depth, blk, width), jnp.float32),
            pltpu.VMEM((depth, blk, width), bf),
            pltpu.VMEM((depth, blk, width), bf),
            pltpu.VMEM((depth, blk, width), bf),
            pltpu.VMEM((depth, blk, width), bf),
        ]
        + [dma((blocks,))] * 2
        + [dma((depth,))] * 4,
        compiler_params=params_of(collective_id=number, has_side_effects=True),
        cost_estimate=BRIEF,
        name="attn_bwd",
    )(order, inv, n1s, w, cosine, sine, qkv, o, lse, go, ghst, x, small, gsmall)


def routing(raw, before, routes):
    count = raw.shape[1]
    ids = lax.broadcasted_iota(jnp.int32, (16, count), 0)
    logits = raw + before
    first, second = ids == routes[0:1], ids == routes[1:2]
    z0 = jnp.sum(jnp.where(first, logits, 0.0), axis=0, keepdims=True)
    z1 = jnp.sum(jnp.where(second, logits, 0.0), axis=0, keepdims=True)
    top = jnp.maximum(z0, z1)
    e0, e1 = jnp.exp(z0 - top), jnp.exp(z1 - top)
    total = e0 + e1
    coef = jnp.where(first, e0 / total, 0.0) + jnp.where(second, e1 / total, 0.0)
    hits = jnp.where(first | second, 1.0, 0.0)
    upto = lax.broadcasted_iota(jnp.int32, (count, count), 0) <= lax.broadcasted_iota(jnp.int32, (count, count), 1)
    place = nn(hits.astype(jnp.bfloat16), jnp.where(upto, 1.0, 0.0).astype(jnp.bfloat16)) - 1.0
    slot = jnp.where(hits > 0, place, -1.0)
    return jnp.concatenate([raw, coef, slot[:NF], logits], axis=0)


def one_hot(slot):
    count = slot.shape[1]
    ids = lax.broadcasted_iota(jnp.int32, (NF, MOST, count), 1)
    hit = ids == slot.astype(jnp.int32)[:, None, :]
    return jnp.where(hit, 1.0, 0.0).reshape(NF * MOST, count)


def slot_values(hot, rows):
    count = rows.shape[1]
    wide = jnp.broadcast_to(rows[:, None, :], (NF, MOST, count)).reshape(NF * MOST, count)
    return jnp.sum(hot * wide, axis=1, keepdims=True)


def swap_rows(own, rows, send, recv, forward_send, forward_recv):
    ctx = lax.axis_index("ctx")
    _, _, y, k = place()
    beside, across = 2 * y + 1 - k, 2 * (1 - y) + k
    far = remote(own, rows.at[2], send.at[0], recv.at[0], ctx, across)
    near = remote(own, rows.at[1], send.at[1], recv.at[1], ctx, beside)
    onward = remote(rows.at[2], rows.at[3], forward_send, forward_recv, ctx, beside)
    far.start()
    near.start()
    return near, far, onward


def sum_rows(parts, beside_in, mid, across_in, send, recv):
    ctx = lax.axis_index("ctx")
    _, _, y, k = place()
    beside, across = 2 * y + 1 - k, 2 * (1 - y) + k
    first = remote(parts.at[3], beside_in.at[1], send.at[0], recv.at[0], ctx, beside)
    second = remote(parts.at[1], beside_in.at[0], send.at[1], recv.at[1], ctx, beside)
    third = remote(mid, across_in, send.at[2], recv.at[2], ctx, across)
    return first, second, third


def ffn_fwd_kernel(
    ub, hst, small, routes, before, wgu, wd,
    ubf, table, ext, x_next,
    rows_s, hot_s, x_s, y_s, coef_s, parts, beside_in, mid, across_in,
    a_send, a_recv, r_send, r_recv,
):
    e = pl.program_id(0)
    packs = ubf.shape[0]
    count, width = ub.shape
    router = small[2 + NC :, :]

    def gathers():
        return swap_rows(ub, rows_s, a_send, a_recv, a_send.at[2], a_recv.at[2])

    def sums():
        return sum_rows(parts, beside_in, mid, across_in, r_send, r_recv)

    @pl.when(e == 0)
    def _():
        barrier, others = greet_packs()
        rows_s[0] = ub[...]

        def prepare(d):
            rows = routing(nt(router, rows_s[d]), before[d], routes[d])
            table[d] = rows
            hot = one_hot(rows[SLOT : SLOT + NF])
            coef_s[d] = slot_values(hot, rows[COEF : COEF + NF])
            hot_low = hot.astype(jnp.bfloat16)
            hot_s[d] = hot_low
            x = nn(hot_low, rows_s[d]).astype(jnp.bfloat16)
            for n in range(NF):
                x_s[n, d * MOST : (d + 1) * MOST, :] = x[n * MOST : (n + 1) * MOST]

        pl.semaphore_wait(barrier, others)
        near, far, onward = gathers()
        prepare(0)
        near.wait_recv()
        prepare(1)
        far.wait_recv()
        onward.start()
        prepare(2)
        onward.wait_recv()
        prepare(3)
        ubf[...] = rows_s[...]
        ext[:count, :] = ub[...]
        rows = table[0]
        ext[count:, :] = jnp.zeros((16, width), jnp.bfloat16)
        ext[count:, :count] = rows[COEF : COEF + 16].astype(jnp.bfloat16)
        slots = jnp.concatenate([rows[SLOT : SLOT + NF], jnp.zeros((16 - NF, count), jnp.float32)], axis=0)
        ext[count:, count : 2 * count] = slots.astype(jnp.bfloat16)
        near.wait_send()
        far.wait_send()
        onward.wait_send()

    x = x_s[e]
    gate, up = nn(x, wgu[0, 0, 0]), nn(x, wgu[0, 0, 1])
    hid = (gate * jax.nn.sigmoid(gate) * up).astype(jnp.bfloat16)
    out = nn(hid, wd[0, 0])
    at = pl.ds(pl.multiple_of(e * MOST, MOST), MOST)
    for d in range(packs):
        y_s[d, at, :] = (out[d * MOST : (d + 1) * MOST] * coef_s[d, at, :]).astype(jnp.bfloat16)

    @pl.when(e == NF - 1)
    def _():
        first, second, third = sums()
        parts[3] = tn(hot_s[3], y_s[3]).astype(jnp.bfloat16)
        first.start()
        parts[1] = tn(hot_s[1], y_s[1]).astype(jnp.bfloat16)
        second.start()
        away = tn(hot_s[2], y_s[2])
        first.wait_recv()
        mid[...] = (away + beside_in[1].astype(jnp.float32)).astype(jnp.bfloat16)
        third.start()
        home = tn(hot_s[0], y_s[0])
        _, _, scale_u, scale_c = mixing_rows(table[0])
        columns = to_columns([scale_u] + scale_c)
        values = hst[...]
        moe = home + columns[0] * ((values * rms_factor(values)) * small[1:2, :].astype(jnp.float32))
        for c in range(NC):
            moe = moe + columns[1 + c] * small[2 + c : 3 + c, :].astype(jnp.float32)
        second.wait_recv()
        moe = moe + beside_in[0].astype(jnp.float32)
        third.wait_recv()
        x_next[...] = values + (moe + across_in[...].astype(jnp.float32))
        first.wait_send()
        second.wait_send()
        third.wait_send()


def whole_spec(dims):
    return pl.BlockSpec(dims, lambda *_: (0,) * len(dims))


def exchange_scratch(packs, count, width):
    bf = jnp.bfloat16
    return [
        pltpu.VMEM((packs, count, width), bf),
        pltpu.VMEM((2, count, width), bf),
        pltpu.VMEM((count, width), bf),
        pltpu.VMEM((count, width), bf),
    ]


def ffn_forward(layer, ub, hst, small, routes, before, wgu, wd, number):
    count, width = ub.shape
    packs = routes.shape[0]
    hidden = wd.shape[2]
    bf = jnp.bfloat16
    outs = [
        shape_of((packs, count, width), bf),
        shape_of((packs, ROUT, count), jnp.float32),
        shape_of((count + 16, width), bf),
        shape_of((count, width), jnp.float32),
    ]
    return pl.pallas_call(
        ffn_fwd_kernel,
        grid=(NF,),
        out_shape=outs,
        in_specs=[whole_spec(a.shape) for a in (ub, hst, small, routes, before)]
        + [
            pl.BlockSpec((1, 1, 2, width, hidden), lambda e: (layer, e, 0, 0, 0)),
            pl.BlockSpec((1, 1, hidden, width), lambda e: (layer, e, 0, 0)),
        ],
        out_specs=[whole_spec(a.shape) for a in outs],
        scratch_shapes=[
            pltpu.VMEM((packs, count, width), bf),
            pltpu.VMEM((packs, NF * MOST, count), bf),
            pltpu.VMEM((NF, packs * MOST, width), bf),
            pltpu.VMEM((packs, NF * MOST, width), bf),
            pltpu.VMEM((packs, NF * MOST, 1), jnp.float32),
        ]
        + exchange_scratch(packs, count, width)
        + [pltpu.SemaphoreType.DMA((3,))] * 4,
        compiler_params=params_of(collective_id=number, has_side_effects=True),
        cost_estimate=BRIEF,
        name="ffn_fwd",
    )(ub, hst, small, routes, before, wgu, wd)


def silu_parts(gate, up, ghid):
    sig = jax.nn.sigmoid(gate)
    act = gate * sig
    dg = (ghid * up * sig * (1.0 + gate * (1.0 - sig))).astype(jnp.bfloat16)
    du = (ghid * act).astype(jnp.bfloat16)
    return act * up, dg, du


def ffn_bwd_kernel(
    gm, gx, ubf, table, hst, small, routes, gprev, wo, ob, wgu, wd,
    ghst, go, gwo, gsmall, glog,
    rows_s, hot_s, x_s, g_s, y_s, coef_s, gc_s, gcoef, gcoef_in, parts, beside_in, mid, across_in,
    a_send, a_recv, r_send, r_recv, c_send, c_recv,
):
    e = pl.program_id(0)
    packs = ubf.shape[0]
    ctx = lax.axis_index("ctx")
    _, _, y, k = place()
    peers = [None, 2 * y + 1 - k, 2 * (1 - y) + k, 2 * (1 - y) + 1 - k]

    def gathers():
        return swap_rows(gm, rows_s, a_send, a_recv, a_send.at[2], a_recv.at[2])

    def sums():
        return sum_rows(parts, beside_in, mid, across_in, r_send, r_recv)

    @pl.when(e == 0)
    def _():
        barrier, others = greet_packs()
        rows_s[0] = gm[...]

        def prepare(d):
            hot = one_hot(table[d, SLOT : SLOT + NF, :])
            coef_s[d] = slot_values(hot, table[d, COEF : COEF + NF, :])
            hot_low = hot.astype(jnp.bfloat16)
            hot_s[d] = hot_low
            x = nn(hot_low, ubf[d]).astype(jnp.bfloat16)
            for n in range(NF):
                x_s[n, d * MOST : (d + 1) * MOST, :] = x[n * MOST : (n + 1) * MOST]

        def spread(d):
            g = nn(hot_s[d], rows_s[d]).astype(jnp.bfloat16)
            for n in range(NF):
                g_s[n, d * MOST : (d + 1) * MOST, :] = g[n * MOST : (n + 1) * MOST]

        pl.semaphore_wait(barrier, others)
        near, far, onward = gathers()
        for d in range(packs):
            prepare(d)
        spread(0)
        near.wait_recv()
        far.wait_recv()
        onward.start()
        spread(1)
        spread(2)
        onward.wait_recv()
        spread(3)
        near.wait_send()
        far.wait_send()
        onward.wait_send()

    x = x_s[e]
    at = pl.ds(pl.multiple_of(e * MOST, MOST), MOST)
    coef = jnp.concatenate([coef_s[d, at, :] for d in range(packs)], axis=0)
    gate, up = nn(x, wgu[0, 0, 0]), nn(x, wgu[0, 0, 1])
    ghid = nt(g_s[e], wd[0, 0])
    hid, dg, du = silu_parts(gate, up, ghid * coef)
    dots = jnp.sum(hid * ghid, axis=1, keepdims=True)
    out = nt(dg, wgu[0, 0, 0]) + nt(du, wgu[0, 0, 1])
    for d in range(packs):
        y_s[d, at, :] = out[d * MOST : (d + 1) * MOST].astype(jnp.bfloat16)
        gc_s[d, at, :] = dots[d * MOST : (d + 1) * MOST]

    @pl.when(e == NF - 1)
    def _():
        first, second, third = sums()

        def coef_copy(d):
            return remote(gcoef.at[d], gcoef_in.at[d - 1], c_send.at[d - 1], c_recv.at[d - 1], ctx, peers[d])

        parts[3] = tn(hot_s[3], y_s[3]).astype(jnp.bfloat16)
        first.start()
        parts[1] = tn(hot_s[1], y_s[1]).astype(jnp.bfloat16)
        second.start()
        for d in range(packs):
            wide = hot_s[d].astype(jnp.float32) * gc_s[d]
            gcoef[d] = jnp.sum(wide.reshape(NF, MOST, wide.shape[1]), axis=1)
            if d > 0:
                coef_copy(d).start()
        away = tn(hot_s[2], y_s[2])
        first.wait_recv()
        mid[...] = (away + beside_in[1].astype(jnp.float32)).astype(jnp.bfloat16)
        third.start()
        home = tn(hot_s[0], y_s[0])
        second.wait_recv()
        home = home + beside_in[0].astype(jnp.float32)
        total = gcoef[0]
        for d in range(1, packs):
            coef_copy(d).wait_recv()
            total = total + gcoef_in[d - 1]
        third.wait_recv()
        home = home + across_in[...].astype(jnp.float32)
        results = middle(
            gx[...], home, total, table[0], routes[...], gprev[...], hst[...], ubf[0],
            small[...], wo[...], ob[...],
        )
        for ref, value in zip((ghst, go, gwo, gsmall, glog), results):
            ref[...] = value
        first.wait_send()
        second.wait_send()
        third.wait_send()
        for d in range(1, packs):
            coef_copy(d).wait_send()


def ffn_backward(layer, gm, gx, ubf, table, hst, small, routes, gprev, wo, ob, wgu, wd, number):
    packs, count, width = ubf.shape
    hidden = wd.shape[2]
    bf, f32 = jnp.bfloat16, jnp.float32
    outs = [
        shape_of((count, width), f32),
        shape_of(ob.shape, bf),
        shape_of((width, width), bf),
        shape_of((1 + NC + 16, width), f32),
        shape_of((16, count), f32),
    ]
    args = (gm, gx, ubf, table, hst, small, routes, gprev, wo, ob)
    dma = pltpu.SemaphoreType.DMA
    return pl.pallas_call(
        ffn_bwd_kernel,
        grid=(NF,),
        out_shape=outs,
        in_specs=[whole_spec(a.shape) for a in args]
        + [
            pl.BlockSpec((1, 1, 2, width, hidden), lambda e: (layer, e, 0, 0, 0)),
            pl.BlockSpec((1, 1, hidden, width), lambda e: (layer, e, 0, 0)),
        ],
        out_specs=[whole_spec(a.shape) for a in outs],
        scratch_shapes=[
            pltpu.VMEM((packs, count, width), bf),
            pltpu.VMEM((packs, NF * MOST, count), bf),
            pltpu.VMEM((NF, packs * MOST, width), bf),
            pltpu.VMEM((NF, packs * MOST, width), bf),
            pltpu.VMEM((packs, NF * MOST, width), bf),
            pltpu.VMEM((packs, NF * MOST, 1), f32),
            pltpu.VMEM((packs, NF * MOST, 1), f32),
            pltpu.VMEM((packs, NF, count), f32),
            pltpu.VMEM((packs - 1, NF, count), f32),
        ]
        + exchange_scratch(packs, count, width)
        + [dma((3,))] * 6,
        compiler_params=params_of(collective_id=number, has_side_effects=True),
        cost_estimate=BRIEF,
        name="ffn_bwd",
    )(*args, wgu, wd)


def slot_rows(ext, weighted):
    rows = ext.astype(jnp.float32)
    count = rows.shape[1] // 3
    coef, slot = rows[:NF, :count], rows[:NF, count : 2 * count].astype(jnp.int32)
    hit = lax.broadcasted_iota(jnp.int32, (NF, MOST, count), 1) == slot[:, None, :]
    hot = jnp.where(hit, coef[:, None, :] if weighted else 1.0, 0.0)
    return hot.astype(jnp.bfloat16).reshape(NF * MOST, count)


def dispatch_kernel(rows, weighted, tail, values, out):
    for d in range(values.shape[0]):
        low = nn(slot_rows(tail[d], weighted), values[d, :rows, :]).astype(jnp.bfloat16)
        out[:, d] = low.reshape(NF, MOST, low.shape[1])


def dispatch(ext, values, weighted):
    devices, _, width = ext.shape
    rows = ext.shape[1] - 16
    some = 4
    out = pl.pallas_call(
        functools.partial(dispatch_kernel, rows, weighted),
        grid=(devices // some,),
        out_shape=shape_of((NF, devices, MOST, width), jnp.bfloat16),
        in_specs=[
            pl.BlockSpec((some, 16, width), lambda d: (d, rows // 16, 0)),
            pl.BlockSpec((some,) + values.shape[1:], lambda d: (d, 0, 0)),
        ],
        out_specs=pl.BlockSpec((NF, some, MOST, width), lambda d: (0, d, 0, 0)),
        compiler_params=params_of(),
        cost_estimate=BRIEF,
        name="dispatch",
    )(ext, values)
    return out.reshape(NF, devices * MOST, width)


def dw_kernel(*refs):
    x, g, wgu, wd, dgu, dd, dg_s, du_s, hid_s = refs[:4] + refs[-5:]
    rows = x.shape[1]
    chunk = 256

    def pieces(i, _):
        part = pl.ds(pl.multiple_of(i * chunk, chunk), chunk)
        xs = x[0, part, :]
        hid, dg, du = silu_parts(nn(xs, wgu[0, 0, 0]), nn(xs, wgu[0, 0, 1]), nt(g[0, part, :], wd[0, 0]))
        hid_s[part, :] = hid.astype(jnp.bfloat16)
        dg_s[part, :] = dg
        du_s[part, :] = du
        return 0

    lax.fori_loop(0, rows // chunk, pieces, 0)

    def first(i, _):
        part = pl.ds(pl.multiple_of(i * 256, 256), 256)
        xs = x[0, :, part]
        dgu[0, 0, 0, part, :] = tn(xs, dg_s[...])
        dgu[0, 0, 1, part, :] = tn(xs, du_s[...])
        return 0

    lax.fori_loop(0, x.shape[2] // 256, first, 0)

    def second(i, _):
        part = pl.ds(pl.multiple_of(i * 256, 256), 256)
        dd[0, 0, part, :] = tn(hid_s[:, part], g[0])
        return 0

    lax.fori_loop(0, hid_s.shape[1] // 256, second, 0)


def weight_grads(layer, first, last, x, g, wgu, wd, earlier):
    _, rows, width = x.shape
    hidden = wd.shape[2]
    gu_spec = pl.BlockSpec((1, 1, 2, width, hidden), lambda e: (layer, e + first, 0, 0, 0))
    d_spec = pl.BlockSpec((1, 1, hidden, width), lambda e: (layer, e + first, 0, 0))
    row_spec = pl.BlockSpec((1, rows, width), lambda e: (e + first, 0, 0))
    return pl.pallas_call(
        dw_kernel,
        grid=(last - first,),
        out_shape=[shape_of(wgu.shape, jnp.float32), shape_of(wd.shape, jnp.float32)],
        in_specs=[row_spec, row_spec, gu_spec, d_spec] + [pl.BlockSpec(memory_space=pl.ANY)] * len(earlier),
        out_specs=[gu_spec, d_spec],
        input_output_aliases={4 + i: i for i in range(len(earlier))},
        scratch_shapes=[pltpu.VMEM((rows, hidden), jnp.bfloat16)] * 3,
        compiler_params=params_of(),
        cost_estimate=BRIEF,
        name="weight_grads",
    )(x, g, wgu, wd, *earlier)


def norm_low(x, gain):
    return ((x * rms_factor(x)) * gain).astype(jnp.bfloat16)


def post_attention(ob, x, wo, gain):
    groups = wo.shape[0]
    inner = wo.shape[1]
    blk = ob.shape[1]
    halves = []
    for h in range(2):
        total = x[h * blk : (h + 1) * blk]
        for g in range(groups):
            total = total + nn(ob[h * groups + g][:, :inner], wo[g])
        halves.append(total)
    hst = jnp.concatenate(halves, axis=0)
    return hst, norm_low(hst, gain)


def mixing_rows(table):
    raw, coef = table[RAW : RAW + 16], table[COEF : COEF + 16]
    pairs = []
    for c in range(NC):
        r0, r1 = raw[NE + 2 * c : NE + 2 * c + 1], raw[NE + 2 * c + 1 : NE + 2 * c + 2]
        top = jnp.maximum(r0, r1)
        e0, e1 = jnp.exp(r0 - top), jnp.exp(r1 - top)
        pairs.append((e0 / (e0 + e1), e1 / (e0 + e1)))
    shares = [coef[NF + 2 + c : NF + 3 + c] for c in range(NC)]
    scale_u = coef[NF + 1 : NF + 2]
    for c in range(NC):
        scale_u = scale_u + shares[c] * pairs[c][0]
    return pairs, shares, scale_u, [shares[c] * pairs[c][1] for c in range(NC)]


def middle(gx, parts, gcoef, table, routes, gprev, hst, ub, small, wo, ob):
    groups = wo.shape[0]
    inner = wo.shape[1]
    blk = ob.shape[1]
    gain = small[1:2].astype(jnp.float32)
    consts = small[2 : 2 + NC].astype(jnp.float32)
    router = small[2 + NC :]
    pairs, shares, scale_u, scale_c = mixing_rows(table)
    columns = to_columns([scale_u] + scale_c)
    factor = rms_factor(hst)
    base = hst * factor
    u = base * gain
    dots = [jnp.sum(gx * u, axis=1, keepdims=True)]
    dots += [jnp.sum(gx * consts[c : c + 1], axis=1, keepdims=True) for c in range(NC)]
    dots = to_rows(dots, 8)
    dot_u = dots[0:1]
    dot_c = [dots[1 + c : 2 + c] for c in range(NC)]
    ids = lax.broadcasted_iota(jnp.int32, (16, gx.shape[0]), 0)
    grads = jnp.concatenate([gcoef, jnp.zeros_like(gcoef)], axis=0)
    grads = jnp.where(ids == NF + 1, dot_u, grads)
    raw_rows = []
    for c in range(NC):
        a0, a1 = pairs[c]
        grads = jnp.where(ids == NF + 2 + c, a0 * dot_u + a1 * dot_c[c], grads)
        g0, g1 = shares[c] * dot_u, shares[c] * dot_c[c]
        both = a0 * g0 + a1 * g1
        raw_rows += [a0 * (g0 - both), a1 * (g1 - both)]
    logits = table[LOGI : LOGI + 16]
    first, second = ids == routes[0:1], ids == routes[1:2]

    def pick(chosen, rows):
        return jnp.sum(jnp.where(chosen, rows, 0.0), axis=0, keepdims=True)

    z0, z1 = pick(first, logits), pick(second, logits)
    top = jnp.maximum(z0, z1)
    e0, e1 = jnp.exp(z0 - top), jnp.exp(z1 - top)
    w0, w1 = e0 / (e0 + e1), e1 / (e0 + e1)
    gg0, gg1 = pick(first, grads), pick(second, grads)
    both = w0 * gg0 + w1 * gg1
    glog = jnp.where(first, w0 * (gg0 - both), 0.0) + jnp.where(second, w1 * (gg1 - both), 0.0) + gprev
    graw = glog
    for index, row in enumerate(raw_rows):
        graw = jnp.where(ids == NE + index, row, graw)
    graw = graw.astype(jnp.bfloat16)
    grad_router = nn(graw, ub)
    gu = gx * columns[0] + tn(graw, router) + parts
    sums = [jnp.sum(gu * base, axis=0, keepdims=True)]
    sums += [jnp.sum(gx * columns[1 + c], axis=0, keepdims=True) for c in range(NC)]
    gb = gu * gain
    ghst = gx + factor * (gb - base * jnp.mean(gb * base, axis=-1, keepdims=True))
    gy = ghst.astype(jnp.bfloat16)
    lanes = ob.shape[2]
    go, gwo = [None] * (2 * groups), []
    for g in range(groups):
        value = nt(gy, wo[g]).astype(jnp.bfloat16)
        value = jnp.concatenate([value, jnp.zeros((value.shape[0], lanes - inner), jnp.bfloat16)], axis=1)
        for h in range(2):
            go[h * groups + g] = value[h * blk : (h + 1) * blk]
        mixed = jnp.concatenate([ob[g], ob[groups + g]], axis=0)
        gwo.append(tn(mixed, gy)[:inner].astype(jnp.bfloat16))
    return ghst, jnp.stack(go), jnp.concatenate(gwo, axis=0), jnp.concatenate(sums + [grad_router], axis=0), glog


def turn_tables(seq):
    half = HEAD_DIM // 2
    frequency = np.exp((-np.log(np.float32(10000.0)) * np.arange(half, dtype=np.float32) / np.float32(half)))
    angles = np.arange(seq, dtype=np.float32)[:, None] * frequency.astype(np.float32)[None, :]
    cosine, sine = np.cos(angles), np.sin(angles)
    cosine = np.concatenate([cosine, cosine] * 2, axis=1).astype(np.float32)
    sine = np.concatenate([-sine, sine] * 2, axis=1).astype(np.float32)
    return jnp.asarray(cosine), jnp.asarray(sine)


def by_heads(
    tokens,
    cotangent,
    seq_lengths,
    block_order,
    routes,
    gains,
    qkv_weights,
    out_weight,
    router,
    const_values,
    w_gate_up,
    w_down,
):
    count, width = tokens.shape[1], tokens.shape[2]
    ctx_size, packs = lax.axis_size("ctx"), lax.axis_size("fsdp")
    blk = count // 2
    seq = blk * ctx_size
    pack = lax.axis_index("fsdp")
    z, xx, y, k = place()
    sequence = z // 2
    shard = width // packs
    f32, bf = jnp.float32, jnp.bfloat16
    everyone = ("ctx", "fsdp")

    cosine, sine = turn_tables(seq)
    routes_t = jnp.swapaxes(routes[:, 0], 1, 2)
    smalls = jnp.concatenate([gains, const_values, jnp.swapaxes(router, 1, 2)], axis=1)
    per_layer = smalls.shape[1]
    ints = jnp.concatenate([routes_t.reshape(-1), block_order[0]])
    places = ints.size
    ints = jnp.pad(ints, (0, -places % shard)).astype(bf).reshape(-1, shard)
    smalls = jnp.concatenate([smalls.reshape(LAYERS * per_layer, shard), ints], axis=0)
    smalls = jnp.pad(smalls, ((0, -smalls.shape[0] % 16), (0, 0)))
    smalls = lax.all_gather(smalls, "fsdp", axis=1, tiled=True)
    ints = smalls[LAYERS * per_layer : LAYERS * per_layer + ints.shape[0]].reshape(-1, packs, shard)
    ints = jnp.swapaxes(ints, 0, 1).reshape(packs, -1).astype(jnp.int32)
    smalls = [smalls[l * per_layer : (l + 1) * per_layer] for l in range(LAYERS)]
    near = jnp.stack([pack, 2 * y + 1 - k, 2 * (1 - y) + k, 2 * (1 - y) + 1 - k])
    routes_f = ints[near][:, : routes_t.size].reshape((packs,) + routes_t.shape)
    order = lax.dynamic_index_in_dim(ints, 2 * y + xx, 0, keepdims=False)
    order = order[routes_t.size : places].reshape(ctx_size, 2)
    order = lax.dynamic_index_in_dim(order, sequence, 1, keepdims=False) - ctx_size * sequence
    ids = jnp.arange(ctx_size, dtype=jnp.int32)
    inv = jnp.sum(jnp.where(order[None, :] == ids[:, None], ids[None, :], 0), axis=1)

    gm_all = [None, lax.all_gather(cotangent[0], everyone, axis=0, tiled=False)]
    x = tokens[0].astype(f32)
    before = jnp.zeros((packs, 16, count), f32)
    kept, ext_all = [], [None] * LAYERS
    for l in range(LAYERS):
        n1s, qkv, o, lse, ob, hst, ub, w, wo = attn_forward(
            l, order, inv, x, smalls[l], qkv_weights, cosine, sine, out_weight, 2 * l
        )
        if l == 1:
            ub, gm_all[1] = lax.optimization_barrier((ub, gm_all[1]))
        ubf, table, ext, x_next = ffn_forward(
            l, ub, hst, smalls[l], routes_f[:, l], before, w_gate_up, w_down, 2 * l + 1
        )
        before = table[:, LOGI : LOGI + 16]
        ext_all[l] = lax.all_gather(ext, everyone, axis=0, tiled=False)
        kept.append((x, n1s, qkv, o, lse, ob, hst, w, wo, ubf, table))
        x = x_next
    output = x
    gm = cotangent[0]
    gx = gm.astype(f32)
    gprev = jnp.zeros((16, count), f32)
    grads = [None] * LAYERS
    for l in reversed(range(LAYERS)):
        x, n1s, qkv, o, lse, ob, hst, w, wo, ubf, table = kept[l]
        number = 2 * LAYERS + 2 * l
        ghst, go, gwo, small, gprev = ffn_backward(
            l, gm, gx, ubf, table, hst, smalls[l], routes_t[l], gprev, wo, ob, w_gate_up, w_down, number
        )
        if l == 1:
            go, ext_all[0] = lax.optimization_barrier((go, ext_all[0]))
        gx, gm, gw = attn_backward(
            order, inv, n1s, w, cosine, sine, qkv, o, lse, go, ghst, x, smalls[l], small, number + 1
        )
        if l > 0:
            gm_all[l - 1] = lax.all_gather(gm, everyone, axis=0, tiled=False)
        grads[l] = jnp.concatenate([gw, gwo], axis=1)

    inner = GROUP_HEADS * HEAD_DIM
    dense = jnp.stack(grads).reshape(LAYERS, packs // 2, 2, shard, 2 * width)
    mine = lax.dynamic_index_in_dim(dense, k, 2, keepdims=False)
    theirs = lax.dynamic_index_in_dim(dense, 1 - k, 2, keepdims=False)
    got = lax.ppermute(theirs, "fsdp", [(i, i ^ 1) for i in range(packs)])
    x0 = dispatch(ext_all[0], ext_all[0], False)
    x0, got = lax.optimization_barrier((x0, got))

    def ordered(swap, first, second):
        return jnp.concatenate([jnp.where(swap, second, first), jnp.where(swap, first, second)], axis=-1)

    def added(first, second):
        return (first.astype(f32) + second.astype(f32)).astype(bf)

    def split(values):
        return values[..., 128 : 128 + 3 * inner], jnp.concatenate([values[..., :128], values[..., width:]], axis=-1)

    (qkv_mine, rest_mine), (qkv_got, rest_got) = split(mine), split(got)
    dense = jnp.concatenate([ordered(k == 1, qkv_mine, qkv_got), added(rest_mine, rest_got)], axis=-1)
    mine = lax.dynamic_index_in_dim(dense, y, 1, keepdims=False)
    theirs = lax.dynamic_index_in_dim(dense, 1 - y, 1, keepdims=False)
    theirs, ext_all[1] = lax.optimization_barrier((theirs, ext_all[1]))
    got = lax.ppermute(theirs, "fsdp", [(i, i ^ 2) for i in range(packs)])
    x1 = dispatch(ext_all[1], ext_all[1], False)
    g1 = dispatch(ext_all[1], gm_all[1], True)
    x1, g1, got = lax.optimization_barrier((x1, g1, got))
    dense = added(mine, got)
    dense, x1 = lax.optimization_barrier((dense, x1))
    got = lax.ppermute(dense, "ctx", [(i, i ^ 1) for i in range(ctx_size)])
    done = weight_grads(1, 0, NF // 2, x1, g1, w_gate_up, w_down, ())
    done, got = lax.optimization_barrier((done, got))
    dense = added(dense, got)
    dense, done = lax.optimization_barrier((dense, done))
    got = lax.ppermute(dense, "ctx", [(i, i ^ 4) for i in range(ctx_size)])
    done = weight_grads(1, NF // 2, NF, x1, g1, w_gate_up, w_down, done)
    done, gm_all[0] = lax.optimization_barrier((done, gm_all[0]))
    g0 = dispatch(ext_all[0], gm_all[0], True)
    g0, got = lax.optimization_barrier((g0, got))
    dense = added(dense, got)
    dense, g0 = lax.optimization_barrier((dense, g0))
    got = lax.ppermute(dense, "ctx", [(i, i ^ 2) for i in range(ctx_size)])
    done = weight_grads(0, 0, NF // 2, x0, g0, w_gate_up, w_down, done)
    done, got = lax.optimization_barrier((done, got))
    pairs = 6 * inner
    rest = dense[..., pairs:].astype(f32) + got[..., pairs:].astype(f32)
    qkv = ordered(z % 2 == 1, dense[..., :pairs], got[..., :pairs]).reshape(LAYERS, shard, 4, 3, inner)
    qkv = jnp.stack([qkv[:, :, :, c, :].reshape(LAYERS, shard, width) for c in range(3)], axis=1).astype(f32)
    small = jnp.swapaxes(rest[..., :128], 1, 2)
    done = weight_grads(0, NF // 2, NF, x0, g0, w_gate_up, w_down, done)
    return (
        output[None],
        gx[None],
        small[:, :2],
        qkv,
        rest[..., 128:],
        rest[..., 2 + NC : 2 + NC + 16],
        small[:, 2 : 2 + NC],
        done[0],
        done[1],
    )


def solution(mesh):
    placed = (
        P("fsdp", "ctx", None),
        P("fsdp", "ctx", None),
        P("fsdp", None),
        P("fsdp", None),
        P(None, "fsdp", "ctx", None),
        P(None, None, "fsdp"),
        P(None, None, "fsdp", None),
        P(None, "fsdp", None),
        P(None, "fsdp", None),
        P(None, None, "fsdp"),
        P(None, None, None, None, "fsdp"),
        P(None, None, "fsdp", None),
    )
    contexts, packs = mesh.shape["ctx"], mesh.shape["fsdp"]
    blocks_of_heads = HEADS // GROUP_HEADS

    def plan(*args):
        tokens = args[0]
        even = tokens.shape[1] * contexts == 2 * MINLEN
        grouped = contexts == 2 * blocks_of_heads and packs == blocks_of_heads
        return (by_heads if even and grouped else shards)(*args)

    return jax.shard_map(
        plan,
        mesh=mesh,
        in_specs=placed,
        out_specs=(
            P("fsdp", "ctx", None),
            P("fsdp", "ctx", None),
            P(None, None, "fsdp"),
            P(None, None, "fsdp", None),
            P(None, "fsdp", None),
            P(None, "fsdp", None),
            P(None, None, "fsdp"),
            P(None, None, None, None, "fsdp"),
            P(None, None, "fsdp", None),
        ),
        check_vma=False,
    )
```

```python
import functools

import jax
import jax.numpy as jnp
import numpy as np
from jax import lax
from jax.experimental import pallas as pl
from jax.experimental.pallas import tpu as pltpu
from jax.sharding import PartitionSpec as P

HEADS = 12
HEAD_DIM = 64
NF = 8
NC = 2
LAYERS = 2
NE = 12
MOST = 64
GROUP_HEADS = 3


def from_behind(x, axis, by):
    devices = lax.axis_size(axis)
    return lax.ppermute(x, axis, [(i, (i + by) % devices) for i in range(devices)])


def layout_tables(lengths, order_row, tok_count):
    block_len = tok_count // 2
    pack_len = order_row.shape[0] * block_len
    pack_rows = jnp.arange(pack_len, dtype=jnp.int32)
    owner = pack_rows // tok_count
    which_half = pack_rows % tok_count // block_len
    block_ids = order_row[2 * owner + which_half]
    pack_pos = block_ids * block_len + pack_rows % block_len
    segment = (pack_pos >= lengths[0]).astype(jnp.int32)
    seq_pos = pack_pos - segment * lengths[0]
    return (pack_pos, segment, seq_pos)


def angle_tables(seq_pos, head_size):
    half_size = head_size // 2
    frequency = jnp.exp(-jnp.log(10000.0) * jnp.arange(half_size, dtype=jnp.float32) / half_size)
    angles = seq_pos.astype(jnp.float32)[:, None] * frequency[None, :]
    return (jnp.cos(angles)[:, None, :], jnp.sin(angles)[:, None, :])


def rotate_pairs(values, cosine_table, sine_table, direction):
    half_size = values.shape[-1] // 2
    first_half = values[..., :half_size]
    second_half = values[..., half_size:]
    return jnp.concatenate(
        [
            first_half * cosine_table - direction * second_half * sine_table,
            second_half * cosine_table + direction * first_half * sine_table,
        ],
        axis=-1,
    )


def rms_parts(values):
    inverse = lax.rsqrt(jnp.mean(values * values, axis=-1, keepdims=True) + 1e-06)
    return (values * inverse, inverse)


def rms_back(grad_normed, base_values, inverse):
    return inverse * (
        grad_normed - base_values * jnp.mean(grad_normed * base_values, axis=-1, keepdims=True)
    )


def expert_forward(inputs_low, gate_up_use, down_use):
    gate_up_out = jnp.einsum(
        "emd,ecdf->ecmf", inputs_low, gate_up_use, preferred_element_type=jnp.float32
    )
    hidden_low = (jax.nn.silu(gate_up_out[:, 0]) * gate_up_out[:, 1]).astype(jnp.bfloat16)
    partial_value = jnp.einsum(
        "emf,efd->emd", hidden_low, down_use, preferred_element_type=jnp.float32
    )
    return (gate_up_out, hidden_low, partial_value)


def expert_backward(inputs_low, gate_up_out, hidden_low, grad_part_low, gate_up_use, down_use):
    grad_down = jnp.einsum(
        "emf,emd->efd", hidden_low, grad_part_low, preferred_element_type=jnp.float32
    )
    grad_hidden = jnp.einsum(
        "emd,efd->emf", grad_part_low, down_use, preferred_element_type=jnp.float32
    )
    gate_out = gate_up_out[:, 0]
    sigmoid_gate = jax.nn.sigmoid(gate_out)
    grad_pair_low = jnp.stack(
        [
            grad_hidden
            * gate_up_out[:, 1]
            * sigmoid_gate
            * (1.0 + gate_out * (1.0 - sigmoid_gate)),
            grad_hidden * gate_out * sigmoid_gate,
        ],
        axis=1,
    ).astype(jnp.bfloat16)
    grad_gate_up = jnp.einsum(
        "emd,ecmf->ecdf", inputs_low, grad_pair_low, preferred_element_type=jnp.float32
    )
    grad_rows = jnp.einsum(
        "ecmf,ecdf->emd", grad_pair_low, gate_up_use, preferred_element_type=jnp.float32
    )
    return (grad_gate_up, grad_down, grad_rows)


def shards(
    tokens,
    cotangent,
    seq_lengths,
    block_order,
    routes,
    gains,
    qkv_weights,
    out_weight,
    router,
    const_values,
    w_gate_up,
    w_down,
):
    tok_count = tokens.shape[1]
    width = tokens.shape[2]
    ctx_size = lax.axis_size("ctx")
    own_index = lax.axis_index("ctx")
    score_scale = HEAD_DIM ** (-0.5)
    pack_pos, segment, seq_pos = layout_tables(seq_lengths[0], block_order[0], tok_count)
    own_start = own_index * tok_count
    query_pos = lax.dynamic_slice_in_dim(pack_pos, own_start, tok_count)
    query_seg = lax.dynamic_slice_in_dim(segment, own_start, tok_count)
    cosine_table, sine_table = angle_tables(
        lax.dynamic_slice_in_dim(seq_pos, own_start, tok_count), HEAD_DIM
    )
    head_shape = (tok_count, HEADS, HEAD_DIM)
    expert_ids = jnp.arange(NE, dtype=jnp.int32)
    slot_ids = jnp.arange(MOST, dtype=jnp.int32)
    row_ids = jnp.arange(tok_count, dtype=jnp.int32)

    def allowed_pairs(key_offset, key_count):
        key_pos = lax.dynamic_slice_in_dim(pack_pos, key_offset, key_count)
        key_seg = lax.dynamic_slice_in_dim(segment, key_offset, key_count)
        return (query_seg[:, None] == key_seg[None, :]) & (key_pos[None, :] <= query_pos[:, None])

    stream = tokens[0].astype(jnp.float32)
    previous = jnp.zeros((tok_count, NE), jnp.float32)
    saved = []
    for layer_index in range(LAYERS):
        gain_all, qkv_all, out_all, router_all, const_all = (
            lax.all_gather(gains[layer_index], "fsdp", axis=1, tiled=True),
            lax.all_gather(qkv_weights[layer_index], "fsdp", axis=1, tiled=True),
            lax.all_gather(out_weight[layer_index], "fsdp", axis=0, tiled=True),
            lax.all_gather(router[layer_index], "fsdp", axis=0, tiled=True),
            lax.all_gather(const_values[layer_index], "fsdp", axis=1, tiled=True),
        )
        gain_float = gain_all.astype(jnp.float32)
        base_one, inverse_one = rms_parts(stream)
        normed_low = (base_one * gain_float[0]).astype(jnp.bfloat16)
        projected = jnp.einsum(
            "td,cde->cte", normed_low, qkv_all, preferred_element_type=jnp.float32
        )
        queries_low = rotate_pairs(
            projected[0].reshape(head_shape), cosine_table, sine_table, 1.0
        ).astype(jnp.bfloat16)
        keys_low = rotate_pairs(
            projected[1].reshape(head_shape), cosine_table, sine_table, 1.0
        ).astype(jnp.bfloat16)
        values_low = projected[2].reshape(head_shape).astype(jnp.bfloat16)

        def fold_step(running, shard_piece, offset, queries_use=queries_low):
            keys_piece, values_piece = shard_piece
            allowed = allowed_pairs(offset, keys_piece.shape[0])[None]
            scores = (
                jnp.einsum(
                    "qhd,khd->hqk", queries_use, keys_piece, preferred_element_type=jnp.float32
                )
                * score_scale
            )
            scores = jnp.where(allowed, scores, -1e30)
            top_old, total_old, accumulated = running
            top_new = jnp.maximum(top_old, jnp.max(scores, axis=-1))
            weights = jnp.where(allowed, jnp.exp(scores - top_new[..., None]), 0.0)
            factor = jnp.exp(top_old - top_new)
            accumulated = jnp.einsum(
                "hqk,khd->hqd",
                weights.astype(jnp.bfloat16),
                values_piece,
                preferred_element_type=jnp.float32,
            )
            return (top_new, jnp.sum(weights, axis=-1), accumulated)

        starting = (
            jnp.full((HEADS, tok_count), -1e30, jnp.float32),
            jnp.zeros((HEADS, tok_count), jnp.float32),
            jnp.zeros((HEADS, tok_count, HEAD_DIM), jnp.float32),
        )
        top_value, total_sum, accumulated = fold_step(
            starting,
            (
                lax.all_gather(keys_low, "ctx", axis=0, tiled=True),
                lax.all_gather(values_low, "ctx", axis=0, tiled=True),
            ),
            jnp.int32(0),
        )
        log_total = top_value + jnp.log(total_sum)
        attended = jnp.transpose(accumulated / total_sum[..., None], (1, 0, 2))
        mixed_low = attended.reshape(tok_count, width).astype(jnp.bfloat16)
        hidden_state = stream + jnp.dot(mixed_low, out_all, preferred_element_type=jnp.float32)
        base_two, inverse_two = rms_parts(hidden_state)
        expert_in = base_two * gain_float[1]
        expert_low = expert_in.astype(jnp.bfloat16)
        raw_logits = jnp.dot(expert_low, router_all, preferred_element_type=jnp.float32)
        logits = raw_logits[:, :NE] + previous
        route_ids = routes[layer_index, 0]
        chosen = route_ids[:, :, None] == expert_ids[None, None, :]
        chosen_f = chosen.astype(jnp.float32)
        hit_count = jnp.sum(chosen.astype(jnp.int32), axis=1)
        slot_index = jnp.cumsum(hit_count, axis=0) - 1
        picked = jnp.sum(chosen_f * logits[:, None, :], axis=-1)
        gate_weights = jax.nn.softmax(picked, axis=-1)
        coeffs = jnp.sum(gate_weights[:, :, None] * chosen_f, axis=1)
        slot_table = jnp.zeros((NF, MOST), jnp.int32)
        for expert in range(NF):
            target = jnp.where(hit_count[:, expert] > 0, slot_index[:, expert], MOST)
            slot_table = slot_table.at[expert, target].set(row_ids, mode="drop")
        filled = (slot_ids[None, :] < jnp.sum(hit_count[:, :NF], axis=0)[:, None]).astype(
            jnp.float32
        )
        rows_low = expert_low[slot_table]
        inputs_low = lax.all_gather(rows_low, "fsdp", axis=1, tiled=True)
        gate_up_out, hidden_low, partial_value = expert_forward(
            inputs_low, w_gate_up[layer_index], w_down[layer_index]
        )
        result = lax.psum_scatter(
            partial_value.astype(jnp.bfloat16), "fsdp", scatter_dimension=1, tiled=True
        ).astype(jnp.float32)
        flat_index = jnp.arange(NF, dtype=jnp.int32)[None, :] * MOST + jnp.clip(
            slot_index[:, :NF], 0, MOST - 1
        )
        token_result = result.reshape(NF * MOST, width)[flat_index]
        expert_mix = (
            jnp.sum(coeffs[:, :NF, None] * token_result, axis=1)
            + coeffs[:, NF + 1 : NF + 2] * expert_in
        )
        mixings = []
        for const_index in range(NC):
            column = NE + 2 * const_index
            mixing = jax.nn.softmax(raw_logits[:, column : column + 2], axis=-1)
            mixings.append(mixing)
            expert_mix = expert_mix + coeffs[:, NF + 2 + const_index : NF + 3 + const_index] * (
                mixing[:, 0:1] * expert_in
                + mixing[:, 1:2] * const_all[const_index].astype(jnp.float32)[None, :]
            )
        saved.append(
            (
                gain_float,
                qkv_all,
                out_all,
                router_all,
                const_all,
                base_one,
                inverse_one,
                normed_low,
                queries_low,
                keys_low,
                values_low,
                log_total,
                attended,
                mixed_low,
                base_two,
                inverse_two,
                expert_in,
                expert_low,
                chosen_f,
                hit_count,
                gate_weights,
                coeffs,
                slot_table,
                filled,
                inputs_low,
                gate_up_out,
                hidden_low,
                flat_index,
                token_result,
                mixings,
            )
        )
        stream = hidden_state + expert_mix
        previous = logits
    grad_stream = cotangent[0].astype(jnp.float32)
    grad_previous = jnp.zeros((tok_count, NE), jnp.float32)
    layer_grads = [None] * LAYERS
    for layer_index in reversed(range(LAYERS)):
        (
            gain_float,
            qkv_all,
            out_all,
            router_all,
            const_all,
            base_one,
            inverse_one,
            normed_low,
            queries_low,
            keys_low,
            values_low,
            log_total,
            attended,
            mixed_low,
            base_two,
            inverse_two,
            expert_in,
            expert_low,
            chosen_f,
            hit_count,
            gate_weights,
            coeffs,
            slot_table,
            filled,
            inputs_low,
            gate_up_out,
            hidden_low,
            flat_index,
            token_result,
            mixings,
        ) = saved[layer_index]
        grad_mix = grad_stream
        dot_input = jnp.sum(grad_mix * expert_in, axis=-1, keepdims=True)
        coef_grads = [
            jnp.sum(grad_mix[:, None, :] * token_result, axis=-1),
            jnp.zeros((tok_count, 1), jnp.float32),
            dot_input,
        ]
        grad_in = grad_mix * coeffs[:, NF + 1 : NF + 2]
        const_cols = []
        const_grads = []
        for const_index in range(NC):
            mixing = mixings[const_index]
            const_row = const_all[const_index].astype(jnp.float32)[None, :]
            dot_const = jnp.sum(grad_mix * const_row, axis=-1, keepdims=True)
            share = coeffs[:, NF + 2 + const_index : NF + 3 + const_index]
            coef_grads.append(mixing[:, 0:1] * dot_input + mixing[:, 1:2] * dot_const)
            grad_in = grad_in + grad_mix * (share * mixing[:, 0:1])
            grad_mixing = share * jnp.concatenate([dot_input, dot_const], axis=1)
            const_cols.append(
                mixing * (grad_mixing - jnp.sum(mixing * grad_mixing, axis=-1, keepdims=True))
            )
            const_grads.append(jnp.sum(grad_mix * (share * mixing[:, 1:2]), axis=0))
        grad_coeffs = jnp.concatenate(coef_grads, axis=1)
        grad_gates = jnp.sum(chosen_f * grad_coeffs[:, None, :], axis=-1)
        grad_picked = gate_weights * (
            grad_gates - jnp.sum(gate_weights * grad_gates, axis=-1, keepdims=True)
        )
        grad_logits = jnp.sum(grad_picked[:, :, None] * chosen_f, axis=1) + grad_previous
        grad_previous = grad_logits
        grad_raw_low = jnp.concatenate([grad_logits] + const_cols, axis=1).astype(jnp.bfloat16)
        grad_router = jnp.einsum(
            "td,tc->dc", expert_low, grad_raw_low, preferred_element_type=jnp.float32
        )
        grad_in = grad_in + jnp.einsum(
            "tc,dc->td", grad_raw_low, router_all, preferred_element_type=jnp.float32
        )
        slot_weight = (
            jnp.take_along_axis(jnp.transpose(coeffs[:, :NF]), slot_table, axis=1) * filled
        )
        grad_result_low = (grad_mix[slot_table] * slot_weight[:, :, None]).astype(jnp.bfloat16)
        grad_part_low = lax.all_gather(grad_result_low, "fsdp", axis=1, tiled=True)
        grad_gate_up, grad_down, grad_rows = expert_backward(
            inputs_low,
            gate_up_out,
            hidden_low,
            grad_part_low,
            w_gate_up[layer_index],
            w_down[layer_index],
        )
        grad_rows = lax.psum_scatter(
            grad_rows.astype(jnp.bfloat16), "fsdp", scatter_dimension=1, tiled=True
        ).astype(jnp.float32)
        token_grads = grad_rows.reshape(NF * MOST, width)[flat_index]
        grad_in = grad_in + jnp.sum(
            jnp.where(hit_count[:, :NF, None] > 0, token_grads, 0.0), axis=1
        )
        grad_gain_two = jnp.sum(grad_in * base_two, axis=0)
        grad_hidden_state = grad_stream + rms_back(grad_in * gain_float[1], base_two, inverse_two)
        grad_out_low = grad_hidden_state.astype(jnp.bfloat16)
        grad_out_w = jnp.einsum(
            "td,te->de", mixed_low, grad_out_low, preferred_element_type=jnp.float32
        )
        grad_attended = (
            jnp.einsum("te,de->td", grad_out_low, out_all, preferred_element_type=jnp.float32)
            .astype(jnp.bfloat16)
            .reshape(head_shape)
        )
        delta = jnp.transpose(jnp.sum(grad_attended.astype(jnp.float32) * attended, axis=-1))

        def visit(
            turn_index,
            carried,
            queries_use=queries_low,
            grad_use=grad_attended,
            log_use=log_total,
            delta_use=delta,
        ):
            keys_piece, values_piece, key_grads, value_grads, query_grads = carried
            source = (own_index - turn_index) % ctx_size
            allowed = allowed_pairs(source * tok_count, tok_count)[None]
            scores = (
                jnp.einsum(
                    "qhd,khd->hqk", queries_use, keys_piece, preferred_element_type=jnp.float32
                )
                * score_scale
            )
            probs = jnp.where(
                allowed, jnp.exp(jnp.where(allowed, scores, -1e30) - log_use[..., None]), 0.0
            )
            value_grads = value_grads + jnp.einsum(
                "hqk,qhd->khd",
                probs.astype(jnp.bfloat16),
                grad_use,
                preferred_element_type=jnp.float32,
            )
            prob_grads = jnp.einsum(
                "qhd,khd->hqk", grad_use, values_piece, preferred_element_type=jnp.float32
            )
            score_grads = (probs * (prob_grads - delta_use[..., None])).astype(jnp.bfloat16)
            query_grads = query_grads + jnp.einsum(
                "hqk,khd->qhd", score_grads, keys_piece, preferred_element_type=jnp.float32
            )
            key_grads = key_grads + jnp.einsum(
                "hqk,qhd->khd", score_grads, queries_use, preferred_element_type=jnp.float32
            )
            keys_piece, values_piece = from_behind((keys_piece, values_piece), "ctx", 1)
            key_grads, value_grads = (
                from_behind(key_grads.astype(jnp.bfloat16), "ctx", 1).astype(key_grads.dtype),
                from_behind(value_grads.astype(jnp.bfloat16), "ctx", 1).astype(value_grads.dtype),
            )
            return (keys_piece, values_piece, key_grads, value_grads, query_grads)

        zero_heads = jnp.zeros(head_shape, jnp.float32)
        finished = lax.fori_loop(
            0, ctx_size, visit, (keys_low, values_low, zero_heads, zero_heads, zero_heads)
        )
        grad_query = (
            rotate_pairs(finished[4] * score_scale, cosine_table, sine_table, -1.0)
            .astype(jnp.bfloat16)
            .reshape(tok_count, width)
        )
        grad_key = (
            rotate_pairs(finished[2] * score_scale, cosine_table, sine_table, -1.0)
            .astype(jnp.bfloat16)
            .reshape(tok_count, width)
        )
        grad_value = finished[3].astype(jnp.bfloat16).reshape(tok_count, width)
        grad_proj_low = jnp.stack([grad_query, grad_key, grad_value], axis=0)
        grad_qkv = jnp.einsum(
            "td,cte->cde", normed_low, grad_proj_low, preferred_element_type=jnp.float32
        )
        grad_normed = jnp.einsum(
            "cte,cde->td", grad_proj_low, qkv_all, preferred_element_type=jnp.float32
        )
        grad_gain_one = jnp.sum(grad_normed * base_one, axis=0)
        grad_stream = grad_hidden_state + rms_back(
            grad_normed * gain_float[0], base_one, inverse_one
        )
        gains_shard, qkv_shard, out_shard, router_shard, const_shard = (
            lax.psum_scatter(
                jnp.stack([grad_gain_one, grad_gain_two]).astype(jnp.bfloat16),
                "fsdp",
                scatter_dimension=1,
                tiled=True,
            ).astype(jnp.float32),
            lax.psum_scatter(
                grad_qkv.astype(jnp.bfloat16), "fsdp", scatter_dimension=1, tiled=True
            ).astype(jnp.float32),
            lax.psum_scatter(
                grad_out_w.astype(jnp.bfloat16), "fsdp", scatter_dimension=0, tiled=True
            ).astype(jnp.float32),
            lax.psum_scatter(
                grad_router.astype(jnp.bfloat16), "fsdp", scatter_dimension=0, tiled=True
            ).astype(jnp.float32),
            lax.psum_scatter(
                jnp.stack(const_grads).astype(jnp.bfloat16), "fsdp", scatter_dimension=1, tiled=True
            ).astype(jnp.float32),
        )
        layer_grads[layer_index] = (
            lax.psum(gains_shard.astype(jnp.bfloat16), "ctx").astype(jnp.float32),
            lax.psum(qkv_shard.astype(jnp.bfloat16), "ctx").astype(jnp.float32),
            lax.psum(out_shard.astype(jnp.bfloat16), "ctx").astype(jnp.float32),
            lax.psum(router_shard.astype(jnp.bfloat16), "ctx").astype(jnp.float32),
            lax.psum(const_shard.astype(jnp.bfloat16), "ctx").astype(jnp.float32),
            lax.psum(grad_gate_up.astype(jnp.bfloat16), "ctx").astype(jnp.float32),
            lax.psum(grad_down.astype(jnp.bfloat16), "ctx").astype(jnp.float32),
        )
    stacked = [
        jnp.stack([layer_grads[layer_index][member_index] for layer_index in range(LAYERS)])
        for member_index in range(7)
    ]
    return (
        stream[None],
        grad_stream[None],
        stacked[0],
        stacked[1],
        stacked[2],
        stacked[3],
        stacked[4],
        stacked[5],
        stacked[6],
    )


MINLEN = 1024
ROUT = 56
RAW, COEF, SLOT, LOGI = 0, 16, 32, 40
VMEM_MB = 60
BRIEF = pl.CostEstimate(flops=1, bytes_accessed=1, transcendentals=0)


def nt(a, b):
    return lax.dot_general(a, b, (((1,), (1,)), ((), ())), preferred_element_type=jnp.float32)


def nn(a, b):
    return lax.dot_general(a, b, (((1,), (0,)), ((), ())), preferred_element_type=jnp.float32)


def tn(a, b):
    return lax.dot_general(a, b, (((0,), (0,)), ((), ())), preferred_element_type=jnp.float32)


def params_of(mb=VMEM_MB, **more):
    return pltpu.CompilerParams(vmem_limit_bytes=mb * 2**20, **more)


def shape_of(dims, kind):
    return jax.ShapeDtypeStruct(dims, kind)


def rms_factor(values):
    return lax.rsqrt(jnp.mean(values * values, axis=-1, keepdims=True) + 1e-06)


def to_rows(columns, count):
    lane = lax.broadcasted_iota(jnp.int32, (columns[0].shape[0], 128), 1)
    packed = jnp.zeros(lane.shape, jnp.float32)
    for index, column in enumerate(columns):
        packed = jnp.where(lane == index, column, packed)
    return jnp.transpose(packed)[:count]


def to_columns(rows):
    count = rows[0].shape[1]
    sub = lax.broadcasted_iota(jnp.int32, (128, count), 0)
    packed = jnp.zeros(sub.shape, jnp.float32)
    for index, row in enumerate(rows):
        packed = jnp.where(sub == index, row, packed)
    packed = jnp.transpose(packed)
    return [packed[:, index : index + 1] for index in range(len(rows))]


def swap_halves(values):
    lanes = values.shape[1]
    lane = lax.broadcasted_iota(jnp.int32, values.shape, 1)
    ahead = pltpu.roll(values, lanes - 32, 1)
    behind = pltpu.roll(values, 32, 1)
    return jnp.where(lane % 64 < 32, ahead, behind)


def spin(values, cosine, sine):
    return values * cosine + swap_halves(values) * sine


def place():
    own, pack = lax.axis_index("ctx"), lax.axis_index("fsdp")
    return own // 2, own % 2, pack // 2, pack % 2


def remote(src, dst, send, recv, ctx, fsdp):
    return pltpu.make_async_remote_copy(
        src_ref=src,
        dst_ref=dst,
        send_sem=send,
        recv_sem=recv,
        device_id=(ctx, fsdp),
        device_id_type=pl.DeviceIdType.MESH,
    )


def greet_plane(contexts, across=False):
    own = lax.axis_index("ctx")
    _, _, y, k = place()
    barrier = pltpu.get_barrier_semaphore()
    if across:
        for core in (k, 1 - k):
            device = (own, 2 * (1 - y) + core)
            pl.semaphore_signal(barrier, inc=1, device_id=device, device_id_type=pl.DeviceIdType.MESH)
    for ctx in range(contexts):
        for core in range(2):

            @pl.when(jnp.logical_or(ctx != own, core != k))
            def _():
                pl.semaphore_signal(barrier, inc=1, device_id=(ctx, 2 * y + core), device_id_type=pl.DeviceIdType.MESH)

    return barrier, 2 * contexts - 1 + (2 if across else 0)


def greet_packs():
    own = lax.axis_index("ctx")
    _, _, y, k = place()
    barrier = pltpu.get_barrier_semaphore()
    for fsdp in (2 * y + 1 - k, 2 * (1 - y) + k, 2 * (1 - y) + 1 - k):
        pl.semaphore_signal(barrier, inc=1, device_id=(own, fsdp), device_id_type=pl.DeviceIdType.MESH)
    return barrier, 3


def attn_fwd_kernel(
    order, inv, x, small, wq, cosine, sine, wo_own,
    n1s, qkv, o, lse, ob, hst, ub, w, wo,
    n1own, n1r, osort, osend, orecv, cols, w_s, wo_s,
    n_send, n_recv, f_send, f_recv, o_send, o_recv, w_send, w_recv, v_send, v_recv,
):
    blocks, blk, _ = n1r.shape
    lanes = o.shape[1]
    seq = blocks * blk
    step = 2 * blk
    own = lax.axis_index("ctx")
    z, xx, y, k = place()
    depth = blocks // 2
    same = xx == k
    pack = lax.axis_index("fsdp")
    inner = wo_own.shape[1]
    beside, over, corner = 2 * y + 1 - k, 2 * (1 - y) + k, 2 * (1 - y) + 1 - k

    barrier, others = greet_plane(blocks, across=True)
    n1 = norm_low(x[...], small[0:1, :].astype(jnp.float32))
    n1own[0] = n1[:blk]
    n1own[1] = n1[blk:]
    pl.semaphore_wait(barrier, others)

    def n1_copy(zz):
        return remote(n1own.at[zz // 2], n1r.at[own], n_send.at[zz], n_recv.at[z], 2 * zz + k, 2 * y + xx)

    for zz in range(depth):
        alone = jnp.logical_and(same, zz == z)

        @pl.when(jnp.logical_not(alone))
        def _():
            n1_copy(zz).start()

        @pl.when(alone)
        def _():
            n1r[own] = n1own[zz // 2]

    for half in range(2):

        @pl.when(z % 2 == half)
        def _():
            for core in range(2):
                first = (2 * half + core) * inner
                for c in range(3):
                    cols[core, :, c * lanes : c * lanes + inner] = wq[0, c, :, first : first + inner]
                    cols[core, :, c * lanes + inner : (c + 1) * lanes] = jnp.zeros((inner, lanes - inner), jnp.bfloat16)

    def rows_of(device):
        return pl.ds(pl.multiple_of(device * inner, inner), inner)

    def w_copy(index):
        device, core = ((beside, 1 - k), (over, k), (corner, 1 - k))[index]
        return remote(cols.at[core], w_s.at[rows_of(pack), :], w_send.at[index], w_recv.at[index], own, device)

    def w_wait(index):
        rows = w_s.at[rows_of((beside, over, corner)[index]), :]
        remote(cols.at[0], rows, w_send.at[index], w_recv.at[index], own, beside).wait_recv()

    w_s[rows_of(pack), :] = cols[k]
    wo_s[pack] = wo_own[0]
    for index in (1, 2, 0):
        w_copy(index).start()
    v_far = remote(wo_s.at[pack], wo_s.at[pack], v_send.at[0], v_recv.at[0], own, over)
    v_near = remote(wo_s.at[pack], wo_s.at[pack], v_send.at[1], v_recv.at[1], own, beside)
    v_on = remote(wo_s.at[over], wo_s.at[over], v_send.at[2], v_recv.at[2], own, beside)
    v_far.start()
    v_near.start()

    def forward_copy(zz):
        slot = n1r.at[2 * zz + k]
        return remote(slot, slot, f_send.at[zz], f_recv.at[zz], own, 2 * y + 1 - k)

    for zz in range(depth):

        @pl.when(jnp.logical_not(jnp.logical_and(same, zz == z)))
        def _():
            remote(n1own.at[0], n1r.at[2 * zz + k], n_send.at[zz], n_recv.at[zz], 2 * zz + k, 2 * y + xx).wait_recv()

        forward_copy(zz).start()
    for zz in range(depth):
        slot = n1r.at[2 * zz + 1 - k]
        remote(slot, slot, f_send.at[zz], f_recv.at[zz], own, 2 * y + 1 - k).wait_recv()

    for index in range(3):
        w_wait(index)
    w[...] = w_s[...]
    for b in range(blocks):
        n1s[b * blk : (b + 1) * blk, :] = n1r[inv[b]]
    for i in range(seq // step):
        part = slice(i * step, (i + 1) * step)
        out = nn(n1s[part, :], w_s[...])
        cos2 = jnp.concatenate([cosine[part, :]] * (lanes // 128), axis=1)
        sin2 = jnp.concatenate([sine[part, :]] * (lanes // 128), axis=1)
        q = spin(out[:, :lanes], cos2, sin2).astype(jnp.bfloat16)
        qkv[part, :lanes] = q * jnp.asarray(HEAD_DIM**-0.5, jnp.bfloat16)
        qkv[part, lanes : 2 * lanes] = spin(out[:, lanes : 2 * lanes], cos2, sin2).astype(jnp.bfloat16)
        qkv[part, 2 * lanes :] = out[:, 2 * lanes :].astype(jnp.bfloat16)
    lane = lax.broadcasted_iota(jnp.int32, (step, 128), 1)
    for i in range(seq // step):
        part = slice(i * step, (i + 1) * step)
        span = (i + 1) * step
        seen = lax.broadcasted_iota(jnp.int32, (step, span), 1) <= (
            lax.broadcasted_iota(jnp.int32, (step, span), 0) + i * step
        )
        logs = jnp.zeros((step, 128), jnp.float32)
        for head in range(GROUP_HEADS):
            tile, side = head // 2, head % 2
            at = tile * 128
            mine = lane // 64 == side
            q = jnp.where(mine, qkv[part, at : at + 128], jnp.asarray(0, jnp.bfloat16))
            s = nt(q, qkv[:span, lanes + at : lanes + at + 128])
            s = jnp.where(seen, s, -1e30)
            top = jnp.max(s, axis=1, keepdims=True)
            p = jnp.exp(s - top)
            total = jnp.sum(p, axis=1, keepdims=True)
            out = nn(p.astype(jnp.bfloat16), qkv[:span, 2 * lanes + at : 2 * lanes + at + 128]) / total
            logs = jnp.where(lane == head, top + jnp.log(total), logs)
            if side == 0:
                kept = jnp.where(mine, out, 0.0)
            else:
                kept = jnp.where(mine, out, kept)
            o[part, at : at + 128] = kept
        lse[part, :] = logs
        osort[2 * i] = o[part, :][:blk].astype(jnp.bfloat16)
        osort[2 * i + 1] = o[part, :][blk:].astype(jnp.bfloat16)

    mine_at = 2 * z + k
    remote(wo_s.at[over], wo_s.at[over], v_send.at[0], v_recv.at[0], own, over).wait_recv()
    v_on.start()

    def o_copy(ctx):
        return remote(osend.at[ctx], orecv.at[mine_at], o_send.at[ctx], o_recv.at[mine_at], ctx, 2 * y + xx)

    for ctx in range(blocks):
        alone = jnp.logical_and(same, ctx == own)
        osend[ctx] = osort[order[ctx]]

        @pl.when(jnp.logical_not(alone))
        def _():
            o_copy(ctx).start()

        @pl.when(alone)
        def _():
            orecv[mine_at] = osend[ctx]

    for src in range(blocks):

        @pl.when(jnp.logical_not(jnp.logical_and(same, src == mine_at)))
        def _():
            remote(osend.at[0], orecv.at[src], o_send.at[0], o_recv.at[src], 2 * (src // 2) + k, 2 * y + src % 2).wait_recv()

    ob[...] = orecv[...]
    remote(wo_s.at[beside], wo_s.at[beside], v_send.at[1], v_recv.at[1], own, beside).wait_recv()
    remote(wo_s.at[corner], wo_s.at[corner], v_send.at[2], v_recv.at[2], own, beside).wait_recv()
    wo[...] = wo_s[...]
    total, low = post_attention(orecv[...], x[...], wo_s[...], small[1:2, :].astype(jnp.float32))
    hst[...] = total
    ub[...] = low
    for zz in range(depth):

        @pl.when(jnp.logical_not(jnp.logical_and(same, zz == z)))
        def _():
            n1_copy(zz).wait_send()

        forward_copy(zz).wait_send()
    for index in range(3):
        w_copy(index).wait_send()
    v_far.wait_send()
    v_near.wait_send()
    v_on.wait_send()
    for ctx in range(blocks):

        @pl.when(jnp.logical_not(jnp.logical_and(same, ctx == own)))
        def _():
            o_copy(ctx).wait_send()


def attn_forward(layer, order, inv, x, small, wq, cosine, sine, wo, number):
    count, width = x.shape
    blocks, blk = order.shape[0], count // 2
    packs, inner = width // wo.shape[1], wo.shape[1]
    lanes = -(-inner // 128) * 128
    seq = blocks * blk
    vm = pl.BlockSpec(memory_space=pltpu.VMEM)
    sm = pl.BlockSpec(memory_space=pltpu.SMEM)
    bf = jnp.bfloat16
    dma = pltpu.SemaphoreType.DMA
    return pl.pallas_call(
        attn_fwd_kernel,
        grid=(1,),
        out_shape=[
            shape_of((seq, width), bf),
            shape_of((seq, 3 * lanes), bf),
            shape_of((seq, lanes), jnp.float32),
            shape_of((seq, 128), jnp.float32),
            shape_of((blocks, blk, lanes), bf),
            shape_of((count, width), jnp.float32),
            shape_of((count, width), bf),
            shape_of((width, 3 * lanes), bf),
            shape_of((packs, inner, width), bf),
        ],
        in_specs=[sm, sm, vm, vm]
        + [pl.BlockSpec((1, 3, inner, width), lambda _: (layer, 0, 0, 0)), vm, vm]
        + [pl.BlockSpec((1, inner, width), lambda _: (layer, 0, 0))],
        out_specs=[vm] * 9,
        scratch_shapes=[
            pltpu.VMEM((2, blk, width), bf),
            pltpu.VMEM((blocks, blk, width), bf),
            pltpu.VMEM((blocks, blk, lanes), bf),
            pltpu.VMEM((blocks, blk, lanes), bf),
            pltpu.VMEM((blocks, blk, lanes), bf),
            pltpu.VMEM((2, inner, 3 * lanes), bf),
            pltpu.VMEM((width, 3 * lanes), bf),
            pltpu.VMEM((packs, inner, width), bf),
        ]
        + [dma((blocks // 2,))] * 4
        + [dma((blocks,))] * 2
        + [dma((3,))] * 4,
        compiler_params=params_of(collective_id=number, has_side_effects=True),
        cost_estimate=BRIEF,
        name="attn_fwd",
    )(order, inv, x, small, wq, cosine, sine, wo)


def attn_bwd_kernel(
    order, inv, n1s, w, cosine, sine, qkv, o, lse, go, ghst, x, small, gsmall, gwo,
    gx, gm, dense,
    gor, gos, grads, acc, gns, sib_out, sib_in, gn_out, gnr, gw, gw_in, go_in, both, both_in,
    o_send, o_recv, s_send, s_recv, g_send, g_recv, r_send, r_recv,
):
    blocks, blk, width = grads.shape
    lanes = o.shape[1]
    seq = blocks * blk
    step = 2 * blk
    zero = jnp.asarray(0, jnp.bfloat16)
    own = lax.axis_index("ctx")
    z, xx, y, k = place()
    depth = blocks // 2
    same = xx == k

    barrier, others = greet_plane(blocks, across=True)
    acc[...] = jnp.zeros_like(acc)
    pl.semaphore_wait(barrier, others)

    def go_copy(unit):
        return remote(go.at[unit], gor.at[own], o_send.at[unit], o_recv.at[own], 2 * (unit // 2) + k, 2 * y + unit % 2)

    for unit in range(blocks):
        alone = jnp.logical_and(same, unit == 2 * z + k)

        @pl.when(jnp.logical_not(alone))
        def _():
            go_copy(unit).start()

        @pl.when(alone)
        def _():
            gor[own] = go[unit]

    for ctx in range(blocks):

        @pl.when(jnp.logical_not(jnp.logical_and(same, ctx == own)))
        def _():
            remote(go.at[0], gor.at[ctx], o_send.at[0], o_recv.at[ctx], ctx, 2 * y + xx).wait_recv()

    for b in range(blocks):
        gos[b * blk : (b + 1) * blk, :] = gor[inv[b]]
    lane = lax.broadcasted_iota(jnp.int32, (step, 128), 1)
    for i in range(seq // step):
        part = slice(i * step, (i + 1) * step)
        span = (i + 1) * step
        seen = lax.broadcasted_iota(jnp.int32, (step, span), 1) <= (
            lax.broadcasted_iota(jnp.int32, (step, span), 0) + i * step
        )
        key_lane = lax.broadcasted_iota(jnp.int32, (span, 128), 1)
        for head in range(GROUP_HEADS):
            tile, side = head // 2, head % 2
            at = tile * 128
            mine = lane // 64 == side
            q = jnp.where(mine, qkv[part, at : at + 128], zero)
            g = jnp.where(mine, gos[part, at : at + 128], zero)
            keys = qkv[:span, lanes + at : lanes + at + 128]
            values = qkv[:span, 2 * lanes + at : 2 * lanes + at + 128]
            delta = jnp.sum(g.astype(jnp.float32) * o[part, at : at + 128], axis=1, keepdims=True)
            s = nt(q, keys)
            p = jnp.where(seen, jnp.exp(jnp.where(seen, s, -1e30) - lse[part, head : head + 1]), 0.0)
            ds = (p * (nt(g, values) - delta)).astype(jnp.bfloat16)
            acc[:span, 2 * lanes + at : 2 * lanes + at + 128] += tn(p.astype(jnp.bfloat16), g)
            acc[:span, lanes + at : lanes + at + 128] += tn(ds, q)
            acc[part, at : at + 128] += nn(ds, jnp.where(key_lane // 64 == side, keys, zero))
    for b in range(blocks):
        part = slice(b * blk, (b + 1) * blk)
        cos2 = jnp.concatenate([cosine[part, :]] * (lanes // 128), axis=1)
        sin2 = jnp.concatenate([sine[part, :]] * (lanes // 128), axis=1)
        grads[b, :, :lanes] = spin(acc[part, :lanes] * HEAD_DIM**-0.5, cos2, -sin2).astype(jnp.bfloat16)
        grads[b, :, lanes : 2 * lanes] = spin(acc[part, lanes : 2 * lanes], cos2, -sin2).astype(jnp.bfloat16)
        grads[b, :, 2 * lanes :] = acc[part, 2 * lanes :].astype(jnp.bfloat16)

    def sib_copy(zz):
        return remote(sib_out.at[zz], sib_in.at[zz], s_send.at[zz], s_recv.at[zz], own, 2 * y + 1 - k)

    def gn_copy(zz):
        return remote(gn_out.at[zz], gnr.at[z], g_send.at[zz], g_recv.at[z], 2 * zz + k, 2 * y + xx)

    gain = small[0:1, :].astype(jnp.float32)
    ggain = jnp.zeros((1, width), jnp.float32)
    for b in range(blocks):
        gns[b] = nt(grads[b], w[...])
        ggain = ggain + jnp.sum(gns[b] * n1s[b * blk : (b + 1) * blk, :].astype(jnp.float32), axis=0, keepdims=True)
    for zz in range(depth):
        sib_out[zz] = gns[order[2 * zz + 1 - k]].astype(jnp.bfloat16)
        sib_copy(zz).start()
    for zz in range(depth):
        sib_copy(zz).wait_recv()
        alone = jnp.logical_and(same, zz == z)
        gn_out[zz] = (gns[order[2 * zz + k]] + sib_in[zz].astype(jnp.float32)).astype(jnp.bfloat16)

        @pl.when(jnp.logical_not(alone))
        def _():
            gn_copy(zz).start()

        @pl.when(alone)
        def _():
            gnr[z] = gn_out[zz]

    packs, inner = gwo.shape[0], gwo.shape[1]
    sums = jnp.concatenate([ggain / gain, gsmall[...]], axis=0)
    sums = jnp.concatenate([sums, jnp.zeros((128 - sums.shape[0], width), jnp.float32)], axis=0)
    sums = jnp.transpose(sums).astype(jnp.bfloat16)
    for f in range(packs):
        rows = slice(f * inner, (f + 1) * inner)
        piece = tn(n1s[:, rows], grads[...].reshape(seq, 3 * lanes)).astype(jnp.bfloat16)
        gw[f, :, :128] = sums[rows]
        for c in range(3):
            gw[f, :, 128 + c * inner : 128 + (c + 1) * inner] = piece[:, c * lanes : c * lanes + inner]
        gw[f, :, 128 + 3 * inner :] = jnp.zeros((inner, gw.shape[2] - 128 - 3 * inner), jnp.bfloat16)

    def home_copy(index):
        source, target = ((gw, gw_in), (gwo, go_in))[index % 2]
        half = index // 2
        return remote(
            source.at[2 * half + 1 - k], target.at[half], r_send.at[index], r_recv.at[index], own, 2 * y + 1 - k
        )

    for index in range(4):
        home_copy(index).start()
    for half in range(2):
        home_copy(2 * half).wait_recv()
        home_copy(2 * half + 1).wait_recv()
        kept, came = gw[2 * half + k], gw_in[half]
        both[half, :, :128] = (kept[:, :128].astype(jnp.float32) + came[:, :128].astype(jnp.float32)).astype(jnp.bfloat16)
        heads = slice(128, 128 + 3 * inner)
        for core in range(2):

            @pl.when(k == core)
            def _():
                both[half, :, 128 + core * 3 * inner : 128 + (core + 1) * 3 * inner] = kept[:, heads]
                both[half, :, 128 + (1 - core) * 3 * inner : 128 + (2 - core) * 3 * inner] = came[:, heads]

        outs = gwo[2 * half + k].astype(jnp.float32) + go_in[half].astype(jnp.float32)
        both[half, :, 128 + 6 * inner :] = outs.astype(jnp.bfloat16)
    over = remote(both.at[1 - y], both_in, r_send.at[4], r_recv.at[4], own, 2 * (1 - y) + k)
    over.start()
    for zz in range(depth):

        @pl.when(jnp.logical_not(jnp.logical_and(same, zz == z)))
        def _():
            remote(gn_out.at[0], gnr.at[zz], g_send.at[0], g_recv.at[zz], 2 * zz + k, 2 * y + xx).wait_recv()

    halves = []
    for h in range(2):
        total = gnr[h * (depth // 2)].astype(jnp.float32)
        for zz in range(1, depth // 2):
            total = total + gnr[h * (depth // 2) + zz].astype(jnp.float32)
        halves.append(total)
    gn = jnp.concatenate(halves, axis=0)
    values = x[...]
    factor = rms_factor(values)
    base = values * factor
    gb = gn * gain
    grad = ghst[...] + factor * (gb - base * jnp.mean(gb * base, axis=-1, keepdims=True))
    gx[...] = grad
    gm[...] = grad.astype(jnp.bfloat16)
    over.wait_recv()
    dense[...] = (both[y].astype(jnp.float32) + both_in[...].astype(jnp.float32)).astype(jnp.bfloat16)
    for index in range(4):
        home_copy(index).wait_send()
    over.wait_send()
    for unit in range(blocks):

        @pl.when(jnp.logical_not(jnp.logical_and(same, unit == 2 * z + k)))
        def _():
            go_copy(unit).wait_send()

    for zz in range(depth):
        sib_copy(zz).wait_send()

        @pl.when(jnp.logical_not(jnp.logical_and(same, zz == z)))
        def _():
            gn_copy(zz).wait_send()


def attn_backward(order, inv, n1s, w, cosine, sine, qkv, o, lse, go, ghst, x, small, gsmall, gwo, number):
    blocks, blk, lanes = go.shape
    seq, width = n1s.shape
    count = x.shape[0]
    packs, inner = gwo.shape[0], gwo.shape[1]
    depth = blocks // 2
    vm = pl.BlockSpec(memory_space=pltpu.VMEM)
    sm = pl.BlockSpec(memory_space=pltpu.SMEM)
    bf = jnp.bfloat16
    dma = pltpu.SemaphoreType.DMA
    return pl.pallas_call(
        attn_bwd_kernel,
        out_shape=[
            shape_of((count, width), jnp.float32),
            shape_of((count, width), bf),
            shape_of((inner, 128 + 6 * inner + width), bf),
        ],
        in_specs=[sm] * 2 + [vm] * 13,
        out_specs=[vm] * 3,
        scratch_shapes=[
            pltpu.VMEM((blocks, blk, lanes), bf),
            pltpu.VMEM((seq, lanes), bf),
            pltpu.VMEM((blocks, blk, 3 * lanes), bf),
            pltpu.VMEM((seq, 3 * lanes), jnp.float32),
            pltpu.VMEM((blocks, blk, width), jnp.float32),
            pltpu.VMEM((depth, blk, width), bf),
            pltpu.VMEM((depth, blk, width), bf),
            pltpu.VMEM((depth, blk, width), bf),
            pltpu.VMEM((depth, blk, width), bf),
            pltpu.VMEM((packs, inner, 3 * lanes), bf),
            pltpu.VMEM((2, inner, 3 * lanes), bf),
            pltpu.VMEM((2, inner, width), bf),
            pltpu.VMEM((2, inner, 128 + 6 * inner + width), bf),
            pltpu.VMEM((inner, 128 + 6 * inner + width), bf),
        ]
        + [dma((blocks,))] * 2
        + [dma((depth,))] * 4
        + [dma((5,))] * 2,
        compiler_params=params_of(collective_id=number, has_side_effects=True),
        cost_estimate=BRIEF,
        name="attn_bwd",
    )(order, inv, n1s, w, cosine, sine, qkv, o, lse, go, ghst, x, small, gsmall, gwo)


def routing(raw, before, routes):
    count = raw.shape[1]
    ids = lax.broadcasted_iota(jnp.int32, (16, count), 0)
    logits = raw + before
    first, second = ids == routes[0:1], ids == routes[1:2]
    z0 = jnp.sum(jnp.where(first, logits, 0.0), axis=0, keepdims=True)
    z1 = jnp.sum(jnp.where(second, logits, 0.0), axis=0, keepdims=True)
    top = jnp.maximum(z0, z1)
    e0, e1 = jnp.exp(z0 - top), jnp.exp(z1 - top)
    total = e0 + e1
    coef = jnp.where(first, e0 / total, 0.0) + jnp.where(second, e1 / total, 0.0)
    hits = jnp.where(first | second, 1.0, 0.0)
    upto = lax.broadcasted_iota(jnp.int32, (count, count), 0) <= lax.broadcasted_iota(jnp.int32, (count, count), 1)
    place = nn(hits.astype(jnp.bfloat16), jnp.where(upto, 1.0, 0.0).astype(jnp.bfloat16)) - 1.0
    slot = jnp.where(hits > 0, place, -1.0)
    return jnp.concatenate([raw, coef, slot[:NF], logits], axis=0)


def one_hot(slot):
    count = slot.shape[1]
    ids = lax.broadcasted_iota(jnp.int32, (NF, MOST, count), 1)
    hit = ids == slot.astype(jnp.int32)[:, None, :]
    return jnp.where(hit, 1.0, 0.0).reshape(NF * MOST, count)


def slot_values(hot, rows):
    count = rows.shape[1]
    wide = jnp.broadcast_to(rows[:, None, :], (NF, MOST, count)).reshape(NF * MOST, count)
    return jnp.sum(hot * wide, axis=1, keepdims=True)


def swap_rows(own, rows, send, recv, forward_send, forward_recv):
    ctx = lax.axis_index("ctx")
    _, _, y, k = place()
    beside, across = 2 * y + 1 - k, 2 * (1 - y) + k
    far = remote(own, rows.at[2], send.at[0], recv.at[0], ctx, across)
    near = remote(own, rows.at[1], send.at[1], recv.at[1], ctx, beside)
    onward = remote(rows.at[2], rows.at[3], forward_send, forward_recv, ctx, beside)
    far.start()
    near.start()
    return near, far, onward


def sum_rows(parts, beside_in, mid, across_in, send, recv):
    ctx = lax.axis_index("ctx")
    _, _, y, k = place()
    beside, across = 2 * y + 1 - k, 2 * (1 - y) + k
    first = remote(parts.at[3], beside_in.at[1], send.at[0], recv.at[0], ctx, beside)
    second = remote(parts.at[1], beside_in.at[0], send.at[1], recv.at[1], ctx, beside)
    third = remote(mid, across_in, send.at[2], recv.at[2], ctx, across)
    return first, second, third


def ffn_fwd_kernel(
    ub, hst, small, routes, before, wgu, wd,
    ubf, table, ext, x_next,
    rows_s, hot_s, x_s, y_s, coef_s, parts, beside_in, mid, across_in,
    a_send, a_recv, r_send, r_recv,
):
    e = pl.program_id(0)
    packs = ubf.shape[0]
    count, width = ub.shape
    router = small[2 + NC :, :]

    def gathers():
        return swap_rows(ub, rows_s, a_send, a_recv, a_send.at[2], a_recv.at[2])

    def sums():
        return sum_rows(parts, beside_in, mid, across_in, r_send, r_recv)

    @pl.when(e == 0)
    def _():
        barrier, others = greet_packs()
        rows_s[0] = ub[...]

        def prepare(d):
            rows = routing(nt(router, rows_s[d]), before[d], routes[d])
            table[d] = rows
            hot = one_hot(rows[SLOT : SLOT + NF])
            coef_s[d] = slot_values(hot, rows[COEF : COEF + NF])
            hot_low = hot.astype(jnp.bfloat16)
            hot_s[d] = hot_low
            x = nn(hot_low, rows_s[d]).astype(jnp.bfloat16)
            for n in range(NF):
                x_s[n, d * MOST : (d + 1) * MOST, :] = x[n * MOST : (n + 1) * MOST]

        pl.semaphore_wait(barrier, others)
        near, far, onward = gathers()
        prepare(0)
        near.wait_recv()
        prepare(1)
        far.wait_recv()
        onward.start()
        prepare(2)
        onward.wait_recv()
        prepare(3)
        ubf[...] = rows_s[...]
        ext[:count, :] = ub[...]
        rows = table[0]
        ext[count:, :] = jnp.zeros((16, width), jnp.bfloat16)
        ext[count:, :count] = rows[COEF : COEF + 16].astype(jnp.bfloat16)
        slots = jnp.concatenate([rows[SLOT : SLOT + NF], jnp.zeros((16 - NF, count), jnp.float32)], axis=0)
        ext[count:, count : 2 * count] = slots.astype(jnp.bfloat16)
        near.wait_send()
        far.wait_send()
        onward.wait_send()

    x = x_s[e]
    gate, up = nn(x, wgu[0, 0, 0]), nn(x, wgu[0, 0, 1])
    hid = (gate * jax.nn.sigmoid(gate) * up).astype(jnp.bfloat16)
    out = nn(hid, wd[0, 0])
    at = pl.ds(pl.multiple_of(e * MOST, MOST), MOST)
    for d in range(packs):
        y_s[d, at, :] = (out[d * MOST : (d + 1) * MOST] * coef_s[d, at, :]).astype(jnp.bfloat16)

    @pl.when(e == NF - 1)
    def _():
        first, second, third = sums()
        parts[3] = tn(hot_s[3], y_s[3]).astype(jnp.bfloat16)
        first.start()
        parts[1] = tn(hot_s[1], y_s[1]).astype(jnp.bfloat16)
        second.start()
        away = tn(hot_s[2], y_s[2])
        first.wait_recv()
        mid[...] = (away + beside_in[1].astype(jnp.float32)).astype(jnp.bfloat16)
        third.start()
        home = tn(hot_s[0], y_s[0])
        _, _, scale_u, scale_c = mixing_rows(table[0])
        columns = to_columns([scale_u] + scale_c)
        values = hst[...]
        moe = home + columns[0] * ((values * rms_factor(values)) * small[1:2, :].astype(jnp.float32))
        for c in range(NC):
            moe = moe + columns[1 + c] * small[2 + c : 3 + c, :].astype(jnp.float32)
        second.wait_recv()
        moe = moe + beside_in[0].astype(jnp.float32)
        third.wait_recv()
        x_next[...] = values + (moe + across_in[...].astype(jnp.float32))
        first.wait_send()
        second.wait_send()
        third.wait_send()


def whole_spec(dims):
    return pl.BlockSpec(dims, lambda *_: (0,) * len(dims))


def exchange_scratch(packs, count, width):
    bf = jnp.bfloat16
    return [
        pltpu.VMEM((packs, count, width), bf),
        pltpu.VMEM((2, count, width), bf),
        pltpu.VMEM((count, width), bf),
        pltpu.VMEM((count, width), bf),
    ]


def ffn_forward(layer, ub, hst, small, routes, before, wgu, wd, number):
    count, width = ub.shape
    packs = routes.shape[0]
    hidden = wd.shape[2]
    bf = jnp.bfloat16
    outs = [
        shape_of((packs, count, width), bf),
        shape_of((packs, ROUT, count), jnp.float32),
        shape_of((count + 16, width), bf),
        shape_of((count, width), jnp.float32),
    ]
    return pl.pallas_call(
        ffn_fwd_kernel,
        grid=(NF,),
        out_shape=outs,
        in_specs=[whole_spec(a.shape) for a in (ub, hst, small, routes, before)]
        + [
            pl.BlockSpec((1, 1, 2, width, hidden), lambda e: (layer, e, 0, 0, 0)),
            pl.BlockSpec((1, 1, hidden, width), lambda e: (layer, e, 0, 0)),
        ],
        out_specs=[whole_spec(a.shape) for a in outs],
        scratch_shapes=[
            pltpu.VMEM((packs, count, width), bf),
            pltpu.VMEM((packs, NF * MOST, count), bf),
            pltpu.VMEM((NF, packs * MOST, width), bf),
            pltpu.VMEM((packs, NF * MOST, width), bf),
            pltpu.VMEM((packs, NF * MOST, 1), jnp.float32),
        ]
        + exchange_scratch(packs, count, width)
        + [pltpu.SemaphoreType.DMA((3,))] * 4,
        compiler_params=params_of(collective_id=number, has_side_effects=True),
        cost_estimate=BRIEF,
        name="ffn_fwd",
    )(ub, hst, small, routes, before, wgu, wd)


def silu_parts(gate, up, ghid):
    sig = jax.nn.sigmoid(gate)
    act = gate * sig
    dg = (ghid * up * sig * (1.0 + gate * (1.0 - sig))).astype(jnp.bfloat16)
    du = (ghid * act).astype(jnp.bfloat16)
    return act * up, dg, du


def ffn_bwd_kernel(
    gm, gx, ubf, table, hst, small, routes, gprev, wo, ob, wgu, wd,
    ghst, go, gwo, gsmall, glog,
    rows_s, hot_s, x_s, g_s, y_s, coef_s, gc_s, gcoef, gcoef_in, parts, beside_in, mid, across_in,
    a_send, a_recv, r_send, r_recv, c_send, c_recv,
):
    e = pl.program_id(0)
    packs = ubf.shape[0]
    ctx = lax.axis_index("ctx")
    _, _, y, k = place()
    peers = [None, 2 * y + 1 - k, 2 * (1 - y) + k, 2 * (1 - y) + 1 - k]

    def gathers():
        return swap_rows(gm, rows_s, a_send, a_recv, a_send.at[2], a_recv.at[2])

    def sums():
        return sum_rows(parts, beside_in, mid, across_in, r_send, r_recv)

    @pl.when(e == 0)
    def _():
        barrier, others = greet_packs()
        rows_s[0] = gm[...]

        def prepare(d):
            hot = one_hot(table[d, SLOT : SLOT + NF, :])
            coef_s[d] = slot_values(hot, table[d, COEF : COEF + NF, :])
            hot_low = hot.astype(jnp.bfloat16)
            hot_s[d] = hot_low
            x = nn(hot_low, ubf[d]).astype(jnp.bfloat16)
            for n in range(NF):
                x_s[n, d * MOST : (d + 1) * MOST, :] = x[n * MOST : (n + 1) * MOST]

        def spread(d):
            g = nn(hot_s[d], rows_s[d]).astype(jnp.bfloat16)
            for n in range(NF):
                g_s[n, d * MOST : (d + 1) * MOST, :] = g[n * MOST : (n + 1) * MOST]

        pl.semaphore_wait(barrier, others)
        near, far, onward = gathers()
        for d in range(packs):
            prepare(d)
        spread(0)
        near.wait_recv()
        far.wait_recv()
        onward.start()
        spread(1)
        spread(2)
        onward.wait_recv()
        spread(3)
        near.wait_send()
        far.wait_send()
        onward.wait_send()

    x = x_s[e]
    at = pl.ds(pl.multiple_of(e * MOST, MOST), MOST)
    coef = jnp.concatenate([coef_s[d, at, :] for d in range(packs)], axis=0)
    gate, up = nn(x, wgu[0, 0, 0]), nn(x, wgu[0, 0, 1])
    ghid = nt(g_s[e], wd[0, 0])
    hid, dg, du = silu_parts(gate, up, ghid * coef)
    dots = jnp.sum(hid * ghid, axis=1, keepdims=True)
    out = nt(dg, wgu[0, 0, 0]) + nt(du, wgu[0, 0, 1])
    for d in range(packs):
        y_s[d, at, :] = out[d * MOST : (d + 1) * MOST].astype(jnp.bfloat16)
        gc_s[d, at, :] = dots[d * MOST : (d + 1) * MOST]

    @pl.when(e == NF - 1)
    def _():
        first, second, third = sums()

        def coef_copy(d):
            return remote(gcoef.at[d], gcoef_in.at[d - 1], c_send.at[d - 1], c_recv.at[d - 1], ctx, peers[d])

        parts[3] = tn(hot_s[3], y_s[3]).astype(jnp.bfloat16)
        first.start()
        parts[1] = tn(hot_s[1], y_s[1]).astype(jnp.bfloat16)
        second.start()
        for d in range(packs):
            wide = hot_s[d].astype(jnp.float32) * gc_s[d]
            gcoef[d] = jnp.sum(wide.reshape(NF, MOST, wide.shape[1]), axis=1)
            if d > 0:
                coef_copy(d).start()
        away = tn(hot_s[2], y_s[2])
        first.wait_recv()
        mid[...] = (away + beside_in[1].astype(jnp.float32)).astype(jnp.bfloat16)
        third.start()
        home = tn(hot_s[0], y_s[0])
        second.wait_recv()
        home = home + beside_in[0].astype(jnp.float32)
        total = gcoef[0]
        for d in range(1, packs):
            coef_copy(d).wait_recv()
            total = total + gcoef_in[d - 1]
        third.wait_recv()
        home = home + across_in[...].astype(jnp.float32)
        results = middle(
            gx[...], home, total, table[0], routes[...], gprev[...], hst[...], ubf[0],
            small[...], wo[...], ob[...],
        )
        for ref, value in zip((ghst, go, gwo, gsmall, glog), results):
            ref[...] = value
        first.wait_send()
        second.wait_send()
        third.wait_send()
        for d in range(1, packs):
            coef_copy(d).wait_send()


def ffn_backward(layer, gm, gx, ubf, table, hst, small, routes, gprev, wo, ob, wgu, wd, number):
    packs, count, width = ubf.shape
    hidden = wd.shape[2]
    bf, f32 = jnp.bfloat16, jnp.float32
    outs = [
        shape_of((count, width), f32),
        shape_of(ob.shape, bf),
        shape_of(wo.shape, bf),
        shape_of((1 + NC + 16, width), f32),
        shape_of((16, count), f32),
    ]
    args = (gm, gx, ubf, table, hst, small, routes, gprev, wo, ob)
    dma = pltpu.SemaphoreType.DMA
    return pl.pallas_call(
        ffn_bwd_kernel,
        grid=(NF,),
        out_shape=outs,
        in_specs=[whole_spec(a.shape) for a in args]
        + [
            pl.BlockSpec((1, 1, 2, width, hidden), lambda e: (layer, e, 0, 0, 0)),
            pl.BlockSpec((1, 1, hidden, width), lambda e: (layer, e, 0, 0)),
        ],
        out_specs=[whole_spec(a.shape) for a in outs],
        scratch_shapes=[
            pltpu.VMEM((packs, count, width), bf),
            pltpu.VMEM((packs, NF * MOST, count), bf),
            pltpu.VMEM((NF, packs * MOST, width), bf),
            pltpu.VMEM((NF, packs * MOST, width), bf),
            pltpu.VMEM((packs, NF * MOST, width), bf),
            pltpu.VMEM((packs, NF * MOST, 1), f32),
            pltpu.VMEM((packs, NF * MOST, 1), f32),
            pltpu.VMEM((packs, NF, count), f32),
            pltpu.VMEM((packs - 1, NF, count), f32),
        ]
        + exchange_scratch(packs, count, width)
        + [dma((3,))] * 6,
        compiler_params=params_of(collective_id=number, has_side_effects=True),
        cost_estimate=BRIEF,
        name="ffn_bwd",
    )(*args, wgu, wd)


def slot_rows(ext, weighted):
    rows = ext.astype(jnp.float32)
    count = rows.shape[1] // 3
    coef, slot = rows[:NF, :count], rows[:NF, count : 2 * count].astype(jnp.int32)
    hit = lax.broadcasted_iota(jnp.int32, (NF, MOST, count), 1) == slot[:, None, :]
    hot = jnp.where(hit, coef[:, None, :] if weighted else 1.0, 0.0)
    return hot.astype(jnp.bfloat16).reshape(NF * MOST, count)


def dispatch_kernel(rows, weighted, tail, values, out):
    for d in range(values.shape[0]):
        low = nn(slot_rows(tail[d], weighted), values[d, :rows, :]).astype(jnp.bfloat16)
        out[:, d] = low.reshape(NF, MOST, low.shape[1])


def dispatch(ext, values, weighted):
    devices, _, width = ext.shape
    rows = ext.shape[1] - 16
    some = 4
    out = pl.pallas_call(
        functools.partial(dispatch_kernel, rows, weighted),
        grid=(devices // some,),
        out_shape=shape_of((NF, devices, MOST, width), jnp.bfloat16),
        in_specs=[
            pl.BlockSpec((some, 16, width), lambda d: (d, rows // 16, 0)),
            pl.BlockSpec((some,) + values.shape[1:], lambda d: (d, 0, 0)),
        ],
        out_specs=pl.BlockSpec((NF, some, MOST, width), lambda d: (0, d, 0, 0)),
        compiler_params=params_of(),
        cost_estimate=BRIEF,
        name="dispatch",
    )(ext, values)
    return out.reshape(NF, devices * MOST, width)


def dw_kernel(*refs):
    x, g, wgu, wd, dgu, dd, dg_s, du_s, hid_s = refs[:4] + refs[-5:]
    rows = x.shape[1]
    chunk = 256

    def pieces(i, _):
        part = pl.ds(pl.multiple_of(i * chunk, chunk), chunk)
        xs = x[0, part, :]
        hid, dg, du = silu_parts(nn(xs, wgu[0, 0, 0]), nn(xs, wgu[0, 0, 1]), nt(g[0, part, :], wd[0, 0]))
        hid_s[part, :] = hid.astype(jnp.bfloat16)
        dg_s[part, :] = dg
        du_s[part, :] = du
        return 0

    lax.fori_loop(0, rows // chunk, pieces, 0)

    def first(i, _):
        part = pl.ds(pl.multiple_of(i * 256, 256), 256)
        xs = x[0, :, part]
        dgu[0, 0, 0, part, :] = tn(xs, dg_s[...])
        dgu[0, 0, 1, part, :] = tn(xs, du_s[...])
        return 0

    lax.fori_loop(0, x.shape[2] // 256, first, 0)

    def second(i, _):
        part = pl.ds(pl.multiple_of(i * 256, 256), 256)
        dd[0, 0, part, :] = tn(hid_s[:, part], g[0])
        return 0

    lax.fori_loop(0, hid_s.shape[1] // 256, second, 0)


def weight_grads(layer, first, last, x, g, wgu, wd, earlier):
    _, rows, width = x.shape
    hidden = wd.shape[2]
    gu_spec = pl.BlockSpec((1, 1, 2, width, hidden), lambda e: (layer, e + first, 0, 0, 0))
    d_spec = pl.BlockSpec((1, 1, hidden, width), lambda e: (layer, e + first, 0, 0))
    row_spec = pl.BlockSpec((1, rows, width), lambda e: (e + first, 0, 0))
    return pl.pallas_call(
        dw_kernel,
        grid=(last - first,),
        out_shape=[shape_of(wgu.shape, jnp.float32), shape_of(wd.shape, jnp.float32)],
        in_specs=[row_spec, row_spec, gu_spec, d_spec] + [pl.BlockSpec(memory_space=pl.ANY)] * len(earlier),
        out_specs=[gu_spec, d_spec],
        input_output_aliases={4 + i: i for i in range(len(earlier))},
        scratch_shapes=[pltpu.VMEM((rows, hidden), jnp.bfloat16)] * 3,
        compiler_params=params_of(),
        cost_estimate=BRIEF,
        name="weight_grads",
    )(x, g, wgu, wd, *earlier)


def norm_low(x, gain):
    return ((x * rms_factor(x)) * gain).astype(jnp.bfloat16)


def post_attention(ob, x, wo, gain):
    groups = wo.shape[0]
    inner = wo.shape[1]
    blk = ob.shape[1]
    halves = []
    for h in range(2):
        total = x[h * blk : (h + 1) * blk]
        for g in range(groups):
            total = total + nn(ob[h * groups + g][:, :inner], wo[g])
        halves.append(total)
    hst = jnp.concatenate(halves, axis=0)
    return hst, norm_low(hst, gain)


def mixing_rows(table):
    raw, coef = table[RAW : RAW + 16], table[COEF : COEF + 16]
    pairs = []
    for c in range(NC):
        r0, r1 = raw[NE + 2 * c : NE + 2 * c + 1], raw[NE + 2 * c + 1 : NE + 2 * c + 2]
        top = jnp.maximum(r0, r1)
        e0, e1 = jnp.exp(r0 - top), jnp.exp(r1 - top)
        pairs.append((e0 / (e0 + e1), e1 / (e0 + e1)))
    shares = [coef[NF + 2 + c : NF + 3 + c] for c in range(NC)]
    scale_u = coef[NF + 1 : NF + 2]
    for c in range(NC):
        scale_u = scale_u + shares[c] * pairs[c][0]
    return pairs, shares, scale_u, [shares[c] * pairs[c][1] for c in range(NC)]


def middle(gx, parts, gcoef, table, routes, gprev, hst, ub, small, wo, ob):
    groups = wo.shape[0]
    inner = wo.shape[1]
    blk = ob.shape[1]
    gain = small[1:2].astype(jnp.float32)
    consts = small[2 : 2 + NC].astype(jnp.float32)
    router = small[2 + NC :]
    pairs, shares, scale_u, scale_c = mixing_rows(table)
    columns = to_columns([scale_u] + scale_c)
    factor = rms_factor(hst)
    base = hst * factor
    u = base * gain
    dots = [jnp.sum(gx * u, axis=1, keepdims=True)]
    dots += [jnp.sum(gx * consts[c : c + 1], axis=1, keepdims=True) for c in range(NC)]
    dots = to_rows(dots, 8)
    dot_u = dots[0:1]
    dot_c = [dots[1 + c : 2 + c] for c in range(NC)]
    ids = lax.broadcasted_iota(jnp.int32, (16, gx.shape[0]), 0)
    grads = jnp.concatenate([gcoef, jnp.zeros_like(gcoef)], axis=0)
    grads = jnp.where(ids == NF + 1, dot_u, grads)
    raw_rows = []
    for c in range(NC):
        a0, a1 = pairs[c]
        grads = jnp.where(ids == NF + 2 + c, a0 * dot_u + a1 * dot_c[c], grads)
        g0, g1 = shares[c] * dot_u, shares[c] * dot_c[c]
        both = a0 * g0 + a1 * g1
        raw_rows += [a0 * (g0 - both), a1 * (g1 - both)]
    logits = table[LOGI : LOGI + 16]
    first, second = ids == routes[0:1], ids == routes[1:2]

    def pick(chosen, rows):
        return jnp.sum(jnp.where(chosen, rows, 0.0), axis=0, keepdims=True)

    z0, z1 = pick(first, logits), pick(second, logits)
    top = jnp.maximum(z0, z1)
    e0, e1 = jnp.exp(z0 - top), jnp.exp(z1 - top)
    w0, w1 = e0 / (e0 + e1), e1 / (e0 + e1)
    gg0, gg1 = pick(first, grads), pick(second, grads)
    both = w0 * gg0 + w1 * gg1
    glog = jnp.where(first, w0 * (gg0 - both), 0.0) + jnp.where(second, w1 * (gg1 - both), 0.0) + gprev
    graw = glog
    for index, row in enumerate(raw_rows):
        graw = jnp.where(ids == NE + index, row, graw)
    graw = graw.astype(jnp.bfloat16)
    grad_router = nn(graw, ub)
    gu = gx * columns[0] + tn(graw, router) + parts
    sums = [jnp.sum(gu * base, axis=0, keepdims=True)]
    sums += [jnp.sum(gx * columns[1 + c], axis=0, keepdims=True) for c in range(NC)]
    gb = gu * gain
    ghst = gx + factor * (gb - base * jnp.mean(gb * base, axis=-1, keepdims=True))
    gy = ghst.astype(jnp.bfloat16)
    lanes = ob.shape[2]
    go, gwo = [None] * (2 * groups), []
    for g in range(groups):
        value = nt(gy, wo[g]).astype(jnp.bfloat16)
        value = jnp.concatenate([value, jnp.zeros((value.shape[0], lanes - inner), jnp.bfloat16)], axis=1)
        for h in range(2):
            go[h * groups + g] = value[h * blk : (h + 1) * blk]
        mixed = jnp.concatenate([ob[g], ob[groups + g]], axis=0)
        gwo.append(tn(mixed, gy)[:inner].astype(jnp.bfloat16))
    return ghst, jnp.stack(go), jnp.stack(gwo), jnp.concatenate(sums + [grad_router], axis=0), glog


def assemble_kernel(ours, theirs, qkv, out, small):
    z, _, _, _ = place()
    layers, shard = ours.shape[0], ours.shape[1]
    inner = GROUP_HEADS * HEAD_DIM
    for l in range(layers):
        small[l] = ours[l, :, :128].astype(jnp.float32) + theirs[l, :, :128].astype(jnp.float32)
        first = 128 + 6 * inner
        out[l] = ours[l, :, first:].astype(jnp.float32) + theirs[l, :, first:].astype(jnp.float32)
        for group in range(4):
            for odd in range(2):

                @pl.when(z % 2 == odd)
                def _():
                    source = ours if group // 2 == odd else theirs
                    for c in range(3):
                        at = 128 + (group % 2) * 3 * inner + c * inner
                        qkv[l, c, :, group * inner : (group + 1) * inner] = source[l, :, at : at + inner].astype(jnp.float32)


def assemble(ours, theirs, width):
    layers, shard, _ = ours.shape
    vm = pl.BlockSpec(memory_space=pltpu.VMEM)
    return pl.pallas_call(
        assemble_kernel,
        out_shape=[
            shape_of((layers, 3, shard, width), jnp.float32),
            shape_of((layers, shard, width), jnp.float32),
            shape_of((layers, shard, 128), jnp.float32),
        ],
        in_specs=[vm] * 2,
        out_specs=[vm] * 3,
        compiler_params=params_of(),
        cost_estimate=BRIEF,
        name="assemble",
    )(ours, theirs)


def turn_tables(seq):
    half = HEAD_DIM // 2
    frequency = np.exp((-np.log(np.float32(10000.0)) * np.arange(half, dtype=np.float32) / np.float32(half)))
    angles = np.arange(seq, dtype=np.float32)[:, None] * frequency.astype(np.float32)[None, :]
    cosine, sine = np.cos(angles), np.sin(angles)
    cosine = np.concatenate([cosine, cosine] * 2, axis=1).astype(np.float32)
    sine = np.concatenate([-sine, sine] * 2, axis=1).astype(np.float32)
    return jnp.asarray(cosine), jnp.asarray(sine)


def by_heads(
    tokens,
    cotangent,
    seq_lengths,
    block_order,
    routes,
    gains,
    qkv_weights,
    out_weight,
    router,
    const_values,
    w_gate_up,
    w_down,
):
    count, width = tokens.shape[1], tokens.shape[2]
    ctx_size, packs = lax.axis_size("ctx"), lax.axis_size("fsdp")
    blk = count // 2
    seq = blk * ctx_size
    pack = lax.axis_index("fsdp")
    z, xx, y, k = place()
    sequence = z // 2
    shard = width // packs
    f32, bf = jnp.float32, jnp.bfloat16
    everyone = ("ctx", "fsdp")

    cosine, sine = turn_tables(seq)
    routes_t = jnp.swapaxes(routes[:, 0], 1, 2)
    smalls = jnp.concatenate([gains, const_values, jnp.swapaxes(router, 1, 2)], axis=1)
    per_layer = smalls.shape[1]
    ints = jnp.concatenate([routes_t.reshape(-1), block_order[0]])
    places = ints.size
    ints = jnp.pad(ints, (0, -places % shard)).astype(bf).reshape(-1, shard)
    smalls = jnp.concatenate([smalls.reshape(LAYERS * per_layer, shard), ints], axis=0)
    smalls = jnp.pad(smalls, ((0, -smalls.shape[0] % 16), (0, 0)))
    smalls = lax.all_gather(smalls, "fsdp", axis=1, tiled=True)
    ints = smalls[LAYERS * per_layer : LAYERS * per_layer + ints.shape[0]].reshape(-1, packs, shard)
    ints = jnp.swapaxes(ints, 0, 1).reshape(packs, -1).astype(jnp.int32)
    smalls = [smalls[l * per_layer : (l + 1) * per_layer] for l in range(LAYERS)]
    near = jnp.stack([pack, 2 * y + 1 - k, 2 * (1 - y) + k, 2 * (1 - y) + 1 - k])
    routes_f = ints[near][:, : routes_t.size].reshape((packs,) + routes_t.shape)
    order = lax.dynamic_index_in_dim(ints, 2 * y + xx, 0, keepdims=False)
    order = order[routes_t.size : places].reshape(ctx_size, 2)
    order = lax.dynamic_index_in_dim(order, sequence, 1, keepdims=False) - ctx_size * sequence
    ids = jnp.arange(ctx_size, dtype=jnp.int32)
    inv = jnp.sum(jnp.where(order[None, :] == ids[:, None], ids[None, :], 0), axis=1)

    gm_all = [None, lax.all_gather(cotangent[0], everyone, axis=0, tiled=False)]
    x = tokens[0].astype(f32)
    before = jnp.zeros((packs, 16, count), f32)
    kept, ext_all = [], [None] * LAYERS
    for l in range(LAYERS):
        n1s, qkv, o, lse, ob, hst, ub, w, wo = attn_forward(
            l, order, inv, x, smalls[l], qkv_weights, cosine, sine, out_weight, 2 * l
        )
        if l == 1:
            ub, gm_all[1] = lax.optimization_barrier((ub, gm_all[1]))
        ubf, table, ext, x_next = ffn_forward(
            l, ub, hst, smalls[l], routes_f[:, l], before, w_gate_up, w_down, 2 * l + 1
        )
        before = table[:, LOGI : LOGI + 16]
        ext_all[l] = lax.all_gather(ext, everyone, axis=0, tiled=False)
        kept.append((x, n1s, qkv, o, lse, ob, hst, w, wo, ubf, table))
        x = x_next
    output = x
    gm = cotangent[0]
    gx = gm.astype(f32)
    gprev = jnp.zeros((16, count), f32)
    grads = [None] * LAYERS
    for l in reversed(range(LAYERS)):
        x, n1s, qkv, o, lse, ob, hst, w, wo, ubf, table = kept[l]
        number = 2 * LAYERS + 2 * l
        ghst, go, gwo, small, gprev = ffn_backward(
            l, gm, gx, ubf, table, hst, smalls[l], routes_t[l], gprev, wo, ob, w_gate_up, w_down, number
        )
        if l == 1:
            go, ext_all[0] = lax.optimization_barrier((go, ext_all[0]))
        gx, gm, grads[l] = attn_backward(
            order, inv, n1s, w, cosine, sine, qkv, o, lse, go, ghst, x, smalls[l], small, gwo, number + 1
        )
        if l > 0:
            gm_all[l - 1] = gm

    dense = jnp.stack(grads)
    dense, gm = lax.optimization_barrier((dense, gm_all[0]))
    gm_all[0] = lax.all_gather(gm, everyone, axis=0, tiled=False)

    def partner(values, distance):
        return lax.ppermute(values, "ctx", [(i, i ^ distance) for i in range(ctx_size)])

    def added(first, second):
        return (first.astype(f32) + second.astype(f32)).astype(bf)

    got = partner(dense, 1)
    x1 = dispatch(ext_all[1], ext_all[1], False)
    g1 = dispatch(ext_all[1], gm_all[1], True)
    x1, g1, got = lax.optimization_barrier((x1, g1, got))
    dense = added(dense, got)
    dense, x1 = lax.optimization_barrier((dense, x1))
    got = partner(dense, 4)
    done = weight_grads(1, 0, NF, x1, g1, w_gate_up, w_down, ())
    done, got = lax.optimization_barrier((done, got))
    dense = added(dense, got)
    dense, ext = lax.optimization_barrier((dense, ext_all[0]))
    got = partner(dense, 2)
    x0 = dispatch(ext, ext, False)
    gm, x0 = lax.optimization_barrier((gm_all[0], x0))
    g0 = dispatch(ext, gm, True)
    done = weight_grads(0, 0, NF // 2, x0, g0, w_gate_up, w_down, done)
    done, got = lax.optimization_barrier((done, got))
    qkv, out, small = assemble(dense, got, width)
    done, qkv, out, small = lax.optimization_barrier((done, qkv, out, small))
    done = weight_grads(0, NF // 2, NF, x0, g0, w_gate_up, w_down, done)
    rows = jnp.swapaxes(small[..., : 2 + NC], 1, 2)
    return (
        output[None],
        gx[None],
        rows[:, :2],
        qkv,
        out,
        small[..., 2 + NC : 2 + NC + 16],
        rows[:, 2:],
        done[0],
        done[1],
    )


def solution(mesh):
    placed = (
        P("fsdp", "ctx", None),
        P("fsdp", "ctx", None),
        P("fsdp", None),
        P("fsdp", None),
        P(None, "fsdp", "ctx", None),
        P(None, None, "fsdp"),
        P(None, None, "fsdp", None),
        P(None, "fsdp", None),
        P(None, "fsdp", None),
        P(None, None, "fsdp"),
        P(None, None, None, None, "fsdp"),
        P(None, None, "fsdp", None),
    )
    contexts, packs = mesh.shape["ctx"], mesh.shape["fsdp"]
    blocks_of_heads = HEADS // GROUP_HEADS

    def plan(*args):
        tokens = args[0]
        even = tokens.shape[1] * contexts == 2 * MINLEN
        grouped = contexts == 2 * blocks_of_heads and packs == blocks_of_heads
        return (by_heads if even and grouped else shards)(*args)

    return jax.shard_map(
        plan,
        mesh=mesh,
        in_specs=placed,
        out_specs=(
            P("fsdp", "ctx", None),
            P("fsdp", "ctx", None),
            P(None, None, "fsdp"),
            P(None, None, "fsdp", None),
            P(None, "fsdp", None),
            P(None, "fsdp", None),
            P(None, None, "fsdp"),
            P(None, None, None, None, "fsdp"),
            P(None, None, "fsdp", None),
        ),
        check_vma=False,
    )
```

```python
import functools

import jax
import jax.numpy as jnp
import numpy as np
from jax import lax
from jax.experimental import pallas as pl
from jax.experimental.pallas import tpu as pltpu
from jax.sharding import PartitionSpec as P

HEADS = 12
HEAD_DIM = 64
NF = 8
NC = 2
LAYERS = 2
NE = 12
MOST = 64
GROUP_HEADS = 3


def from_behind(x, axis, by):
    devices = lax.axis_size(axis)
    return lax.ppermute(x, axis, [(i, (i + by) % devices) for i in range(devices)])


def layout_tables(lengths, order_row, tok_count):
    block_len = tok_count // 2
    pack_len = order_row.shape[0] * block_len
    pack_rows = jnp.arange(pack_len, dtype=jnp.int32)
    owner = pack_rows // tok_count
    which_half = pack_rows % tok_count // block_len
    block_ids = order_row[2 * owner + which_half]
    pack_pos = block_ids * block_len + pack_rows % block_len
    segment = (pack_pos >= lengths[0]).astype(jnp.int32)
    seq_pos = pack_pos - segment * lengths[0]
    return (pack_pos, segment, seq_pos)


def angle_tables(seq_pos, head_size):
    half_size = head_size // 2
    frequency = jnp.exp(-jnp.log(10000.0) * jnp.arange(half_size, dtype=jnp.float32) / half_size)
    angles = seq_pos.astype(jnp.float32)[:, None] * frequency[None, :]
    return (jnp.cos(angles)[:, None, :], jnp.sin(angles)[:, None, :])


def rotate_pairs(values, cosine_table, sine_table, direction):
    half_size = values.shape[-1] // 2
    first_half = values[..., :half_size]
    second_half = values[..., half_size:]
    return jnp.concatenate(
        [
            first_half * cosine_table - direction * second_half * sine_table,
            second_half * cosine_table + direction * first_half * sine_table,
        ],
        axis=-1,
    )


def rms_parts(values):
    inverse = lax.rsqrt(jnp.mean(values * values, axis=-1, keepdims=True) + 1e-06)
    return (values * inverse, inverse)


def rms_back(grad_normed, base_values, inverse):
    return inverse * (
        grad_normed - base_values * jnp.mean(grad_normed * base_values, axis=-1, keepdims=True)
    )


def expert_forward(inputs_low, gate_up_use, down_use):
    gate_up_out = jnp.einsum(
        "emd,ecdf->ecmf", inputs_low, gate_up_use, preferred_element_type=jnp.float32
    )
    hidden_low = (jax.nn.silu(gate_up_out[:, 0]) * gate_up_out[:, 1]).astype(jnp.bfloat16)
    partial_value = jnp.einsum(
        "emf,efd->emd", hidden_low, down_use, preferred_element_type=jnp.float32
    )
    return (gate_up_out, hidden_low, partial_value)


def expert_backward(inputs_low, gate_up_out, hidden_low, grad_part_low, gate_up_use, down_use):
    grad_down = jnp.einsum(
        "emf,emd->efd", hidden_low, grad_part_low, preferred_element_type=jnp.float32
    )
    grad_hidden = jnp.einsum(
        "emd,efd->emf", grad_part_low, down_use, preferred_element_type=jnp.float32
    )
    gate_out = gate_up_out[:, 0]
    sigmoid_gate = jax.nn.sigmoid(gate_out)
    grad_pair_low = jnp.stack(
        [
            grad_hidden
            * gate_up_out[:, 1]
            * sigmoid_gate
            * (1.0 + gate_out * (1.0 - sigmoid_gate)),
            grad_hidden * gate_out * sigmoid_gate,
        ],
        axis=1,
    ).astype(jnp.bfloat16)
    grad_gate_up = jnp.einsum(
        "emd,ecmf->ecdf", inputs_low, grad_pair_low, preferred_element_type=jnp.float32
    )
    grad_rows = jnp.einsum(
        "ecmf,ecdf->emd", grad_pair_low, gate_up_use, preferred_element_type=jnp.float32
    )
    return (grad_gate_up, grad_down, grad_rows)


def shards(
    tokens,
    cotangent,
    seq_lengths,
    block_order,
    routes,
    gains,
    qkv_weights,
    out_weight,
    router,
    const_values,
    w_gate_up,
    w_down,
):
    tok_count = tokens.shape[1]
    width = tokens.shape[2]
    ctx_size = lax.axis_size("ctx")
    own_index = lax.axis_index("ctx")
    score_scale = HEAD_DIM ** (-0.5)
    pack_pos, segment, seq_pos = layout_tables(seq_lengths[0], block_order[0], tok_count)
    own_start = own_index * tok_count
    query_pos = lax.dynamic_slice_in_dim(pack_pos, own_start, tok_count)
    query_seg = lax.dynamic_slice_in_dim(segment, own_start, tok_count)
    cosine_table, sine_table = angle_tables(
        lax.dynamic_slice_in_dim(seq_pos, own_start, tok_count), HEAD_DIM
    )
    head_shape = (tok_count, HEADS, HEAD_DIM)
    expert_ids = jnp.arange(NE, dtype=jnp.int32)
    slot_ids = jnp.arange(MOST, dtype=jnp.int32)
    row_ids = jnp.arange(tok_count, dtype=jnp.int32)

    def allowed_pairs(key_offset, key_count):
        key_pos = lax.dynamic_slice_in_dim(pack_pos, key_offset, key_count)
        key_seg = lax.dynamic_slice_in_dim(segment, key_offset, key_count)
        return (query_seg[:, None] == key_seg[None, :]) & (key_pos[None, :] <= query_pos[:, None])

    stream = tokens[0].astype(jnp.float32)
    previous = jnp.zeros((tok_count, NE), jnp.float32)
    saved = []
    for layer_index in range(LAYERS):
        gain_all, qkv_all, out_all, router_all, const_all = (
            lax.all_gather(gains[layer_index], "fsdp", axis=1, tiled=True),
            lax.all_gather(qkv_weights[layer_index], "fsdp", axis=1, tiled=True),
            lax.all_gather(out_weight[layer_index], "fsdp", axis=0, tiled=True),
            lax.all_gather(router[layer_index], "fsdp", axis=0, tiled=True),
            lax.all_gather(const_values[layer_index], "fsdp", axis=1, tiled=True),
        )
        gain_float = gain_all.astype(jnp.float32)
        base_one, inverse_one = rms_parts(stream)
        normed_low = (base_one * gain_float[0]).astype(jnp.bfloat16)
        projected = jnp.einsum(
            "td,cde->cte", normed_low, qkv_all, preferred_element_type=jnp.float32
        )
        queries_low = rotate_pairs(
            projected[0].reshape(head_shape), cosine_table, sine_table, 1.0
        ).astype(jnp.bfloat16)
        keys_low = rotate_pairs(
            projected[1].reshape(head_shape), cosine_table, sine_table, 1.0
        ).astype(jnp.bfloat16)
        values_low = projected[2].reshape(head_shape).astype(jnp.bfloat16)

        def fold_step(running, shard_piece, offset, queries_use=queries_low):
            keys_piece, values_piece = shard_piece
            allowed = allowed_pairs(offset, keys_piece.shape[0])[None]
            scores = (
                jnp.einsum(
                    "qhd,khd->hqk", queries_use, keys_piece, preferred_element_type=jnp.float32
                )
                * score_scale
            )
            scores = jnp.where(allowed, scores, -1e30)
            top_old, total_old, accumulated = running
            top_new = jnp.maximum(top_old, jnp.max(scores, axis=-1))
            weights = jnp.where(allowed, jnp.exp(scores - top_new[..., None]), 0.0)
            factor = jnp.exp(top_old - top_new)
            accumulated = jnp.einsum(
                "hqk,khd->hqd",
                weights.astype(jnp.bfloat16),
                values_piece,
                preferred_element_type=jnp.float32,
            )
            return (top_new, jnp.sum(weights, axis=-1), accumulated)

        starting = (
            jnp.full((HEADS, tok_count), -1e30, jnp.float32),
            jnp.zeros((HEADS, tok_count), jnp.float32),
            jnp.zeros((HEADS, tok_count, HEAD_DIM), jnp.float32),
        )
        top_value, total_sum, accumulated = fold_step(
            starting,
            (
                lax.all_gather(keys_low, "ctx", axis=0, tiled=True),
                lax.all_gather(values_low, "ctx", axis=0, tiled=True),
            ),
            jnp.int32(0),
        )
        log_total = top_value + jnp.log(total_sum)
        attended = jnp.transpose(accumulated / total_sum[..., None], (1, 0, 2))
        mixed_low = attended.reshape(tok_count, width).astype(jnp.bfloat16)
        hidden_state = stream + jnp.dot(mixed_low, out_all, preferred_element_type=jnp.float32)
        base_two, inverse_two = rms_parts(hidden_state)
        expert_in = base_two * gain_float[1]
        expert_low = expert_in.astype(jnp.bfloat16)
        raw_logits = jnp.dot(expert_low, router_all, preferred_element_type=jnp.float32)
        logits = raw_logits[:, :NE] + previous
        route_ids = routes[layer_index, 0]
        chosen = route_ids[:, :, None] == expert_ids[None, None, :]
        chosen_f = chosen.astype(jnp.float32)
        hit_count = jnp.sum(chosen.astype(jnp.int32), axis=1)
        slot_index = jnp.cumsum(hit_count, axis=0) - 1
        picked = jnp.sum(chosen_f * logits[:, None, :], axis=-1)
        gate_weights = jax.nn.softmax(picked, axis=-1)
        coeffs = jnp.sum(gate_weights[:, :, None] * chosen_f, axis=1)
        slot_table = jnp.zeros((NF, MOST), jnp.int32)
        for expert in range(NF):
            target = jnp.where(hit_count[:, expert] > 0, slot_index[:, expert], MOST)
            slot_table = slot_table.at[expert, target].set(row_ids, mode="drop")
        filled = (slot_ids[None, :] < jnp.sum(hit_count[:, :NF], axis=0)[:, None]).astype(
            jnp.float32
        )
        rows_low = expert_low[slot_table]
        inputs_low = lax.all_gather(rows_low, "fsdp", axis=1, tiled=True)
        gate_up_out, hidden_low, partial_value = expert_forward(
            inputs_low, w_gate_up[layer_index], w_down[layer_index]
        )
        result = lax.psum_scatter(
            partial_value.astype(jnp.bfloat16), "fsdp", scatter_dimension=1, tiled=True
        ).astype(jnp.float32)
        flat_index = jnp.arange(NF, dtype=jnp.int32)[None, :] * MOST + jnp.clip(
            slot_index[:, :NF], 0, MOST - 1
        )
        token_result = result.reshape(NF * MOST, width)[flat_index]
        expert_mix = (
            jnp.sum(coeffs[:, :NF, None] * token_result, axis=1)
            + coeffs[:, NF + 1 : NF + 2] * expert_in
        )
        mixings = []
        for const_index in range(NC):
            column = NE + 2 * const_index
            mixing = jax.nn.softmax(raw_logits[:, column : column + 2], axis=-1)
            mixings.append(mixing)
            expert_mix = expert_mix + coeffs[:, NF + 2 + const_index : NF + 3 + const_index] * (
                mixing[:, 0:1] * expert_in
                + mixing[:, 1:2] * const_all[const_index].astype(jnp.float32)[None, :]
            )
        saved.append(
            (
                gain_float,
                qkv_all,
                out_all,
                router_all,
                const_all,
                base_one,
                inverse_one,
                normed_low,
                queries_low,
                keys_low,
                values_low,
                log_total,
                attended,
                mixed_low,
                base_two,
                inverse_two,
                expert_in,
                expert_low,
                chosen_f,
                hit_count,
                gate_weights,
                coeffs,
                slot_table,
                filled,
                inputs_low,
                gate_up_out,
                hidden_low,
                flat_index,
                token_result,
                mixings,
            )
        )
        stream = hidden_state + expert_mix
        previous = logits
    grad_stream = cotangent[0].astype(jnp.float32)
    grad_previous = jnp.zeros((tok_count, NE), jnp.float32)
    layer_grads = [None] * LAYERS
    for layer_index in reversed(range(LAYERS)):
        (
            gain_float,
            qkv_all,
            out_all,
            router_all,
            const_all,
            base_one,
            inverse_one,
            normed_low,
            queries_low,
            keys_low,
            values_low,
            log_total,
            attended,
            mixed_low,
            base_two,
            inverse_two,
            expert_in,
            expert_low,
            chosen_f,
            hit_count,
            gate_weights,
            coeffs,
            slot_table,
            filled,
            inputs_low,
            gate_up_out,
            hidden_low,
            flat_index,
            token_result,
            mixings,
        ) = saved[layer_index]
        grad_mix = grad_stream
        dot_input = jnp.sum(grad_mix * expert_in, axis=-1, keepdims=True)
        coef_grads = [
            jnp.sum(grad_mix[:, None, :] * token_result, axis=-1),
            jnp.zeros((tok_count, 1), jnp.float32),
            dot_input,
        ]
        grad_in = grad_mix * coeffs[:, NF + 1 : NF + 2]
        const_cols = []
        const_grads = []
        for const_index in range(NC):
            mixing = mixings[const_index]
            const_row = const_all[const_index].astype(jnp.float32)[None, :]
            dot_const = jnp.sum(grad_mix * const_row, axis=-1, keepdims=True)
            share = coeffs[:, NF + 2 + const_index : NF + 3 + const_index]
            coef_grads.append(mixing[:, 0:1] * dot_input + mixing[:, 1:2] * dot_const)
            grad_in = grad_in + grad_mix * (share * mixing[:, 0:1])
            grad_mixing = share * jnp.concatenate([dot_input, dot_const], axis=1)
            const_cols.append(
                mixing * (grad_mixing - jnp.sum(mixing * grad_mixing, axis=-1, keepdims=True))
            )
            const_grads.append(jnp.sum(grad_mix * (share * mixing[:, 1:2]), axis=0))
        grad_coeffs = jnp.concatenate(coef_grads, axis=1)
        grad_gates = jnp.sum(chosen_f * grad_coeffs[:, None, :], axis=-1)
        grad_picked = gate_weights * (
            grad_gates - jnp.sum(gate_weights * grad_gates, axis=-1, keepdims=True)
        )
        grad_logits = jnp.sum(grad_picked[:, :, None] * chosen_f, axis=1) + grad_previous
        grad_previous = grad_logits
        grad_raw_low = jnp.concatenate([grad_logits] + const_cols, axis=1).astype(jnp.bfloat16)
        grad_router = jnp.einsum(
            "td,tc->dc", expert_low, grad_raw_low, preferred_element_type=jnp.float32
        )
        grad_in = grad_in + jnp.einsum(
            "tc,dc->td", grad_raw_low, router_all, preferred_element_type=jnp.float32
        )
        slot_weight = (
            jnp.take_along_axis(jnp.transpose(coeffs[:, :NF]), slot_table, axis=1) * filled
        )
        grad_result_low = (grad_mix[slot_table] * slot_weight[:, :, None]).astype(jnp.bfloat16)
        grad_part_low = lax.all_gather(grad_result_low, "fsdp", axis=1, tiled=True)
        grad_gate_up, grad_down, grad_rows = expert_backward(
            inputs_low,
            gate_up_out,
            hidden_low,
            grad_part_low,
            w_gate_up[layer_index],
            w_down[layer_index],
        )
        grad_rows = lax.psum_scatter(
            grad_rows.astype(jnp.bfloat16), "fsdp", scatter_dimension=1, tiled=True
        ).astype(jnp.float32)
        token_grads = grad_rows.reshape(NF * MOST, width)[flat_index]
        grad_in = grad_in + jnp.sum(
            jnp.where(hit_count[:, :NF, None] > 0, token_grads, 0.0), axis=1
        )
        grad_gain_two = jnp.sum(grad_in * base_two, axis=0)
        grad_hidden_state = grad_stream + rms_back(grad_in * gain_float[1], base_two, inverse_two)
        grad_out_low = grad_hidden_state.astype(jnp.bfloat16)
        grad_out_w = jnp.einsum(
            "td,te->de", mixed_low, grad_out_low, preferred_element_type=jnp.float32
        )
        grad_attended = (
            jnp.einsum("te,de->td", grad_out_low, out_all, preferred_element_type=jnp.float32)
            .astype(jnp.bfloat16)
            .reshape(head_shape)
        )
        delta = jnp.transpose(jnp.sum(grad_attended.astype(jnp.float32) * attended, axis=-1))

        def visit(
            turn_index,
            carried,
            queries_use=queries_low,
            grad_use=grad_attended,
            log_use=log_total,
            delta_use=delta,
        ):
            keys_piece, values_piece, key_grads, value_grads, query_grads = carried
            source = (own_index - turn_index) % ctx_size
            allowed = allowed_pairs(source * tok_count, tok_count)[None]
            scores = (
                jnp.einsum(
                    "qhd,khd->hqk", queries_use, keys_piece, preferred_element_type=jnp.float32
                )
                * score_scale
            )
            probs = jnp.where(
                allowed, jnp.exp(jnp.where(allowed, scores, -1e30) - log_use[..., None]), 0.0
            )
            value_grads = value_grads + jnp.einsum(
                "hqk,qhd->khd",
                probs.astype(jnp.bfloat16),
                grad_use,
                preferred_element_type=jnp.float32,
            )
            prob_grads = jnp.einsum(
                "qhd,khd->hqk", grad_use, values_piece, preferred_element_type=jnp.float32
            )
            score_grads = (probs * (prob_grads - delta_use[..., None])).astype(jnp.bfloat16)
            query_grads = query_grads + jnp.einsum(
                "hqk,khd->qhd", score_grads, keys_piece, preferred_element_type=jnp.float32
            )
            key_grads = key_grads + jnp.einsum(
                "hqk,qhd->khd", score_grads, queries_use, preferred_element_type=jnp.float32
            )
            keys_piece, values_piece = from_behind((keys_piece, values_piece), "ctx", 1)
            key_grads, value_grads = (
                from_behind(key_grads.astype(jnp.bfloat16), "ctx", 1).astype(key_grads.dtype),
                from_behind(value_grads.astype(jnp.bfloat16), "ctx", 1).astype(value_grads.dtype),
            )
            return (keys_piece, values_piece, key_grads, value_grads, query_grads)

        zero_heads = jnp.zeros(head_shape, jnp.float32)
        finished = lax.fori_loop(
            0, ctx_size, visit, (keys_low, values_low, zero_heads, zero_heads, zero_heads)
        )
        grad_query = (
            rotate_pairs(finished[4] * score_scale, cosine_table, sine_table, -1.0)
            .astype(jnp.bfloat16)
            .reshape(tok_count, width)
        )
        grad_key = (
            rotate_pairs(finished[2] * score_scale, cosine_table, sine_table, -1.0)
            .astype(jnp.bfloat16)
            .reshape(tok_count, width)
        )
        grad_value = finished[3].astype(jnp.bfloat16).reshape(tok_count, width)
        grad_proj_low = jnp.stack([grad_query, grad_key, grad_value], axis=0)
        grad_qkv = jnp.einsum(
            "td,cte->cde", normed_low, grad_proj_low, preferred_element_type=jnp.float32
        )
        grad_normed = jnp.einsum(
            "cte,cde->td", grad_proj_low, qkv_all, preferred_element_type=jnp.float32
        )
        grad_gain_one = jnp.sum(grad_normed * base_one, axis=0)
        grad_stream = grad_hidden_state + rms_back(
            grad_normed * gain_float[0], base_one, inverse_one
        )
        gains_shard, qkv_shard, out_shard, router_shard, const_shard = (
            lax.psum_scatter(
                jnp.stack([grad_gain_one, grad_gain_two]).astype(jnp.bfloat16),
                "fsdp",
                scatter_dimension=1,
                tiled=True,
            ).astype(jnp.float32),
            lax.psum_scatter(
                grad_qkv.astype(jnp.bfloat16), "fsdp", scatter_dimension=1, tiled=True
            ).astype(jnp.float32),
            lax.psum_scatter(
                grad_out_w.astype(jnp.bfloat16), "fsdp", scatter_dimension=0, tiled=True
            ).astype(jnp.float32),
            lax.psum_scatter(
                grad_router.astype(jnp.bfloat16), "fsdp", scatter_dimension=0, tiled=True
            ).astype(jnp.float32),
            lax.psum_scatter(
                jnp.stack(const_grads).astype(jnp.bfloat16), "fsdp", scatter_dimension=1, tiled=True
            ).astype(jnp.float32),
        )
        layer_grads[layer_index] = (
            lax.psum(gains_shard.astype(jnp.bfloat16), "ctx").astype(jnp.float32),
            lax.psum(qkv_shard.astype(jnp.bfloat16), "ctx").astype(jnp.float32),
            lax.psum(out_shard.astype(jnp.bfloat16), "ctx").astype(jnp.float32),
            lax.psum(router_shard.astype(jnp.bfloat16), "ctx").astype(jnp.float32),
            lax.psum(const_shard.astype(jnp.bfloat16), "ctx").astype(jnp.float32),
            lax.psum(grad_gate_up.astype(jnp.bfloat16), "ctx").astype(jnp.float32),
            lax.psum(grad_down.astype(jnp.bfloat16), "ctx").astype(jnp.float32),
        )
    stacked = [
        jnp.stack([layer_grads[layer_index][member_index] for layer_index in range(LAYERS)])
        for member_index in range(7)
    ]
    return (
        stream[None],
        grad_stream[None],
        stacked[0],
        stacked[1],
        stacked[2],
        stacked[3],
        stacked[4],
        stacked[5],
        stacked[6],
    )


MINLEN = 1024
ROUT = 56
RAW, COEF, SLOT, LOGI = 0, 16, 32, 40
VMEM_MB = 60
BRIEF = pl.CostEstimate(flops=1, bytes_accessed=1, transcendentals=0)


def nt(a, b):
    return lax.dot_general(a, b, (((1,), (1,)), ((), ())), preferred_element_type=jnp.float32)


def nn(a, b):
    return lax.dot_general(a, b, (((1,), (0,)), ((), ())), preferred_element_type=jnp.float32)


def tn(a, b):
    return lax.dot_general(a, b, (((0,), (0,)), ((), ())), preferred_element_type=jnp.float32)


def params_of(mb=VMEM_MB, **more):
    return pltpu.CompilerParams(vmem_limit_bytes=mb * 2**20, **more)


def shape_of(dims, kind):
    return jax.ShapeDtypeStruct(dims, kind)


def rms_factor(values):
    return lax.rsqrt(jnp.mean(values * values, axis=-1, keepdims=True) + 1e-06)


def to_rows(columns, count):
    lane = lax.broadcasted_iota(jnp.int32, (columns[0].shape[0], 128), 1)
    packed = jnp.zeros(lane.shape, jnp.float32)
    for index, column in enumerate(columns):
        packed = jnp.where(lane == index, column, packed)
    return jnp.transpose(packed)[:count]


def to_columns(rows):
    count = rows[0].shape[1]
    sub = lax.broadcasted_iota(jnp.int32, (128, count), 0)
    packed = jnp.zeros(sub.shape, jnp.float32)
    for index, row in enumerate(rows):
        packed = jnp.where(sub == index, row, packed)
    packed = jnp.transpose(packed)
    return [packed[:, index : index + 1] for index in range(len(rows))]


def swap_halves(values):
    lanes = values.shape[1]
    lane = lax.broadcasted_iota(jnp.int32, values.shape, 1)
    ahead = pltpu.roll(values, lanes - 32, 1)
    behind = pltpu.roll(values, 32, 1)
    return jnp.where(lane % 64 < 32, ahead, behind)


def spin(values, cosine, sine):
    return values * cosine + swap_halves(values) * sine


def place():
    own, pack = lax.axis_index("ctx"), lax.axis_index("fsdp")
    return own // 2, own % 2, pack // 2, pack % 2


def remote(src, dst, send, recv, ctx, fsdp):
    return pltpu.make_async_remote_copy(
        src_ref=src,
        dst_ref=dst,
        send_sem=send,
        recv_sem=recv,
        device_id=(ctx, fsdp),
        device_id_type=pl.DeviceIdType.MESH,
    )


def greet_plane(contexts, across=False):
    own = lax.axis_index("ctx")
    _, _, y, k = place()
    barrier = pltpu.get_barrier_semaphore()
    if across:
        for core in (k, 1 - k):
            device = (own, 2 * (1 - y) + core)
            pl.semaphore_signal(barrier, inc=1, device_id=device, device_id_type=pl.DeviceIdType.MESH)
    for ctx in range(contexts):
        for core in range(2):

            @pl.when(jnp.logical_or(ctx != own, core != k))
            def _():
                pl.semaphore_signal(barrier, inc=1, device_id=(ctx, 2 * y + core), device_id_type=pl.DeviceIdType.MESH)

    return barrier, 2 * contexts - 1 + (2 if across else 0)


def greet_packs():
    own = lax.axis_index("ctx")
    _, _, y, k = place()
    barrier = pltpu.get_barrier_semaphore()
    for fsdp in (2 * y + 1 - k, 2 * (1 - y) + k, 2 * (1 - y) + 1 - k):
        pl.semaphore_signal(barrier, inc=1, device_id=(own, fsdp), device_id_type=pl.DeviceIdType.MESH)
    return barrier, 3


def attn_fwd_kernel(
    order, inv, x, small, wq, cosine, sine, wo_own,
    n1s, qkv, o, lse, ob, hst, ub, w, wo,
    n1own, n1r, osort, osend, orecv, cols, w_s, wo_s,
    n_send, n_recv, f_send, f_recv, o_send, o_recv, w_send, w_recv, v_send, v_recv,
):
    blocks, blk, _ = n1r.shape
    lanes = o.shape[1]
    seq = blocks * blk
    step = 2 * blk
    own = lax.axis_index("ctx")
    z, xx, y, k = place()
    depth = blocks // 2
    same = xx == k
    pack = lax.axis_index("fsdp")
    inner = wo_own.shape[1]
    beside, over, corner = 2 * y + 1 - k, 2 * (1 - y) + k, 2 * (1 - y) + 1 - k

    barrier, others = greet_plane(blocks, across=True)
    n1 = norm_low(x[...], small[0:1, :].astype(jnp.float32))
    n1own[0] = n1[:blk]
    n1own[1] = n1[blk:]
    pl.semaphore_wait(barrier, others)

    def n1_copy(zz):
        return remote(n1own.at[zz // 2], n1r.at[own], n_send.at[zz], n_recv.at[z], 2 * zz + k, 2 * y + xx)

    for zz in range(depth):
        alone = jnp.logical_and(same, zz == z)

        @pl.when(jnp.logical_not(alone))
        def _():
            n1_copy(zz).start()

        @pl.when(alone)
        def _():
            n1r[own] = n1own[zz // 2]

    for half in range(2):

        @pl.when(z % 2 == half)
        def _():
            for core in range(2):
                first = (2 * half + core) * inner
                for c in range(3):
                    cols[core, :, c * lanes : c * lanes + inner] = wq[0, c, :, first : first + inner]
                    cols[core, :, c * lanes + inner : (c + 1) * lanes] = jnp.zeros((inner, lanes - inner), jnp.bfloat16)

    def rows_of(device):
        return pl.ds(pl.multiple_of(device * inner, inner), inner)

    def w_copy(index):
        device, core = ((beside, 1 - k), (over, k), (corner, 1 - k))[index]
        return remote(cols.at[core], w_s.at[rows_of(pack), :], w_send.at[index], w_recv.at[index], own, device)

    def w_wait(index):
        rows = w_s.at[rows_of((beside, over, corner)[index]), :]
        remote(cols.at[0], rows, w_send.at[index], w_recv.at[index], own, beside).wait_recv()

    w_s[rows_of(pack), :] = cols[k]
    wo_s[pack] = wo_own[0]
    for index in (1, 2, 0):
        w_copy(index).start()
    v_far = remote(wo_s.at[pack], wo_s.at[pack], v_send.at[0], v_recv.at[0], own, over)
    v_near = remote(wo_s.at[pack], wo_s.at[pack], v_send.at[1], v_recv.at[1], own, beside)
    v_on = remote(wo_s.at[over], wo_s.at[over], v_send.at[2], v_recv.at[2], own, beside)
    v_far.start()
    v_near.start()

    def forward_copy(zz):
        slot = n1r.at[2 * zz + k]
        return remote(slot, slot, f_send.at[zz], f_recv.at[zz], own, 2 * y + 1 - k)

    for zz in range(depth):

        @pl.when(jnp.logical_not(jnp.logical_and(same, zz == z)))
        def _():
            remote(n1own.at[0], n1r.at[2 * zz + k], n_send.at[zz], n_recv.at[zz], 2 * zz + k, 2 * y + xx).wait_recv()

        forward_copy(zz).start()
    for zz in range(depth):
        slot = n1r.at[2 * zz + 1 - k]
        remote(slot, slot, f_send.at[zz], f_recv.at[zz], own, 2 * y + 1 - k).wait_recv()

    for index in range(3):
        w_wait(index)
    w[...] = w_s[...]
    for b in range(blocks):
        n1s[b * blk : (b + 1) * blk, :] = n1r[inv[b]]
    for i in range(seq // step):
        part = slice(i * step, (i + 1) * step)
        out = nn(n1s[part, :], w_s[...])
        cos2 = jnp.concatenate([cosine[part, :]] * (lanes // 128), axis=1)
        sin2 = jnp.concatenate([sine[part, :]] * (lanes // 128), axis=1)
        q = spin(out[:, :lanes], cos2, sin2).astype(jnp.bfloat16)
        qkv[part, :lanes] = q * jnp.asarray(HEAD_DIM**-0.5, jnp.bfloat16)
        qkv[part, lanes : 2 * lanes] = spin(out[:, lanes : 2 * lanes], cos2, sin2).astype(jnp.bfloat16)
        qkv[part, 2 * lanes :] = out[:, 2 * lanes :].astype(jnp.bfloat16)
    lane = lax.broadcasted_iota(jnp.int32, (step, 128), 1)
    for i in range(seq // step):
        part = slice(i * step, (i + 1) * step)
        span = (i + 1) * step
        seen = lax.broadcasted_iota(jnp.int32, (step, span), 1) <= (
            lax.broadcasted_iota(jnp.int32, (step, span), 0) + i * step
        )
        logs = jnp.zeros((step, 128), jnp.float32)
        for head in range(GROUP_HEADS):
            tile, side = head // 2, head % 2
            at = tile * 128
            mine = lane // 64 == side
            q = jnp.where(mine, qkv[part, at : at + 128], jnp.asarray(0, jnp.bfloat16))
            s = nt(q, qkv[:span, lanes + at : lanes + at + 128])
            s = jnp.where(seen, s, -1e30)
            top = jnp.max(s, axis=1, keepdims=True)
            p = jnp.exp(s - top)
            total = jnp.sum(p, axis=1, keepdims=True)
            out = nn(p.astype(jnp.bfloat16), qkv[:span, 2 * lanes + at : 2 * lanes + at + 128]) / total
            logs = jnp.where(lane == head, top + jnp.log(total), logs)
            if side == 0:
                kept = jnp.where(mine, out, 0.0)
            else:
                kept = jnp.where(mine, out, kept)
            o[part, at : at + 128] = kept
        lse[part, :] = logs
        osort[2 * i] = o[part, :][:blk].astype(jnp.bfloat16)
        osort[2 * i + 1] = o[part, :][blk:].astype(jnp.bfloat16)

    mine_at = 2 * z + k
    remote(wo_s.at[over], wo_s.at[over], v_send.at[0], v_recv.at[0], own, over).wait_recv()
    v_on.start()

    def o_copy(ctx):
        return remote(osend.at[ctx], orecv.at[mine_at], o_send.at[ctx], o_recv.at[mine_at], ctx, 2 * y + xx)

    for ctx in range(blocks):
        alone = jnp.logical_and(same, ctx == own)
        osend[ctx] = osort[order[ctx]]

        @pl.when(jnp.logical_not(alone))
        def _():
            o_copy(ctx).start()

        @pl.when(alone)
        def _():
            orecv[mine_at] = osend[ctx]

    for src in range(blocks):

        @pl.when(jnp.logical_not(jnp.logical_and(same, src == mine_at)))
        def _():
            remote(osend.at[0], orecv.at[src], o_send.at[0], o_recv.at[src], 2 * (src // 2) + k, 2 * y + src % 2).wait_recv()

    ob[...] = orecv[...]
    remote(wo_s.at[beside], wo_s.at[beside], v_send.at[1], v_recv.at[1], own, beside).wait_recv()
    remote(wo_s.at[corner], wo_s.at[corner], v_send.at[2], v_recv.at[2], own, beside).wait_recv()
    wo[...] = wo_s[...]
    total, low = post_attention(orecv[...], x[...], wo_s[...], small[1:2, :].astype(jnp.float32))
    hst[...] = total
    ub[...] = low
    for zz in range(depth):

        @pl.when(jnp.logical_not(jnp.logical_and(same, zz == z)))
        def _():
            n1_copy(zz).wait_send()

        forward_copy(zz).wait_send()
    for index in range(3):
        w_copy(index).wait_send()
    v_far.wait_send()
    v_near.wait_send()
    v_on.wait_send()
    for ctx in range(blocks):

        @pl.when(jnp.logical_not(jnp.logical_and(same, ctx == own)))
        def _():
            o_copy(ctx).wait_send()


def attn_forward(layer, order, inv, x, small, wq, cosine, sine, wo, number):
    count, width = x.shape
    blocks, blk = order.shape[0], count // 2
    packs, inner = width // wo.shape[1], wo.shape[1]
    lanes = -(-inner // 128) * 128
    seq = blocks * blk
    vm = pl.BlockSpec(memory_space=pltpu.VMEM)
    sm = pl.BlockSpec(memory_space=pltpu.SMEM)
    bf = jnp.bfloat16
    dma = pltpu.SemaphoreType.DMA
    return pl.pallas_call(
        attn_fwd_kernel,
        grid=(1,),
        out_shape=[
            shape_of((seq, width), bf),
            shape_of((seq, 3 * lanes), bf),
            shape_of((seq, lanes), jnp.float32),
            shape_of((seq, 128), jnp.float32),
            shape_of((blocks, blk, lanes), bf),
            shape_of((count, width), jnp.float32),
            shape_of((count, width), bf),
            shape_of((width, 3 * lanes), bf),
            shape_of((packs, inner, width), bf),
        ],
        in_specs=[sm, sm, vm, vm]
        + [pl.BlockSpec((1, 3, inner, width), lambda _: (layer, 0, 0, 0)), vm, vm]
        + [pl.BlockSpec((1, inner, width), lambda _: (layer, 0, 0))],
        out_specs=[vm] * 9,
        scratch_shapes=[
            pltpu.VMEM((2, blk, width), bf),
            pltpu.VMEM((blocks, blk, width), bf),
            pltpu.VMEM((blocks, blk, lanes), bf),
            pltpu.VMEM((blocks, blk, lanes), bf),
            pltpu.VMEM((blocks, blk, lanes), bf),
            pltpu.VMEM((2, inner, 3 * lanes), bf),
            pltpu.VMEM((width, 3 * lanes), bf),
            pltpu.VMEM((packs, inner, width), bf),
        ]
        + [dma((blocks // 2,))] * 4
        + [dma((blocks,))] * 2
        + [dma((3,))] * 4,
        compiler_params=params_of(collective_id=number, has_side_effects=True),
        cost_estimate=BRIEF,
        name="attn_fwd",
    )(order, inv, x, small, wq, cosine, sine, wo)


def attn_bwd_kernel(
    order, inv, n1s, w, cosine, sine, qkv, o, lse, go, ghst, x, small, gsmall, gwo,
    gx, gm, dense,
    gor, gos, grads, acc, gns, sib_out, sib_in, gn_out, gnr, gw, gw_in, both, both_in, wo_in, wo_both, wo_over,
    o_send, o_recv, s_send, s_recv, g_send, g_recv, r_send, r_recv, w_send, w_recv,
):
    blocks, blk, width = grads.shape
    lanes = o.shape[1]
    seq = blocks * blk
    step = 2 * blk
    zero = jnp.asarray(0, jnp.bfloat16)
    own = lax.axis_index("ctx")
    z, xx, y, k = place()
    depth = blocks // 2
    same = xx == k

    barrier, others = greet_plane(blocks, across=True)
    acc[...] = jnp.zeros_like(acc)
    pl.semaphore_wait(barrier, others)

    def go_copy(unit):
        return remote(go.at[unit], gor.at[own], o_send.at[unit], o_recv.at[own], 2 * (unit // 2) + k, 2 * y + unit % 2)

    for unit in range(blocks):
        alone = jnp.logical_and(same, unit == 2 * z + k)

        @pl.when(jnp.logical_not(alone))
        def _():
            go_copy(unit).start()

        @pl.when(alone)
        def _():
            gor[own] = go[unit]

    def wo_copy(half):
        return remote(
            gwo.at[2 * half + 1 - k], wo_in.at[half], w_send.at[half], w_recv.at[half], own, 2 * y + 1 - k
        )

    wo_far = remote(wo_both.at[1 - y], wo_over, w_send.at[2], w_recv.at[2], own, 2 * (1 - y) + k)
    wo_copy(0).start()
    wo_copy(1).start()
    for ctx in range(blocks):

        @pl.when(jnp.logical_not(jnp.logical_and(same, ctx == own)))
        def _():
            remote(go.at[0], gor.at[ctx], o_send.at[0], o_recv.at[ctx], ctx, 2 * y + xx).wait_recv()

    for half in range(2):
        wo_copy(half).wait_recv()
        total = gwo[2 * half + k].astype(jnp.float32) + wo_in[half].astype(jnp.float32)
        wo_both[half] = total.astype(jnp.bfloat16)
    wo_far.start()
    for b in range(blocks):
        gos[b * blk : (b + 1) * blk, :] = gor[inv[b]]
    lane = lax.broadcasted_iota(jnp.int32, (step, 128), 1)
    for i in range(seq // step):
        part = slice(i * step, (i + 1) * step)
        span = (i + 1) * step
        seen = lax.broadcasted_iota(jnp.int32, (step, span), 1) <= (
            lax.broadcasted_iota(jnp.int32, (step, span), 0) + i * step
        )
        key_lane = lax.broadcasted_iota(jnp.int32, (span, 128), 1)
        for head in range(GROUP_HEADS):
            tile, side = head // 2, head % 2
            at = tile * 128
            mine = lane // 64 == side
            q = jnp.where(mine, qkv[part, at : at + 128], zero)
            g = jnp.where(mine, gos[part, at : at + 128], zero)
            keys = qkv[:span, lanes + at : lanes + at + 128]
            values = qkv[:span, 2 * lanes + at : 2 * lanes + at + 128]
            delta = jnp.sum(g.astype(jnp.float32) * o[part, at : at + 128], axis=1, keepdims=True)
            s = nt(q, keys)
            p = jnp.where(seen, jnp.exp(jnp.where(seen, s, -1e30) - lse[part, head : head + 1]), 0.0)
            ds = (p * (nt(g, values) - delta)).astype(jnp.bfloat16)
            acc[:span, 2 * lanes + at : 2 * lanes + at + 128] += tn(p.astype(jnp.bfloat16), g)
            acc[:span, lanes + at : lanes + at + 128] += tn(ds, q)
            acc[part, at : at + 128] += nn(ds, jnp.where(key_lane // 64 == side, keys, zero))
    for b in range(blocks):
        part = slice(b * blk, (b + 1) * blk)
        cos2 = jnp.concatenate([cosine[part, :]] * (lanes // 128), axis=1)
        sin2 = jnp.concatenate([sine[part, :]] * (lanes // 128), axis=1)
        grads[b, :, :lanes] = spin(acc[part, :lanes] * HEAD_DIM**-0.5, cos2, -sin2).astype(jnp.bfloat16)
        grads[b, :, lanes : 2 * lanes] = spin(acc[part, lanes : 2 * lanes], cos2, -sin2).astype(jnp.bfloat16)
        grads[b, :, 2 * lanes :] = acc[part, 2 * lanes :].astype(jnp.bfloat16)

    def sib_copy(zz):
        return remote(sib_out.at[zz], sib_in.at[zz], s_send.at[zz], s_recv.at[zz], own, 2 * y + 1 - k)

    def gn_copy(zz):
        return remote(gn_out.at[zz], gnr.at[z], g_send.at[zz], g_recv.at[z], 2 * zz + k, 2 * y + xx)

    gain = small[0:1, :].astype(jnp.float32)
    ggain = jnp.zeros((1, width), jnp.float32)
    for b in range(blocks):
        gns[b] = nt(grads[b], w[...])
        ggain = ggain + jnp.sum(gns[b] * n1s[b * blk : (b + 1) * blk, :].astype(jnp.float32), axis=0, keepdims=True)
    for zz in range(depth):
        sib_out[zz] = gns[order[2 * zz + 1 - k]].astype(jnp.bfloat16)
        sib_copy(zz).start()
    for zz in range(depth):
        sib_copy(zz).wait_recv()
        alone = jnp.logical_and(same, zz == z)
        gn_out[zz] = (gns[order[2 * zz + k]] + sib_in[zz].astype(jnp.float32)).astype(jnp.bfloat16)

        @pl.when(jnp.logical_not(alone))
        def _():
            gn_copy(zz).start()

        @pl.when(alone)
        def _():
            gnr[z] = gn_out[zz]

    packs, inner = gwo.shape[0], gwo.shape[1]
    sums = jnp.concatenate([ggain / gain, gsmall[...]], axis=0)
    sums = jnp.concatenate([sums, jnp.zeros((128 - sums.shape[0], width), jnp.float32)], axis=0)
    gw[:, :128] = jnp.transpose(sums).astype(jnp.bfloat16)
    gw[:, 128 + 3 * inner :] = jnp.zeros((width, gw.shape[1] - 128 - 3 * inner), jnp.bfloat16)
    for i in range(width // 256):
        part = slice(i * 256, (i + 1) * 256)
        piece = tn(n1s[:, part], grads[...].reshape(seq, 3 * lanes)).astype(jnp.bfloat16)
        for c in range(3):
            gw[part, 128 + c * inner : 128 + (c + 1) * inner] = piece[:, c * lanes : c * lanes + inner]

    def rows_of(f):
        return pl.ds(pl.multiple_of(f * inner, inner), inner)

    def home_copy(half):
        rows = gw.at[rows_of(2 * half + 1 - k), :]
        return remote(rows, gw_in.at[half], r_send.at[half], r_recv.at[half], own, 2 * y + 1 - k)

    for half in range(2):
        home_copy(half).start()
    for half in range(2):
        home_copy(half).wait_recv()
        kept, came = gw[rows_of(2 * half + k), :], gw_in[half]
        both[half, :, :128] = (kept[:, :128].astype(jnp.float32) + came[:, :128].astype(jnp.float32)).astype(jnp.bfloat16)
        heads = slice(128, 128 + 3 * inner)
        for core in range(2):

            @pl.when(k == core)
            def _():
                both[half, :, 128 + core * 3 * inner : 128 + (core + 1) * 3 * inner] = kept[:, heads]
                both[half, :, 128 + (1 - core) * 3 * inner : 128 + (2 - core) * 3 * inner] = came[:, heads]

    over = remote(both.at[1 - y], both_in, r_send.at[2], r_recv.at[2], own, 2 * (1 - y) + k)
    over.start()
    for zz in range(depth):

        @pl.when(jnp.logical_not(jnp.logical_and(same, zz == z)))
        def _():
            remote(gn_out.at[0], gnr.at[zz], g_send.at[0], g_recv.at[zz], 2 * zz + k, 2 * y + xx).wait_recv()

    halves = []
    for h in range(2):
        total = gnr[h * (depth // 2)].astype(jnp.float32)
        for zz in range(1, depth // 2):
            total = total + gnr[h * (depth // 2) + zz].astype(jnp.float32)
        halves.append(total)
    gn = jnp.concatenate(halves, axis=0)
    values = x[...]
    factor = rms_factor(values)
    base = values * factor
    gb = gn * gain
    grad = ghst[...] + factor * (gb - base * jnp.mean(gb * base, axis=-1, keepdims=True))
    gx[...] = grad
    gm[...] = grad.astype(jnp.bfloat16)
    wo_far.wait_recv()
    edge = both.shape[2]
    dense[:, edge:] = (wo_both[y].astype(jnp.float32) + wo_over[...].astype(jnp.float32)).astype(jnp.bfloat16)
    over.wait_recv()
    dense[:, :edge] = (both[y].astype(jnp.float32) + both_in[...].astype(jnp.float32)).astype(jnp.bfloat16)
    for half in range(2):
        home_copy(half).wait_send()
        wo_copy(half).wait_send()
    wo_far.wait_send()
    over.wait_send()
    for unit in range(blocks):

        @pl.when(jnp.logical_not(jnp.logical_and(same, unit == 2 * z + k)))
        def _():
            go_copy(unit).wait_send()

    for zz in range(depth):
        sib_copy(zz).wait_send()

        @pl.when(jnp.logical_not(jnp.logical_and(same, zz == z)))
        def _():
            gn_copy(zz).wait_send()


def attn_backward(order, inv, n1s, w, cosine, sine, qkv, o, lse, go, ghst, x, small, gsmall, gwo, number):
    blocks, blk, lanes = go.shape
    seq, width = n1s.shape
    count = x.shape[0]
    packs, inner = gwo.shape[0], gwo.shape[1]
    depth = blocks // 2
    vm = pl.BlockSpec(memory_space=pltpu.VMEM)
    sm = pl.BlockSpec(memory_space=pltpu.SMEM)
    bf = jnp.bfloat16
    dma = pltpu.SemaphoreType.DMA
    return pl.pallas_call(
        attn_bwd_kernel,
        out_shape=[
            shape_of((count, width), jnp.float32),
            shape_of((count, width), bf),
            shape_of((inner, 128 + 6 * inner + width), bf),
        ],
        in_specs=[sm] * 2 + [vm] * 13,
        out_specs=[vm] * 3,
        scratch_shapes=[
            pltpu.VMEM((blocks, blk, lanes), bf),
            pltpu.VMEM((seq, lanes), bf),
            pltpu.VMEM((blocks, blk, 3 * lanes), bf),
            pltpu.VMEM((seq, 3 * lanes), jnp.float32),
            pltpu.VMEM((blocks, blk, width), jnp.float32),
            pltpu.VMEM((depth, blk, width), bf),
            pltpu.VMEM((depth, blk, width), bf),
            pltpu.VMEM((depth, blk, width), bf),
            pltpu.VMEM((depth, blk, width), bf),
            pltpu.VMEM((packs * inner, 3 * lanes), bf),
            pltpu.VMEM((2, inner, 3 * lanes), bf),
            pltpu.VMEM((2, inner, 128 + 6 * inner), bf),
            pltpu.VMEM((inner, 128 + 6 * inner), bf),
            pltpu.VMEM((2, inner, width), bf),
            pltpu.VMEM((2, inner, width), bf),
            pltpu.VMEM((inner, width), bf),
        ]
        + [dma((blocks,))] * 2
        + [dma((depth,))] * 4
        + [dma((3,))] * 4,
        compiler_params=params_of(collective_id=number, has_side_effects=True),
        cost_estimate=BRIEF,
        name="attn_bwd",
    )(order, inv, n1s, w, cosine, sine, qkv, o, lse, go, ghst, x, small, gsmall, gwo)


def routing(raw, before, routes):
    count = raw.shape[1]
    ids = lax.broadcasted_iota(jnp.int32, (16, count), 0)
    logits = raw + before
    first, second = ids == routes[0:1], ids == routes[1:2]
    z0 = jnp.sum(jnp.where(first, logits, 0.0), axis=0, keepdims=True)
    z1 = jnp.sum(jnp.where(second, logits, 0.0), axis=0, keepdims=True)
    top = jnp.maximum(z0, z1)
    e0, e1 = jnp.exp(z0 - top), jnp.exp(z1 - top)
    total = e0 + e1
    coef = jnp.where(first, e0 / total, 0.0) + jnp.where(second, e1 / total, 0.0)
    hits = jnp.where(first | second, 1.0, 0.0)
    upto = lax.broadcasted_iota(jnp.int32, (count, count), 0) <= lax.broadcasted_iota(jnp.int32, (count, count), 1)
    place = nn(hits.astype(jnp.bfloat16), jnp.where(upto, 1.0, 0.0).astype(jnp.bfloat16)) - 1.0
    slot = jnp.where(hits > 0, place, -1.0)
    return jnp.concatenate([raw, coef, slot[:NF], logits], axis=0)


def one_hot(slot):
    count = slot.shape[1]
    ids = lax.broadcasted_iota(jnp.int32, (NF, MOST, count), 1)
    hit = ids == slot.astype(jnp.int32)[:, None, :]
    return jnp.where(hit, 1.0, 0.0).reshape(NF * MOST, count)


def slot_values(hot, rows):
    count = rows.shape[1]
    wide = jnp.broadcast_to(rows[:, None, :], (NF, MOST, count)).reshape(NF * MOST, count)
    return jnp.sum(hot * wide, axis=1, keepdims=True)


def swap_rows(own, rows, send, recv, forward_send, forward_recv):
    ctx = lax.axis_index("ctx")
    _, _, y, k = place()
    beside, across = 2 * y + 1 - k, 2 * (1 - y) + k
    far = remote(own, rows.at[2], send.at[0], recv.at[0], ctx, across)
    near = remote(own, rows.at[1], send.at[1], recv.at[1], ctx, beside)
    onward = remote(rows.at[2], rows.at[3], forward_send, forward_recv, ctx, beside)
    far.start()
    near.start()
    return near, far, onward


def sum_rows(parts, beside_in, mid, across_in, send, recv):
    ctx = lax.axis_index("ctx")
    _, _, y, k = place()
    beside, across = 2 * y + 1 - k, 2 * (1 - y) + k
    first = remote(parts.at[3], beside_in.at[1], send.at[0], recv.at[0], ctx, beside)
    second = remote(parts.at[1], beside_in.at[0], send.at[1], recv.at[1], ctx, beside)
    third = remote(mid, across_in, send.at[2], recv.at[2], ctx, across)
    return first, second, third


def ffn_fwd_kernel(
    ub, hst, small, routes, before, wgu, wd,
    ubf, table, ext, x_next,
    rows_s, hot_s, x_s, y_s, coef_s, parts, beside_in, mid, across_in,
    a_send, a_recv, r_send, r_recv,
):
    e = pl.program_id(0)
    packs = ubf.shape[0]
    count, width = ub.shape
    router = small[2 + NC :, :]

    def gathers():
        return swap_rows(ub, rows_s, a_send, a_recv, a_send.at[2], a_recv.at[2])

    def sums():
        return sum_rows(parts, beside_in, mid, across_in, r_send, r_recv)

    @pl.when(e == 0)
    def _():
        barrier, others = greet_packs()
        rows_s[0] = ub[...]

        def prepare(d):
            rows = routing(nt(router, rows_s[d]), before[d], routes[d])
            table[d] = rows
            hot = one_hot(rows[SLOT : SLOT + NF])
            coef_s[d] = slot_values(hot, rows[COEF : COEF + NF])
            hot_low = hot.astype(jnp.bfloat16)
            hot_s[d] = hot_low
            x = nn(hot_low, rows_s[d]).astype(jnp.bfloat16)
            for n in range(NF):
                x_s[n, d * MOST : (d + 1) * MOST, :] = x[n * MOST : (n + 1) * MOST]

        pl.semaphore_wait(barrier, others)
        near, far, onward = gathers()
        prepare(0)
        near.wait_recv()
        prepare(1)
        far.wait_recv()
        onward.start()
        prepare(2)
        onward.wait_recv()
        prepare(3)
        ubf[...] = rows_s[...]
        ext[:count, :] = ub[...]
        rows = table[0]
        ext[count:, :] = jnp.zeros((16, width), jnp.bfloat16)
        ext[count:, :count] = rows[COEF : COEF + 16].astype(jnp.bfloat16)
        slots = jnp.concatenate([rows[SLOT : SLOT + NF], jnp.zeros((16 - NF, count), jnp.float32)], axis=0)
        ext[count:, count : 2 * count] = slots.astype(jnp.bfloat16)
        near.wait_send()
        far.wait_send()
        onward.wait_send()

    x = x_s[e]
    gate, up = nn(x, wgu[0, 0, 0]), nn(x, wgu[0, 0, 1])
    hid = (gate * jax.nn.sigmoid(gate) * up).astype(jnp.bfloat16)
    out = nn(hid, wd[0, 0])
    at = pl.ds(pl.multiple_of(e * MOST, MOST), MOST)
    for d in range(packs):
        y_s[d, at, :] = (out[d * MOST : (d + 1) * MOST] * coef_s[d, at, :]).astype(jnp.bfloat16)

    @pl.when(e == NF - 1)
    def _():
        first, second, third = sums()
        parts[3] = tn(hot_s[3], y_s[3]).astype(jnp.bfloat16)
        first.start()
        parts[1] = tn(hot_s[1], y_s[1]).astype(jnp.bfloat16)
        second.start()
        away = tn(hot_s[2], y_s[2])
        first.wait_recv()
        mid[...] = (away + beside_in[1].astype(jnp.float32)).astype(jnp.bfloat16)
        third.start()
        home = tn(hot_s[0], y_s[0])
        _, _, scale_u, scale_c = mixing_rows(table[0])
        columns = to_columns([scale_u] + scale_c)
        values = hst[...]
        moe = home + columns[0] * ((values * rms_factor(values)) * small[1:2, :].astype(jnp.float32))
        for c in range(NC):
            moe = moe + columns[1 + c] * small[2 + c : 3 + c, :].astype(jnp.float32)
        second.wait_recv()
        moe = moe + beside_in[0].astype(jnp.float32)
        third.wait_recv()
        x_next[...] = values + (moe + across_in[...].astype(jnp.float32))
        first.wait_send()
        second.wait_send()
        third.wait_send()


def whole_spec(dims):
    return pl.BlockSpec(dims, lambda *_: (0,) * len(dims))


def exchange_scratch(packs, count, width):
    bf = jnp.bfloat16
    return [
        pltpu.VMEM((packs, count, width), bf),
        pltpu.VMEM((2, count, width), bf),
        pltpu.VMEM((count, width), bf),
        pltpu.VMEM((count, width), bf),
    ]


def ffn_forward(layer, ub, hst, small, routes, before, wgu, wd, number):
    count, width = ub.shape
    packs = routes.shape[0]
    hidden = wd.shape[2]
    bf = jnp.bfloat16
    outs = [
        shape_of((packs, count, width), bf),
        shape_of((packs, ROUT, count), jnp.float32),
        shape_of((count + 16, width), bf),
        shape_of((count, width), jnp.float32),
    ]
    return pl.pallas_call(
        ffn_fwd_kernel,
        grid=(NF,),
        out_shape=outs,
        in_specs=[whole_spec(a.shape) for a in (ub, hst, small, routes, before)]
        + [
            pl.BlockSpec((1, 1, 2, width, hidden), lambda e: (layer, e, 0, 0, 0)),
            pl.BlockSpec((1, 1, hidden, width), lambda e: (layer, e, 0, 0)),
        ],
        out_specs=[whole_spec(a.shape) for a in outs],
        scratch_shapes=[
            pltpu.VMEM((packs, count, width), bf),
            pltpu.VMEM((packs, NF * MOST, count), bf),
            pltpu.VMEM((NF, packs * MOST, width), bf),
            pltpu.VMEM((packs, NF * MOST, width), bf),
            pltpu.VMEM((packs, NF * MOST, 1), jnp.float32),
        ]
        + exchange_scratch(packs, count, width)
        + [pltpu.SemaphoreType.DMA((3,))] * 4,
        compiler_params=params_of(collective_id=number, has_side_effects=True),
        cost_estimate=BRIEF,
        name="ffn_fwd",
    )(ub, hst, small, routes, before, wgu, wd)


def silu_parts(gate, up, ghid):
    sig = jax.nn.sigmoid(gate)
    act = gate * sig
    dg = (ghid * up * sig * (1.0 + gate * (1.0 - sig))).astype(jnp.bfloat16)
    du = (ghid * act).astype(jnp.bfloat16)
    return act * up, dg, du


def ffn_bwd_kernel(
    gm, gx, ubf, table, hst, small, routes, gprev, wo, ob, wgu, wd,
    ghst, go, gwo, gsmall, glog,
    rows_s, hot_s, x_s, g_s, y_s, coef_s, gc_s, gcoef, gcoef_in, parts, beside_in, mid, across_in,
    a_send, a_recv, r_send, r_recv, c_send, c_recv,
):
    e = pl.program_id(0)
    packs = ubf.shape[0]
    ctx = lax.axis_index("ctx")
    _, _, y, k = place()
    peers = [None, 2 * y + 1 - k, 2 * (1 - y) + k, 2 * (1 - y) + 1 - k]

    def gathers():
        return swap_rows(gm, rows_s, a_send, a_recv, a_send.at[2], a_recv.at[2])

    def sums():
        return sum_rows(parts, beside_in, mid, across_in, r_send, r_recv)

    @pl.when(e == 0)
    def _():
        barrier, others = greet_packs()
        rows_s[0] = gm[...]

        def prepare(d):
            hot = one_hot(table[d, SLOT : SLOT + NF, :])
            coef_s[d] = slot_values(hot, table[d, COEF : COEF + NF, :])
            hot_low = hot.astype(jnp.bfloat16)
            hot_s[d] = hot_low
            x = nn(hot_low, ubf[d]).astype(jnp.bfloat16)
            for n in range(NF):
                x_s[n, d * MOST : (d + 1) * MOST, :] = x[n * MOST : (n + 1) * MOST]

        def spread(d):
            g = nn(hot_s[d], rows_s[d]).astype(jnp.bfloat16)
            for n in range(NF):
                g_s[n, d * MOST : (d + 1) * MOST, :] = g[n * MOST : (n + 1) * MOST]

        pl.semaphore_wait(barrier, others)
        near, far, onward = gathers()
        for d in range(packs):
            prepare(d)
        spread(0)
        near.wait_recv()
        far.wait_recv()
        onward.start()
        spread(1)
        spread(2)
        onward.wait_recv()
        spread(3)
        near.wait_send()
        far.wait_send()
        onward.wait_send()

    x = x_s[e]
    at = pl.ds(pl.multiple_of(e * MOST, MOST), MOST)
    coef = jnp.concatenate([coef_s[d, at, :] for d in range(packs)], axis=0)
    gate, up = nn(x, wgu[0, 0, 0]), nn(x, wgu[0, 0, 1])
    ghid = nt(g_s[e], wd[0, 0])
    hid, dg, du = silu_parts(gate, up, ghid * coef)
    dots = jnp.sum(hid * ghid, axis=1, keepdims=True)
    out = nt(dg, wgu[0, 0, 0]) + nt(du, wgu[0, 0, 1])
    for d in range(packs):
        y_s[d, at, :] = out[d * MOST : (d + 1) * MOST].astype(jnp.bfloat16)
        gc_s[d, at, :] = dots[d * MOST : (d + 1) * MOST]

    @pl.when(e == NF - 1)
    def _():
        first, second, third = sums()

        def coef_copy(d):
            return remote(gcoef.at[d], gcoef_in.at[d - 1], c_send.at[d - 1], c_recv.at[d - 1], ctx, peers[d])

        parts[3] = tn(hot_s[3], y_s[3]).astype(jnp.bfloat16)
        first.start()
        parts[1] = tn(hot_s[1], y_s[1]).astype(jnp.bfloat16)
        second.start()
        for d in range(packs):
            wide = hot_s[d].astype(jnp.float32) * gc_s[d]
            gcoef[d] = jnp.sum(wide.reshape(NF, MOST, wide.shape[1]), axis=1)
            if d > 0:
                coef_copy(d).start()
        away = tn(hot_s[2], y_s[2])
        first.wait_recv()
        mid[...] = (away + beside_in[1].astype(jnp.float32)).astype(jnp.bfloat16)
        third.start()
        home = tn(hot_s[0], y_s[0])
        second.wait_recv()
        home = home + beside_in[0].astype(jnp.float32)
        total = gcoef[0]
        for d in range(1, packs):
            coef_copy(d).wait_recv()
            total = total + gcoef_in[d - 1]
        third.wait_recv()
        home = home + across_in[...].astype(jnp.float32)
        results = middle(
            gx[...], home, total, table[0], routes[...], gprev[...], hst[...], ubf[0],
            small[...], wo[...], ob[...],
        )
        for ref, value in zip((ghst, go, gwo, gsmall, glog), results):
            ref[...] = value
        first.wait_send()
        second.wait_send()
        third.wait_send()
        for d in range(1, packs):
            coef_copy(d).wait_send()


def ffn_backward(layer, gm, gx, ubf, table, hst, small, routes, gprev, wo, ob, wgu, wd, number):
    packs, count, width = ubf.shape
    hidden = wd.shape[2]
    bf, f32 = jnp.bfloat16, jnp.float32
    outs = [
        shape_of((count, width), f32),
        shape_of(ob.shape, bf),
        shape_of(wo.shape, bf),
        shape_of((1 + NC + 16, width), f32),
        shape_of((16, count), f32),
    ]
    args = (gm, gx, ubf, table, hst, small, routes, gprev, wo, ob)
    dma = pltpu.SemaphoreType.DMA
    return pl.pallas_call(
        ffn_bwd_kernel,
        grid=(NF,),
        out_shape=outs,
        in_specs=[whole_spec(a.shape) for a in args]
        + [
            pl.BlockSpec((1, 1, 2, width, hidden), lambda e: (layer, e, 0, 0, 0)),
            pl.BlockSpec((1, 1, hidden, width), lambda e: (layer, e, 0, 0)),
        ],
        out_specs=[whole_spec(a.shape) for a in outs],
        scratch_shapes=[
            pltpu.VMEM((packs, count, width), bf),
            pltpu.VMEM((packs, NF * MOST, count), bf),
            pltpu.VMEM((NF, packs * MOST, width), bf),
            pltpu.VMEM((NF, packs * MOST, width), bf),
            pltpu.VMEM((packs, NF * MOST, width), bf),
            pltpu.VMEM((packs, NF * MOST, 1), f32),
            pltpu.VMEM((packs, NF * MOST, 1), f32),
            pltpu.VMEM((packs, NF, count), f32),
            pltpu.VMEM((packs - 1, NF, count), f32),
        ]
        + exchange_scratch(packs, count, width)
        + [dma((3,))] * 6,
        compiler_params=params_of(collective_id=number, has_side_effects=True),
        cost_estimate=BRIEF,
        name="ffn_bwd",
    )(*args, wgu, wd)


PACK = 80


def pack_kernel(counts, bases, totals, tail, ext, gm, out, buf, carry, blank, sems):
    step = pl.program_id(0)
    some, count, width = gm.shape

    @pl.when(step == 0)
    def _():
        carry[...] = jnp.zeros_like(carry)
        blank[...] = jnp.zeros_like(blank)

    def whole_groups(d, e):
        at = d * NF + e
        return (bases[at] % 16 + counts[at]) // 16

    def each_copy(block, what):
        for i in range(some):
            for e in range(NF):
                groups = whole_groups(block * some + i, e)
                start = pl.multiple_of(bases[(block * some + i) * NF + e] // 16 * 16, 16)
                for n in range(1, PACK // 16):

                    @pl.when(groups == n)
                    def _():
                        source = buf.at[block % 2, i, e, pl.ds(0, 16 * n), :]
                        what(pltpu.make_async_copy(source, out.at[e, pl.ds(start, 16 * n), :], sems.at[block % 2, i, e]))

    def begin(copy):
        copy.start()

    def end(copy):
        copy.wait()

    @pl.when(step >= 2)
    def _():
        each_copy(step - 2, end)

    ids = lax.broadcasted_iota(jnp.int32, (PACK, count), 0)
    side = step % 2
    for i in range(some):
        d = step * some + i
        rows = tail[i].astype(jnp.float32)
        slot = rows[:NF, count : 2 * count].astype(jnp.int32)
        slot = jnp.where(slot < 0, -PACK, slot)
        hot, weighted = [], []
        for e in range(NF):
            hit = ids == slot[e : e + 1] + bases[d * NF + e] % 16
            hot.append(jnp.where(hit, 1.0, 0.0).astype(jnp.bfloat16))
            weighted.append(jnp.where(hit, rows[e : e + 1, :count], 0.0).astype(jnp.bfloat16))
        low = nn(jnp.concatenate(hot, axis=0), ext[i, :count, :]).astype(jnp.bfloat16)
        low_g = nn(jnp.concatenate(weighted, axis=0), gm[i]).astype(jnp.bfloat16)
        for lanes, values in ((slice(0, width), low), (slice(width, 2 * width), low_g)):
            for e in range(NF):
                buf[side, i, e, :, lanes] = values[e * PACK : (e + 1) * PACK]
    for i in range(some):
        for e in range(NF):
            buf[side, i, e, :16, :] += carry[e]
            group = pl.multiple_of(whole_groups(step * some + i, e) * 16, 16)
            carry[e] = buf[side, i, e, pl.ds(group, 16), :]
    each_copy(step, begin)

    @pl.when(step == pl.num_programs(0) - 1)
    def _():
        last = pl.num_programs(0)
        each_copy(last - 2, end)
        each_copy(last - 1, end)
        copies = []
        for e in range(NF):
            start = pl.multiple_of(totals[e] // 16 * 16, 16)
            copies.append(pltpu.make_async_copy(carry.at[e], out.at[e, pl.ds(start, 16), :], sems.at[0, 0, e]))
            rest = out.at[e, pl.ds(start + 16, blank.shape[0]), :]
            copies.append(pltpu.make_async_copy(blank, rest, sems.at[1, 0, e]))
        for copy in copies:
            copy.start()
        for copy in copies:
            copy.wait()


def expert_counts(ext):
    count = ext.shape[2] // 3
    slot = ext[:, ext.shape[1] - 16 : ext.shape[1] - 16 + NF, count : 2 * count].astype(jnp.float32)
    counts = (jnp.max(slot, axis=2) + 1.0).astype(jnp.int32)
    upto = jnp.cumsum(counts, axis=0)
    return counts.reshape(-1), (upto - counts).reshape(-1), upto[-1]


def pack_rows(numbers, ext, gm):
    devices, count, width = gm.shape
    some, blank = 4, 256
    bf = jnp.bfloat16
    return pl.pallas_call(
        pack_kernel,
        grid_spec=pltpu.PrefetchScalarGridSpec(
            num_scalar_prefetch=3,
            grid=(devices // some,),
            in_specs=[
                pl.BlockSpec((some, 16, width), lambda d, *_: (d, count // 16, 0)),
                pl.BlockSpec((some,) + ext.shape[1:], lambda d, *_: (d, 0, 0)),
                pl.BlockSpec((some, count, width), lambda d, *_: (d, 0, 0)),
            ],
            out_specs=pl.BlockSpec(memory_space=pl.ANY),
            scratch_shapes=[
                pltpu.VMEM((2, some, NF, PACK, 2 * width), bf),
                pltpu.VMEM((NF, 16, 2 * width), bf),
                pltpu.VMEM((blank, 2 * width), bf),
                pltpu.SemaphoreType.DMA((2, some, NF)),
            ],
        ),
        out_shape=shape_of((NF, devices * MOST + 16 + blank, 2 * width), bf),
        compiler_params=params_of(),
        cost_estimate=BRIEF,
        name="pack_rows",
    )(*numbers, ext, ext, gm)


def dw_kernel(first, totals, packed, wgu, wd, *refs):
    dgu, dd, dg_s, du_s, hid_s = refs[-5:]
    total = totals[first + pl.program_id(0)]
    width = packed.shape[2] // 2
    chunk = 512

    def pieces(part):
        xs, gs = packed[0, part, :width], packed[0, part, width:]
        hid, dg, du = silu_parts(nn(xs, wgu[0, 0, 0]), nn(xs, wgu[0, 0, 1]), nt(gs, wd[0, 0]))
        hid_s[part, :] = hid.astype(jnp.bfloat16)
        dg_s[part, :] = dg
        du_s[part, :] = du

    def chunk_of(i, _):
        pieces(pl.ds(pl.multiple_of(i * chunk, chunk), chunk))
        return 0

    needed = jnp.maximum((total + 255) // 256, 1)
    lax.fori_loop(0, needed // 2, chunk_of, 0)

    @pl.when(needed % 2 == 1)
    def _():
        pieces(pl.ds(pl.multiple_of((needed - 1) * 256, 256), 256))

    for size in range(1, hid_s.shape[0] // 256 + 1):

        @pl.when(needed == size)
        def _():
            rows = 256 * size

            def inputs(i, _):
                part = pl.ds(pl.multiple_of(i * 256, 256), 256)
                xs = packed[0, :rows, part]
                dgu[0, 0, 0, part, :] = tn(xs, dg_s[:rows, :])
                dgu[0, 0, 1, part, :] = tn(xs, du_s[:rows, :])
                return 0

            lax.fori_loop(0, width // 256, inputs, 0)

            def outputs(i, _):
                part = pl.ds(pl.multiple_of(i * 256, 256), 256)
                dd[0, 0, part, :] = tn(hid_s[:rows, part], packed[0, :rows, width:])
                return 0

            lax.fori_loop(0, hid_s.shape[1] // 256, outputs, 0)


def weight_grads(layer, first, last, totals, packed, wgu, wd, earlier):
    _, rows, both = packed.shape
    hidden, width = wd.shape[2], wd.shape[3]
    gu_spec = pl.BlockSpec((1, 1, 2, width, hidden), lambda e, *_: (layer, e + first, 0, 0, 0))
    d_spec = pl.BlockSpec((1, 1, hidden, width), lambda e, *_: (layer, e + first, 0, 0))
    row_spec = pl.BlockSpec((1, rows, both), lambda e, *_: (e + first, 0, 0))
    return pl.pallas_call(
        functools.partial(dw_kernel, first),
        grid_spec=pltpu.PrefetchScalarGridSpec(
            num_scalar_prefetch=1,
            grid=(last - first,),
            in_specs=[row_spec, gu_spec, d_spec] + [pl.BlockSpec(memory_space=pl.ANY)] * len(earlier),
            out_specs=[gu_spec, d_spec],
            scratch_shapes=[pltpu.VMEM((rows // 256 * 256 - 256, hidden), jnp.bfloat16)] * 3,
        ),
        out_shape=[shape_of(wgu.shape, jnp.float32), shape_of(wd.shape, jnp.float32)],
        input_output_aliases={4 + i: i for i in range(len(earlier))},
        compiler_params=params_of(),
        cost_estimate=BRIEF,
        name="weight_grads",
    )(totals, packed, wgu, wd, *earlier)


def norm_low(x, gain):
    return ((x * rms_factor(x)) * gain).astype(jnp.bfloat16)


def post_attention(ob, x, wo, gain):
    groups = wo.shape[0]
    inner = wo.shape[1]
    blk = ob.shape[1]
    halves = []
    for h in range(2):
        total = x[h * blk : (h + 1) * blk]
        for g in range(groups):
            total = total + nn(ob[h * groups + g][:, :inner], wo[g])
        halves.append(total)
    hst = jnp.concatenate(halves, axis=0)
    return hst, norm_low(hst, gain)


def mixing_rows(table):
    raw, coef = table[RAW : RAW + 16], table[COEF : COEF + 16]
    pairs = []
    for c in range(NC):
        r0, r1 = raw[NE + 2 * c : NE + 2 * c + 1], raw[NE + 2 * c + 1 : NE + 2 * c + 2]
        top = jnp.maximum(r0, r1)
        e0, e1 = jnp.exp(r0 - top), jnp.exp(r1 - top)
        pairs.append((e0 / (e0 + e1), e1 / (e0 + e1)))
    shares = [coef[NF + 2 + c : NF + 3 + c] for c in range(NC)]
    scale_u = coef[NF + 1 : NF + 2]
    for c in range(NC):
        scale_u = scale_u + shares[c] * pairs[c][0]
    return pairs, shares, scale_u, [shares[c] * pairs[c][1] for c in range(NC)]


def middle(gx, parts, gcoef, table, routes, gprev, hst, ub, small, wo, ob):
    groups = wo.shape[0]
    inner = wo.shape[1]
    blk = ob.shape[1]
    gain = small[1:2].astype(jnp.float32)
    consts = small[2 : 2 + NC].astype(jnp.float32)
    router = small[2 + NC :]
    pairs, shares, scale_u, scale_c = mixing_rows(table)
    columns = to_columns([scale_u] + scale_c)
    factor = rms_factor(hst)
    base = hst * factor
    u = base * gain
    dots = [jnp.sum(gx * u, axis=1, keepdims=True)]
    dots += [jnp.sum(gx * consts[c : c + 1], axis=1, keepdims=True) for c in range(NC)]
    dots = to_rows(dots, 8)
    dot_u = dots[0:1]
    dot_c = [dots[1 + c : 2 + c] for c in range(NC)]
    ids = lax.broadcasted_iota(jnp.int32, (16, gx.shape[0]), 0)
    grads = jnp.concatenate([gcoef, jnp.zeros_like(gcoef)], axis=0)
    grads = jnp.where(ids == NF + 1, dot_u, grads)
    raw_rows = []
    for c in range(NC):
        a0, a1 = pairs[c]
        grads = jnp.where(ids == NF + 2 + c, a0 * dot_u + a1 * dot_c[c], grads)
        g0, g1 = shares[c] * dot_u, shares[c] * dot_c[c]
        both = a0 * g0 + a1 * g1
        raw_rows += [a0 * (g0 - both), a1 * (g1 - both)]
    logits = table[LOGI : LOGI + 16]
    first, second = ids == routes[0:1], ids == routes[1:2]

    def pick(chosen, rows):
        return jnp.sum(jnp.where(chosen, rows, 0.0), axis=0, keepdims=True)

    z0, z1 = pick(first, logits), pick(second, logits)
    top = jnp.maximum(z0, z1)
    e0, e1 = jnp.exp(z0 - top), jnp.exp(z1 - top)
    w0, w1 = e0 / (e0 + e1), e1 / (e0 + e1)
    gg0, gg1 = pick(first, grads), pick(second, grads)
    both = w0 * gg0 + w1 * gg1
    glog = jnp.where(first, w0 * (gg0 - both), 0.0) + jnp.where(second, w1 * (gg1 - both), 0.0) + gprev
    graw = glog
    for index, row in enumerate(raw_rows):
        graw = jnp.where(ids == NE + index, row, graw)
    graw = graw.astype(jnp.bfloat16)
    grad_router = nn(graw, ub)
    gu = gx * columns[0] + tn(graw, router) + parts
    sums = [jnp.sum(gu * base, axis=0, keepdims=True)]
    sums += [jnp.sum(gx * columns[1 + c], axis=0, keepdims=True) for c in range(NC)]
    gb = gu * gain
    ghst = gx + factor * (gb - base * jnp.mean(gb * base, axis=-1, keepdims=True))
    gy = ghst.astype(jnp.bfloat16)
    lanes = ob.shape[2]
    go, gwo = [None] * (2 * groups), []
    for g in range(groups):
        value = nt(gy, wo[g]).astype(jnp.bfloat16)
        value = jnp.concatenate([value, jnp.zeros((value.shape[0], lanes - inner), jnp.bfloat16)], axis=1)
        for h in range(2):
            go[h * groups + g] = value[h * blk : (h + 1) * blk]
        mixed = jnp.concatenate([ob[g], ob[groups + g]], axis=0)
        gwo.append(tn(mixed, gy)[:inner].astype(jnp.bfloat16))
    return ghst, jnp.stack(go), jnp.stack(gwo), jnp.concatenate(sums + [grad_router], axis=0), glog


def assemble_kernel(ours, theirs, qkv, out, small):
    z, _, _, _ = place()
    layers, shard = ours.shape[0], ours.shape[1]
    inner = GROUP_HEADS * HEAD_DIM
    for l in range(layers):
        small[l] = ours[l, :, :128].astype(jnp.float32) + theirs[l, :, :128].astype(jnp.float32)
        first = 128 + 6 * inner
        out[l] = ours[l, :, first:].astype(jnp.float32) + theirs[l, :, first:].astype(jnp.float32)
        for group in range(4):
            for odd in range(2):

                @pl.when(z % 2 == odd)
                def _():
                    source = ours if group // 2 == odd else theirs
                    for c in range(3):
                        at = 128 + (group % 2) * 3 * inner + c * inner
                        qkv[l, c, :, group * inner : (group + 1) * inner] = source[l, :, at : at + inner].astype(jnp.float32)


def assemble(ours, theirs, width):
    layers, shard, _ = ours.shape
    vm = pl.BlockSpec(memory_space=pltpu.VMEM)
    return pl.pallas_call(
        assemble_kernel,
        out_shape=[
            shape_of((layers, 3, shard, width), jnp.float32),
            shape_of((layers, shard, width), jnp.float32),
            shape_of((layers, shard, 128), jnp.float32),
        ],
        in_specs=[vm] * 2,
        out_specs=[vm] * 3,
        compiler_params=params_of(),
        cost_estimate=BRIEF,
        name="assemble",
    )(ours, theirs)


def turn_tables(seq):
    half = HEAD_DIM // 2
    frequency = np.exp((-np.log(np.float32(10000.0)) * np.arange(half, dtype=np.float32) / np.float32(half)))
    angles = np.arange(seq, dtype=np.float32)[:, None] * frequency.astype(np.float32)[None, :]
    cosine, sine = np.cos(angles), np.sin(angles)
    cosine = np.concatenate([cosine, cosine] * 2, axis=1).astype(np.float32)
    sine = np.concatenate([-sine, sine] * 2, axis=1).astype(np.float32)
    return jnp.asarray(cosine), jnp.asarray(sine)


def by_heads(
    tokens,
    cotangent,
    seq_lengths,
    block_order,
    routes,
    gains,
    qkv_weights,
    out_weight,
    router,
    const_values,
    w_gate_up,
    w_down,
):
    count, width = tokens.shape[1], tokens.shape[2]
    ctx_size, packs = lax.axis_size("ctx"), lax.axis_size("fsdp")
    blk = count // 2
    seq = blk * ctx_size
    pack = lax.axis_index("fsdp")
    z, xx, y, k = place()
    sequence = z // 2
    shard = width // packs
    f32, bf = jnp.float32, jnp.bfloat16
    everyone = ("ctx", "fsdp")

    cosine, sine = turn_tables(seq)
    routes_t = jnp.swapaxes(routes[:, 0], 1, 2)
    smalls = jnp.concatenate([gains, const_values, jnp.swapaxes(router, 1, 2)], axis=1)
    per_layer = smalls.shape[1]
    ints = jnp.concatenate([routes_t.reshape(-1), block_order[0]])
    places = ints.size
    ints = jnp.pad(ints, (0, -places % shard)).astype(bf).reshape(-1, shard)
    smalls = jnp.concatenate([smalls.reshape(LAYERS * per_layer, shard), ints], axis=0)
    smalls = jnp.pad(smalls, ((0, -smalls.shape[0] % 16), (0, 0)))
    smalls = lax.all_gather(smalls, "fsdp", axis=1, tiled=True)
    ints = smalls[LAYERS * per_layer : LAYERS * per_layer + ints.shape[0]].reshape(-1, packs, shard)
    ints = jnp.swapaxes(ints, 0, 1).reshape(packs, -1).astype(jnp.int32)
    smalls = [smalls[l * per_layer : (l + 1) * per_layer] for l in range(LAYERS)]
    near = jnp.stack([pack, 2 * y + 1 - k, 2 * (1 - y) + k, 2 * (1 - y) + 1 - k])
    routes_f = ints[near][:, : routes_t.size].reshape((packs,) + routes_t.shape)
    order = lax.dynamic_index_in_dim(ints, 2 * y + xx, 0, keepdims=False)
    order = order[routes_t.size : places].reshape(ctx_size, 2)
    order = lax.dynamic_index_in_dim(order, sequence, 1, keepdims=False) - ctx_size * sequence
    ids = jnp.arange(ctx_size, dtype=jnp.int32)
    inv = jnp.sum(jnp.where(order[None, :] == ids[:, None], ids[None, :], 0), axis=1)

    gm_all = [None, lax.all_gather(cotangent[0], everyone, axis=0, tiled=False)]
    x = tokens[0].astype(f32)
    before = jnp.zeros((packs, 16, count), f32)
    kept, ext_all = [], [None] * LAYERS
    for l in range(LAYERS):
        n1s, qkv, o, lse, ob, hst, ub, w, wo = attn_forward(
            l, order, inv, x, smalls[l], qkv_weights, cosine, sine, out_weight, 2 * l
        )
        if l == 1:
            ub, gm_all[1] = lax.optimization_barrier((ub, gm_all[1]))
        ubf, table, ext, x_next = ffn_forward(
            l, ub, hst, smalls[l], routes_f[:, l], before, w_gate_up, w_down, 2 * l + 1
        )
        before = table[:, LOGI : LOGI + 16]
        ext_all[l] = lax.all_gather(ext, everyone, axis=0, tiled=False)
        kept.append((x, n1s, qkv, o, lse, ob, hst, w, wo, ubf, table))
        x = x_next
    output = x
    gm = cotangent[0]
    gx = gm.astype(f32)
    gprev = jnp.zeros((16, count), f32)
    grads = [None] * LAYERS
    for l in reversed(range(LAYERS)):
        x, n1s, qkv, o, lse, ob, hst, w, wo, ubf, table = kept[l]
        number = 2 * LAYERS + 2 * l
        ghst, go, gwo, small, gprev = ffn_backward(
            l, gm, gx, ubf, table, hst, smalls[l], routes_t[l], gprev, wo, ob, w_gate_up, w_down, number
        )
        if l == 1:
            go, ext_all[0] = lax.optimization_barrier((go, ext_all[0]))
        gx, gm, grads[l] = attn_backward(
            order, inv, n1s, w, cosine, sine, qkv, o, lse, go, ghst, x, smalls[l], small, gwo, number + 1
        )
        if l > 0:
            gm_all[l - 1] = gm

    dense = jnp.stack(grads)
    dense, gm = lax.optimization_barrier((dense, gm_all[0]))
    gm_all[0] = lax.all_gather(gm, everyone, axis=0, tiled=False)

    def partner(values, distance):
        return lax.ppermute(values, "ctx", [(i, i ^ distance) for i in range(ctx_size)])

    def added(first, second):
        return (first.astype(f32) + second.astype(f32)).astype(bf)

    half = NF // 2
    numbers = expert_counts(ext_all[1])
    packed = pack_rows(numbers, ext_all[1], gm_all[1])
    done = weight_grads(1, 0, half, numbers[2], packed, w_gate_up, w_down, ())
    dense, done = lax.optimization_barrier((dense, done))
    got = partner(dense, 1)
    done = weight_grads(1, half, NF, numbers[2], packed, w_gate_up, w_down, done)
    done, got = lax.optimization_barrier((done, got))
    dense = added(dense, got)
    dense, ext, gm = lax.optimization_barrier((dense, ext_all[0], gm_all[0]))
    got = partner(dense, 4)
    numbers = expert_counts(ext)
    packed = pack_rows(numbers, ext, gm)
    done = weight_grads(0, 0, half, numbers[2], packed, w_gate_up, w_down, done)
    done, got = lax.optimization_barrier((done, got))
    dense = added(dense, got)
    dense, done = lax.optimization_barrier((dense, done))
    got = partner(dense, 2)
    done = weight_grads(0, half, NF, numbers[2], packed, w_gate_up, w_down, done)
    done, got = lax.optimization_barrier((done, got))
    qkv, out, small = assemble(dense, got, width)
    rows = jnp.swapaxes(small[..., : 2 + NC], 1, 2)
    return (
        output[None],
        gx[None],
        rows[:, :2],
        qkv,
        out,
        small[..., 2 + NC : 2 + NC + 16],
        rows[:, 2:],
        done[0],
        done[1],
    )


def solution(mesh):
    placed = (
        P("fsdp", "ctx", None),
        P("fsdp", "ctx", None),
        P("fsdp", None),
        P("fsdp", None),
        P(None, "fsdp", "ctx", None),
        P(None, None, "fsdp"),
        P(None, None, "fsdp", None),
        P(None, "fsdp", None),
        P(None, "fsdp", None),
        P(None, None, "fsdp"),
        P(None, None, None, None, "fsdp"),
        P(None, None, "fsdp", None),
    )
    contexts, packs = mesh.shape["ctx"], mesh.shape["fsdp"]
    blocks_of_heads = HEADS // GROUP_HEADS

    def plan(*args):
        tokens = args[0]
        even = tokens.shape[1] * contexts == 2 * MINLEN
        grouped = contexts == 2 * blocks_of_heads and packs == blocks_of_heads
        return (by_heads if even and grouped else shards)(*args)

    return jax.shard_map(
        plan,
        mesh=mesh,
        in_specs=placed,
        out_specs=(
            P("fsdp", "ctx", None),
            P("fsdp", "ctx", None),
            P(None, None, "fsdp"),
            P(None, None, "fsdp", None),
            P(None, "fsdp", None),
            P(None, "fsdp", None),
            P(None, None, "fsdp"),
            P(None, None, None, None, "fsdp"),
            P(None, None, "fsdp", None),
        ),
        check_vma=False,
    )
```

```python
import functools

import jax
import jax.numpy as jnp
import numpy as np
from jax import lax
from jax.experimental import pallas as pl
from jax.experimental.pallas import tpu as pltpu
from jax.sharding import PartitionSpec as P

HEADS = 12
HEAD_DIM = 64
NF = 8
NC = 2
LAYERS = 2
NE = 12
MOST = 64
GROUP_HEADS = 3


def from_behind(x, axis, by):
    devices = lax.axis_size(axis)
    return lax.ppermute(x, axis, [(i, (i + by) % devices) for i in range(devices)])


def layout_tables(lengths, order_row, tok_count):
    block_len = tok_count // 2
    pack_len = order_row.shape[0] * block_len
    pack_rows = jnp.arange(pack_len, dtype=jnp.int32)
    owner = pack_rows // tok_count
    which_half = pack_rows % tok_count // block_len
    block_ids = order_row[2 * owner + which_half]
    pack_pos = block_ids * block_len + pack_rows % block_len
    segment = (pack_pos >= lengths[0]).astype(jnp.int32)
    seq_pos = pack_pos - segment * lengths[0]
    return (pack_pos, segment, seq_pos)


def angle_tables(seq_pos, head_size):
    half_size = head_size // 2
    frequency = jnp.exp(-jnp.log(10000.0) * jnp.arange(half_size, dtype=jnp.float32) / half_size)
    angles = seq_pos.astype(jnp.float32)[:, None] * frequency[None, :]
    return (jnp.cos(angles)[:, None, :], jnp.sin(angles)[:, None, :])


def rotate_pairs(values, cosine_table, sine_table, direction):
    half_size = values.shape[-1] // 2
    first_half = values[..., :half_size]
    second_half = values[..., half_size:]
    return jnp.concatenate(
        [
            first_half * cosine_table - direction * second_half * sine_table,
            second_half * cosine_table + direction * first_half * sine_table,
        ],
        axis=-1,
    )


def rms_parts(values):
    inverse = lax.rsqrt(jnp.mean(values * values, axis=-1, keepdims=True) + 1e-06)
    return (values * inverse, inverse)


def rms_back(grad_normed, base_values, inverse):
    return inverse * (
        grad_normed - base_values * jnp.mean(grad_normed * base_values, axis=-1, keepdims=True)
    )


def expert_forward(inputs_low, gate_up_use, down_use):
    gate_up_out = jnp.einsum(
        "emd,ecdf->ecmf", inputs_low, gate_up_use, preferred_element_type=jnp.float32
    )
    hidden_low = (jax.nn.silu(gate_up_out[:, 0]) * gate_up_out[:, 1]).astype(jnp.bfloat16)
    partial_value = jnp.einsum(
        "emf,efd->emd", hidden_low, down_use, preferred_element_type=jnp.float32
    )
    return (gate_up_out, hidden_low, partial_value)


def expert_backward(inputs_low, gate_up_out, hidden_low, grad_part_low, gate_up_use, down_use):
    grad_down = jnp.einsum(
        "emf,emd->efd", hidden_low, grad_part_low, preferred_element_type=jnp.float32
    )
    grad_hidden = jnp.einsum(
        "emd,efd->emf", grad_part_low, down_use, preferred_element_type=jnp.float32
    )
    gate_out = gate_up_out[:, 0]
    sigmoid_gate = jax.nn.sigmoid(gate_out)
    grad_pair_low = jnp.stack(
        [
            grad_hidden
            * gate_up_out[:, 1]
            * sigmoid_gate
            * (1.0 + gate_out * (1.0 - sigmoid_gate)),
            grad_hidden * gate_out * sigmoid_gate,
        ],
        axis=1,
    ).astype(jnp.bfloat16)
    grad_gate_up = jnp.einsum(
        "emd,ecmf->ecdf", inputs_low, grad_pair_low, preferred_element_type=jnp.float32
    )
    grad_rows = jnp.einsum(
        "ecmf,ecdf->emd", grad_pair_low, gate_up_use, preferred_element_type=jnp.float32
    )
    return (grad_gate_up, grad_down, grad_rows)


def shards(
    tokens,
    cotangent,
    seq_lengths,
    block_order,
    routes,
    gains,
    qkv_weights,
    out_weight,
    router,
    const_values,
    w_gate_up,
    w_down,
):
    tok_count = tokens.shape[1]
    width = tokens.shape[2]
    ctx_size = lax.axis_size("ctx")
    own_index = lax.axis_index("ctx")
    score_scale = HEAD_DIM ** (-0.5)
    pack_pos, segment, seq_pos = layout_tables(seq_lengths[0], block_order[0], tok_count)
    own_start = own_index * tok_count
    query_pos = lax.dynamic_slice_in_dim(pack_pos, own_start, tok_count)
    query_seg = lax.dynamic_slice_in_dim(segment, own_start, tok_count)
    cosine_table, sine_table = angle_tables(
        lax.dynamic_slice_in_dim(seq_pos, own_start, tok_count), HEAD_DIM
    )
    head_shape = (tok_count, HEADS, HEAD_DIM)
    expert_ids = jnp.arange(NE, dtype=jnp.int32)
    slot_ids = jnp.arange(MOST, dtype=jnp.int32)
    row_ids = jnp.arange(tok_count, dtype=jnp.int32)

    def allowed_pairs(key_offset, key_count):
        key_pos = lax.dynamic_slice_in_dim(pack_pos, key_offset, key_count)
        key_seg = lax.dynamic_slice_in_dim(segment, key_offset, key_count)
        return (query_seg[:, None] == key_seg[None, :]) & (key_pos[None, :] <= query_pos[:, None])

    stream = tokens[0].astype(jnp.float32)
    previous = jnp.zeros((tok_count, NE), jnp.float32)
    saved = []
    for layer_index in range(LAYERS):
        gain_all, qkv_all, out_all, router_all, const_all = (
            lax.all_gather(gains[layer_index], "fsdp", axis=1, tiled=True),
            lax.all_gather(qkv_weights[layer_index], "fsdp", axis=1, tiled=True),
            lax.all_gather(out_weight[layer_index], "fsdp", axis=0, tiled=True),
            lax.all_gather(router[layer_index], "fsdp", axis=0, tiled=True),
            lax.all_gather(const_values[layer_index], "fsdp", axis=1, tiled=True),
        )
        gain_float = gain_all.astype(jnp.float32)
        base_one, inverse_one = rms_parts(stream)
        normed_low = (base_one * gain_float[0]).astype(jnp.bfloat16)
        projected = jnp.einsum(
            "td,cde->cte", normed_low, qkv_all, preferred_element_type=jnp.float32
        )
        queries_low = rotate_pairs(
            projected[0].reshape(head_shape), cosine_table, sine_table, 1.0
        ).astype(jnp.bfloat16)
        keys_low = rotate_pairs(
            projected[1].reshape(head_shape), cosine_table, sine_table, 1.0
        ).astype(jnp.bfloat16)
        values_low = projected[2].reshape(head_shape).astype(jnp.bfloat16)

        def fold_step(running, shard_piece, offset, queries_use=queries_low):
            keys_piece, values_piece = shard_piece
            allowed = allowed_pairs(offset, keys_piece.shape[0])[None]
            scores = (
                jnp.einsum(
                    "qhd,khd->hqk", queries_use, keys_piece, preferred_element_type=jnp.float32
                )
                * score_scale
            )
            scores = jnp.where(allowed, scores, -1e30)
            top_old, total_old, accumulated = running
            top_new = jnp.maximum(top_old, jnp.max(scores, axis=-1))
            weights = jnp.where(allowed, jnp.exp(scores - top_new[..., None]), 0.0)
            factor = jnp.exp(top_old - top_new)
            accumulated = jnp.einsum(
                "hqk,khd->hqd",
                weights.astype(jnp.bfloat16),
                values_piece,
                preferred_element_type=jnp.float32,
            )
            return (top_new, jnp.sum(weights, axis=-1), accumulated)

        starting = (
            jnp.full((HEADS, tok_count), -1e30, jnp.float32),
            jnp.zeros((HEADS, tok_count), jnp.float32),
            jnp.zeros((HEADS, tok_count, HEAD_DIM), jnp.float32),
        )
        top_value, total_sum, accumulated = fold_step(
            starting,
            (
                lax.all_gather(keys_low, "ctx", axis=0, tiled=True),
                lax.all_gather(values_low, "ctx", axis=0, tiled=True),
            ),
            jnp.int32(0),
        )
        log_total = top_value + jnp.log(total_sum)
        attended = jnp.transpose(accumulated / total_sum[..., None], (1, 0, 2))
        mixed_low = attended.reshape(tok_count, width).astype(jnp.bfloat16)
        hidden_state = stream + jnp.dot(mixed_low, out_all, preferred_element_type=jnp.float32)
        base_two, inverse_two = rms_parts(hidden_state)
        expert_in = base_two * gain_float[1]
        expert_low = expert_in.astype(jnp.bfloat16)
        raw_logits = jnp.dot(expert_low, router_all, preferred_element_type=jnp.float32)
        logits = raw_logits[:, :NE] + previous
        route_ids = routes[layer_index, 0]
        chosen = route_ids[:, :, None] == expert_ids[None, None, :]
        chosen_f = chosen.astype(jnp.float32)
        hit_count = jnp.sum(chosen.astype(jnp.int32), axis=1)
        slot_index = jnp.cumsum(hit_count, axis=0) - 1
        picked = jnp.sum(chosen_f * logits[:, None, :], axis=-1)
        gate_weights = jax.nn.softmax(picked, axis=-1)
        coeffs = jnp.sum(gate_weights[:, :, None] * chosen_f, axis=1)
        slot_table = jnp.zeros((NF, MOST), jnp.int32)
        for expert in range(NF):
            target = jnp.where(hit_count[:, expert] > 0, slot_index[:, expert], MOST)
            slot_table = slot_table.at[expert, target].set(row_ids, mode="drop")
        filled = (slot_ids[None, :] < jnp.sum(hit_count[:, :NF], axis=0)[:, None]).astype(
            jnp.float32
        )
        rows_low = expert_low[slot_table]
        inputs_low = lax.all_gather(rows_low, "fsdp", axis=1, tiled=True)
        gate_up_out, hidden_low, partial_value = expert_forward(
            inputs_low, w_gate_up[layer_index], w_down[layer_index]
        )
        result = lax.psum_scatter(
            partial_value.astype(jnp.bfloat16), "fsdp", scatter_dimension=1, tiled=True
        ).astype(jnp.float32)
        flat_index = jnp.arange(NF, dtype=jnp.int32)[None, :] * MOST + jnp.clip(
            slot_index[:, :NF], 0, MOST - 1
        )
        token_result = result.reshape(NF * MOST, width)[flat_index]
        expert_mix = (
            jnp.sum(coeffs[:, :NF, None] * token_result, axis=1)
            + coeffs[:, NF + 1 : NF + 2] * expert_in
        )
        mixings = []
        for const_index in range(NC):
            column = NE + 2 * const_index
            mixing = jax.nn.softmax(raw_logits[:, column : column + 2], axis=-1)
            mixings.append(mixing)
            expert_mix = expert_mix + coeffs[:, NF + 2 + const_index : NF + 3 + const_index] * (
                mixing[:, 0:1] * expert_in
                + mixing[:, 1:2] * const_all[const_index].astype(jnp.float32)[None, :]
            )
        saved.append(
            (
                gain_float,
                qkv_all,
                out_all,
                router_all,
                const_all,
                base_one,
                inverse_one,
                normed_low,
                queries_low,
                keys_low,
                values_low,
                log_total,
                attended,
                mixed_low,
                base_two,
                inverse_two,
                expert_in,
                expert_low,
                chosen_f,
                hit_count,
                gate_weights,
                coeffs,
                slot_table,
                filled,
                inputs_low,
                gate_up_out,
                hidden_low,
                flat_index,
                token_result,
                mixings,
            )
        )
        stream = hidden_state + expert_mix
        previous = logits
    grad_stream = cotangent[0].astype(jnp.float32)
    grad_previous = jnp.zeros((tok_count, NE), jnp.float32)
    layer_grads = [None] * LAYERS
    for layer_index in reversed(range(LAYERS)):
        (
            gain_float,
            qkv_all,
            out_all,
            router_all,
            const_all,
            base_one,
            inverse_one,
            normed_low,
            queries_low,
            keys_low,
            values_low,
            log_total,
            attended,
            mixed_low,
            base_two,
            inverse_two,
            expert_in,
            expert_low,
            chosen_f,
            hit_count,
            gate_weights,
            coeffs,
            slot_table,
            filled,
            inputs_low,
            gate_up_out,
            hidden_low,
            flat_index,
            token_result,
            mixings,
        ) = saved[layer_index]
        grad_mix = grad_stream
        dot_input = jnp.sum(grad_mix * expert_in, axis=-1, keepdims=True)
        coef_grads = [
            jnp.sum(grad_mix[:, None, :] * token_result, axis=-1),
            jnp.zeros((tok_count, 1), jnp.float32),
            dot_input,
        ]
        grad_in = grad_mix * coeffs[:, NF + 1 : NF + 2]
        const_cols = []
        const_grads = []
        for const_index in range(NC):
            mixing = mixings[const_index]
            const_row = const_all[const_index].astype(jnp.float32)[None, :]
            dot_const = jnp.sum(grad_mix * const_row, axis=-1, keepdims=True)
            share = coeffs[:, NF + 2 + const_index : NF + 3 + const_index]
            coef_grads.append(mixing[:, 0:1] * dot_input + mixing[:, 1:2] * dot_const)
            grad_in = grad_in + grad_mix * (share * mixing[:, 0:1])
            grad_mixing = share * jnp.concatenate([dot_input, dot_const], axis=1)
            const_cols.append(
                mixing * (grad_mixing - jnp.sum(mixing * grad_mixing, axis=-1, keepdims=True))
            )
            const_grads.append(jnp.sum(grad_mix * (share * mixing[:, 1:2]), axis=0))
        grad_coeffs = jnp.concatenate(coef_grads, axis=1)
        grad_gates = jnp.sum(chosen_f * grad_coeffs[:, None, :], axis=-1)
        grad_picked = gate_weights * (
            grad_gates - jnp.sum(gate_weights * grad_gates, axis=-1, keepdims=True)
        )
        grad_logits = jnp.sum(grad_picked[:, :, None] * chosen_f, axis=1) + grad_previous
        grad_previous = grad_logits
        grad_raw_low = jnp.concatenate([grad_logits] + const_cols, axis=1).astype(jnp.bfloat16)
        grad_router = jnp.einsum(
            "td,tc->dc", expert_low, grad_raw_low, preferred_element_type=jnp.float32
        )
        grad_in = grad_in + jnp.einsum(
            "tc,dc->td", grad_raw_low, router_all, preferred_element_type=jnp.float32
        )
        slot_weight = (
            jnp.take_along_axis(jnp.transpose(coeffs[:, :NF]), slot_table, axis=1) * filled
        )
        grad_result_low = (grad_mix[slot_table] * slot_weight[:, :, None]).astype(jnp.bfloat16)
        grad_part_low = lax.all_gather(grad_result_low, "fsdp", axis=1, tiled=True)
        grad_gate_up, grad_down, grad_rows = expert_backward(
            inputs_low,
            gate_up_out,
            hidden_low,
            grad_part_low,
            w_gate_up[layer_index],
            w_down[layer_index],
        )
        grad_rows = lax.psum_scatter(
            grad_rows.astype(jnp.bfloat16), "fsdp", scatter_dimension=1, tiled=True
        ).astype(jnp.float32)
        token_grads = grad_rows.reshape(NF * MOST, width)[flat_index]
        grad_in = grad_in + jnp.sum(
            jnp.where(hit_count[:, :NF, None] > 0, token_grads, 0.0), axis=1
        )
        grad_gain_two = jnp.sum(grad_in * base_two, axis=0)
        grad_hidden_state = grad_stream + rms_back(grad_in * gain_float[1], base_two, inverse_two)
        grad_out_low = grad_hidden_state.astype(jnp.bfloat16)
        grad_out_w = jnp.einsum(
            "td,te->de", mixed_low, grad_out_low, preferred_element_type=jnp.float32
        )
        grad_attended = (
            jnp.einsum("te,de->td", grad_out_low, out_all, preferred_element_type=jnp.float32)
            .astype(jnp.bfloat16)
            .reshape(head_shape)
        )
        delta = jnp.transpose(jnp.sum(grad_attended.astype(jnp.float32) * attended, axis=-1))

        def visit(
            turn_index,
            carried,
            queries_use=queries_low,
            grad_use=grad_attended,
            log_use=log_total,
            delta_use=delta,
        ):
            keys_piece, values_piece, key_grads, value_grads, query_grads = carried
            source = (own_index - turn_index) % ctx_size
            allowed = allowed_pairs(source * tok_count, tok_count)[None]
            scores = (
                jnp.einsum(
                    "qhd,khd->hqk", queries_use, keys_piece, preferred_element_type=jnp.float32
                )
                * score_scale
            )
            probs = jnp.where(
                allowed, jnp.exp(jnp.where(allowed, scores, -1e30) - log_use[..., None]), 0.0
            )
            value_grads = value_grads + jnp.einsum(
                "hqk,qhd->khd",
                probs.astype(jnp.bfloat16),
                grad_use,
                preferred_element_type=jnp.float32,
            )
            prob_grads = jnp.einsum(
                "qhd,khd->hqk", grad_use, values_piece, preferred_element_type=jnp.float32
            )
            score_grads = (probs * (prob_grads - delta_use[..., None])).astype(jnp.bfloat16)
            query_grads = query_grads + jnp.einsum(
                "hqk,khd->qhd", score_grads, keys_piece, preferred_element_type=jnp.float32
            )
            key_grads = key_grads + jnp.einsum(
                "hqk,qhd->khd", score_grads, queries_use, preferred_element_type=jnp.float32
            )
            keys_piece, values_piece = from_behind((keys_piece, values_piece), "ctx", 1)
            key_grads, value_grads = (
                from_behind(key_grads.astype(jnp.bfloat16), "ctx", 1).astype(key_grads.dtype),
                from_behind(value_grads.astype(jnp.bfloat16), "ctx", 1).astype(value_grads.dtype),
            )
            return (keys_piece, values_piece, key_grads, value_grads, query_grads)

        zero_heads = jnp.zeros(head_shape, jnp.float32)
        finished = lax.fori_loop(
            0, ctx_size, visit, (keys_low, values_low, zero_heads, zero_heads, zero_heads)
        )
        grad_query = (
            rotate_pairs(finished[4] * score_scale, cosine_table, sine_table, -1.0)
            .astype(jnp.bfloat16)
            .reshape(tok_count, width)
        )
        grad_key = (
            rotate_pairs(finished[2] * score_scale, cosine_table, sine_table, -1.0)
            .astype(jnp.bfloat16)
            .reshape(tok_count, width)
        )
        grad_value = finished[3].astype(jnp.bfloat16).reshape(tok_count, width)
        grad_proj_low = jnp.stack([grad_query, grad_key, grad_value], axis=0)
        grad_qkv = jnp.einsum(
            "td,cte->cde", normed_low, grad_proj_low, preferred_element_type=jnp.float32
        )
        grad_normed = jnp.einsum(
            "cte,cde->td", grad_proj_low, qkv_all, preferred_element_type=jnp.float32
        )
        grad_gain_one = jnp.sum(grad_normed * base_one, axis=0)
        grad_stream = grad_hidden_state + rms_back(
            grad_normed * gain_float[0], base_one, inverse_one
        )
        gains_shard, qkv_shard, out_shard, router_shard, const_shard = (
            lax.psum_scatter(
                jnp.stack([grad_gain_one, grad_gain_two]).astype(jnp.bfloat16),
                "fsdp",
                scatter_dimension=1,
                tiled=True,
            ).astype(jnp.float32),
            lax.psum_scatter(
                grad_qkv.astype(jnp.bfloat16), "fsdp", scatter_dimension=1, tiled=True
            ).astype(jnp.float32),
            lax.psum_scatter(
                grad_out_w.astype(jnp.bfloat16), "fsdp", scatter_dimension=0, tiled=True
            ).astype(jnp.float32),
            lax.psum_scatter(
                grad_router.astype(jnp.bfloat16), "fsdp", scatter_dimension=0, tiled=True
            ).astype(jnp.float32),
            lax.psum_scatter(
                jnp.stack(const_grads).astype(jnp.bfloat16), "fsdp", scatter_dimension=1, tiled=True
            ).astype(jnp.float32),
        )
        layer_grads[layer_index] = (
            lax.psum(gains_shard.astype(jnp.bfloat16), "ctx").astype(jnp.float32),
            lax.psum(qkv_shard.astype(jnp.bfloat16), "ctx").astype(jnp.float32),
            lax.psum(out_shard.astype(jnp.bfloat16), "ctx").astype(jnp.float32),
            lax.psum(router_shard.astype(jnp.bfloat16), "ctx").astype(jnp.float32),
            lax.psum(const_shard.astype(jnp.bfloat16), "ctx").astype(jnp.float32),
            lax.psum(grad_gate_up.astype(jnp.bfloat16), "ctx").astype(jnp.float32),
            lax.psum(grad_down.astype(jnp.bfloat16), "ctx").astype(jnp.float32),
        )
    stacked = [
        jnp.stack([layer_grads[layer_index][member_index] for layer_index in range(LAYERS)])
        for member_index in range(7)
    ]
    return (
        stream[None],
        grad_stream[None],
        stacked[0],
        stacked[1],
        stacked[2],
        stacked[3],
        stacked[4],
        stacked[5],
        stacked[6],
    )


MINLEN = 1024
ROUT = 56
RAW, COEF, SLOT, LOGI = 0, 16, 32, 40
VMEM_MB = 60
BRIEF = pl.CostEstimate(flops=1, bytes_accessed=1, transcendentals=0)


def nt(a, b):
    return lax.dot_general(a, b, (((1,), (1,)), ((), ())), preferred_element_type=jnp.float32)


def nn(a, b):
    return lax.dot_general(a, b, (((1,), (0,)), ((), ())), preferred_element_type=jnp.float32)


def tn(a, b):
    return lax.dot_general(a, b, (((0,), (0,)), ((), ())), preferred_element_type=jnp.float32)


def params_of(mb=VMEM_MB, **more):
    return pltpu.CompilerParams(vmem_limit_bytes=mb * 2**20, **more)


def shape_of(dims, kind):
    return jax.ShapeDtypeStruct(dims, kind)


def rms_factor(values):
    return lax.rsqrt(jnp.mean(values * values, axis=-1, keepdims=True) + 1e-06)


def to_rows(columns, count):
    lane = lax.broadcasted_iota(jnp.int32, (columns[0].shape[0], 128), 1)
    packed = jnp.zeros(lane.shape, jnp.float32)
    for index, column in enumerate(columns):
        packed = jnp.where(lane == index, column, packed)
    return jnp.transpose(packed)[:count]


def to_columns(rows):
    count = rows[0].shape[1]
    sub = lax.broadcasted_iota(jnp.int32, (128, count), 0)
    packed = jnp.zeros(sub.shape, jnp.float32)
    for index, row in enumerate(rows):
        packed = jnp.where(sub == index, row, packed)
    packed = jnp.transpose(packed)
    return [packed[:, index : index + 1] for index in range(len(rows))]


def swap_halves(values):
    lanes = values.shape[1]
    lane = lax.broadcasted_iota(jnp.int32, values.shape, 1)
    ahead = pltpu.roll(values, lanes - 32, 1)
    behind = pltpu.roll(values, 32, 1)
    return jnp.where(lane % 64 < 32, ahead, behind)


def spin(values, cosine, sine):
    return values * cosine + swap_halves(values) * sine


def place():
    own, pack = lax.axis_index("ctx"), lax.axis_index("fsdp")
    return own // 2, own % 2, pack // 2, pack % 2


def remote(src, dst, send, recv, ctx, fsdp):
    return pltpu.make_async_remote_copy(
        src_ref=src,
        dst_ref=dst,
        send_sem=send,
        recv_sem=recv,
        device_id=(ctx, fsdp),
        device_id_type=pl.DeviceIdType.MESH,
    )


def greet_plane(contexts, across=False):
    own = lax.axis_index("ctx")
    _, _, y, k = place()
    barrier = pltpu.get_barrier_semaphore()
    if across:
        for core in (k, 1 - k):
            device = (own, 2 * (1 - y) + core)
            pl.semaphore_signal(barrier, inc=1, device_id=device, device_id_type=pl.DeviceIdType.MESH)
    for ctx in range(contexts):
        for core in range(2):

            @pl.when(jnp.logical_or(ctx != own, core != k))
            def _():
                pl.semaphore_signal(barrier, inc=1, device_id=(ctx, 2 * y + core), device_id_type=pl.DeviceIdType.MESH)

    return barrier, 2 * contexts - 1 + (2 if across else 0)


def greet_packs():
    own = lax.axis_index("ctx")
    _, _, y, k = place()
    barrier = pltpu.get_barrier_semaphore()
    for fsdp in (2 * y + 1 - k, 2 * (1 - y) + k, 2 * (1 - y) + 1 - k):
        pl.semaphore_signal(barrier, inc=1, device_id=(own, fsdp), device_id_type=pl.DeviceIdType.MESH)
    return barrier, 3


def attn_fwd_kernel(
    order, inv, x, small, wq, cosine, sine, wo_own,
    n1s, qkv, o, lse, ob, hst, ub, w, wo,
    n1own, n1r, osort, osend, orecv, cols, w_s, wo_s,
    n_send, n_recv, f_send, f_recv, p_send, o_send, o_recv, w_send, w_recv, v_send, v_recv,
):
    blocks, blk, _ = n1r.shape
    lanes = o.shape[1]
    seq = blocks * blk
    step = 2 * blk
    own = lax.axis_index("ctx")
    z, xx, y, k = place()
    depth = blocks // 2
    same = xx == k
    pack = lax.axis_index("fsdp")
    inner = wo_own.shape[1]
    beside, over, corner = 2 * y + 1 - k, 2 * (1 - y) + k, 2 * (1 - y) + 1 - k

    barrier, others = greet_plane(blocks, across=True)
    n1 = norm_low(x[...], small[0:1, :].astype(jnp.float32))
    n1own[0] = n1[:blk]
    n1own[1] = n1[blk:]
    pl.semaphore_wait(barrier, others)

    def n1_copy(zz):
        return remote(n1own.at[zz // 2], n1r.at[own], n_send.at[zz], n_recv.at[z], 2 * zz + k, 2 * y + xx)

    def sent(zz):
        there = jnp.logical_not(jnp.logical_and(same, zz == z))
        return there if zz in (1, 2) else jnp.logical_and(there, z // 2 == zz // 2)

    def passed(zz):
        return jnp.logical_and(z // 2 != zz // 2, jnp.logical_or(z == 1, z == 2))

    def pass_copy(zz):
        slot = n1r.at[2 * zz + k]
        other = z // 2 * 2 + 1 - z % 2
        return remote(slot, slot, p_send.at[zz], n_recv.at[zz], 2 * other + xx, 2 * y + k)

    for zz in range(depth):

        @pl.when(sent(zz))
        def _():
            n1_copy(zz).start()

        @pl.when(jnp.logical_and(same, zz == z))
        def _():
            n1r[own] = n1own[zz // 2]

    for half in range(2):

        @pl.when(z % 2 == half)
        def _():
            for core in range(2):
                first = (2 * half + core) * inner
                for c in range(3):
                    cols[core, :, c * lanes : c * lanes + inner] = wq[0, c, :, first : first + inner]
                    cols[core, :, c * lanes + inner : (c + 1) * lanes] = jnp.zeros((inner, lanes - inner), jnp.bfloat16)

    def rows_of(device):
        return pl.ds(pl.multiple_of(device * inner, inner), inner)

    def w_copy(index):
        device, core = ((beside, 1 - k), (over, k), (corner, 1 - k))[index]
        return remote(cols.at[core], w_s.at[rows_of(pack), :], w_send.at[index], w_recv.at[index], own, device)

    def w_wait(index):
        rows = w_s.at[rows_of((beside, over, corner)[index]), :]
        remote(cols.at[0], rows, w_send.at[index], w_recv.at[index], own, beside).wait_recv()

    w_s[rows_of(pack), :] = cols[k]
    wo_s[pack] = wo_own[0]
    for index in (1, 2, 0):
        w_copy(index).start()
    v_far = remote(wo_s.at[pack], wo_s.at[pack], v_send.at[0], v_recv.at[0], own, over)
    v_near = remote(wo_s.at[pack], wo_s.at[pack], v_send.at[1], v_recv.at[1], own, beside)
    v_on = remote(wo_s.at[over], wo_s.at[over], v_send.at[2], v_recv.at[2], own, beside)
    v_far.start()
    v_near.start()

    def forward_copy(zz):
        slot = n1r.at[2 * zz + k]
        return remote(slot, slot, f_send.at[zz], f_recv.at[zz], own, 2 * y + 1 - k)

    for zz in range(depth):

        @pl.when(jnp.logical_not(jnp.logical_and(same, zz == z)))
        def _():
            remote(n1own.at[0], n1r.at[2 * zz + k], n_send.at[zz], n_recv.at[zz], 2 * zz + k, 2 * y + xx).wait_recv()

        @pl.when(passed(zz))
        def _():
            pass_copy(zz).start()

        forward_copy(zz).start()
    for zz in range(depth):
        slot = n1r.at[2 * zz + 1 - k]
        remote(slot, slot, f_send.at[zz], f_recv.at[zz], own, 2 * y + 1 - k).wait_recv()

    for index in range(3):
        w_wait(index)
    w[...] = w_s[...]
    for b in range(blocks):
        n1s[b * blk : (b + 1) * blk, :] = n1r[inv[b]]
    for i in range(seq // step):
        part = slice(i * step, (i + 1) * step)
        out = nn(n1s[part, :], w_s[...])
        cos2 = jnp.concatenate([cosine[part, :]] * (lanes // 128), axis=1)
        sin2 = jnp.concatenate([sine[part, :]] * (lanes // 128), axis=1)
        q = spin(out[:, :lanes], cos2, sin2).astype(jnp.bfloat16)
        qkv[part, :lanes] = q * jnp.asarray(HEAD_DIM**-0.5, jnp.bfloat16)
        qkv[part, lanes : 2 * lanes] = spin(out[:, lanes : 2 * lanes], cos2, sin2).astype(jnp.bfloat16)
        qkv[part, 2 * lanes :] = out[:, 2 * lanes :].astype(jnp.bfloat16)
    lane = lax.broadcasted_iota(jnp.int32, (step, 128), 1)
    for i in range(seq // step):
        part = slice(i * step, (i + 1) * step)
        span = (i + 1) * step
        seen = lax.broadcasted_iota(jnp.int32, (step, span), 1) <= (
            lax.broadcasted_iota(jnp.int32, (step, span), 0) + i * step
        )
        logs = jnp.zeros((step, 128), jnp.float32)
        for head in range(GROUP_HEADS):
            tile, side = head // 2, head % 2
            at = tile * 128
            mine = lane // 64 == side
            q = jnp.where(mine, qkv[part, at : at + 128], jnp.asarray(0, jnp.bfloat16))
            s = nt(q, qkv[:span, lanes + at : lanes + at + 128])
            s = jnp.where(seen, s, -1e30)
            top = jnp.max(s, axis=1, keepdims=True)
            p = jnp.exp(s - top)
            total = jnp.sum(p, axis=1, keepdims=True)
            out = nn(p.astype(jnp.bfloat16), qkv[:span, 2 * lanes + at : 2 * lanes + at + 128]) / total
            logs = jnp.where(lane == head, top + jnp.log(total), logs)
            if side == 0:
                kept = jnp.where(mine, out, 0.0)
            else:
                kept = jnp.where(mine, out, kept)
            o[part, at : at + 128] = kept
        lse[part, :] = logs
        osort[2 * i] = o[part, :][:blk].astype(jnp.bfloat16)
        osort[2 * i + 1] = o[part, :][blk:].astype(jnp.bfloat16)

    mine_at = 2 * z + k
    remote(wo_s.at[over], wo_s.at[over], v_send.at[0], v_recv.at[0], own, over).wait_recv()
    v_on.start()

    def o_copy(ctx):
        return remote(osend.at[ctx], orecv.at[mine_at], o_send.at[ctx], o_recv.at[mine_at], ctx, 2 * y + xx)

    for ctx in range(blocks):
        alone = jnp.logical_and(same, ctx == own)
        osend[ctx] = osort[order[ctx]]

        @pl.when(jnp.logical_not(alone))
        def _():
            o_copy(ctx).start()

        @pl.when(alone)
        def _():
            orecv[mine_at] = osend[ctx]

    for src in range(blocks):

        @pl.when(jnp.logical_not(jnp.logical_and(same, src == mine_at)))
        def _():
            remote(osend.at[0], orecv.at[src], o_send.at[0], o_recv.at[src], 2 * (src // 2) + k, 2 * y + src % 2).wait_recv()

    ob[...] = orecv[...]
    remote(wo_s.at[beside], wo_s.at[beside], v_send.at[1], v_recv.at[1], own, beside).wait_recv()
    remote(wo_s.at[corner], wo_s.at[corner], v_send.at[2], v_recv.at[2], own, beside).wait_recv()
    wo[...] = wo_s[...]
    total, low = post_attention(orecv[...], x[...], wo_s[...], small[1:2, :].astype(jnp.float32))
    hst[...] = total
    ub[...] = low
    for zz in range(depth):

        @pl.when(sent(zz))
        def _():
            n1_copy(zz).wait_send()

        @pl.when(passed(zz))
        def _():
            pass_copy(zz).wait_send()

        forward_copy(zz).wait_send()
    for index in range(3):
        w_copy(index).wait_send()
    v_far.wait_send()
    v_near.wait_send()
    v_on.wait_send()
    for ctx in range(blocks):

        @pl.when(jnp.logical_not(jnp.logical_and(same, ctx == own)))
        def _():
            o_copy(ctx).wait_send()


def attn_forward(layer, order, inv, x, small, wq, cosine, sine, wo, number):
    count, width = x.shape
    blocks, blk = order.shape[0], count // 2
    packs, inner = width // wo.shape[1], wo.shape[1]
    lanes = -(-inner // 128) * 128
    seq = blocks * blk
    vm = pl.BlockSpec(memory_space=pltpu.VMEM)
    sm = pl.BlockSpec(memory_space=pltpu.SMEM)
    bf = jnp.bfloat16
    dma = pltpu.SemaphoreType.DMA
    return pl.pallas_call(
        attn_fwd_kernel,
        grid=(1,),
        out_shape=[
            shape_of((seq, width), bf),
            shape_of((seq, 3 * lanes), bf),
            shape_of((seq, lanes), jnp.float32),
            shape_of((seq, 128), jnp.float32),
            shape_of((blocks, blk, lanes), bf),
            shape_of((count, width), jnp.float32),
            shape_of((count, width), bf),
            shape_of((width, 3 * lanes), bf),
            shape_of((packs, inner, width), bf),
        ],
        in_specs=[sm, sm, vm, vm]
        + [pl.BlockSpec((1, 3, inner, width), lambda _: (layer, 0, 0, 0)), vm, vm]
        + [pl.BlockSpec((1, inner, width), lambda _: (layer, 0, 0))],
        out_specs=[vm] * 9,
        scratch_shapes=[
            pltpu.VMEM((2, blk, width), bf),
            pltpu.VMEM((blocks, blk, width), bf),
            pltpu.VMEM((blocks, blk, lanes), bf),
            pltpu.VMEM((blocks, blk, lanes), bf),
            pltpu.VMEM((blocks, blk, lanes), bf),
            pltpu.VMEM((2, inner, 3 * lanes), bf),
            pltpu.VMEM((width, 3 * lanes), bf),
            pltpu.VMEM((packs, inner, width), bf),
        ]
        + [dma((blocks // 2,))] * 5
        + [dma((blocks,))] * 2
        + [dma((3,))] * 4,
        compiler_params=params_of(collective_id=number, has_side_effects=True),
        cost_estimate=BRIEF,
        name="attn_fwd",
    )(order, inv, x, small, wq, cosine, sine, wo)


def attn_bwd_kernel(
    order, inv, n1s, w, cosine, sine, qkv, o, lse, go, ghst, x, small, gsmall, gwo,
    gx, gm, dense,
    gor, gos, grads, acc, gns, sib_out, sib_in, gn_out, gnr, gw, gw_in, both, both_in, wo_in, wo_both, wo_over, probs,
    o_send, o_recv, s_send, s_recv, g_send, g_recv, r_send, r_recv, w_send, w_recv,
):
    blocks, blk, width = grads.shape
    lanes = o.shape[1]
    seq = blocks * blk
    step = 2 * blk
    zero = jnp.asarray(0, jnp.bfloat16)
    own = lax.axis_index("ctx")
    z, xx, y, k = place()
    depth = blocks // 2
    same = xx == k

    barrier, others = greet_plane(blocks, across=True)
    acc[...] = jnp.zeros_like(acc)
    pl.semaphore_wait(barrier, others)

    def go_copy(unit):
        return remote(go.at[unit], gor.at[own], o_send.at[unit], o_recv.at[own], 2 * (unit // 2) + k, 2 * y + unit % 2)

    for unit in range(blocks):
        alone = jnp.logical_and(same, unit == 2 * z + k)

        @pl.when(jnp.logical_not(alone))
        def _():
            go_copy(unit).start()

        @pl.when(alone)
        def _():
            gor[own] = go[unit]

    def wo_copy(half):
        return remote(
            gwo.at[2 * half + 1 - k], wo_in.at[half], w_send.at[half], w_recv.at[half], own, 2 * y + 1 - k
        )

    wo_far = remote(wo_both.at[1 - y], wo_over, w_send.at[2], w_recv.at[2], own, 2 * (1 - y) + k)
    wo_copy(0).start()
    wo_copy(1).start()
    lane = lax.broadcasted_iota(jnp.int32, (step, 128), 1)
    for i in range(seq // step):
        part = slice(i * step, (i + 1) * step)
        span = (i + 1) * step
        seen = lax.broadcasted_iota(jnp.int32, (step, span), 1) <= (
            lax.broadcasted_iota(jnp.int32, (step, span), 0) + i * step
        )
        for head in range(GROUP_HEADS):
            at = head // 2 * 128
            q = jnp.where(lane // 64 == head % 2, qkv[part, at : at + 128], zero)
            s = nt(q, qkv[:span, lanes + at : lanes + at + 128])
            p = jnp.exp(jnp.where(seen, s, -1e30) - lse[part, head : head + 1])
            probs[head, part, :span] = jnp.where(seen, p, 0.0)
    for ctx in range(blocks):

        @pl.when(jnp.logical_not(jnp.logical_and(same, ctx == own)))
        def _():
            remote(go.at[0], gor.at[ctx], o_send.at[0], o_recv.at[ctx], ctx, 2 * y + xx).wait_recv()

    for half in range(2):
        wo_copy(half).wait_recv()
        total = gwo[2 * half + k].astype(jnp.float32) + wo_in[half].astype(jnp.float32)
        wo_both[half] = total.astype(jnp.bfloat16)
    wo_far.start()
    for b in range(blocks):
        gos[b * blk : (b + 1) * blk, :] = gor[inv[b]]
    for i in range(seq // step):
        part = slice(i * step, (i + 1) * step)
        span = (i + 1) * step
        key_lane = lax.broadcasted_iota(jnp.int32, (span, 128), 1)
        for head in range(GROUP_HEADS):
            tile, side = head // 2, head % 2
            at = tile * 128
            mine = lane // 64 == side
            q = jnp.where(mine, qkv[part, at : at + 128], zero)
            g = jnp.where(mine, gos[part, at : at + 128], zero)
            keys = qkv[:span, lanes + at : lanes + at + 128]
            values = qkv[:span, 2 * lanes + at : 2 * lanes + at + 128]
            delta = jnp.sum(g.astype(jnp.float32) * o[part, at : at + 128], axis=1, keepdims=True)
            p = probs[head, part, :span]
            ds = (p * (nt(g, values) - delta)).astype(jnp.bfloat16)
            acc[:span, 2 * lanes + at : 2 * lanes + at + 128] += tn(p.astype(jnp.bfloat16), g)
            acc[:span, lanes + at : lanes + at + 128] += tn(ds, q)
            acc[part, at : at + 128] += nn(ds, jnp.where(key_lane // 64 == side, keys, zero))
    for b in range(blocks):
        part = slice(b * blk, (b + 1) * blk)
        cos2 = jnp.concatenate([cosine[part, :]] * (lanes // 128), axis=1)
        sin2 = jnp.concatenate([sine[part, :]] * (lanes // 128), axis=1)
        grads[b, :, :lanes] = spin(acc[part, :lanes] * HEAD_DIM**-0.5, cos2, -sin2).astype(jnp.bfloat16)
        grads[b, :, lanes : 2 * lanes] = spin(acc[part, lanes : 2 * lanes], cos2, -sin2).astype(jnp.bfloat16)
        grads[b, :, 2 * lanes :] = acc[part, 2 * lanes :].astype(jnp.bfloat16)

    def sib_copy(zz):
        return remote(sib_out.at[zz], sib_in.at[zz], s_send.at[zz], s_recv.at[zz], own, 2 * y + 1 - k)

    def gn_copy(zz):
        return remote(gn_out.at[zz], gnr.at[z], g_send.at[zz], g_recv.at[z], 2 * zz + k, 2 * y + xx)

    gain = small[0:1, :].astype(jnp.float32)
    ggain = jnp.zeros((1, width), jnp.float32)
    for b in range(blocks):
        gns[b] = nt(grads[b], w[...])
        ggain = ggain + jnp.sum(gns[b] * n1s[b * blk : (b + 1) * blk, :].astype(jnp.float32), axis=0, keepdims=True)
    for zz in range(depth):
        sib_out[zz] = gns[order[2 * zz + 1 - k]].astype(jnp.bfloat16)
        sib_copy(zz).start()
    for zz in range(depth):
        sib_copy(zz).wait_recv()
        alone = jnp.logical_and(same, zz == z)
        gn_out[zz] = (gns[order[2 * zz + k]] + sib_in[zz].astype(jnp.float32)).astype(jnp.bfloat16)

        @pl.when(jnp.logical_not(alone))
        def _():
            gn_copy(zz).start()

        @pl.when(alone)
        def _():
            gnr[z] = gn_out[zz]

    packs, inner = gwo.shape[0], gwo.shape[1]
    sums = jnp.concatenate([ggain / gain, gsmall[...]], axis=0)
    sums = jnp.concatenate([sums, jnp.zeros((128 - sums.shape[0], width), jnp.float32)], axis=0)
    gw[:, :128] = jnp.transpose(sums).astype(jnp.bfloat16)
    gw[:, 128 + 3 * inner :] = jnp.zeros((width, gw.shape[1] - 128 - 3 * inner), jnp.bfloat16)
    for i in range(width // 256):
        part = slice(i * 256, (i + 1) * 256)
        piece = tn(n1s[:, part], grads[...].reshape(seq, 3 * lanes)).astype(jnp.bfloat16)
        for c in range(3):
            gw[part, 128 + c * inner : 128 + (c + 1) * inner] = piece[:, c * lanes : c * lanes + inner]

    def rows_of(f):
        return pl.ds(pl.multiple_of(f * inner, inner), inner)

    def home_copy(half):
        rows = gw.at[rows_of(2 * half + 1 - k), :]
        return remote(rows, gw_in.at[half], r_send.at[half], r_recv.at[half], own, 2 * y + 1 - k)

    for half in range(2):
        home_copy(half).start()
    for half in range(2):
        home_copy(half).wait_recv()
        kept, came = gw[rows_of(2 * half + k), :], gw_in[half]
        both[half, :, :128] = (kept[:, :128].astype(jnp.float32) + came[:, :128].astype(jnp.float32)).astype(jnp.bfloat16)
        heads = slice(128, 128 + 3 * inner)
        for core in range(2):

            @pl.when(k == core)
            def _():
                both[half, :, 128 + core * 3 * inner : 128 + (core + 1) * 3 * inner] = kept[:, heads]
                both[half, :, 128 + (1 - core) * 3 * inner : 128 + (2 - core) * 3 * inner] = came[:, heads]

    over = remote(both.at[1 - y], both_in, r_send.at[2], r_recv.at[2], own, 2 * (1 - y) + k)
    over.start()
    for zz in range(depth):

        @pl.when(jnp.logical_not(jnp.logical_and(same, zz == z)))
        def _():
            remote(gn_out.at[0], gnr.at[zz], g_send.at[0], g_recv.at[zz], 2 * zz + k, 2 * y + xx).wait_recv()

    halves = []
    for h in range(2):
        total = gnr[h * (depth // 2)].astype(jnp.float32)
        for zz in range(1, depth // 2):
            total = total + gnr[h * (depth // 2) + zz].astype(jnp.float32)
        halves.append(total)
    gn = jnp.concatenate(halves, axis=0)
    values = x[...]
    factor = rms_factor(values)
    base = values * factor
    gb = gn * gain
    grad = ghst[...] + factor * (gb - base * jnp.mean(gb * base, axis=-1, keepdims=True))
    gx[...] = grad
    gm[...] = grad.astype(jnp.bfloat16)
    wo_far.wait_recv()
    edge = both.shape[2]
    dense[:, edge:] = (wo_both[y].astype(jnp.float32) + wo_over[...].astype(jnp.float32)).astype(jnp.bfloat16)
    over.wait_recv()
    dense[:, :edge] = (both[y].astype(jnp.float32) + both_in[...].astype(jnp.float32)).astype(jnp.bfloat16)
    for half in range(2):
        home_copy(half).wait_send()
        wo_copy(half).wait_send()
    wo_far.wait_send()
    over.wait_send()
    for unit in range(blocks):

        @pl.when(jnp.logical_not(jnp.logical_and(same, unit == 2 * z + k)))
        def _():
            go_copy(unit).wait_send()

    for zz in range(depth):
        sib_copy(zz).wait_send()

        @pl.when(jnp.logical_not(jnp.logical_and(same, zz == z)))
        def _():
            gn_copy(zz).wait_send()


def attn_backward(order, inv, n1s, w, cosine, sine, qkv, o, lse, go, ghst, x, small, gsmall, gwo, number):
    blocks, blk, lanes = go.shape
    seq, width = n1s.shape
    count = x.shape[0]
    packs, inner = gwo.shape[0], gwo.shape[1]
    depth = blocks // 2
    vm = pl.BlockSpec(memory_space=pltpu.VMEM)
    sm = pl.BlockSpec(memory_space=pltpu.SMEM)
    bf = jnp.bfloat16
    dma = pltpu.SemaphoreType.DMA
    return pl.pallas_call(
        attn_bwd_kernel,
        out_shape=[
            shape_of((count, width), jnp.float32),
            shape_of((count, width), bf),
            shape_of((inner, 128 + 6 * inner + width), bf),
        ],
        in_specs=[sm] * 2 + [vm] * 13,
        out_specs=[vm] * 3,
        scratch_shapes=[
            pltpu.VMEM((blocks, blk, lanes), bf),
            pltpu.VMEM((seq, lanes), bf),
            pltpu.VMEM((blocks, blk, 3 * lanes), bf),
            pltpu.VMEM((seq, 3 * lanes), jnp.float32),
            pltpu.VMEM((blocks, blk, width), jnp.float32),
            pltpu.VMEM((depth, blk, width), bf),
            pltpu.VMEM((depth, blk, width), bf),
            pltpu.VMEM((depth, blk, width), bf),
            pltpu.VMEM((depth, blk, width), bf),
            pltpu.VMEM((packs * inner, 3 * lanes), bf),
            pltpu.VMEM((2, inner, 3 * lanes), bf),
            pltpu.VMEM((2, inner, 128 + 6 * inner), bf),
            pltpu.VMEM((inner, 128 + 6 * inner), bf),
            pltpu.VMEM((2, inner, width), bf),
            pltpu.VMEM((2, inner, width), bf),
            pltpu.VMEM((inner, width), bf),
            pltpu.VMEM((GROUP_HEADS, seq, seq), jnp.float32),
        ]
        + [dma((blocks,))] * 2
        + [dma((depth,))] * 4
        + [dma((3,))] * 4,
        compiler_params=params_of(collective_id=number, has_side_effects=True),
        cost_estimate=BRIEF,
        name="attn_bwd",
    )(order, inv, n1s, w, cosine, sine, qkv, o, lse, go, ghst, x, small, gsmall, gwo)


def routing(raw, before, routes):
    count = raw.shape[1]
    ids = lax.broadcasted_iota(jnp.int32, (16, count), 0)
    logits = raw + before
    first, second = ids == routes[0:1], ids == routes[1:2]
    z0 = jnp.sum(jnp.where(first, logits, 0.0), axis=0, keepdims=True)
    z1 = jnp.sum(jnp.where(second, logits, 0.0), axis=0, keepdims=True)
    top = jnp.maximum(z0, z1)
    e0, e1 = jnp.exp(z0 - top), jnp.exp(z1 - top)
    total = e0 + e1
    coef = jnp.where(first, e0 / total, 0.0) + jnp.where(second, e1 / total, 0.0)
    hits = jnp.where(first | second, 1.0, 0.0)
    upto = lax.broadcasted_iota(jnp.int32, (count, count), 0) <= lax.broadcasted_iota(jnp.int32, (count, count), 1)
    place = nn(hits.astype(jnp.bfloat16), jnp.where(upto, 1.0, 0.0).astype(jnp.bfloat16)) - 1.0
    slot = jnp.where(hits > 0, place, -1.0)
    return jnp.concatenate([raw, coef, slot[:NF], logits], axis=0)


def one_hot(slot):
    count = slot.shape[1]
    ids = lax.broadcasted_iota(jnp.int32, (NF, MOST, count), 1)
    hit = ids == slot.astype(jnp.int32)[:, None, :]
    return jnp.where(hit, 1.0, 0.0).reshape(NF * MOST, count)


def slot_values(hot, rows):
    count = rows.shape[1]
    wide = jnp.broadcast_to(rows[:, None, :], (NF, MOST, count)).reshape(NF * MOST, count)
    return jnp.sum(hot * wide, axis=1, keepdims=True)


def swap_rows(own, rows, send, recv, forward_send, forward_recv):
    ctx = lax.axis_index("ctx")
    _, _, y, k = place()
    beside, across = 2 * y + 1 - k, 2 * (1 - y) + k
    far = remote(own, rows.at[2], send.at[0], recv.at[0], ctx, across)
    near = remote(own, rows.at[1], send.at[1], recv.at[1], ctx, beside)
    onward = remote(rows.at[2], rows.at[3], forward_send, forward_recv, ctx, beside)
    far.start()
    near.start()
    return near, far, onward


def sum_rows(parts, beside_in, mid, across_in, send, recv):
    ctx = lax.axis_index("ctx")
    _, _, y, k = place()
    beside, across = 2 * y + 1 - k, 2 * (1 - y) + k
    first = remote(parts.at[3], beside_in.at[1], send.at[0], recv.at[0], ctx, beside)
    second = remote(parts.at[1], beside_in.at[0], send.at[1], recv.at[1], ctx, beside)
    third = remote(mid, across_in, send.at[2], recv.at[2], ctx, across)
    return first, second, third


def ffn_fwd_kernel(
    ub, hst, small, routes, before, wgu, wd,
    ubf, table, ext, x_next,
    rows_s, hot_s, x_s, y_s, coef_s, parts, beside_in, mid, across_in,
    a_send, a_recv, r_send, r_recv,
):
    e = pl.program_id(0)
    packs = ubf.shape[0]
    count, width = ub.shape
    router = small[2 + NC :, :]

    def gathers():
        return swap_rows(ub, rows_s, a_send, a_recv, a_send.at[2], a_recv.at[2])

    def sums():
        return sum_rows(parts, beside_in, mid, across_in, r_send, r_recv)

    @pl.when(e == 0)
    def _():
        barrier, others = greet_packs()
        rows_s[0] = ub[...]

        def prepare(d):
            rows = routing(nt(router, rows_s[d]), before[d], routes[d])
            table[d] = rows
            hot = one_hot(rows[SLOT : SLOT + NF])
            coef_s[d] = slot_values(hot, rows[COEF : COEF + NF])
            hot_low = hot.astype(jnp.bfloat16)
            hot_s[d] = hot_low
            x = nn(hot_low, rows_s[d]).astype(jnp.bfloat16)
            for n in range(NF):
                x_s[n, d * MOST : (d + 1) * MOST, :] = x[n * MOST : (n + 1) * MOST]

        pl.semaphore_wait(barrier, others)
        near, far, onward = gathers()
        prepare(0)
        near.wait_recv()
        prepare(1)
        far.wait_recv()
        onward.start()
        prepare(2)
        onward.wait_recv()
        prepare(3)
        ubf[...] = rows_s[...]
        ext[:count, :] = ub[...]
        rows = table[0]
        ext[count:, :] = jnp.zeros((16, width), jnp.bfloat16)
        ext[count:, :count] = rows[COEF : COEF + 16].astype(jnp.bfloat16)
        slots = jnp.concatenate([rows[SLOT : SLOT + NF], jnp.zeros((16 - NF, count), jnp.float32)], axis=0)
        ext[count:, count : 2 * count] = slots.astype(jnp.bfloat16)
        near.wait_send()
        far.wait_send()
        onward.wait_send()

    x = x_s[e]
    gate, up = nn(x, wgu[0, 0, 0]), nn(x, wgu[0, 0, 1])
    hid = (gate * jax.nn.sigmoid(gate) * up).astype(jnp.bfloat16)
    out = nn(hid, wd[0, 0])
    at = pl.ds(pl.multiple_of(e * MOST, MOST), MOST)
    for d in range(packs):
        y_s[d, at, :] = (out[d * MOST : (d + 1) * MOST] * coef_s[d, at, :]).astype(jnp.bfloat16)

    @pl.when(e == NF - 1)
    def _():
        first, second, third = sums()
        parts[3] = tn(hot_s[3], y_s[3]).astype(jnp.bfloat16)
        first.start()
        parts[1] = tn(hot_s[1], y_s[1]).astype(jnp.bfloat16)
        second.start()
        away = tn(hot_s[2], y_s[2])
        first.wait_recv()
        mid[...] = (away + beside_in[1].astype(jnp.float32)).astype(jnp.bfloat16)
        third.start()
        home = tn(hot_s[0], y_s[0])
        _, _, scale_u, scale_c = mixing_rows(table[0])
        columns = to_columns([scale_u] + scale_c)
        values = hst[...]
        moe = home + columns[0] * ((values * rms_factor(values)) * small[1:2, :].astype(jnp.float32))
        for c in range(NC):
            moe = moe + columns[1 + c] * small[2 + c : 3 + c, :].astype(jnp.float32)
        second.wait_recv()
        moe = moe + beside_in[0].astype(jnp.float32)
        third.wait_recv()
        x_next[...] = values + (moe + across_in[...].astype(jnp.float32))
        first.wait_send()
        second.wait_send()
        third.wait_send()


def whole_spec(dims):
    return pl.BlockSpec(dims, lambda *_: (0,) * len(dims))


def exchange_scratch(packs, count, width):
    bf = jnp.bfloat16
    return [
        pltpu.VMEM((packs, count, width), bf),
        pltpu.VMEM((2, count, width), bf),
        pltpu.VMEM((count, width), bf),
        pltpu.VMEM((count, width), bf),
    ]


def ffn_forward(layer, ub, hst, small, routes, before, wgu, wd, number):
    count, width = ub.shape
    packs = routes.shape[0]
    hidden = wd.shape[2]
    bf = jnp.bfloat16
    outs = [
        shape_of((packs, count, width), bf),
        shape_of((packs, ROUT, count), jnp.float32),
        shape_of((count + 16, width), bf),
        shape_of((count, width), jnp.float32),
    ]
    return pl.pallas_call(
        ffn_fwd_kernel,
        grid=(NF,),
        out_shape=outs,
        in_specs=[whole_spec(a.shape) for a in (ub, hst, small, routes, before)]
        + [
            pl.BlockSpec((1, 1, 2, width, hidden), lambda e: (layer, e, 0, 0, 0)),
            pl.BlockSpec((1, 1, hidden, width), lambda e: (layer, e, 0, 0)),
        ],
        out_specs=[whole_spec(a.shape) for a in outs],
        scratch_shapes=[
            pltpu.VMEM((packs, count, width), bf),
            pltpu.VMEM((packs, NF * MOST, count), bf),
            pltpu.VMEM((NF, packs * MOST, width), bf),
            pltpu.VMEM((packs, NF * MOST, width), bf),
            pltpu.VMEM((packs, NF * MOST, 1), jnp.float32),
        ]
        + exchange_scratch(packs, count, width)
        + [pltpu.SemaphoreType.DMA((3,))] * 4,
        compiler_params=params_of(collective_id=number, has_side_effects=True),
        cost_estimate=BRIEF,
        name="ffn_fwd",
    )(ub, hst, small, routes, before, wgu, wd)


def silu_parts(gate, up, ghid):
    sig = jax.nn.sigmoid(gate)
    act = gate * sig
    dg = (ghid * up * sig * (1.0 + gate * (1.0 - sig))).astype(jnp.bfloat16)
    du = (ghid * act).astype(jnp.bfloat16)
    return act * up, dg, du


def ffn_bwd_kernel(
    gm, gx, ubf, table, hst, small, routes, gprev, wo, ob, wgu, wd,
    ghst, go, gwo, gsmall, glog,
    rows_s, hot_s, x_s, g_s, y_s, coef_s, gc_s, gcoef, gcoef_in, parts, beside_in, mid, across_in,
    a_send, a_recv, r_send, r_recv, c_send, c_recv,
):
    e = pl.program_id(0)
    packs = ubf.shape[0]
    ctx = lax.axis_index("ctx")
    _, _, y, k = place()
    peers = [None, 2 * y + 1 - k, 2 * (1 - y) + k, 2 * (1 - y) + 1 - k]

    def gathers():
        return swap_rows(gm, rows_s, a_send, a_recv, a_send.at[2], a_recv.at[2])

    def sums():
        return sum_rows(parts, beside_in, mid, across_in, r_send, r_recv)

    @pl.when(e == 0)
    def _():
        barrier, others = greet_packs()
        rows_s[0] = gm[...]

        def prepare(d):
            hot = one_hot(table[d, SLOT : SLOT + NF, :])
            coef_s[d] = slot_values(hot, table[d, COEF : COEF + NF, :])
            hot_low = hot.astype(jnp.bfloat16)
            hot_s[d] = hot_low
            x = nn(hot_low, ubf[d]).astype(jnp.bfloat16)
            for n in range(NF):
                x_s[n, d * MOST : (d + 1) * MOST, :] = x[n * MOST : (n + 1) * MOST]

        def spread(d):
            g = nn(hot_s[d], rows_s[d]).astype(jnp.bfloat16)
            for n in range(NF):
                g_s[n, d * MOST : (d + 1) * MOST, :] = g[n * MOST : (n + 1) * MOST]

        pl.semaphore_wait(barrier, others)
        near, far, onward = gathers()
        for d in range(packs):
            prepare(d)
        spread(0)
        near.wait_recv()
        far.wait_recv()
        onward.start()
        spread(1)
        spread(2)
        onward.wait_recv()
        spread(3)
        near.wait_send()
        far.wait_send()
        onward.wait_send()

    x = x_s[e]
    at = pl.ds(pl.multiple_of(e * MOST, MOST), MOST)
    coef = jnp.concatenate([coef_s[d, at, :] for d in range(packs)], axis=0)
    gate, up = nn(x, wgu[0, 0, 0]), nn(x, wgu[0, 0, 1])
    ghid = nt(g_s[e], wd[0, 0])
    hid, dg, du = silu_parts(gate, up, ghid * coef)
    dots = jnp.sum(hid * ghid, axis=1, keepdims=True)
    out = nt(dg, wgu[0, 0, 0]) + nt(du, wgu[0, 0, 1])
    for d in range(packs):
        y_s[d, at, :] = out[d * MOST : (d + 1) * MOST].astype(jnp.bfloat16)
        gc_s[d, at, :] = dots[d * MOST : (d + 1) * MOST]

    @pl.when(e == NF - 1)
    def _():
        first, second, third = sums()

        def coef_copy(d):
            return remote(gcoef.at[d], gcoef_in.at[d - 1], c_send.at[d - 1], c_recv.at[d - 1], ctx, peers[d])

        parts[3] = tn(hot_s[3], y_s[3]).astype(jnp.bfloat16)
        first.start()
        parts[1] = tn(hot_s[1], y_s[1]).astype(jnp.bfloat16)
        second.start()
        for d in range(packs):
            wide = hot_s[d].astype(jnp.float32) * gc_s[d]
            gcoef[d] = jnp.sum(wide.reshape(NF, MOST, wide.shape[1]), axis=1)
            if d > 0:
                coef_copy(d).start()
        away = tn(hot_s[2], y_s[2])
        first.wait_recv()
        mid[...] = (away + beside_in[1].astype(jnp.float32)).astype(jnp.bfloat16)
        third.start()
        home = tn(hot_s[0], y_s[0])
        second.wait_recv()
        home = home + beside_in[0].astype(jnp.float32)
        total = gcoef[0]
        for d in range(1, packs):
            coef_copy(d).wait_recv()
            total = total + gcoef_in[d - 1]
        third.wait_recv()
        home = home + across_in[...].astype(jnp.float32)
        results = middle(
            gx[...], home, total, table[0], routes[...], gprev[...], hst[...], ubf[0],
            small[...], wo[...], ob[...],
        )
        for ref, value in zip((ghst, go, gwo, gsmall, glog), results):
            ref[...] = value
        first.wait_send()
        second.wait_send()
        third.wait_send()
        for d in range(1, packs):
            coef_copy(d).wait_send()


def ffn_backward(layer, gm, gx, ubf, table, hst, small, routes, gprev, wo, ob, wgu, wd, number):
    packs, count, width = ubf.shape
    hidden = wd.shape[2]
    bf, f32 = jnp.bfloat16, jnp.float32
    outs = [
        shape_of((count, width), f32),
        shape_of(ob.shape, bf),
        shape_of(wo.shape, bf),
        shape_of((1 + NC + 16, width), f32),
        shape_of((16, count), f32),
    ]
    args = (gm, gx, ubf, table, hst, small, routes, gprev, wo, ob)
    dma = pltpu.SemaphoreType.DMA
    return pl.pallas_call(
        ffn_bwd_kernel,
        grid=(NF,),
        out_shape=outs,
        in_specs=[whole_spec(a.shape) for a in args]
        + [
            pl.BlockSpec((1, 1, 2, width, hidden), lambda e: (layer, e, 0, 0, 0)),
            pl.BlockSpec((1, 1, hidden, width), lambda e: (layer, e, 0, 0)),
        ],
        out_specs=[whole_spec(a.shape) for a in outs],
        scratch_shapes=[
            pltpu.VMEM((packs, count, width), bf),
            pltpu.VMEM((packs, NF * MOST, count), bf),
            pltpu.VMEM((NF, packs * MOST, width), bf),
            pltpu.VMEM((NF, packs * MOST, width), bf),
            pltpu.VMEM((packs, NF * MOST, width), bf),
            pltpu.VMEM((packs, NF * MOST, 1), f32),
            pltpu.VMEM((packs, NF * MOST, 1), f32),
            pltpu.VMEM((packs, NF, count), f32),
            pltpu.VMEM((packs - 1, NF, count), f32),
        ]
        + exchange_scratch(packs, count, width)
        + [dma((3,))] * 6,
        compiler_params=params_of(collective_id=number, has_side_effects=True),
        cost_estimate=BRIEF,
        name="ffn_bwd",
    )(*args, wgu, wd)


PACK = 80


def pack_kernel(counts, bases, totals, tail, ext, gm, out, buf, carry, blank, sems):
    step = pl.program_id(0)
    some, count, width = gm.shape

    @pl.when(step == 0)
    def _():
        carry[...] = jnp.zeros_like(carry)
        blank[...] = jnp.zeros_like(blank)

    def whole_groups(d, e):
        at = d * NF + e
        return (bases[at] % 16 + counts[at]) // 16

    def each_copy(block, what):
        for i in range(some):
            for e in range(NF):
                groups = whole_groups(block * some + i, e)
                start = pl.multiple_of(bases[(block * some + i) * NF + e] // 16 * 16, 16)
                for n in range(1, PACK // 16):

                    @pl.when(groups == n)
                    def _():
                        source = buf.at[block % 2, i, e, pl.ds(0, 16 * n), :]
                        what(pltpu.make_async_copy(source, out.at[e, pl.ds(start, 16 * n), :], sems.at[block % 2, i, e]))

    def begin(copy):
        copy.start()

    def end(copy):
        copy.wait()

    @pl.when(step >= 2)
    def _():
        each_copy(step - 2, end)

    ids = lax.broadcasted_iota(jnp.int32, (PACK, count), 0)
    side = step % 2
    for i in range(some):
        d = step * some + i
        rows = tail[i].astype(jnp.float32)
        slot = rows[:NF, count : 2 * count].astype(jnp.int32)
        slot = jnp.where(slot < 0, -PACK, slot)
        hot, weighted = [], []
        for e in range(NF):
            hit = ids == slot[e : e + 1] + bases[d * NF + e] % 16
            hot.append(jnp.where(hit, 1.0, 0.0).astype(jnp.bfloat16))
            weighted.append(jnp.where(hit, rows[e : e + 1, :count], 0.0).astype(jnp.bfloat16))
        low = nn(jnp.concatenate(hot, axis=0), ext[i, :count, :]).astype(jnp.bfloat16)
        low_g = nn(jnp.concatenate(weighted, axis=0), gm[i]).astype(jnp.bfloat16)
        for lanes, values in ((slice(0, width), low), (slice(width, 2 * width), low_g)):
            for e in range(NF):
                buf[side, i, e, :, lanes] = values[e * PACK : (e + 1) * PACK]
    for i in range(some):
        for e in range(NF):
            buf[side, i, e, :16, :] += carry[e]
            group = pl.multiple_of(whole_groups(step * some + i, e) * 16, 16)
            carry[e] = buf[side, i, e, pl.ds(group, 16), :]
    each_copy(step, begin)

    @pl.when(step == pl.num_programs(0) - 1)
    def _():
        last = pl.num_programs(0)
        each_copy(last - 2, end)
        each_copy(last - 1, end)
        copies = []
        for e in range(NF):
            start = pl.multiple_of(totals[e] // 16 * 16, 16)
            copies.append(pltpu.make_async_copy(carry.at[e], out.at[e, pl.ds(start, 16), :], sems.at[0, 0, e]))
            rest = out.at[e, pl.ds(start + 16, blank.shape[0]), :]
            copies.append(pltpu.make_async_copy(blank, rest, sems.at[1, 0, e]))
        for copy in copies:
            copy.start()
        for copy in copies:
            copy.wait()


def expert_counts(ext):
    count = ext.shape[2] // 3
    slot = ext[:, ext.shape[1] - 16 : ext.shape[1] - 16 + NF, count : 2 * count].astype(jnp.float32)
    counts = (jnp.max(slot, axis=2) + 1.0).astype(jnp.int32)
    upto = jnp.cumsum(counts, axis=0)
    return counts.reshape(-1), (upto - counts).reshape(-1), upto[-1]


def pack_rows(numbers, ext, gm):
    devices, count, width = gm.shape
    some, blank = 4, 256
    bf = jnp.bfloat16
    return pl.pallas_call(
        pack_kernel,
        grid_spec=pltpu.PrefetchScalarGridSpec(
            num_scalar_prefetch=3,
            grid=(devices // some,),
            in_specs=[
                pl.BlockSpec((some, 16, width), lambda d, *_: (d, count // 16, 0)),
                pl.BlockSpec((some,) + ext.shape[1:], lambda d, *_: (d, 0, 0)),
                pl.BlockSpec((some, count, width), lambda d, *_: (d, 0, 0)),
            ],
            out_specs=pl.BlockSpec(memory_space=pl.ANY),
            scratch_shapes=[
                pltpu.VMEM((2, some, NF, PACK, 2 * width), bf),
                pltpu.VMEM((NF, 16, 2 * width), bf),
                pltpu.VMEM((blank, 2 * width), bf),
                pltpu.SemaphoreType.DMA((2, some, NF)),
            ],
        ),
        out_shape=shape_of((NF, devices * MOST + 16 + blank, 2 * width), bf),
        compiler_params=params_of(),
        cost_estimate=BRIEF,
        name="pack_rows",
    )(*numbers, ext, ext, gm)


def dw_kernel(first, totals, packed, wgu, wd, *refs):
    dgu, dd, pair_s, hid_s = refs[-4:]
    hidden = hid_s.shape[1]
    total = totals[first + pl.program_id(0)]
    width = packed.shape[2] // 2
    chunk = 1024

    def pieces(part):
        xs, gs = packed[0, part, :width], packed[0, part, width:]
        hid, dg, du = silu_parts(nn(xs, wgu[0, 0, 0]), nn(xs, wgu[0, 0, 1]), nt(gs, wd[0, 0]))
        hid_s[part, :] = hid.astype(jnp.bfloat16)
        pair_s[part, :hidden] = dg
        pair_s[part, hidden:] = du

    def chunk_of(i, _):
        pieces(pl.ds(pl.multiple_of(i * chunk, chunk), chunk))
        return 0

    needed = jnp.maximum((total + 255) // 256, 1)
    lax.fori_loop(0, needed // 4, chunk_of, 0)

    @pl.when(needed % 4 >= 2)
    def _():
        pieces(pl.ds(pl.multiple_of(needed // 4 * chunk, 512), 512))

    @pl.when(needed % 2 == 1)
    def _():
        pieces(pl.ds(pl.multiple_of((needed - 1) * 256, 256), 256))

    for size in range(1, hid_s.shape[0] // 256 + 1):

        @pl.when(needed == size)
        def _():
            rows = 256 * size

            def inputs(i, _):
                part = pl.ds(pl.multiple_of(i * 384, 384), 384)
                xs = packed[0, :rows, part]
                both = tn(xs, pair_s[:rows, :])
                dgu[0, 0, 0, part, :] = both[:, :hidden]
                dgu[0, 0, 1, part, :] = both[:, hidden:]
                return 0

            lax.fori_loop(0, width // 384, inputs, 0)

            def outputs(i, _):
                part = pl.ds(pl.multiple_of(i * 512, 512), 512)
                dd[0, 0, part, :] = tn(hid_s[:rows, part], packed[0, :rows, width:])
                return 0

            lax.fori_loop(0, hid_s.shape[1] // 512, outputs, 0)


def weight_grads(layer, first, last, totals, packed, wgu, wd, earlier):
    _, rows, both = packed.shape
    hidden, width = wd.shape[2], wd.shape[3]
    gu_spec = pl.BlockSpec((1, 1, 2, width, hidden), lambda e, *_: (layer, e + first, 0, 0, 0))
    d_spec = pl.BlockSpec((1, 1, hidden, width), lambda e, *_: (layer, e + first, 0, 0))
    row_spec = pl.BlockSpec((1, rows, both), lambda e, *_: (e + first, 0, 0))
    return pl.pallas_call(
        functools.partial(dw_kernel, first),
        grid_spec=pltpu.PrefetchScalarGridSpec(
            num_scalar_prefetch=1,
            grid=(last - first,),
            in_specs=[row_spec, gu_spec, d_spec] + [pl.BlockSpec(memory_space=pl.ANY)] * len(earlier),
            out_specs=[gu_spec, d_spec],
            scratch_shapes=[
                pltpu.VMEM((rows // 256 * 256 - 256, 2 * hidden), jnp.bfloat16),
                pltpu.VMEM((rows // 256 * 256 - 256, hidden), jnp.bfloat16),
            ],
        ),
        out_shape=[shape_of(wgu.shape, jnp.float32), shape_of(wd.shape, jnp.float32)],
        input_output_aliases={4 + i: i for i in range(len(earlier))},
        compiler_params=params_of(),
        cost_estimate=BRIEF,
        name="weight_grads",
    )(totals, packed, wgu, wd, *earlier)


def norm_low(x, gain):
    return ((x * rms_factor(x)) * gain).astype(jnp.bfloat16)


def post_attention(ob, x, wo, gain):
    groups = wo.shape[0]
    inner = wo.shape[1]
    blk = ob.shape[1]
    halves = []
    for h in range(2):
        total = x[h * blk : (h + 1) * blk]
        for g in range(groups):
            total = total + nn(ob[h * groups + g][:, :inner], wo[g])
        halves.append(total)
    hst = jnp.concatenate(halves, axis=0)
    return hst, norm_low(hst, gain)


def mixing_rows(table):
    raw, coef = table[RAW : RAW + 16], table[COEF : COEF + 16]
    pairs = []
    for c in range(NC):
        r0, r1 = raw[NE + 2 * c : NE + 2 * c + 1], raw[NE + 2 * c + 1 : NE + 2 * c + 2]
        top = jnp.maximum(r0, r1)
        e0, e1 = jnp.exp(r0 - top), jnp.exp(r1 - top)
        pairs.append((e0 / (e0 + e1), e1 / (e0 + e1)))
    shares = [coef[NF + 2 + c : NF + 3 + c] for c in range(NC)]
    scale_u = coef[NF + 1 : NF + 2]
    for c in range(NC):
        scale_u = scale_u + shares[c] * pairs[c][0]
    return pairs, shares, scale_u, [shares[c] * pairs[c][1] for c in range(NC)]


def middle(gx, parts, gcoef, table, routes, gprev, hst, ub, small, wo, ob):
    groups = wo.shape[0]
    inner = wo.shape[1]
    blk = ob.shape[1]
    gain = small[1:2].astype(jnp.float32)
    consts = small[2 : 2 + NC].astype(jnp.float32)
    router = small[2 + NC :]
    pairs, shares, scale_u, scale_c = mixing_rows(table)
    columns = to_columns([scale_u] + scale_c)
    factor = rms_factor(hst)
    base = hst * factor
    u = base * gain
    dots = [jnp.sum(gx * u, axis=1, keepdims=True)]
    dots += [jnp.sum(gx * consts[c : c + 1], axis=1, keepdims=True) for c in range(NC)]
    dots = to_rows(dots, 8)
    dot_u = dots[0:1]
    dot_c = [dots[1 + c : 2 + c] for c in range(NC)]
    ids = lax.broadcasted_iota(jnp.int32, (16, gx.shape[0]), 0)
    grads = jnp.concatenate([gcoef, jnp.zeros_like(gcoef)], axis=0)
    grads = jnp.where(ids == NF + 1, dot_u, grads)
    raw_rows = []
    for c in range(NC):
        a0, a1 = pairs[c]
        grads = jnp.where(ids == NF + 2 + c, a0 * dot_u + a1 * dot_c[c], grads)
        g0, g1 = shares[c] * dot_u, shares[c] * dot_c[c]
        both = a0 * g0 + a1 * g1
        raw_rows += [a0 * (g0 - both), a1 * (g1 - both)]
    logits = table[LOGI : LOGI + 16]
    first, second = ids == routes[0:1], ids == routes[1:2]

    def pick(chosen, rows):
        return jnp.sum(jnp.where(chosen, rows, 0.0), axis=0, keepdims=True)

    z0, z1 = pick(first, logits), pick(second, logits)
    top = jnp.maximum(z0, z1)
    e0, e1 = jnp.exp(z0 - top), jnp.exp(z1 - top)
    w0, w1 = e0 / (e0 + e1), e1 / (e0 + e1)
    gg0, gg1 = pick(first, grads), pick(second, grads)
    both = w0 * gg0 + w1 * gg1
    glog = jnp.where(first, w0 * (gg0 - both), 0.0) + jnp.where(second, w1 * (gg1 - both), 0.0) + gprev
    graw = glog
    for index, row in enumerate(raw_rows):
        graw = jnp.where(ids == NE + index, row, graw)
    graw = graw.astype(jnp.bfloat16)
    grad_router = nn(graw, ub)
    gu = gx * columns[0] + tn(graw, router) + parts
    sums = [jnp.sum(gu * base, axis=0, keepdims=True)]
    sums += [jnp.sum(gx * columns[1 + c], axis=0, keepdims=True) for c in range(NC)]
    gb = gu * gain
    ghst = gx + factor * (gb - base * jnp.mean(gb * base, axis=-1, keepdims=True))
    gy = ghst.astype(jnp.bfloat16)
    lanes = ob.shape[2]
    go, gwo = [None] * (2 * groups), []
    for g in range(groups):
        value = nt(gy, wo[g]).astype(jnp.bfloat16)
        value = jnp.concatenate([value, jnp.zeros((value.shape[0], lanes - inner), jnp.bfloat16)], axis=1)
        for h in range(2):
            go[h * groups + g] = value[h * blk : (h + 1) * blk]
        mixed = jnp.concatenate([ob[g], ob[groups + g]], axis=0)
        gwo.append(tn(mixed, gy)[:inner].astype(jnp.bfloat16))
    return ghst, jnp.stack(go), jnp.stack(gwo), jnp.concatenate(sums + [grad_router], axis=0), glog


def assemble_kernel(ours, theirs, qkv, out, gains, router, consts):
    z, _, _, _ = place()
    layers = ours.shape[0]
    inner = GROUP_HEADS * HEAD_DIM
    for l in range(layers):
        small = ours[l, :, :128].astype(jnp.float32) + theirs[l, :, :128].astype(jnp.float32)
        router[l] = small[:, 2 + NC : 2 + NC + 16]
        rows = jnp.transpose(small)
        gains[l] = rows[:2]
        consts[l] = rows[2 : 2 + NC]
        first = 128 + 6 * inner
        out[l] = ours[l, :, first:].astype(jnp.float32) + theirs[l, :, first:].astype(jnp.float32)
        for group in range(4):
            for odd in range(2):

                @pl.when(z % 2 == odd)
                def _():
                    source = ours if group // 2 == odd else theirs
                    for c in range(3):
                        at = 128 + (group % 2) * 3 * inner + c * inner
                        qkv[l, c, :, group * inner : (group + 1) * inner] = source[l, :, at : at + inner].astype(jnp.float32)


def assemble(ours, theirs, width):
    layers, shard, _ = ours.shape
    vm = pl.BlockSpec(memory_space=pltpu.VMEM)
    f32 = jnp.float32
    return pl.pallas_call(
        assemble_kernel,
        out_shape=[
            shape_of((layers, 3, shard, width), f32),
            shape_of((layers, shard, width), f32),
            shape_of((layers, 2, shard), f32),
            shape_of((layers, shard, 16), f32),
            shape_of((layers, NC, shard), f32),
        ],
        in_specs=[vm] * 2,
        out_specs=[vm] * 5,
        compiler_params=params_of(),
        cost_estimate=BRIEF,
        name="assemble",
    )(ours, theirs)


def turn_tables(seq):
    half = HEAD_DIM // 2
    frequency = np.exp((-np.log(np.float32(10000.0)) * np.arange(half, dtype=np.float32) / np.float32(half)))
    angles = np.arange(seq, dtype=np.float32)[:, None] * frequency.astype(np.float32)[None, :]
    cosine, sine = np.cos(angles), np.sin(angles)
    cosine = np.concatenate([cosine, cosine] * 2, axis=1).astype(np.float32)
    sine = np.concatenate([-sine, sine] * 2, axis=1).astype(np.float32)
    return jnp.asarray(cosine), jnp.asarray(sine)


def by_heads(
    tokens,
    cotangent,
    seq_lengths,
    block_order,
    routes,
    gains,
    qkv_weights,
    out_weight,
    router,
    const_values,
    w_gate_up,
    w_down,
):
    count, width = tokens.shape[1], tokens.shape[2]
    ctx_size, packs = lax.axis_size("ctx"), lax.axis_size("fsdp")
    blk = count // 2
    seq = blk * ctx_size
    pack = lax.axis_index("fsdp")
    z, xx, y, k = place()
    sequence = z // 2
    shard = width // packs
    f32, bf = jnp.float32, jnp.bfloat16
    everyone = ("ctx", "fsdp")

    cosine, sine = turn_tables(seq)
    routes_t = jnp.swapaxes(routes[:, 0], 1, 2)
    smalls = jnp.concatenate([gains, const_values, jnp.swapaxes(router, 1, 2)], axis=1)
    per_layer = smalls.shape[1]
    ints = jnp.concatenate([routes_t.reshape(-1), block_order[0]])
    places = ints.size
    ints = jnp.pad(ints, (0, -places % shard)).astype(bf).reshape(-1, shard)
    smalls = jnp.concatenate([smalls.reshape(LAYERS * per_layer, shard), ints], axis=0)
    smalls = jnp.pad(smalls, ((0, -smalls.shape[0] % 16), (0, 0)))
    smalls = lax.all_gather(smalls, "fsdp", axis=1, tiled=True)
    ints = smalls[LAYERS * per_layer : LAYERS * per_layer + ints.shape[0]].reshape(-1, packs, shard)
    ints = jnp.swapaxes(ints, 0, 1).reshape(packs, -1).astype(jnp.int32)
    smalls = [smalls[l * per_layer : (l + 1) * per_layer] for l in range(LAYERS)]
    near = jnp.stack([pack, 2 * y + 1 - k, 2 * (1 - y) + k, 2 * (1 - y) + 1 - k])
    routes_f = ints[near][:, : routes_t.size].reshape((packs,) + routes_t.shape)
    order = lax.dynamic_index_in_dim(ints, 2 * y + xx, 0, keepdims=False)
    order = order[routes_t.size : places].reshape(ctx_size, 2)
    order = lax.dynamic_index_in_dim(order, sequence, 1, keepdims=False) - ctx_size * sequence
    ids = jnp.arange(ctx_size, dtype=jnp.int32)
    inv = jnp.sum(jnp.where(order[None, :] == ids[:, None], ids[None, :], 0), axis=1)

    gm_all = [None, lax.all_gather(cotangent[0], everyone, axis=0, tiled=False)]
    x = tokens[0].astype(f32)
    before = jnp.zeros((packs, 16, count), f32)
    kept, ext_all = [], [None] * LAYERS
    for l in range(LAYERS):
        n1s, qkv, o, lse, ob, hst, ub, w, wo = attn_forward(
            l, order, inv, x, smalls[l], qkv_weights, cosine, sine, out_weight, 2 * l
        )
        if l == 1:
            ub, gm_all[1] = lax.optimization_barrier((ub, gm_all[1]))
            hst, first_ext = lax.optimization_barrier((hst, ext_all[0]))
            ext_all[0] = lax.all_gather(first_ext, everyone, axis=0, tiled=False)
        ubf, table, ext, x_next = ffn_forward(
            l, ub, hst, smalls[l], routes_f[:, l], before, w_gate_up, w_down, 2 * l + 1
        )
        before = table[:, LOGI : LOGI + 16]
        ext_all[l] = ext if l == 0 else lax.all_gather(ext, everyone, axis=0, tiled=False)
        kept.append((x, n1s, qkv, o, lse, ob, hst, w, wo, ubf, table))
        x = x_next
    output = x
    gm = cotangent[0]
    gx = gm.astype(f32)
    gprev = jnp.zeros((16, count), f32)
    grads = [None] * LAYERS
    for l in reversed(range(LAYERS)):
        x, n1s, qkv, o, lse, ob, hst, w, wo, ubf, table = kept[l]
        number = 2 * LAYERS + 2 * l
        ghst, go, gwo, small, gprev = ffn_backward(
            l, gm, gx, ubf, table, hst, smalls[l], routes_t[l], gprev, wo, ob, w_gate_up, w_down, number
        )
        if l == 1:
            go, ext_all[0] = lax.optimization_barrier((go, ext_all[0]))
        gx, gm, grads[l] = attn_backward(
            order, inv, n1s, w, cosine, sine, qkv, o, lse, go, ghst, x, smalls[l], small, gwo, number + 1
        )
        if l > 0:
            gm_all[l - 1] = gm

    dense = jnp.stack(grads)
    dense, gm = lax.optimization_barrier((dense, gm_all[0]))
    gm_all[0] = lax.all_gather(gm, everyone, axis=0, tiled=False)

    def partner(values, distance):
        return lax.ppermute(values, "ctx", [(i, i ^ distance) for i in range(ctx_size)])

    def added(first, second):
        return (first.astype(f32) + second.astype(f32)).astype(bf)

    half = NF // 2
    numbers = expert_counts(ext_all[1])
    packed = pack_rows(numbers, ext_all[1], gm_all[1])
    dense, packed = lax.optimization_barrier((dense, packed))
    got = partner(dense, 1)
    done = weight_grads(1, 0, NF, numbers[2], packed, w_gate_up, w_down, ())
    done, got = lax.optimization_barrier((done, got))
    dense = added(dense, got)
    dense, ext, gm = lax.optimization_barrier((dense, ext_all[0], gm_all[0]))
    got = partner(dense, 4)
    numbers = expert_counts(ext)
    packed = pack_rows(numbers, ext, gm)
    done = weight_grads(0, 0, half, numbers[2], packed, w_gate_up, w_down, done)
    done, got = lax.optimization_barrier((done, got))
    dense = added(dense, got)
    dense, done = lax.optimization_barrier((dense, done))
    got = partner(dense, 2)
    done = weight_grads(0, half, NF, numbers[2], packed, w_gate_up, w_down, done)
    done, got = lax.optimization_barrier((done, got))
    qkv, out, gain_grad, router_grad, const_grad = assemble(dense, got, width)
    return (
        output[None],
        gx[None],
        gain_grad,
        qkv,
        out,
        router_grad,
        const_grad,
        done[0],
        done[1],
    )


def solution(mesh):
    placed = (
        P("fsdp", "ctx", None),
        P("fsdp", "ctx", None),
        P("fsdp", None),
        P("fsdp", None),
        P(None, "fsdp", "ctx", None),
        P(None, None, "fsdp"),
        P(None, None, "fsdp", None),
        P(None, "fsdp", None),
        P(None, "fsdp", None),
        P(None, None, "fsdp"),
        P(None, None, None, None, "fsdp"),
        P(None, None, "fsdp", None),
    )
    contexts, packs = mesh.shape["ctx"], mesh.shape["fsdp"]
    blocks_of_heads = HEADS // GROUP_HEADS

    def plan(*args):
        tokens = args[0]
        even = tokens.shape[1] * contexts == 2 * MINLEN
        grouped = contexts == 2 * blocks_of_heads and packs == blocks_of_heads
        return (by_heads if even and grouped else shards)(*args)

    return jax.shard_map(
        plan,
        mesh=mesh,
        in_specs=placed,
        out_specs=(
            P("fsdp", "ctx", None),
            P("fsdp", "ctx", None),
            P(None, None, "fsdp"),
            P(None, None, "fsdp", None),
            P(None, "fsdp", None),
            P(None, "fsdp", None),
            P(None, None, "fsdp"),
            P(None, None, None, None, "fsdp"),
            P(None, None, "fsdp", None),
        ),
        check_vma=False,
    )
```

```python
import functools

import jax
import jax.numpy as jnp
import numpy as np
from jax import lax
from jax.experimental import pallas as pl
from jax.experimental.pallas import tpu as pltpu
from jax.sharding import PartitionSpec as P

HEADS = 12
HEAD_DIM = 64
NF = 8
NC = 2
LAYERS = 2
NE = 12
MOST = 64
GROUP_HEADS = 3


def from_behind(x, axis, by):
    devices = lax.axis_size(axis)
    return lax.ppermute(x, axis, [(i, (i + by) % devices) for i in range(devices)])


def layout_tables(lengths, order_row, tok_count):
    block_len = tok_count // 2
    pack_len = order_row.shape[0] * block_len
    pack_rows = jnp.arange(pack_len, dtype=jnp.int32)
    owner = pack_rows // tok_count
    which_half = pack_rows % tok_count // block_len
    block_ids = order_row[2 * owner + which_half]
    pack_pos = block_ids * block_len + pack_rows % block_len
    segment = (pack_pos >= lengths[0]).astype(jnp.int32)
    seq_pos = pack_pos - segment * lengths[0]
    return (pack_pos, segment, seq_pos)


def angle_tables(seq_pos, head_size):
    half_size = head_size // 2
    frequency = jnp.exp(-jnp.log(10000.0) * jnp.arange(half_size, dtype=jnp.float32) / half_size)
    angles = seq_pos.astype(jnp.float32)[:, None] * frequency[None, :]
    return (jnp.cos(angles)[:, None, :], jnp.sin(angles)[:, None, :])


def rotate_pairs(values, cosine_table, sine_table, direction):
    half_size = values.shape[-1] // 2
    first_half = values[..., :half_size]
    second_half = values[..., half_size:]
    return jnp.concatenate(
        [
            first_half * cosine_table - direction * second_half * sine_table,
            second_half * cosine_table + direction * first_half * sine_table,
        ],
        axis=-1,
    )


def rms_parts(values):
    inverse = lax.rsqrt(jnp.mean(values * values, axis=-1, keepdims=True) + 1e-06)
    return (values * inverse, inverse)


def rms_back(grad_normed, base_values, inverse):
    return inverse * (
        grad_normed - base_values * jnp.mean(grad_normed * base_values, axis=-1, keepdims=True)
    )


def expert_forward(inputs_low, gate_up_use, down_use):
    gate_up_out = jnp.einsum(
        "emd,ecdf->ecmf", inputs_low, gate_up_use, preferred_element_type=jnp.float32
    )
    hidden_low = (jax.nn.silu(gate_up_out[:, 0]) * gate_up_out[:, 1]).astype(jnp.bfloat16)
    partial_value = jnp.einsum(
        "emf,efd->emd", hidden_low, down_use, preferred_element_type=jnp.float32
    )
    return (gate_up_out, hidden_low, partial_value)


def expert_backward(inputs_low, gate_up_out, hidden_low, grad_part_low, gate_up_use, down_use):
    grad_down = jnp.einsum(
        "emf,emd->efd", hidden_low, grad_part_low, preferred_element_type=jnp.float32
    )
    grad_hidden = jnp.einsum(
        "emd,efd->emf", grad_part_low, down_use, preferred_element_type=jnp.float32
    )
    gate_out = gate_up_out[:, 0]
    sigmoid_gate = jax.nn.sigmoid(gate_out)
    grad_pair_low = jnp.stack(
        [
            grad_hidden
            * gate_up_out[:, 1]
            * sigmoid_gate
            * (1.0 + gate_out * (1.0 - sigmoid_gate)),
            grad_hidden * gate_out * sigmoid_gate,
        ],
        axis=1,
    ).astype(jnp.bfloat16)
    grad_gate_up = jnp.einsum(
        "emd,ecmf->ecdf", inputs_low, grad_pair_low, preferred_element_type=jnp.float32
    )
    grad_rows = jnp.einsum(
        "ecmf,ecdf->emd", grad_pair_low, gate_up_use, preferred_element_type=jnp.float32
    )
    return (grad_gate_up, grad_down, grad_rows)


def shards(
    tokens,
    cotangent,
    seq_lengths,
    block_order,
    routes,
    gains,
    qkv_weights,
    out_weight,
    router,
    const_values,
    w_gate_up,
    w_down,
):
    tok_count = tokens.shape[1]
    width = tokens.shape[2]
    ctx_size = lax.axis_size("ctx")
    own_index = lax.axis_index("ctx")
    score_scale = HEAD_DIM ** (-0.5)
    pack_pos, segment, seq_pos = layout_tables(seq_lengths[0], block_order[0], tok_count)
    own_start = own_index * tok_count
    query_pos = lax.dynamic_slice_in_dim(pack_pos, own_start, tok_count)
    query_seg = lax.dynamic_slice_in_dim(segment, own_start, tok_count)
    cosine_table, sine_table = angle_tables(
        lax.dynamic_slice_in_dim(seq_pos, own_start, tok_count), HEAD_DIM
    )
    head_shape = (tok_count, HEADS, HEAD_DIM)
    expert_ids = jnp.arange(NE, dtype=jnp.int32)
    slot_ids = jnp.arange(MOST, dtype=jnp.int32)
    row_ids = jnp.arange(tok_count, dtype=jnp.int32)

    def allowed_pairs(key_offset, key_count):
        key_pos = lax.dynamic_slice_in_dim(pack_pos, key_offset, key_count)
        key_seg = lax.dynamic_slice_in_dim(segment, key_offset, key_count)
        return (query_seg[:, None] == key_seg[None, :]) & (key_pos[None, :] <= query_pos[:, None])

    stream = tokens[0].astype(jnp.float32)
    previous = jnp.zeros((tok_count, NE), jnp.float32)
    saved = []
    for layer_index in range(LAYERS):
        gain_all, qkv_all, out_all, router_all, const_all = (
            lax.all_gather(gains[layer_index], "fsdp", axis=1, tiled=True),
            lax.all_gather(qkv_weights[layer_index], "fsdp", axis=1, tiled=True),
            lax.all_gather(out_weight[layer_index], "fsdp", axis=0, tiled=True),
            lax.all_gather(router[layer_index], "fsdp", axis=0, tiled=True),
            lax.all_gather(const_values[layer_index], "fsdp", axis=1, tiled=True),
        )
        gain_float = gain_all.astype(jnp.float32)
        base_one, inverse_one = rms_parts(stream)
        normed_low = (base_one * gain_float[0]).astype(jnp.bfloat16)
        projected = jnp.einsum(
            "td,cde->cte", normed_low, qkv_all, preferred_element_type=jnp.float32
        )
        queries_low = rotate_pairs(
            projected[0].reshape(head_shape), cosine_table, sine_table, 1.0
        ).astype(jnp.bfloat16)
        keys_low = rotate_pairs(
            projected[1].reshape(head_shape), cosine_table, sine_table, 1.0
        ).astype(jnp.bfloat16)
        values_low = projected[2].reshape(head_shape).astype(jnp.bfloat16)

        def fold_step(running, shard_piece, offset, queries_use=queries_low):
            keys_piece, values_piece = shard_piece
            allowed = allowed_pairs(offset, keys_piece.shape[0])[None]
            scores = (
                jnp.einsum(
                    "qhd,khd->hqk", queries_use, keys_piece, preferred_element_type=jnp.float32
                )
                * score_scale
            )
            scores = jnp.where(allowed, scores, -1e30)
            top_old, total_old, accumulated = running
            top_new = jnp.maximum(top_old, jnp.max(scores, axis=-1))
            weights = jnp.where(allowed, jnp.exp(scores - top_new[..., None]), 0.0)
            factor = jnp.exp(top_old - top_new)
            accumulated = jnp.einsum(
                "hqk,khd->hqd",
                weights.astype(jnp.bfloat16),
                values_piece,
                preferred_element_type=jnp.float32,
            )
            return (top_new, jnp.sum(weights, axis=-1), accumulated)

        starting = (
            jnp.full((HEADS, tok_count), -1e30, jnp.float32),
            jnp.zeros((HEADS, tok_count), jnp.float32),
            jnp.zeros((HEADS, tok_count, HEAD_DIM), jnp.float32),
        )
        top_value, total_sum, accumulated = fold_step(
            starting,
            (
                lax.all_gather(keys_low, "ctx", axis=0, tiled=True),
                lax.all_gather(values_low, "ctx", axis=0, tiled=True),
            ),
            jnp.int32(0),
        )
        log_total = top_value + jnp.log(total_sum)
        attended = jnp.transpose(accumulated / total_sum[..., None], (1, 0, 2))
        mixed_low = attended.reshape(tok_count, width).astype(jnp.bfloat16)
        hidden_state = stream + jnp.dot(mixed_low, out_all, preferred_element_type=jnp.float32)
        base_two, inverse_two = rms_parts(hidden_state)
        expert_in = base_two * gain_float[1]
        expert_low = expert_in.astype(jnp.bfloat16)
        raw_logits = jnp.dot(expert_low, router_all, preferred_element_type=jnp.float32)
        logits = raw_logits[:, :NE] + previous
        route_ids = routes[layer_index, 0]
        chosen = route_ids[:, :, None] == expert_ids[None, None, :]
        chosen_f = chosen.astype(jnp.float32)
        hit_count = jnp.sum(chosen.astype(jnp.int32), axis=1)
        slot_index = jnp.cumsum(hit_count, axis=0) - 1
        picked = jnp.sum(chosen_f * logits[:, None, :], axis=-1)
        gate_weights = jax.nn.softmax(picked, axis=-1)
        coeffs = jnp.sum(gate_weights[:, :, None] * chosen_f, axis=1)
        slot_table = jnp.zeros((NF, MOST), jnp.int32)
        for expert in range(NF):
            target = jnp.where(hit_count[:, expert] > 0, slot_index[:, expert], MOST)
            slot_table = slot_table.at[expert, target].set(row_ids, mode="drop")
        filled = (slot_ids[None, :] < jnp.sum(hit_count[:, :NF], axis=0)[:, None]).astype(
            jnp.float32
        )
        rows_low = expert_low[slot_table]
        inputs_low = lax.all_gather(rows_low, "fsdp", axis=1, tiled=True)
        gate_up_out, hidden_low, partial_value = expert_forward(
            inputs_low, w_gate_up[layer_index], w_down[layer_index]
        )
        result = lax.psum_scatter(
            partial_value.astype(jnp.bfloat16), "fsdp", scatter_dimension=1, tiled=True
        ).astype(jnp.float32)
        flat_index = jnp.arange(NF, dtype=jnp.int32)[None, :] * MOST + jnp.clip(
            slot_index[:, :NF], 0, MOST - 1
        )
        token_result = result.reshape(NF * MOST, width)[flat_index]
        expert_mix = (
            jnp.sum(coeffs[:, :NF, None] * token_result, axis=1)
            + coeffs[:, NF + 1 : NF + 2] * expert_in
        )
        mixings = []
        for const_index in range(NC):
            column = NE + 2 * const_index
            mixing = jax.nn.softmax(raw_logits[:, column : column + 2], axis=-1)
            mixings.append(mixing)
            expert_mix = expert_mix + coeffs[:, NF + 2 + const_index : NF + 3 + const_index] * (
                mixing[:, 0:1] * expert_in
                + mixing[:, 1:2] * const_all[const_index].astype(jnp.float32)[None, :]
            )
        saved.append(
            (
                gain_float,
                qkv_all,
                out_all,
                router_all,
                const_all,
                base_one,
                inverse_one,
                normed_low,
                queries_low,
                keys_low,
                values_low,
                log_total,
                attended,
                mixed_low,
                base_two,
                inverse_two,
                expert_in,
                expert_low,
                chosen_f,
                hit_count,
                gate_weights,
                coeffs,
                slot_table,
                filled,
                inputs_low,
                gate_up_out,
                hidden_low,
                flat_index,
                token_result,
                mixings,
            )
        )
        stream = hidden_state + expert_mix
        previous = logits
    grad_stream = cotangent[0].astype(jnp.float32)
    grad_previous = jnp.zeros((tok_count, NE), jnp.float32)
    layer_grads = [None] * LAYERS
    for layer_index in reversed(range(LAYERS)):
        (
            gain_float,
            qkv_all,
            out_all,
            router_all,
            const_all,
            base_one,
            inverse_one,
            normed_low,
            queries_low,
            keys_low,
            values_low,
            log_total,
            attended,
            mixed_low,
            base_two,
            inverse_two,
            expert_in,
            expert_low,
            chosen_f,
            hit_count,
            gate_weights,
            coeffs,
            slot_table,
            filled,
            inputs_low,
            gate_up_out,
            hidden_low,
            flat_index,
            token_result,
            mixings,
        ) = saved[layer_index]
        grad_mix = grad_stream
        dot_input = jnp.sum(grad_mix * expert_in, axis=-1, keepdims=True)
        coef_grads = [
            jnp.sum(grad_mix[:, None, :] * token_result, axis=-1),
            jnp.zeros((tok_count, 1), jnp.float32),
            dot_input,
        ]
        grad_in = grad_mix * coeffs[:, NF + 1 : NF + 2]
        const_cols = []
        const_grads = []
        for const_index in range(NC):
            mixing = mixings[const_index]
            const_row = const_all[const_index].astype(jnp.float32)[None, :]
            dot_const = jnp.sum(grad_mix * const_row, axis=-1, keepdims=True)
            share = coeffs[:, NF + 2 + const_index : NF + 3 + const_index]
            coef_grads.append(mixing[:, 0:1] * dot_input + mixing[:, 1:2] * dot_const)
            grad_in = grad_in + grad_mix * (share * mixing[:, 0:1])
            grad_mixing = share * jnp.concatenate([dot_input, dot_const], axis=1)
            const_cols.append(
                mixing * (grad_mixing - jnp.sum(mixing * grad_mixing, axis=-1, keepdims=True))
            )
            const_grads.append(jnp.sum(grad_mix * (share * mixing[:, 1:2]), axis=0))
        grad_coeffs = jnp.concatenate(coef_grads, axis=1)
        grad_gates = jnp.sum(chosen_f * grad_coeffs[:, None, :], axis=-1)
        grad_picked = gate_weights * (
            grad_gates - jnp.sum(gate_weights * grad_gates, axis=-1, keepdims=True)
        )
        grad_logits = jnp.sum(grad_picked[:, :, None] * chosen_f, axis=1) + grad_previous
        grad_previous = grad_logits
        grad_raw_low = jnp.concatenate([grad_logits] + const_cols, axis=1).astype(jnp.bfloat16)
        grad_router = jnp.einsum(
            "td,tc->dc", expert_low, grad_raw_low, preferred_element_type=jnp.float32
        )
        grad_in = grad_in + jnp.einsum(
            "tc,dc->td", grad_raw_low, router_all, preferred_element_type=jnp.float32
        )
        slot_weight = (
            jnp.take_along_axis(jnp.transpose(coeffs[:, :NF]), slot_table, axis=1) * filled
        )
        grad_result_low = (grad_mix[slot_table] * slot_weight[:, :, None]).astype(jnp.bfloat16)
        grad_part_low = lax.all_gather(grad_result_low, "fsdp", axis=1, tiled=True)
        grad_gate_up, grad_down, grad_rows = expert_backward(
            inputs_low,
            gate_up_out,
            hidden_low,
            grad_part_low,
            w_gate_up[layer_index],
            w_down[layer_index],
        )
        grad_rows = lax.psum_scatter(
            grad_rows.astype(jnp.bfloat16), "fsdp", scatter_dimension=1, tiled=True
        ).astype(jnp.float32)
        token_grads = grad_rows.reshape(NF * MOST, width)[flat_index]
        grad_in = grad_in + jnp.sum(
            jnp.where(hit_count[:, :NF, None] > 0, token_grads, 0.0), axis=1
        )
        grad_gain_two = jnp.sum(grad_in * base_two, axis=0)
        grad_hidden_state = grad_stream + rms_back(grad_in * gain_float[1], base_two, inverse_two)
        grad_out_low = grad_hidden_state.astype(jnp.bfloat16)
        grad_out_w = jnp.einsum(
            "td,te->de", mixed_low, grad_out_low, preferred_element_type=jnp.float32
        )
        grad_attended = (
            jnp.einsum("te,de->td", grad_out_low, out_all, preferred_element_type=jnp.float32)
            .astype(jnp.bfloat16)
            .reshape(head_shape)
        )
        delta = jnp.transpose(jnp.sum(grad_attended.astype(jnp.float32) * attended, axis=-1))

        def visit(
            turn_index,
            carried,
            queries_use=queries_low,
            grad_use=grad_attended,
            log_use=log_total,
            delta_use=delta,
        ):
            keys_piece, values_piece, key_grads, value_grads, query_grads = carried
            source = (own_index - turn_index) % ctx_size
            allowed = allowed_pairs(source * tok_count, tok_count)[None]
            scores = (
                jnp.einsum(
                    "qhd,khd->hqk", queries_use, keys_piece, preferred_element_type=jnp.float32
                )
                * score_scale
            )
            probs = jnp.where(
                allowed, jnp.exp(jnp.where(allowed, scores, -1e30) - log_use[..., None]), 0.0
            )
            value_grads = value_grads + jnp.einsum(
                "hqk,qhd->khd",
                probs.astype(jnp.bfloat16),
                grad_use,
                preferred_element_type=jnp.float32,
            )
            prob_grads = jnp.einsum(
                "qhd,khd->hqk", grad_use, values_piece, preferred_element_type=jnp.float32
            )
            score_grads = (probs * (prob_grads - delta_use[..., None])).astype(jnp.bfloat16)
            query_grads = query_grads + jnp.einsum(
                "hqk,khd->qhd", score_grads, keys_piece, preferred_element_type=jnp.float32
            )
            key_grads = key_grads + jnp.einsum(
                "hqk,qhd->khd", score_grads, queries_use, preferred_element_type=jnp.float32
            )
            keys_piece, values_piece = from_behind((keys_piece, values_piece), "ctx", 1)
            key_grads, value_grads = (
                from_behind(key_grads.astype(jnp.bfloat16), "ctx", 1).astype(key_grads.dtype),
                from_behind(value_grads.astype(jnp.bfloat16), "ctx", 1).astype(value_grads.dtype),
            )
            return (keys_piece, values_piece, key_grads, value_grads, query_grads)

        zero_heads = jnp.zeros(head_shape, jnp.float32)
        finished = lax.fori_loop(
            0, ctx_size, visit, (keys_low, values_low, zero_heads, zero_heads, zero_heads)
        )
        grad_query = (
            rotate_pairs(finished[4] * score_scale, cosine_table, sine_table, -1.0)
            .astype(jnp.bfloat16)
            .reshape(tok_count, width)
        )
        grad_key = (
            rotate_pairs(finished[2] * score_scale, cosine_table, sine_table, -1.0)
            .astype(jnp.bfloat16)
            .reshape(tok_count, width)
        )
        grad_value = finished[3].astype(jnp.bfloat16).reshape(tok_count, width)
        grad_proj_low = jnp.stack([grad_query, grad_key, grad_value], axis=0)
        grad_qkv = jnp.einsum(
            "td,cte->cde", normed_low, grad_proj_low, preferred_element_type=jnp.float32
        )
        grad_normed = jnp.einsum(
            "cte,cde->td", grad_proj_low, qkv_all, preferred_element_type=jnp.float32
        )
        grad_gain_one = jnp.sum(grad_normed * base_one, axis=0)
        grad_stream = grad_hidden_state + rms_back(
            grad_normed * gain_float[0], base_one, inverse_one
        )
        gains_shard, qkv_shard, out_shard, router_shard, const_shard = (
            lax.psum_scatter(
                jnp.stack([grad_gain_one, grad_gain_two]).astype(jnp.bfloat16),
                "fsdp",
                scatter_dimension=1,
                tiled=True,
            ).astype(jnp.float32),
            lax.psum_scatter(
                grad_qkv.astype(jnp.bfloat16), "fsdp", scatter_dimension=1, tiled=True
            ).astype(jnp.float32),
            lax.psum_scatter(
                grad_out_w.astype(jnp.bfloat16), "fsdp", scatter_dimension=0, tiled=True
            ).astype(jnp.float32),
            lax.psum_scatter(
                grad_router.astype(jnp.bfloat16), "fsdp", scatter_dimension=0, tiled=True
            ).astype(jnp.float32),
            lax.psum_scatter(
                jnp.stack(const_grads).astype(jnp.bfloat16), "fsdp", scatter_dimension=1, tiled=True
            ).astype(jnp.float32),
        )
        layer_grads[layer_index] = (
            lax.psum(gains_shard.astype(jnp.bfloat16), "ctx").astype(jnp.float32),
            lax.psum(qkv_shard.astype(jnp.bfloat16), "ctx").astype(jnp.float32),
            lax.psum(out_shard.astype(jnp.bfloat16), "ctx").astype(jnp.float32),
            lax.psum(router_shard.astype(jnp.bfloat16), "ctx").astype(jnp.float32),
            lax.psum(const_shard.astype(jnp.bfloat16), "ctx").astype(jnp.float32),
            lax.psum(grad_gate_up.astype(jnp.bfloat16), "ctx").astype(jnp.float32),
            lax.psum(grad_down.astype(jnp.bfloat16), "ctx").astype(jnp.float32),
        )
    stacked = [
        jnp.stack([layer_grads[layer_index][member_index] for layer_index in range(LAYERS)])
        for member_index in range(7)
    ]
    return (
        stream[None],
        grad_stream[None],
        stacked[0],
        stacked[1],
        stacked[2],
        stacked[3],
        stacked[4],
        stacked[5],
        stacked[6],
    )


MINLEN = 1024
ROUT = 56
RAW, COEF, SLOT, LOGI = 0, 16, 32, 40
VMEM_MB = 60
BRIEF = pl.CostEstimate(flops=1, bytes_accessed=1, transcendentals=0)


def nt(a, b):
    return lax.dot_general(a, b, (((1,), (1,)), ((), ())), preferred_element_type=jnp.float32)


def nn(a, b):
    return lax.dot_general(a, b, (((1,), (0,)), ((), ())), preferred_element_type=jnp.float32)


def tn(a, b):
    return lax.dot_general(a, b, (((0,), (0,)), ((), ())), preferred_element_type=jnp.float32)


def params_of(mb=VMEM_MB, **more):
    return pltpu.CompilerParams(vmem_limit_bytes=mb * 2**20, **more)


def shape_of(dims, kind):
    return jax.ShapeDtypeStruct(dims, kind)


def rms_factor(values):
    return lax.rsqrt(jnp.mean(values * values, axis=-1, keepdims=True) + 1e-06)


def to_rows(columns, count):
    lane = lax.broadcasted_iota(jnp.int32, (columns[0].shape[0], 128), 1)
    packed = jnp.zeros(lane.shape, jnp.float32)
    for index, column in enumerate(columns):
        packed = jnp.where(lane == index, column, packed)
    return jnp.transpose(packed)[:count]


def to_columns(rows):
    count = rows[0].shape[1]
    sub = lax.broadcasted_iota(jnp.int32, (128, count), 0)
    packed = jnp.zeros(sub.shape, jnp.float32)
    for index, row in enumerate(rows):
        packed = jnp.where(sub == index, row, packed)
    packed = jnp.transpose(packed)
    return [packed[:, index : index + 1] for index in range(len(rows))]


def swap_halves(values):
    lanes = values.shape[1]
    lane = lax.broadcasted_iota(jnp.int32, values.shape, 1)
    ahead = pltpu.roll(values, lanes - 32, 1)
    behind = pltpu.roll(values, 32, 1)
    return jnp.where(lane % 64 < 32, ahead, behind)


def spin(values, cosine, sine):
    return values * cosine + swap_halves(values) * sine


def place():
    own, pack = lax.axis_index("ctx"), lax.axis_index("fsdp")
    return own // 2, own % 2, pack // 2, pack % 2


def remote(src, dst, send, recv, ctx, fsdp):
    return pltpu.make_async_remote_copy(
        src_ref=src,
        dst_ref=dst,
        send_sem=send,
        recv_sem=recv,
        device_id=(ctx, fsdp),
        device_id_type=pl.DeviceIdType.MESH,
    )


def greet_plane(contexts, across=False):
    own = lax.axis_index("ctx")
    _, _, y, k = place()
    barrier = pltpu.get_barrier_semaphore()
    if across:
        for core in (k, 1 - k):
            device = (own, 2 * (1 - y) + core)
            pl.semaphore_signal(barrier, inc=1, device_id=device, device_id_type=pl.DeviceIdType.MESH)
    for ctx in range(contexts):
        for core in range(2):

            @pl.when(jnp.logical_or(ctx != own, core != k))
            def _():
                pl.semaphore_signal(barrier, inc=1, device_id=(ctx, 2 * y + core), device_id_type=pl.DeviceIdType.MESH)

    return barrier, 2 * contexts - 1 + (2 if across else 0)


def greet_packs():
    own = lax.axis_index("ctx")
    _, _, y, k = place()
    barrier = pltpu.get_barrier_semaphore()
    for fsdp in (2 * y + 1 - k, 2 * (1 - y) + k, 2 * (1 - y) + 1 - k):
        pl.semaphore_signal(barrier, inc=1, device_id=(own, fsdp), device_id_type=pl.DeviceIdType.MESH)
    return barrier, 3


def attn_fwd_kernel(
    order, inv, x, small, wq, cosine, sine, wo_own,
    n1s, qkv, o, lse, ob, hst, ub, w, wo,
    n1own, n1r, osort, osend, orecv, cols, w_s, wo_s,
    n_send, n_recv, f_send, f_recv, o_send, o_recv, w_send, w_recv, v_send, v_recv,
):
    blocks, blk, _ = n1r.shape
    lanes = o.shape[1]
    seq = blocks * blk
    step = 2 * blk
    own = lax.axis_index("ctx")
    z, xx, y, k = place()
    depth = blocks // 2
    same = xx == k
    pack = lax.axis_index("fsdp")
    inner = wo_own.shape[1]
    beside, over, corner = 2 * y + 1 - k, 2 * (1 - y) + k, 2 * (1 - y) + 1 - k

    barrier, others = greet_plane(blocks, across=True)
    n1 = norm_low(x[...], small[0:1, :].astype(jnp.float32))
    n1own[0] = n1[:blk]
    n1own[1] = n1[blk:]
    pl.semaphore_wait(barrier, others)

    def n1_copy(zz):
        return remote(n1own.at[zz // 2], n1r.at[own], n_send.at[zz], n_recv.at[z], 2 * zz + k, 2 * y + xx)

    for zz in range(depth):
        alone = jnp.logical_and(same, zz == z)

        @pl.when(jnp.logical_not(alone))
        def _():
            n1_copy(zz).start()

        @pl.when(alone)
        def _():
            n1r[own] = n1own[zz // 2]

    for half in range(2):

        @pl.when(z % 2 == half)
        def _():
            for core in range(2):
                first = (2 * half + core) * inner
                for c in range(3):
                    cols[core, :, c * lanes : c * lanes + inner] = wq[0, c, :, first : first + inner]
                    cols[core, :, c * lanes + inner : (c + 1) * lanes] = jnp.zeros((inner, lanes - inner), jnp.bfloat16)

    def rows_of(device):
        return pl.ds(pl.multiple_of(device * inner, inner), inner)

    def w_copy(index):
        device, core = ((beside, 1 - k), (over, k), (corner, 1 - k))[index]
        return remote(cols.at[core], w_s.at[rows_of(pack), :], w_send.at[index], w_recv.at[index], own, device)

    def w_wait(index):
        rows = w_s.at[rows_of((beside, over, corner)[index]), :]
        remote(cols.at[0], rows, w_send.at[index], w_recv.at[index], own, beside).wait_recv()

    w_s[rows_of(pack), :] = cols[k]
    wo_s[pack] = wo_own[0]
    for index in (1, 2, 0):
        w_copy(index).start()
    v_far = remote(wo_s.at[pack], wo_s.at[pack], v_send.at[0], v_recv.at[0], own, over)
    v_near = remote(wo_s.at[pack], wo_s.at[pack], v_send.at[1], v_recv.at[1], own, beside)
    v_on = remote(wo_s.at[over], wo_s.at[over], v_send.at[2], v_recv.at[2], own, beside)
    v_far.start()
    v_near.start()

    def forward_copy(zz):
        slot = n1r.at[2 * zz + k]
        return remote(slot, slot, f_send.at[zz], f_recv.at[zz], own, 2 * y + 1 - k)

    for zz in range(depth):

        @pl.when(jnp.logical_not(jnp.logical_and(same, zz == z)))
        def _():
            remote(n1own.at[0], n1r.at[2 * zz + k], n_send.at[zz], n_recv.at[zz], 2 * zz + k, 2 * y + xx).wait_recv()

        forward_copy(zz).start()
    for zz in range(depth):
        slot = n1r.at[2 * zz + 1 - k]
        remote(slot, slot, f_send.at[zz], f_recv.at[zz], own, 2 * y + 1 - k).wait_recv()

    for index in range(3):
        w_wait(index)
    w[...] = w_s[...]
    for b in range(blocks):
        n1s[b * blk : (b + 1) * blk, :] = n1r[inv[b]]
    for i in range(seq // step):
        part = slice(i * step, (i + 1) * step)
        out = nn(n1s[part, :], w_s[...])
        cos2 = jnp.concatenate([cosine[part, :]] * (lanes // 128), axis=1)
        sin2 = jnp.concatenate([sine[part, :]] * (lanes // 128), axis=1)
        q = spin(out[:, :lanes], cos2, sin2).astype(jnp.bfloat16)
        qkv[part, :lanes] = q * jnp.asarray(HEAD_DIM**-0.5, jnp.bfloat16)
        qkv[part, lanes : 2 * lanes] = spin(out[:, lanes : 2 * lanes], cos2, sin2).astype(jnp.bfloat16)
        qkv[part, 2 * lanes :] = out[:, 2 * lanes :].astype(jnp.bfloat16)
    lane = lax.broadcasted_iota(jnp.int32, (step, 128), 1)
    for i in range(seq // step):
        part = slice(i * step, (i + 1) * step)
        span = (i + 1) * step
        seen = lax.broadcasted_iota(jnp.int32, (step, span), 1) <= (
            lax.broadcasted_iota(jnp.int32, (step, span), 0) + i * step
        )
        logs = jnp.zeros((step, 128), jnp.float32)
        for head in range(GROUP_HEADS):
            tile, side = head // 2, head % 2
            at = tile * 128
            mine = lane // 64 == side
            q = jnp.where(mine, qkv[part, at : at + 128], jnp.asarray(0, jnp.bfloat16))
            s = nt(q, qkv[:span, lanes + at : lanes + at + 128])
            s = jnp.where(seen, s, -1e30)
            top = jnp.max(s, axis=1, keepdims=True)
            p = jnp.exp(s - top)
            total = jnp.sum(p, axis=1, keepdims=True)
            out = nn(p.astype(jnp.bfloat16), qkv[:span, 2 * lanes + at : 2 * lanes + at + 128]) / total
            logs = jnp.where(lane == head, top + jnp.log(total), logs)
            if side == 0:
                kept = jnp.where(mine, out, 0.0)
            else:
                kept = jnp.where(mine, out, kept)
            o[part, at : at + 128] = kept
        lse[part, :] = logs
        osort[2 * i] = o[part, :][:blk].astype(jnp.bfloat16)
        osort[2 * i + 1] = o[part, :][blk:].astype(jnp.bfloat16)

    mine_at = 2 * z + k
    remote(wo_s.at[over], wo_s.at[over], v_send.at[0], v_recv.at[0], own, over).wait_recv()
    v_on.start()

    def o_copy(ctx):
        return remote(osend.at[ctx], orecv.at[mine_at], o_send.at[ctx], o_recv.at[mine_at], ctx, 2 * y + xx)

    for ctx in range(blocks):
        alone = jnp.logical_and(same, ctx == own)
        osend[ctx] = osort[order[ctx]]

        @pl.when(jnp.logical_not(alone))
        def _():
            o_copy(ctx).start()

        @pl.when(alone)
        def _():
            orecv[mine_at] = osend[ctx]

    for src in range(blocks):

        @pl.when(jnp.logical_not(jnp.logical_and(same, src == mine_at)))
        def _():
            remote(osend.at[0], orecv.at[src], o_send.at[0], o_recv.at[src], 2 * (src // 2) + k, 2 * y + src % 2).wait_recv()

    ob[...] = orecv[...]
    remote(wo_s.at[beside], wo_s.at[beside], v_send.at[1], v_recv.at[1], own, beside).wait_recv()
    remote(wo_s.at[corner], wo_s.at[corner], v_send.at[2], v_recv.at[2], own, beside).wait_recv()
    wo[...] = wo_s[...]
    total, low = post_attention(orecv[...], x[...], wo_s[...], small[1:2, :].astype(jnp.float32))
    hst[...] = total
    ub[...] = low
    for zz in range(depth):

        @pl.when(jnp.logical_not(jnp.logical_and(same, zz == z)))
        def _():
            n1_copy(zz).wait_send()

        forward_copy(zz).wait_send()
    for index in range(3):
        w_copy(index).wait_send()
    v_far.wait_send()
    v_near.wait_send()
    v_on.wait_send()
    for ctx in range(blocks):

        @pl.when(jnp.logical_not(jnp.logical_and(same, ctx == own)))
        def _():
            o_copy(ctx).wait_send()


def attn_forward(layer, order, inv, x, small, wq, cosine, sine, wo, number):
    count, width = x.shape
    blocks, blk = order.shape[0], count // 2
    packs, inner = width // wo.shape[1], wo.shape[1]
    lanes = -(-inner // 128) * 128
    seq = blocks * blk
    vm = pl.BlockSpec(memory_space=pltpu.VMEM)
    sm = pl.BlockSpec(memory_space=pltpu.SMEM)
    bf = jnp.bfloat16
    dma = pltpu.SemaphoreType.DMA
    return pl.pallas_call(
        attn_fwd_kernel,
        grid=(1,),
        out_shape=[
            shape_of((seq, width), bf),
            shape_of((seq, 3 * lanes), bf),
            shape_of((seq, lanes), jnp.float32),
            shape_of((seq, 128), jnp.float32),
            shape_of((blocks, blk, lanes), bf),
            shape_of((count, width), jnp.float32),
            shape_of((count, width), bf),
            shape_of((width, 3 * lanes), bf),
            shape_of((packs, inner, width), bf),
        ],
        in_specs=[sm, sm, vm, vm]
        + [pl.BlockSpec((1, 3, inner, width), lambda _: (layer, 0, 0, 0)), vm, vm]
        + [pl.BlockSpec((1, inner, width), lambda _: (layer, 0, 0))],
        out_specs=[vm] * 9,
        scratch_shapes=[
            pltpu.VMEM((2, blk, width), bf),
            pltpu.VMEM((blocks, blk, width), bf),
            pltpu.VMEM((blocks, blk, lanes), bf),
            pltpu.VMEM((blocks, blk, lanes), bf),
            pltpu.VMEM((blocks, blk, lanes), bf),
            pltpu.VMEM((2, inner, 3 * lanes), bf),
            pltpu.VMEM((width, 3 * lanes), bf),
            pltpu.VMEM((packs, inner, width), bf),
        ]
        + [dma((blocks // 2,))] * 4
        + [dma((blocks,))] * 2
        + [dma((3,))] * 4,
        compiler_params=params_of(collective_id=number, has_side_effects=True),
        cost_estimate=BRIEF,
        name="attn_fwd",
    )(order, inv, x, small, wq, cosine, sine, wo)


def attn_bwd_kernel(
    order, inv, n1s, w, cosine, sine, qkv, o, lse, go, ghst, x, small, gsmall, gwo,
    gx, gm, dense,
    gor, gos, grads, acc, gns, sib_out, sib_in, gn_out, gnr, gw, gw_in, both, both_in, wo_in, wo_both, wo_over, probs,
    o_send, o_recv, s_send, s_recv, g_send, g_recv, r_send, r_recv, w_send, w_recv,
):
    blocks, blk, width = grads.shape
    lanes = o.shape[1]
    seq = blocks * blk
    step = 2 * blk
    zero = jnp.asarray(0, jnp.bfloat16)
    own = lax.axis_index("ctx")
    z, xx, y, k = place()
    depth = blocks // 2
    same = xx == k

    barrier, others = greet_plane(blocks, across=True)
    acc[...] = jnp.zeros_like(acc)
    pl.semaphore_wait(barrier, others)

    def go_copy(unit):
        return remote(go.at[unit], gor.at[own], o_send.at[unit], o_recv.at[own], 2 * (unit // 2) + k, 2 * y + unit % 2)

    for unit in range(blocks):
        alone = jnp.logical_and(same, unit == 2 * z + k)

        @pl.when(jnp.logical_not(alone))
        def _():
            go_copy(unit).start()

        @pl.when(alone)
        def _():
            gor[own] = go[unit]

    def wo_copy(half):
        return remote(
            gwo.at[2 * half + 1 - k], wo_in.at[half], w_send.at[half], w_recv.at[half], own, 2 * y + 1 - k
        )

    wo_far = remote(wo_both.at[1 - y], wo_over, w_send.at[2], w_recv.at[2], own, 2 * (1 - y) + k)
    wo_copy(0).start()
    wo_copy(1).start()
    lane = lax.broadcasted_iota(jnp.int32, (step, 128), 1)
    for i in range(seq // step):
        part = slice(i * step, (i + 1) * step)
        span = (i + 1) * step
        seen = lax.broadcasted_iota(jnp.int32, (step, span), 1) <= (
            lax.broadcasted_iota(jnp.int32, (step, span), 0) + i * step
        )
        for head in range(GROUP_HEADS):
            at = head // 2 * 128
            q = jnp.where(lane // 64 == head % 2, qkv[part, at : at + 128], zero)
            s = nt(q, qkv[:span, lanes + at : lanes + at + 128])
            p = jnp.exp(jnp.where(seen, s, -1e30) - lse[part, head : head + 1])
            probs[head, part, :span] = jnp.where(seen, p, 0.0)
    for ctx in range(blocks):

        @pl.when(jnp.logical_not(jnp.logical_and(same, ctx == own)))
        def _():
            remote(go.at[0], gor.at[ctx], o_send.at[0], o_recv.at[ctx], ctx, 2 * y + xx).wait_recv()

    for half in range(2):
        wo_copy(half).wait_recv()
        total = gwo[2 * half + k].astype(jnp.float32) + wo_in[half].astype(jnp.float32)
        wo_both[half] = total.astype(jnp.bfloat16)
    wo_far.start()
    for b in range(blocks):
        gos[b * blk : (b + 1) * blk, :] = gor[inv[b]]
    for i in range(seq // step):
        part = slice(i * step, (i + 1) * step)
        span = (i + 1) * step
        key_lane = lax.broadcasted_iota(jnp.int32, (span, 128), 1)
        for head in range(GROUP_HEADS):
            tile, side = head // 2, head % 2
            at = tile * 128
            mine = lane // 64 == side
            q = jnp.where(mine, qkv[part, at : at + 128], zero)
            g = jnp.where(mine, gos[part, at : at + 128], zero)
            keys = qkv[:span, lanes + at : lanes + at + 128]
            values = qkv[:span, 2 * lanes + at : 2 * lanes + at + 128]
            delta = jnp.sum(g.astype(jnp.float32) * o[part, at : at + 128], axis=1, keepdims=True)
            p = probs[head, part, :span]
            ds = (p * (nt(g, values) - delta)).astype(jnp.bfloat16)
            acc[:span, 2 * lanes + at : 2 * lanes + at + 128] += tn(p.astype(jnp.bfloat16), g)
            acc[:span, lanes + at : lanes + at + 128] += tn(ds, q)
            acc[part, at : at + 128] += nn(ds, jnp.where(key_lane // 64 == side, keys, zero))
    for b in range(blocks):
        part = slice(b * blk, (b + 1) * blk)
        cos2 = jnp.concatenate([cosine[part, :]] * (lanes // 128), axis=1)
        sin2 = jnp.concatenate([sine[part, :]] * (lanes // 128), axis=1)
        grads[b, :, :lanes] = spin(acc[part, :lanes] * HEAD_DIM**-0.5, cos2, -sin2).astype(jnp.bfloat16)
        grads[b, :, lanes : 2 * lanes] = spin(acc[part, lanes : 2 * lanes], cos2, -sin2).astype(jnp.bfloat16)
        grads[b, :, 2 * lanes :] = acc[part, 2 * lanes :].astype(jnp.bfloat16)

    def sib_copy(zz):
        return remote(sib_out.at[zz], sib_in.at[zz], s_send.at[zz], s_recv.at[zz], own, 2 * y + 1 - k)

    def gn_copy(zz):
        return remote(gn_out.at[zz], gnr.at[z], g_send.at[zz], g_recv.at[z], 2 * zz + k, 2 * y + xx)

    gain = small[0:1, :].astype(jnp.float32)
    ggain = jnp.zeros((1, width), jnp.float32)
    for b in range(blocks):
        gns[b] = nt(grads[b], w[...])
        ggain = ggain + jnp.sum(gns[b] * n1s[b * blk : (b + 1) * blk, :].astype(jnp.float32), axis=0, keepdims=True)
    for zz in range(depth):
        sib_out[zz] = gns[order[2 * zz + 1 - k]].astype(jnp.bfloat16)
        sib_copy(zz).start()
    for zz in range(depth):
        sib_copy(zz).wait_recv()
        alone = jnp.logical_and(same, zz == z)
        gn_out[zz] = (gns[order[2 * zz + k]] + sib_in[zz].astype(jnp.float32)).astype(jnp.bfloat16)

        @pl.when(jnp.logical_not(alone))
        def _():
            gn_copy(zz).start()

        @pl.when(alone)
        def _():
            gnr[z] = gn_out[zz]

    packs, inner = gwo.shape[0], gwo.shape[1]
    sums = jnp.concatenate([ggain / gain, gsmall[...]], axis=0)
    sums = jnp.concatenate([sums, jnp.zeros((128 - sums.shape[0], width), jnp.float32)], axis=0)
    gw[:, :128] = jnp.transpose(sums).astype(jnp.bfloat16)
    gw[:, 128 + 3 * inner :] = jnp.zeros((width, gw.shape[1] - 128 - 3 * inner), jnp.bfloat16)
    for i in range(width // 256):
        part = slice(i * 256, (i + 1) * 256)
        piece = tn(n1s[:, part], grads[...].reshape(seq, 3 * lanes)).astype(jnp.bfloat16)
        for c in range(3):
            gw[part, 128 + c * inner : 128 + (c + 1) * inner] = piece[:, c * lanes : c * lanes + inner]

    def rows_of(f):
        return pl.ds(pl.multiple_of(f * inner, inner), inner)

    def home_copy(half):
        rows = gw.at[rows_of(2 * half + 1 - k), :]
        return remote(rows, gw_in.at[half], r_send.at[half], r_recv.at[half], own, 2 * y + 1 - k)

    for half in range(2):
        home_copy(half).start()
    for half in range(2):
        home_copy(half).wait_recv()
        kept, came = gw[rows_of(2 * half + k), :], gw_in[half]
        both[half, :, :128] = (kept[:, :128].astype(jnp.float32) + came[:, :128].astype(jnp.float32)).astype(jnp.bfloat16)
        heads = slice(128, 128 + 3 * inner)
        for core in range(2):

            @pl.when(k == core)
            def _():
                both[half, :, 128 + core * 3 * inner : 128 + (core + 1) * 3 * inner] = kept[:, heads]
                both[half, :, 128 + (1 - core) * 3 * inner : 128 + (2 - core) * 3 * inner] = came[:, heads]

    over = remote(both.at[1 - y], both_in, r_send.at[2], r_recv.at[2], own, 2 * (1 - y) + k)
    over.start()
    values = x[...]
    factor = rms_factor(values)
    base = values * factor
    for zz in range(depth):

        @pl.when(jnp.logical_not(jnp.logical_and(same, zz == z)))
        def _():
            remote(gn_out.at[0], gnr.at[zz], g_send.at[0], g_recv.at[zz], 2 * zz + k, 2 * y + xx).wait_recv()

    halves = []
    for h in range(2):
        total = gnr[h * (depth // 2)].astype(jnp.float32)
        for zz in range(1, depth // 2):
            total = total + gnr[h * (depth // 2) + zz].astype(jnp.float32)
        halves.append(total)
    gn = jnp.concatenate(halves, axis=0)
    gb = gn * gain
    grad = ghst[...] + factor * (gb - base * jnp.mean(gb * base, axis=-1, keepdims=True))
    gx[...] = grad
    gm[...] = grad.astype(jnp.bfloat16)
    wo_far.wait_recv()
    edge = both.shape[2]
    dense[:, edge:] = (wo_both[y].astype(jnp.float32) + wo_over[...].astype(jnp.float32)).astype(jnp.bfloat16)
    over.wait_recv()
    dense[:, :edge] = (both[y].astype(jnp.float32) + both_in[...].astype(jnp.float32)).astype(jnp.bfloat16)
    for half in range(2):
        home_copy(half).wait_send()
        wo_copy(half).wait_send()
    wo_far.wait_send()
    over.wait_send()
    for unit in range(blocks):

        @pl.when(jnp.logical_not(jnp.logical_and(same, unit == 2 * z + k)))
        def _():
            go_copy(unit).wait_send()

    for zz in range(depth):
        sib_copy(zz).wait_send()

        @pl.when(jnp.logical_not(jnp.logical_and(same, zz == z)))
        def _():
            gn_copy(zz).wait_send()


def attn_backward(order, inv, n1s, w, cosine, sine, qkv, o, lse, go, ghst, x, small, gsmall, gwo, number):
    blocks, blk, lanes = go.shape
    seq, width = n1s.shape
    count = x.shape[0]
    packs, inner = gwo.shape[0], gwo.shape[1]
    depth = blocks // 2
    vm = pl.BlockSpec(memory_space=pltpu.VMEM)
    sm = pl.BlockSpec(memory_space=pltpu.SMEM)
    bf = jnp.bfloat16
    dma = pltpu.SemaphoreType.DMA
    return pl.pallas_call(
        attn_bwd_kernel,
        out_shape=[
            shape_of((count, width), jnp.float32),
            shape_of((count, width), bf),
            shape_of((inner, 128 + 6 * inner + width), bf),
        ],
        in_specs=[sm] * 2 + [vm] * 13,
        out_specs=[vm] * 3,
        scratch_shapes=[
            pltpu.VMEM((blocks, blk, lanes), bf),
            pltpu.VMEM((seq, lanes), bf),
            pltpu.VMEM((blocks, blk, 3 * lanes), bf),
            pltpu.VMEM((seq, 3 * lanes), jnp.float32),
            pltpu.VMEM((blocks, blk, width), jnp.float32),
            pltpu.VMEM((depth, blk, width), bf),
            pltpu.VMEM((depth, blk, width), bf),
            pltpu.VMEM((depth, blk, width), bf),
            pltpu.VMEM((depth, blk, width), bf),
            pltpu.VMEM((packs * inner, 3 * lanes), bf),
            pltpu.VMEM((2, inner, 3 * lanes), bf),
            pltpu.VMEM((2, inner, 128 + 6 * inner), bf),
            pltpu.VMEM((inner, 128 + 6 * inner), bf),
            pltpu.VMEM((2, inner, width), bf),
            pltpu.VMEM((2, inner, width), bf),
            pltpu.VMEM((inner, width), bf),
            pltpu.VMEM((GROUP_HEADS, seq, seq), jnp.float32),
        ]
        + [dma((blocks,))] * 2
        + [dma((depth,))] * 4
        + [dma((3,))] * 4,
        compiler_params=params_of(collective_id=number, has_side_effects=True),
        cost_estimate=BRIEF,
        name="attn_bwd",
    )(order, inv, n1s, w, cosine, sine, qkv, o, lse, go, ghst, x, small, gsmall, gwo)


def routing(raw, before, routes):
    count = raw.shape[1]
    ids = lax.broadcasted_iota(jnp.int32, (16, count), 0)
    logits = raw + before
    first, second = ids == routes[0:1], ids == routes[1:2]
    z0 = jnp.sum(jnp.where(first, logits, 0.0), axis=0, keepdims=True)
    z1 = jnp.sum(jnp.where(second, logits, 0.0), axis=0, keepdims=True)
    top = jnp.maximum(z0, z1)
    e0, e1 = jnp.exp(z0 - top), jnp.exp(z1 - top)
    total = e0 + e1
    coef = jnp.where(first, e0 / total, 0.0) + jnp.where(second, e1 / total, 0.0)
    hits = jnp.where(first | second, 1.0, 0.0)
    upto = lax.broadcasted_iota(jnp.int32, (count, count), 0) <= lax.broadcasted_iota(jnp.int32, (count, count), 1)
    place = nn(hits.astype(jnp.bfloat16), jnp.where(upto, 1.0, 0.0).astype(jnp.bfloat16)) - 1.0
    slot = jnp.where(hits > 0, place, -1.0)
    return jnp.concatenate([raw, coef, slot[:NF], logits], axis=0)


def one_hot(slot):
    count = slot.shape[1]
    ids = lax.broadcasted_iota(jnp.int32, (NF, MOST, count), 1)
    hit = ids == slot.astype(jnp.int32)[:, None, :]
    return jnp.where(hit, 1.0, 0.0).reshape(NF * MOST, count)


def slot_values(hot, rows):
    count = rows.shape[1]
    wide = jnp.broadcast_to(rows[:, None, :], (NF, MOST, count)).reshape(NF * MOST, count)
    return jnp.sum(hot * wide, axis=1, keepdims=True)


def swap_rows(own, rows, send, recv, forward_send, forward_recv):
    ctx = lax.axis_index("ctx")
    _, _, y, k = place()
    beside, across = 2 * y + 1 - k, 2 * (1 - y) + k
    far = remote(own, rows.at[2], send.at[0], recv.at[0], ctx, across)
    near = remote(own, rows.at[1], send.at[1], recv.at[1], ctx, beside)
    onward = remote(rows.at[2], rows.at[3], forward_send, forward_recv, ctx, beside)
    far.start()
    near.start()
    return near, far, onward


def sum_rows(parts, beside_in, mid, across_in, send, recv):
    ctx = lax.axis_index("ctx")
    _, _, y, k = place()
    beside, across = 2 * y + 1 - k, 2 * (1 - y) + k
    first = remote(parts.at[3], beside_in.at[1], send.at[0], recv.at[0], ctx, beside)
    second = remote(parts.at[1], beside_in.at[0], send.at[1], recv.at[1], ctx, beside)
    third = remote(mid, across_in, send.at[2], recv.at[2], ctx, across)
    return first, second, third


def ffn_fwd_kernel(
    ub, hst, small, routes, before, wgu, wd,
    ubf, table, ext, x_next,
    rows_s, hot_s, x_s, y_s, coef_s, parts, beside_in, mid, across_in,
    a_send, a_recv, r_send, r_recv,
):
    e = pl.program_id(0)
    packs = ubf.shape[0]
    count, width = ub.shape
    router = small[2 + NC :, :]

    def gathers():
        return swap_rows(ub, rows_s, a_send, a_recv, a_send.at[2], a_recv.at[2])

    def sums():
        return sum_rows(parts, beside_in, mid, across_in, r_send, r_recv)

    @pl.when(e == 0)
    def _():
        barrier, others = greet_packs()
        rows_s[0] = ub[...]

        def prepare(d):
            rows = routing(nt(router, rows_s[d]), before[d, LOGI : LOGI + 16, :], routes[d])
            table[d] = rows
            hot = one_hot(rows[SLOT : SLOT + NF])
            coef_s[d] = slot_values(hot, rows[COEF : COEF + NF])
            hot_low = hot.astype(jnp.bfloat16)
            hot_s[d] = hot_low
            x = nn(hot_low, rows_s[d]).astype(jnp.bfloat16)
            for n in range(NF):
                x_s[n, d * MOST : (d + 1) * MOST, :] = x[n * MOST : (n + 1) * MOST]

        pl.semaphore_wait(barrier, others)
        near, far, onward = gathers()
        prepare(0)
        near.wait_recv()
        prepare(1)
        far.wait_recv()
        onward.start()
        prepare(2)
        onward.wait_recv()
        prepare(3)
        ubf[...] = rows_s[...]
        ext[:count, :] = ub[...]
        rows = table[0]
        ext[count:, :] = jnp.zeros((16, width), jnp.bfloat16)
        ext[count:, :count] = rows[COEF : COEF + 16].astype(jnp.bfloat16)
        slots = jnp.concatenate([rows[SLOT : SLOT + NF], jnp.zeros((16 - NF, count), jnp.float32)], axis=0)
        ext[count:, count : 2 * count] = slots.astype(jnp.bfloat16)
        near.wait_send()
        far.wait_send()
        onward.wait_send()

    x = x_s[e]
    gate, up = nn(x, wgu[0, 0, 0]), nn(x, wgu[0, 0, 1])
    hid = (gate * jax.nn.sigmoid(gate) * up).astype(jnp.bfloat16)
    out = nn(hid, wd[0, 0])
    at = pl.ds(pl.multiple_of(e * MOST, MOST), MOST)
    for d in range(packs):
        y_s[d, at, :] = (out[d * MOST : (d + 1) * MOST] * coef_s[d, at, :]).astype(jnp.bfloat16)

    @pl.when(e == NF - 1)
    def _():
        first, second, third = sums()
        parts[3] = tn(hot_s[3], y_s[3]).astype(jnp.bfloat16)
        first.start()
        parts[1] = tn(hot_s[1], y_s[1]).astype(jnp.bfloat16)
        second.start()
        away = tn(hot_s[2], y_s[2])
        first.wait_recv()
        mid[...] = (away + beside_in[1].astype(jnp.float32)).astype(jnp.bfloat16)
        third.start()
        home = tn(hot_s[0], y_s[0])
        _, _, scale_u, scale_c = mixing_rows(table[0])
        columns = to_columns([scale_u] + scale_c)
        values = hst[...]
        moe = home + columns[0] * ((values * rms_factor(values)) * small[1:2, :].astype(jnp.float32))
        for c in range(NC):
            moe = moe + columns[1 + c] * small[2 + c : 3 + c, :].astype(jnp.float32)
        second.wait_recv()
        moe = moe + beside_in[0].astype(jnp.float32)
        third.wait_recv()
        x_next[...] = values + (moe + across_in[...].astype(jnp.float32))
        first.wait_send()
        second.wait_send()
        third.wait_send()


def whole_spec(dims):
    return pl.BlockSpec(dims, lambda *_: (0,) * len(dims))


def exchange_scratch(packs, count, width):
    bf = jnp.bfloat16
    return [
        pltpu.VMEM((packs, count, width), bf),
        pltpu.VMEM((2, count, width), bf),
        pltpu.VMEM((count, width), bf),
        pltpu.VMEM((count, width), bf),
    ]


def ffn_forward(layer, ub, hst, small, routes, before, wgu, wd, number):
    count, width = ub.shape
    packs = routes.shape[0]
    hidden = wd.shape[2]
    bf = jnp.bfloat16
    outs = [
        shape_of((packs, count, width), bf),
        shape_of((packs, ROUT, count), jnp.float32),
        shape_of((count + 16, width), bf),
        shape_of((count, width), jnp.float32),
    ]
    return pl.pallas_call(
        ffn_fwd_kernel,
        grid=(NF,),
        out_shape=outs,
        in_specs=[whole_spec(a.shape) for a in (ub, hst, small, routes, before)]
        + [
            pl.BlockSpec((1, 1, 2, width, hidden), lambda e: (layer, e, 0, 0, 0)),
            pl.BlockSpec((1, 1, hidden, width), lambda e: (layer, e, 0, 0)),
        ],
        out_specs=[whole_spec(a.shape) for a in outs],
        scratch_shapes=[
            pltpu.VMEM((packs, count, width), bf),
            pltpu.VMEM((packs, NF * MOST, count), bf),
            pltpu.VMEM((NF, packs * MOST, width), bf),
            pltpu.VMEM((packs, NF * MOST, width), bf),
            pltpu.VMEM((packs, NF * MOST, 1), jnp.float32),
        ]
        + exchange_scratch(packs, count, width)
        + [pltpu.SemaphoreType.DMA((3,))] * 4,
        compiler_params=params_of(collective_id=number, has_side_effects=True),
        cost_estimate=BRIEF,
        name="ffn_fwd",
    )(ub, hst, small, routes, before, wgu, wd)


def silu_parts(gate, up, ghid):
    sig = jax.nn.sigmoid(gate)
    act = gate * sig
    dg = (ghid * up * sig * (1.0 + gate * (1.0 - sig))).astype(jnp.bfloat16)
    du = (ghid * act).astype(jnp.bfloat16)
    return act * up, dg, du


def ffn_bwd_kernel(
    gm, gx, ubf, table, hst, small, routes, gprev, wo, ob, wgu, wd,
    ghst, go, gwo, gsmall, glog,
    rows_s, hot_s, x_s, g_s, y_s, coef_s, gc_s, gcoef, gcoef_in, parts, beside_in, mid, across_in,
    a_send, a_recv, r_send, r_recv, c_send, c_recv,
):
    e = pl.program_id(0)
    packs = ubf.shape[0]
    ctx = lax.axis_index("ctx")
    _, _, y, k = place()
    peers = [None, 2 * y + 1 - k, 2 * (1 - y) + k, 2 * (1 - y) + 1 - k]

    def gathers():
        return swap_rows(gm, rows_s, a_send, a_recv, a_send.at[2], a_recv.at[2])

    def sums():
        return sum_rows(parts, beside_in, mid, across_in, r_send, r_recv)

    @pl.when(e == 0)
    def _():
        barrier, others = greet_packs()
        rows_s[0] = gm[...]

        def prepare(d):
            hot = one_hot(table[d, SLOT : SLOT + NF, :])
            coef_s[d] = slot_values(hot, table[d, COEF : COEF + NF, :])
            hot_low = hot.astype(jnp.bfloat16)
            hot_s[d] = hot_low
            x = nn(hot_low, ubf[d]).astype(jnp.bfloat16)
            for n in range(NF):
                x_s[n, d * MOST : (d + 1) * MOST, :] = x[n * MOST : (n + 1) * MOST]

        def spread(d):
            g = nn(hot_s[d], rows_s[d]).astype(jnp.bfloat16)
            for n in range(NF):
                g_s[n, d * MOST : (d + 1) * MOST, :] = g[n * MOST : (n + 1) * MOST]

        pl.semaphore_wait(barrier, others)
        near, far, onward = gathers()
        for d in range(packs):
            prepare(d)
        spread(0)
        near.wait_recv()
        far.wait_recv()
        onward.start()
        spread(1)
        spread(2)
        onward.wait_recv()
        spread(3)
        near.wait_send()
        far.wait_send()
        onward.wait_send()

    x = x_s[e]
    at = pl.ds(pl.multiple_of(e * MOST, MOST), MOST)
    coef = jnp.concatenate([coef_s[d, at, :] for d in range(packs)], axis=0)
    gate, up = nn(x, wgu[0, 0, 0]), nn(x, wgu[0, 0, 1])
    ghid = nt(g_s[e], wd[0, 0])
    hid, dg, du = silu_parts(gate, up, ghid * coef)
    dots = jnp.sum(hid * ghid, axis=1, keepdims=True)
    out = nt(dg, wgu[0, 0, 0]) + nt(du, wgu[0, 0, 1])
    for d in range(packs):
        y_s[d, at, :] = out[d * MOST : (d + 1) * MOST].astype(jnp.bfloat16)
        gc_s[d, at, :] = dots[d * MOST : (d + 1) * MOST]

    @pl.when(e == NF - 1)
    def _():
        first, second, third = sums()

        def coef_copy(d):
            return remote(gcoef.at[d], gcoef_in.at[d - 1], c_send.at[d - 1], c_recv.at[d - 1], ctx, peers[d])

        parts[3] = tn(hot_s[3], y_s[3]).astype(jnp.bfloat16)
        first.start()
        parts[1] = tn(hot_s[1], y_s[1]).astype(jnp.bfloat16)
        second.start()
        for d in range(packs):
            wide = hot_s[d].astype(jnp.float32) * gc_s[d]
            gcoef[d] = jnp.sum(wide.reshape(NF, MOST, wide.shape[1]), axis=1)
            if d > 0:
                coef_copy(d).start()
        away = tn(hot_s[2], y_s[2])
        first.wait_recv()
        mid[...] = (away + beside_in[1].astype(jnp.float32)).astype(jnp.bfloat16)
        third.start()
        home = tn(hot_s[0], y_s[0])
        ready = middle_ready(gx[...], table[0], hst[...], small[...])
        second.wait_recv()
        home = home + beside_in[0].astype(jnp.float32)
        total = gcoef[0]
        for d in range(1, packs):
            coef_copy(d).wait_recv()
            total = total + gcoef_in[d - 1]
        third.wait_recv()
        home = home + across_in[...].astype(jnp.float32)
        results = middle(
            ready, gx[...], home, total, table[0], routes[...], gprev[...], ubf[0], small[...], wo[...], ob[...]
        )
        for ref, value in zip((ghst, go, gwo, gsmall, glog), results):
            ref[...] = value
        first.wait_send()
        second.wait_send()
        third.wait_send()
        for d in range(1, packs):
            coef_copy(d).wait_send()


def ffn_backward(layer, gm, gx, ubf, table, hst, small, routes, gprev, wo, ob, wgu, wd, number):
    packs, count, width = ubf.shape
    hidden = wd.shape[2]
    bf, f32 = jnp.bfloat16, jnp.float32
    outs = [
        shape_of((count, width), f32),
        shape_of(ob.shape, bf),
        shape_of(wo.shape, bf),
        shape_of((1 + NC + 16, width), f32),
        shape_of((16, count), f32),
    ]
    args = (gm, gx, ubf, table, hst, small, routes, gprev, wo, ob)
    dma = pltpu.SemaphoreType.DMA
    return pl.pallas_call(
        ffn_bwd_kernel,
        grid=(NF,),
        out_shape=outs,
        in_specs=[whole_spec(a.shape) for a in args]
        + [
            pl.BlockSpec((1, 1, 2, width, hidden), lambda e: (layer, e, 0, 0, 0)),
            pl.BlockSpec((1, 1, hidden, width), lambda e: (layer, e, 0, 0)),
        ],
        out_specs=[whole_spec(a.shape) for a in outs],
        scratch_shapes=[
            pltpu.VMEM((packs, count, width), bf),
            pltpu.VMEM((packs, NF * MOST, count), bf),
            pltpu.VMEM((NF, packs * MOST, width), bf),
            pltpu.VMEM((NF, packs * MOST, width), bf),
            pltpu.VMEM((packs, NF * MOST, width), bf),
            pltpu.VMEM((packs, NF * MOST, 1), f32),
            pltpu.VMEM((packs, NF * MOST, 1), f32),
            pltpu.VMEM((packs, NF, count), f32),
            pltpu.VMEM((packs - 1, NF, count), f32),
        ]
        + exchange_scratch(packs, count, width)
        + [dma((3,))] * 6,
        compiler_params=params_of(collective_id=number, has_side_effects=True),
        cost_estimate=BRIEF,
        name="ffn_bwd",
    )(*args, wgu, wd)


PACK = 80


def pack_kernel(counts, bases, totals, tail, ext, gm, out, buf, carry, blank, sems):
    step = pl.program_id(0)
    some, count, width = gm.shape

    @pl.when(step == 0)
    def _():
        carry[...] = jnp.zeros_like(carry)
        blank[...] = jnp.zeros_like(blank)

    def whole_groups(d, e):
        at = d * NF + e
        return (bases[at] % 16 + counts[at]) // 16

    def each_copy(block, what):
        for i in range(some):
            for e in range(NF):
                groups = whole_groups(block * some + i, e)
                start = pl.multiple_of(bases[(block * some + i) * NF + e] // 16 * 16, 16)
                for n in range(1, PACK // 16):

                    @pl.when(groups == n)
                    def _():
                        source = buf.at[block % 2, i, e, pl.ds(0, 16 * n), :]
                        what(pltpu.make_async_copy(source, out.at[e, pl.ds(start, 16 * n), :], sems.at[block % 2, i, e]))

    def begin(copy):
        copy.start()

    def end(copy):
        copy.wait()

    @pl.when(step >= 2)
    def _():
        each_copy(step - 2, end)

    ids = lax.broadcasted_iota(jnp.int32, (PACK, count), 0)
    side = step % 2
    for i in range(some):
        d = step * some + i
        rows = tail[i].astype(jnp.float32)
        slot = rows[:NF, count : 2 * count].astype(jnp.int32)
        slot = jnp.where(slot < 0, -PACK, slot)
        hot, weighted = [], []
        for e in range(NF):
            hit = ids == slot[e : e + 1] + bases[d * NF + e] % 16
            hot.append(jnp.where(hit, 1.0, 0.0).astype(jnp.bfloat16))
            weighted.append(jnp.where(hit, rows[e : e + 1, :count], 0.0).astype(jnp.bfloat16))
        low = nn(jnp.concatenate(hot, axis=0), ext[i, :count, :]).astype(jnp.bfloat16)
        low_g = nn(jnp.concatenate(weighted, axis=0), gm[i]).astype(jnp.bfloat16)
        for lanes, values in ((slice(0, width), low), (slice(width, 2 * width), low_g)):
            for e in range(NF):
                buf[side, i, e, :, lanes] = values[e * PACK : (e + 1) * PACK]
    for i in range(some):
        for e in range(NF):
            buf[side, i, e, :16, :] += carry[e]
            group = pl.multiple_of(whole_groups(step * some + i, e) * 16, 16)
            carry[e] = buf[side, i, e, pl.ds(group, 16), :]
    each_copy(step, begin)

    @pl.when(step == pl.num_programs(0) - 1)
    def _():
        last = pl.num_programs(0)
        each_copy(last - 2, end)
        each_copy(last - 1, end)
        copies = []
        for e in range(NF):
            start = pl.multiple_of(totals[e] // 16 * 16, 16)
            copies.append(pltpu.make_async_copy(carry.at[e], out.at[e, pl.ds(start, 16), :], sems.at[0, 0, e]))
            rest = out.at[e, pl.ds(start + 16, blank.shape[0]), :]
            copies.append(pltpu.make_async_copy(blank, rest, sems.at[1, 0, e]))
        for copy in copies:
            copy.start()
        for copy in copies:
            copy.wait()


def expert_counts(ext):
    count = ext.shape[2] // 3
    slot = ext[:, ext.shape[1] - 16 : ext.shape[1] - 16 + NF, count : 2 * count].astype(jnp.float32)
    counts = (jnp.max(slot, axis=2) + 1.0).astype(jnp.int32)
    upto = jnp.cumsum(counts, axis=0)
    return counts.reshape(-1), (upto - counts).reshape(-1), upto[-1]


def pack_rows(numbers, ext, gm):
    devices, count, width = gm.shape
    some, blank = 4, 256
    bf = jnp.bfloat16
    return pl.pallas_call(
        pack_kernel,
        grid_spec=pltpu.PrefetchScalarGridSpec(
            num_scalar_prefetch=3,
            grid=(devices // some,),
            in_specs=[
                pl.BlockSpec((some, 16, width), lambda d, *_: (d, count // 16, 0)),
                pl.BlockSpec((some,) + ext.shape[1:], lambda d, *_: (d, 0, 0)),
                pl.BlockSpec((some, count, width), lambda d, *_: (d, 0, 0)),
            ],
            out_specs=pl.BlockSpec(memory_space=pl.ANY),
            scratch_shapes=[
                pltpu.VMEM((2, some, NF, PACK, 2 * width), bf),
                pltpu.VMEM((NF, 16, 2 * width), bf),
                pltpu.VMEM((blank, 2 * width), bf),
                pltpu.SemaphoreType.DMA((2, some, NF)),
            ],
        ),
        out_shape=shape_of((NF, devices * MOST + 16 + blank, 2 * width), bf),
        compiler_params=params_of(),
        cost_estimate=BRIEF,
        name="pack_rows",
    )(*numbers, ext, ext, gm)


def dw_kernel(first, totals, packed, wgu, wd, *refs):
    dgu, dd, pair_s, hid_s = refs[-4:]
    hidden = hid_s.shape[1]
    total = totals[first + pl.program_id(0)]
    width = packed.shape[2] // 2
    chunk = 1024

    def pieces(part):
        xs, gs = packed[0, part, :width], packed[0, part, width:]
        hid, dg, du = silu_parts(nn(xs, wgu[0, 0, 0]), nn(xs, wgu[0, 0, 1]), nt(gs, wd[0, 0]))
        hid_s[part, :] = hid.astype(jnp.bfloat16)
        pair_s[part, :hidden] = dg
        pair_s[part, hidden:] = du

    def chunk_of(i, _):
        pieces(pl.ds(pl.multiple_of(i * chunk, chunk), chunk))
        return 0

    needed = jnp.maximum((total + 255) // 256, 1)
    lax.fori_loop(0, needed // 4, chunk_of, 0)

    @pl.when(needed % 4 >= 2)
    def _():
        pieces(pl.ds(pl.multiple_of(needed // 4 * chunk, 512), 512))

    @pl.when(needed % 2 == 1)
    def _():
        pieces(pl.ds(pl.multiple_of((needed - 1) * 256, 256), 256))

    for size in range(1, hid_s.shape[0] // 256 + 1):

        @pl.when(needed == size)
        def _():
            rows = 256 * size

            def inputs(i, _):
                part = pl.ds(pl.multiple_of(i * 384, 384), 384)
                xs = packed[0, :rows, part]
                both = tn(xs, pair_s[:rows, :])
                dgu[0, 0, 0, part, :] = both[:, :hidden]
                dgu[0, 0, 1, part, :] = both[:, hidden:]
                return 0

            lax.fori_loop(0, width // 384, inputs, 0)

            def outputs(i, _):
                part = pl.ds(pl.multiple_of(i * 512, 512), 512)
                dd[0, 0, part, :] = tn(hid_s[:rows, part], packed[0, :rows, width:])
                return 0

            lax.fori_loop(0, hid_s.shape[1] // 512, outputs, 0)


def weight_grads(layer, first, last, totals, packed, wgu, wd, earlier):
    _, rows, both = packed.shape
    hidden, width = wd.shape[2], wd.shape[3]
    gu_spec = pl.BlockSpec((1, 1, 2, width, hidden), lambda e, *_: (layer, e + first, 0, 0, 0))
    d_spec = pl.BlockSpec((1, 1, hidden, width), lambda e, *_: (layer, e + first, 0, 0))
    row_spec = pl.BlockSpec((1, rows, both), lambda e, *_: (e + first, 0, 0))
    return pl.pallas_call(
        functools.partial(dw_kernel, first),
        grid_spec=pltpu.PrefetchScalarGridSpec(
            num_scalar_prefetch=1,
            grid=(last - first,),
            in_specs=[row_spec, gu_spec, d_spec] + [pl.BlockSpec(memory_space=pl.ANY)] * len(earlier),
            out_specs=[gu_spec, d_spec],
            scratch_shapes=[
                pltpu.VMEM((rows // 256 * 256 - 256, 2 * hidden), jnp.bfloat16),
                pltpu.VMEM((rows // 256 * 256 - 256, hidden), jnp.bfloat16),
            ],
        ),
        out_shape=[shape_of(wgu.shape, jnp.float32), shape_of(wd.shape, jnp.float32)],
        input_output_aliases={4 + i: i for i in range(len(earlier))},
        compiler_params=params_of(),
        cost_estimate=BRIEF,
        name="weight_grads",
    )(totals, packed, wgu, wd, *earlier)


def norm_low(x, gain):
    return ((x * rms_factor(x)) * gain).astype(jnp.bfloat16)


def post_attention(ob, x, wo, gain):
    groups = wo.shape[0]
    inner = wo.shape[1]
    blk = ob.shape[1]
    halves = []
    for h in range(2):
        total = x[h * blk : (h + 1) * blk]
        for g in range(groups):
            total = total + nn(ob[h * groups + g][:, :inner], wo[g])
        halves.append(total)
    hst = jnp.concatenate(halves, axis=0)
    return hst, norm_low(hst, gain)


def mixing_rows(table):
    raw, coef = table[RAW : RAW + 16], table[COEF : COEF + 16]
    pairs = []
    for c in range(NC):
        r0, r1 = raw[NE + 2 * c : NE + 2 * c + 1], raw[NE + 2 * c + 1 : NE + 2 * c + 2]
        top = jnp.maximum(r0, r1)
        e0, e1 = jnp.exp(r0 - top), jnp.exp(r1 - top)
        pairs.append((e0 / (e0 + e1), e1 / (e0 + e1)))
    shares = [coef[NF + 2 + c : NF + 3 + c] for c in range(NC)]
    scale_u = coef[NF + 1 : NF + 2]
    for c in range(NC):
        scale_u = scale_u + shares[c] * pairs[c][0]
    return pairs, shares, scale_u, [shares[c] * pairs[c][1] for c in range(NC)]


def middle_ready(gx, table, hst, small):
    gain = small[1:2].astype(jnp.float32)
    consts = small[2 : 2 + NC].astype(jnp.float32)
    pairs, shares, scale_u, scale_c = mixing_rows(table)
    columns = to_columns([scale_u] + scale_c)
    factor = rms_factor(hst)
    base = hst * factor
    u = base * gain
    dots = [jnp.sum(gx * u, axis=1, keepdims=True)]
    dots += [jnp.sum(gx * consts[c : c + 1], axis=1, keepdims=True) for c in range(NC)]
    dots = to_rows(dots, 8)
    const_sums = [jnp.sum(gx * columns[1 + c], axis=0, keepdims=True) for c in range(NC)]
    return pairs, shares, gain, factor, base, dots, const_sums, gx * columns[0]


def middle(ready, gx, parts, gcoef, table, routes, gprev, ub, small, wo, ob):
    pairs, shares, gain, factor, base, dots, const_sums, grad_in = ready
    groups = wo.shape[0]
    inner = wo.shape[1]
    blk = ob.shape[1]
    router = small[2 + NC :]
    dot_u = dots[0:1]
    dot_c = [dots[1 + c : 2 + c] for c in range(NC)]
    ids = lax.broadcasted_iota(jnp.int32, (16, gx.shape[0]), 0)
    grads = jnp.concatenate([gcoef, jnp.zeros_like(gcoef)], axis=0)
    grads = jnp.where(ids == NF + 1, dot_u, grads)
    raw_rows = []
    for c in range(NC):
        a0, a1 = pairs[c]
        grads = jnp.where(ids == NF + 2 + c, a0 * dot_u + a1 * dot_c[c], grads)
        g0, g1 = shares[c] * dot_u, shares[c] * dot_c[c]
        both = a0 * g0 + a1 * g1
        raw_rows += [a0 * (g0 - both), a1 * (g1 - both)]
    logits = table[LOGI : LOGI + 16]
    first, second = ids == routes[0:1], ids == routes[1:2]

    def pick(chosen, rows):
        return jnp.sum(jnp.where(chosen, rows, 0.0), axis=0, keepdims=True)

    z0, z1 = pick(first, logits), pick(second, logits)
    top = jnp.maximum(z0, z1)
    e0, e1 = jnp.exp(z0 - top), jnp.exp(z1 - top)
    w0, w1 = e0 / (e0 + e1), e1 / (e0 + e1)
    gg0, gg1 = pick(first, grads), pick(second, grads)
    both = w0 * gg0 + w1 * gg1
    glog = jnp.where(first, w0 * (gg0 - both), 0.0) + jnp.where(second, w1 * (gg1 - both), 0.0) + gprev
    graw = glog
    for index, row in enumerate(raw_rows):
        graw = jnp.where(ids == NE + index, row, graw)
    graw = graw.astype(jnp.bfloat16)
    grad_router = nn(graw, ub)
    gu = grad_in + tn(graw, router) + parts
    sums = [jnp.sum(gu * base, axis=0, keepdims=True)]
    sums += const_sums
    gb = gu * gain
    ghst = gx + factor * (gb - base * jnp.mean(gb * base, axis=-1, keepdims=True))
    gy = ghst.astype(jnp.bfloat16)
    lanes = ob.shape[2]
    go, gwo = [None] * (2 * groups), []
    for g in range(groups):
        value = nt(gy, wo[g]).astype(jnp.bfloat16)
        value = jnp.concatenate([value, jnp.zeros((value.shape[0], lanes - inner), jnp.bfloat16)], axis=1)
        for h in range(2):
            go[h * groups + g] = value[h * blk : (h + 1) * blk]
        mixed = jnp.concatenate([ob[g], ob[groups + g]], axis=0)
        gwo.append(tn(mixed, gy)[:inner].astype(jnp.bfloat16))
    return ghst, jnp.stack(go), jnp.stack(gwo), jnp.concatenate(sums + [grad_router], axis=0), glog


def assemble_kernel(ours, theirs, qkv, out, gains, router, consts):
    z, _, _, _ = place()
    layers = ours.shape[0]
    inner = GROUP_HEADS * HEAD_DIM
    for l in range(layers):
        small = ours[l, :, :128].astype(jnp.float32) + theirs[l, :, :128].astype(jnp.float32)
        router[l] = small[:, 2 + NC : 2 + NC + 16]
        rows = jnp.transpose(small)
        gains[l] = rows[:2]
        consts[l] = rows[2 : 2 + NC]
        first = 128 + 6 * inner
        out[l] = ours[l, :, first:].astype(jnp.float32) + theirs[l, :, first:].astype(jnp.float32)
        for group in range(4):
            for odd in range(2):

                @pl.when(z % 2 == odd)
                def _():
                    source = ours if group // 2 == odd else theirs
                    for c in range(3):
                        at = 128 + (group % 2) * 3 * inner + c * inner
                        qkv[l, c, :, group * inner : (group + 1) * inner] = source[l, :, at : at + inner].astype(jnp.float32)


def assemble(ours, theirs, width):
    layers, shard, _ = ours.shape
    vm = pl.BlockSpec(memory_space=pltpu.VMEM)
    f32 = jnp.float32
    return pl.pallas_call(
        assemble_kernel,
        out_shape=[
            shape_of((layers, 3, shard, width), f32),
            shape_of((layers, shard, width), f32),
            shape_of((layers, 2, shard), f32),
            shape_of((layers, shard, 16), f32),
            shape_of((layers, NC, shard), f32),
        ],
        in_specs=[vm] * 2,
        out_specs=[vm] * 5,
        compiler_params=params_of(),
        cost_estimate=BRIEF,
        name="assemble",
    )(ours, theirs)


def turn_tables(seq):
    half = HEAD_DIM // 2
    frequency = np.exp((-np.log(np.float32(10000.0)) * np.arange(half, dtype=np.float32) / np.float32(half)))
    angles = np.arange(seq, dtype=np.float32)[:, None] * frequency.astype(np.float32)[None, :]
    cosine, sine = np.cos(angles), np.sin(angles)
    cosine = np.concatenate([cosine, cosine] * 2, axis=1).astype(np.float32)
    sine = np.concatenate([-sine, sine] * 2, axis=1).astype(np.float32)
    return jnp.asarray(cosine), jnp.asarray(sine)


def by_heads(
    tokens,
    cotangent,
    seq_lengths,
    block_order,
    routes,
    gains,
    qkv_weights,
    out_weight,
    router,
    const_values,
    w_gate_up,
    w_down,
):
    count, width = tokens.shape[1], tokens.shape[2]
    ctx_size, packs = lax.axis_size("ctx"), lax.axis_size("fsdp")
    blk = count // 2
    seq = blk * ctx_size
    pack = lax.axis_index("fsdp")
    z, xx, y, k = place()
    sequence = z // 2
    shard = width // packs
    f32, bf = jnp.float32, jnp.bfloat16
    everyone = ("ctx", "fsdp")

    cosine, sine = turn_tables(seq)
    routes_t = jnp.swapaxes(routes[:, 0], 1, 2)
    smalls = jnp.concatenate([gains, const_values, jnp.swapaxes(router, 1, 2)], axis=1)
    per_layer = smalls.shape[1]
    ints = jnp.concatenate([routes_t.reshape(-1), block_order[0]])
    places = ints.size
    ints = jnp.pad(ints, (0, -places % shard)).astype(bf).reshape(-1, shard)
    smalls = jnp.concatenate([smalls.reshape(LAYERS * per_layer, shard), ints], axis=0)
    smalls = jnp.pad(smalls, ((0, -smalls.shape[0] % 16), (0, 0)))
    smalls = lax.all_gather(smalls, "fsdp", axis=1, tiled=True)
    ints = smalls[LAYERS * per_layer : LAYERS * per_layer + ints.shape[0]].reshape(-1, packs, shard)
    ints = jnp.swapaxes(ints, 0, 1).reshape(packs, -1).astype(jnp.int32)
    smalls = [smalls[l * per_layer : (l + 1) * per_layer] for l in range(LAYERS)]
    near = jnp.stack([pack, 2 * y + 1 - k, 2 * (1 - y) + k, 2 * (1 - y) + 1 - k])
    routes_f = ints[near][:, : routes_t.size].reshape((packs,) + routes_t.shape)
    order = lax.dynamic_index_in_dim(ints, 2 * y + xx, 0, keepdims=False)
    order = order[routes_t.size : places].reshape(ctx_size, 2)
    order = lax.dynamic_index_in_dim(order, sequence, 1, keepdims=False) - ctx_size * sequence
    ids = jnp.arange(ctx_size, dtype=jnp.int32)
    inv = jnp.sum(jnp.where(order[None, :] == ids[:, None], ids[None, :], 0), axis=1)

    gm_all = [None, lax.all_gather(cotangent[0], everyone, axis=0, tiled=False)]
    x = tokens[0].astype(f32)
    before = jnp.zeros((packs, ROUT, count), f32)
    kept, ext_all = [], [None] * LAYERS
    for l in range(LAYERS):
        n1s, qkv, o, lse, ob, hst, ub, w, wo = attn_forward(
            l, order, inv, x, smalls[l], qkv_weights, cosine, sine, out_weight, 2 * l
        )
        if l == 1:
            ub, gm_all[1] = lax.optimization_barrier((ub, gm_all[1]))
            hst, first_ext = lax.optimization_barrier((hst, ext_all[0]))
            ext_all[0] = lax.all_gather(first_ext, everyone, axis=0, tiled=False)
        ubf, table, ext, x_next = ffn_forward(
            l, ub, hst, smalls[l], routes_f[:, l], before, w_gate_up, w_down, 2 * l + 1
        )
        before = table
        ext_all[l] = ext if l == 0 else lax.all_gather(ext, everyone, axis=0, tiled=False)
        kept.append((x, n1s, qkv, o, lse, ob, hst, w, wo, ubf, table))
        x = x_next
    output = x
    gm = cotangent[0]
    gx = gm.astype(f32)
    gprev = jnp.zeros((16, count), f32)
    grads = [None] * LAYERS
    for l in reversed(range(LAYERS)):
        x, n1s, qkv, o, lse, ob, hst, w, wo, ubf, table = kept[l]
        number = 2 * LAYERS + 2 * l
        ghst, go, gwo, small, gprev = ffn_backward(
            l, gm, gx, ubf, table, hst, smalls[l], routes_t[l], gprev, wo, ob, w_gate_up, w_down, number
        )
        if l == 0:
            go, ext_all[0] = lax.optimization_barrier((go, ext_all[0]))
        gx, gm, grads[l] = attn_backward(
            order, inv, n1s, w, cosine, sine, qkv, o, lse, go, ghst, x, smalls[l], small, gwo, number + 1
        )
        if l > 0:
            gm_all[l - 1] = gm

    dense = jnp.stack(grads)
    dense, gm = lax.optimization_barrier((dense, gm_all[0]))
    gm_all[0] = lax.all_gather(gm, everyone, axis=0, tiled=False)

    def partner(values, distance):
        return lax.ppermute(values, "ctx", [(i, i ^ distance) for i in range(ctx_size)])

    def added(first, second):
        return (first.astype(f32) + second.astype(f32)).astype(bf)

    half = NF // 2
    numbers = expert_counts(ext_all[1])
    packed = pack_rows(numbers, ext_all[1], gm_all[1])
    dense, packed = lax.optimization_barrier((dense, packed))
    got = partner(dense, 1)
    done = weight_grads(1, 0, NF, numbers[2], packed, w_gate_up, w_down, ())
    done, got = lax.optimization_barrier((done, got))
    dense = added(dense, got)
    dense, ext, gm = lax.optimization_barrier((dense, ext_all[0], gm_all[0]))
    got = partner(dense, 4)
    numbers = expert_counts(ext)
    packed = pack_rows(numbers, ext, gm)
    done = weight_grads(0, 0, half, numbers[2], packed, w_gate_up, w_down, done)
    done, got = lax.optimization_barrier((done, got))
    dense = added(dense, got)
    dense, done = lax.optimization_barrier((dense, done))
    got = partner(dense, 2)
    done = weight_grads(0, half, NF, numbers[2], packed, w_gate_up, w_down, done)
    done, got = lax.optimization_barrier((done, got))
    qkv, out, gain_grad, router_grad, const_grad = assemble(dense, got, width)
    return (
        output[None],
        gx[None],
        gain_grad,
        qkv,
        out,
        router_grad,
        const_grad,
        done[0],
        done[1],
    )


def solution(mesh):
    placed = (
        P("fsdp", "ctx", None),
        P("fsdp", "ctx", None),
        P("fsdp", None),
        P("fsdp", None),
        P(None, "fsdp", "ctx", None),
        P(None, None, "fsdp"),
        P(None, None, "fsdp", None),
        P(None, "fsdp", None),
        P(None, "fsdp", None),
        P(None, None, "fsdp"),
        P(None, None, None, None, "fsdp"),
        P(None, None, "fsdp", None),
    )
    contexts, packs = mesh.shape["ctx"], mesh.shape["fsdp"]
    blocks_of_heads = HEADS // GROUP_HEADS

    def plan(*args):
        tokens = args[0]
        even = tokens.shape[1] * contexts == 2 * MINLEN
        grouped = contexts == 2 * blocks_of_heads and packs == blocks_of_heads
        return (by_heads if even and grouped else shards)(*args)

    return jax.shard_map(
        plan,
        mesh=mesh,
        in_specs=placed,
        out_specs=(
            P("fsdp", "ctx", None),
            P("fsdp", "ctx", None),
            P(None, None, "fsdp"),
            P(None, None, "fsdp", None),
            P(None, "fsdp", None),
            P(None, "fsdp", None),
            P(None, None, "fsdp"),
            P(None, None, None, None, "fsdp"),
            P(None, None, "fsdp", None),
        ),
        check_vma=False,
    )
```

```python
import functools

import jax
import jax.numpy as jnp
import numpy as np
from jax import lax
from jax.experimental import pallas as pl
from jax.experimental.pallas import tpu as pltpu
from jax.sharding import PartitionSpec as P

HEADS = 12
HEAD_DIM = 64
NF = 8
NC = 2
LAYERS = 2
NE = 12
MOST = 64
GROUP_HEADS = 3


def from_behind(x, axis, by):
    devices = lax.axis_size(axis)
    return lax.ppermute(x, axis, [(i, (i + by) % devices) for i in range(devices)])


def layout_tables(lengths, order_row, tok_count):
    block_len = tok_count // 2
    pack_len = order_row.shape[0] * block_len
    pack_rows = jnp.arange(pack_len, dtype=jnp.int32)
    owner = pack_rows // tok_count
    which_half = pack_rows % tok_count // block_len
    block_ids = order_row[2 * owner + which_half]
    pack_pos = block_ids * block_len + pack_rows % block_len
    segment = (pack_pos >= lengths[0]).astype(jnp.int32)
    seq_pos = pack_pos - segment * lengths[0]
    return (pack_pos, segment, seq_pos)


def angle_tables(seq_pos, head_size):
    half_size = head_size // 2
    frequency = jnp.exp(-jnp.log(10000.0) * jnp.arange(half_size, dtype=jnp.float32) / half_size)
    angles = seq_pos.astype(jnp.float32)[:, None] * frequency[None, :]
    return (jnp.cos(angles)[:, None, :], jnp.sin(angles)[:, None, :])


def rotate_pairs(values, cosine_table, sine_table, direction):
    half_size = values.shape[-1] // 2
    first_half = values[..., :half_size]
    second_half = values[..., half_size:]
    return jnp.concatenate(
        [
            first_half * cosine_table - direction * second_half * sine_table,
            second_half * cosine_table + direction * first_half * sine_table,
        ],
        axis=-1,
    )


def rms_parts(values):
    inverse = lax.rsqrt(jnp.mean(values * values, axis=-1, keepdims=True) + 1e-06)
    return (values * inverse, inverse)


def rms_back(grad_normed, base_values, inverse):
    return inverse * (
        grad_normed - base_values * jnp.mean(grad_normed * base_values, axis=-1, keepdims=True)
    )


def expert_forward(inputs_low, gate_up_use, down_use):
    gate_up_out = jnp.einsum(
        "emd,ecdf->ecmf", inputs_low, gate_up_use, preferred_element_type=jnp.float32
    )
    hidden_low = (jax.nn.silu(gate_up_out[:, 0]) * gate_up_out[:, 1]).astype(jnp.bfloat16)
    partial_value = jnp.einsum(
        "emf,efd->emd", hidden_low, down_use, preferred_element_type=jnp.float32
    )
    return (gate_up_out, hidden_low, partial_value)


def expert_backward(inputs_low, gate_up_out, hidden_low, grad_part_low, gate_up_use, down_use):
    grad_down = jnp.einsum(
        "emf,emd->efd", hidden_low, grad_part_low, preferred_element_type=jnp.float32
    )
    grad_hidden = jnp.einsum(
        "emd,efd->emf", grad_part_low, down_use, preferred_element_type=jnp.float32
    )
    gate_out = gate_up_out[:, 0]
    sigmoid_gate = jax.nn.sigmoid(gate_out)
    grad_pair_low = jnp.stack(
        [
            grad_hidden
            * gate_up_out[:, 1]
            * sigmoid_gate
            * (1.0 + gate_out * (1.0 - sigmoid_gate)),
            grad_hidden * gate_out * sigmoid_gate,
        ],
        axis=1,
    ).astype(jnp.bfloat16)
    grad_gate_up = jnp.einsum(
        "emd,ecmf->ecdf", inputs_low, grad_pair_low, preferred_element_type=jnp.float32
    )
    grad_rows = jnp.einsum(
        "ecmf,ecdf->emd", grad_pair_low, gate_up_use, preferred_element_type=jnp.float32
    )
    return (grad_gate_up, grad_down, grad_rows)


def shards(
    tokens,
    cotangent,
    seq_lengths,
    block_order,
    routes,
    gains,
    qkv_weights,
    out_weight,
    router,
    const_values,
    w_gate_up,
    w_down,
):
    tok_count = tokens.shape[1]
    width = tokens.shape[2]
    ctx_size = lax.axis_size("ctx")
    own_index = lax.axis_index("ctx")
    score_scale = HEAD_DIM ** (-0.5)
    pack_pos, segment, seq_pos = layout_tables(seq_lengths[0], block_order[0], tok_count)
    own_start = own_index * tok_count
    query_pos = lax.dynamic_slice_in_dim(pack_pos, own_start, tok_count)
    query_seg = lax.dynamic_slice_in_dim(segment, own_start, tok_count)
    cosine_table, sine_table = angle_tables(
        lax.dynamic_slice_in_dim(seq_pos, own_start, tok_count), HEAD_DIM
    )
    head_shape = (tok_count, HEADS, HEAD_DIM)
    expert_ids = jnp.arange(NE, dtype=jnp.int32)
    slot_ids = jnp.arange(MOST, dtype=jnp.int32)
    row_ids = jnp.arange(tok_count, dtype=jnp.int32)

    def allowed_pairs(key_offset, key_count):
        key_pos = lax.dynamic_slice_in_dim(pack_pos, key_offset, key_count)
        key_seg = lax.dynamic_slice_in_dim(segment, key_offset, key_count)
        return (query_seg[:, None] == key_seg[None, :]) & (key_pos[None, :] <= query_pos[:, None])

    stream = tokens[0].astype(jnp.float32)
    previous = jnp.zeros((tok_count, NE), jnp.float32)
    saved = []
    for layer_index in range(LAYERS):
        gain_all, qkv_all, out_all, router_all, const_all = (
            lax.all_gather(gains[layer_index], "fsdp", axis=1, tiled=True),
            lax.all_gather(qkv_weights[layer_index], "fsdp", axis=1, tiled=True),
            lax.all_gather(out_weight[layer_index], "fsdp", axis=0, tiled=True),
            lax.all_gather(router[layer_index], "fsdp", axis=0, tiled=True),
            lax.all_gather(const_values[layer_index], "fsdp", axis=1, tiled=True),
        )
        gain_float = gain_all.astype(jnp.float32)
        base_one, inverse_one = rms_parts(stream)
        normed_low = (base_one * gain_float[0]).astype(jnp.bfloat16)
        projected = jnp.einsum(
            "td,cde->cte", normed_low, qkv_all, preferred_element_type=jnp.float32
        )
        queries_low = rotate_pairs(
            projected[0].reshape(head_shape), cosine_table, sine_table, 1.0
        ).astype(jnp.bfloat16)
        keys_low = rotate_pairs(
            projected[1].reshape(head_shape), cosine_table, sine_table, 1.0
        ).astype(jnp.bfloat16)
        values_low = projected[2].reshape(head_shape).astype(jnp.bfloat16)

        def fold_step(running, shard_piece, offset, queries_use=queries_low):
            keys_piece, values_piece = shard_piece
            allowed = allowed_pairs(offset, keys_piece.shape[0])[None]
            scores = (
                jnp.einsum(
                    "qhd,khd->hqk", queries_use, keys_piece, preferred_element_type=jnp.float32
                )
                * score_scale
            )
            scores = jnp.where(allowed, scores, -1e30)
            top_old, total_old, accumulated = running
            top_new = jnp.maximum(top_old, jnp.max(scores, axis=-1))
            weights = jnp.where(allowed, jnp.exp(scores - top_new[..., None]), 0.0)
            factor = jnp.exp(top_old - top_new)
            accumulated = jnp.einsum(
                "hqk,khd->hqd",
                weights.astype(jnp.bfloat16),
                values_piece,
                preferred_element_type=jnp.float32,
            )
            return (top_new, jnp.sum(weights, axis=-1), accumulated)

        starting = (
            jnp.full((HEADS, tok_count), -1e30, jnp.float32),
            jnp.zeros((HEADS, tok_count), jnp.float32),
            jnp.zeros((HEADS, tok_count, HEAD_DIM), jnp.float32),
        )
        top_value, total_sum, accumulated = fold_step(
            starting,
            (
                lax.all_gather(keys_low, "ctx", axis=0, tiled=True),
                lax.all_gather(values_low, "ctx", axis=0, tiled=True),
            ),
            jnp.int32(0),
        )
        log_total = top_value + jnp.log(total_sum)
        attended = jnp.transpose(accumulated / total_sum[..., None], (1, 0, 2))
        mixed_low = attended.reshape(tok_count, width).astype(jnp.bfloat16)
        hidden_state = stream + jnp.dot(mixed_low, out_all, preferred_element_type=jnp.float32)
        base_two, inverse_two = rms_parts(hidden_state)
        expert_in = base_two * gain_float[1]
        expert_low = expert_in.astype(jnp.bfloat16)
        raw_logits = jnp.dot(expert_low, router_all, preferred_element_type=jnp.float32)
        logits = raw_logits[:, :NE] + previous
        route_ids = routes[layer_index, 0]
        chosen = route_ids[:, :, None] == expert_ids[None, None, :]
        chosen_f = chosen.astype(jnp.float32)
        hit_count = jnp.sum(chosen.astype(jnp.int32), axis=1)
        slot_index = jnp.cumsum(hit_count, axis=0) - 1
        picked = jnp.sum(chosen_f * logits[:, None, :], axis=-1)
        gate_weights = jax.nn.softmax(picked, axis=-1)
        coeffs = jnp.sum(gate_weights[:, :, None] * chosen_f, axis=1)
        slot_table = jnp.zeros((NF, MOST), jnp.int32)
        for expert in range(NF):
            target = jnp.where(hit_count[:, expert] > 0, slot_index[:, expert], MOST)
            slot_table = slot_table.at[expert, target].set(row_ids, mode="drop")
        filled = (slot_ids[None, :] < jnp.sum(hit_count[:, :NF], axis=0)[:, None]).astype(
            jnp.float32
        )
        rows_low = expert_low[slot_table]
        inputs_low = lax.all_gather(rows_low, "fsdp", axis=1, tiled=True)
        gate_up_out, hidden_low, partial_value = expert_forward(
            inputs_low, w_gate_up[layer_index], w_down[layer_index]
        )
        result = lax.psum_scatter(
            partial_value.astype(jnp.bfloat16), "fsdp", scatter_dimension=1, tiled=True
        ).astype(jnp.float32)
        flat_index = jnp.arange(NF, dtype=jnp.int32)[None, :] * MOST + jnp.clip(
            slot_index[:, :NF], 0, MOST - 1
        )
        token_result = result.reshape(NF * MOST, width)[flat_index]
        expert_mix = (
            jnp.sum(coeffs[:, :NF, None] * token_result, axis=1)
            + coeffs[:, NF + 1 : NF + 2] * expert_in
        )
        mixings = []
        for const_index in range(NC):
            column = NE + 2 * const_index
            mixing = jax.nn.softmax(raw_logits[:, column : column + 2], axis=-1)
            mixings.append(mixing)
            expert_mix = expert_mix + coeffs[:, NF + 2 + const_index : NF + 3 + const_index] * (
                mixing[:, 0:1] * expert_in
                + mixing[:, 1:2] * const_all[const_index].astype(jnp.float32)[None, :]
            )
        saved.append(
            (
                gain_float,
                qkv_all,
                out_all,
                router_all,
                const_all,
                base_one,
                inverse_one,
                normed_low,
                queries_low,
                keys_low,
                values_low,
                log_total,
                attended,
                mixed_low,
                base_two,
                inverse_two,
                expert_in,
                expert_low,
                chosen_f,
                hit_count,
                gate_weights,
                coeffs,
                slot_table,
                filled,
                inputs_low,
                gate_up_out,
                hidden_low,
                flat_index,
                token_result,
                mixings,
            )
        )
        stream = hidden_state + expert_mix
        previous = logits
    grad_stream = cotangent[0].astype(jnp.float32)
    grad_previous = jnp.zeros((tok_count, NE), jnp.float32)
    layer_grads = [None] * LAYERS
    for layer_index in reversed(range(LAYERS)):
        (
            gain_float,
            qkv_all,
            out_all,
            router_all,
            const_all,
            base_one,
            inverse_one,
            normed_low,
            queries_low,
            keys_low,
            values_low,
            log_total,
            attended,
            mixed_low,
            base_two,
            inverse_two,
            expert_in,
            expert_low,
            chosen_f,
            hit_count,
            gate_weights,
            coeffs,
            slot_table,
            filled,
            inputs_low,
            gate_up_out,
            hidden_low,
            flat_index,
            token_result,
            mixings,
        ) = saved[layer_index]
        grad_mix = grad_stream
        dot_input = jnp.sum(grad_mix * expert_in, axis=-1, keepdims=True)
        coef_grads = [
            jnp.sum(grad_mix[:, None, :] * token_result, axis=-1),
            jnp.zeros((tok_count, 1), jnp.float32),
            dot_input,
        ]
        grad_in = grad_mix * coeffs[:, NF + 1 : NF + 2]
        const_cols = []
        const_grads = []
        for const_index in range(NC):
            mixing = mixings[const_index]
            const_row = const_all[const_index].astype(jnp.float32)[None, :]
            dot_const = jnp.sum(grad_mix * const_row, axis=-1, keepdims=True)
            share = coeffs[:, NF + 2 + const_index : NF + 3 + const_index]
            coef_grads.append(mixing[:, 0:1] * dot_input + mixing[:, 1:2] * dot_const)
            grad_in = grad_in + grad_mix * (share * mixing[:, 0:1])
            grad_mixing = share * jnp.concatenate([dot_input, dot_const], axis=1)
            const_cols.append(
                mixing * (grad_mixing - jnp.sum(mixing * grad_mixing, axis=-1, keepdims=True))
            )
            const_grads.append(jnp.sum(grad_mix * (share * mixing[:, 1:2]), axis=0))
        grad_coeffs = jnp.concatenate(coef_grads, axis=1)
        grad_gates = jnp.sum(chosen_f * grad_coeffs[:, None, :], axis=-1)
        grad_picked = gate_weights * (
            grad_gates - jnp.sum(gate_weights * grad_gates, axis=-1, keepdims=True)
        )
        grad_logits = jnp.sum(grad_picked[:, :, None] * chosen_f, axis=1) + grad_previous
        grad_previous = grad_logits
        grad_raw_low = jnp.concatenate([grad_logits] + const_cols, axis=1).astype(jnp.bfloat16)
        grad_router = jnp.einsum(
            "td,tc->dc", expert_low, grad_raw_low, preferred_element_type=jnp.float32
        )
        grad_in = grad_in + jnp.einsum(
            "tc,dc->td", grad_raw_low, router_all, preferred_element_type=jnp.float32
        )
        slot_weight = (
            jnp.take_along_axis(jnp.transpose(coeffs[:, :NF]), slot_table, axis=1) * filled
        )
        grad_result_low = (grad_mix[slot_table] * slot_weight[:, :, None]).astype(jnp.bfloat16)
        grad_part_low = lax.all_gather(grad_result_low, "fsdp", axis=1, tiled=True)
        grad_gate_up, grad_down, grad_rows = expert_backward(
            inputs_low,
            gate_up_out,
            hidden_low,
            grad_part_low,
            w_gate_up[layer_index],
            w_down[layer_index],
        )
        grad_rows = lax.psum_scatter(
            grad_rows.astype(jnp.bfloat16), "fsdp", scatter_dimension=1, tiled=True
        ).astype(jnp.float32)
        token_grads = grad_rows.reshape(NF * MOST, width)[flat_index]
        grad_in = grad_in + jnp.sum(
            jnp.where(hit_count[:, :NF, None] > 0, token_grads, 0.0), axis=1
        )
        grad_gain_two = jnp.sum(grad_in * base_two, axis=0)
        grad_hidden_state = grad_stream + rms_back(grad_in * gain_float[1], base_two, inverse_two)
        grad_out_low = grad_hidden_state.astype(jnp.bfloat16)
        grad_out_w = jnp.einsum(
            "td,te->de", mixed_low, grad_out_low, preferred_element_type=jnp.float32
        )
        grad_attended = (
            jnp.einsum("te,de->td", grad_out_low, out_all, preferred_element_type=jnp.float32)
            .astype(jnp.bfloat16)
            .reshape(head_shape)
        )
        delta = jnp.transpose(jnp.sum(grad_attended.astype(jnp.float32) * attended, axis=-1))

        def visit(
            turn_index,
            carried,
            queries_use=queries_low,
            grad_use=grad_attended,
            log_use=log_total,
            delta_use=delta,
        ):
            keys_piece, values_piece, key_grads, value_grads, query_grads = carried
            source = (own_index - turn_index) % ctx_size
            allowed = allowed_pairs(source * tok_count, tok_count)[None]
            scores = (
                jnp.einsum(
                    "qhd,khd->hqk", queries_use, keys_piece, preferred_element_type=jnp.float32
                )
                * score_scale
            )
            probs = jnp.where(
                allowed, jnp.exp(jnp.where(allowed, scores, -1e30) - log_use[..., None]), 0.0
            )
            value_grads = value_grads + jnp.einsum(
                "hqk,qhd->khd",
                probs.astype(jnp.bfloat16),
                grad_use,
                preferred_element_type=jnp.float32,
            )
            prob_grads = jnp.einsum(
                "qhd,khd->hqk", grad_use, values_piece, preferred_element_type=jnp.float32
            )
            score_grads = (probs * (prob_grads - delta_use[..., None])).astype(jnp.bfloat16)
            query_grads = query_grads + jnp.einsum(
                "hqk,khd->qhd", score_grads, keys_piece, preferred_element_type=jnp.float32
            )
            key_grads = key_grads + jnp.einsum(
                "hqk,qhd->khd", score_grads, queries_use, preferred_element_type=jnp.float32
            )
            keys_piece, values_piece = from_behind((keys_piece, values_piece), "ctx", 1)
            key_grads, value_grads = (
                from_behind(key_grads.astype(jnp.bfloat16), "ctx", 1).astype(key_grads.dtype),
                from_behind(value_grads.astype(jnp.bfloat16), "ctx", 1).astype(value_grads.dtype),
            )
            return (keys_piece, values_piece, key_grads, value_grads, query_grads)

        zero_heads = jnp.zeros(head_shape, jnp.float32)
        finished = lax.fori_loop(
            0, ctx_size, visit, (keys_low, values_low, zero_heads, zero_heads, zero_heads)
        )
        grad_query = (
            rotate_pairs(finished[4] * score_scale, cosine_table, sine_table, -1.0)
            .astype(jnp.bfloat16)
            .reshape(tok_count, width)
        )
        grad_key = (
            rotate_pairs(finished[2] * score_scale, cosine_table, sine_table, -1.0)
            .astype(jnp.bfloat16)
            .reshape(tok_count, width)
        )
        grad_value = finished[3].astype(jnp.bfloat16).reshape(tok_count, width)
        grad_proj_low = jnp.stack([grad_query, grad_key, grad_value], axis=0)
        grad_qkv = jnp.einsum(
            "td,cte->cde", normed_low, grad_proj_low, preferred_element_type=jnp.float32
        )
        grad_normed = jnp.einsum(
            "cte,cde->td", grad_proj_low, qkv_all, preferred_element_type=jnp.float32
        )
        grad_gain_one = jnp.sum(grad_normed * base_one, axis=0)
        grad_stream = grad_hidden_state + rms_back(
            grad_normed * gain_float[0], base_one, inverse_one
        )
        gains_shard, qkv_shard, out_shard, router_shard, const_shard = (
            lax.psum_scatter(
                jnp.stack([grad_gain_one, grad_gain_two]).astype(jnp.bfloat16),
                "fsdp",
                scatter_dimension=1,
                tiled=True,
            ).astype(jnp.float32),
            lax.psum_scatter(
                grad_qkv.astype(jnp.bfloat16), "fsdp", scatter_dimension=1, tiled=True
            ).astype(jnp.float32),
            lax.psum_scatter(
                grad_out_w.astype(jnp.bfloat16), "fsdp", scatter_dimension=0, tiled=True
            ).astype(jnp.float32),
            lax.psum_scatter(
                grad_router.astype(jnp.bfloat16), "fsdp", scatter_dimension=0, tiled=True
            ).astype(jnp.float32),
            lax.psum_scatter(
                jnp.stack(const_grads).astype(jnp.bfloat16), "fsdp", scatter_dimension=1, tiled=True
            ).astype(jnp.float32),
        )
        layer_grads[layer_index] = (
            lax.psum(gains_shard.astype(jnp.bfloat16), "ctx").astype(jnp.float32),
            lax.psum(qkv_shard.astype(jnp.bfloat16), "ctx").astype(jnp.float32),
            lax.psum(out_shard.astype(jnp.bfloat16), "ctx").astype(jnp.float32),
            lax.psum(router_shard.astype(jnp.bfloat16), "ctx").astype(jnp.float32),
            lax.psum(const_shard.astype(jnp.bfloat16), "ctx").astype(jnp.float32),
            lax.psum(grad_gate_up.astype(jnp.bfloat16), "ctx").astype(jnp.float32),
            lax.psum(grad_down.astype(jnp.bfloat16), "ctx").astype(jnp.float32),
        )
    stacked = [
        jnp.stack([layer_grads[layer_index][member_index] for layer_index in range(LAYERS)])
        for member_index in range(7)
    ]
    return (
        stream[None],
        grad_stream[None],
        stacked[0],
        stacked[1],
        stacked[2],
        stacked[3],
        stacked[4],
        stacked[5],
        stacked[6],
    )


MINLEN = 1024
ROUT = 56
RAW, COEF, SLOT, LOGI = 0, 16, 32, 40
VMEM_MB = 60
BRIEF = pl.CostEstimate(flops=1, bytes_accessed=1, transcendentals=0)


def nt(a, b):
    return lax.dot_general(a, b, (((1,), (1,)), ((), ())), preferred_element_type=jnp.float32)


def nn(a, b):
    return lax.dot_general(a, b, (((1,), (0,)), ((), ())), preferred_element_type=jnp.float32)


def tn(a, b):
    return lax.dot_general(a, b, (((0,), (0,)), ((), ())), preferred_element_type=jnp.float32)


def params_of(mb=VMEM_MB, **more):
    return pltpu.CompilerParams(vmem_limit_bytes=mb * 2**20, **more)


def shape_of(dims, kind):
    return jax.ShapeDtypeStruct(dims, kind)


def rms_factor(values):
    return lax.rsqrt(jnp.mean(values * values, axis=-1, keepdims=True) + 1e-06)


def to_rows(columns, count):
    lane = lax.broadcasted_iota(jnp.int32, (columns[0].shape[0], 128), 1)
    packed = jnp.zeros(lane.shape, jnp.float32)
    for index, column in enumerate(columns):
        packed = jnp.where(lane == index, column, packed)
    return jnp.transpose(packed)[:count]


def to_columns(rows):
    count = rows[0].shape[1]
    sub = lax.broadcasted_iota(jnp.int32, (128, count), 0)
    packed = jnp.zeros(sub.shape, jnp.float32)
    for index, row in enumerate(rows):
        packed = jnp.where(sub == index, row, packed)
    packed = jnp.transpose(packed)
    return [packed[:, index : index + 1] for index in range(len(rows))]


def swap_halves(values):
    lanes = values.shape[1]
    lane = lax.broadcasted_iota(jnp.int32, values.shape, 1)
    ahead = pltpu.roll(values, lanes - 32, 1)
    behind = pltpu.roll(values, 32, 1)
    return jnp.where(lane % 64 < 32, ahead, behind)


def spin(values, cosine, sine):
    return values * cosine + swap_halves(values) * sine


def place():
    own, pack = lax.axis_index("ctx"), lax.axis_index("fsdp")
    return own // 2, own % 2, pack // 2, pack % 2


def remote(src, dst, send, recv, ctx, fsdp):
    return pltpu.make_async_remote_copy(
        src_ref=src,
        dst_ref=dst,
        send_sem=send,
        recv_sem=recv,
        device_id=(ctx, fsdp),
        device_id_type=pl.DeviceIdType.MESH,
    )


def greet_plane(contexts, across=False):
    own = lax.axis_index("ctx")
    _, _, y, k = place()
    barrier = pltpu.get_barrier_semaphore()
    if across:
        for core in (k, 1 - k):
            device = (own, 2 * (1 - y) + core)
            pl.semaphore_signal(barrier, inc=1, device_id=device, device_id_type=pl.DeviceIdType.MESH)
    for ctx in range(contexts):
        for core in range(2):

            @pl.when(jnp.logical_or(ctx != own, core != k))
            def _():
                pl.semaphore_signal(barrier, inc=1, device_id=(ctx, 2 * y + core), device_id_type=pl.DeviceIdType.MESH)

    return barrier, 2 * contexts - 1 + (2 if across else 0)


def greet_packs():
    own = lax.axis_index("ctx")
    _, _, y, k = place()
    barrier = pltpu.get_barrier_semaphore()
    for fsdp in (2 * y + 1 - k, 2 * (1 - y) + k, 2 * (1 - y) + 1 - k):
        pl.semaphore_signal(barrier, inc=1, device_id=(own, fsdp), device_id_type=pl.DeviceIdType.MESH)
    return barrier, 3


def attn_fwd_kernel(
    order, inv, x, small, wq, cosine, sine, wo_own,
    n1s, qkv, o, lse, ob, hst, ub, w, wo,
    n1own, n1r, osort, osend, orecv, cols, w_s, wo_s,
    n_send, n_recv, f_send, f_recv, o_send, o_recv, w_send, w_recv, v_send, v_recv,
):
    blocks, blk, _ = n1r.shape
    lanes = o.shape[1]
    seq = blocks * blk
    step = 2 * blk
    own = lax.axis_index("ctx")
    z, xx, y, k = place()
    depth = blocks // 2
    same = xx == k
    pack = lax.axis_index("fsdp")
    inner = wo_own.shape[1]
    beside, over, corner = 2 * y + 1 - k, 2 * (1 - y) + k, 2 * (1 - y) + 1 - k

    barrier, others = greet_plane(blocks, across=True)
    n1 = norm_low(x[...], small[0:1, :].astype(jnp.float32))
    n1own[0] = n1[:blk]
    n1own[1] = n1[blk:]
    pl.semaphore_wait(barrier, others)

    def n1_copy(zz):
        return remote(n1own.at[zz // 2], n1r.at[own], n_send.at[zz], n_recv.at[z], 2 * zz + k, 2 * y + xx)

    for zz in range(depth):
        alone = jnp.logical_and(same, zz == z)

        @pl.when(jnp.logical_not(alone))
        def _():
            n1_copy(zz).start()

        @pl.when(alone)
        def _():
            n1r[own] = n1own[zz // 2]

    for half in range(2):

        @pl.when(z % 2 == half)
        def _():
            for core in range(2):
                first = (2 * half + core) * inner
                for c in range(3):
                    cols[core, :, c * lanes : c * lanes + inner] = wq[0, c, :, first : first + inner]
                    cols[core, :, c * lanes + inner : (c + 1) * lanes] = jnp.zeros((inner, lanes - inner), jnp.bfloat16)

    def rows_of(device):
        return pl.ds(pl.multiple_of(device * inner, inner), inner)

    def w_copy(index):
        device, core = ((beside, 1 - k), (over, k), (corner, 1 - k))[index]
        return remote(cols.at[core], w_s.at[rows_of(pack), :], w_send.at[index], w_recv.at[index], own, device)

    def w_wait(index):
        rows = w_s.at[rows_of((beside, over, corner)[index]), :]
        remote(cols.at[0], rows, w_send.at[index], w_recv.at[index], own, beside).wait_recv()

    w_s[rows_of(pack), :] = cols[k]
    wo_s[pack] = wo_own[0]
    for index in (1, 2, 0):
        w_copy(index).start()
    v_far = remote(wo_s.at[pack], wo_s.at[pack], v_send.at[0], v_recv.at[0], own, over)
    v_near = remote(wo_s.at[pack], wo_s.at[pack], v_send.at[1], v_recv.at[1], own, beside)
    v_on = remote(wo_s.at[over], wo_s.at[over], v_send.at[2], v_recv.at[2], own, beside)
    v_far.start()
    v_near.start()

    def forward_copy(zz):
        slot = n1r.at[2 * zz + k]
        return remote(slot, slot, f_send.at[zz], f_recv.at[zz], own, 2 * y + 1 - k)

    for zz in range(depth):

        @pl.when(jnp.logical_not(jnp.logical_and(same, zz == z)))
        def _():
            remote(n1own.at[0], n1r.at[2 * zz + k], n_send.at[zz], n_recv.at[zz], 2 * zz + k, 2 * y + xx).wait_recv()

        forward_copy(zz).start()
    for zz in range(depth):
        slot = n1r.at[2 * zz + 1 - k]
        remote(slot, slot, f_send.at[zz], f_recv.at[zz], own, 2 * y + 1 - k).wait_recv()

    for index in range(3):
        w_wait(index)
    w[...] = w_s[...]
    for b in range(blocks):
        n1s[b * blk : (b + 1) * blk, :] = n1r[inv[b]]
    for i in range(seq // step):
        part = slice(i * step, (i + 1) * step)
        out = nn(n1s[part, :], w_s[...])
        cos2 = jnp.concatenate([cosine[part, :]] * (lanes // 128), axis=1)
        sin2 = jnp.concatenate([sine[part, :]] * (lanes // 128), axis=1)
        q = spin(out[:, :lanes], cos2, sin2).astype(jnp.bfloat16)
        qkv[part, :lanes] = q * jnp.asarray(HEAD_DIM**-0.5, jnp.bfloat16)
        qkv[part, lanes : 2 * lanes] = spin(out[:, lanes : 2 * lanes], cos2, sin2).astype(jnp.bfloat16)
        qkv[part, 2 * lanes :] = out[:, 2 * lanes :].astype(jnp.bfloat16)
    lane = lax.broadcasted_iota(jnp.int32, (step, 128), 1)
    for i in range(seq // step):
        part = slice(i * step, (i + 1) * step)
        span = (i + 1) * step
        seen = lax.broadcasted_iota(jnp.int32, (step, span), 1) <= (
            lax.broadcasted_iota(jnp.int32, (step, span), 0) + i * step
        )
        logs = jnp.zeros((step, 128), jnp.float32)
        for head in range(GROUP_HEADS):
            tile, side = head // 2, head % 2
            at = tile * 128
            mine = lane // 64 == side
            q = jnp.where(mine, qkv[part, at : at + 128], jnp.asarray(0, jnp.bfloat16))
            s = nt(q, qkv[:span, lanes + at : lanes + at + 128])
            s = jnp.where(seen, s, -1e30)
            top = jnp.max(s, axis=1, keepdims=True)
            p = jnp.exp(s - top)
            total = jnp.sum(p, axis=1, keepdims=True)
            out = nn(p.astype(jnp.bfloat16), qkv[:span, 2 * lanes + at : 2 * lanes + at + 128]) / total
            logs = jnp.where(lane == head, top + jnp.log(total), logs)
            if side == 0:
                kept = jnp.where(mine, out, 0.0)
            else:
                kept = jnp.where(mine, out, kept)
            o[part, at : at + 128] = kept
        lse[part, :] = logs
        osort[2 * i] = o[part, :][:blk].astype(jnp.bfloat16)
        osort[2 * i + 1] = o[part, :][blk:].astype(jnp.bfloat16)

    mine_at = 2 * z + k
    remote(wo_s.at[over], wo_s.at[over], v_send.at[0], v_recv.at[0], own, over).wait_recv()
    v_on.start()

    def o_copy(ctx):
        return remote(osend.at[ctx], orecv.at[mine_at], o_send.at[ctx], o_recv.at[mine_at], ctx, 2 * y + xx)

    for ctx in range(blocks):
        alone = jnp.logical_and(same, ctx == own)
        osend[ctx] = osort[order[ctx]]

        @pl.when(jnp.logical_not(alone))
        def _():
            o_copy(ctx).start()

        @pl.when(alone)
        def _():
            orecv[mine_at] = osend[ctx]

    for src in range(blocks):

        @pl.when(jnp.logical_not(jnp.logical_and(same, src == mine_at)))
        def _():
            remote(osend.at[0], orecv.at[src], o_send.at[0], o_recv.at[src], 2 * (src // 2) + k, 2 * y + src % 2).wait_recv()

    ob[...] = orecv[...]
    remote(wo_s.at[beside], wo_s.at[beside], v_send.at[1], v_recv.at[1], own, beside).wait_recv()
    remote(wo_s.at[corner], wo_s.at[corner], v_send.at[2], v_recv.at[2], own, beside).wait_recv()
    wo[...] = wo_s[...]
    total, low = post_attention(orecv[...], x[...], wo_s[...], small[1:2, :].astype(jnp.float32))
    hst[...] = total
    ub[...] = low
    for zz in range(depth):

        @pl.when(jnp.logical_not(jnp.logical_and(same, zz == z)))
        def _():
            n1_copy(zz).wait_send()

        forward_copy(zz).wait_send()
    for index in range(3):
        w_copy(index).wait_send()
    v_far.wait_send()
    v_near.wait_send()
    v_on.wait_send()
    for ctx in range(blocks):

        @pl.when(jnp.logical_not(jnp.logical_and(same, ctx == own)))
        def _():
            o_copy(ctx).wait_send()


def attn_forward(layer, order, inv, x, small, wq, cosine, sine, wo, number):
    count, width = x.shape
    blocks, blk = order.shape[0], count // 2
    packs, inner = width // wo.shape[1], wo.shape[1]
    lanes = -(-inner // 128) * 128
    seq = blocks * blk
    vm = pl.BlockSpec(memory_space=pltpu.VMEM)
    sm = pl.BlockSpec(memory_space=pltpu.SMEM)
    bf = jnp.bfloat16
    dma = pltpu.SemaphoreType.DMA
    return pl.pallas_call(
        attn_fwd_kernel,
        grid=(1,),
        out_shape=[
            shape_of((seq, width), bf),
            shape_of((seq, 3 * lanes), bf),
            shape_of((seq, lanes), jnp.float32),
            shape_of((seq, 128), jnp.float32),
            shape_of((blocks, blk, lanes), bf),
            shape_of((count, width), jnp.float32),
            shape_of((count, width), bf),
            shape_of((width, 3 * lanes), bf),
            shape_of((packs, inner, width), bf),
        ],
        in_specs=[sm, sm, vm, vm]
        + [pl.BlockSpec((1, 3, inner, width), lambda _: (layer, 0, 0, 0)), vm, vm]
        + [pl.BlockSpec((1, inner, width), lambda _: (layer, 0, 0))],
        out_specs=[vm] * 9,
        scratch_shapes=[
            pltpu.VMEM((2, blk, width), bf),
            pltpu.VMEM((blocks, blk, width), bf),
            pltpu.VMEM((blocks, blk, lanes), bf),
            pltpu.VMEM((blocks, blk, lanes), bf),
            pltpu.VMEM((blocks, blk, lanes), bf),
            pltpu.VMEM((2, inner, 3 * lanes), bf),
            pltpu.VMEM((width, 3 * lanes), bf),
            pltpu.VMEM((packs, inner, width), bf),
        ]
        + [dma((blocks // 2,))] * 4
        + [dma((blocks,))] * 2
        + [dma((3,))] * 4,
        compiler_params=params_of(44, collective_id=number, has_side_effects=True),
        cost_estimate=BRIEF,
        name="attn_fwd",
    )(order, inv, x, small, wq, cosine, sine, wo)


def attn_bwd_kernel(
    order, inv, n1s, w, cosine, sine, qkv, o, lse, go, ghst, x, small, gsmall, gwo,
    gx, gm, dense,
    gor, gos, grads, acc, gns, sib_out, sib_in, gn_out, gnr, gw, gw_in, both, both_in, wo_in, wo_both, wo_over, probs,
    o_send, o_recv, s_send, s_recv, g_send, g_recv, r_send, r_recv, w_send, w_recv,
):
    blocks, blk, width = grads.shape
    lanes = o.shape[1]
    seq = blocks * blk
    step = 2 * blk
    zero = jnp.asarray(0, jnp.bfloat16)
    own = lax.axis_index("ctx")
    z, xx, y, k = place()
    depth = blocks // 2
    same = xx == k

    barrier, others = greet_plane(blocks, across=True)
    acc[...] = jnp.zeros_like(acc)
    pl.semaphore_wait(barrier, others)

    def go_copy(unit):
        return remote(go.at[unit], gor.at[own], o_send.at[unit], o_recv.at[own], 2 * (unit // 2) + k, 2 * y + unit % 2)

    for unit in range(blocks):
        alone = jnp.logical_and(same, unit == 2 * z + k)

        @pl.when(jnp.logical_not(alone))
        def _():
            go_copy(unit).start()

        @pl.when(alone)
        def _():
            gor[own] = go[unit]

    def wo_copy(half):
        return remote(
            gwo.at[2 * half + 1 - k], wo_in.at[half], w_send.at[half], w_recv.at[half], own, 2 * y + 1 - k
        )

    wo_far = remote(wo_both.at[1 - y], wo_over, w_send.at[2], w_recv.at[2], own, 2 * (1 - y) + k)
    wo_copy(0).start()
    wo_copy(1).start()
    lane = lax.broadcasted_iota(jnp.int32, (step, 128), 1)
    for i in range(seq // step):
        part = slice(i * step, (i + 1) * step)
        span = (i + 1) * step
        seen = lax.broadcasted_iota(jnp.int32, (step, span), 1) <= (
            lax.broadcasted_iota(jnp.int32, (step, span), 0) + i * step
        )
        for head in range(GROUP_HEADS):
            at = head // 2 * 128
            q = jnp.where(lane // 64 == head % 2, qkv[part, at : at + 128], zero)
            s = nt(q, qkv[:span, lanes + at : lanes + at + 128])
            p = jnp.exp(jnp.where(seen, s, -1e30) - lse[part, head : head + 1])
            probs[head, part, :span] = jnp.where(seen, p, 0.0)
    for ctx in range(blocks):

        @pl.when(jnp.logical_not(jnp.logical_and(same, ctx == own)))
        def _():
            remote(go.at[0], gor.at[ctx], o_send.at[0], o_recv.at[ctx], ctx, 2 * y + xx).wait_recv()

    for half in range(2):
        wo_copy(half).wait_recv()
        total = gwo[2 * half + k].astype(jnp.float32) + wo_in[half].astype(jnp.float32)
        wo_both[half] = total.astype(jnp.bfloat16)
    wo_far.start()
    for b in range(blocks):
        gos[b * blk : (b + 1) * blk, :] = gor[inv[b]]
    for i in range(seq // step):
        part = slice(i * step, (i + 1) * step)
        span = (i + 1) * step
        key_lane = lax.broadcasted_iota(jnp.int32, (span, 128), 1)
        for head in range(GROUP_HEADS):
            tile, side = head // 2, head % 2
            at = tile * 128
            mine = lane // 64 == side
            q = jnp.where(mine, qkv[part, at : at + 128], zero)
            g = jnp.where(mine, gos[part, at : at + 128], zero)
            keys = qkv[:span, lanes + at : lanes + at + 128]
            values = qkv[:span, 2 * lanes + at : 2 * lanes + at + 128]
            delta = jnp.sum(g.astype(jnp.float32) * o[part, at : at + 128], axis=1, keepdims=True)
            p = probs[head, part, :span]
            ds = (p * (nt(g, values) - delta)).astype(jnp.bfloat16)
            acc[:span, 2 * lanes + at : 2 * lanes + at + 128] += tn(p.astype(jnp.bfloat16), g)
            acc[:span, lanes + at : lanes + at + 128] += tn(ds, q)
            acc[part, at : at + 128] += nn(ds, jnp.where(key_lane // 64 == side, keys, zero))
    for b in range(blocks):
        part = slice(b * blk, (b + 1) * blk)
        cos2 = jnp.concatenate([cosine[part, :]] * (lanes // 128), axis=1)
        sin2 = jnp.concatenate([sine[part, :]] * (lanes // 128), axis=1)
        grads[b, :, :lanes] = spin(acc[part, :lanes] * HEAD_DIM**-0.5, cos2, -sin2).astype(jnp.bfloat16)
        grads[b, :, lanes : 2 * lanes] = spin(acc[part, lanes : 2 * lanes], cos2, -sin2).astype(jnp.bfloat16)
        grads[b, :, 2 * lanes :] = acc[part, 2 * lanes :].astype(jnp.bfloat16)

    def sib_copy(zz):
        return remote(sib_out.at[zz], sib_in.at[zz], s_send.at[zz], s_recv.at[zz], own, 2 * y + 1 - k)

    def gn_copy(zz):
        return remote(gn_out.at[zz], gnr.at[z], g_send.at[zz], g_recv.at[z], 2 * zz + k, 2 * y + xx)

    gain = small[0:1, :].astype(jnp.float32)
    ggain = jnp.zeros((1, width), jnp.float32)
    for b in range(blocks):
        gns[b] = nt(grads[b], w[...])
        ggain = ggain + jnp.sum(gns[b] * n1s[b * blk : (b + 1) * blk, :].astype(jnp.float32), axis=0, keepdims=True)
    for zz in range(depth):
        sib_out[zz] = gns[order[2 * zz + 1 - k]].astype(jnp.bfloat16)
        sib_copy(zz).start()
    for zz in range(depth):
        sib_copy(zz).wait_recv()
        alone = jnp.logical_and(same, zz == z)
        gn_out[zz] = (gns[order[2 * zz + k]] + sib_in[zz].astype(jnp.float32)).astype(jnp.bfloat16)

        @pl.when(jnp.logical_not(alone))
        def _():
            gn_copy(zz).start()

        @pl.when(alone)
        def _():
            gnr[z] = gn_out[zz]

    packs, inner = gwo.shape[0], gwo.shape[1]
    sums = jnp.concatenate([ggain / gain, gsmall[...]], axis=0)
    sums = jnp.concatenate([sums, jnp.zeros((128 - sums.shape[0], width), jnp.float32)], axis=0)
    gw[:, :128] = jnp.transpose(sums).astype(jnp.bfloat16)
    gw[:, 128 + 3 * inner :] = jnp.zeros((width, gw.shape[1] - 128 - 3 * inner), jnp.bfloat16)
    for i in range(width // 256):
        part = slice(i * 256, (i + 1) * 256)
        piece = tn(n1s[:, part], grads[...].reshape(seq, 3 * lanes)).astype(jnp.bfloat16)
        for c in range(3):
            gw[part, 128 + c * inner : 128 + (c + 1) * inner] = piece[:, c * lanes : c * lanes + inner]

    def rows_of(f):
        return pl.ds(pl.multiple_of(f * inner, inner), inner)

    def home_copy(half):
        rows = gw.at[rows_of(2 * half + 1 - k), :]
        return remote(rows, gw_in.at[half], r_send.at[half], r_recv.at[half], own, 2 * y + 1 - k)

    for half in range(2):
        home_copy(half).start()
    for half in range(2):
        home_copy(half).wait_recv()
        kept, came = gw[rows_of(2 * half + k), :], gw_in[half]
        both[half, :, :128] = (kept[:, :128].astype(jnp.float32) + came[:, :128].astype(jnp.float32)).astype(jnp.bfloat16)
        heads = slice(128, 128 + 3 * inner)
        for core in range(2):

            @pl.when(k == core)
            def _():
                both[half, :, 128 + core * 3 * inner : 128 + (core + 1) * 3 * inner] = kept[:, heads]
                both[half, :, 128 + (1 - core) * 3 * inner : 128 + (2 - core) * 3 * inner] = came[:, heads]

    over = remote(both.at[1 - y], both_in, r_send.at[2], r_recv.at[2], own, 2 * (1 - y) + k)
    over.start()
    values = x[...]
    factor = rms_factor(values)
    base = values * factor
    for zz in range(depth):

        @pl.when(jnp.logical_not(jnp.logical_and(same, zz == z)))
        def _():
            remote(gn_out.at[0], gnr.at[zz], g_send.at[0], g_recv.at[zz], 2 * zz + k, 2 * y + xx).wait_recv()

    halves = []
    for h in range(2):
        total = gnr[h * (depth // 2)].astype(jnp.float32)
        for zz in range(1, depth // 2):
            total = total + gnr[h * (depth // 2) + zz].astype(jnp.float32)
        halves.append(total)
    gn = jnp.concatenate(halves, axis=0)
    gb = gn * gain
    grad = ghst[...] + factor * (gb - base * jnp.mean(gb * base, axis=-1, keepdims=True))
    gx[...] = grad
    gm[...] = grad.astype(jnp.bfloat16)
    wo_far.wait_recv()
    edge = both.shape[2]
    dense[:, edge:] = (wo_both[y].astype(jnp.float32) + wo_over[...].astype(jnp.float32)).astype(jnp.bfloat16)
    over.wait_recv()
    dense[:, :edge] = (both[y].astype(jnp.float32) + both_in[...].astype(jnp.float32)).astype(jnp.bfloat16)
    for half in range(2):
        home_copy(half).wait_send()
        wo_copy(half).wait_send()
    wo_far.wait_send()
    over.wait_send()
    for unit in range(blocks):

        @pl.when(jnp.logical_not(jnp.logical_and(same, unit == 2 * z + k)))
        def _():
            go_copy(unit).wait_send()

    for zz in range(depth):
        sib_copy(zz).wait_send()

        @pl.when(jnp.logical_not(jnp.logical_and(same, zz == z)))
        def _():
            gn_copy(zz).wait_send()


def attn_backward(order, inv, n1s, w, cosine, sine, qkv, o, lse, go, ghst, x, small, gsmall, gwo, number):
    blocks, blk, lanes = go.shape
    seq, width = n1s.shape
    count = x.shape[0]
    packs, inner = gwo.shape[0], gwo.shape[1]
    depth = blocks // 2
    vm = pl.BlockSpec(memory_space=pltpu.VMEM)
    sm = pl.BlockSpec(memory_space=pltpu.SMEM)
    bf = jnp.bfloat16
    dma = pltpu.SemaphoreType.DMA
    return pl.pallas_call(
        attn_bwd_kernel,
        out_shape=[
            shape_of((count, width), jnp.float32),
            shape_of((count, width), bf),
            shape_of((inner, 128 + 6 * inner + width), bf),
        ],
        in_specs=[sm] * 2 + [vm] * 13,
        out_specs=[vm] * 3,
        scratch_shapes=[
            pltpu.VMEM((blocks, blk, lanes), bf),
            pltpu.VMEM((seq, lanes), bf),
            pltpu.VMEM((blocks, blk, 3 * lanes), bf),
            pltpu.VMEM((seq, 3 * lanes), jnp.float32),
            pltpu.VMEM((blocks, blk, width), jnp.float32),
            pltpu.VMEM((depth, blk, width), bf),
            pltpu.VMEM((depth, blk, width), bf),
            pltpu.VMEM((depth, blk, width), bf),
            pltpu.VMEM((depth, blk, width), bf),
            pltpu.VMEM((packs * inner, 3 * lanes), bf),
            pltpu.VMEM((2, inner, 3 * lanes), bf),
            pltpu.VMEM((2, inner, 128 + 6 * inner), bf),
            pltpu.VMEM((inner, 128 + 6 * inner), bf),
            pltpu.VMEM((2, inner, width), bf),
            pltpu.VMEM((2, inner, width), bf),
            pltpu.VMEM((inner, width), bf),
            pltpu.VMEM((GROUP_HEADS, seq, seq), jnp.float32),
        ]
        + [dma((blocks,))] * 2
        + [dma((depth,))] * 4
        + [dma((3,))] * 4,
        compiler_params=params_of(54, collective_id=number, has_side_effects=True),
        cost_estimate=BRIEF,
        name="attn_bwd",
    )(order, inv, n1s, w, cosine, sine, qkv, o, lse, go, ghst, x, small, gsmall, gwo)


def routing(raw, before, routes):
    count = raw.shape[1]
    ids = lax.broadcasted_iota(jnp.int32, (16, count), 0)
    logits = raw + before
    first, second = ids == routes[0:1], ids == routes[1:2]
    z0 = jnp.sum(jnp.where(first, logits, 0.0), axis=0, keepdims=True)
    z1 = jnp.sum(jnp.where(second, logits, 0.0), axis=0, keepdims=True)
    top = jnp.maximum(z0, z1)
    e0, e1 = jnp.exp(z0 - top), jnp.exp(z1 - top)
    total = e0 + e1
    coef = jnp.where(first, e0 / total, 0.0) + jnp.where(second, e1 / total, 0.0)
    hits = jnp.where(first | second, 1.0, 0.0)
    upto = lax.broadcasted_iota(jnp.int32, (count, count), 0) <= lax.broadcasted_iota(jnp.int32, (count, count), 1)
    place = nn(hits.astype(jnp.bfloat16), jnp.where(upto, 1.0, 0.0).astype(jnp.bfloat16)) - 1.0
    slot = jnp.where(hits > 0, place, -1.0)
    return jnp.concatenate([raw, coef, slot[:NF], logits], axis=0)


def one_hot(slot):
    count = slot.shape[1]
    ids = lax.broadcasted_iota(jnp.int32, (NF, MOST, count), 1)
    hit = ids == slot.astype(jnp.int32)[:, None, :]
    return jnp.where(hit, 1.0, 0.0).reshape(NF * MOST, count)


def slot_values(hot, rows):
    count = rows.shape[1]
    wide = jnp.broadcast_to(rows[:, None, :], (NF, MOST, count)).reshape(NF * MOST, count)
    return jnp.sum(hot * wide, axis=1, keepdims=True)


def swap_rows(own, rows, send, recv, forward_send, forward_recv):
    ctx = lax.axis_index("ctx")
    _, _, y, k = place()
    beside, across = 2 * y + 1 - k, 2 * (1 - y) + k
    far = remote(own, rows.at[2], send.at[0], recv.at[0], ctx, across)
    near = remote(own, rows.at[1], send.at[1], recv.at[1], ctx, beside)
    onward = remote(rows.at[2], rows.at[3], forward_send, forward_recv, ctx, beside)
    far.start()
    near.start()
    return near, far, onward


def sum_rows(parts, beside_in, mid, across_in, send, recv):
    ctx = lax.axis_index("ctx")
    _, _, y, k = place()
    beside, across = 2 * y + 1 - k, 2 * (1 - y) + k
    first = remote(parts.at[3], beside_in.at[1], send.at[0], recv.at[0], ctx, beside)
    second = remote(parts.at[1], beside_in.at[0], send.at[1], recv.at[1], ctx, beside)
    third = remote(mid, across_in, send.at[2], recv.at[2], ctx, across)
    return first, second, third


def ffn_fwd_kernel(
    ub, hst, small, routes, before, wgu, wd,
    ubf, table, ext, x_next,
    rows_s, hot_s, x_s, y_s, coef_s, parts, beside_in, mid, across_in,
    a_send, a_recv, r_send, r_recv,
):
    e = pl.program_id(0)
    packs = ubf.shape[0]
    count, width = ub.shape
    router = small[2 + NC :, :]

    def gathers():
        return swap_rows(ub, rows_s, a_send, a_recv, a_send.at[2], a_recv.at[2])

    def sums():
        return sum_rows(parts, beside_in, mid, across_in, r_send, r_recv)

    @pl.when(e == 0)
    def _():
        barrier, others = greet_packs()
        rows_s[0] = ub[...]

        def prepare(d):
            rows = routing(nt(router, rows_s[d]), before[d, LOGI : LOGI + 16, :], routes[d])
            table[d] = rows
            hot = one_hot(rows[SLOT : SLOT + NF])
            coef_s[d] = slot_values(hot, rows[COEF : COEF + NF])
            hot_low = hot.astype(jnp.bfloat16)
            hot_s[d] = hot_low
            x = nn(hot_low, rows_s[d]).astype(jnp.bfloat16)
            for n in range(NF):
                x_s[n, d * MOST : (d + 1) * MOST, :] = x[n * MOST : (n + 1) * MOST]

        pl.semaphore_wait(barrier, others)
        near, far, onward = gathers()
        prepare(0)
        near.wait_recv()
        prepare(1)
        far.wait_recv()
        onward.start()
        prepare(2)
        onward.wait_recv()
        prepare(3)
        ubf[...] = rows_s[...]
        ext[:count, :] = ub[...]
        rows = table[0]
        ext[count:, :] = jnp.zeros((16, width), jnp.bfloat16)
        ext[count:, :count] = rows[COEF : COEF + 16].astype(jnp.bfloat16)
        slots = jnp.concatenate([rows[SLOT : SLOT + NF], jnp.zeros((16 - NF, count), jnp.float32)], axis=0)
        ext[count:, count : 2 * count] = slots.astype(jnp.bfloat16)
        near.wait_send()
        far.wait_send()
        onward.wait_send()

    x = x_s[e]
    gate, up = nn(x, wgu[0, 0, 0]), nn(x, wgu[0, 0, 1])
    hid = (gate * jax.nn.sigmoid(gate) * up).astype(jnp.bfloat16)
    out = nn(hid, wd[0, 0])
    at = pl.ds(pl.multiple_of(e * MOST, MOST), MOST)
    for d in range(packs):
        y_s[d, at, :] = (out[d * MOST : (d + 1) * MOST] * coef_s[d, at, :]).astype(jnp.bfloat16)

    @pl.when(e == NF - 1)
    def _():
        first, second, third = sums()
        parts[3] = tn(hot_s[3], y_s[3]).astype(jnp.bfloat16)
        first.start()
        parts[1] = tn(hot_s[1], y_s[1]).astype(jnp.bfloat16)
        second.start()
        away = tn(hot_s[2], y_s[2])
        first.wait_recv()
        mid[...] = (away + beside_in[1].astype(jnp.float32)).astype(jnp.bfloat16)
        third.start()
        home = tn(hot_s[0], y_s[0])
        _, _, scale_u, scale_c = mixing_rows(table[0])
        columns = to_columns([scale_u] + scale_c)
        values = hst[...]
        moe = home + columns[0] * ((values * rms_factor(values)) * small[1:2, :].astype(jnp.float32))
        for c in range(NC):
            moe = moe + columns[1 + c] * small[2 + c : 3 + c, :].astype(jnp.float32)
        second.wait_recv()
        moe = moe + beside_in[0].astype(jnp.float32)
        third.wait_recv()
        x_next[...] = values + (moe + across_in[...].astype(jnp.float32))
        first.wait_send()
        second.wait_send()
        third.wait_send()


def whole_spec(dims):
    return pl.BlockSpec(dims, lambda *_: (0,) * len(dims))


def exchange_scratch(packs, count, width):
    bf = jnp.bfloat16
    return [
        pltpu.VMEM((packs, count, width), bf),
        pltpu.VMEM((2, count, width), bf),
        pltpu.VMEM((count, width), bf),
        pltpu.VMEM((count, width), bf),
    ]


def ffn_forward(layer, ub, hst, small, routes, before, wgu, wd, number):
    count, width = ub.shape
    packs = routes.shape[0]
    hidden = wd.shape[2]
    bf = jnp.bfloat16
    outs = [
        shape_of((packs, count, width), bf),
        shape_of((packs, ROUT, count), jnp.float32),
        shape_of((count + 16, width), bf),
        shape_of((count, width), jnp.float32),
    ]
    return pl.pallas_call(
        ffn_fwd_kernel,
        grid=(NF,),
        out_shape=outs,
        in_specs=[whole_spec(a.shape) for a in (ub, hst, small, routes, before)]
        + [
            pl.BlockSpec((1, 1, 2, width, hidden), lambda e: (layer, e, 0, 0, 0)),
            pl.BlockSpec((1, 1, hidden, width), lambda e: (layer, e, 0, 0)),
        ],
        out_specs=[whole_spec(a.shape) for a in outs],
        scratch_shapes=[
            pltpu.VMEM((packs, count, width), bf),
            pltpu.VMEM((packs, NF * MOST, count), bf),
            pltpu.VMEM((NF, packs * MOST, width), bf),
            pltpu.VMEM((packs, NF * MOST, width), bf),
            pltpu.VMEM((packs, NF * MOST, 1), jnp.float32),
        ]
        + exchange_scratch(packs, count, width)
        + [pltpu.SemaphoreType.DMA((3,))] * 4,
        compiler_params=params_of(40, collective_id=number, has_side_effects=True),
        cost_estimate=BRIEF,
        name="ffn_fwd",
    )(ub, hst, small, routes, before, wgu, wd)


def silu_parts(gate, up, ghid):
    sig = jax.nn.sigmoid(gate)
    act = gate * sig
    dg = (ghid * up * sig * (1.0 + gate * (1.0 - sig))).astype(jnp.bfloat16)
    du = (ghid * act).astype(jnp.bfloat16)
    return act * up, dg, du


def ffn_bwd_kernel(
    gm, gx, ubf, table, hst, small, routes, gprev, wo, ob, wgu, wd,
    ghst, go, gwo, gsmall, glog,
    rows_s, hot_s, x_s, g_s, y_s, coef_s, gc_s, gcoef, gcoef_in, parts, beside_in, mid, across_in,
    a_send, a_recv, r_send, r_recv, c_send, c_recv,
):
    e = pl.program_id(0)
    packs = ubf.shape[0]
    ctx = lax.axis_index("ctx")
    _, _, y, k = place()
    peers = [None, 2 * y + 1 - k, 2 * (1 - y) + k, 2 * (1 - y) + 1 - k]

    def gathers():
        return swap_rows(gm, rows_s, a_send, a_recv, a_send.at[2], a_recv.at[2])

    def sums():
        return sum_rows(parts, beside_in, mid, across_in, r_send, r_recv)

    @pl.when(e == 0)
    def _():
        barrier, others = greet_packs()
        rows_s[0] = gm[...]

        def prepare(d):
            hot = one_hot(table[d, SLOT : SLOT + NF, :])
            coef_s[d] = slot_values(hot, table[d, COEF : COEF + NF, :])
            hot_low = hot.astype(jnp.bfloat16)
            hot_s[d] = hot_low
            x = nn(hot_low, ubf[d]).astype(jnp.bfloat16)
            for n in range(NF):
                x_s[n, d * MOST : (d + 1) * MOST, :] = x[n * MOST : (n + 1) * MOST]

        def spread(d):
            g = nn(hot_s[d], rows_s[d]).astype(jnp.bfloat16)
            for n in range(NF):
                g_s[n, d * MOST : (d + 1) * MOST, :] = g[n * MOST : (n + 1) * MOST]

        pl.semaphore_wait(barrier, others)
        near, far, onward = gathers()
        for d in range(packs):
            prepare(d)
        spread(0)
        near.wait_recv()
        far.wait_recv()
        onward.start()
        spread(1)
        spread(2)
        onward.wait_recv()
        spread(3)
        near.wait_send()
        far.wait_send()
        onward.wait_send()

    x = x_s[e]
    at = pl.ds(pl.multiple_of(e * MOST, MOST), MOST)
    coef = jnp.concatenate([coef_s[d, at, :] for d in range(packs)], axis=0)
    gate, up = nn(x, wgu[0, 0, 0]), nn(x, wgu[0, 0, 1])
    ghid = nt(g_s[e], wd[0, 0])
    hid, dg, du = silu_parts(gate, up, ghid * coef)
    dots = jnp.sum(hid * ghid, axis=1, keepdims=True)
    out = nt(dg, wgu[0, 0, 0]) + nt(du, wgu[0, 0, 1])
    for d in range(packs):
        y_s[d, at, :] = out[d * MOST : (d + 1) * MOST].astype(jnp.bfloat16)
        gc_s[d, at, :] = dots[d * MOST : (d + 1) * MOST]

    @pl.when(e == NF - 1)
    def _():
        first, second, third = sums()

        def coef_copy(d):
            return remote(gcoef.at[d], gcoef_in.at[d - 1], c_send.at[d - 1], c_recv.at[d - 1], ctx, peers[d])

        parts[3] = tn(hot_s[3], y_s[3]).astype(jnp.bfloat16)
        first.start()
        parts[1] = tn(hot_s[1], y_s[1]).astype(jnp.bfloat16)
        second.start()
        for d in range(packs):
            wide = hot_s[d].astype(jnp.float32) * gc_s[d]
            gcoef[d] = jnp.sum(wide.reshape(NF, MOST, wide.shape[1]), axis=1)
            if d > 0:
                coef_copy(d).start()
        away = tn(hot_s[2], y_s[2])
        first.wait_recv()
        mid[...] = (away + beside_in[1].astype(jnp.float32)).astype(jnp.bfloat16)
        third.start()
        home = tn(hot_s[0], y_s[0])
        ready = middle_ready(gx[...], table[0], hst[...], small[...])
        second.wait_recv()
        home = home + beside_in[0].astype(jnp.float32)
        total = gcoef[0]
        for d in range(1, packs):
            coef_copy(d).wait_recv()
            total = total + gcoef_in[d - 1]
        third.wait_recv()
        home = home + across_in[...].astype(jnp.float32)
        results = middle(
            ready, gx[...], home, total, table[0], routes[...], gprev[...], ubf[0], small[...], wo[...], ob[...]
        )
        for ref, value in zip((ghst, go, gwo, gsmall, glog), results):
            ref[...] = value
        first.wait_send()
        second.wait_send()
        third.wait_send()
        for d in range(1, packs):
            coef_copy(d).wait_send()


def ffn_backward(layer, gm, gx, ubf, table, hst, small, routes, gprev, wo, ob, wgu, wd, number):
    packs, count, width = ubf.shape
    hidden = wd.shape[2]
    bf, f32 = jnp.bfloat16, jnp.float32
    outs = [
        shape_of((count, width), f32),
        shape_of(ob.shape, bf),
        shape_of(wo.shape, bf),
        shape_of((1 + NC + 16, width), f32),
        shape_of((16, count), f32),
    ]
    args = (gm, gx, ubf, table, hst, small, routes, gprev, wo, ob)
    dma = pltpu.SemaphoreType.DMA
    return pl.pallas_call(
        ffn_bwd_kernel,
        grid=(NF,),
        out_shape=outs,
        in_specs=[whole_spec(a.shape) for a in args]
        + [
            pl.BlockSpec((1, 1, 2, width, hidden), lambda e: (layer, e, 0, 0, 0)),
            pl.BlockSpec((1, 1, hidden, width), lambda e: (layer, e, 0, 0)),
        ],
        out_specs=[whole_spec(a.shape) for a in outs],
        scratch_shapes=[
            pltpu.VMEM((packs, count, width), bf),
            pltpu.VMEM((packs, NF * MOST, count), bf),
            pltpu.VMEM((NF, packs * MOST, width), bf),
            pltpu.VMEM((NF, packs * MOST, width), bf),
            pltpu.VMEM((packs, NF * MOST, width), bf),
            pltpu.VMEM((packs, NF * MOST, 1), f32),
            pltpu.VMEM((packs, NF * MOST, 1), f32),
            pltpu.VMEM((packs, NF, count), f32),
            pltpu.VMEM((packs - 1, NF, count), f32),
        ]
        + exchange_scratch(packs, count, width)
        + [dma((3,))] * 6,
        compiler_params=params_of(50, collective_id=number, has_side_effects=True),
        cost_estimate=BRIEF,
        name="ffn_bwd",
    )(*args, wgu, wd)


PACK = 80


def pack_kernel(counts, bases, totals, tail, ext, gm, out, buf, carry, blank, sems):
    step = pl.program_id(0)
    some, count, width = gm.shape

    @pl.when(step == 0)
    def _():
        carry[...] = jnp.zeros_like(carry)
        blank[...] = jnp.zeros_like(blank)

    def whole_groups(d, e):
        at = d * NF + e
        return (bases[at] % 16 + counts[at]) // 16

    def each_copy(block, what):
        for i in range(some):
            for e in range(NF):
                groups = whole_groups(block * some + i, e)
                start = pl.multiple_of(bases[(block * some + i) * NF + e] // 16 * 16, 16)
                for n in range(1, PACK // 16):

                    @pl.when(groups == n)
                    def _():
                        source = buf.at[block % 2, i, e, pl.ds(0, 16 * n), :]
                        what(pltpu.make_async_copy(source, out.at[e, pl.ds(start, 16 * n), :], sems.at[block % 2, i, e]))

    def begin(copy):
        copy.start()

    def end(copy):
        copy.wait()

    @pl.when(step >= 2)
    def _():
        each_copy(step - 2, end)

    ids = lax.broadcasted_iota(jnp.int32, (PACK, count), 0)
    side = step % 2
    for i in range(some):
        d = step * some + i
        rows = tail[i].astype(jnp.float32)
        slot = rows[:NF, count : 2 * count].astype(jnp.int32)
        slot = jnp.where(slot < 0, -PACK, slot)
        hot, weighted = [], []
        for e in range(NF):
            hit = ids == slot[e : e + 1] + bases[d * NF + e] % 16
            hot.append(jnp.where(hit, 1.0, 0.0).astype(jnp.bfloat16))
            weighted.append(jnp.where(hit, rows[e : e + 1, :count], 0.0).astype(jnp.bfloat16))
        low = nn(jnp.concatenate(hot, axis=0), ext[i, :count, :]).astype(jnp.bfloat16)
        low_g = nn(jnp.concatenate(weighted, axis=0), gm[i]).astype(jnp.bfloat16)
        for lanes, values in ((slice(0, width), low), (slice(width, 2 * width), low_g)):
            for e in range(NF):
                buf[side, i, e, :, lanes] = values[e * PACK : (e + 1) * PACK]
    for i in range(some):
        for e in range(NF):
            buf[side, i, e, :16, :] += carry[e]
            group = pl.multiple_of(whole_groups(step * some + i, e) * 16, 16)
            carry[e] = buf[side, i, e, pl.ds(group, 16), :]
    each_copy(step, begin)

    @pl.when(step == pl.num_programs(0) - 1)
    def _():
        last = pl.num_programs(0)
        each_copy(last - 2, end)
        each_copy(last - 1, end)
        copies = []
        for e in range(NF):
            start = pl.multiple_of(totals[e] // 16 * 16, 16)
            copies.append(pltpu.make_async_copy(carry.at[e], out.at[e, pl.ds(start, 16), :], sems.at[0, 0, e]))
            rest = out.at[e, pl.ds(start + 16, blank.shape[0]), :]
            copies.append(pltpu.make_async_copy(blank, rest, sems.at[1, 0, e]))
        for copy in copies:
            copy.start()
        for copy in copies:
            copy.wait()


def expert_counts(ext):
    count = ext.shape[2] // 3
    slot = ext[:, ext.shape[1] - 16 : ext.shape[1] - 16 + NF, count : 2 * count].astype(jnp.float32)
    counts = (jnp.max(slot, axis=2) + 1.0).astype(jnp.int32)
    upto = jnp.cumsum(counts, axis=0)
    return counts.reshape(-1), (upto - counts).reshape(-1), upto[-1]


def pack_rows(numbers, ext, gm):
    devices, count, width = gm.shape
    some, blank = 4, 256
    bf = jnp.bfloat16
    return pl.pallas_call(
        pack_kernel,
        grid_spec=pltpu.PrefetchScalarGridSpec(
            num_scalar_prefetch=3,
            grid=(devices // some,),
            in_specs=[
                pl.BlockSpec((some, 16, width), lambda d, *_: (d, count // 16, 0)),
                pl.BlockSpec((some,) + ext.shape[1:], lambda d, *_: (d, 0, 0)),
                pl.BlockSpec((some, count, width), lambda d, *_: (d, 0, 0)),
            ],
            out_specs=pl.BlockSpec(memory_space=pl.ANY),
            scratch_shapes=[
                pltpu.VMEM((2, some, NF, PACK, 2 * width), bf),
                pltpu.VMEM((NF, 16, 2 * width), bf),
                pltpu.VMEM((blank, 2 * width), bf),
                pltpu.SemaphoreType.DMA((2, some, NF)),
            ],
        ),
        out_shape=shape_of((NF, devices * MOST + 16 + blank, 2 * width), bf),
        compiler_params=params_of(),
        cost_estimate=BRIEF,
        name="pack_rows",
    )(*numbers, ext, ext, gm)


def dw_kernel(first, totals, packed, wgu, wd, *refs):
    dgu, dd, pair_s, hid_s = refs[-4:]
    hidden = hid_s.shape[1]
    total = totals[first + pl.program_id(0)]
    width = packed.shape[2] // 2
    chunk = 1024

    def pieces(part):
        xs, gs = packed[0, part, :width], packed[0, part, width:]
        hid, dg, du = silu_parts(nn(xs, wgu[0, 0, 0]), nn(xs, wgu[0, 0, 1]), nt(gs, wd[0, 0]))
        hid_s[part, :] = hid.astype(jnp.bfloat16)
        pair_s[part, :hidden] = dg
        pair_s[part, hidden:] = du

    def chunk_of(i, _):
        pieces(pl.ds(pl.multiple_of(i * chunk, chunk), chunk))
        return 0

    needed = jnp.maximum((total + 255) // 256, 1)
    lax.fori_loop(0, needed // 4, chunk_of, 0)

    @pl.when(needed % 4 >= 2)
    def _():
        pieces(pl.ds(pl.multiple_of(needed // 4 * chunk, 512), 512))

    @pl.when(needed % 2 == 1)
    def _():
        pieces(pl.ds(pl.multiple_of((needed - 1) * 256, 256), 256))

    for size in range(1, hid_s.shape[0] // 256 + 1):

        @pl.when(needed == size)
        def _():
            rows = 256 * size

            def inputs(i, _):
                part = pl.ds(pl.multiple_of(i * 384, 384), 384)
                xs = packed[0, :rows, part]
                both = tn(xs, pair_s[:rows, :])
                dgu[0, 0, 0, part, :] = both[:, :hidden]
                dgu[0, 0, 1, part, :] = both[:, hidden:]
                return 0

            lax.fori_loop(0, width // 384, inputs, 0)

            def outputs(i, _):
                part = pl.ds(pl.multiple_of(i * 512, 512), 512)
                dd[0, 0, part, :] = tn(hid_s[:rows, part], packed[0, :rows, width:])
                return 0

            lax.fori_loop(0, hid_s.shape[1] // 512, outputs, 0)


def weight_grads(layer, first, last, totals, packed, wgu, wd, earlier):
    _, rows, both = packed.shape
    hidden, width = wd.shape[2], wd.shape[3]
    gu_spec = pl.BlockSpec((1, 1, 2, width, hidden), lambda e, *_: (layer, e + first, 0, 0, 0))
    d_spec = pl.BlockSpec((1, 1, hidden, width), lambda e, *_: (layer, e + first, 0, 0))
    row_spec = pl.BlockSpec((1, rows, both), lambda e, *_: (e + first, 0, 0))
    return pl.pallas_call(
        functools.partial(dw_kernel, first),
        grid_spec=pltpu.PrefetchScalarGridSpec(
            num_scalar_prefetch=1,
            grid=(last - first,),
            in_specs=[row_spec, gu_spec, d_spec] + [pl.BlockSpec(memory_space=pl.ANY)] * len(earlier),
            out_specs=[gu_spec, d_spec],
            scratch_shapes=[
                pltpu.VMEM((rows // 256 * 256 - 256, 2 * hidden), jnp.bfloat16),
                pltpu.VMEM((rows // 256 * 256 - 256, hidden), jnp.bfloat16),
            ],
        ),
        out_shape=[shape_of(wgu.shape, jnp.float32), shape_of(wd.shape, jnp.float32)],
        input_output_aliases={4 + i: i for i in range(len(earlier))},
        compiler_params=params_of(),
        cost_estimate=BRIEF,
        name="weight_grads",
    )(totals, packed, wgu, wd, *earlier)


def norm_low(x, gain):
    return ((x * rms_factor(x)) * gain).astype(jnp.bfloat16)


def post_attention(ob, x, wo, gain):
    groups = wo.shape[0]
    inner = wo.shape[1]
    blk = ob.shape[1]
    halves = []
    for h in range(2):
        total = x[h * blk : (h + 1) * blk]
        for g in range(groups):
            total = total + nn(ob[h * groups + g][:, :inner], wo[g])
        halves.append(total)
    hst = jnp.concatenate(halves, axis=0)
    return hst, norm_low(hst, gain)


def mixing_rows(table):
    raw, coef = table[RAW : RAW + 16], table[COEF : COEF + 16]
    pairs = []
    for c in range(NC):
        r0, r1 = raw[NE + 2 * c : NE + 2 * c + 1], raw[NE + 2 * c + 1 : NE + 2 * c + 2]
        top = jnp.maximum(r0, r1)
        e0, e1 = jnp.exp(r0 - top), jnp.exp(r1 - top)
        pairs.append((e0 / (e0 + e1), e1 / (e0 + e1)))
    shares = [coef[NF + 2 + c : NF + 3 + c] for c in range(NC)]
    scale_u = coef[NF + 1 : NF + 2]
    for c in range(NC):
        scale_u = scale_u + shares[c] * pairs[c][0]
    return pairs, shares, scale_u, [shares[c] * pairs[c][1] for c in range(NC)]


def middle_ready(gx, table, hst, small):
    gain = small[1:2].astype(jnp.float32)
    consts = small[2 : 2 + NC].astype(jnp.float32)
    pairs, shares, scale_u, scale_c = mixing_rows(table)
    columns = to_columns([scale_u] + scale_c)
    factor = rms_factor(hst)
    base = hst * factor
    u = base * gain
    dots = [jnp.sum(gx * u, axis=1, keepdims=True)]
    dots += [jnp.sum(gx * consts[c : c + 1], axis=1, keepdims=True) for c in range(NC)]
    dots = to_rows(dots, 8)
    const_sums = [jnp.sum(gx * columns[1 + c], axis=0, keepdims=True) for c in range(NC)]
    return pairs, shares, gain, factor, base, dots, const_sums, gx * columns[0]


def middle(ready, gx, parts, gcoef, table, routes, gprev, ub, small, wo, ob):
    pairs, shares, gain, factor, base, dots, const_sums, grad_in = ready
    groups = wo.shape[0]
    inner = wo.shape[1]
    blk = ob.shape[1]
    router = small[2 + NC :]
    dot_u = dots[0:1]
    dot_c = [dots[1 + c : 2 + c] for c in range(NC)]
    ids = lax.broadcasted_iota(jnp.int32, (16, gx.shape[0]), 0)
    grads = jnp.concatenate([gcoef, jnp.zeros_like(gcoef)], axis=0)
    grads = jnp.where(ids == NF + 1, dot_u, grads)
    raw_rows = []
    for c in range(NC):
        a0, a1 = pairs[c]
        grads = jnp.where(ids == NF + 2 + c, a0 * dot_u + a1 * dot_c[c], grads)
        g0, g1 = shares[c] * dot_u, shares[c] * dot_c[c]
        both = a0 * g0 + a1 * g1
        raw_rows += [a0 * (g0 - both), a1 * (g1 - both)]
    logits = table[LOGI : LOGI + 16]
    first, second = ids == routes[0:1], ids == routes[1:2]

    def pick(chosen, rows):
        return jnp.sum(jnp.where(chosen, rows, 0.0), axis=0, keepdims=True)

    z0, z1 = pick(first, logits), pick(second, logits)
    top = jnp.maximum(z0, z1)
    e0, e1 = jnp.exp(z0 - top), jnp.exp(z1 - top)
    w0, w1 = e0 / (e0 + e1), e1 / (e0 + e1)
    gg0, gg1 = pick(first, grads), pick(second, grads)
    both = w0 * gg0 + w1 * gg1
    glog = jnp.where(first, w0 * (gg0 - both), 0.0) + jnp.where(second, w1 * (gg1 - both), 0.0) + gprev
    graw = glog
    for index, row in enumerate(raw_rows):
        graw = jnp.where(ids == NE + index, row, graw)
    graw = graw.astype(jnp.bfloat16)
    grad_router = nn(graw, ub)
    gu = grad_in + tn(graw, router) + parts
    sums = [jnp.sum(gu * base, axis=0, keepdims=True)]
    sums += const_sums
    gb = gu * gain
    ghst = gx + factor * (gb - base * jnp.mean(gb * base, axis=-1, keepdims=True))
    gy = ghst.astype(jnp.bfloat16)
    lanes = ob.shape[2]
    go, gwo = [None] * (2 * groups), []
    for g in range(groups):
        value = nt(gy, wo[g]).astype(jnp.bfloat16)
        value = jnp.concatenate([value, jnp.zeros((value.shape[0], lanes - inner), jnp.bfloat16)], axis=1)
        for h in range(2):
            go[h * groups + g] = value[h * blk : (h + 1) * blk]
        mixed = jnp.concatenate([ob[g], ob[groups + g]], axis=0)
        gwo.append(tn(mixed, gy)[:inner].astype(jnp.bfloat16))
    return ghst, jnp.stack(go), jnp.stack(gwo), jnp.concatenate(sums + [grad_router], axis=0), glog


def assemble_kernel(ours, theirs, qkv, out, gains, router, consts):
    z, _, _, _ = place()
    layers = ours.shape[0]
    inner = GROUP_HEADS * HEAD_DIM
    for l in range(layers):
        small = ours[l, :, :128].astype(jnp.float32) + theirs[l, :, :128].astype(jnp.float32)
        router[l] = small[:, 2 + NC : 2 + NC + 16]
        rows = jnp.transpose(small)
        gains[l] = rows[:2]
        consts[l] = rows[2 : 2 + NC]
        first = 128 + 6 * inner
        out[l] = ours[l, :, first:].astype(jnp.float32) + theirs[l, :, first:].astype(jnp.float32)
        for group in range(4):
            for odd in range(2):

                @pl.when(z % 2 == odd)
                def _():
                    source = ours if group // 2 == odd else theirs
                    for c in range(3):
                        at = 128 + (group % 2) * 3 * inner + c * inner
                        qkv[l, c, :, group * inner : (group + 1) * inner] = source[l, :, at : at + inner].astype(jnp.float32)


def assemble(ours, theirs, width):
    layers, shard, _ = ours.shape
    vm = pl.BlockSpec(memory_space=pltpu.VMEM)
    f32 = jnp.float32
    return pl.pallas_call(
        assemble_kernel,
        out_shape=[
            shape_of((layers, 3, shard, width), f32),
            shape_of((layers, shard, width), f32),
            shape_of((layers, 2, shard), f32),
            shape_of((layers, shard, 16), f32),
            shape_of((layers, NC, shard), f32),
        ],
        in_specs=[vm] * 2,
        out_specs=[vm] * 5,
        compiler_params=params_of(),
        cost_estimate=BRIEF,
        name="assemble",
    )(ours, theirs)


def turn_tables(seq):
    half = HEAD_DIM // 2
    frequency = np.exp((-np.log(np.float32(10000.0)) * np.arange(half, dtype=np.float32) / np.float32(half)))
    angles = np.arange(seq, dtype=np.float32)[:, None] * frequency.astype(np.float32)[None, :]
    cosine, sine = np.cos(angles), np.sin(angles)
    cosine = np.concatenate([cosine, cosine] * 2, axis=1).astype(np.float32)
    sine = np.concatenate([-sine, sine] * 2, axis=1).astype(np.float32)
    return jnp.asarray(cosine), jnp.asarray(sine)


def by_heads(
    tokens,
    cotangent,
    seq_lengths,
    block_order,
    routes,
    gains,
    qkv_weights,
    out_weight,
    router,
    const_values,
    w_gate_up,
    w_down,
):
    count, width = tokens.shape[1], tokens.shape[2]
    ctx_size, packs = lax.axis_size("ctx"), lax.axis_size("fsdp")
    blk = count // 2
    seq = blk * ctx_size
    pack = lax.axis_index("fsdp")
    z, xx, y, k = place()
    sequence = z // 2
    shard = width // packs
    f32, bf = jnp.float32, jnp.bfloat16
    everyone = ("ctx", "fsdp")

    cosine, sine = turn_tables(seq)
    routes_t = jnp.swapaxes(routes[:, 0], 1, 2)
    smalls = jnp.concatenate([gains, const_values, jnp.swapaxes(router, 1, 2)], axis=1)
    per_layer = smalls.shape[1]
    ints = jnp.concatenate([routes_t.reshape(-1), block_order[0]])
    places = ints.size
    ints = jnp.pad(ints, (0, -places % shard)).astype(bf).reshape(-1, shard)
    smalls = jnp.concatenate([smalls.reshape(LAYERS * per_layer, shard), ints], axis=0)
    smalls = jnp.pad(smalls, ((0, -smalls.shape[0] % 16), (0, 0)))
    smalls = lax.all_gather(smalls, "fsdp", axis=1, tiled=True)
    ints = smalls[LAYERS * per_layer : LAYERS * per_layer + ints.shape[0]].reshape(-1, packs, shard)
    ints = jnp.swapaxes(ints, 0, 1).reshape(packs, -1).astype(jnp.int32)
    smalls = [smalls[l * per_layer : (l + 1) * per_layer] for l in range(LAYERS)]
    near = jnp.stack([pack, 2 * y + 1 - k, 2 * (1 - y) + k, 2 * (1 - y) + 1 - k])
    routes_f = ints[near][:, : routes_t.size].reshape((packs,) + routes_t.shape)
    order = lax.dynamic_index_in_dim(ints, 2 * y + xx, 0, keepdims=False)
    order = order[routes_t.size : places].reshape(ctx_size, 2)
    order = lax.dynamic_index_in_dim(order, sequence, 1, keepdims=False) - ctx_size * sequence
    ids = jnp.arange(ctx_size, dtype=jnp.int32)
    inv = jnp.sum(jnp.where(order[None, :] == ids[:, None], ids[None, :], 0), axis=1)

    gm_all = [None, lax.all_gather(cotangent[0], everyone, axis=0, tiled=False)]
    x = tokens[0].astype(f32)
    before = jnp.zeros((packs, ROUT, count), f32)
    kept, ext_all = [], [None] * LAYERS
    for l in range(LAYERS):
        n1s, qkv, o, lse, ob, hst, ub, w, wo = attn_forward(
            l, order, inv, x, smalls[l], qkv_weights, cosine, sine, out_weight, 2 * l
        )
        if l == 1:
            ub, gm_all[1] = lax.optimization_barrier((ub, gm_all[1]))
            hst, first_ext = lax.optimization_barrier((hst, ext_all[0]))
            ext_all[0] = lax.all_gather(first_ext, everyone, axis=0, tiled=False)
        ubf, table, ext, x_next = ffn_forward(
            l, ub, hst, smalls[l], routes_f[:, l], before, w_gate_up, w_down, 2 * l + 1
        )
        before = table
        ext_all[l] = ext if l == 0 else lax.all_gather(ext, everyone, axis=0, tiled=False)
        kept.append((x, n1s, qkv, o, lse, ob, hst, w, wo, ubf, table))
        x = x_next
    output = x
    gm = cotangent[0]
    gx = gm.astype(f32)
    gprev = jnp.zeros((16, count), f32)
    grads = [None] * LAYERS
    for l in reversed(range(LAYERS)):
        x, n1s, qkv, o, lse, ob, hst, w, wo, ubf, table = kept[l]
        number = 2 * LAYERS + 2 * l
        ghst, go, gwo, small, gprev = ffn_backward(
            l, gm, gx, ubf, table, hst, smalls[l], routes_t[l], gprev, wo, ob, w_gate_up, w_down, number
        )
        if l == 0:
            go, ext_all[0] = lax.optimization_barrier((go, ext_all[0]))
        gx, gm, grads[l] = attn_backward(
            order, inv, n1s, w, cosine, sine, qkv, o, lse, go, ghst, x, smalls[l], small, gwo, number + 1
        )
        if l > 0:
            gm_all[l - 1] = gm

    dense = jnp.stack(grads)
    dense, gm = lax.optimization_barrier((dense, gm_all[0]))
    gm_all[0] = lax.all_gather(gm, everyone, axis=0, tiled=False)

    def partner(values, distance):
        return lax.ppermute(values, "ctx", [(i, i ^ distance) for i in range(ctx_size)])

    def added(first, second):
        return (first.astype(f32) + second.astype(f32)).astype(bf)

    half = NF // 2
    numbers = expert_counts(ext_all[1])
    packed = pack_rows(numbers, ext_all[1], gm_all[1])
    dense, packed = lax.optimization_barrier((dense, packed))
    got = partner(dense, 1)
    done = weight_grads(1, 0, NF, numbers[2], packed, w_gate_up, w_down, ())
    done, got = lax.optimization_barrier((done, got))
    dense = added(dense, got)
    dense, ext, gm = lax.optimization_barrier((dense, ext_all[0], gm_all[0]))
    got = partner(dense, 4)
    numbers = expert_counts(ext)
    packed = pack_rows(numbers, ext, gm)
    done = weight_grads(0, 0, half, numbers[2], packed, w_gate_up, w_down, done)
    done, got = lax.optimization_barrier((done, got))
    dense = added(dense, got)
    dense, done = lax.optimization_barrier((dense, done))
    got = partner(dense, 2)
    done = weight_grads(0, half, NF, numbers[2], packed, w_gate_up, w_down, done)
    done, got = lax.optimization_barrier((done, got))
    qkv, out, gain_grad, router_grad, const_grad = assemble(dense, got, width)
    return (
        output[None],
        gx[None],
        gain_grad,
        qkv,
        out,
        router_grad,
        const_grad,
        done[0],
        done[1],
    )


def solution(mesh):
    placed = (
        P("fsdp", "ctx", None),
        P("fsdp", "ctx", None),
        P("fsdp", None),
        P("fsdp", None),
        P(None, "fsdp", "ctx", None),
        P(None, None, "fsdp"),
        P(None, None, "fsdp", None),
        P(None, "fsdp", None),
        P(None, "fsdp", None),
        P(None, None, "fsdp"),
        P(None, None, None, None, "fsdp"),
        P(None, None, "fsdp", None),
    )
    contexts, packs = mesh.shape["ctx"], mesh.shape["fsdp"]
    blocks_of_heads = HEADS // GROUP_HEADS

    def plan(*args):
        tokens = args[0]
        even = tokens.shape[1] * contexts == 2 * MINLEN
        grouped = contexts == 2 * blocks_of_heads and packs == blocks_of_heads
        return (by_heads if even and grouped else shards)(*args)

    return jax.shard_map(
        plan,
        mesh=mesh,
        in_specs=placed,
        out_specs=(
            P("fsdp", "ctx", None),
            P("fsdp", "ctx", None),
            P(None, None, "fsdp"),
            P(None, None, "fsdp", None),
            P(None, "fsdp", None),
            P(None, "fsdp", None),
            P(None, None, "fsdp"),
            P(None, None, None, None, "fsdp"),
            P(None, None, "fsdp", None),
        ),
        check_vma=False,
    )
```

```python
import functools

import jax
import jax.numpy as jnp
import numpy as np
from jax import lax
from jax.experimental import pallas as pl
from jax.experimental.pallas import tpu as pltpu
from jax.sharding import PartitionSpec as P

HEADS = 12
HEAD_DIM = 64
NF = 8
NC = 2
LAYERS = 2
NE = 12
MOST = 64
GROUP_HEADS = 3


def from_behind(x, axis, by):
    devices = lax.axis_size(axis)
    return lax.ppermute(x, axis, [(i, (i + by) % devices) for i in range(devices)])


def layout_tables(lengths, order_row, tok_count):
    block_len = tok_count // 2
    pack_len = order_row.shape[0] * block_len
    pack_rows = jnp.arange(pack_len, dtype=jnp.int32)
    owner = pack_rows // tok_count
    which_half = pack_rows % tok_count // block_len
    block_ids = order_row[2 * owner + which_half]
    pack_pos = block_ids * block_len + pack_rows % block_len
    segment = (pack_pos >= lengths[0]).astype(jnp.int32)
    seq_pos = pack_pos - segment * lengths[0]
    return (pack_pos, segment, seq_pos)


def angle_tables(seq_pos, head_size):
    half_size = head_size // 2
    frequency = jnp.exp(-jnp.log(10000.0) * jnp.arange(half_size, dtype=jnp.float32) / half_size)
    angles = seq_pos.astype(jnp.float32)[:, None] * frequency[None, :]
    return (jnp.cos(angles)[:, None, :], jnp.sin(angles)[:, None, :])


def rotate_pairs(values, cosine_table, sine_table, direction):
    half_size = values.shape[-1] // 2
    first_half = values[..., :half_size]
    second_half = values[..., half_size:]
    return jnp.concatenate(
        [
            first_half * cosine_table - direction * second_half * sine_table,
            second_half * cosine_table + direction * first_half * sine_table,
        ],
        axis=-1,
    )


def rms_parts(values):
    inverse = lax.rsqrt(jnp.mean(values * values, axis=-1, keepdims=True) + 1e-06)
    return (values * inverse, inverse)


def rms_back(grad_normed, base_values, inverse):
    return inverse * (
        grad_normed - base_values * jnp.mean(grad_normed * base_values, axis=-1, keepdims=True)
    )


def expert_forward(inputs_low, gate_up_use, down_use):
    gate_up_out = jnp.einsum(
        "emd,ecdf->ecmf", inputs_low, gate_up_use, preferred_element_type=jnp.float32
    )
    hidden_low = (jax.nn.silu(gate_up_out[:, 0]) * gate_up_out[:, 1]).astype(jnp.bfloat16)
    partial_value = jnp.einsum(
        "emf,efd->emd", hidden_low, down_use, preferred_element_type=jnp.float32
    )
    return (gate_up_out, hidden_low, partial_value)


def expert_backward(inputs_low, gate_up_out, hidden_low, grad_part_low, gate_up_use, down_use):
    grad_down = jnp.einsum(
        "emf,emd->efd", hidden_low, grad_part_low, preferred_element_type=jnp.float32
    )
    grad_hidden = jnp.einsum(
        "emd,efd->emf", grad_part_low, down_use, preferred_element_type=jnp.float32
    )
    gate_out = gate_up_out[:, 0]
    sigmoid_gate = jax.nn.sigmoid(gate_out)
    grad_pair_low = jnp.stack(
        [
            grad_hidden
            * gate_up_out[:, 1]
            * sigmoid_gate
            * (1.0 + gate_out * (1.0 - sigmoid_gate)),
            grad_hidden * gate_out * sigmoid_gate,
        ],
        axis=1,
    ).astype(jnp.bfloat16)
    grad_gate_up = jnp.einsum(
        "emd,ecmf->ecdf", inputs_low, grad_pair_low, preferred_element_type=jnp.float32
    )
    grad_rows = jnp.einsum(
        "ecmf,ecdf->emd", grad_pair_low, gate_up_use, preferred_element_type=jnp.float32
    )
    return (grad_gate_up, grad_down, grad_rows)


def shards(
    tokens,
    cotangent,
    seq_lengths,
    block_order,
    routes,
    gains,
    qkv_weights,
    out_weight,
    router,
    const_values,
    w_gate_up,
    w_down,
):
    tok_count = tokens.shape[1]
    width = tokens.shape[2]
    ctx_size = lax.axis_size("ctx")
    own_index = lax.axis_index("ctx")
    score_scale = HEAD_DIM ** (-0.5)
    pack_pos, segment, seq_pos = layout_tables(seq_lengths[0], block_order[0], tok_count)
    own_start = own_index * tok_count
    query_pos = lax.dynamic_slice_in_dim(pack_pos, own_start, tok_count)
    query_seg = lax.dynamic_slice_in_dim(segment, own_start, tok_count)
    cosine_table, sine_table = angle_tables(
        lax.dynamic_slice_in_dim(seq_pos, own_start, tok_count), HEAD_DIM
    )
    head_shape = (tok_count, HEADS, HEAD_DIM)
    expert_ids = jnp.arange(NE, dtype=jnp.int32)
    slot_ids = jnp.arange(MOST, dtype=jnp.int32)
    row_ids = jnp.arange(tok_count, dtype=jnp.int32)

    def allowed_pairs(key_offset, key_count):
        key_pos = lax.dynamic_slice_in_dim(pack_pos, key_offset, key_count)
        key_seg = lax.dynamic_slice_in_dim(segment, key_offset, key_count)
        return (query_seg[:, None] == key_seg[None, :]) & (key_pos[None, :] <= query_pos[:, None])

    stream = tokens[0].astype(jnp.float32)
    previous = jnp.zeros((tok_count, NE), jnp.float32)
    saved = []
    for layer_index in range(LAYERS):
        gain_all, qkv_all, out_all, router_all, const_all = (
            lax.all_gather(gains[layer_index], "fsdp", axis=1, tiled=True),
            lax.all_gather(qkv_weights[layer_index], "fsdp", axis=1, tiled=True),
            lax.all_gather(out_weight[layer_index], "fsdp", axis=0, tiled=True),
            lax.all_gather(router[layer_index], "fsdp", axis=0, tiled=True),
            lax.all_gather(const_values[layer_index], "fsdp", axis=1, tiled=True),
        )
        gain_float = gain_all.astype(jnp.float32)
        base_one, inverse_one = rms_parts(stream)
        normed_low = (base_one * gain_float[0]).astype(jnp.bfloat16)
        projected = jnp.einsum(
            "td,cde->cte", normed_low, qkv_all, preferred_element_type=jnp.float32
        )
        queries_low = rotate_pairs(
            projected[0].reshape(head_shape), cosine_table, sine_table, 1.0
        ).astype(jnp.bfloat16)
        keys_low = rotate_pairs(
            projected[1].reshape(head_shape), cosine_table, sine_table, 1.0
        ).astype(jnp.bfloat16)
        values_low = projected[2].reshape(head_shape).astype(jnp.bfloat16)

        def fold_step(running, shard_piece, offset, queries_use=queries_low):
            keys_piece, values_piece = shard_piece
            allowed = allowed_pairs(offset, keys_piece.shape[0])[None]
            scores = (
                jnp.einsum(
                    "qhd,khd->hqk", queries_use, keys_piece, preferred_element_type=jnp.float32
                )
                * score_scale
            )
            scores = jnp.where(allowed, scores, -1e30)
            top_old, total_old, accumulated = running
            top_new = jnp.maximum(top_old, jnp.max(scores, axis=-1))
            weights = jnp.where(allowed, jnp.exp(scores - top_new[..., None]), 0.0)
            factor = jnp.exp(top_old - top_new)
            accumulated = jnp.einsum(
                "hqk,khd->hqd",
                weights.astype(jnp.bfloat16),
                values_piece,
                preferred_element_type=jnp.float32,
            )
            return (top_new, jnp.sum(weights, axis=-1), accumulated)

        starting = (
            jnp.full((HEADS, tok_count), -1e30, jnp.float32),
            jnp.zeros((HEADS, tok_count), jnp.float32),
            jnp.zeros((HEADS, tok_count, HEAD_DIM), jnp.float32),
        )
        top_value, total_sum, accumulated = fold_step(
            starting,
            (
                lax.all_gather(keys_low, "ctx", axis=0, tiled=True),
                lax.all_gather(values_low, "ctx", axis=0, tiled=True),
            ),
            jnp.int32(0),
        )
        log_total = top_value + jnp.log(total_sum)
        attended = jnp.transpose(accumulated / total_sum[..., None], (1, 0, 2))
        mixed_low = attended.reshape(tok_count, width).astype(jnp.bfloat16)
        hidden_state = stream + jnp.dot(mixed_low, out_all, preferred_element_type=jnp.float32)
        base_two, inverse_two = rms_parts(hidden_state)
        expert_in = base_two * gain_float[1]
        expert_low = expert_in.astype(jnp.bfloat16)
        raw_logits = jnp.dot(expert_low, router_all, preferred_element_type=jnp.float32)
        logits = raw_logits[:, :NE] + previous
        route_ids = routes[layer_index, 0]
        chosen = route_ids[:, :, None] == expert_ids[None, None, :]
        chosen_f = chosen.astype(jnp.float32)
        hit_count = jnp.sum(chosen.astype(jnp.int32), axis=1)
        slot_index = jnp.cumsum(hit_count, axis=0) - 1
        picked = jnp.sum(chosen_f * logits[:, None, :], axis=-1)
        gate_weights = jax.nn.softmax(picked, axis=-1)
        coeffs = jnp.sum(gate_weights[:, :, None] * chosen_f, axis=1)
        slot_table = jnp.zeros((NF, MOST), jnp.int32)
        for expert in range(NF):
            target = jnp.where(hit_count[:, expert] > 0, slot_index[:, expert], MOST)
            slot_table = slot_table.at[expert, target].set(row_ids, mode="drop")
        filled = (slot_ids[None, :] < jnp.sum(hit_count[:, :NF], axis=0)[:, None]).astype(
            jnp.float32
        )
        rows_low = expert_low[slot_table]
        inputs_low = lax.all_gather(rows_low, "fsdp", axis=1, tiled=True)
        gate_up_out, hidden_low, partial_value = expert_forward(
            inputs_low, w_gate_up[layer_index], w_down[layer_index]
        )
        result = lax.psum_scatter(
            partial_value.astype(jnp.bfloat16), "fsdp", scatter_dimension=1, tiled=True
        ).astype(jnp.float32)
        flat_index = jnp.arange(NF, dtype=jnp.int32)[None, :] * MOST + jnp.clip(
            slot_index[:, :NF], 0, MOST - 1
        )
        token_result = result.reshape(NF * MOST, width)[flat_index]
        expert_mix = (
            jnp.sum(coeffs[:, :NF, None] * token_result, axis=1)
            + coeffs[:, NF + 1 : NF + 2] * expert_in
        )
        mixings = []
        for const_index in range(NC):
            column = NE + 2 * const_index
            mixing = jax.nn.softmax(raw_logits[:, column : column + 2], axis=-1)
            mixings.append(mixing)
            expert_mix = expert_mix + coeffs[:, NF + 2 + const_index : NF + 3 + const_index] * (
                mixing[:, 0:1] * expert_in
                + mixing[:, 1:2] * const_all[const_index].astype(jnp.float32)[None, :]
            )
        saved.append(
            (
                gain_float,
                qkv_all,
                out_all,
                router_all,
                const_all,
                base_one,
                inverse_one,
                normed_low,
                queries_low,
                keys_low,
                values_low,
                log_total,
                attended,
                mixed_low,
                base_two,
                inverse_two,
                expert_in,
                expert_low,
                chosen_f,
                hit_count,
                gate_weights,
                coeffs,
                slot_table,
                filled,
                inputs_low,
                gate_up_out,
                hidden_low,
                flat_index,
                token_result,
                mixings,
            )
        )
        stream = hidden_state + expert_mix
        previous = logits
    grad_stream = cotangent[0].astype(jnp.float32)
    grad_previous = jnp.zeros((tok_count, NE), jnp.float32)
    layer_grads = [None] * LAYERS
    for layer_index in reversed(range(LAYERS)):
        (
            gain_float,
            qkv_all,
            out_all,
            router_all,
            const_all,
            base_one,
            inverse_one,
            normed_low,
            queries_low,
            keys_low,
            values_low,
            log_total,
            attended,
            mixed_low,
            base_two,
            inverse_two,
            expert_in,
            expert_low,
            chosen_f,
            hit_count,
            gate_weights,
            coeffs,
            slot_table,
            filled,
            inputs_low,
            gate_up_out,
            hidden_low,
            flat_index,
            token_result,
            mixings,
        ) = saved[layer_index]
        grad_mix = grad_stream
        dot_input = jnp.sum(grad_mix * expert_in, axis=-1, keepdims=True)
        coef_grads = [
            jnp.sum(grad_mix[:, None, :] * token_result, axis=-1),
            jnp.zeros((tok_count, 1), jnp.float32),
            dot_input,
        ]
        grad_in = grad_mix * coeffs[:, NF + 1 : NF + 2]
        const_cols = []
        const_grads = []
        for const_index in range(NC):
            mixing = mixings[const_index]
            const_row = const_all[const_index].astype(jnp.float32)[None, :]
            dot_const = jnp.sum(grad_mix * const_row, axis=-1, keepdims=True)
            share = coeffs[:, NF + 2 + const_index : NF + 3 + const_index]
            coef_grads.append(mixing[:, 0:1] * dot_input + mixing[:, 1:2] * dot_const)
            grad_in = grad_in + grad_mix * (share * mixing[:, 0:1])
            grad_mixing = share * jnp.concatenate([dot_input, dot_const], axis=1)
            const_cols.append(
                mixing * (grad_mixing - jnp.sum(mixing * grad_mixing, axis=-1, keepdims=True))
            )
            const_grads.append(jnp.sum(grad_mix * (share * mixing[:, 1:2]), axis=0))
        grad_coeffs = jnp.concatenate(coef_grads, axis=1)
        grad_gates = jnp.sum(chosen_f * grad_coeffs[:, None, :], axis=-1)
        grad_picked = gate_weights * (
            grad_gates - jnp.sum(gate_weights * grad_gates, axis=-1, keepdims=True)
        )
        grad_logits = jnp.sum(grad_picked[:, :, None] * chosen_f, axis=1) + grad_previous
        grad_previous = grad_logits
        grad_raw_low = jnp.concatenate([grad_logits] + const_cols, axis=1).astype(jnp.bfloat16)
        grad_router = jnp.einsum(
            "td,tc->dc", expert_low, grad_raw_low, preferred_element_type=jnp.float32
        )
        grad_in = grad_in + jnp.einsum(
            "tc,dc->td", grad_raw_low, router_all, preferred_element_type=jnp.float32
        )
        slot_weight = (
            jnp.take_along_axis(jnp.transpose(coeffs[:, :NF]), slot_table, axis=1) * filled
        )
        grad_result_low = (grad_mix[slot_table] * slot_weight[:, :, None]).astype(jnp.bfloat16)
        grad_part_low = lax.all_gather(grad_result_low, "fsdp", axis=1, tiled=True)
        grad_gate_up, grad_down, grad_rows = expert_backward(
            inputs_low,
            gate_up_out,
            hidden_low,
            grad_part_low,
            w_gate_up[layer_index],
            w_down[layer_index],
        )
        grad_rows = lax.psum_scatter(
            grad_rows.astype(jnp.bfloat16), "fsdp", scatter_dimension=1, tiled=True
        ).astype(jnp.float32)
        token_grads = grad_rows.reshape(NF * MOST, width)[flat_index]
        grad_in = grad_in + jnp.sum(
            jnp.where(hit_count[:, :NF, None] > 0, token_grads, 0.0), axis=1
        )
        grad_gain_two = jnp.sum(grad_in * base_two, axis=0)
        grad_hidden_state = grad_stream + rms_back(grad_in * gain_float[1], base_two, inverse_two)
        grad_out_low = grad_hidden_state.astype(jnp.bfloat16)
        grad_out_w = jnp.einsum(
            "td,te->de", mixed_low, grad_out_low, preferred_element_type=jnp.float32
        )
        grad_attended = (
            jnp.einsum("te,de->td", grad_out_low, out_all, preferred_element_type=jnp.float32)
            .astype(jnp.bfloat16)
            .reshape(head_shape)
        )
        delta = jnp.transpose(jnp.sum(grad_attended.astype(jnp.float32) * attended, axis=-1))

        def visit(
            turn_index,
            carried,
            queries_use=queries_low,
            grad_use=grad_attended,
            log_use=log_total,
            delta_use=delta,
        ):
            keys_piece, values_piece, key_grads, value_grads, query_grads = carried
            source = (own_index - turn_index) % ctx_size
            allowed = allowed_pairs(source * tok_count, tok_count)[None]
            scores = (
                jnp.einsum(
                    "qhd,khd->hqk", queries_use, keys_piece, preferred_element_type=jnp.float32
                )
                * score_scale
            )
            probs = jnp.where(
                allowed, jnp.exp(jnp.where(allowed, scores, -1e30) - log_use[..., None]), 0.0
            )
            value_grads = value_grads + jnp.einsum(
                "hqk,qhd->khd",
                probs.astype(jnp.bfloat16),
                grad_use,
                preferred_element_type=jnp.float32,
            )
            prob_grads = jnp.einsum(
                "qhd,khd->hqk", grad_use, values_piece, preferred_element_type=jnp.float32
            )
            score_grads = (probs * (prob_grads - delta_use[..., None])).astype(jnp.bfloat16)
            query_grads = query_grads + jnp.einsum(
                "hqk,khd->qhd", score_grads, keys_piece, preferred_element_type=jnp.float32
            )
            key_grads = key_grads + jnp.einsum(
                "hqk,qhd->khd", score_grads, queries_use, preferred_element_type=jnp.float32
            )
            keys_piece, values_piece = from_behind((keys_piece, values_piece), "ctx", 1)
            key_grads, value_grads = (
                from_behind(key_grads.astype(jnp.bfloat16), "ctx", 1).astype(key_grads.dtype),
                from_behind(value_grads.astype(jnp.bfloat16), "ctx", 1).astype(value_grads.dtype),
            )
            return (keys_piece, values_piece, key_grads, value_grads, query_grads)

        zero_heads = jnp.zeros(head_shape, jnp.float32)
        finished = lax.fori_loop(
            0, ctx_size, visit, (keys_low, values_low, zero_heads, zero_heads, zero_heads)
        )
        grad_query = (
            rotate_pairs(finished[4] * score_scale, cosine_table, sine_table, -1.0)
            .astype(jnp.bfloat16)
            .reshape(tok_count, width)
        )
        grad_key = (
            rotate_pairs(finished[2] * score_scale, cosine_table, sine_table, -1.0)
            .astype(jnp.bfloat16)
            .reshape(tok_count, width)
        )
        grad_value = finished[3].astype(jnp.bfloat16).reshape(tok_count, width)
        grad_proj_low = jnp.stack([grad_query, grad_key, grad_value], axis=0)
        grad_qkv = jnp.einsum(
            "td,cte->cde", normed_low, grad_proj_low, preferred_element_type=jnp.float32
        )
        grad_normed = jnp.einsum(
            "cte,cde->td", grad_proj_low, qkv_all, preferred_element_type=jnp.float32
        )
        grad_gain_one = jnp.sum(grad_normed * base_one, axis=0)
        grad_stream = grad_hidden_state + rms_back(
            grad_normed * gain_float[0], base_one, inverse_one
        )
        gains_shard, qkv_shard, out_shard, router_shard, const_shard = (
            lax.psum_scatter(
                jnp.stack([grad_gain_one, grad_gain_two]).astype(jnp.bfloat16),
                "fsdp",
                scatter_dimension=1,
                tiled=True,
            ).astype(jnp.float32),
            lax.psum_scatter(
                grad_qkv.astype(jnp.bfloat16), "fsdp", scatter_dimension=1, tiled=True
            ).astype(jnp.float32),
            lax.psum_scatter(
                grad_out_w.astype(jnp.bfloat16), "fsdp", scatter_dimension=0, tiled=True
            ).astype(jnp.float32),
            lax.psum_scatter(
                grad_router.astype(jnp.bfloat16), "fsdp", scatter_dimension=0, tiled=True
            ).astype(jnp.float32),
            lax.psum_scatter(
                jnp.stack(const_grads).astype(jnp.bfloat16), "fsdp", scatter_dimension=1, tiled=True
            ).astype(jnp.float32),
        )
        layer_grads[layer_index] = (
            lax.psum(gains_shard.astype(jnp.bfloat16), "ctx").astype(jnp.float32),
            lax.psum(qkv_shard.astype(jnp.bfloat16), "ctx").astype(jnp.float32),
            lax.psum(out_shard.astype(jnp.bfloat16), "ctx").astype(jnp.float32),
            lax.psum(router_shard.astype(jnp.bfloat16), "ctx").astype(jnp.float32),
            lax.psum(const_shard.astype(jnp.bfloat16), "ctx").astype(jnp.float32),
            lax.psum(grad_gate_up.astype(jnp.bfloat16), "ctx").astype(jnp.float32),
            lax.psum(grad_down.astype(jnp.bfloat16), "ctx").astype(jnp.float32),
        )
    stacked = [
        jnp.stack([layer_grads[layer_index][member_index] for layer_index in range(LAYERS)])
        for member_index in range(7)
    ]
    return (
        stream[None],
        grad_stream[None],
        stacked[0],
        stacked[1],
        stacked[2],
        stacked[3],
        stacked[4],
        stacked[5],
        stacked[6],
    )


MINLEN = 1024
ROUT = 56
RAW, COEF, SLOT, LOGI = 0, 16, 32, 40
VMEM_MB = 60
BRIEF = pl.CostEstimate(flops=1, bytes_accessed=1, transcendentals=0)


def nt(a, b):
    return lax.dot_general(a, b, (((1,), (1,)), ((), ())), preferred_element_type=jnp.float32)


def nn(a, b):
    return lax.dot_general(a, b, (((1,), (0,)), ((), ())), preferred_element_type=jnp.float32)


def tn(a, b):
    return lax.dot_general(a, b, (((0,), (0,)), ((), ())), preferred_element_type=jnp.float32)


def params_of(mb=VMEM_MB, **more):
    return pltpu.CompilerParams(vmem_limit_bytes=mb * 2**20, **more)


def shape_of(dims, kind):
    return jax.ShapeDtypeStruct(dims, kind)


def rms_factor(values):
    return lax.rsqrt(jnp.mean(values * values, axis=-1, keepdims=True) + 1e-06)


def to_rows(columns, count):
    lane = lax.broadcasted_iota(jnp.int32, (columns[0].shape[0], 128), 1)
    packed = jnp.zeros(lane.shape, jnp.float32)
    for index, column in enumerate(columns):
        packed = jnp.where(lane == index, column, packed)
    return jnp.transpose(packed)[:count]


def to_columns(rows):
    count = rows[0].shape[1]
    sub = lax.broadcasted_iota(jnp.int32, (128, count), 0)
    packed = jnp.zeros(sub.shape, jnp.float32)
    for index, row in enumerate(rows):
        packed = jnp.where(sub == index, row, packed)
    packed = jnp.transpose(packed)
    return [packed[:, index : index + 1] for index in range(len(rows))]


def swap_halves(values):
    lanes = values.shape[1]
    lane = lax.broadcasted_iota(jnp.int32, values.shape, 1)
    ahead = pltpu.roll(values, lanes - 32, 1)
    behind = pltpu.roll(values, 32, 1)
    return jnp.where(lane % 64 < 32, ahead, behind)


def spin(values, cosine, sine):
    return values * cosine + swap_halves(values) * sine


def place():
    own, pack = lax.axis_index("ctx"), lax.axis_index("fsdp")
    return own // 2, own % 2, pack // 2, pack % 2


def remote(src, dst, send, recv, ctx, fsdp):
    return pltpu.make_async_remote_copy(
        src_ref=src,
        dst_ref=dst,
        send_sem=send,
        recv_sem=recv,
        device_id=(ctx, fsdp),
        device_id_type=pl.DeviceIdType.MESH,
    )


def greet_plane(contexts, across=False):
    own = lax.axis_index("ctx")
    _, _, y, k = place()
    barrier = pltpu.get_barrier_semaphore()
    if across:
        for core in (k, 1 - k):
            device = (own, 2 * (1 - y) + core)
            pl.semaphore_signal(barrier, inc=1, device_id=device, device_id_type=pl.DeviceIdType.MESH)
    for ctx in range(contexts):
        for core in range(2):

            @pl.when(jnp.logical_or(ctx != own, core != k))
            def _():
                pl.semaphore_signal(barrier, inc=1, device_id=(ctx, 2 * y + core), device_id_type=pl.DeviceIdType.MESH)

    return barrier, 2 * contexts - 1 + (2 if across else 0)


def greet_packs():
    own = lax.axis_index("ctx")
    _, _, y, k = place()
    barrier = pltpu.get_barrier_semaphore()
    for fsdp in (2 * y + 1 - k, 2 * (1 - y) + k, 2 * (1 - y) + 1 - k):
        pl.semaphore_signal(barrier, inc=1, device_id=(own, fsdp), device_id_type=pl.DeviceIdType.MESH)
    return barrier, 3


def attn_fwd_kernel(
    order, inv, x, small, wq, cosine, sine, wo_own,
    n1s_h, qkv_h, o, lse, ob, hst, ub, w_h, wo_h,
    n1own, n1r, osort, osend, orecv, cols, w_s, wo_s, n1s, qkv,
    n_send, n_recv, f_send, f_recv, o_send, o_recv, w_send, w_recv, v_send, v_recv, early,
):
    blocks, blk, _ = n1r.shape
    lanes = o.shape[1]
    seq = blocks * blk
    step = 2 * blk
    own = lax.axis_index("ctx")
    z, xx, y, k = place()
    depth = blocks // 2
    same = xx == k
    pack = lax.axis_index("fsdp")
    inner = wo_own.shape[1]
    beside, over, corner = 2 * y + 1 - k, 2 * (1 - y) + k, 2 * (1 - y) + 1 - k

    barrier, others = greet_plane(blocks, across=True)
    n1 = norm_low(x[...], small[0:1, :].astype(jnp.float32))
    n1own[0] = n1[:blk]
    n1own[1] = n1[blk:]
    pl.semaphore_wait(barrier, others)

    def n1_copy(zz):
        return remote(n1own.at[zz // 2], n1r.at[own], n_send.at[zz], n_recv.at[z], 2 * zz + k, 2 * y + xx)

    for zz in range(depth):
        alone = jnp.logical_and(same, zz == z)

        @pl.when(jnp.logical_not(alone))
        def _():
            n1_copy(zz).start()

        @pl.when(alone)
        def _():
            n1r[own] = n1own[zz // 2]

    for half in range(2):

        @pl.when(z % 2 == half)
        def _():
            for core in range(2):
                first = (2 * half + core) * inner
                for c in range(3):
                    cols[core, :, c * lanes : c * lanes + inner] = wq[0, c, :, first : first + inner]
                    cols[core, :, c * lanes + inner : (c + 1) * lanes] = jnp.zeros((inner, lanes - inner), jnp.bfloat16)

    def rows_of(device):
        return pl.ds(pl.multiple_of(device * inner, inner), inner)

    def w_copy(index):
        device, core = ((beside, 1 - k), (over, k), (corner, 1 - k))[index]
        return remote(cols.at[core], w_s.at[rows_of(pack), :], w_send.at[index], w_recv.at[index], own, device)

    def w_wait(index):
        rows = w_s.at[rows_of((beside, over, corner)[index]), :]
        remote(cols.at[0], rows, w_send.at[index], w_recv.at[index], own, beside).wait_recv()

    w_s[rows_of(pack), :] = cols[k]
    wo_s[pack] = wo_own[0]
    for index in (1, 2, 0):
        w_copy(index).start()
    v_far = remote(wo_s.at[pack], wo_s.at[pack], v_send.at[0], v_recv.at[0], own, over)
    v_near = remote(wo_s.at[pack], wo_s.at[pack], v_send.at[1], v_recv.at[1], own, beside)
    v_on = remote(wo_s.at[over], wo_s.at[over], v_send.at[2], v_recv.at[2], own, beside)
    v_far.start()
    v_near.start()

    def forward_copy(zz):
        slot = n1r.at[2 * zz + k]
        return remote(slot, slot, f_send.at[zz], f_recv.at[zz], own, 2 * y + 1 - k)

    for zz in range(depth):

        @pl.when(jnp.logical_not(jnp.logical_and(same, zz == z)))
        def _():
            remote(n1own.at[0], n1r.at[2 * zz + k], n_send.at[zz], n_recv.at[zz], 2 * zz + k, 2 * y + xx).wait_recv()

        forward_copy(zz).start()
    for zz in range(depth):
        slot = n1r.at[2 * zz + 1 - k]
        remote(slot, slot, f_send.at[zz], f_recv.at[zz], own, 2 * y + 1 - k).wait_recv()

    for index in range(3):
        w_wait(index)
    stores = [
        pltpu.make_async_copy(source, target, early.at[index])
        for index, (source, target) in enumerate(((w_s, w_h), (n1s, n1s_h), (qkv, qkv_h), (wo_s, wo_h)))
    ]
    stores[0].start()
    for b in range(blocks):
        n1s[b * blk : (b + 1) * blk, :] = n1r[inv[b]]
    stores[1].start()
    for i in range(seq // step):
        part = slice(i * step, (i + 1) * step)
        out = nn(n1s[part, :], w_s[...])
        cos2 = jnp.concatenate([cosine[part, :]] * (lanes // 128), axis=1)
        sin2 = jnp.concatenate([sine[part, :]] * (lanes // 128), axis=1)
        q = spin(out[:, :lanes], cos2, sin2).astype(jnp.bfloat16)
        qkv[part, :lanes] = q * jnp.asarray(HEAD_DIM**-0.5, jnp.bfloat16)
        qkv[part, lanes : 2 * lanes] = spin(out[:, lanes : 2 * lanes], cos2, sin2).astype(jnp.bfloat16)
        qkv[part, 2 * lanes :] = out[:, 2 * lanes :].astype(jnp.bfloat16)
    stores[2].start()
    lane = lax.broadcasted_iota(jnp.int32, (step, 128), 1)
    for i in range(seq // step):
        part = slice(i * step, (i + 1) * step)
        span = (i + 1) * step
        seen = lax.broadcasted_iota(jnp.int32, (step, span), 1) <= (
            lax.broadcasted_iota(jnp.int32, (step, span), 0) + i * step
        )
        logs = jnp.zeros((step, 128), jnp.float32)
        for head in range(GROUP_HEADS):
            tile, side = head // 2, head % 2
            at = tile * 128
            mine = lane // 64 == side
            q = jnp.where(mine, qkv[part, at : at + 128], jnp.asarray(0, jnp.bfloat16))
            s = nt(q, qkv[:span, lanes + at : lanes + at + 128])
            s = jnp.where(seen, s, -1e30)
            top = jnp.max(s, axis=1, keepdims=True)
            p = jnp.exp(s - top)
            total = jnp.sum(p, axis=1, keepdims=True)
            out = nn(p.astype(jnp.bfloat16), qkv[:span, 2 * lanes + at : 2 * lanes + at + 128]) / total
            logs = jnp.where(lane == head, top + jnp.log(total), logs)
            if side == 0:
                kept = jnp.where(mine, out, 0.0)
            else:
                kept = jnp.where(mine, out, kept)
            o[part, at : at + 128] = kept
        lse[part, :] = logs
        osort[2 * i] = o[part, :][:blk].astype(jnp.bfloat16)
        osort[2 * i + 1] = o[part, :][blk:].astype(jnp.bfloat16)

    mine_at = 2 * z + k
    remote(wo_s.at[over], wo_s.at[over], v_send.at[0], v_recv.at[0], own, over).wait_recv()
    v_on.start()

    def o_copy(ctx):
        return remote(osend.at[ctx], orecv.at[mine_at], o_send.at[ctx], o_recv.at[mine_at], ctx, 2 * y + xx)

    for ctx in range(blocks):
        alone = jnp.logical_and(same, ctx == own)
        osend[ctx] = osort[order[ctx]]

        @pl.when(jnp.logical_not(alone))
        def _():
            o_copy(ctx).start()

        @pl.when(alone)
        def _():
            orecv[mine_at] = osend[ctx]

    for src in range(blocks):

        @pl.when(jnp.logical_not(jnp.logical_and(same, src == mine_at)))
        def _():
            remote(osend.at[0], orecv.at[src], o_send.at[0], o_recv.at[src], 2 * (src // 2) + k, 2 * y + src % 2).wait_recv()

    ob[...] = orecv[...]
    remote(wo_s.at[beside], wo_s.at[beside], v_send.at[1], v_recv.at[1], own, beside).wait_recv()
    remote(wo_s.at[corner], wo_s.at[corner], v_send.at[2], v_recv.at[2], own, beside).wait_recv()
    stores[3].start()
    total, low = post_attention(orecv[...], x[...], wo_s[...], small[1:2, :].astype(jnp.float32))
    hst[...] = total
    ub[...] = low
    for zz in range(depth):

        @pl.when(jnp.logical_not(jnp.logical_and(same, zz == z)))
        def _():
            n1_copy(zz).wait_send()

        forward_copy(zz).wait_send()
    for index in range(3):
        w_copy(index).wait_send()
    v_far.wait_send()
    v_near.wait_send()
    v_on.wait_send()
    for store in stores:
        store.wait()
    for ctx in range(blocks):

        @pl.when(jnp.logical_not(jnp.logical_and(same, ctx == own)))
        def _():
            o_copy(ctx).wait_send()


def attn_forward(layer, order, inv, x, small, wq, cosine, sine, wo, number):
    count, width = x.shape
    blocks, blk = order.shape[0], count // 2
    packs, inner = width // wo.shape[1], wo.shape[1]
    lanes = -(-inner // 128) * 128
    seq = blocks * blk
    hm = pl.BlockSpec(memory_space=pl.ANY)
    vm = pl.BlockSpec(memory_space=pltpu.VMEM)
    sm = pl.BlockSpec(memory_space=pltpu.SMEM)
    bf = jnp.bfloat16
    dma = pltpu.SemaphoreType.DMA
    return pl.pallas_call(
        attn_fwd_kernel,
        grid=(1,),
        out_shape=[
            shape_of((seq, width), bf),
            shape_of((seq, 3 * lanes), bf),
            shape_of((seq, lanes), jnp.float32),
            shape_of((seq, 128), jnp.float32),
            shape_of((blocks, blk, lanes), bf),
            shape_of((count, width), jnp.float32),
            shape_of((count, width), bf),
            shape_of((width, 3 * lanes), bf),
            shape_of((packs, inner, width), bf),
        ],
        in_specs=[sm, sm, vm, vm]
        + [pl.BlockSpec((1, 3, inner, width), lambda _: (layer, 0, 0, 0)), vm, vm]
        + [pl.BlockSpec((1, inner, width), lambda _: (layer, 0, 0))],
        out_specs=[hm, hm] + [vm] * 5 + [hm, hm],
        scratch_shapes=[
            pltpu.VMEM((2, blk, width), bf),
            pltpu.VMEM((blocks, blk, width), bf),
            pltpu.VMEM((blocks, blk, lanes), bf),
            pltpu.VMEM((blocks, blk, lanes), bf),
            pltpu.VMEM((blocks, blk, lanes), bf),
            pltpu.VMEM((2, inner, 3 * lanes), bf),
            pltpu.VMEM((width, 3 * lanes), bf),
            pltpu.VMEM((packs, inner, width), bf),
            pltpu.VMEM((seq, width), bf),
            pltpu.VMEM((seq, 3 * lanes), bf),
        ]
        + [dma((blocks // 2,))] * 4
        + [dma((blocks,))] * 2
        + [dma((3,))] * 4
        + [dma((4,))],
        compiler_params=params_of(collective_id=number, has_side_effects=True),
        cost_estimate=BRIEF,
        name="attn_fwd",
    )(order, inv, x, small, wq, cosine, sine, wo)


def attn_bwd_kernel(
    order, inv, n1s_h, w_h, cosine_h, sine_h, qkv, o_h, lse, go, ghst, x, small, gsmall, gwo,
    gx, gm, dense,
    gor, gos, grads, acc, gns, sib_out, sib_in, gn_out, gnr, gw, gw_in, both, both_in, wo_in, wo_both, wo_over, probs, n1s, w, cosine, sine, o,
    o_send, o_recv, s_send, s_recv, g_send, g_recv, r_send, r_recv, w_send, w_recv, late,
):
    blocks, blk, width = grads.shape
    lanes = o.shape[1]
    seq = blocks * blk
    step = 2 * blk
    zero = jnp.asarray(0, jnp.bfloat16)
    own = lax.axis_index("ctx")
    z, xx, y, k = place()
    depth = blocks // 2
    same = xx == k

    loads = [
        pltpu.make_async_copy(source, target, late.at[index])
        for index, (source, target) in enumerate(
            ((o_h, o), (n1s_h, n1s), (w_h, w), (cosine_h, cosine), (sine_h, sine))
        )
    ]
    for load in loads:
        load.start()
    barrier, others = greet_plane(blocks, across=True)
    acc[...] = jnp.zeros_like(acc)
    pl.semaphore_wait(barrier, others)

    def go_copy(unit):
        return remote(go.at[unit], gor.at[own], o_send.at[unit], o_recv.at[own], 2 * (unit // 2) + k, 2 * y + unit % 2)

    for unit in range(blocks):
        alone = jnp.logical_and(same, unit == 2 * z + k)

        @pl.when(jnp.logical_not(alone))
        def _():
            go_copy(unit).start()

        @pl.when(alone)
        def _():
            gor[own] = go[unit]

    def wo_copy(half):
        return remote(
            gwo.at[2 * half + 1 - k], wo_in.at[half], w_send.at[half], w_recv.at[half], own, 2 * y + 1 - k
        )

    wo_far = remote(wo_both.at[1 - y], wo_over, w_send.at[2], w_recv.at[2], own, 2 * (1 - y) + k)
    wo_copy(0).start()
    wo_copy(1).start()
    lane = lax.broadcasted_iota(jnp.int32, (step, 128), 1)
    for i in range(seq // step):
        part = slice(i * step, (i + 1) * step)
        span = (i + 1) * step
        seen = lax.broadcasted_iota(jnp.int32, (step, span), 1) <= (
            lax.broadcasted_iota(jnp.int32, (step, span), 0) + i * step
        )
        for head in range(GROUP_HEADS):
            at = head // 2 * 128
            q = jnp.where(lane // 64 == head % 2, qkv[part, at : at + 128], zero)
            s = nt(q, qkv[:span, lanes + at : lanes + at + 128])
            p = jnp.exp(jnp.where(seen, s, -1e30) - lse[part, head : head + 1])
            probs[head, part, :span] = jnp.where(seen, p, 0.0)
    for ctx in range(blocks):

        @pl.when(jnp.logical_not(jnp.logical_and(same, ctx == own)))
        def _():
            remote(go.at[0], gor.at[ctx], o_send.at[0], o_recv.at[ctx], ctx, 2 * y + xx).wait_recv()

    for load in loads:
        load.wait()
    for half in range(2):
        wo_copy(half).wait_recv()
        total = gwo[2 * half + k].astype(jnp.float32) + wo_in[half].astype(jnp.float32)
        wo_both[half] = total.astype(jnp.bfloat16)
    wo_far.start()
    for b in range(blocks):
        gos[b * blk : (b + 1) * blk, :] = gor[inv[b]]
    for i in range(seq // step):
        part = slice(i * step, (i + 1) * step)
        span = (i + 1) * step
        key_lane = lax.broadcasted_iota(jnp.int32, (span, 128), 1)
        for head in range(GROUP_HEADS):
            tile, side = head // 2, head % 2
            at = tile * 128
            mine = lane // 64 == side
            q = jnp.where(mine, qkv[part, at : at + 128], zero)
            g = jnp.where(mine, gos[part, at : at + 128], zero)
            keys = qkv[:span, lanes + at : lanes + at + 128]
            values = qkv[:span, 2 * lanes + at : 2 * lanes + at + 128]
            delta = jnp.sum(g.astype(jnp.float32) * o[part, at : at + 128], axis=1, keepdims=True)
            p = probs[head, part, :span]
            ds = (p * (nt(g, values) - delta)).astype(jnp.bfloat16)
            acc[:span, 2 * lanes + at : 2 * lanes + at + 128] += tn(p.astype(jnp.bfloat16), g)
            acc[:span, lanes + at : lanes + at + 128] += tn(ds, q)
            acc[part, at : at + 128] += nn(ds, jnp.where(key_lane // 64 == side, keys, zero))
    for b in range(blocks):
        part = slice(b * blk, (b + 1) * blk)
        cos2 = jnp.concatenate([cosine[part, :]] * (lanes // 128), axis=1)
        sin2 = jnp.concatenate([sine[part, :]] * (lanes // 128), axis=1)
        grads[b, :, :lanes] = spin(acc[part, :lanes] * HEAD_DIM**-0.5, cos2, -sin2).astype(jnp.bfloat16)
        grads[b, :, lanes : 2 * lanes] = spin(acc[part, lanes : 2 * lanes], cos2, -sin2).astype(jnp.bfloat16)
        grads[b, :, 2 * lanes :] = acc[part, 2 * lanes :].astype(jnp.bfloat16)

    def sib_copy(zz):
        return remote(sib_out.at[zz], sib_in.at[zz], s_send.at[zz], s_recv.at[zz], own, 2 * y + 1 - k)

    def gn_copy(zz):
        return remote(gn_out.at[zz], gnr.at[z], g_send.at[zz], g_recv.at[z], 2 * zz + k, 2 * y + xx)

    gain = small[0:1, :].astype(jnp.float32)
    ggain = jnp.zeros((1, width), jnp.float32)
    for b in range(blocks):
        gns[b] = nt(grads[b], w[...])
        ggain = ggain + jnp.sum(gns[b] * n1s[b * blk : (b + 1) * blk, :].astype(jnp.float32), axis=0, keepdims=True)
    for zz in range(depth):
        sib_out[zz] = gns[order[2 * zz + 1 - k]].astype(jnp.bfloat16)
        sib_copy(zz).start()
    for zz in range(depth):
        sib_copy(zz).wait_recv()
        alone = jnp.logical_and(same, zz == z)
        gn_out[zz] = (gns[order[2 * zz + k]] + sib_in[zz].astype(jnp.float32)).astype(jnp.bfloat16)

        @pl.when(jnp.logical_not(alone))
        def _():
            gn_copy(zz).start()

        @pl.when(alone)
        def _():
            gnr[z] = gn_out[zz]

    packs, inner = gwo.shape[0], gwo.shape[1]
    sums = jnp.concatenate([ggain / gain, gsmall[...]], axis=0)
    sums = jnp.concatenate([sums, jnp.zeros((128 - sums.shape[0], width), jnp.float32)], axis=0)
    gw[:, :128] = jnp.transpose(sums).astype(jnp.bfloat16)
    gw[:, 128 + 3 * inner :] = jnp.zeros((width, gw.shape[1] - 128 - 3 * inner), jnp.bfloat16)
    for i in range(width // 256):
        part = slice(i * 256, (i + 1) * 256)
        piece = tn(n1s[:, part], grads[...].reshape(seq, 3 * lanes)).astype(jnp.bfloat16)
        for c in range(3):
            gw[part, 128 + c * inner : 128 + (c + 1) * inner] = piece[:, c * lanes : c * lanes + inner]

    def rows_of(f):
        return pl.ds(pl.multiple_of(f * inner, inner), inner)

    def home_copy(half):
        rows = gw.at[rows_of(2 * half + 1 - k), :]
        return remote(rows, gw_in.at[half], r_send.at[half], r_recv.at[half], own, 2 * y + 1 - k)

    for half in range(2):
        home_copy(half).start()
    for half in range(2):
        home_copy(half).wait_recv()
        kept, came = gw[rows_of(2 * half + k), :], gw_in[half]
        both[half, :, :128] = (kept[:, :128].astype(jnp.float32) + came[:, :128].astype(jnp.float32)).astype(jnp.bfloat16)
        heads = slice(128, 128 + 3 * inner)
        for core in range(2):

            @pl.when(k == core)
            def _():
                both[half, :, 128 + core * 3 * inner : 128 + (core + 1) * 3 * inner] = kept[:, heads]
                both[half, :, 128 + (1 - core) * 3 * inner : 128 + (2 - core) * 3 * inner] = came[:, heads]

    over = remote(both.at[1 - y], both_in, r_send.at[2], r_recv.at[2], own, 2 * (1 - y) + k)
    over.start()
    values = x[...]
    factor = rms_factor(values)
    base = values * factor
    for zz in range(depth):

        @pl.when(jnp.logical_not(jnp.logical_and(same, zz == z)))
        def _():
            remote(gn_out.at[0], gnr.at[zz], g_send.at[0], g_recv.at[zz], 2 * zz + k, 2 * y + xx).wait_recv()

    halves = []
    for h in range(2):
        total = gnr[h * (depth // 2)].astype(jnp.float32)
        for zz in range(1, depth // 2):
            total = total + gnr[h * (depth // 2) + zz].astype(jnp.float32)
        halves.append(total)
    gn = jnp.concatenate(halves, axis=0)
    gb = gn * gain
    grad = ghst[...] + factor * (gb - base * jnp.mean(gb * base, axis=-1, keepdims=True))
    gx[...] = grad
    gm[...] = grad.astype(jnp.bfloat16)
    wo_far.wait_recv()
    edge = both.shape[2]
    dense[:, edge:] = (wo_both[y].astype(jnp.float32) + wo_over[...].astype(jnp.float32)).astype(jnp.bfloat16)
    over.wait_recv()
    dense[:, :edge] = (both[y].astype(jnp.float32) + both_in[...].astype(jnp.float32)).astype(jnp.bfloat16)
    for half in range(2):
        home_copy(half).wait_send()
        wo_copy(half).wait_send()
    wo_far.wait_send()
    over.wait_send()
    for unit in range(blocks):

        @pl.when(jnp.logical_not(jnp.logical_and(same, unit == 2 * z + k)))
        def _():
            go_copy(unit).wait_send()

    for zz in range(depth):
        sib_copy(zz).wait_send()

        @pl.when(jnp.logical_not(jnp.logical_and(same, zz == z)))
        def _():
            gn_copy(zz).wait_send()


def attn_backward(order, inv, n1s, w, cosine, sine, qkv, o, lse, go, ghst, x, small, gsmall, gwo, number):
    blocks, blk, lanes = go.shape
    seq, width = n1s.shape
    count = x.shape[0]
    packs, inner = gwo.shape[0], gwo.shape[1]
    depth = blocks // 2
    hm = pl.BlockSpec(memory_space=pl.ANY)
    vm = pl.BlockSpec(memory_space=pltpu.VMEM)
    sm = pl.BlockSpec(memory_space=pltpu.SMEM)
    bf = jnp.bfloat16
    dma = pltpu.SemaphoreType.DMA
    return pl.pallas_call(
        attn_bwd_kernel,
        out_shape=[
            shape_of((count, width), jnp.float32),
            shape_of((count, width), bf),
            shape_of((inner, 128 + 6 * inner + width), bf),
        ],
        in_specs=[sm] * 2 + [hm] * 4 + [vm, hm] + [vm] * 7,
        out_specs=[vm] * 3,
        scratch_shapes=[
            pltpu.VMEM((blocks, blk, lanes), bf),
            pltpu.VMEM((seq, lanes), bf),
            pltpu.VMEM((blocks, blk, 3 * lanes), bf),
            pltpu.VMEM((seq, 3 * lanes), jnp.float32),
            pltpu.VMEM((blocks, blk, width), jnp.float32),
            pltpu.VMEM((depth, blk, width), bf),
            pltpu.VMEM((depth, blk, width), bf),
            pltpu.VMEM((depth, blk, width), bf),
            pltpu.VMEM((depth, blk, width), bf),
            pltpu.VMEM((packs * inner, 3 * lanes), bf),
            pltpu.VMEM((2, inner, 3 * lanes), bf),
            pltpu.VMEM((2, inner, 128 + 6 * inner), bf),
            pltpu.VMEM((inner, 128 + 6 * inner), bf),
            pltpu.VMEM((2, inner, width), bf),
            pltpu.VMEM((2, inner, width), bf),
            pltpu.VMEM((inner, width), bf),
            pltpu.VMEM((GROUP_HEADS, seq, seq), jnp.float32),
            pltpu.VMEM(n1s.shape, bf),
            pltpu.VMEM(w.shape, bf),
            pltpu.VMEM(cosine.shape, jnp.float32),
            pltpu.VMEM(sine.shape, jnp.float32),
            pltpu.VMEM(o.shape, jnp.float32),
        ]
        + [dma((blocks,))] * 2
        + [dma((depth,))] * 4
        + [dma((3,))] * 4
        + [dma((5,))],
        compiler_params=params_of(collective_id=number, has_side_effects=True),
        cost_estimate=BRIEF,
        name="attn_bwd",
    )(order, inv, n1s, w, cosine, sine, qkv, o, lse, go, ghst, x, small, gsmall, gwo)


def routing(raw, before, routes):
    count = raw.shape[1]
    ids = lax.broadcasted_iota(jnp.int32, (16, count), 0)
    logits = raw + before
    first, second = ids == routes[0:1], ids == routes[1:2]
    z0 = jnp.sum(jnp.where(first, logits, 0.0), axis=0, keepdims=True)
    z1 = jnp.sum(jnp.where(second, logits, 0.0), axis=0, keepdims=True)
    top = jnp.maximum(z0, z1)
    e0, e1 = jnp.exp(z0 - top), jnp.exp(z1 - top)
    total = e0 + e1
    coef = jnp.where(first, e0 / total, 0.0) + jnp.where(second, e1 / total, 0.0)
    hits = jnp.where(first | second, 1.0, 0.0)
    upto = lax.broadcasted_iota(jnp.int32, (count, count), 0) <= lax.broadcasted_iota(jnp.int32, (count, count), 1)
    place = nn(hits.astype(jnp.bfloat16), jnp.where(upto, 1.0, 0.0).astype(jnp.bfloat16)) - 1.0
    slot = jnp.where(hits > 0, place, -1.0)
    return jnp.concatenate([raw, coef, slot[:NF], logits], axis=0)


def one_hot(slot):
    count = slot.shape[1]
    ids = lax.broadcasted_iota(jnp.int32, (NF, MOST, count), 1)
    hit = ids == slot.astype(jnp.int32)[:, None, :]
    return jnp.where(hit, 1.0, 0.0).reshape(NF * MOST, count)


def slot_values(hot, rows):
    count = rows.shape[1]
    wide = jnp.broadcast_to(rows[:, None, :], (NF, MOST, count)).reshape(NF * MOST, count)
    return jnp.sum(hot * wide, axis=1, keepdims=True)


def swap_rows(own, rows, send, recv, forward_send, forward_recv):
    ctx = lax.axis_index("ctx")
    _, _, y, k = place()
    beside, across = 2 * y + 1 - k, 2 * (1 - y) + k
    far = remote(own, rows.at[2], send.at[0], recv.at[0], ctx, across)
    near = remote(own, rows.at[1], send.at[1], recv.at[1], ctx, beside)
    onward = remote(rows.at[2], rows.at[3], forward_send, forward_recv, ctx, beside)
    far.start()
    near.start()
    return near, far, onward


def sum_rows(parts, beside_in, mid, across_in, send, recv):
    ctx = lax.axis_index("ctx")
    _, _, y, k = place()
    beside, across = 2 * y + 1 - k, 2 * (1 - y) + k
    first = remote(parts.at[3], beside_in.at[1], send.at[0], recv.at[0], ctx, beside)
    second = remote(parts.at[1], beside_in.at[0], send.at[1], recv.at[1], ctx, beside)
    third = remote(mid, across_in, send.at[2], recv.at[2], ctx, across)
    return first, second, third


def ffn_fwd_kernel(
    ub, hst, small, routes, before, wgu, wd,
    ubf, table, ext, x_next,
    rows_s, hot_s, x_s, y_s, coef_s, parts, beside_in, mid, across_in,
    a_send, a_recv, r_send, r_recv,
):
    e = pl.program_id(0)
    packs = ubf.shape[0]
    count, width = ub.shape
    router = small[2 + NC :, :]

    def gathers():
        return swap_rows(ub, rows_s, a_send, a_recv, a_send.at[2], a_recv.at[2])

    def sums():
        return sum_rows(parts, beside_in, mid, across_in, r_send, r_recv)

    @pl.when(e == 0)
    def _():
        barrier, others = greet_packs()
        rows_s[0] = ub[...]

        def prepare(d):
            rows = routing(nt(router, rows_s[d]), before[d, LOGI : LOGI + 16, :], routes[d])
            table[d] = rows
            hot = one_hot(rows[SLOT : SLOT + NF])
            coef_s[d] = slot_values(hot, rows[COEF : COEF + NF])
            hot_low = hot.astype(jnp.bfloat16)
            hot_s[d] = hot_low
            x = nn(hot_low, rows_s[d]).astype(jnp.bfloat16)
            for n in range(NF):
                x_s[n, d * MOST : (d + 1) * MOST, :] = x[n * MOST : (n + 1) * MOST]

        pl.semaphore_wait(barrier, others)
        near, far, onward = gathers()
        prepare(0)
        near.wait_recv()
        prepare(1)
        far.wait_recv()
        onward.start()
        prepare(2)
        onward.wait_recv()
        prepare(3)
        ubf[...] = rows_s[...]
        ext[:count, :] = ub[...]
        rows = table[0]
        ext[count:, :] = jnp.zeros((16, width), jnp.bfloat16)
        ext[count:, :count] = rows[COEF : COEF + 16].astype(jnp.bfloat16)
        slots = jnp.concatenate([rows[SLOT : SLOT + NF], jnp.zeros((16 - NF, count), jnp.float32)], axis=0)
        ext[count:, count : 2 * count] = slots.astype(jnp.bfloat16)
        near.wait_send()
        far.wait_send()
        onward.wait_send()

    x = x_s[e]
    gate, up = nn(x, wgu[0, 0, 0]), nn(x, wgu[0, 0, 1])
    hid = (gate * jax.nn.sigmoid(gate) * up).astype(jnp.bfloat16)
    out = nn(hid, wd[0, 0])
    at = pl.ds(pl.multiple_of(e * MOST, MOST), MOST)
    for d in range(packs):
        y_s[d, at, :] = (out[d * MOST : (d + 1) * MOST] * coef_s[d, at, :]).astype(jnp.bfloat16)

    @pl.when(e == NF - 1)
    def _():
        first, second, third = sums()
        parts[3] = tn(hot_s[3], y_s[3]).astype(jnp.bfloat16)
        first.start()
        parts[1] = tn(hot_s[1], y_s[1]).astype(jnp.bfloat16)
        second.start()
        away = tn(hot_s[2], y_s[2])
        first.wait_recv()
        mid[...] = (away + beside_in[1].astype(jnp.float32)).astype(jnp.bfloat16)
        third.start()
        home = tn(hot_s[0], y_s[0])
        _, _, scale_u, scale_c = mixing_rows(table[0])
        columns = to_columns([scale_u] + scale_c)
        values = hst[...]
        moe = home + columns[0] * ((values * rms_factor(values)) * small[1:2, :].astype(jnp.float32))
        for c in range(NC):
            moe = moe + columns[1 + c] * small[2 + c : 3 + c, :].astype(jnp.float32)
        second.wait_recv()
        moe = moe + beside_in[0].astype(jnp.float32)
        third.wait_recv()
        x_next[...] = values + (moe + across_in[...].astype(jnp.float32))
        first.wait_send()
        second.wait_send()
        third.wait_send()


def whole_spec(dims):
    return pl.BlockSpec(dims, lambda *_: (0,) * len(dims))


def exchange_scratch(packs, count, width):
    bf = jnp.bfloat16
    return [
        pltpu.VMEM((packs, count, width), bf),
        pltpu.VMEM((2, count, width), bf),
        pltpu.VMEM((count, width), bf),
        pltpu.VMEM((count, width), bf),
    ]


def ffn_forward(layer, ub, hst, small, routes, before, wgu, wd, number):
    count, width = ub.shape
    packs = routes.shape[0]
    hidden = wd.shape[2]
    bf = jnp.bfloat16
    outs = [
        shape_of((packs, count, width), bf),
        shape_of((packs, ROUT, count), jnp.float32),
        shape_of((count + 16, width), bf),
        shape_of((count, width), jnp.float32),
    ]
    return pl.pallas_call(
        ffn_fwd_kernel,
        grid=(NF,),
        out_shape=outs,
        in_specs=[whole_spec(a.shape) for a in (ub, hst, small, routes, before)]
        + [
            pl.BlockSpec((1, 1, 2, width, hidden), lambda e: (layer, e, 0, 0, 0)),
            pl.BlockSpec((1, 1, hidden, width), lambda e: (layer, e, 0, 0)),
        ],
        out_specs=[whole_spec(a.shape) for a in outs],
        scratch_shapes=[
            pltpu.VMEM((packs, count, width), bf),
            pltpu.VMEM((packs, NF * MOST, count), bf),
            pltpu.VMEM((NF, packs * MOST, width), bf),
            pltpu.VMEM((packs, NF * MOST, width), bf),
            pltpu.VMEM((packs, NF * MOST, 1), jnp.float32),
        ]
        + exchange_scratch(packs, count, width)
        + [pltpu.SemaphoreType.DMA((3,))] * 4,
        compiler_params=params_of(collective_id=number, has_side_effects=True),
        cost_estimate=BRIEF,
        name="ffn_fwd",
    )(ub, hst, small, routes, before, wgu, wd)


def silu_parts(gate, up, ghid):
    sig = jax.nn.sigmoid(gate)
    act = gate * sig
    dg = (ghid * up * sig * (1.0 + gate * (1.0 - sig))).astype(jnp.bfloat16)
    du = (ghid * act).astype(jnp.bfloat16)
    return act * up, dg, du


def ffn_bwd_kernel(
    gm, gx, ubf, table, hst, small, routes, gprev, wo, ob, wgu, wd,
    ghst, go, gwo, gsmall, glog,
    rows_s, hot_s, x_s, g_s, y_s, coef_s, gc_s, gcoef, gcoef_in, parts, beside_in, mid, across_in,
    a_send, a_recv, r_send, r_recv, c_send, c_recv,
):
    e = pl.program_id(0)
    packs = ubf.shape[0]
    ctx = lax.axis_index("ctx")
    _, _, y, k = place()
    peers = [None, 2 * y + 1 - k, 2 * (1 - y) + k, 2 * (1 - y) + 1 - k]

    def gathers():
        return swap_rows(gm, rows_s, a_send, a_recv, a_send.at[2], a_recv.at[2])

    def sums():
        return sum_rows(parts, beside_in, mid, across_in, r_send, r_recv)

    @pl.when(e == 0)
    def _():
        barrier, others = greet_packs()
        rows_s[0] = gm[...]

        def prepare(d):
            hot = one_hot(table[d, SLOT : SLOT + NF, :])
            coef_s[d] = slot_values(hot, table[d, COEF : COEF + NF, :])
            hot_low = hot.astype(jnp.bfloat16)
            hot_s[d] = hot_low
            x = nn(hot_low, ubf[d]).astype(jnp.bfloat16)
            for n in range(NF):
                x_s[n, d * MOST : (d + 1) * MOST, :] = x[n * MOST : (n + 1) * MOST]

        def spread(d):
            g = nn(hot_s[d], rows_s[d]).astype(jnp.bfloat16)
            for n in range(NF):
                g_s[n, d * MOST : (d + 1) * MOST, :] = g[n * MOST : (n + 1) * MOST]

        pl.semaphore_wait(barrier, others)
        near, far, onward = gathers()
        for d in range(packs):
            prepare(d)
        spread(0)
        near.wait_recv()
        far.wait_recv()
        onward.start()
        spread(1)
        spread(2)
        onward.wait_recv()
        spread(3)
        near.wait_send()
        far.wait_send()
        onward.wait_send()

    x = x_s[e]
    at = pl.ds(pl.multiple_of(e * MOST, MOST), MOST)
    coef = jnp.concatenate([coef_s[d, at, :] for d in range(packs)], axis=0)
    gate, up = nn(x, wgu[0, 0, 0]), nn(x, wgu[0, 0, 1])
    ghid = nt(g_s[e], wd[0, 0])
    hid, dg, du = silu_parts(gate, up, ghid * coef)
    dots = jnp.sum(hid * ghid, axis=1, keepdims=True)
    out = nt(dg, wgu[0, 0, 0]) + nt(du, wgu[0, 0, 1])
    for d in range(packs):
        y_s[d, at, :] = out[d * MOST : (d + 1) * MOST].astype(jnp.bfloat16)
        gc_s[d, at, :] = dots[d * MOST : (d + 1) * MOST]

    @pl.when(e == NF - 1)
    def _():
        first, second, third = sums()

        def coef_copy(d):
            return remote(gcoef.at[d], gcoef_in.at[d - 1], c_send.at[d - 1], c_recv.at[d - 1], ctx, peers[d])

        parts[3] = tn(hot_s[3], y_s[3]).astype(jnp.bfloat16)
        first.start()
        parts[1] = tn(hot_s[1], y_s[1]).astype(jnp.bfloat16)
        second.start()
        for d in range(packs):
            wide = hot_s[d].astype(jnp.float32) * gc_s[d]
            gcoef[d] = jnp.sum(wide.reshape(NF, MOST, wide.shape[1]), axis=1)
            if d > 0:
                coef_copy(d).start()
        away = tn(hot_s[2], y_s[2])
        first.wait_recv()
        mid[...] = (away + beside_in[1].astype(jnp.float32)).astype(jnp.bfloat16)
        third.start()
        home = tn(hot_s[0], y_s[0])
        ready = middle_ready(gx[...], table[0], hst[...], small[...])
        second.wait_recv()
        home = home + beside_in[0].astype(jnp.float32)
        total = gcoef[0]
        for d in range(1, packs):
            coef_copy(d).wait_recv()
            total = total + gcoef_in[d - 1]
        third.wait_recv()
        home = home + across_in[...].astype(jnp.float32)
        results = middle(
            ready, gx[...], home, total, table[0], routes[...], gprev[...], ubf[0], small[...], wo[...], ob[...]
        )
        for ref, value in zip((ghst, go, gwo, gsmall, glog), results):
            ref[...] = value
        first.wait_send()
        second.wait_send()
        third.wait_send()
        for d in range(1, packs):
            coef_copy(d).wait_send()


def ffn_backward(layer, gm, gx, ubf, table, hst, small, routes, gprev, wo, ob, wgu, wd, number):
    packs, count, width = ubf.shape
    hidden = wd.shape[2]
    bf, f32 = jnp.bfloat16, jnp.float32
    outs = [
        shape_of((count, width), f32),
        shape_of(ob.shape, bf),
        shape_of(wo.shape, bf),
        shape_of((1 + NC + 16, width), f32),
        shape_of((16, count), f32),
    ]
    args = (gm, gx, ubf, table, hst, small, routes, gprev, wo, ob)
    dma = pltpu.SemaphoreType.DMA
    return pl.pallas_call(
        ffn_bwd_kernel,
        grid=(NF,),
        out_shape=outs,
        in_specs=[whole_spec(a.shape) for a in args]
        + [
            pl.BlockSpec((1, 1, 2, width, hidden), lambda e: (layer, e, 0, 0, 0)),
            pl.BlockSpec((1, 1, hidden, width), lambda e: (layer, e, 0, 0)),
        ],
        out_specs=[whole_spec(a.shape) for a in outs],
        scratch_shapes=[
            pltpu.VMEM((packs, count, width), bf),
            pltpu.VMEM((packs, NF * MOST, count), bf),
            pltpu.VMEM((NF, packs * MOST, width), bf),
            pltpu.VMEM((NF, packs * MOST, width), bf),
            pltpu.VMEM((packs, NF * MOST, width), bf),
            pltpu.VMEM((packs, NF * MOST, 1), f32),
            pltpu.VMEM((packs, NF * MOST, 1), f32),
            pltpu.VMEM((packs, NF, count), f32),
            pltpu.VMEM((packs - 1, NF, count), f32),
        ]
        + exchange_scratch(packs, count, width)
        + [dma((3,))] * 6,
        compiler_params=params_of(collective_id=number, has_side_effects=True),
        cost_estimate=BRIEF,
        name="ffn_bwd",
    )(*args, wgu, wd)


PACK = 80


def pack_kernel(counts, bases, totals, tail, ext, gm, out, buf, carry, blank, sems):
    step = pl.program_id(0)
    some, count, width = gm.shape

    @pl.when(step == 0)
    def _():
        carry[...] = jnp.zeros_like(carry)
        blank[...] = jnp.zeros_like(blank)

    def whole_groups(d, e):
        at = d * NF + e
        return (bases[at] % 16 + counts[at]) // 16

    def each_copy(block, what):
        for i in range(some):
            for e in range(NF):
                groups = whole_groups(block * some + i, e)
                start = pl.multiple_of(bases[(block * some + i) * NF + e] // 16 * 16, 16)
                for n in range(1, PACK // 16):

                    @pl.when(groups == n)
                    def _():
                        source = buf.at[block % 2, i, e, pl.ds(0, 16 * n), :]
                        what(pltpu.make_async_copy(source, out.at[e, pl.ds(start, 16 * n), :], sems.at[block % 2, i, e]))

    def begin(copy):
        copy.start()

    def end(copy):
        copy.wait()

    @pl.when(step >= 2)
    def _():
        each_copy(step - 2, end)

    ids = lax.broadcasted_iota(jnp.int32, (PACK, count), 0)
    side = step % 2
    for i in range(some):
        d = step * some + i
        rows = tail[i].astype(jnp.float32)
        slot = rows[:NF, count : 2 * count].astype(jnp.int32)
        slot = jnp.where(slot < 0, -PACK, slot)
        hot, weighted = [], []
        for e in range(NF):
            hit = ids == slot[e : e + 1] + bases[d * NF + e] % 16
            hot.append(jnp.where(hit, 1.0, 0.0).astype(jnp.bfloat16))
            weighted.append(jnp.where(hit, rows[e : e + 1, :count], 0.0).astype(jnp.bfloat16))
        low = nn(jnp.concatenate(hot, axis=0), ext[i, :count, :]).astype(jnp.bfloat16)
        low_g = nn(jnp.concatenate(weighted, axis=0), gm[i]).astype(jnp.bfloat16)
        for lanes, values in ((slice(0, width), low), (slice(width, 2 * width), low_g)):
            for e in range(NF):
                buf[side, i, e, :, lanes] = values[e * PACK : (e + 1) * PACK]
    for i in range(some):
        for e in range(NF):
            buf[side, i, e, :16, :] += carry[e]
            group = pl.multiple_of(whole_groups(step * some + i, e) * 16, 16)
            carry[e] = buf[side, i, e, pl.ds(group, 16), :]
    each_copy(step, begin)

    @pl.when(step == pl.num_programs(0) - 1)
    def _():
        last = pl.num_programs(0)
        each_copy(last - 2, end)
        each_copy(last - 1, end)
        copies = []
        for e in range(NF):
            start = pl.multiple_of(totals[e] // 16 * 16, 16)
            copies.append(pltpu.make_async_copy(carry.at[e], out.at[e, pl.ds(start, 16), :], sems.at[0, 0, e]))
            rest = out.at[e, pl.ds(start + 16, blank.shape[0]), :]
            copies.append(pltpu.make_async_copy(blank, rest, sems.at[1, 0, e]))
        for copy in copies:
            copy.start()
        for copy in copies:
            copy.wait()


def expert_counts(ext):
    count = ext.shape[2] // 3
    slot = ext[:, ext.shape[1] - 16 : ext.shape[1] - 16 + NF, count : 2 * count].astype(jnp.float32)
    counts = (jnp.max(slot, axis=2) + 1.0).astype(jnp.int32)
    upto = jnp.cumsum(counts, axis=0)
    return counts.reshape(-1), (upto - counts).reshape(-1), upto[-1]


def pack_rows(numbers, ext, gm):
    devices, count, width = gm.shape
    some, blank = 4, 256
    bf = jnp.bfloat16
    return pl.pallas_call(
        pack_kernel,
        grid_spec=pltpu.PrefetchScalarGridSpec(
            num_scalar_prefetch=3,
            grid=(devices // some,),
            in_specs=[
                pl.BlockSpec((some, 16, width), lambda d, *_: (d, count // 16, 0)),
                pl.BlockSpec((some,) + ext.shape[1:], lambda d, *_: (d, 0, 0)),
                pl.BlockSpec((some, count, width), lambda d, *_: (d, 0, 0)),
            ],
            out_specs=pl.BlockSpec(memory_space=pl.ANY),
            scratch_shapes=[
                pltpu.VMEM((2, some, NF, PACK, 2 * width), bf),
                pltpu.VMEM((NF, 16, 2 * width), bf),
                pltpu.VMEM((blank, 2 * width), bf),
                pltpu.SemaphoreType.DMA((2, some, NF)),
            ],
        ),
        out_shape=shape_of((NF, devices * MOST + 16 + blank, 2 * width), bf),
        compiler_params=params_of(),
        cost_estimate=BRIEF,
        name="pack_rows",
    )(*numbers, ext, ext, gm)


def dw_kernel(first, totals, packed, wgu, wd, *refs):
    dgu, dd, pair_s, hid_s = refs[-4:]
    hidden = hid_s.shape[1]
    total = totals[first + pl.program_id(0)]
    width = packed.shape[2] // 2
    chunk = 1024

    def pieces(part):
        xs, gs = packed[0, part, :width], packed[0, part, width:]
        hid, dg, du = silu_parts(nn(xs, wgu[0, 0, 0]), nn(xs, wgu[0, 0, 1]), nt(gs, wd[0, 0]))
        hid_s[part, :] = hid.astype(jnp.bfloat16)
        pair_s[part, :hidden] = dg
        pair_s[part, hidden:] = du

    def chunk_of(i, _):
        pieces(pl.ds(pl.multiple_of(i * chunk, chunk), chunk))
        return 0

    needed = jnp.maximum((total + 255) // 256, 1)
    lax.fori_loop(0, needed // 4, chunk_of, 0)

    @pl.when(needed % 4 >= 2)
    def _():
        pieces(pl.ds(pl.multiple_of(needed // 4 * chunk, 512), 512))

    @pl.when(needed % 2 == 1)
    def _():
        pieces(pl.ds(pl.multiple_of((needed - 1) * 256, 256), 256))

    for size in range(1, hid_s.shape[0] // 256 + 1):

        @pl.when(needed == size)
        def _():
            rows = 256 * size

            def inputs(i, _):
                part = pl.ds(pl.multiple_of(i * 384, 384), 384)
                xs = packed[0, :rows, part]
                both = tn(xs, pair_s[:rows, :])
                dgu[0, 0, 0, part, :] = both[:, :hidden]
                dgu[0, 0, 1, part, :] = both[:, hidden:]
                return 0

            lax.fori_loop(0, width // 384, inputs, 0)

            def outputs(i, _):
                part = pl.ds(pl.multiple_of(i * 512, 512), 512)
                dd[0, 0, part, :] = tn(hid_s[:rows, part], packed[0, :rows, width:])
                return 0

            lax.fori_loop(0, hid_s.shape[1] // 512, outputs, 0)


def weight_grads(layer, first, last, totals, packed, wgu, wd, earlier):
    _, rows, both = packed.shape
    hidden, width = wd.shape[2], wd.shape[3]
    gu_spec = pl.BlockSpec((1, 1, 2, width, hidden), lambda e, *_: (layer, e + first, 0, 0, 0))
    d_spec = pl.BlockSpec((1, 1, hidden, width), lambda e, *_: (layer, e + first, 0, 0))
    row_spec = pl.BlockSpec((1, rows, both), lambda e, *_: (e + first, 0, 0))
    return pl.pallas_call(
        functools.partial(dw_kernel, first),
        grid_spec=pltpu.PrefetchScalarGridSpec(
            num_scalar_prefetch=1,
            grid=(last - first,),
            in_specs=[row_spec, gu_spec, d_spec] + [pl.BlockSpec(memory_space=pl.ANY)] * len(earlier),
            out_specs=[gu_spec, d_spec],
            scratch_shapes=[
                pltpu.VMEM((rows // 256 * 256 - 256, 2 * hidden), jnp.bfloat16),
                pltpu.VMEM((rows // 256 * 256 - 256, hidden), jnp.bfloat16),
            ],
        ),
        out_shape=[shape_of(wgu.shape, jnp.float32), shape_of(wd.shape, jnp.float32)],
        input_output_aliases={4 + i: i for i in range(len(earlier))},
        compiler_params=params_of(),
        cost_estimate=BRIEF,
        name="weight_grads",
    )(totals, packed, wgu, wd, *earlier)


def norm_low(x, gain):
    return ((x * rms_factor(x)) * gain).astype(jnp.bfloat16)


def post_attention(ob, x, wo, gain):
    groups = wo.shape[0]
    inner = wo.shape[1]
    blk = ob.shape[1]
    halves = []
    for h in range(2):
        total = x[h * blk : (h + 1) * blk]
        for g in range(groups):
            total = total + nn(ob[h * groups + g][:, :inner], wo[g])
        halves.append(total)
    hst = jnp.concatenate(halves, axis=0)
    return hst, norm_low(hst, gain)


def mixing_rows(table):
    raw, coef = table[RAW : RAW + 16], table[COEF : COEF + 16]
    pairs = []
    for c in range(NC):
        r0, r1 = raw[NE + 2 * c : NE + 2 * c + 1], raw[NE + 2 * c + 1 : NE + 2 * c + 2]
        top = jnp.maximum(r0, r1)
        e0, e1 = jnp.exp(r0 - top), jnp.exp(r1 - top)
        pairs.append((e0 / (e0 + e1), e1 / (e0 + e1)))
    shares = [coef[NF + 2 + c : NF + 3 + c] for c in range(NC)]
    scale_u = coef[NF + 1 : NF + 2]
    for c in range(NC):
        scale_u = scale_u + shares[c] * pairs[c][0]
    return pairs, shares, scale_u, [shares[c] * pairs[c][1] for c in range(NC)]


def middle_ready(gx, table, hst, small):
    gain = small[1:2].astype(jnp.float32)
    consts = small[2 : 2 + NC].astype(jnp.float32)
    pairs, shares, scale_u, scale_c = mixing_rows(table)
    columns = to_columns([scale_u] + scale_c)
    factor = rms_factor(hst)
    base = hst * factor
    u = base * gain
    dots = [jnp.sum(gx * u, axis=1, keepdims=True)]
    dots += [jnp.sum(gx * consts[c : c + 1], axis=1, keepdims=True) for c in range(NC)]
    dots = to_rows(dots, 8)
    const_sums = [jnp.sum(gx * columns[1 + c], axis=0, keepdims=True) for c in range(NC)]
    return pairs, shares, gain, factor, base, dots, const_sums, gx * columns[0]


def middle(ready, gx, parts, gcoef, table, routes, gprev, ub, small, wo, ob):
    pairs, shares, gain, factor, base, dots, const_sums, grad_in = ready
    groups = wo.shape[0]
    inner = wo.shape[1]
    blk = ob.shape[1]
    router = small[2 + NC :]
    dot_u = dots[0:1]
    dot_c = [dots[1 + c : 2 + c] for c in range(NC)]
    ids = lax.broadcasted_iota(jnp.int32, (16, gx.shape[0]), 0)
    grads = jnp.concatenate([gcoef, jnp.zeros_like(gcoef)], axis=0)
    grads = jnp.where(ids == NF + 1, dot_u, grads)
    raw_rows = []
    for c in range(NC):
        a0, a1 = pairs[c]
        grads = jnp.where(ids == NF + 2 + c, a0 * dot_u + a1 * dot_c[c], grads)
        g0, g1 = shares[c] * dot_u, shares[c] * dot_c[c]
        both = a0 * g0 + a1 * g1
        raw_rows += [a0 * (g0 - both), a1 * (g1 - both)]
    logits = table[LOGI : LOGI + 16]
    first, second = ids == routes[0:1], ids == routes[1:2]

    def pick(chosen, rows):
        return jnp.sum(jnp.where(chosen, rows, 0.0), axis=0, keepdims=True)

    z0, z1 = pick(first, logits), pick(second, logits)
    top = jnp.maximum(z0, z1)
    e0, e1 = jnp.exp(z0 - top), jnp.exp(z1 - top)
    w0, w1 = e0 / (e0 + e1), e1 / (e0 + e1)
    gg0, gg1 = pick(first, grads), pick(second, grads)
    both = w0 * gg0 + w1 * gg1
    glog = jnp.where(first, w0 * (gg0 - both), 0.0) + jnp.where(second, w1 * (gg1 - both), 0.0) + gprev
    graw = glog
    for index, row in enumerate(raw_rows):
        graw = jnp.where(ids == NE + index, row, graw)
    graw = graw.astype(jnp.bfloat16)
    grad_router = nn(graw, ub)
    gu = grad_in + tn(graw, router) + parts
    sums = [jnp.sum(gu * base, axis=0, keepdims=True)]
    sums += const_sums
    gb = gu * gain
    ghst = gx + factor * (gb - base * jnp.mean(gb * base, axis=-1, keepdims=True))
    gy = ghst.astype(jnp.bfloat16)
    lanes = ob.shape[2]
    go, gwo = [None] * (2 * groups), []
    for g in range(groups):
        value = nt(gy, wo[g]).astype(jnp.bfloat16)
        value = jnp.concatenate([value, jnp.zeros((value.shape[0], lanes - inner), jnp.bfloat16)], axis=1)
        for h in range(2):
            go[h * groups + g] = value[h * blk : (h + 1) * blk]
        mixed = jnp.concatenate([ob[g], ob[groups + g]], axis=0)
        gwo.append(tn(mixed, gy)[:inner].astype(jnp.bfloat16))
    return ghst, jnp.stack(go), jnp.stack(gwo), jnp.concatenate(sums + [grad_router], axis=0), glog


def assemble_kernel(ours, theirs, qkv, out, gains, router, consts):
    z, _, _, _ = place()
    layers = ours.shape[0]
    inner = GROUP_HEADS * HEAD_DIM
    for l in range(layers):
        small = ours[l, :, :128].astype(jnp.float32) + theirs[l, :, :128].astype(jnp.float32)
        router[l] = small[:, 2 + NC : 2 + NC + 16]
        rows = jnp.transpose(small)
        gains[l] = rows[:2]
        consts[l] = rows[2 : 2 + NC]
        first = 128 + 6 * inner
        out[l] = ours[l, :, first:].astype(jnp.float32) + theirs[l, :, first:].astype(jnp.float32)
        for group in range(4):
            for odd in range(2):

                @pl.when(z % 2 == odd)
                def _():
                    source = ours if group // 2 == odd else theirs
                    for c in range(3):
                        at = 128 + (group % 2) * 3 * inner + c * inner
                        qkv[l, c, :, group * inner : (group + 1) * inner] = source[l, :, at : at + inner].astype(jnp.float32)


def assemble(ours, theirs, width):
    layers, shard, _ = ours.shape
    vm = pl.BlockSpec(memory_space=pltpu.VMEM)
    f32 = jnp.float32
    return pl.pallas_call(
        assemble_kernel,
        out_shape=[
            shape_of((layers, 3, shard, width), f32),
            shape_of((layers, shard, width), f32),
            shape_of((layers, 2, shard), f32),
            shape_of((layers, shard, 16), f32),
            shape_of((layers, NC, shard), f32),
        ],
        in_specs=[vm] * 2,
        out_specs=[vm] * 5,
        compiler_params=params_of(),
        cost_estimate=BRIEF,
        name="assemble",
    )(ours, theirs)


def turn_tables(seq):
    half = HEAD_DIM // 2
    frequency = np.exp((-np.log(np.float32(10000.0)) * np.arange(half, dtype=np.float32) / np.float32(half)))
    angles = np.arange(seq, dtype=np.float32)[:, None] * frequency.astype(np.float32)[None, :]
    cosine, sine = np.cos(angles), np.sin(angles)
    cosine = np.concatenate([cosine, cosine] * 2, axis=1).astype(np.float32)
    sine = np.concatenate([-sine, sine] * 2, axis=1).astype(np.float32)
    return jnp.asarray(cosine), jnp.asarray(sine)


def by_heads(
    tokens,
    cotangent,
    seq_lengths,
    block_order,
    routes,
    gains,
    qkv_weights,
    out_weight,
    router,
    const_values,
    w_gate_up,
    w_down,
):
    count, width = tokens.shape[1], tokens.shape[2]
    ctx_size, packs = lax.axis_size("ctx"), lax.axis_size("fsdp")
    blk = count // 2
    seq = blk * ctx_size
    pack = lax.axis_index("fsdp")
    z, xx, y, k = place()
    sequence = z // 2
    shard = width // packs
    f32, bf = jnp.float32, jnp.bfloat16
    everyone = ("ctx", "fsdp")

    cosine, sine = turn_tables(seq)
    routes_t = jnp.swapaxes(routes[:, 0], 1, 2)
    smalls = jnp.concatenate([gains, const_values, jnp.swapaxes(router, 1, 2)], axis=1)
    per_layer = smalls.shape[1]
    ints = jnp.concatenate([routes_t.reshape(-1), block_order[0]])
    places = ints.size
    ints = jnp.pad(ints, (0, -places % shard)).astype(bf).reshape(-1, shard)
    smalls = jnp.concatenate([smalls.reshape(LAYERS * per_layer, shard), ints], axis=0)
    smalls = jnp.pad(smalls, ((0, -smalls.shape[0] % 16), (0, 0)))
    smalls = lax.all_gather(smalls, "fsdp", axis=1, tiled=True)
    ints = smalls[LAYERS * per_layer : LAYERS * per_layer + ints.shape[0]].reshape(-1, packs, shard)
    ints = jnp.swapaxes(ints, 0, 1).reshape(packs, -1).astype(jnp.int32)
    smalls = [smalls[l * per_layer : (l + 1) * per_layer] for l in range(LAYERS)]
    near = jnp.stack([pack, 2 * y + 1 - k, 2 * (1 - y) + k, 2 * (1 - y) + 1 - k])
    routes_f = ints[near][:, : routes_t.size].reshape((packs,) + routes_t.shape)
    order = lax.dynamic_index_in_dim(ints, 2 * y + xx, 0, keepdims=False)
    order = order[routes_t.size : places].reshape(ctx_size, 2)
    order = lax.dynamic_index_in_dim(order, sequence, 1, keepdims=False) - ctx_size * sequence
    ids = jnp.arange(ctx_size, dtype=jnp.int32)
    inv = jnp.sum(jnp.where(order[None, :] == ids[:, None], ids[None, :], 0), axis=1)

    gm_all = [None, lax.all_gather(cotangent[0], everyone, axis=0, tiled=False)]
    x = tokens[0].astype(f32)
    before = jnp.zeros((packs, ROUT, count), f32)
    kept, ext_all = [], [None] * LAYERS
    for l in range(LAYERS):
        n1s, qkv, o, lse, ob, hst, ub, w, wo = attn_forward(
            l, order, inv, x, smalls[l], qkv_weights, cosine, sine, out_weight, 2 * l
        )
        if l == 1:
            ub, gm_all[1] = lax.optimization_barrier((ub, gm_all[1]))
            hst, first_ext = lax.optimization_barrier((hst, ext_all[0]))
            ext_all[0] = lax.all_gather(first_ext, everyone, axis=0, tiled=False)
        ubf, table, ext, x_next = ffn_forward(
            l, ub, hst, smalls[l], routes_f[:, l], before, w_gate_up, w_down, 2 * l + 1
        )
        before = table
        ext_all[l] = ext if l == 0 else lax.all_gather(ext, everyone, axis=0, tiled=False)
        kept.append((x, n1s, qkv, o, lse, ob, hst, w, wo, ubf, table))
        x = x_next
    output = x
    gm = cotangent[0]
    gx = gm.astype(f32)
    gprev = jnp.zeros((16, count), f32)
    grads = [None] * LAYERS
    for l in reversed(range(LAYERS)):
        x, n1s, qkv, o, lse, ob, hst, w, wo, ubf, table = kept[l]
        number = 2 * LAYERS + 2 * l
        ghst, go, gwo, small, gprev = ffn_backward(
            l, gm, gx, ubf, table, hst, smalls[l], routes_t[l], gprev, wo, ob, w_gate_up, w_down, number
        )
        if l == 0:
            go, ext_all[0] = lax.optimization_barrier((go, ext_all[0]))
        gx, gm, grads[l] = attn_backward(
            order, inv, n1s, w, cosine, sine, qkv, o, lse, go, ghst, x, smalls[l], small, gwo, number + 1
        )
        if l > 0:
            gm_all[l - 1] = gm

    dense = jnp.stack(grads)
    dense, gm = lax.optimization_barrier((dense, gm_all[0]))
    gm_all[0] = lax.all_gather(gm, everyone, axis=0, tiled=False)

    def partner(values, distance):
        return lax.ppermute(values, "ctx", [(i, i ^ distance) for i in range(ctx_size)])

    def added(first, second):
        return (first.astype(f32) + second.astype(f32)).astype(bf)

    half = NF // 2
    numbers = expert_counts(ext_all[1])
    packed = pack_rows(numbers, ext_all[1], gm_all[1])
    dense, packed = lax.optimization_barrier((dense, packed))
    got = partner(dense, 1)
    done = weight_grads(1, 0, NF, numbers[2], packed, w_gate_up, w_down, ())
    done, got = lax.optimization_barrier((done, got))
    dense = added(dense, got)
    dense, ext, gm = lax.optimization_barrier((dense, ext_all[0], gm_all[0]))
    got = partner(dense, 4)
    numbers = expert_counts(ext)
    packed = pack_rows(numbers, ext, gm)
    done = weight_grads(0, 0, half, numbers[2], packed, w_gate_up, w_down, done)
    done, got = lax.optimization_barrier((done, got))
    dense = added(dense, got)
    dense, done = lax.optimization_barrier((dense, done))
    got = partner(dense, 2)
    done = weight_grads(0, half, NF, numbers[2], packed, w_gate_up, w_down, done)
    done, got = lax.optimization_barrier((done, got))
    qkv, out, gain_grad, router_grad, const_grad = assemble(dense, got, width)
    return (
        output[None],
        gx[None],
        gain_grad,
        qkv,
        out,
        router_grad,
        const_grad,
        done[0],
        done[1],
    )


def solution(mesh):
    placed = (
        P("fsdp", "ctx", None),
        P("fsdp", "ctx", None),
        P("fsdp", None),
        P("fsdp", None),
        P(None, "fsdp", "ctx", None),
        P(None, None, "fsdp"),
        P(None, None, "fsdp", None),
        P(None, "fsdp", None),
        P(None, "fsdp", None),
        P(None, None, "fsdp"),
        P(None, None, None, None, "fsdp"),
        P(None, None, "fsdp", None),
    )
    contexts, packs = mesh.shape["ctx"], mesh.shape["fsdp"]
    blocks_of_heads = HEADS // GROUP_HEADS

    def plan(*args):
        tokens = args[0]
        even = tokens.shape[1] * contexts == 2 * MINLEN
        grouped = contexts == 2 * blocks_of_heads and packs == blocks_of_heads
        return (by_heads if even and grouped else shards)(*args)

    return jax.shard_map(
        plan,
        mesh=mesh,
        in_specs=placed,
        out_specs=(
            P("fsdp", "ctx", None),
            P("fsdp", "ctx", None),
            P(None, None, "fsdp"),
            P(None, None, "fsdp", None),
            P(None, "fsdp", None),
            P(None, "fsdp", None),
            P(None, None, "fsdp"),
            P(None, None, None, None, "fsdp"),
            P(None, None, "fsdp", None),
        ),
        check_vma=False,
    )
```
